128 devices in a mesh: fsdp: 16 (over y_hi, z, core), rep: 8 (over x, y_lo).
Axes of the slice: x: 4, y: 4 (y_hi: 2, y_lo: 2; y = y_hi * 2 + y_lo), z: 4, core: 2. Of those that a mesh axis runs over, the one named last changes fastest.
Arguments:
- tokens: bfloat16 [32768, 1536], P(('fsdp', 'rep')), may hold values from -6 to 6
- cotangent: bfloat16 [32768, 1536], P(('fsdp', 'rep')), may hold values from -6 to 6
- lengths: int32 [16, 3], replicated, may hold values from 1 to 2046, as said below
- w_in: float32 [1536, 6400], P('fsdp'), may hold values from -0.15625 to 0.15625
- w_dt: float32 [1536, 48], P('fsdp'), may hold values from -0.15625 to 0.15625
- w_out: float32 [3072, 1536], P('fsdp'), may hold values from -0.109375 to 0.109375
- small: float32 [21392], P('fsdp'), may hold values from -6 to 1.5, as said below
- first_in: float32 [1536, 6400], P('fsdp'), may hold values from -80 to 80
- first_dt: float32 [1536, 48], P('fsdp'), may hold values from -12 to 12
- first_out: float32 [3072, 1536], P('fsdp'), may hold values from -128 to 128
- first_small: float32 [21392], P('fsdp'), may hold values from -64 to 64
- second_in: float32 [1536, 6400], P('fsdp'), may hold values from 16.384 to 65.536
- second_dt: float32 [1536, 48], P('fsdp'), may hold values from 0.32768 to 1.31072
- second_out: float32 [3072, 1536], P('fsdp'), may hold values from 32.768 to 131.072
- second_small: float32 [21392], P('fsdp'), may hold values from 8.192 to 32.768
Outputs:
- block_out: float32 [32768, 1536], P(('fsdp', 'rep'))
- input_grad: float32 [32768, 1536], P(('fsdp', 'rep'))
- grad_in: float32 [1536, 6400], P('fsdp')
- grad_dt: float32 [1536, 48], P('fsdp')
- grad_out: float32 [3072, 1536], P('fsdp')
- grad_small: float32 [21392], P('fsdp')
- new_first_in: float32 [1536, 6400], P('fsdp')
- new_first_dt: float32 [1536, 48], P('fsdp')
- new_first_out: float32 [3072, 1536], P('fsdp')
- new_first_small: float32 [21392], P('fsdp')
- new_second_in: float32 [1536, 6400], P('fsdp')
- new_second_dt: float32 [1536, 48], P('fsdp')
- new_second_out: float32 [3072, 1536], P('fsdp')
- new_second_small: float32 [21392], P('fsdp')
- new_in: float32 [1536, 6400], P('fsdp')
- new_dt: float32 [1536, 48], P('fsdp')
- new_out: float32 [3072, 1536], P('fsdp')
- new_small: float32 [21392], P('fsdp')
The draws below stay inside these ranges and needn't reach their ends.
Inputs may be any that keep to these rules, and one draw needn't show every extreme that they name: Row f holds the lengths of the three sequences that fill pack f from its position 0; the rest of its 2048 positions is padding. The first and third are at most 64 long, the padding at most 128, so the second begins within the first 256 positions and ends within the last 256. In every draw some pack has first and third sequences of length 1 and no padding. `small`: layout as in the reference program: gains in 0.7 to 1.3, taps within 1.5 in magnitude, conv_bias within 0.5, dt_bias -6 to -2.5, a_log -3 to 0.7, d_skip 0.5 to 1.5.
All inputs are finite; a program needn't handle non-finite values.
Results may differ from the reference program's by a relative error of at most 0.003.
The reference program's roundings to bfloat16 on the way count: a program that leaves them out, or rounds other values in their place, can miss the bound.
Values may be sent and summed in bfloat16 or wider, within the bound.
No kernel may reach another device: no remote copies, remote signals or barrier semaphores. Data moves between devices by JAX's collectives and lax.ppermute only.
A program may use at most 320 MiB of HBM per device.

```python
import math
import jax
import jax.numpy as jnp
from jax import lax

D = 1536
H = 48
P_SIZE = 64
N = 128
CONV = 4
TOK_DEV = 256
STEP = 10
DI = 3072
SMALL = 21392
PACK = 2048
TOKENS = 32768
N_FSDP = 16
N_REP = 8


def draw_lengths(key, part):
    key = jax.random.fold_in(key, 11)
    keys = jax.random.split(key, 4)
    leading = jax.random.randint(keys[0], (N_FSDP,), 1, TOK_DEV // 4 + 1)
    trailing = jax.random.randint(keys[1], (N_FSDP,), 1, TOK_DEV // 4 + 1)
    padding = jax.random.randint(keys[2], (N_FSDP,), 0, TOK_DEV // 2 + 1)
    chosen = jax.random.randint(keys[3], (), 0, N_FSDP)
    picked = jnp.arange(N_FSDP, dtype=jnp.int32) == chosen
    leading = jnp.where(picked, 1, leading)
    trailing = jnp.where(picked, 1, trailing)
    padding = jnp.where(picked, 0, padding)
    middle = PACK - padding - leading - trailing
    return jnp.stack([leading, middle, trailing], 1).astype(jnp.int32)


def draw_small(key, part):
    key = jax.random.fold_in(key, 7)
    keys = jax.random.split(key, 7)
    channels = H * P_SIZE + 2 * N
    gain_in = jax.random.uniform(keys[0], (D,), jnp.float32, 0.7, 1.3)
    gain_out = jax.random.uniform(keys[1], (H * P_SIZE,), jnp.float32, 0.7, 1.3)
    conv_taps = jnp.clip(0.5 * jax.random.normal(keys[2], (CONV * channels,), jnp.float32), -1.5, 1.5)
    conv_bias = jax.random.uniform(keys[3], (channels,), jnp.float32, -0.5, 0.5)
    dt_bias = jax.random.uniform(keys[4], (H,), jnp.float32, -6.0, -2.5)
    a_log = jax.random.uniform(keys[5], (H,), jnp.float32, -3.0, 0.7)
    d_skip = jax.random.uniform(keys[6], (H,), jnp.float32, 0.5, 1.5)
    return jnp.concatenate([gain_in, gain_out, conv_taps, conv_bias, dt_bias, a_log, d_skip]).astype(jnp.float32)


def level_of(own_key, dims, cuts, least, largest):
    gain = 1.0
    for dim, parts in cuts:
        draws = jax.random.uniform(jax.random.fold_in(jax.random.fold_in(own_key, 6), dim), (parts,), jnp.float32, least / len(cuts), largest / len(cuts))
        gain = gain * jnp.repeat(jnp.exp(draws), dims[dim] // parts).reshape((-1,) + (1,) * (len(dims) - 1 - dim))
    return gain


def normal_values(stream_key, shape, deviation, limit, cuts=(), held_as=jnp.bfloat16):
    factor_of = level_of(stream_key, shape, cuts, -0.22, 0.18) if cuts else 1.0
    entries = jax.random.normal(stream_key, shape, jnp.float32) * deviation * factor_of
    return jnp.minimum(jnp.maximum(entries, -limit), limit).astype(held_as)


def setup_inputs(seed: int = 0) -> dict:
    splits = jax.random.split(jax.random.key(seed), 16)
    return {
        "tokens": normal_values(splits[0], (TOKENS, D), 1.0, 6.0, ((0, 128),)),
        "cotangent": normal_values(splits[1], (TOKENS, D), 1.0, 6.0, ((0, 128),)),
        "lengths": draw_lengths(jax.random.fold_in(splits[15], 71), 0),
        "w_in": normal_values(splits[3], (D, 2 * DI + 2 * N), D ** -0.5, 0.15625, ((0, 16),), jnp.float32),
        "w_dt": normal_values(splits[4], (D, H), D ** -0.5, 0.15625, ((0, 16),), jnp.float32),
        "w_out": normal_values(splits[5], (DI, D), DI ** -0.5, 0.109375, ((0, 16),), jnp.float32),
        "small": draw_small(jax.random.fold_in(splits[15], 71), 0),
        "first_in": normal_values(splits[7], (D, 2 * DI + 2 * N), (0.08 * TOKENS ** 0.5), 80.0, ((0, 16),), jnp.float32),
        "first_dt": normal_values(splits[8], (D, H), (0.011 * TOKENS ** 0.5), 12.0, ((0, 16),), jnp.float32),
        "first_out": normal_values(splits[9], (DI, D), (0.11 * TOKENS ** 0.5), 128.0, ((0, 16),), jnp.float32),
        "first_small": normal_values(splits[10], (SMALL,), (0.055 * TOKENS ** 0.5), 64.0, ((0, 16),), jnp.float32),
        "second_in": jnp.clip(jnp.exp(math.log(65.536) - 1.3862944 * jax.random.uniform(splits[11], (D, 2 * DI + 2 * N), jnp.float32) ** level_of(splits[11], (D, 2 * DI + 2 * N), ((0, 16),), -0.2, 0.2)), 16.384, 65.536),
        "second_dt": jnp.clip(jnp.exp(math.log(1.31072) - 1.3862944 * jax.random.uniform(splits[12], (D, H), jnp.float32) ** level_of(splits[12], (D, H), ((0, 16),), -0.2, 0.2)), 0.32768, 1.31072),
        "second_out": jnp.clip(jnp.exp(math.log(131.072) - 1.3862944 * jax.random.uniform(splits[13], (DI, D), jnp.float32) ** level_of(splits[13], (DI, D), ((0, 16),), -0.2, 0.2)), 32.768, 131.072),
        "second_small": jnp.clip(jnp.exp(math.log(32.768) - 1.3862944 * jax.random.uniform(splits[14], (SMALL,), jnp.float32) ** level_of(splits[14], (SMALL,), ((0, 16),), -0.2, 0.2)), 8.192, 32.768),
    }


NORM_EPS = 1e-05
BETA_ONE = 0.9
BETA_TWO = 0.999
ADAM_EPS = 1e-08
WEIGHT_DECAY = 0.1
RATE_MATRIX = 0.04
RATE_SMALL = 0.4
PRECISE = lax.Precision.HIGHEST

@jax.custom_vjp
def low(v):
    return lax.optimization_barrier(v.astype(jnp.bfloat16)).astype(jnp.float32)

@jax.custom_vjp
def low_back(v):
    return v

def low_keep(v):
    return (low(v), None)

def low_pass(kept, grad):
    return (grad,)

def back_keep(v):
    return (v, None)

def back_low(kept, grad):
    return (low(grad),)
low.defvjp(low_keep, low_pass)
low_back.defvjp(back_keep, back_low)

def unpack_small(vector):
    inner_width = H * P_SIZE
    channels = inner_width + 2 * N
    offset = 0
    gain_in = vector[offset:offset + D]
    offset = offset + D
    gain_out = vector[offset:offset + inner_width]
    offset = offset + inner_width
    conv_taps = vector[offset:offset + CONV * channels].reshape(CONV, channels)
    offset = offset + CONV * channels
    conv_bias = vector[offset:offset + channels]
    offset = offset + channels
    dt_bias = vector[offset:offset + H]
    a_log = vector[offset + H:offset + 2 * H]
    d_skip = vector[offset + 2 * H:offset + 3 * H]
    return (gain_in, gain_out, conv_taps, conv_bias, dt_bias, a_log, d_skip)

def segment_at(positions, seg_ends):
    counted = lax.optimization_barrier(jnp.sum((positions[:, None] >= seg_ends[None, :]).astype(jnp.int32), axis=1)).astype(jnp.int32)
    return jnp.where(positions < 0, jnp.int32(-1), counted).astype(jnp.int32)

def conv_part(extended, dt_raw, conv_taps, conv_bias, dt_bias, a_log, same_masks):
    row_count = dt_raw.shape[0]
    conv_width = conv_taps.shape[0]
    inner_width = H * P_SIZE
    summed = conv_bias[None, :] + conv_taps[conv_width - 1][None, :] * extended[conv_width - 1:]
    for offset in range(1, conv_width):
        tap_index = conv_width - 1 - offset
        summed = summed + conv_taps[tap_index][None, :] * extended[tap_index:tap_index + row_count] * same_masks[offset][:, None]
    active = jax.nn.silu(summed)
    heads_x = active[:, :inner_width].reshape(row_count, H, P_SIZE)
    state_b = active[:, inner_width:inner_width + N]
    state_c = active[:, inner_width + N:]
    step_dt = jax.nn.softplus(dt_raw + dt_bias[None, :])
    log_decay = -step_dt * jnp.exp(a_log)[None, :]
    return (heads_x, state_b, state_c, step_dt, log_decay)

def block_terms(carry_state, prior_segment, heads_x, state_b, state_c, step_dt, log_decay, segments):
    block_rows = heads_x.shape[0]
    cumulative = jnp.cumsum(log_decay, axis=0)
    positions_in = jnp.arange(block_rows, dtype=jnp.int32)
    same_seg = ((segments[:, None] == segments[None, :]) & (positions_in[:, None] >= positions_in[None, :])).astype(jnp.float32)
    span_logs = cumulative.T[:, :, None] - cumulative.T[:, None, :]
    decay_matrix = jnp.exp(jnp.where(same_seg[None] > 0, span_logs, 0.0)) * same_seg[None]
    scores = jnp.dot(state_c, state_b.T, precision=PRECISE)
    mixing = decay_matrix * scores[None] * step_dt.T[:, None, :]
    outputs = jnp.einsum('hts,shp->thp', mixing, heads_x, precision=PRECISE)
    entering = (segments == prior_segment).astype(jnp.float32)[:, None] * jnp.exp(cumulative)
    outputs = outputs + entering[:, :, None] * jnp.einsum('tn,hpn->thp', state_c, carry_state, precision=PRECISE)
    leaving = (segments == segments[-1]).astype(jnp.float32)[:, None] * jnp.exp(cumulative[-1][None, :] - cumulative) * step_dt
    passing = (segments[-1] == prior_segment).astype(jnp.float32) * jnp.exp(cumulative[-1])
    new_state = passing[:, None, None] * carry_state + jnp.einsum('sh,shp,sn->hpn', leaving, heads_x, state_b, precision=PRECISE)
    return (new_state, outputs)

def reshape_blocks(array, block_rows):
    return array.reshape((array.shape[0] // block_rows, block_rows) + array.shape[1:])

def local_scan(heads_x, state_b, state_c, step_dt, log_decay, segments, entry_segment, block_rows):
    row_count = heads_x.shape[0]
    priors = jnp.concatenate([jnp.reshape(entry_segment, (1,)).astype(jnp.int32), segments[block_rows - 1:row_count - 1:block_rows]]).astype(jnp.int32)

    def advance(carry_state, pieces):
        return block_terms(carry_state, pieces[6], pieces[0], pieces[1], pieces[2], pieces[3], pieces[4], pieces[5])
    start_state = jnp.zeros((heads_x.shape[1], heads_x.shape[2], state_b.shape[1]), jnp.float32)
    pieces = (reshape_blocks(heads_x, block_rows), reshape_blocks(state_b, block_rows), reshape_blocks(state_c, block_rows), reshape_blocks(step_dt, block_rows), reshape_blocks(log_decay, block_rows), reshape_blocks(segments, block_rows), priors)
    final_state, outputs = lax.scan(jax.checkpoint(advance), start_state, pieces)
    return (outputs.reshape(heads_x.shape), final_state)

def pack_forward(inputs, pack_lengths, full_in, full_dt, full_out, small_parts, block_rows):
    gain_in, gain_out, conv_taps, conv_bias, dt_bias, a_log, d_skip = small_parts
    row_count = inputs.shape[0]
    inner_width = H * P_SIZE
    seg_ends = jnp.cumsum(pack_lengths).astype(jnp.int32)
    positions = jnp.arange(row_count, dtype=jnp.int32)
    segments = segment_at(positions, seg_ends)
    live_rows = (segments < 3).astype(jnp.float32)
    same_masks = jnp.stack([(segment_at(positions - offset, seg_ends) == segments).astype(jnp.float32) for offset in range(CONV)], 0)
    normed = low(inputs * lax.rsqrt(lax.optimization_barrier(jnp.mean(inputs * inputs, axis=1, keepdims=True)) + NORM_EPS) * gain_in[None, :])
    projected = low_back(jnp.dot(normed, full_in, precision=PRECISE))
    gate_z = projected[:, :inner_width]
    conv_input = low(projected[:, inner_width:])
    dt_raw = low_back(jnp.dot(normed, full_dt, precision=PRECISE))
    extended = jnp.concatenate([jnp.zeros((CONV - 1, conv_input.shape[1]), jnp.float32), conv_input], 0)
    heads_x, state_b, state_c, step_dt, log_decay = conv_part(extended, dt_raw, conv_taps, conv_bias, dt_bias, a_log, same_masks)
    scanned, final_state = local_scan(heads_x, state_b, state_c, step_dt, log_decay, segments, jnp.int32(-1), block_rows)
    mixed = scanned + d_skip[None, :, None] * heads_x
    gated = mixed.reshape(row_count, inner_width) * jax.nn.silu(gate_z)
    out_normed = low(gated * lax.rsqrt(lax.optimization_barrier(jnp.mean(gated * gated, axis=1, keepdims=True)) + NORM_EPS) * gain_out[None, :])
    branch = low_back(jnp.dot(out_normed, full_out, precision=PRECISE))
    return inputs + live_rows[:, None] * branch

def adam_update(weight, gradient, moment_one, moment_two, learn_rate, decay_rate):
    moment_one = BETA_ONE * moment_one + (1.0 - BETA_ONE) * gradient
    moment_two = BETA_TWO * moment_two + (1.0 - BETA_TWO) * gradient * gradient
    scaled = moment_one / (1.0 - BETA_ONE ** STEP) / (jnp.sqrt(moment_two / (1.0 - BETA_TWO ** STEP)) + ADAM_EPS)
    return (weight - learn_rate * (scaled + decay_rate * weight), moment_one, moment_two)

def reference(tokens, cotangent, lengths, w_in, w_dt, w_out, small, first_in, first_dt, first_out, first_small, second_in, second_dt, second_out, second_small):
    block_rows = math.gcd(TOK_DEV, 256)
    pack_rows = N_REP * TOK_DEV

    def forward(inputs, weight_in, weight_dt, weight_out, small_vector):
        full_in = low(weight_in)
        full_dt = low(weight_dt)
        full_out = low(weight_out)
        small_parts = unpack_small(low(small_vector))

        def per_pack(packed):
            return pack_forward(packed[0], packed[1], full_in, full_dt, full_out, small_parts, block_rows)
        outputs = lax.map(jax.checkpoint(per_pack), (inputs.reshape(N_FSDP, pack_rows, D), lengths))
        return outputs.reshape(TOKENS, D)
    block_out, pullback = jax.vjp(forward, tokens.astype(jnp.float32), w_in, w_dt, w_out, small)
    input_grad, grad_in, grad_dt, grad_out, grad_small = pullback(cotangent.astype(jnp.float32))
    new_in, new_first_in, new_second_in = adam_update(w_in, grad_in, first_in, second_in, RATE_MATRIX, WEIGHT_DECAY)
    new_dt, new_first_dt, new_second_dt = adam_update(w_dt, grad_dt, first_dt, second_dt, RATE_MATRIX, WEIGHT_DECAY)
    new_out, new_first_out, new_second_out = adam_update(w_out, grad_out, first_out, second_out, RATE_MATRIX, WEIGHT_DECAY)
    new_small, new_first_small, new_second_small = adam_update(small, grad_small, first_small, second_small, RATE_SMALL, 0.0)
    return (block_out, input_grad, grad_in, grad_dt, grad_out, grad_small, new_first_in, new_first_dt, new_first_out, new_first_small, new_second_in, new_second_dt, new_second_out, new_second_small, new_in, new_dt, new_out, new_small)
```

```python
import jax
import jax.numpy as jnp
from jax import lax
from jax.experimental import pallas as pl
from jax.experimental.pallas import tpu as pltpu
from jax.sharding import PartitionSpec as P

D = 1536
H = 48
P_SIZE = 64
N = 128
CONV = 4
STEP = 10
DI = 3072
CHANNELS = DI + 2 * N
SMALL = 21392
N_FSDP = 16
N_REP = 8
ROWS = 256
PACK = 2048
OWN = DI // N_REP
OWN_H = H // N_REP
OWN_BC = 2 * N // N_REP
SHARD_IN = D // N_FSDP
SHARD_OUT = DI // N_FSDP
SHARD_SMALL = SMALL // N_FSDP
TAIL = 512
WIDE = 384
CHUNK = 128
CHUNKS = PACK // CHUNK
VMEM_LIMIT = 40 * 1024 * 1024

NORM_EPS = 1e-05
BETA_ONE = 0.9
BETA_TWO = 0.999
ADAM_EPS = 1e-08
WEIGHT_DECAY = 0.1
RATE_MATRIX = 0.04
RATE_SMALL = 0.4
PRECISE = lax.Precision.HIGHEST
BF16 = jnp.bfloat16
F32 = jnp.float32


def move(value, target):
    pairs = []
    for f in range(N_FSDP):
        for r in range(N_REP):
            yh, z, c, x, yl = target(f // 8, (f // 2) % 4, f % 2, r // 2, r % 2)
            pairs.append((f * N_REP + r, ((yh % 2) * 8 + (z % 4) * 2 + c % 2) * N_REP + (x % 4) * 2 + yl % 2))
    return lax.ppermute(value, ("fsdp", "rep"), pairs)


def along_x(steps):
    return lambda yh, z, c, x, yl: (yh, z, c, x + steps, yl)


def along_z(steps):
    return lambda yh, z, c, x, yl: (yh, z + steps, c, x, yl)


def swap_y(yh, z, c, x, yl):
    return (yh, z, c, x, yl + 1)


def swap_y_hi(yh, z, c, x, yl):
    return (yh + 1, z, c, x, yl)


def swap_core(yh, z, c, x, yl):
    return (yh, z, c + 1, x, yl)


class Place:
    def __init__(self):
        f = lax.axis_index("fsdp")
        r = lax.axis_index("rep")
        self.f, self.r = f, r
        self.yh, self.z, self.c = f // 8, (f // 2) % 4, f % 2
        self.x, self.yl = r // 2, r % 2


def at(value, index, axis=0):
    return lax.dynamic_index_in_dim(value, index, axis, keepdims=False)


def gather_rep_wide(value, place):
    rows = value.shape[0]
    half = rows // 2
    from_left = move(value, along_x(1))
    from_right = move(value, along_x(-1))
    partner = move(value, swap_y)
    far_top = move(from_left[:half], along_x(1))
    far_low = move(from_right[half:], along_x(-1))
    partner_left = move(from_left, swap_y)
    partner_right_top = move(partner[:half], along_x(-1))
    partner_right_low = move(from_right[half:], swap_y)
    partner_far_top = move(partner_left[:half], along_x(1))
    partner_far_low = move(partner_right_low, along_x(-1))
    pieces = (
        (value, 0, 0, 0),
        (from_left, 3, 0, 0),
        (from_right, 1, 0, 0),
        (partner, 0, 1, 0),
        (far_top, 2, 0, 0),
        (far_low, 2, 0, half),
        (partner_left, 3, 1, 0),
        (partner_right_top, 1, 1, 0),
        (partner_right_low, 1, 1, half),
        (partner_far_top, 2, 1, 0),
        (partner_far_low, 2, 1, half),
    )
    out = jnp.zeros((N_REP * rows, value.shape[1]), value.dtype)
    for piece, dx, dy, start in pieces:
        offset = (((place.x + dx) % 4) * 2 + (place.yl + dy) % 2) * rows + start
        out = lax.dynamic_update_slice(out, piece, (offset, jnp.int32(0)))
    return out


def both(mine, other, second):
    first = jnp.where(second == 0, mine, other)
    last = jnp.where(second == 0, other, mine)
    return jnp.stack([first, last], 0)


def put(out, piece, axis, index):
    starts = [jnp.int32(0)] * out.ndim
    starts[axis] = jnp.int32(index)
    return lax.dynamic_update_slice(out, jnp.expand_dims(piece, axis), tuple(starts))


def gather_ring(pair, step, here, axis=0):
    left = move(pair, step(1))
    right = move(pair, step(-1))
    half = pair.shape[0] // 2
    far = jnp.concatenate([move(left[:half], step(1)), move(right[half:], step(-1))], 0)
    shape = pair.shape[:axis] + (4,) + pair.shape[axis:]
    out = jnp.zeros(shape, pair.dtype)
    for piece, offset in ((pair, 0), (right, 1), (left, 3), (far, 2)):
        out = put(out, piece, axis, (here + offset) % 4)
    return out


def gather_rep(value, place):
    pair = both(value, move(value, swap_y), place.yl)
    out = gather_ring(pair, along_x, place.x)
    return out.reshape((N_REP,) + value.shape)


def gather_halves(halves, place):
    mine = jnp.where(place.c == 0, halves[0], halves[1])
    sent = jnp.where(place.c == 0, halves[1], halves[0])
    cores = both(mine, move(sent, swap_core), place.c)
    pair = both(cores, move(cores, swap_y_hi), place.yh)
    ring = gather_ring(pair, along_z, place.z, 1).reshape((N_FSDP,) + mine.shape)
    return ring, move(ring, swap_core)


def sum_rep(value):
    steps = [move(value, along_x(step)) for step in (1, 3, 2)]
    value = value + steps[0] + steps[1] + steps[2]
    return value + move(value, swap_y)


def sum_all(value):
    value = sum_rep(value)
    steps = [move(value, along_z(step)) for step in (1, 3, 2)]
    value = value + steps[0] + steps[1] + steps[2]
    value = value + move(value, swap_core)
    return value + move(value, swap_y_hi)


def with_rows(block, extra):
    width = block.shape[-1]
    flat = block.reshape(-1, width)
    return flat if extra is None else jnp.concatenate([flat, extra], 0)


def scatter_fsdp(value, extra, place):
    count, width = value.shape[1:]
    split = value.reshape(2, 4, 2, count, width)
    more = 0 if extra is None else extra.shape[0]

    def receive(block, target, base, add_to):
        got = move(with_rows(block, base), target)
        rows = got.shape[0] - more
        return got[:rows].reshape(add_to.shape), got[rows:]

    total = at(split, place.c, 2)
    got, got_extra = receive(at(split, 1 - place.c, 2), swap_core, extra, total)
    total = total + got
    if more:
        extra = extra + got_extra
    z_sum = at(total, place.z, 1)
    found = [receive(at(total, (place.z + step) % 4, 1), along_z(step), extra, z_sum) for step in (1, 3, 2)]
    z_sum = z_sum + found[0][0] + found[1][0] + found[2][0]
    if more:
        extra = extra + found[0][1] + found[1][1] + found[2][1]
    mine = at(z_sum, place.yh)
    got, got_extra = receive(at(z_sum, 1 - place.yh), swap_y_hi, extra, mine)
    if more:
        extra = extra + got_extra
    return mine + got, extra


def rows_to_owners(value, place):
    width = value.shape[1]
    split = value.reshape(4, 2, ROWS, width)
    kept = []
    sent = []
    for step in (0, 1, 3, 2):
        block = at(split, (place.x + step) % 4)
        got = block if step == 0 else move(block, along_x(step))
        kept.append(at(got, place.yl))
        sent.append(at(got, 1 - place.yl))
    other = move(jnp.stack(sent, 0), swap_y)
    out = jnp.zeros((4, 2, ROWS, width), value.dtype)
    zero = jnp.int32(0)
    for k, step in enumerate((0, 1, 3, 2)):
        source = (place.x - step) % 4
        out = lax.dynamic_update_slice(out, kept[k][None, None], (source, place.yl, zero, zero))
        out = lax.dynamic_update_slice(out, other[k][None, None], (source, 1 - place.yl, zero, zero))
    return out.reshape(N_REP, ROWS, width)


def sum_to_owners(value, place):
    count = value.shape[0] // N_REP
    split = value.reshape(4, 2, count, value.shape[1])
    total = at(split, place.x)
    for step in (1, 3, 2):
        total = total + move(at(split, (place.x + step) % 4), along_x(step))
    return at(total, place.yl) + move(at(total, 1 - place.yl), swap_y)


def adam_update(weight, gradient, moment_one, moment_two, learn_rate, decay_rate):
    moment_one = BETA_ONE * moment_one + (1.0 - BETA_ONE) * gradient
    moment_two = BETA_TWO * moment_two + (1.0 - BETA_TWO) * gradient * gradient
    scaled = (
        moment_one
        / (1.0 - BETA_ONE**STEP)
        / (jnp.sqrt(moment_two / (1.0 - BETA_TWO**STEP)) + ADAM_EPS)
    )
    return (weight - learn_rate * (scaled + decay_rate * weight), moment_one, moment_two)


def contract_rows(left_side, right_side):
    return lax.dot_general(
        left_side, right_side, (((0,), (0,)), ((), ())), preferred_element_type=F32
    )


def contract_cols(left_side, right_side):
    return lax.dot_general(
        left_side, right_side, (((1,), (1,)), ((), ())), preferred_element_type=F32
    )


def matmul(left_side, right_side):
    return jnp.dot(left_side, right_side, preferred_element_type=F32)


def segment_at(positions, seg_ends):
    counted = jnp.sum((positions[:, None] >= seg_ends[None, :]).astype(jnp.int32), axis=1)
    return jnp.where(positions < 0, jnp.int32(-1), counted)


def split_two(value):
    high = value.astype(BF16)
    return high, (value - high.astype(F32)).astype(BF16)


def split_three(value):
    high = value.astype(BF16)
    rest = value - high.astype(F32)
    middle = rest.astype(BF16)
    return high, middle, (rest - middle.astype(F32)).astype(BF16)


def product(left, right, left_dim, right_dim):
    return lax.dot_general(
        left, right, (((left_dim,), (right_dim,)), ((), ())), preferred_element_type=F32
    )


def joined_product(left_parts, right_parts, left_dim=1, right_dim=0):
    left_high, left_low = left_parts
    right_high, right_low = right_parts
    return product(
        jnp.concatenate([left_high, left_high, left_low], left_dim),
        jnp.concatenate([right_high, right_low, right_high], right_dim),
        left_dim,
        right_dim,
    )


def precise_product(left, right, left_dim=1, right_dim=0):
    return joined_product(split_two(left), split_two(right), left_dim, right_dim)


def ones_product(ones, value):
    return product(jnp.concatenate([ones] * 3, 1), jnp.concatenate(split_three(value), 0), 1, 0)


def spread(per_head, lane):
    return jnp.concatenate(
        [
            jnp.where(lane < P_SIZE, per_head[:, 2 * k : 2 * k + 1], per_head[:, 2 * k + 1 : 2 * k + 2])
            for k in range(OWN_H // 2)
        ],
        1,
    )


def head_sums(value):
    column = lax.broadcasted_iota(jnp.int32, (OWN, N), 0)
    head = lax.broadcasted_iota(jnp.int32, (OWN, N), 1)
    members = ((column >= head * P_SIZE) & (column < (head + 1) * P_SIZE)).astype(F32).astype(BF16)
    high, low = split_two(value)
    return product(jnp.concatenate([high, low], 1), jnp.concatenate([members, members], 0), 1, 0)


def two_heads(pair, lane):
    zero = jnp.zeros_like(pair)
    return jnp.concatenate([jnp.where(lane < P_SIZE, pair, zero), jnp.where(lane < P_SIZE, zero, pair)], 0)


def chunk_facts(ends, chunk, dt_pre, par):
    column = lax.broadcasted_iota(jnp.int32, (CHUNK, 1), 0) + chunk * CHUNK
    row = lax.broadcasted_iota(jnp.int32, (1, CHUNK), 1) + chunk * CHUNK

    def segment(position):
        counted = jnp.zeros_like(position)
        for k in range(3):
            counted = counted + (position >= ends[k]).astype(jnp.int32)
        return jnp.where(position < 0, -1, counted)

    def one_segment(position):
        counted = jnp.int32(0)
        for k in range(3):
            counted = counted + (position >= ends[k]).astype(jnp.int32)
        return jnp.where(position < 0, -1, counted)

    here_column, here_row = segment(column), segment(row)
    prior = one_segment(chunk * CHUNK - 1)
    last = one_segment(chunk * CHUNK + CHUNK - 1)
    lane = lax.broadcasted_iota(jnp.int32, (CHUNK, N), 1)
    shifted = dt_pre + par[6:7, :N]
    soft = jnp.maximum(shifted, 0.0) + jnp.log1p(jnp.exp(-jnp.abs(shifted)))
    step = jnp.where(lane < OWN_H, soft, 0.0)
    decay = step * par[7:8, :N]
    tri_row = lax.broadcasted_iota(jnp.int32, (CHUNK, CHUNK), 0)
    tri_column = lax.broadcasted_iota(jnp.int32, (CHUNK, CHUNK), 1)
    lower = (tri_row >= tri_column).astype(F32).astype(BF16)
    upper = (tri_row <= tri_column).astype(F32).astype(BF16)
    total = ones_product(lower, decay)
    entering = (here_column == prior).astype(F32) * jnp.exp(total)
    end = total[CHUNK - 1 : CHUNK]
    leaving = (here_column == last).astype(F32) * jnp.exp(jnp.minimum(end - total, 0.0))
    passing = jnp.where(last == prior, 1.0, 0.0) * jnp.exp(end)
    return dict(
        column=column,
        segment=segment,
        here_column=here_column,
        here_row=here_row,
        lane=lane,
        shifted=shifted,
        step=step,
        decay=decay,
        total=total,
        entering=entering,
        leaving=leaving,
        passing=passing,
        tri_row=tri_row,
        tri_column=tri_column,
        upper=upper,
    )


def forward_kernel(ends, proj, par, pre_out, mixed_out, state_out, extended, state):
    chunk = pl.program_id(0)

    @pl.when(chunk == 0)
    def _():
        extended[0:8, :] = jnp.zeros((8, 640), F32)
        state[...] = jnp.zeros_like(state)

    facts = chunk_facts(ends, chunk, proj[:, 1024:1152], par)
    lane = facts["lane"]
    conv = proj[:, OWN:1024].astype(BF16).astype(F32)
    extended[8 : 8 + CHUNK, :] = conv
    pre = par[4:5] + par[3:4] * conv
    for back in range(1, CONV):
        same = (facts["segment"](facts["column"] - back) == facts["here_column"]).astype(F32)
        pre = pre + par[3 - back : 4 - back] * (extended[8 - back : 8 - back + CHUNK, :] * same)
    extended[0:8, :] = extended[CHUNK : CHUNK + 8, :]
    pre_out[...] = pre
    act = pre * jax.nn.sigmoid(pre)
    own_x, state_b, state_c = act[:, :OWN], act[:, OWN : OWN + N], act[:, OWN + N :]
    stepped = own_x * spread(facts["step"], lane)
    b_parts, c_parts = split_two(state_b), split_two(state_c)
    inside = (facts["tri_row"] >= facts["tri_column"]) & (facts["here_column"] == facts["here_row"])
    scores = jnp.where(inside, joined_product(c_parts, b_parts, 1, 1), 0.0)
    total_rows = facts["total"].T
    state_in = state[...]
    state_out[...] = state_in
    outs = []
    for pair in range(OWN_H // 2):
        mixing = []
        for head in (2 * pair, 2 * pair + 1):
            span = facts["total"][:, head : head + 1] - total_rows[head : head + 1, :]
            mixing.append(jnp.exp(jnp.minimum(span, 0.0)) * scores)
        inner = two_heads(stepped[:, pair * N : pair * N + N], lane)
        outs.append(precise_product(jnp.concatenate(mixing, 1), inner))
    scanned = jnp.concatenate(outs, 1) + spread(facts["entering"], lane) * joined_product(
        c_parts, split_two(state_in)
    )
    state[...] = spread(facts["passing"], lane[:1]) * state_in + precise_product(
        state_b.T, stepped * spread(facts["leaving"], lane)
    )
    mixed_out[...] = scanned + par[5:6, :OWN] * own_x


def run_forward(ends, proj, par):
    chunked = lambda width: pl.BlockSpec((CHUNK, width), lambda i: (i, 0))
    return pl.pallas_call(
        forward_kernel,
        grid=(CHUNKS,),
        in_specs=[
            pl.BlockSpec(memory_space=pltpu.SMEM),
            chunked(1152),
            pl.BlockSpec((16, 640), lambda i: (0, 0)),
        ],
        out_specs=[chunked(640), chunked(OWN), pl.BlockSpec((N, OWN), lambda i: (i, 0))],
        out_shape=[
            jax.ShapeDtypeStruct((PACK, 640), F32),
            jax.ShapeDtypeStruct((PACK, OWN), F32),
            jax.ShapeDtypeStruct((CHUNKS * N, OWN), F32),
        ],
        scratch_shapes=[pltpu.VMEM((CHUNK + 8, 640), F32), pltpu.VMEM((N, OWN), F32)],
        compiler_params=pltpu.CompilerParams(
            dimension_semantics=("arbitrary",), vmem_limit_bytes=VMEM_LIMIT
        ),
        cost_estimate=pl.CostEstimate(flops=8_000_000_000, bytes_accessed=24_000_000, transcendentals=3_000_000),
        name="scan_forward",
    )(ends, proj, par)


def backward_kernel(
    ends, conv_in, dt_in, pre_in, mixed_in, grad_mixed, state_all, par,
    grad_x, grad_dt, grad_bc, sums, head_acc,
    carried, extended, end_dot,
):
    step_index = pl.program_id(0)
    chunk = CHUNKS - 1 - step_index

    @pl.when(step_index == 0)
    def _():
        carried[...] = jnp.zeros_like(carried)
        extended[CHUNK : CHUNK + 8, :] = jnp.zeros((8, OWN), F32)
        end_dot[...] = jnp.zeros_like(end_dot)
        sums[...] = jnp.zeros_like(sums)
        head_acc[...] = jnp.zeros_like(head_acc)

    facts = chunk_facts(ends, chunk, dt_in[...], par)
    lane = facts["lane"]
    pre = pre_in[...]
    sig = jax.nn.sigmoid(pre)
    act = pre * sig
    own_x, state_b, state_c = act[:, :OWN], act[:, OWN : OWN + N], act[:, OWN + N :]
    step = facts["step"]
    step_wide = spread(step, lane)
    stepped = own_x * step_wide
    skip = par[5:6, :OWN]
    scanned = mixed_in[...] - skip * own_x
    grad_m = grad_mixed[...]
    sums[6:7] += jnp.sum(grad_m * own_x, 0, keepdims=True)

    b_parts, c_parts = split_two(state_b), split_two(state_c)
    inside = (facts["tri_row"] <= facts["tri_column"]) & (facts["here_column"] == facts["here_row"])
    scores = jnp.where(inside, joined_product(b_parts, c_parts, 1, 1), 0.0)
    total_rows = facts["total"].T
    grad_scores = jnp.zeros((CHUNK, CHUNK), F32)
    grad_stepped = []
    for pair in range(OWN_H // 2):
        columns = slice(pair * N, pair * N + N)
        grad_pair = grad_m[:, columns]
        high, low = split_two(grad_pair)
        stepped_parts = split_two(two_heads(stepped[:, columns], lane))
        grad_mixing = joined_product(stepped_parts, (high, low), 1, 1)
        mixing = []
        for k in range(2):
            head = 2 * pair + k
            span = total_rows[head : head + 1, :] - facts["total"][:, head : head + 1]
            decays = jnp.exp(jnp.minimum(span, 0.0))
            mixing.append(decays * scores)
            grad_scores = grad_scores + decays * grad_mixing[k * CHUNK : (k + 1) * CHUNK]
        grad_stepped.append(
            joined_product(
                split_two(jnp.concatenate(mixing, 1)), (two_heads(high, lane), two_heads(low, lane))
            )
        )
    grad_scores = jnp.where(inside, grad_scores, 0.0)
    carry = carried[...]
    carry_parts = split_two(carry)
    leaving = spread(facts["leaving"], lane)
    grad_stepped = jnp.concatenate(grad_stepped, 1) + leaving * joined_product(b_parts, carry_parts)
    state_in = state_all[...]
    entered = spread(facts["entering"], lane) * grad_m
    entered_parts = split_two(entered)
    grad_b = precise_product(grad_scores, state_c) + joined_product(
        split_two(leaving * stepped), carry_parts, 1, 1
    )
    grad_c = precise_product(grad_scores.T, state_b) + joined_product(
        entered_parts, split_two(state_in), 1, 1
    )
    grad_bc[0:N, :] = grad_b.T
    grad_bc[N:, :] = grad_c.T
    new_carry = spread(facts["passing"], lane[:1]) * carry + joined_product(
        split_two(state_c.T), entered_parts
    )
    carried[...] = new_carry

    grad_step = head_sums(own_x * grad_stepped)
    last_row = lax.broadcasted_iota(jnp.int32, (CHUNK, N), 0) == CHUNK - 1
    grad_total = head_sums(grad_m * scanned) - step * grad_step
    grad_total = grad_total + jnp.where(last_row, end_dot[0:1, :], 0.0)
    grad_decay = ones_product(facts["upper"], grad_total)
    end_dot[...] = head_sums(
        jnp.broadcast_to(jnp.sum(new_carry * state_in, 0, keepdims=True), (8, OWN))
    )
    grad_pre_dt = (grad_step + grad_decay * par[7:8, :N]) * jax.nn.sigmoid(facts["shifted"])
    grad_pre_dt = jnp.where(lane < OWN_H, grad_pre_dt, 0.0)
    grad_dt[...] = grad_pre_dt.astype(BF16)
    head_acc[0:1] += jnp.sum(grad_pre_dt, 0, keepdims=True)
    head_acc[1:2] += jnp.sum(grad_decay * facts["decay"], 0, keepdims=True)

    sig_x, pre_x = sig[:, :OWN], pre[:, :OWN]
    grad_pre = (step_wide * grad_stepped + skip * grad_m) * (sig_x * (1.0 + pre_x * (1.0 - sig_x)))
    extended[0:CHUNK, :] = grad_pre
    conv = conv_in[...].astype(BF16).astype(F32)
    sums[5:6] += jnp.sum(grad_pre, 0, keepdims=True)
    sums[4:5] += jnp.sum(conv * grad_pre, 0, keepdims=True)
    grad_conv = par[3:4, :OWN] * grad_pre
    for ahead in range(1, CONV):
        same = (facts["segment"](facts["column"] + ahead) == facts["here_column"]).astype(F32)
        later = extended[ahead : ahead + CHUNK, :] * same
        sums[4 - ahead : 5 - ahead] += jnp.sum(conv * later, 0, keepdims=True)
        grad_conv = grad_conv + par[3 - ahead : 4 - ahead, :OWN] * later
    extended[CHUNK : CHUNK + 8, :] = extended[0:8, :]
    grad_x[...] = grad_conv.astype(BF16)


def run_backward(ends, proj, pre, mixed, grad_mixed, states, par):
    back = lambda i: (CHUNKS - 1 - i, 0)
    chunked = lambda width: pl.BlockSpec((CHUNK, width), back)
    fixed = lambda shape: pl.BlockSpec(shape, lambda i: (0, 0))
    return pl.pallas_call(
        backward_kernel,
        grid=(CHUNKS,),
        in_specs=[
            pl.BlockSpec(memory_space=pltpu.SMEM),
            pl.BlockSpec((CHUNK, OWN), lambda i: (CHUNKS - 1 - i, 1)),
            pl.BlockSpec((CHUNK, N), lambda i: (CHUNKS - 1 - i, 8)),
            chunked(640),
            chunked(OWN),
            chunked(OWN),
            pl.BlockSpec((N, OWN), back),
            fixed((16, 640)),
        ],
        out_specs=[
            chunked(OWN),
            chunked(N),
            pl.BlockSpec((2 * N, CHUNK), lambda i: (0, CHUNKS - 1 - i)),
            fixed((8, OWN)),
            fixed((8, N)),
        ],
        out_shape=[
            jax.ShapeDtypeStruct((PACK, OWN), BF16),
            jax.ShapeDtypeStruct((PACK, N), BF16),
            jax.ShapeDtypeStruct((2 * N, PACK), F32),
            jax.ShapeDtypeStruct((8, OWN), F32),
            jax.ShapeDtypeStruct((8, N), F32),
        ],
        scratch_shapes=[
            pltpu.VMEM((N, OWN), F32),
            pltpu.VMEM((CHUNK + 8, OWN), F32),
            pltpu.VMEM((8, N), F32),
        ],
        compiler_params=pltpu.CompilerParams(
            dimension_semantics=("arbitrary",), vmem_limit_bytes=VMEM_LIMIT
        ),
        cost_estimate=pl.CostEstimate(flops=20_000_000_000, bytes_accessed=32_000_000, transcendentals=6_000_000),
        name="scan_backward",
    )(ends, proj, proj, pre, mixed, grad_mixed, states, par)


def project_kernel(tokens, gain, w_z, w_x, w_rest, normed_out, proj):
    values = tokens[...].astype(F32)
    scale = lax.rsqrt(jnp.mean(values * values, axis=1, keepdims=True) + NORM_EPS)
    normed = (values * scale * gain[...]).astype(BF16)
    normed_out[...] = normed
    proj[:, :WIDE] = matmul(normed, w_z[...])
    proj[:, WIDE : 2 * WIDE] = matmul(normed, w_x[...])
    proj[:, 2 * WIDE :] = matmul(normed, w_rest[...])


def run_project(tokens, gain, w_z, w_x, w_rest):
    rows = lambda width: pl.BlockSpec((ROWS, width), lambda i: (i, 0))
    fixed = lambda shape: pl.BlockSpec(shape, lambda i: (0, 0))
    return pl.pallas_call(
        project_kernel,
        grid=(PACK // ROWS,),
        in_specs=[rows(D), fixed((1, D)), fixed((D, WIDE)), fixed((D, WIDE)), fixed((D, WIDE))],
        out_specs=[rows(D), rows(3 * WIDE)],
        out_shape=[jax.ShapeDtypeStruct((PACK, D), BF16), jax.ShapeDtypeStruct((PACK, 3 * WIDE), F32)],
        compiler_params=pltpu.CompilerParams(
            dimension_semantics=("arbitrary",), vmem_limit_bytes=VMEM_LIMIT
        ),
        cost_estimate=pl.CostEstimate(flops=7_250_000_000, bytes_accessed=26_000_000, transcendentals=0),
        name="project",
    )(tokens, gain, w_z, w_x, w_rest)


def column_sums(value):
    ones = jnp.ones((8, value.shape[1]), BF16)
    return product(jnp.concatenate([ones] * 3, 1), jnp.concatenate(split_three(value), 1), 1, 1)


def out_grad_kernel(grad_branch, w_out, mixed, gate_in, gain, grad_out, sums):
    total = jnp.zeros((ROWS, WIDE), F32)
    for k in range(4):
        total = total + product(
            grad_branch[:, k * WIDE : (k + 1) * WIDE], w_out[k * WIDE : (k + 1) * WIDE, :], 1, 1
        )
    grad_out[...] = total
    gate = gate_in[...]
    gated = mixed[...] * (gate * jax.nn.sigmoid(gate))
    row = lax.broadcasted_iota(jnp.int32, (8, ROWS), 0)
    sums[...] = jnp.where(row == 0, column_sums(gated * gated), column_sums(total * gain[...] * gated))


def run_out_grad(grad_branch, w_out, mixed, proj, gain):
    rows = lambda width: pl.BlockSpec((ROWS, width), lambda i: (i, 0))
    fixed = lambda shape: pl.BlockSpec(shape, lambda i: (0, 0))
    return pl.pallas_call(
        out_grad_kernel,
        grid=(PACK // ROWS,),
        in_specs=[rows(D), fixed((D, WIDE)), rows(OWN), rows(OWN), fixed((1, OWN))],
        out_specs=[rows(OWN), pl.BlockSpec((8, ROWS), lambda i: (0, i))],
        out_shape=[jax.ShapeDtypeStruct((PACK, OWN), F32), jax.ShapeDtypeStruct((8, PACK), F32)],
        compiler_params=pltpu.CompilerParams(
            dimension_semantics=("arbitrary",), vmem_limit_bytes=VMEM_LIMIT
        ),
        cost_estimate=pl.CostEstimate(flops=2_420_000_000, bytes_accessed=17_000_000, transcendentals=800_000),
        name="out_grad",
    )(grad_branch, w_out, mixed, proj, gain)


def gate_kernel(
    grad_out, mixed_in, gate_in, sums, gain, grad_branch, normed,
    low_out, grad_mixed, grad_weights, grad_gain,
):
    step = pl.program_id(0)
    rows = grad_out.shape[0]
    mixed, gate, grad_o = mixed_in[...], gate_in[...], grad_out[...]
    stats = jnp.concatenate([sums[...], jnp.zeros((N - 8, rows), F32)], 0).T
    out_scale = lax.rsqrt(stats[:, 0:1] * (1.0 / DI) + NORM_EPS)
    pull = out_scale * out_scale * out_scale * (stats[:, 1:2] * (1.0 / DI))
    gate_sig = jax.nn.sigmoid(gate)
    silu = gate * gate_sig
    gated = mixed * silu
    unit = gated * out_scale
    low = (unit * gain[...]).astype(BF16)
    grad_gated = out_scale * (grad_o * gain[...]) - gated * pull
    grad_mixed[...] = grad_gated * silu
    grad_z = (grad_gated * mixed * (gate_sig * (1.0 + gate * (1.0 - gate_sig)))).astype(BF16)
    low_out[:, :OWN] = low
    low_out[:, OWN:] = grad_z
    gain_part = jnp.sum(grad_o * unit, 0, keepdims=True)

    @pl.when(step == 0)
    def _():
        grad_gain[...] = jnp.zeros_like(grad_gain)
        grad_weights[...] = jnp.zeros_like(grad_weights)

    grad_gain[0:1] += gain_part
    for k in range(4):
        part = product(low, grad_branch[:, k * WIDE : (k + 1) * WIDE], 0, 0)
        for m in range(4):
            grad_weights[4 * k + m, :SHARD_IN] += part[m * SHARD_IN : (m + 1) * SHARD_IN]
    part = product(normed[...], grad_z, 0, 0)
    for f in range(N_FSDP):
        grad_weights[f, SHARD_IN:] += part[f * SHARD_IN : (f + 1) * SHARD_IN]


def run_gate(grad_out, mixed, proj, sums, gain, grad_branch, normed):
    count = 256
    rows = lambda width: pl.BlockSpec((count, width), lambda i: (i, 0))
    fixed = lambda shape: pl.BlockSpec(shape, lambda i: (0,) * len(shape))
    return pl.pallas_call(
        gate_kernel,
        grid=(PACK // count,),
        in_specs=[
            rows(OWN),
            rows(OWN),
            rows(OWN),
            pl.BlockSpec((8, count), lambda i: (0, i)),
            fixed((1, OWN)),
            rows(D),
            rows(D),
        ],
        out_specs=[rows(2 * OWN), rows(OWN), fixed((N_FSDP, 2 * SHARD_IN, WIDE)), fixed((8, OWN))],
        out_shape=[
            jax.ShapeDtypeStruct((PACK, 2 * OWN), BF16),
            jax.ShapeDtypeStruct((PACK, OWN), F32),
            jax.ShapeDtypeStruct((N_FSDP, 2 * SHARD_IN, WIDE), F32),
            jax.ShapeDtypeStruct((8, OWN), F32),
        ],
        compiler_params=pltpu.CompilerParams(
            dimension_semantics=("arbitrary",), vmem_limit_bytes=VMEM_LIMIT
        ),
        cost_estimate=pl.CostEstimate(flops=4_840_000_000, bytes_accessed=34_000_000, transcendentals=800_000),
        name="gate_backward",
    )(grad_out, mixed, proj, sums, gain, grad_branch, normed)


def body(
    tokens,
    cotangent,
    lengths,
    w_in,
    w_dt,
    w_out,
    small,
    first_in,
    first_dt,
    first_out,
    first_small,
    second_in,
    second_dt,
    second_out,
    second_small,
):
    place = Place()
    r = place.r
    pack_lengths = lax.dynamic_slice_in_dim(lengths, place.f, 1, 0)[0]
    seg_ends = jnp.cumsum(pack_lengths)
    own_positions = r * ROWS + jnp.arange(ROWS, dtype=jnp.int32)
    own_live = (segment_at(own_positions, seg_ends) < 3).astype(F32)

    full_tokens = gather_rep_wide(tokens, place)
    own_branch = (cotangent.astype(F32) * own_live[:, None]).astype(BF16)
    own_branch, _ = lax.optimization_barrier((own_branch, full_tokens))
    grad_branch = gather_rep_wide(own_branch, place)

    in_low = w_in.astype(BF16)
    out_low_shard = w_out.astype(BF16)
    dt_low = w_dt.astype(BF16)
    small_rows = jnp.pad(small.astype(BF16), (0, 4 * WIDE - SHARD_SMALL)).reshape(4, WIDE)
    small_rows = jnp.concatenate([small_rows, jnp.zeros((12, WIDE), BF16)], 0)
    zero = jnp.int32(0)
    out_piece = lax.dynamic_slice(
        out_low_shard, (SHARD_IN * (place.x // 2), WIDE * ((place.x % 2) * 2 + place.yl)), (SHARD_IN, WIDE)
    )
    out_piece = move(
        out_piece, lambda yh, z, c, x, yl: (x % 2, yl * 2 + c, x // 2, yh * 2 + z // 2, z % 2)
    )
    rest = jnp.concatenate(
        [
            in_low[:, 2 * DI :],
            lax.dynamic_slice_in_dim(dt_low, r * OWN_H, OWN_H, 1),
            jnp.zeros((SHARD_IN, 2), BF16),
            dt_low,
            jnp.zeros((SHARD_IN, N - 8 - H), BF16),
        ],
        1,
    )
    first_halves = [
        jnp.concatenate([lax.dynamic_slice_in_dim(in_low, DI + r * OWN, OWN, 1), small_rows], 0),
        jnp.concatenate([rest, small_rows], 0),
    ]
    first_mine, first_other = gather_halves(first_halves, place)
    second_mine, second_other = gather_halves(
        [lax.dynamic_slice_in_dim(in_low, r * OWN, OWN, 1), out_piece], place
    )
    vector = first_mine[:, SHARD_IN : SHARD_IN + 4].reshape(N_FSDP, 4 * WIDE)[:, :SHARD_SMALL]
    vector = vector.reshape(-1).astype(F32)
    first_mine, first_other = first_mine[:, :SHARD_IN], first_other[:, :SHARD_IN]

    def ordered(mine, other):
        return (
            jnp.where(place.c == 0, mine, other).reshape(D, WIDE),
            jnp.where(place.c == 0, other, mine).reshape(D, WIDE),
        )

    slice_x, slice_rest = ordered(first_mine, first_other)
    slice_z, slice_out = ordered(second_mine, second_other)
    full_dt = slice_rest[:, 2 * N + 8 : 2 * N + 8 + H]

    in_low, _ = lax.optimization_barrier((in_low, second_other))
    full_in = lax.all_gather(in_low, "fsdp", axis=0, tiled=True)
    out_low_shard, _ = lax.optimization_barrier((out_low_shard, full_in))
    full_out = lax.all_gather(out_low_shard, "fsdp", axis=0, tiled=True)

    offset = 0
    gain_in = vector[:D]
    offset = D
    gain_out = lax.dynamic_slice_in_dim(vector, offset + r * OWN, OWN, 0)
    offset += DI
    taps = vector[offset : offset + (CONV + 1) * CHANNELS].reshape(CONV + 1, CHANNELS)
    offset += (CONV + 1) * CHANNELS
    per_head = vector[offset:].reshape(3, H)
    dt_bias, a_log, d_skip = lax.dynamic_slice_in_dim(per_head, r * OWN_H, OWN_H, 1)
    taps_bc = taps[:, DI:]
    conv_par = jnp.concatenate([lax.dynamic_slice_in_dim(taps, r * OWN, OWN, 1), taps_bc], 1)
    head_par = jnp.stack(
        [
            jnp.pad(jnp.broadcast_to(d_skip[:, None], (OWN_H, P_SIZE)).reshape(-1), (0, 2 * N)),
            jnp.pad(dt_bias, (0, 640 - OWN_H)),
            jnp.pad(-jnp.exp(a_log), (0, 640 - OWN_H)),
        ],
        0,
    )
    par = jnp.concatenate([conv_par, head_par, jnp.zeros((8, 640), F32)], 0)
    gain_row = gain_out[None, :]

    normed, proj = run_project(full_tokens, gain_in[None, :], slice_z, slice_x, slice_rest)
    pre, mixed, states = run_forward(seg_ends, proj, par)
    grad_normed_out, sums = run_out_grad(grad_branch, slice_out, mixed, proj, gain_row)
    sums = jnp.concatenate([sum_rep(sums[:2].reshape(32, 128)).reshape(2, PACK), jnp.zeros((6, PACK), F32)], 0)

    low_rows, grad_mixed, early_grads, grad_gain = run_gate(
        grad_normed_out, mixed, proj, sums, gain_row, grad_branch, normed
    )
    first_rows = rows_to_owners(low_rows, place)
    early_part, _ = scatter_fsdp(early_grads, None, place)
    out_part = move(
        early_part[:SHARD_IN],
        lambda yh, z, c, x, yl: (x // 2, (x % 2) * 2 + yl, z % 2, 2 * c + yh, z // 2),
    )
    early_parts = gather_rep(jnp.concatenate([out_part, early_part[SHARD_IN:]], 0), place)
    grad_out = early_parts[:, :SHARD_IN].reshape(2, 4, SHARD_IN, WIDE).transpose(0, 2, 1, 3).reshape(SHARD_OUT, D)
    z_parts = early_parts[:, SHARD_IN:]

    grad_x, grad_dtraw, grad_bc, grad_sums, grad_heads = run_backward(
        seg_ends, proj, pre, mixed, grad_mixed, states, par
    )
    grad_bc = sum_to_owners(grad_bc, place)
    own_taps = lax.dynamic_slice_in_dim(taps_bc, r * OWN_BC, OWN_BC, 1)
    own_pre = lax.dynamic_slice_in_dim(pre, OWN + r * OWN_BC, OWN_BC, 1).T
    own_conv = lax.dynamic_slice_in_dim(proj, 2 * OWN + r * OWN_BC, OWN_BC, 1).T
    own_conv = own_conv.astype(BF16).astype(F32)
    sig = jax.nn.sigmoid(own_pre)
    grad_pre = grad_bc * (sig * (1.0 + own_pre * (1.0 - sig)))
    positions = jnp.arange(PACK, dtype=jnp.int32)
    segments = segment_at(positions, seg_ends)
    grad_conv_bc = own_taps[CONV - 1][:, None] * grad_pre
    grad_taps_bc = [jnp.sum(own_conv * grad_pre, 1)]
    for ahead in range(1, CONV):
        same = (segment_at(positions + ahead, seg_ends) == segments) & (positions + ahead < PACK)
        later = jnp.concatenate([grad_pre[:, ahead:], jnp.zeros((OWN_BC, ahead), F32)], 1)
        later = later * same.astype(F32)[None, :]
        grad_taps_bc.insert(0, jnp.sum(own_conv * later, 1))
        grad_conv_bc = grad_conv_bc + own_taps[CONV - 1 - ahead][:, None] * later
    grad_bias_bc = jnp.sum(grad_pre, 1)
    grad_tail = jnp.concatenate(
        [
            grad_x,
            grad_conv_bc.T.astype(BF16),
            grad_dtraw[:, :OWN_H],
            jnp.zeros((PACK, TAIL - OWN - OWN_BC - OWN_H), BF16),
        ],
        1,
    )

    grad_tail_own = contract_rows(normed, grad_tail).reshape(N_FSDP, SHARD_IN, TAIL)
    row = lambda value: jnp.pad(value, (0, OWN - value.shape[0]))[None, :]
    head_columns = jnp.concatenate(
        [grad_gain[0:1]]
        + [grad_sums[1:6]]
        + [row(grad_heads[1, :OWN_H]), row(grad_sums[6].reshape(OWN_H, P_SIZE).sum(1))],
        0,
    )
    bc_columns = jnp.stack(
        [jnp.pad(grad_heads[0, :OWN_H], (0, OWN_BC - OWN_H))]
        + grad_taps_bc
        + [grad_bias_bc, jnp.zeros_like(grad_bias_bc), jnp.zeros_like(grad_bias_bc)],
        0,
    )
    small_own = jnp.concatenate(
        [head_columns, bc_columns, jnp.zeros((8, TAIL - OWN - OWN_BC), F32)], 1
    )

    tail_part, small_sum = scatter_fsdp(grad_tail_own, small_own, place)
    tail_parts = gather_rep(jnp.concatenate([tail_part, small_sum], 0), place)
    small_parts = tail_parts[:, SHARD_IN:]
    tail_parts = tail_parts[:, :SHARD_IN]

    def columns(parts):
        return parts.transpose(1, 0, 2).reshape(parts.shape[1], -1)

    grad_in = jnp.concatenate(
        [columns(z_parts), columns(tail_parts[:, :, :OWN]), columns(tail_parts[:, :, OWN : OWN + OWN_BC])], 1
    )
    grad_dt = columns(tail_parts[:, :, OWN + OWN_BC : OWN + OWN_BC + OWN_H])

    tail_rows = rows_to_owners(grad_tail, place)
    row_grads = jnp.concatenate(
        [columns(first_rows[:, :, OWN:]), columns(tail_rows[:, :, :OWN]), columns(tail_rows[:, :, OWN : OWN + OWN_BC])], 1
    )
    dt_rows = columns(tail_rows[:, :, OWN + OWN_BC : OWN + OWN_BC + OWN_H])
    grad_h = contract_cols(row_grads, full_in) + contract_cols(dt_rows, full_dt)
    own_inputs = tokens.astype(F32)
    own_scale = lax.rsqrt(jnp.mean(own_inputs * own_inputs, axis=1, keepdims=True) + NORM_EPS)
    unit = own_inputs * own_scale
    grad_gain_in = sum_all(jnp.sum(grad_h * unit, 0).reshape(12, 128)).reshape(-1)
    grad_unit = grad_h * gain_in[None, :]
    grad_inputs = own_scale * (grad_unit - unit * jnp.mean(grad_unit * unit, axis=1, keepdims=True))
    input_grad = cotangent.astype(F32) + grad_inputs

    branch = matmul(columns(first_rows[:, :, :OWN]), full_out)
    block_out = own_inputs + own_live[:, None] * branch

    def channels(row):
        return jnp.concatenate(
            [small_parts[:, row, :OWN].reshape(-1), small_parts[:, row, OWN : OWN + OWN_BC].reshape(-1)]
        )

    grad_small_all = jnp.concatenate(
        [grad_gain_in, small_parts[:, 0, :OWN].reshape(-1)]
        + [channels(row) for row in range(1, 6)]
        + [
            small_parts[:, 0, OWN : OWN + OWN_H].reshape(-1),
            small_parts[:, 6, :OWN_H].reshape(-1),
            small_parts[:, 7, :OWN_H].reshape(-1),
        ]
    )
    grad_small = lax.dynamic_slice_in_dim(grad_small_all, place.f * SHARD_SMALL, SHARD_SMALL, 0)

    new_in, new_first_in, new_second_in = adam_update(
        w_in, grad_in, first_in, second_in, RATE_MATRIX, WEIGHT_DECAY
    )
    new_dt, new_first_dt, new_second_dt = adam_update(
        w_dt, grad_dt, first_dt, second_dt, RATE_MATRIX, WEIGHT_DECAY
    )
    new_out, new_first_out, new_second_out = adam_update(
        w_out, grad_out, first_out, second_out, RATE_MATRIX, WEIGHT_DECAY
    )
    new_small, new_first_small, new_second_small = adam_update(
        small, grad_small, first_small, second_small, RATE_SMALL, 0.0
    )
    return (
        block_out,
        input_grad,
        grad_in,
        grad_dt,
        grad_out,
        grad_small,
        new_first_in,
        new_first_dt,
        new_first_out,
        new_first_small,
        new_second_in,
        new_second_dt,
        new_second_out,
        new_second_small,
        new_in,
        new_dt,
        new_out,
        new_small,
    )


def solution(mesh):
    rows = P(("fsdp", "rep"), None)
    matrix = P("fsdp", None)
    vector = P("fsdp")
    group = (matrix, matrix, matrix, vector)
    return jax.shard_map(
        body,
        mesh=mesh,
        in_specs=(rows, rows, P()) + group * 3,
        out_specs=(rows, rows) + group * 4,
        check_vma=False,
    )
```

```python
from functools import partial

import jax
import jax.numpy as jnp
from jax import lax
from jax.experimental import pallas as pl
from jax.experimental.pallas import tpu as pltpu
from jax.sharding import PartitionSpec as P

D = 1536
H = 48
P_SIZE = 64
N = 128
CONV = 4
STEP = 10
DI = 3072
CHANNELS = DI + 2 * N
SMALL = 21392
N_FSDP = 16
N_REP = 8
ROWS = 256
PACK = 2048
OWN = DI // N_REP
OWN_H = H // N_REP
OWN_BC = 2 * N // N_REP
SHARD_IN = D // N_FSDP
SHARD_OUT = DI // N_FSDP
SHARD_SMALL = SMALL // N_FSDP
TAIL = 512
WIDE = 384
CHUNK = 128
CHUNKS = PACK // CHUNK
HALF = CHUNKS // 2
VMEM_LIMIT = 40 * 1024 * 1024

NORM_EPS = 1e-05
BETA_ONE = 0.9
BETA_TWO = 0.999
ADAM_EPS = 1e-08
WEIGHT_DECAY = 0.1
RATE_MATRIX = 0.04
RATE_SMALL = 0.4
PRECISE = lax.Precision.HIGHEST
BF16 = jnp.bfloat16
F32 = jnp.float32


def move(value, target):
    pairs = []
    for f in range(N_FSDP):
        for r in range(N_REP):
            yh, z, c, x, yl = target(f // 8, (f // 2) % 4, f % 2, r // 2, r % 2)
            pairs.append((f * N_REP + r, ((yh % 2) * 8 + (z % 4) * 2 + c % 2) * N_REP + (x % 4) * 2 + yl % 2))
    return lax.ppermute(value, ("fsdp", "rep"), pairs)


def along_x(steps):
    return lambda yh, z, c, x, yl: (yh, z, c, x + steps, yl)


def along_z(steps):
    return lambda yh, z, c, x, yl: (yh, z + steps, c, x, yl)


def swap_y(yh, z, c, x, yl):
    return (yh, z, c, x, yl + 1)


def swap_y_hi(yh, z, c, x, yl):
    return (yh + 1, z, c, x, yl)


def swap_core(yh, z, c, x, yl):
    return (yh, z, c + 1, x, yl)


class Place:
    def __init__(self):
        f = lax.axis_index("fsdp")
        r = lax.axis_index("rep")
        self.f, self.r = f, r
        self.yh, self.z, self.c = f // 8, (f // 2) % 4, f % 2
        self.x, self.yl = r // 2, r % 2


def at(value, index, axis=0):
    return lax.dynamic_index_in_dim(value, index, axis, keepdims=False)


def tie(values, *others):
    return lax.optimization_barrier((values, others))[0]


def both(mine, other, second):
    first = jnp.where(second == 0, mine, other)
    last = jnp.where(second == 0, other, mine)
    return jnp.stack([first, last], 0)


def put(out, piece, axis, index):
    starts = [jnp.int32(0)] * out.ndim
    starts[axis] = jnp.int32(index)
    return lax.dynamic_update_slice(out, jnp.expand_dims(piece, axis), tuple(starts))


def in_ring_order(pieces, here, axis):
    first = pieces[0]
    out = jnp.zeros(first.shape[:axis] + (4,) + first.shape[axis:], first.dtype)
    for offset, piece in enumerate(pieces):
        out = put(out, piece, axis, (here + offset) % 4)
    return out


def exchange_rep(value):
    found = {(0, 0): value}
    for dx, dy in ((1, 0), (3, 0), (0, 1), (2, 0), (1, 1), (3, 1), (2, 1)):
        found[dx, dy] = move(value, lambda yh, z, c, x, yl: (yh, z, c, x - dx, yl + dy))
    return [found[k // 2, k % 2] for k in range(N_REP)]


def sum_rep(value):
    value = value + move(value, swap_y)
    value = value + move(value, lambda yh, z, c, x, yl: (yh, z, c, x ^ 1, yl))
    return value + move(value, lambda yh, z, c, x, yl: (yh, z, c, x ^ 2, yl))


def sum_all(value):
    value = sum_rep(value)
    value = value + move(value, swap_core)
    value = value + move(value, lambda yh, z, c, x, yl: (yh, z ^ 1, c, x, yl))
    value = value + move(value, lambda yh, z, c, x, yl: (yh, z ^ 2, c, x, yl))
    return value + move(value, swap_y_hi)


def with_rows(block, extra):
    width = block.shape[-1]
    flat = block.reshape(-1, width)
    return flat if extra is None else jnp.concatenate([flat, extra], 0)


def received(block, target, base, add_to):
    got = move(with_rows(block, base), target)
    rows = got.shape[0] - (0 if base is None else base.shape[0])
    return got[:rows].reshape(add_to.shape), got[rows:]


def scatter_ring(keep, got, extra, place):
    z_sum = at(keep, place.z, 1) + at(got, place.z, 1)
    found = []
    for step in (1, 3, 2):
        there = (place.z + step) % 4
        found.append(received(at(keep, there, 1) + at(got, there, 1), along_z(step), extra, z_sum))
    z_sum = z_sum + found[0][0] + found[1][0] + found[2][0]
    if extra is not None:
        extra = extra + found[0][1] + found[1][1] + found[2][1]
    mine = at(z_sum, place.yh)
    more, more_extra = received(at(z_sum, 1 - place.yh), swap_y_hi, extra, mine)
    return mine + more, (None if extra is None else extra + more_extra)


def adam_update(weight, gradient, moment_one, moment_two, learn_rate, decay_rate):
    moment_one = BETA_ONE * moment_one + (1.0 - BETA_ONE) * gradient
    moment_two = BETA_TWO * moment_two + (1.0 - BETA_TWO) * gradient * gradient
    scaled = (
        moment_one
        / (1.0 - BETA_ONE**STEP)
        / (jnp.sqrt(moment_two / (1.0 - BETA_TWO**STEP)) + ADAM_EPS)
    )
    return (weight - learn_rate * (scaled + decay_rate * weight), moment_one, moment_two)


def contract_rows(left_side, right_side):
    return lax.dot_general(
        left_side, right_side, (((0,), (0,)), ((), ())), preferred_element_type=F32
    )


def contract_cols(left_side, right_side):
    return lax.dot_general(
        left_side, right_side, (((1,), (1,)), ((), ())), preferred_element_type=F32
    )


def matmul(left_side, right_side):
    return jnp.dot(left_side, right_side, preferred_element_type=F32)


def segment_at(positions, seg_ends):
    counted = jnp.sum((positions[:, None] >= seg_ends[None, :]).astype(jnp.int32), axis=1)
    return jnp.where(positions < 0, jnp.int32(-1), counted)


def split_two(value):
    high = value.astype(BF16)
    return high, (value - high.astype(F32)).astype(BF16)


def split_three(value):
    high = value.astype(BF16)
    rest = value - high.astype(F32)
    middle = rest.astype(BF16)
    return high, middle, (rest - middle.astype(F32)).astype(BF16)


def product(left, right, left_dim, right_dim):
    return lax.dot_general(
        left, right, (((left_dim,), (right_dim,)), ((), ())), preferred_element_type=F32
    )


def joined_product(left_parts, right_parts, left_dim=1, right_dim=0):
    left_high, left_low = left_parts
    right_high, right_low = right_parts
    return product(
        jnp.concatenate([left_high, left_high, left_low], left_dim),
        jnp.concatenate([right_high, right_low, right_high], right_dim),
        left_dim,
        right_dim,
    )


def precise_product(left, right, left_dim=1, right_dim=0):
    return joined_product(split_two(left), split_two(right), left_dim, right_dim)


def ones_product(ones, value):
    return product(jnp.concatenate([ones] * 3, 1), jnp.concatenate(split_three(value), 0), 1, 0)


def spread(per_head, lane):
    return jnp.concatenate(
        [
            jnp.where(lane < P_SIZE, per_head[:, 2 * k : 2 * k + 1], per_head[:, 2 * k + 1 : 2 * k + 2])
            for k in range(OWN_H // 2)
        ],
        1,
    )


def head_sums(value):
    column = lax.broadcasted_iota(jnp.int32, (OWN, N), 0)
    head = lax.broadcasted_iota(jnp.int32, (OWN, N), 1)
    members = ((column >= head * P_SIZE) & (column < (head + 1) * P_SIZE)).astype(F32).astype(BF16)
    high, low = split_two(value)
    return product(jnp.concatenate([high, low], 1), jnp.concatenate([members, members], 0), 1, 0)


def two_heads(pair, lane):
    zero = jnp.zeros_like(pair)
    return jnp.concatenate([jnp.where(lane < P_SIZE, pair, zero), jnp.where(lane < P_SIZE, zero, pair)], 0)


def chunk_facts(ends, chunk, dt_pre, par):
    column = lax.broadcasted_iota(jnp.int32, (CHUNK, 1), 0) + chunk * CHUNK
    row = lax.broadcasted_iota(jnp.int32, (1, CHUNK), 1) + chunk * CHUNK

    def segment(position):
        counted = jnp.zeros_like(position)
        for k in range(3):
            counted = counted + (position >= ends[k]).astype(jnp.int32)
        return jnp.where(position < 0, -1, counted)

    def one_segment(position):
        counted = jnp.int32(0)
        for k in range(3):
            counted = counted + (position >= ends[k]).astype(jnp.int32)
        return jnp.where(position < 0, -1, counted)

    here_column, here_row = segment(column), segment(row)
    prior = one_segment(chunk * CHUNK - 1)
    last = one_segment(chunk * CHUNK + CHUNK - 1)
    lane = lax.broadcasted_iota(jnp.int32, (CHUNK, N), 1)
    shifted = dt_pre + par[6:7, :N]
    soft = jnp.maximum(shifted, 0.0) + jnp.log1p(jnp.exp(-jnp.abs(shifted)))
    step = jnp.where(lane < OWN_H, soft, 0.0)
    decay = step * par[7:8, :N]
    tri_row = lax.broadcasted_iota(jnp.int32, (CHUNK, CHUNK), 0)
    tri_column = lax.broadcasted_iota(jnp.int32, (CHUNK, CHUNK), 1)
    lower = (tri_row >= tri_column).astype(F32).astype(BF16)
    upper = (tri_row <= tri_column).astype(F32).astype(BF16)
    total = ones_product(lower, decay)
    entering = (here_column == prior).astype(F32) * jnp.exp(total)
    end = total[CHUNK - 1 : CHUNK]
    leaving = (here_column == last).astype(F32) * jnp.exp(jnp.minimum(end - total, 0.0))
    passing = jnp.where(last == prior, 1.0, 0.0) * jnp.exp(end)
    return dict(
        column=column,
        segment=segment,
        here_column=here_column,
        here_row=here_row,
        lane=lane,
        shifted=shifted,
        step=step,
        decay=decay,
        total=total,
        entering=entering,
        leaving=leaving,
        passing=passing,
        tri_row=tri_row,
        tri_column=tri_column,
        upper=upper,
    )


def forward_kernel(part, ends, proj, par, *refs):
    if part:
        carry_in, refs = refs[3], refs[4:]
    pre_out, mixed_out, state_out, carry_out, extended, state = refs
    chunk = pl.program_id(0) + part * HALF

    @pl.when(pl.program_id(0) == 0)
    def _():
        if part:
            state[...] = carry_in[:N, :OWN]
            extended[0:8, :] = carry_in[N:, :]
        else:
            state[...] = jnp.zeros_like(state)
            extended[0:8, :] = jnp.zeros((8, 640), F32)

    facts = chunk_facts(ends, chunk, proj[:, 1024:1152], par)
    lane = facts["lane"]
    conv = proj[:, OWN:1024].astype(BF16).astype(F32)
    extended[8 : 8 + CHUNK, :] = conv
    pre = par[4:5] + par[3:4] * conv
    for back in range(1, CONV):
        same = (facts["segment"](facts["column"] - back) == facts["here_column"]).astype(F32)
        pre = pre + par[3 - back : 4 - back] * (extended[8 - back : 8 - back + CHUNK, :] * same)
    extended[0:8, :] = extended[CHUNK : CHUNK + 8, :]
    pre_out[...] = pre
    act = pre * jax.nn.sigmoid(pre)
    own_x, state_b, state_c = act[:, :OWN], act[:, OWN : OWN + N], act[:, OWN + N :]
    stepped = own_x * spread(facts["step"], lane)
    b_parts, c_parts = split_two(state_b), split_two(state_c)
    inside = (facts["tri_row"] >= facts["tri_column"]) & (facts["here_column"] == facts["here_row"])
    scores = jnp.where(inside, joined_product(c_parts, b_parts, 1, 1), 0.0)
    total_rows = facts["total"].T
    state_in = state[...]
    state_out[...] = state_in
    outs = []
    for pair in range(OWN_H // 2):
        mixing = []
        for head in (2 * pair, 2 * pair + 1):
            span = facts["total"][:, head : head + 1] - total_rows[head : head + 1, :]
            mixing.append(jnp.exp(jnp.minimum(span, 0.0)) * scores)
        inner = two_heads(stepped[:, pair * N : pair * N + N], lane)
        outs.append(precise_product(jnp.concatenate(mixing, 1), inner))
    scanned = jnp.concatenate(outs, 1) + spread(facts["entering"], lane) * joined_product(
        c_parts, split_two(state_in)
    )
    state[...] = spread(facts["passing"], lane[:1]) * state_in + precise_product(
        state_b.T, stepped * spread(facts["leaving"], lane)
    )
    mixed_out[...] = scanned + par[5:6, :OWN] * own_x

    @pl.when(pl.program_id(0) == HALF - 1)
    def _():
        carry_out[:N, :OWN] = state[...]
        carry_out[:N, OWN:] = jnp.zeros((N, 640 - OWN), F32)
        carry_out[N:, :] = extended[0:8, :]


def run_forward(part, ends, proj, par, before=()):
    here = lambda i: (i + part * HALF, 0)
    chunked = lambda width: pl.BlockSpec((CHUNK, width), here)
    fixed = lambda shape: pl.BlockSpec(shape, lambda i: (0, 0))
    carry = fixed((N + 8, 640))
    return pl.pallas_call(
        partial(forward_kernel, part),
        grid=(HALF,),
        in_specs=[pl.BlockSpec(memory_space=pltpu.SMEM), chunked(1152), fixed((16, 640))]
        + ([pl.BlockSpec(memory_space=pl.ANY)] * 3 + [carry] if part else []),
        out_specs=[chunked(640), chunked(OWN), pl.BlockSpec((N, OWN), here), carry],
        out_shape=[
            jax.ShapeDtypeStruct((PACK, 640), F32),
            jax.ShapeDtypeStruct((PACK, OWN), F32),
            jax.ShapeDtypeStruct((CHUNKS * N, OWN), F32),
            jax.ShapeDtypeStruct((N + 8, 640), F32),
        ],
        input_output_aliases={3: 0, 4: 1, 5: 2} if part else {},
        scratch_shapes=[pltpu.VMEM((CHUNK + 8, 640), F32), pltpu.VMEM((N, OWN), F32)],
        compiler_params=pltpu.CompilerParams(
            dimension_semantics=("arbitrary",), vmem_limit_bytes=VMEM_LIMIT
        ),
        cost_estimate=pl.CostEstimate(flops=8_000_000_000, bytes_accessed=12_000_000, transcendentals=1_500_000),
        name="scan_forward",
    )(ends, proj, par, *before)


def backward_kernel(part, ends, conv_in, dt_in, pre_in, mixed_in, grad_mixed, state_all, par, *refs):
    if part:
        carry_in, sums_in, head_in, refs = refs[3], refs[4], refs[5], refs[6:]
    grad_x, grad_dt, grad_bc, sums, head_acc, carry_out, carried, extended, end_dot = refs
    step_index = pl.program_id(0)
    chunk = CHUNKS - 1 - part * HALF - step_index

    @pl.when(step_index == 0)
    def _():
        if part:
            carried[...] = carry_in[:N, :]
            extended[CHUNK : CHUNK + 8, :] = carry_in[N : N + 8, :]
            end_dot[...] = carry_in[N + 8 :, :N]
            sums[...] = sums_in[...]
            head_acc[...] = head_in[...]
        else:
            carried[...] = jnp.zeros_like(carried)
            extended[CHUNK : CHUNK + 8, :] = jnp.zeros((8, OWN), F32)
            end_dot[...] = jnp.zeros_like(end_dot)
            sums[...] = jnp.zeros_like(sums)
            head_acc[...] = jnp.zeros_like(head_acc)

    facts = chunk_facts(ends, chunk, dt_in[...], par)
    lane = facts["lane"]
    pre = pre_in[...]
    sig = jax.nn.sigmoid(pre)
    act = pre * sig
    own_x, state_b, state_c = act[:, :OWN], act[:, OWN : OWN + N], act[:, OWN + N :]
    step = facts["step"]
    step_wide = spread(step, lane)
    stepped = own_x * step_wide
    skip = par[5:6, :OWN]
    scanned = mixed_in[...] - skip * own_x
    grad_m = grad_mixed[...]
    sums[6:7] += jnp.sum(grad_m * own_x, 0, keepdims=True)

    b_parts, c_parts = split_two(state_b), split_two(state_c)
    inside = (facts["tri_row"] <= facts["tri_column"]) & (facts["here_column"] == facts["here_row"])
    scores = jnp.where(inside, joined_product(b_parts, c_parts, 1, 1), 0.0)
    total_rows = facts["total"].T
    grad_scores = jnp.zeros((CHUNK, CHUNK), F32)
    grad_stepped = []
    for pair in range(OWN_H // 2):
        columns = slice(pair * N, pair * N + N)
        grad_pair = grad_m[:, columns]
        high, low = split_two(grad_pair)
        stepped_parts = split_two(two_heads(stepped[:, columns], lane))
        grad_mixing = joined_product(stepped_parts, (high, low), 1, 1)
        mixing = []
        for k in range(2):
            head = 2 * pair + k
            span = total_rows[head : head + 1, :] - facts["total"][:, head : head + 1]
            decays = jnp.exp(jnp.minimum(span, 0.0))
            mixing.append(decays * scores)
            grad_scores = grad_scores + decays * grad_mixing[k * CHUNK : (k + 1) * CHUNK]
        grad_stepped.append(
            joined_product(
                split_two(jnp.concatenate(mixing, 1)), (two_heads(high, lane), two_heads(low, lane))
            )
        )
    grad_scores = jnp.where(inside, grad_scores, 0.0)
    carry = carried[...]
    carry_parts = split_two(carry)
    leaving = spread(facts["leaving"], lane)
    grad_stepped = jnp.concatenate(grad_stepped, 1) + leaving * joined_product(b_parts, carry_parts)
    state_in = state_all[...]
    entered = spread(facts["entering"], lane) * grad_m
    entered_parts = split_two(entered)
    grad_b = precise_product(grad_scores, state_c) + joined_product(
        split_two(leaving * stepped), carry_parts, 1, 1
    )
    grad_c = precise_product(grad_scores.T, state_b) + joined_product(
        entered_parts, split_two(state_in), 1, 1
    )
    grad_bc[0:N, :] = grad_b.T
    grad_bc[N:, :] = grad_c.T
    new_carry = spread(facts["passing"], lane[:1]) * carry + joined_product(
        split_two(state_c.T), entered_parts
    )
    carried[...] = new_carry

    grad_step = head_sums(own_x * grad_stepped)
    last_row = lax.broadcasted_iota(jnp.int32, (CHUNK, N), 0) == CHUNK - 1
    grad_total = head_sums(grad_m * scanned) - step * grad_step
    grad_total = grad_total + jnp.where(last_row, end_dot[0:1, :], 0.0)
    grad_decay = ones_product(facts["upper"], grad_total)
    end_dot[...] = head_sums(
        jnp.broadcast_to(jnp.sum(new_carry * state_in, 0, keepdims=True), (8, OWN))
    )
    grad_pre_dt = (grad_step + grad_decay * par[7:8, :N]) * jax.nn.sigmoid(facts["shifted"])
    grad_pre_dt = jnp.where(lane < OWN_H, grad_pre_dt, 0.0)
    grad_dt[...] = grad_pre_dt.astype(BF16)
    head_acc[0:1] += jnp.sum(grad_pre_dt, 0, keepdims=True)
    head_acc[1:2] += jnp.sum(grad_decay * facts["decay"], 0, keepdims=True)

    sig_x, pre_x = sig[:, :OWN], pre[:, :OWN]
    grad_pre = (step_wide * grad_stepped + skip * grad_m) * (sig_x * (1.0 + pre_x * (1.0 - sig_x)))
    extended[0:CHUNK, :] = grad_pre
    conv = conv_in[...].astype(BF16).astype(F32)
    sums[5:6] += jnp.sum(grad_pre, 0, keepdims=True)
    sums[4:5] += jnp.sum(conv * grad_pre, 0, keepdims=True)
    grad_conv = par[3:4, :OWN] * grad_pre
    for ahead in range(1, CONV):
        same = (facts["segment"](facts["column"] + ahead) == facts["here_column"]).astype(F32)
        later = extended[ahead : ahead + CHUNK, :] * same
        sums[4 - ahead : 5 - ahead] += jnp.sum(conv * later, 0, keepdims=True)
        grad_conv = grad_conv + par[3 - ahead : 4 - ahead, :OWN] * later
    extended[CHUNK : CHUNK + 8, :] = extended[0:8, :]
    grad_x[...] = grad_conv.astype(BF16)

    @pl.when(step_index == HALF - 1)
    def _():
        carry_out[:N, :] = carried[...]
        carry_out[N : N + 8, :] = extended[CHUNK : CHUNK + 8, :]
        carry_out[N + 8 :, :N] = end_dot[...]
        carry_out[N + 8 :, N:] = jnp.zeros((8, OWN - N), F32)


def run_backward(part, ends, proj, pre, mixed, grad_mixed, states, par, before=()):
    last = CHUNKS - 1 - part * HALF
    chunked = lambda width, column=0: pl.BlockSpec((CHUNK, width), lambda i: (last - i, column))
    fixed = lambda shape: pl.BlockSpec(shape, lambda i: (0, 0))
    carry = [fixed((N + 16, OWN)), fixed((8, OWN)), fixed((8, N))]
    return pl.pallas_call(
        partial(backward_kernel, part),
        grid=(HALF,),
        in_specs=[
            pl.BlockSpec(memory_space=pltpu.SMEM),
            chunked(OWN, 1),
            chunked(N, 8),
            chunked(640),
            chunked(OWN),
            chunked(OWN),
            pl.BlockSpec((N, OWN), lambda i: (last - i, 0)),
            fixed((16, 640)),
        ]
        + ([pl.BlockSpec(memory_space=pl.ANY)] * 3 + carry if part else []),
        out_specs=[
            chunked(OWN),
            chunked(N),
            pl.BlockSpec((2 * N, CHUNK), lambda i: (0, last - i)),
            carry[1],
            carry[2],
            carry[0],
        ],
        out_shape=[
            jax.ShapeDtypeStruct((PACK, OWN), BF16),
            jax.ShapeDtypeStruct((PACK, N), BF16),
            jax.ShapeDtypeStruct((2 * N, PACK), F32),
            jax.ShapeDtypeStruct((8, OWN), F32),
            jax.ShapeDtypeStruct((8, N), F32),
            jax.ShapeDtypeStruct((N + 16, OWN), F32),
        ],
        input_output_aliases={8: 0, 9: 1, 10: 2} if part else {},
        scratch_shapes=[
            pltpu.VMEM((N, OWN), F32),
            pltpu.VMEM((CHUNK + 8, OWN), F32),
            pltpu.VMEM((8, N), F32),
        ],
        compiler_params=pltpu.CompilerParams(
            dimension_semantics=("arbitrary",), vmem_limit_bytes=VMEM_LIMIT
        ),
        cost_estimate=pl.CostEstimate(flops=12_000_000_000, bytes_accessed=16_000_000, transcendentals=3_000_000),
        name="scan_backward",
    )(ends, proj, proj, pre, mixed, grad_mixed, states, par, *before)


PARTS = (1, 1, 1, 2, 2, 2, 1, 1)


def load_block(step, pieces, block):
    first = 0
    for slot, count in enumerate(PARTS):
        refs = pieces[first : first + count]
        first += count

        @pl.when(step == slot)
        def _(refs=refs):
            if len(refs) == 1:
                block[...] = refs[0][...]
            else:
                block[: ROWS // 2, :] = refs[0][...]
                block[ROWS // 2 :, :] = refs[1][...]


def piece_specs():
    return [
        pl.BlockSpec((ROWS // count, D), lambda i, table: (0, 0)) for count in PARTS for _ in range(count)
    ]


def project_kernel(table, *refs):
    pieces, (gain, weight, normed_out, proj, block) = refs[:11], refs[11:]
    load_block(pl.program_id(0), pieces, block)
    values = block[...].astype(F32)
    scale = lax.rsqrt(jnp.mean(values * values, axis=1, keepdims=True) + NORM_EPS)
    normed = (values * scale * gain[...]).astype(BF16)
    normed_out[...] = normed
    proj[...] = matmul(normed, weight[...])


def run_project(table, pieces, gain, weight):
    fixed = lambda shape: pl.BlockSpec(shape, lambda i, table: (0, 0))
    placed = lambda width: pl.BlockSpec((ROWS, width), lambda i, table: (table[i], 0))
    return pl.pallas_call(
        project_kernel,
        grid_spec=pltpu.PrefetchScalarGridSpec(
            num_scalar_prefetch=1,
            grid=(N_REP,),
            in_specs=piece_specs() + [fixed((1, D)), fixed((D, 3 * WIDE))],
            out_specs=[placed(D), placed(3 * WIDE)],
            scratch_shapes=[pltpu.VMEM((ROWS, D), BF16)],
        ),
        out_shape=[jax.ShapeDtypeStruct((PACK, D), BF16), jax.ShapeDtypeStruct((PACK, 3 * WIDE), F32)],
        compiler_params=pltpu.CompilerParams(
            dimension_semantics=("arbitrary",), vmem_limit_bytes=VMEM_LIMIT
        ),
        cost_estimate=pl.CostEstimate(flops=7_250_000_000, bytes_accessed=26_000_000, transcendentals=0),
        name="project",
    )(table, *pieces, gain, weight)


def row_sums(value):
    folded = value[:, :N] + value[:, N : 2 * N] + value[:, 2 * N :]
    return jnp.sum(folded.T, 0, keepdims=True)


def out_grad_kernel(table, *refs):
    pieces = refs[:11]
    w_out, mixed, gate_in, gain, branch_out, grad_out, sums, block, turned = refs[11:]

    @pl.when(pl.program_id(0) == 0)
    def _():
        for k in range(4):
            turned[k * WIDE : (k + 1) * WIDE, :] = w_out[k * WIDE : (k + 1) * WIDE, :].T

    load_block(pl.program_id(0), pieces, block)
    branch = block[...]
    branch_out[...] = branch
    total = matmul(branch, turned[...])
    grad_out[...] = total
    gate = gate_in[...]
    gated = mixed[...] * (gate * jax.nn.sigmoid(gate))
    row = lax.broadcasted_iota(jnp.int32, (8, ROWS), 0)
    sums[...] = jnp.where(
        row == 0, row_sums(gated * gated), jnp.where(row == 1, row_sums(total * gain[...] * gated), 0.0)
    )


def run_out_grad(table, pieces, w_out, mixed, proj, gain):
    fixed = lambda shape: pl.BlockSpec(shape, lambda i, table: (0, 0))
    placed = lambda width: pl.BlockSpec((ROWS, width), lambda i, table: (table[i], 0))
    return pl.pallas_call(
        out_grad_kernel,
        grid_spec=pltpu.PrefetchScalarGridSpec(
            num_scalar_prefetch=1,
            grid=(N_REP,),
            in_specs=piece_specs() + [fixed((D, WIDE)), placed(OWN), placed(OWN), fixed((1, OWN))],
            out_specs=[placed(D), placed(OWN), pl.BlockSpec((8, ROWS), lambda i, table: (0, table[i]))],
            scratch_shapes=[pltpu.VMEM((ROWS, D), BF16), pltpu.VMEM((D, WIDE), BF16)],
        ),
        out_shape=[
            jax.ShapeDtypeStruct((PACK, D), BF16),
            jax.ShapeDtypeStruct((PACK, OWN), F32),
            jax.ShapeDtypeStruct((8, PACK), F32),
        ],
        compiler_params=pltpu.CompilerParams(
            dimension_semantics=("arbitrary",), vmem_limit_bytes=VMEM_LIMIT
        ),
        cost_estimate=pl.CostEstimate(flops=2_420_000_000, bytes_accessed=23_000_000, transcendentals=800_000),
        name="out_grad",
    )(table, *pieces, w_out, mixed, proj, gain)


def gate_kernel(
    where, grad_out, mixed_in, gate_in, sums, gain, grad_branch, normed,
    row_zero, row_one, row_two, row_three, grad_mixed, keep, give, grad_gain, total,
):
    step = pl.program_id(0)
    rows = grad_out.shape[0]
    mixed, gate, grad_o = mixed_in[...], gate_in[...], grad_out[...]
    stats = jnp.concatenate([sums[...], jnp.zeros((N - 8, rows), F32)], 0).T
    out_scale = lax.rsqrt(stats[:, 0:1] * (1.0 / DI) + NORM_EPS)
    pull = out_scale * out_scale * out_scale * (stats[:, 1:2] * (1.0 / DI))
    gate_sig = jax.nn.sigmoid(gate)
    silu = gate * gate_sig
    gated = mixed * silu
    unit = gated * out_scale
    low = (unit * gain[...]).astype(BF16)
    grad_gated = out_scale * (grad_o * gain[...]) - gated * pull
    grad_mixed[...] = grad_gated * silu
    grad_z = (grad_gated * mixed * (gate_sig * (1.0 + gate * (1.0 - gate_sig)))).astype(BF16)
    ahead = (step - where[1] + 4) % 4
    for slot, ref in enumerate((row_zero, row_one, row_two, row_three)):

        @pl.when(ahead == slot)
        def _(ref=ref):
            ref[:, :OWN] = low
            ref[:, OWN:] = grad_z

    @pl.when(step == 0)
    def _():
        grad_gain[...] = jnp.zeros_like(grad_gain)
        total[...] = jnp.zeros_like(total)

    grad_gain[0:1] += jnp.sum(grad_o * unit, 0, keepdims=True)
    for k in range(4):
        part = product(low, grad_branch[:, k * WIDE : (k + 1) * WIDE], 0, 0)
        for m in range(4):
            total[4 * k + m, :SHARD_IN] += part[m * SHARD_IN : (m + 1) * SHARD_IN]
    part = product(normed[...], grad_z, 0, 0)
    for f in range(N_FSDP):
        total[f, SHARD_IN:] += part[f * SHARD_IN : (f + 1) * SHARD_IN]

    @pl.when(step == pl.num_programs(0) - 1)
    def _():
        for k in range(N_FSDP // 2):
            keep[k] = total[2 * k + where[0]]
            give[k] = total[2 * k + 1 - where[0]]


def run_gate(where, grad_out, mixed, proj, sums, gain, grad_branch, normed):
    count = 2 * ROWS
    rows = lambda width: pl.BlockSpec((count, width), lambda i: (i, 0))
    fixed = lambda shape: pl.BlockSpec(shape, lambda i: (0,) * len(shape))
    half = (N_FSDP // 2, 2 * SHARD_IN, WIDE)
    return pl.pallas_call(
        gate_kernel,
        grid=(PACK // count,),
        in_specs=[
            pl.BlockSpec(memory_space=pltpu.SMEM),
            rows(OWN),
            rows(OWN),
            rows(OWN),
            pl.BlockSpec((8, count), lambda i: (0, i)),
            fixed((1, OWN)),
            rows(D),
            rows(D),
        ],
        out_specs=[fixed((count, 2 * OWN))] * 4 + [rows(OWN), fixed(half), fixed(half), fixed((8, OWN))],
        out_shape=[jax.ShapeDtypeStruct((count, 2 * OWN), BF16)] * 4
        + [
            jax.ShapeDtypeStruct((PACK, OWN), F32),
            jax.ShapeDtypeStruct(half, F32),
            jax.ShapeDtypeStruct(half, F32),
            jax.ShapeDtypeStruct((8, OWN), F32),
        ],
        scratch_shapes=[pltpu.VMEM((N_FSDP, 2 * SHARD_IN, WIDE), F32)],
        compiler_params=pltpu.CompilerParams(
            dimension_semantics=("arbitrary",), vmem_limit_bytes=VMEM_LIMIT
        ),
        cost_estimate=pl.CostEstimate(flops=4_840_000_000, bytes_accessed=34_000_000, transcendentals=800_000),
        name="gate_backward",
    )(where, grad_out, mixed, proj, sums, gain, grad_branch, normed)


def own_rows(step, table, mine, other, block, columns):
    for k in range(4):

        @pl.when(step == 2 * k)
        def _(k=k):
            block[...] = mine[k][pl.ds(pl.multiple_of(table[8] * ROWS, ROWS), ROWS), columns]

        @pl.when(step == 2 * k + 1)
        def _(k=k):
            block[...] = other[k * ROWS : (k + 1) * ROWS, columns]


def block_out_kernel(table, *refs):
    mine, (other, weight, tokens, live, out, block) = refs[:4], refs[4:]
    step = pl.program_id(0)
    own_rows(step, table, mine, other, block, slice(0, OWN))
    part = matmul(block[...], weight[...])

    @pl.when(step == 0)
    def _():
        out[...] = part

    @pl.when(step > 0)
    def _():
        out[...] += part

    @pl.when(step == N_REP - 1)
    def _():
        out[...] = tokens[...].astype(F32) + live[...] * out[...]


def run_block_out(table, mine, other, weight, tokens, live):
    fixed = lambda shape: pl.BlockSpec(shape, lambda i, table: (0, 0))
    return pl.pallas_call(
        block_out_kernel,
        grid_spec=pltpu.PrefetchScalarGridSpec(
            num_scalar_prefetch=1,
            grid=(N_REP,),
            in_specs=[fixed((2 * ROWS, 2 * OWN))] * 4
            + [
                fixed((4 * ROWS, 2 * OWN)),
                pl.BlockSpec((OWN, D), lambda i, table: (table[i], 0)),
                fixed((ROWS, D)),
                fixed((ROWS, 1)),
            ],
            out_specs=fixed((ROWS, D)),
            scratch_shapes=[pltpu.VMEM((ROWS, OWN), BF16)],
        ),
        out_shape=jax.ShapeDtypeStruct((ROWS, D), F32),
        compiler_params=pltpu.CompilerParams(
            dimension_semantics=("arbitrary",), vmem_limit_bytes=VMEM_LIMIT
        ),
        cost_estimate=pl.CostEstimate(flops=2_420_000_000, bytes_accessed=14_000_000, transcendentals=0),
        name="block_out",
    )(table, *mine, other, weight, tokens, live)


def input_grad_kernel(table, *refs):
    mine, refs = refs[:4], refs[4:]
    other, tail, rest, w_z, w_x, w_bc, w_dt, tokens, cotangent, gain, out, gain_out, block = refs
    step = pl.program_id(0)
    own_rows(step, table, mine, other, block, slice(OWN, 2 * OWN))
    part = contract_cols(block[...], w_z[...]) + contract_cols(tail[0, :, :OWN], w_x[...])

    @pl.when(step == 0)
    def _():
        out[...] = part

    @pl.when(step > 0)
    def _():
        out[...] += part

    @pl.when(step == N_REP - 1)
    def _():
        grad_h = out[...] + contract_cols(rest[:, : 2 * N], w_bc[...]) + contract_cols(rest[:, 2 * N :], w_dt[...])
        values = tokens[...].astype(F32)
        scale = lax.rsqrt(jnp.mean(values * values, axis=1, keepdims=True) + NORM_EPS)
        unit = values * scale
        gain_out[...] = jnp.broadcast_to(jnp.sum(grad_h * unit, 0, keepdims=True), gain_out.shape)
        grad_unit = grad_h * gain[...]
        inner = jnp.mean(grad_unit * unit, axis=1, keepdims=True)
        out[...] = cotangent[...].astype(F32) + scale * (grad_unit - unit * inner)


def run_input_grad(table, mine, other, tail, rest, full_in, low_dt, tokens, cotangent, gain):
    fixed = lambda shape: pl.BlockSpec(shape, lambda i, table: (0, 0))
    return pl.pallas_call(
        input_grad_kernel,
        grid_spec=pltpu.PrefetchScalarGridSpec(
            num_scalar_prefetch=1,
            grid=(N_REP,),
            in_specs=[fixed((2 * ROWS, 2 * OWN))] * 4
            + [
                fixed((4 * ROWS, 2 * OWN)),
                pl.BlockSpec((1, ROWS, TAIL), lambda i, table: (table[i], 0, 0)),
                fixed((ROWS, 3 * N)),
                pl.BlockSpec((D, OWN), lambda i, table: (0, table[i])),
                pl.BlockSpec((D, OWN), lambda i, table: (0, N_REP + table[i])),
                pl.BlockSpec((D, 2 * N), lambda i, table: (0, DI // N)),
                fixed((D, N)),
                fixed((ROWS, D)),
                fixed((ROWS, D)),
                fixed((1, D)),
            ],
            out_specs=[fixed((ROWS, D)), fixed((8, D))],
            scratch_shapes=[pltpu.VMEM((ROWS, OWN), BF16)],
        ),
        out_shape=[jax.ShapeDtypeStruct((ROWS, D), F32), jax.ShapeDtypeStruct((8, D), F32)],
        compiler_params=pltpu.CompilerParams(
            dimension_semantics=("arbitrary",), vmem_limit_bytes=VMEM_LIMIT
        ),
        cost_estimate=pl.CostEstimate(flops=5_100_000_000, bytes_accessed=30_000_000, transcendentals=0),
        name="input_grad",
    )(table, *mine, other, tail, rest, full_in, full_in, full_in, low_dt, tokens, cotangent, gain)


def adam_in_kernel(table, *refs):
    early, (tail, rest, weight, first, second) = refs[:N_REP], refs[N_REP : N_REP + 5]
    grad_out, first_out, second_out, weight_out, grad = refs[N_REP + 5 :]
    step = pl.program_id(0)
    for slot in range(N_REP):

        @pl.when(step == slot)
        def _(slot=slot):
            grad[...] = early[slot][SHARD_IN:, :]

    @pl.when((step >= N_REP) & (step < 2 * N_REP))
    def _():
        grad[...] = tail[jnp.clip(step - N_REP, 0, N_REP - 1), :SHARD_IN, :OWN]

    @pl.when(step == 2 * N_REP)
    def _():
        grad[...] = rest[...]

    new_weight, new_first, new_second = adam_update(
        weight[...], grad[...], first[...], second[...], RATE_MATRIX, WEIGHT_DECAY
    )
    grad_out[...] = grad[...]
    first_out[...] = new_first
    second_out[...] = new_second
    weight_out[...] = new_weight


def run_adam_in(table, early, tail, rest, weight, first, second):
    fixed = lambda shape: pl.BlockSpec(shape, lambda i, table: (0,) * len(shape))
    column = pl.BlockSpec((SHARD_IN, WIDE), lambda i, table: (0, table[i]))
    shape = jax.ShapeDtypeStruct(weight.shape, F32)
    return pl.pallas_call(
        adam_in_kernel,
        grid_spec=pltpu.PrefetchScalarGridSpec(
            num_scalar_prefetch=1,
            grid=(2 * N_REP + 1,),
            in_specs=[fixed((2 * SHARD_IN, WIDE))] * N_REP
            + [fixed(tail.shape), fixed((SHARD_IN, WIDE)), column, column, column],
            out_specs=[column] * 4,
            scratch_shapes=[pltpu.VMEM((SHARD_IN, WIDE), F32)],
        ),
        out_shape=[shape] * 4,
        compiler_params=pltpu.CompilerParams(
            dimension_semantics=("arbitrary",), vmem_limit_bytes=VMEM_LIMIT
        ),
        cost_estimate=pl.CostEstimate(flops=10_000_000, bytes_accessed=22_000_000, transcendentals=1_200_000),
        name="adam_in",
    )(table, *early, tail, rest, weight, first, second)


def adam_out_kernel(table, *refs):
    early, (weight, first, second) = refs[:N_REP], refs[N_REP : N_REP + 3]
    grad_out, first_out, second_out, weight_out, grad = refs[N_REP + 3 :]
    for slot in range(N_REP):

        @pl.when(pl.program_id(0) == slot)
        def _(slot=slot):
            grad[...] = early[slot][:SHARD_IN, :]

    new_weight, new_first, new_second = adam_update(
        weight[...], grad[...], first[...], second[...], RATE_MATRIX, WEIGHT_DECAY
    )
    grad_out[...] = grad[...]
    first_out[...] = new_first
    second_out[...] = new_second
    weight_out[...] = new_weight


def run_adam_out(table, early, weight, first, second):
    fixed = lambda shape: pl.BlockSpec(shape, lambda i, table: (0,) * len(shape))
    part = pl.BlockSpec((SHARD_IN, WIDE), lambda i, table: (table[i] // 4, table[i] % 4))
    shape = jax.ShapeDtypeStruct(weight.shape, F32)
    return pl.pallas_call(
        adam_out_kernel,
        grid_spec=pltpu.PrefetchScalarGridSpec(
            num_scalar_prefetch=1,
            grid=(N_REP,),
            in_specs=[fixed((2 * SHARD_IN, WIDE))] * N_REP + [part] * 3,
            out_specs=[part] * 4,
            scratch_shapes=[pltpu.VMEM((SHARD_IN, WIDE), F32)],
        ),
        out_shape=[shape] * 4,
        compiler_params=pltpu.CompilerParams(
            dimension_semantics=("arbitrary",), vmem_limit_bytes=VMEM_LIMIT
        ),
        cost_estimate=pl.CostEstimate(flops=5_000_000, bytes_accessed=12_000_000, transcendentals=600_000),
        name="adam_out",
    )(table, *early, weight, first, second)


def body(
    tokens,
    cotangent,
    lengths,
    w_in,
    w_dt,
    w_out,
    small,
    first_in,
    first_dt,
    first_out,
    first_small,
    second_in,
    second_dt,
    second_out,
    second_small,
):
    place = Place()
    r = place.r
    zero = jnp.int32(0)
    pack_lengths = lax.dynamic_slice_in_dim(lengths, place.f, 1, 0)[0]
    seg_ends = jnp.cumsum(pack_lengths)
    own_positions = r * ROWS + jnp.arange(ROWS, dtype=jnp.int32)
    own_live = (segment_at(own_positions, seg_ends) < 3).astype(F32)[:, None]
    slots = jnp.arange(N_REP, dtype=jnp.int32)
    ahead = ((place.x + slots // 2) % 4) * 2 + (place.yl + slots) % 2
    behind = ((place.x - slots // 2) % 4) * 2 + (place.yl + slots) % 2
    half = ROWS // 2

    in_low = w_in.astype(BF16)
    dt_low = w_dt.astype(BF16)
    small_rows = jnp.pad(small.astype(BF16), (0, 16 * 1152 - SHARD_SMALL)).reshape(16, 1152)
    weight_block = jnp.concatenate(
        [
            jnp.concatenate(
                [
                    lax.dynamic_slice_in_dim(in_low, r * OWN, OWN, 1),
                    lax.dynamic_slice_in_dim(in_low, DI + r * OWN, OWN, 1),
                    in_low[:, 2 * DI :],
                    lax.dynamic_slice_in_dim(dt_low, r * OWN_H, OWN_H, 1),
                    jnp.zeros((SHARD_IN, 2), BF16),
                    dt_low,
                    jnp.zeros((SHARD_IN, N - 8 - H), BF16),
                ],
                1,
            ),
            small_rows,
        ],
        0,
    )
    out_low_shard = w_out.astype(BF16)
    out_piece = lax.dynamic_slice(
        out_low_shard, (SHARD_IN * (place.x // 2), WIDE * ((place.x % 2) * 2 + place.yl)), (SHARD_IN, WIDE)
    )

    from_left = move(tokens, along_x(1))
    from_right = move(tokens, along_x(-1))
    partner = move(tokens, swap_y)
    weight_pair = both(weight_block, move(weight_block, swap_y_hi), place.yh)
    out_piece = move(
        out_piece, lambda yh, z, c, x, yl: (x % 2, yl * 2 + c, x // 2, yh * 2 + z // 2, z % 2)
    )
    slice_out = lax.all_gather(out_piece, "fsdp", axis=0, tiled=True)

    from_left, from_right, partner, weight_pair = lax.optimization_barrier(
        (from_left, from_right, partner, weight_pair)
    )
    far_top = move(from_left[:half], along_x(1))
    far_low = move(from_right[half:], along_x(-1))
    partner_left = move(from_left, swap_y)
    weight_left = move(weight_pair, along_z(1))
    weight_right = move(weight_pair, along_z(-1))

    far_top, far_low, partner_left, weight_left, weight_right = lax.optimization_barrier(
        (far_top, far_low, partner_left, weight_left, weight_right)
    )
    right_top = move(partner[:half], along_x(-1))
    right_low = move(from_right[half:], swap_y)
    weight_far = jnp.concatenate(
        [move(weight_left[:1], along_z(1)), move(weight_right[1:], along_z(-1))], 0
    )

    right_top, right_low, weight_far, partner_left = lax.optimization_barrier(
        (right_top, right_low, weight_far, partner_left)
    )
    partner_far_top = move(partner_left[:half], along_x(1))
    partner_far_low = move(right_low, along_x(-1))
    weight_ring = in_ring_order([weight_pair, weight_right, weight_far, weight_left], place.z, 1)
    weight_other = move(weight_ring, swap_core)
    cores = [jnp.where(place.c == 0, weight_ring, weight_other), jnp.where(place.c == 0, weight_other, weight_ring)]
    slice_in = jnp.stack([core[:, :, :SHARD_IN] for core in cores], 2).reshape(D, 1152)
    vector = jnp.stack([core[:, :, SHARD_IN : SHARD_IN + 2] for core in cores], 2)
    vector = vector.reshape(N_FSDP, 2 * 1152)[:, :SHARD_SMALL].reshape(-1).astype(F32)
    token_pieces = [
        tokens, partner, from_right, right_top, right_low, far_top, far_low,
        partner_far_top, partner_far_low, from_left, partner_left,
    ]

    full_in = lax.all_gather(tie(in_low, slice_out), "fsdp", axis=0, tiled=True)
    full_out = lax.all_gather(tie(out_low_shard, full_in), "fsdp", axis=0, tiled=True)

    offset = 0
    gain_in = vector[None, :D]
    offset = D
    gain_row = lax.dynamic_slice_in_dim(vector, offset + r * OWN, OWN, 0)[None, :]
    offset += DI
    taps = vector[offset : offset + (CONV + 1) * CHANNELS].reshape(CONV + 1, CHANNELS)
    offset += (CONV + 1) * CHANNELS
    per_head = vector[offset:].reshape(3, H)
    dt_bias, a_log, d_skip = lax.dynamic_slice_in_dim(per_head, r * OWN_H, OWN_H, 1)
    taps_bc = taps[:, DI:]
    conv_par = jnp.concatenate([lax.dynamic_slice_in_dim(taps, r * OWN, OWN, 1), taps_bc], 1)
    head_par = jnp.stack(
        [
            jnp.pad(jnp.broadcast_to(d_skip[:, None], (OWN_H, P_SIZE)).reshape(-1), (0, 2 * N)),
            jnp.pad(dt_bias, (0, 640 - OWN_H)),
            jnp.pad(-jnp.exp(a_log), (0, 640 - OWN_H)),
        ],
        0,
    )
    par = jnp.concatenate([conv_par, head_par, jnp.zeros((8, 640), F32)], 0)

    branch = (cotangent.astype(F32) * own_live).astype(BF16)
    branch = tie(branch, partner_far_top, partner_far_low)
    b_left = move(branch, along_x(1))
    b_right = move(branch, along_x(-1))
    b_partner = move(branch, swap_y)
    normed, proj = run_project(ahead, token_pieces, gain_in, slice_in)
    b_left, b_right, b_partner, proj = lax.optimization_barrier((b_left, b_right, b_partner, proj))
    b_far_top = move(b_left[:half], along_x(1))
    b_far_low = move(b_right[half:], along_x(-1))
    b_partner_left = move(b_left, swap_y)
    b_right_top = move(b_partner[:half], along_x(-1))
    b_right_low = move(b_right[half:], swap_y)
    before = run_forward(0, seg_ends, proj, par)
    b_far_top, b_far_low, b_partner_left, b_right_top, b_right_low, before = lax.optimization_barrier(
        (b_far_top, b_far_low, b_partner_left, b_right_top, b_right_low, before)
    )
    b_partner_far_top = move(b_partner_left[:half], along_x(1))
    b_partner_far_low = move(b_right_low, along_x(-1))
    pre, mixed, states, _ = run_forward(1, seg_ends, proj, par, before)
    branch_pieces = [
        branch, b_partner, b_right, b_right_top, b_right_low, b_far_top, b_far_low,
        b_partner_far_top, b_partner_far_low, b_left, b_partner_left,
    ]
    grad_branch, grad_normed_out, sums = run_out_grad(ahead, branch_pieces, slice_out, mixed, proj, gain_row)
    sums = sum_rep(sums[:2].reshape(32, 128)).reshape(2, PACK)
    sums = jnp.concatenate([sums, jnp.zeros((6, PACK), F32)], 0)

    where = jnp.stack([place.c, place.x, place.yl])
    row_zero, row_one, row_two, row_three, grad_mixed, keep, give, grad_gain = run_gate(
        where, grad_normed_out, mixed, proj, sums, gain_row, grad_branch, normed
    )

    row_one = move(row_one, along_x(1))
    row_three = move(row_three, along_x(3))
    row_two = move(row_two, along_x(2))
    got = move(give, swap_core)
    before = run_backward(0, seg_ends, proj, pre, mixed, grad_mixed, states, par)
    row_one, row_two, row_three, got, before = lax.optimization_barrier(
        (row_one, row_two, row_three, got, before)
    )
    mine_rows = [row_zero, row_one, row_two, row_three]
    far_rows = jnp.concatenate(
        [lax.dynamic_slice_in_dim(rows, (1 - place.yl) * ROWS, ROWS, 0) for rows in mine_rows], 0
    )
    other_rows = move(far_rows, swap_y)
    split = (2, 4, 2 * SHARD_IN, WIDE)
    early_part, _ = scatter_ring(keep.reshape(split), got.reshape(split), None, place)
    grad_x, grad_dtraw, grad_bc, grad_sums, grad_heads, _ = run_backward(
        1, seg_ends, proj, pre, mixed, grad_mixed, states, par, (before[0], before[1], before[2], before[5], before[3], before[4])
    )
    out_part = move(
        early_part[:SHARD_IN],
        lambda yh, z, c, x, yl: (x // 2, (x % 2) * 2 + yl, z % 2, 2 * c + yh, z // 2),
    )
    early_parts = exchange_rep(jnp.concatenate([out_part, early_part[SHARD_IN:]], 0))

    grad_bc = lax.all_to_all(grad_bc, "rep", 0, 0, tiled=True).reshape(N_REP, OWN_BC, PACK).sum(0)
    own_taps = lax.dynamic_slice_in_dim(taps_bc, r * OWN_BC, OWN_BC, 1)
    own_pre = lax.dynamic_slice_in_dim(pre, OWN + r * OWN_BC, OWN_BC, 1).T
    own_conv = lax.dynamic_slice_in_dim(proj, 2 * OWN + r * OWN_BC, OWN_BC, 1).T
    own_conv = own_conv.astype(BF16).astype(F32)
    sig = jax.nn.sigmoid(own_pre)
    grad_pre = grad_bc * (sig * (1.0 + own_pre * (1.0 - sig)))
    positions = jnp.arange(PACK, dtype=jnp.int32)
    segments = segment_at(positions, seg_ends)
    grad_conv_bc = own_taps[CONV - 1][:, None] * grad_pre
    grad_taps_bc = [jnp.sum(own_conv * grad_pre, 1)]
    for later_by in range(1, CONV):
        same = (segment_at(positions + later_by, seg_ends) == segments) & (positions + later_by < PACK)
        later = jnp.concatenate([grad_pre[:, later_by:], jnp.zeros((OWN_BC, later_by), F32)], 1)
        later = later * same.astype(F32)[None, :]
        grad_taps_bc.insert(0, jnp.sum(own_conv * later, 1))
        grad_conv_bc = grad_conv_bc + own_taps[CONV - 1 - later_by][:, None] * later
    grad_bias_bc = jnp.sum(grad_pre, 1)
    grad_tail = jnp.concatenate(
        [
            grad_x,
            grad_conv_bc.T.astype(BF16),
            grad_dtraw[:, :OWN_H],
            jnp.zeros((PACK, TAIL - OWN - OWN_BC - OWN_H), BF16),
        ],
        1,
    )

    grad_tail_own = contract_rows(normed, grad_tail).reshape(2, 4, 2, SHARD_IN, TAIL)
    row = lambda value: jnp.pad(value, (0, OWN - value.shape[0]))[None, :]
    head_columns = jnp.concatenate(
        [grad_gain[0:1]]
        + [grad_sums[1:6]]
        + [row(grad_heads[1, :OWN_H]), row(grad_sums[6].reshape(OWN_H, P_SIZE).sum(1))],
        0,
    )
    bc_columns = jnp.stack(
        [jnp.pad(grad_heads[0, :OWN_H], (0, OWN_BC - OWN_H))]
        + grad_taps_bc
        + [grad_bias_bc, jnp.zeros_like(grad_bias_bc), jnp.zeros_like(grad_bias_bc)],
        0,
    )
    small_own = jnp.concatenate(
        [head_columns, bc_columns, jnp.zeros((8, TAIL - OWN - OWN_BC), F32)], 1
    )
    tail_keep = at(grad_tail_own, place.c, 2)
    tail_got, small_got = received(at(grad_tail_own, 1 - place.c, 2), swap_core, small_own, tail_keep)
    tail_part, small_sum = scatter_ring(tail_keep, tail_got, small_own + small_got, place)

    tail_rows = lax.all_to_all(grad_tail, "rep", 0, 0, tiled=True).reshape(N_REP, ROWS, TAIL)

    def columns(parts):
        return parts.transpose(1, 0, 2).reshape(parts.shape[1], -1)

    rest_rows = jnp.concatenate(
        [
            columns(tail_rows[:, :, OWN : OWN + OWN_BC]),
            jnp.zeros((ROWS, 8), BF16),
            columns(tail_rows[:, :, OWN + OWN_BC : OWN + OWN_BC + OWN_H]),
            jnp.zeros((ROWS, N - 8 - H), BF16),
        ],
        1,
    )
    behind_table = jnp.concatenate([behind, place.yl[None]])
    input_grad, grad_gain_in = run_input_grad(
        behind_table, mine_rows, other_rows, tail_rows, rest_rows, full_in, slice_in[:, 1024:1152],
        tokens, cotangent, gain_in,
    )
    grad_gain_in = sum_all(grad_gain_in[0].reshape(12, 128)).reshape(-1)

    block_out = run_block_out(behind_table, mine_rows, other_rows, full_out, tokens, own_live)

    tail_block = jnp.concatenate([tail_part, small_sum], 0)
    tail_parts = lax.all_to_all(
        jnp.broadcast_to(tail_block[None], (N_REP,) + tail_block.shape), "rep", 0, 0, tiled=True
    )
    small_parts = tail_parts[:, SHARD_IN:]

    def channels(row):
        return jnp.concatenate(
            [small_parts[:, row, :OWN].reshape(-1), small_parts[:, row, OWN : OWN + OWN_BC].reshape(-1)]
        )

    grad_small_all = jnp.concatenate(
        [grad_gain_in, small_parts[:, 0, :OWN].reshape(-1)]
        + [channels(row) for row in range(1, 6)]
        + [
            small_parts[:, 0, OWN : OWN + OWN_H].reshape(-1),
            small_parts[:, 6, :OWN_H].reshape(-1),
            small_parts[:, 7, :OWN_H].reshape(-1),
        ]
    )
    grad_small = lax.dynamic_slice_in_dim(grad_small_all, place.f * SHARD_SMALL, SHARD_SMALL, 0)
    grad_dt = columns(tail_parts[:, :SHARD_IN, OWN + OWN_BC : OWN + OWN_BC + OWN_H])
    rest_grad = jnp.pad(columns(tail_parts[:, :SHARD_IN, OWN : OWN + OWN_BC]), ((0, 0), (0, WIDE - 2 * N)))

    in_table = jnp.concatenate([ahead, jnp.arange(N_REP, 2 * N_REP + 1, dtype=jnp.int32)])
    grad_in, new_first_in, new_second_in, new_in = run_adam_in(
        in_table, early_parts, tail_parts, rest_grad, w_in, first_in, second_in
    )
    grad_out, new_first_out, new_second_out, new_out = run_adam_out(
        ahead, early_parts, w_out, first_out, second_out
    )
    new_dt, new_first_dt, new_second_dt = adam_update(
        w_dt, grad_dt, first_dt, second_dt, RATE_MATRIX, WEIGHT_DECAY
    )
    new_small, new_first_small, new_second_small = adam_update(
        small, grad_small, first_small, second_small, RATE_SMALL, 0.0
    )
    return (
        block_out,
        input_grad,
        grad_in,
        grad_dt,
        grad_out,
        grad_small,
        new_first_in,
        new_first_dt,
        new_first_out,
        new_first_small,
        new_second_in,
        new_second_dt,
        new_second_out,
        new_second_small,
        new_in,
        new_dt,
        new_out,
        new_small,
    )


def solution(mesh):
    rows = P(("fsdp", "rep"), None)
    matrix = P("fsdp", None)
    vector = P("fsdp")
    group = (matrix, matrix, matrix, vector)
    return jax.shard_map(
        body,
        mesh=mesh,
        in_specs=(rows, rows, P()) + group * 3,
        out_specs=(rows, rows) + group * 4,
        check_vma=False,
    )
```

```python
from functools import partial

import jax
import jax.numpy as jnp
from jax import lax
from jax.experimental import pallas as pl
from jax.experimental.pallas import tpu as pltpu
from jax.sharding import PartitionSpec as P

D = 1536
H = 48
P_SIZE = 64
N = 128
CONV = 4
STEP = 10
DI = 3072
CHANNELS = DI + 2 * N
SMALL = 21392
N_FSDP = 16
N_REP = 8
ROWS = 256
PACK = 2048
OWN = DI // N_REP
OWN_H = H // N_REP
OWN_BC = 2 * N // N_REP
SHARD_IN = D // N_FSDP
SHARD_OUT = DI // N_FSDP
SHARD_SMALL = SMALL // N_FSDP
WIDE = 384
CHUNK = 128
CHUNKS = PACK // CHUNK
HALF = CHUNKS // 2
VMEM_LIMIT = 60 * 1024 * 1024

NORM_EPS = 1e-05
BETA_ONE = 0.9
BETA_TWO = 0.999
ADAM_EPS = 1e-08
WEIGHT_DECAY = 0.1
RATE_MATRIX = 0.04
RATE_SMALL = 0.4
PRECISE = lax.Precision.HIGHEST
BF16 = jnp.bfloat16
F32 = jnp.float32


def move(value, target):
    pairs = []
    for f in range(N_FSDP):
        for r in range(N_REP):
            yh, z, c, x, yl = target(f // 8, (f // 2) % 4, f % 2, r // 2, r % 2)
            pairs.append((f * N_REP + r, ((yh % 2) * 8 + (z % 4) * 2 + c % 2) * N_REP + (x % 4) * 2 + yl % 2))
    return lax.ppermute(value, ("fsdp", "rep"), pairs)


def along_x(steps):
    return lambda yh, z, c, x, yl: (yh, z, c, x + steps, yl)


def along_z(steps):
    return lambda yh, z, c, x, yl: (yh, z + steps, c, x, yl)


def swap_y(yh, z, c, x, yl):
    return (yh, z, c, x, yl + 1)


def swap_y_hi(yh, z, c, x, yl):
    return (yh + 1, z, c, x, yl)


def swap_core(yh, z, c, x, yl):
    return (yh, z, c + 1, x, yl)


class Place:
    def __init__(self):
        f = lax.axis_index("fsdp")
        r = lax.axis_index("rep")
        self.f, self.r = f, r
        self.yh, self.z, self.c = f // 8, (f // 2) % 4, f % 2
        self.x, self.yl = r // 2, r % 2


def at(value, index, axis=0):
    return lax.dynamic_index_in_dim(value, index, axis, keepdims=False)


def tie(values, *others):
    return lax.optimization_barrier((values, others))[0]


def both(mine, other, second):
    first = jnp.where(second == 0, mine, other)
    last = jnp.where(second == 0, other, mine)
    return jnp.stack([first, last], 0)


def put(out, piece, axis, index):
    starts = [jnp.int32(0)] * out.ndim
    starts[axis] = jnp.int32(index)
    return lax.dynamic_update_slice(out, jnp.expand_dims(piece, axis), tuple(starts))


def in_ring_order(pieces, here, axis):
    first = pieces[0]
    out = jnp.zeros(first.shape[:axis] + (4,) + first.shape[axis:], first.dtype)
    for offset, piece in enumerate(pieces):
        out = put(out, piece, axis, (here + offset) % 4)
    return out


def exchange(value, axis):
    return lax.all_to_all(value, axis, 0, 0, tiled=True)


def share_rep(value):
    return exchange(jnp.broadcast_to(value[None], (N_REP,) + value.shape), "rep")


def sum_rep(value):
    value = value + move(value, swap_y)
    value = value + move(value, lambda yh, z, c, x, yl: (yh, z, c, x ^ 1, yl))
    return value + move(value, lambda yh, z, c, x, yl: (yh, z, c, x ^ 2, yl))


def sum_all(value):
    value = sum_rep(value)
    value = value + move(value, swap_core)
    value = value + move(value, lambda yh, z, c, x, yl: (yh, z ^ 1, c, x, yl))
    value = value + move(value, lambda yh, z, c, x, yl: (yh, z ^ 2, c, x, yl))
    return value + move(value, swap_y_hi)


def adam_update(weight, gradient, moment_one, moment_two, learn_rate, decay_rate):
    moment_one = BETA_ONE * moment_one + (1.0 - BETA_ONE) * gradient
    moment_two = BETA_TWO * moment_two + (1.0 - BETA_TWO) * gradient * gradient
    scaled = (
        moment_one
        / (1.0 - BETA_ONE**STEP)
        / (jnp.sqrt(moment_two / (1.0 - BETA_TWO**STEP)) + ADAM_EPS)
    )
    return (weight - learn_rate * (scaled + decay_rate * weight), moment_one, moment_two)


def contract_rows(left_side, right_side):
    return lax.dot_general(
        left_side, right_side, (((0,), (0,)), ((), ())), preferred_element_type=F32
    )


def contract_cols(left_side, right_side):
    return lax.dot_general(
        left_side, right_side, (((1,), (1,)), ((), ())), preferred_element_type=F32
    )


def matmul(left_side, right_side):
    return jnp.dot(left_side, right_side, preferred_element_type=F32)


def segment_at(positions, seg_ends):
    counted = jnp.sum((positions[:, None] >= seg_ends[None, :]).astype(jnp.int32), axis=1)
    return jnp.where(positions < 0, jnp.int32(-1), counted)


def split_two(value):
    high = value.astype(BF16)
    return high, (value - high.astype(F32)).astype(BF16)


def split_three(value):
    high = value.astype(BF16)
    rest = value - high.astype(F32)
    middle = rest.astype(BF16)
    return high, middle, (rest - middle.astype(F32)).astype(BF16)


def product(left, right, left_dim, right_dim):
    return lax.dot_general(
        left, right, (((left_dim,), (right_dim,)), ((), ())), preferred_element_type=F32
    )


def joined_product(left_parts, right_parts, left_dim=1, right_dim=0):
    left_high, left_low = left_parts
    right_high, right_low = right_parts
    return product(
        jnp.concatenate([left_high, left_high, left_low], left_dim),
        jnp.concatenate([right_high, right_low, right_high], right_dim),
        left_dim,
        right_dim,
    )


def precise_product(left, right, left_dim=1, right_dim=0):
    return joined_product(split_two(left), split_two(right), left_dim, right_dim)


def ones_product(ones, value):
    return product(jnp.concatenate([ones] * 3, 1), jnp.concatenate(split_three(value), 0), 1, 0)


def spread(per_head, lane):
    return jnp.concatenate(
        [
            jnp.where(lane < P_SIZE, per_head[:, 2 * k : 2 * k + 1], per_head[:, 2 * k + 1 : 2 * k + 2])
            for k in range(OWN_H // 2)
        ],
        1,
    )


def head_sums(value):
    column = lax.broadcasted_iota(jnp.int32, (OWN, N), 0)
    head = lax.broadcasted_iota(jnp.int32, (OWN, N), 1)
    members = ((column >= head * P_SIZE) & (column < (head + 1) * P_SIZE)).astype(F32).astype(BF16)
    high, low = split_two(value)
    return product(jnp.concatenate([high, low], 1), jnp.concatenate([members, members], 0), 1, 0)


def two_heads(pair, lane):
    zero = jnp.zeros_like(pair)
    return jnp.concatenate([jnp.where(lane < P_SIZE, pair, zero), jnp.where(lane < P_SIZE, zero, pair)], 0)


def chunk_facts(ends, chunk, dt_pre, par):
    column = lax.broadcasted_iota(jnp.int32, (CHUNK, 1), 0) + chunk * CHUNK
    row = lax.broadcasted_iota(jnp.int32, (1, CHUNK), 1) + chunk * CHUNK

    def segment(position):
        counted = jnp.zeros_like(position)
        for k in range(3):
            counted = counted + (position >= ends[k]).astype(jnp.int32)
        return jnp.where(position < 0, -1, counted)

    def one_segment(position):
        counted = jnp.int32(0)
        for k in range(3):
            counted = counted + (position >= ends[k]).astype(jnp.int32)
        return jnp.where(position < 0, -1, counted)

    here_column, here_row = segment(column), segment(row)
    prior = one_segment(chunk * CHUNK - 1)
    last = one_segment(chunk * CHUNK + CHUNK - 1)
    lane = lax.broadcasted_iota(jnp.int32, (CHUNK, N), 1)
    shifted = dt_pre + par[6:7, :N]
    soft = jnp.maximum(shifted, 0.0) + jnp.log1p(jnp.exp(-jnp.abs(shifted)))
    step = jnp.where(lane < OWN_H, soft, 0.0)
    decay = step * par[7:8, :N]
    tri_row = lax.broadcasted_iota(jnp.int32, (CHUNK, CHUNK), 0)
    tri_column = lax.broadcasted_iota(jnp.int32, (CHUNK, CHUNK), 1)
    lower = (tri_row >= tri_column).astype(F32).astype(BF16)
    upper = (tri_row <= tri_column).astype(F32).astype(BF16)
    total = ones_product(lower, decay)
    entering = (here_column == prior).astype(F32) * jnp.exp(total)
    end = total[CHUNK - 1 : CHUNK]
    leaving = (here_column == last).astype(F32) * jnp.exp(jnp.minimum(end - total, 0.0))
    passing = jnp.where(last == prior, 1.0, 0.0) * jnp.exp(end)
    return dict(
        column=column,
        segment=segment,
        here_column=here_column,
        here_row=here_row,
        lane=lane,
        shifted=shifted,
        step=step,
        decay=decay,
        total=total,
        entering=entering,
        leaving=leaving,
        passing=passing,
        tri_row=tri_row,
        tri_column=tri_column,
        upper=upper,
    )


def forward_kernel(part, ends, proj, par, *refs):
    if part:
        carry_in, refs = refs[3], refs[4:]
    pre_out, mixed_out, state_out, carry_out, extended, state = refs
    chunk = pl.program_id(0) + part * HALF

    @pl.when(pl.program_id(0) == 0)
    def _():
        if part:
            state[...] = carry_in[:N, :OWN]
            extended[0:8, :] = carry_in[N:, :]
        else:
            state[...] = jnp.zeros_like(state)
            extended[0:8, :] = jnp.zeros((8, 640), F32)

    facts = chunk_facts(ends, chunk, proj[:, 1024:1152], par)
    lane = facts["lane"]
    conv = proj[:, OWN:1024].astype(BF16).astype(F32)
    extended[8 : 8 + CHUNK, :] = conv
    pre = par[4:5] + par[3:4] * conv
    for back in range(1, CONV):
        same = (facts["segment"](facts["column"] - back) == facts["here_column"]).astype(F32)
        pre = pre + par[3 - back : 4 - back] * (extended[8 - back : 8 - back + CHUNK, :] * same)
    extended[0:8, :] = extended[CHUNK : CHUNK + 8, :]
    pre_out[...] = pre
    act = pre * jax.nn.sigmoid(pre)
    own_x, state_b, state_c = act[:, :OWN], act[:, OWN : OWN + N], act[:, OWN + N :]
    stepped = own_x * spread(facts["step"], lane)
    b_parts, c_parts = split_two(state_b), split_two(state_c)
    inside = (facts["tri_row"] >= facts["tri_column"]) & (facts["here_column"] == facts["here_row"])
    scores = jnp.where(inside, joined_product(c_parts, b_parts, 1, 1), 0.0)
    total_rows = facts["total"].T
    state_in = state[...]
    state_out[...] = state_in
    outs = []
    for pair in range(OWN_H // 2):
        mixing = []
        for head in (2 * pair, 2 * pair + 1):
            span = facts["total"][:, head : head + 1] - total_rows[head : head + 1, :]
            mixing.append(jnp.exp(jnp.minimum(span, 0.0)) * scores)
        inner = two_heads(stepped[:, pair * N : pair * N + N], lane)
        outs.append(precise_product(jnp.concatenate(mixing, 1), inner))
    scanned = jnp.concatenate(outs, 1) + spread(facts["entering"], lane) * joined_product(
        c_parts, split_two(state_in)
    )
    state[...] = spread(facts["passing"], lane[:1]) * state_in + precise_product(
        state_b.T, stepped * spread(facts["leaving"], lane)
    )
    mixed_out[...] = scanned + par[5:6, :OWN] * own_x

    @pl.when(pl.program_id(0) == HALF - 1)
    def _():
        carry_out[:N, :OWN] = state[...]
        carry_out[:N, OWN:] = jnp.zeros((N, 640 - OWN), F32)
        carry_out[N:, :] = extended[0:8, :]


def run_forward(part, ends, proj, par, before=()):
    here = lambda i: (i + part * HALF, 0)
    chunked = lambda width: pl.BlockSpec((CHUNK, width), here)
    fixed = lambda shape: pl.BlockSpec(shape, lambda i: (0, 0))
    carry = fixed((N + 8, 640))
    return pl.pallas_call(
        partial(forward_kernel, part),
        grid=(HALF,),
        in_specs=[pl.BlockSpec(memory_space=pltpu.SMEM), chunked(1152), fixed((16, 640))]
        + ([pl.BlockSpec(memory_space=pl.ANY)] * 3 + [carry] if part else []),
        out_specs=[chunked(640), chunked(OWN), pl.BlockSpec((N, OWN), here), carry],
        out_shape=[
            jax.ShapeDtypeStruct((PACK, 640), F32),
            jax.ShapeDtypeStruct((PACK, OWN), F32),
            jax.ShapeDtypeStruct((CHUNKS * N, OWN), F32),
            jax.ShapeDtypeStruct((N + 8, 640), F32),
        ],
        input_output_aliases={3: 0, 4: 1, 5: 2} if part else {},
        scratch_shapes=[pltpu.VMEM((CHUNK + 8, 640), F32), pltpu.VMEM((N, OWN), F32)],
        compiler_params=pltpu.CompilerParams(
            dimension_semantics=("arbitrary",), vmem_limit_bytes=VMEM_LIMIT
        ),
        cost_estimate=pl.CostEstimate(flops=8_000_000_000, bytes_accessed=12_000_000, transcendentals=1_500_000),
        name="scan_forward",
    )(ends, proj, par, *before)


def backward_kernel(part, ends, conv_in, dt_in, pre_in, mixed_in, grad_mixed, state_all, par, *refs):
    if part:
        carry_in, sums_in, head_in, refs = refs[3], refs[4], refs[5], refs[6:]
    grad_x, grad_dt, grad_bc, sums, head_acc, carry_out, carried, extended, end_dot = refs
    step_index = pl.program_id(0)
    chunk = CHUNKS - 1 - part * HALF - step_index

    @pl.when(step_index == 0)
    def _():
        if part:
            carried[...] = carry_in[:N, :]
            extended[CHUNK : CHUNK + 8, :] = carry_in[N : N + 8, :]
            end_dot[...] = carry_in[N + 8 :, :N]
            sums[...] = sums_in[...]
            head_acc[...] = head_in[...]
        else:
            carried[...] = jnp.zeros_like(carried)
            extended[CHUNK : CHUNK + 8, :] = jnp.zeros((8, OWN), F32)
            end_dot[...] = jnp.zeros_like(end_dot)
            sums[...] = jnp.zeros_like(sums)
            head_acc[...] = jnp.zeros_like(head_acc)

    facts = chunk_facts(ends, chunk, dt_in[...], par)
    lane = facts["lane"]
    pre = pre_in[...]
    sig = jax.nn.sigmoid(pre)
    act = pre * sig
    own_x, state_b, state_c = act[:, :OWN], act[:, OWN : OWN + N], act[:, OWN + N :]
    step = facts["step"]
    step_wide = spread(step, lane)
    stepped = own_x * step_wide
    skip = par[5:6, :OWN]
    scanned = mixed_in[...] - skip * own_x
    grad_m = grad_mixed[...]
    sums[6:7] += jnp.sum(grad_m * own_x, 0, keepdims=True)

    b_parts, c_parts = split_two(state_b), split_two(state_c)
    inside = (facts["tri_row"] <= facts["tri_column"]) & (facts["here_column"] == facts["here_row"])
    scores = jnp.where(inside, joined_product(b_parts, c_parts, 1, 1), 0.0)
    total_rows = facts["total"].T
    grad_scores = jnp.zeros((CHUNK, CHUNK), F32)
    grad_stepped = []
    for pair in range(OWN_H // 2):
        columns = slice(pair * N, pair * N + N)
        grad_pair = grad_m[:, columns]
        high, low = split_two(grad_pair)
        stepped_parts = split_two(two_heads(stepped[:, columns], lane))
        grad_mixing = joined_product(stepped_parts, (high, low), 1, 1)
        mixing = []
        for k in range(2):
            head = 2 * pair + k
            span = total_rows[head : head + 1, :] - facts["total"][:, head : head + 1]
            decays = jnp.exp(jnp.minimum(span, 0.0))
            mixing.append(decays * scores)
            grad_scores = grad_scores + decays * grad_mixing[k * CHUNK : (k + 1) * CHUNK]
        grad_stepped.append(
            joined_product(
                split_two(jnp.concatenate(mixing, 1)), (two_heads(high, lane), two_heads(low, lane))
            )
        )
    grad_scores = jnp.where(inside, grad_scores, 0.0)
    carry = carried[...]
    carry_parts = split_two(carry)
    leaving = spread(facts["leaving"], lane)
    grad_stepped = jnp.concatenate(grad_stepped, 1) + leaving * joined_product(b_parts, carry_parts)
    state_in = state_all[...]
    entered = spread(facts["entering"], lane) * grad_m
    entered_parts = split_two(entered)
    grad_b = precise_product(grad_scores, state_c) + joined_product(
        split_two(leaving * stepped), carry_parts, 1, 1
    )
    grad_c = precise_product(grad_scores.T, state_b) + joined_product(
        entered_parts, split_two(state_in), 1, 1
    )
    grad_bc[0:N, :] = grad_b.T.astype(BF16)
    grad_bc[N:, :] = grad_c.T.astype(BF16)
    new_carry = spread(facts["passing"], lane[:1]) * carry + joined_product(
        split_two(state_c.T), entered_parts
    )
    carried[...] = new_carry

    grad_step = head_sums(own_x * grad_stepped)
    last_row = lax.broadcasted_iota(jnp.int32, (CHUNK, N), 0) == CHUNK - 1
    grad_total = head_sums(grad_m * scanned) - step * grad_step
    grad_total = grad_total + jnp.where(last_row, end_dot[0:1, :], 0.0)
    grad_decay = ones_product(facts["upper"], grad_total)
    end_dot[...] = head_sums(
        jnp.broadcast_to(jnp.sum(new_carry * state_in, 0, keepdims=True), (8, OWN))
    )
    grad_pre_dt = (grad_step + grad_decay * par[7:8, :N]) * jax.nn.sigmoid(facts["shifted"])
    grad_pre_dt = jnp.where(lane < OWN_H, grad_pre_dt, 0.0)
    grad_dt[...] = grad_pre_dt.astype(BF16)
    head_acc[0:1] += jnp.sum(grad_pre_dt, 0, keepdims=True)
    head_acc[1:2] += jnp.sum(grad_decay * facts["decay"], 0, keepdims=True)

    sig_x, pre_x = sig[:, :OWN], pre[:, :OWN]
    grad_pre = (step_wide * grad_stepped + skip * grad_m) * (sig_x * (1.0 + pre_x * (1.0 - sig_x)))
    extended[0:CHUNK, :] = grad_pre
    conv = conv_in[...].astype(BF16).astype(F32)
    sums[5:6] += jnp.sum(grad_pre, 0, keepdims=True)
    sums[4:5] += jnp.sum(conv * grad_pre, 0, keepdims=True)
    grad_conv = par[3:4, :OWN] * grad_pre
    for ahead in range(1, CONV):
        same = (facts["segment"](facts["column"] + ahead) == facts["here_column"]).astype(F32)
        later = extended[ahead : ahead + CHUNK, :] * same
        sums[4 - ahead : 5 - ahead] += jnp.sum(conv * later, 0, keepdims=True)
        grad_conv = grad_conv + par[3 - ahead : 4 - ahead, :OWN] * later
    extended[CHUNK : CHUNK + 8, :] = extended[0:8, :]
    grad_x[...] = grad_conv.astype(BF16)

    @pl.when(step_index == HALF - 1)
    def _():
        carry_out[:N, :] = carried[...]
        carry_out[N : N + 8, :] = extended[CHUNK : CHUNK + 8, :]
        carry_out[N + 8 :, :N] = end_dot[...]
        carry_out[N + 8 :, N:] = jnp.zeros((8, OWN - N), F32)


def run_backward(part, ends, proj, pre, mixed, grad_mixed, states, par, before=()):
    last = CHUNKS - 1 - part * HALF
    chunked = lambda width, column=0: pl.BlockSpec((CHUNK, width), lambda i: (last - i, column))
    fixed = lambda shape: pl.BlockSpec(shape, lambda i: (0, 0))
    carry = [fixed((N + 16, OWN)), fixed((8, OWN)), fixed((8, N))]
    return pl.pallas_call(
        partial(backward_kernel, part),
        grid=(HALF,),
        in_specs=[
            pl.BlockSpec(memory_space=pltpu.SMEM),
            chunked(OWN, 1),
            chunked(N, 8),
            chunked(640),
            chunked(OWN),
            chunked(OWN),
            pl.BlockSpec((N, OWN), lambda i: (last - i, 0)),
            fixed((16, 640)),
        ]
        + ([pl.BlockSpec(memory_space=pl.ANY)] * 3 + carry if part else []),
        out_specs=[
            chunked(OWN),
            chunked(N),
            pl.BlockSpec((2 * N, CHUNK), lambda i: (0, last - i)),
            carry[1],
            carry[2],
            carry[0],
        ],
        out_shape=[
            jax.ShapeDtypeStruct((PACK, OWN), BF16),
            jax.ShapeDtypeStruct((PACK, N), BF16),
            jax.ShapeDtypeStruct((2 * N, PACK), BF16),
            jax.ShapeDtypeStruct((8, OWN), F32),
            jax.ShapeDtypeStruct((8, N), F32),
            jax.ShapeDtypeStruct((N + 16, OWN), F32),
        ],
        input_output_aliases={8: 0, 9: 1, 10: 2} if part else {},
        scratch_shapes=[
            pltpu.VMEM((N, OWN), F32),
            pltpu.VMEM((CHUNK + 8, OWN), F32),
            pltpu.VMEM((8, N), F32),
        ],
        compiler_params=pltpu.CompilerParams(
            dimension_semantics=("arbitrary",), vmem_limit_bytes=VMEM_LIMIT
        ),
        cost_estimate=pl.CostEstimate(flops=12_000_000_000, bytes_accessed=16_000_000, transcendentals=3_000_000),
        name="scan_backward",
    )(ends, proj, proj, pre, mixed, grad_mixed, states, par, *before)


PARTS = (1, 1, 1, 1, 2, 2, 1, 1)
PIECES = sum(PARTS)


def load_block(step, pieces, block):
    first = 0
    for slot, count in enumerate(PARTS):
        refs = pieces[first : first + count]
        first += count

        @pl.when(step == slot)
        def _(refs=refs):
            if len(refs) == 1:
                block[...] = refs[0][...]
            else:
                block[: ROWS // 2, :] = refs[0][...]
                block[ROWS // 2 :, :] = refs[1][...]


def piece_specs():
    return [
        pl.BlockSpec((ROWS // count, D), lambda i, table: (0, 0)) for count in PARTS for _ in range(count)
    ]


def project_kernel(table, *refs):
    pieces, (gain, mine, other, normed_out, proj, dt_out, block, weight) = refs[:PIECES], refs[PIECES:]

    @pl.when(pl.program_id(0) == 0)
    def _():
        core = table[N_REP]
        for k in range(N_FSDP // 2):
            for ref, place in ((mine, 2 * k + core), (other, 2 * k + 1 - core)):
                weight[pl.ds(pl.multiple_of(place * SHARD_IN, SHARD_IN), SHARD_IN), :] = ref[k]
        dt_out[...] = weight[:, 1024:]

    load_block(pl.program_id(0), pieces, block)
    values = block[...].astype(F32)
    scale = lax.rsqrt(jnp.mean(values * values, axis=1, keepdims=True) + NORM_EPS)
    normed = (values * scale * gain[...]).astype(BF16)
    normed_out[...] = normed
    proj[...] = matmul(normed, weight[...])


def run_project(table, pieces, gain, mine, other):
    fixed = lambda shape: pl.BlockSpec(shape, lambda i, table: (0, 0))
    placed = lambda width: pl.BlockSpec((ROWS, width), lambda i, table: (table[i], 0))
    return pl.pallas_call(
        project_kernel,
        grid_spec=pltpu.PrefetchScalarGridSpec(
            num_scalar_prefetch=1,
            grid=(N_REP,),
            in_specs=piece_specs()
            + [fixed((1, D))]
            + [pl.BlockSpec((N_FSDP // 2, SHARD_IN, 3 * WIDE), lambda i, table: (0, 0, 0))] * 2,
            out_specs=[placed(D), placed(3 * WIDE), fixed((D, N))],
            scratch_shapes=[pltpu.VMEM((ROWS, D), BF16), pltpu.VMEM((D, 3 * WIDE), BF16)],
        ),
        out_shape=[
            jax.ShapeDtypeStruct((PACK, D), BF16),
            jax.ShapeDtypeStruct((PACK, 3 * WIDE), F32),
            jax.ShapeDtypeStruct((D, N), BF16),
        ],
        compiler_params=pltpu.CompilerParams(
            dimension_semantics=("arbitrary",), vmem_limit_bytes=VMEM_LIMIT
        ),
        cost_estimate=pl.CostEstimate(flops=7_250_000_000, bytes_accessed=26_000_000, transcendentals=0),
        name="project",
    )(table, *pieces, gain, mine, other)


def row_sums(value):
    folded = value[:, :N] + value[:, N : 2 * N] + value[:, 2 * N :]
    return jnp.sum(folded.T, 0, keepdims=True)


def out_grad_kernel(table, *refs):
    pieces = refs[:PIECES]
    w_out, mixed, gate_in, gain, branch_out, grad_out, sums, block, turned = refs[PIECES:]

    @pl.when(pl.program_id(0) == 0)
    def _():
        turned[...] = w_out[...].T

    load_block(pl.program_id(0), pieces, block)
    branch = block[...]
    branch_out[...] = branch
    total = matmul(branch, turned[...])
    grad_out[...] = total
    gate = gate_in[...]
    gated = mixed[...] * (gate * jax.nn.sigmoid(gate))
    row = lax.broadcasted_iota(jnp.int32, (8, ROWS), 0)
    sums[...] = jnp.where(
        row == 0, row_sums(gated * gated), jnp.where(row == 1, row_sums(total * gain[...] * gated), 0.0)
    )


def run_out_grad(table, pieces, w_out, mixed, proj, gain):
    fixed = lambda shape: pl.BlockSpec(shape, lambda i, table: (0, 0))
    placed = lambda width: pl.BlockSpec((ROWS, width), lambda i, table: (table[i], 0))
    return pl.pallas_call(
        out_grad_kernel,
        grid_spec=pltpu.PrefetchScalarGridSpec(
            num_scalar_prefetch=1,
            grid=(N_REP,),
            in_specs=piece_specs()
            + [pl.BlockSpec((OWN, D), lambda i, table: (table[N_REP], 0))]
            + [placed(OWN), placed(OWN), fixed((1, OWN))],
            out_specs=[placed(D), placed(OWN), pl.BlockSpec((8, ROWS), lambda i, table: (0, table[i]))],
            scratch_shapes=[pltpu.VMEM((ROWS, D), BF16), pltpu.VMEM((D, WIDE), BF16)],
        ),
        out_shape=[
            jax.ShapeDtypeStruct((PACK, D), BF16),
            jax.ShapeDtypeStruct((PACK, OWN), F32),
            jax.ShapeDtypeStruct((8, PACK), F32),
        ],
        compiler_params=pltpu.CompilerParams(
            dimension_semantics=("arbitrary",), vmem_limit_bytes=VMEM_LIMIT
        ),
        cost_estimate=pl.CostEstimate(flops=2_420_000_000, bytes_accessed=23_000_000, transcendentals=800_000),
        name="out_grad",
    )(table, *pieces, w_out, mixed, proj, gain)


def gate_kernel(
    grad_out, mixed_in, gate_in, sums, gain, grad_branch, normed,
    low_out, grad_mixed, total, grad_gain,
):
    step = pl.program_id(0)
    rows = grad_out.shape[0]
    mixed, gate, grad_o = mixed_in[...], gate_in[...], grad_out[...]
    stats = jnp.concatenate([sums[...], jnp.zeros((N - 8, rows), F32)], 0).T
    out_scale = lax.rsqrt(stats[:, 0:1] * (1.0 / DI) + NORM_EPS)
    pull = out_scale * out_scale * out_scale * (stats[:, 1:2] * (1.0 / DI))
    gate_sig = jax.nn.sigmoid(gate)
    silu = gate * gate_sig
    gated = mixed * silu
    unit = gated * out_scale
    low = (unit * gain[...]).astype(BF16)
    grad_gated = out_scale * (grad_o * gain[...]) - gated * pull
    grad_mixed[...] = grad_gated * silu
    grad_z = (grad_gated * mixed * (gate_sig * (1.0 + gate * (1.0 - gate_sig)))).astype(BF16)
    low_out[:, :OWN] = low
    low_out[:, OWN:] = grad_z

    @pl.when(step == 0)
    def _():
        grad_gain[...] = jnp.zeros_like(grad_gain)
        total[...] = jnp.zeros_like(total)

    grad_gain[0:1] += jnp.sum(grad_o * unit, 0, keepdims=True)
    for k in range(4):
        part = product(low, grad_branch[:, k * WIDE : (k + 1) * WIDE], 0, 0)
        for m in range(4):
            total[4 * k + m, :SHARD_IN] += part[m * SHARD_IN : (m + 1) * SHARD_IN]
    part = product(normed[...], grad_z, 0, 0)
    for f in range(N_FSDP):
        total[f, SHARD_IN:] += part[f * SHARD_IN : (f + 1) * SHARD_IN]


def run_gate(grad_out, mixed, proj, sums, gain, grad_branch, normed):
    count = 2 * ROWS
    rows = lambda width: pl.BlockSpec((count, width), lambda i: (i, 0))
    fixed = lambda shape: pl.BlockSpec(shape, lambda i: (0,) * len(shape))
    return pl.pallas_call(
        gate_kernel,
        grid=(PACK // count,),
        in_specs=[
            rows(OWN),
            rows(OWN),
            rows(OWN),
            pl.BlockSpec((8, count), lambda i: (0, i)),
            fixed((1, OWN)),
            rows(D),
            rows(D),
        ],
        out_specs=[rows(2 * OWN), rows(OWN), fixed((N_FSDP, 2 * SHARD_IN, WIDE)), fixed((8, OWN))],
        out_shape=[
            jax.ShapeDtypeStruct((PACK, 2 * OWN), BF16),
            jax.ShapeDtypeStruct((PACK, OWN), F32),
            jax.ShapeDtypeStruct((N_FSDP, 2 * SHARD_IN, WIDE), F32),
            jax.ShapeDtypeStruct((8, OWN), F32),
        ],
        compiler_params=pltpu.CompilerParams(
            dimension_semantics=("arbitrary",), vmem_limit_bytes=VMEM_LIMIT
        ),
        cost_estimate=pl.CostEstimate(flops=4_840_000_000, bytes_accessed=34_000_000, transcendentals=800_000),
        name="gate_backward",
    )(grad_out, mixed, proj, sums, gain, grad_branch, normed)


def block_out_kernel(rows, weight, tokens, live, out):
    step = pl.program_id(0)
    part = matmul(rows[0], weight[...])

    @pl.when(step == 0)
    def _():
        out[...] = part

    @pl.when(step > 0)
    def _():
        out[...] += part

    @pl.when(step == N_REP - 1)
    def _():
        out[...] = tokens[...].astype(F32) + live[...] * out[...]


def run_block_out(rows, weight, tokens, live):
    fixed = lambda shape: pl.BlockSpec(shape, lambda i: (0, 0))
    return pl.pallas_call(
        block_out_kernel,
        grid=(N_REP,),
        in_specs=[
            pl.BlockSpec((1, ROWS, OWN), lambda i: (i, 0, 0)),
            pl.BlockSpec((OWN, D), lambda i: (i, 0)),
            fixed((ROWS, D)),
            fixed((ROWS, 1)),
        ],
        out_specs=fixed((ROWS, D)),
        out_shape=jax.ShapeDtypeStruct((ROWS, D), F32),
        compiler_params=pltpu.CompilerParams(
            dimension_semantics=("arbitrary",), vmem_limit_bytes=VMEM_LIMIT
        ),
        cost_estimate=pl.CostEstimate(flops=2_420_000_000, bytes_accessed=14_000_000, transcendentals=0),
        name="block_out",
    )(rows, weight, tokens, live)


def z_grad_kernel(rows, weight, out):
    part = contract_cols(rows[0], weight[...])

    @pl.when(pl.program_id(0) == 0)
    def _():
        out[...] = part

    @pl.when(pl.program_id(0) > 0)
    def _():
        out[...] += part


def run_z_grad(rows, full_in):
    return pl.pallas_call(
        z_grad_kernel,
        grid=(N_REP,),
        in_specs=[
            pl.BlockSpec((1, ROWS, OWN), lambda i: (i, 0, 1)),
            pl.BlockSpec((D, OWN), lambda i: (0, i)),
        ],
        out_specs=pl.BlockSpec((ROWS, D), lambda i: (0, 0)),
        out_shape=jax.ShapeDtypeStruct((ROWS, D), F32),
        compiler_params=pltpu.CompilerParams(
            dimension_semantics=("arbitrary",), vmem_limit_bytes=VMEM_LIMIT
        ),
        cost_estimate=pl.CostEstimate(flops=2_420_000_000, bytes_accessed=14_000_000, transcendentals=0),
        name="z_grad",
    )(rows, full_in)


def input_grad_kernel(grad_z, rows, rest, w_x, w_bc, w_dt, tokens, cotangent, gain, out, gain_out):
    step = pl.program_id(0)
    part = contract_cols(rows[0], w_x[...])

    @pl.when(step == 0)
    def _():
        out[...] = grad_z[...] + part

    @pl.when(step > 0)
    def _():
        out[...] += part

    @pl.when(step == N_REP - 1)
    def _():
        grad_h = out[...] + contract_cols(rest[:, : 2 * N], w_bc[...]) + contract_cols(rest[:, 2 * N :], w_dt[...])
        values = tokens[...].astype(F32)
        scale = lax.rsqrt(jnp.mean(values * values, axis=1, keepdims=True) + NORM_EPS)
        unit = values * scale
        gain_out[...] = jnp.broadcast_to(jnp.sum(grad_h * unit, 0, keepdims=True), gain_out.shape)
        grad_unit = grad_h * gain[...]
        inner = jnp.mean(grad_unit * unit, axis=1, keepdims=True)
        out[...] = cotangent[...].astype(F32) + scale * (grad_unit - unit * inner)


def run_input_grad(grad_z, rows, rest, full_in, low_dt, tokens, cotangent, gain):
    fixed = lambda shape: pl.BlockSpec(shape, lambda i: (0, 0))
    return pl.pallas_call(
        input_grad_kernel,
        grid=(N_REP,),
        in_specs=[
            fixed((ROWS, D)),
            pl.BlockSpec((1, ROWS, OWN), lambda i: (i, 0, 0)),
            fixed((ROWS, 3 * N)),
            pl.BlockSpec((D, OWN), lambda i: (0, N_REP + i)),
            pl.BlockSpec((D, 2 * N), lambda i: (0, DI // N)),
            fixed((D, N)),
            fixed((ROWS, D)),
            fixed((ROWS, D)),
            fixed((1, D)),
        ],
        out_specs=[fixed((ROWS, D)), fixed((8, D))],
        out_shape=[jax.ShapeDtypeStruct((ROWS, D), F32), jax.ShapeDtypeStruct((8, D), F32)],
        compiler_params=pltpu.CompilerParams(
            dimension_semantics=("arbitrary",), vmem_limit_bytes=VMEM_LIMIT
        ),
        cost_estimate=pl.CostEstimate(flops=2_700_000_000, bytes_accessed=18_000_000, transcendentals=0),
        name="input_grad",
    )(grad_z, rows, rest, full_in, full_in, low_dt, tokens, cotangent, gain)


def adam_step(grad, weight, first, second, grad_out, first_out, second_out, weight_out):
    new_weight, new_first, new_second = adam_update(
        weight[...], grad, first[...], second[...], RATE_MATRIX, WEIGHT_DECAY
    )
    grad_out[...] = grad
    first_out[...] = new_first
    second_out[...] = new_second
    weight_out[...] = new_weight


def adam_in_kernel(early, tail, rest, *refs):
    arrays, grad = refs[:7], refs[7]
    step = pl.program_id(0)
    half = N_REP // 2

    @pl.when(step < half)
    def _():
        grad[:, :WIDE] = early[0, SHARD_IN:]
        grad[:, WIDE:] = early[1, SHARD_IN:]

    @pl.when((step >= half) & (step < 2 * half))
    def _():
        grad[:, :WIDE] = tail[0]
        grad[:, WIDE:] = tail[1]

    @pl.when(step == 2 * half)
    def _():
        grad[...] = rest[...]

    adam_step(grad[...], *arrays)


def run_adam_in(early, tail, rest, weight, first, second):
    half = N_REP // 2
    column = pl.BlockSpec((SHARD_IN, 2 * WIDE), lambda i: (0, i))
    shape = jax.ShapeDtypeStruct(weight.shape, F32)
    return pl.pallas_call(
        adam_in_kernel,
        grid=(2 * half + 1,),
        in_specs=[
            pl.BlockSpec((2, 2 * SHARD_IN, WIDE), lambda i: (jnp.minimum(i, half - 1), 0, 0)),
            pl.BlockSpec((2, SHARD_IN, WIDE), lambda i: (jnp.clip(i - half, 0, half - 1), 0, 0)),
            pl.BlockSpec((SHARD_IN, 2 * WIDE), lambda i: (0, 0)),
            column,
            column,
            column,
        ],
        out_specs=[column] * 4,
        out_shape=[shape] * 4,
        scratch_shapes=[pltpu.VMEM((SHARD_IN, 2 * WIDE), F32)],
        compiler_params=pltpu.CompilerParams(
            dimension_semantics=("arbitrary",), vmem_limit_bytes=VMEM_LIMIT
        ),
        cost_estimate=pl.CostEstimate(flops=10_000_000, bytes_accessed=22_000_000, transcendentals=1_200_000),
        name="adam_in",
    )(early, tail, rest, weight, first, second)


def adam_out_kernel(early, *refs):
    arrays, grad = refs[:7], refs[7]
    for k in range(4):
        grad[:, k * WIDE : (k + 1) * WIDE] = early[k, :SHARD_IN]
    adam_step(grad[...], *arrays)


def run_adam_out(early, weight, first, second):
    part = pl.BlockSpec((SHARD_IN, D), lambda i: (i, 0))
    shape = jax.ShapeDtypeStruct(weight.shape, F32)
    return pl.pallas_call(
        adam_out_kernel,
        grid=(2,),
        in_specs=[pl.BlockSpec((4, 2 * SHARD_IN, WIDE), lambda i: (i, 0, 0))] + [part] * 3,
        out_specs=[part] * 4,
        out_shape=[shape] * 4,
        scratch_shapes=[pltpu.VMEM((SHARD_IN, D), F32)],
        compiler_params=pltpu.CompilerParams(
            dimension_semantics=("arbitrary",), vmem_limit_bytes=VMEM_LIMIT
        ),
        cost_estimate=pl.CostEstimate(flops=5_000_000, bytes_accessed=12_000_000, transcendentals=600_000),
        name="adam_out",
    )(early, weight, first, second)


def body(
    tokens,
    cotangent,
    lengths,
    w_in,
    w_dt,
    w_out,
    small,
    first_in,
    first_dt,
    first_out,
    first_small,
    second_in,
    second_dt,
    second_out,
    second_small,
):
    place = Place()
    r = place.r
    zero = jnp.int32(0)
    pack_lengths = lax.dynamic_slice_in_dim(lengths, place.f, 1, 0)[0]
    seg_ends = jnp.cumsum(pack_lengths)
    own_positions = r * ROWS + jnp.arange(ROWS, dtype=jnp.int32)
    own_live = (segment_at(own_positions, seg_ends) < 3).astype(F32)[:, None]
    slots = jnp.arange(N_REP, dtype=jnp.int32)
    ahead = ((place.x + slots // 2) % 4) * 2 + (place.yl + slots) % 2
    half = ROWS // 2

    in_low = w_in.astype(BF16)
    dt_low = w_dt.astype(BF16)
    full_out = lax.all_gather(w_out.astype(BF16), "fsdp", axis=0, tiled=True)
    full_in = lax.all_gather(tie(in_low, full_out), "fsdp", axis=0, tiled=True)

    small_block = jnp.pad(small.astype(BF16), (0, 16 * N - SHARD_SMALL)).reshape(1, 16, N)
    small_all = exchange(jnp.broadcast_to(small_block, (N_FSDP, 16, N)), "fsdp")
    vector = small_all.reshape(N_FSDP, 16 * N)[:, :SHARD_SMALL].reshape(-1).astype(F32)

    weight_block = jnp.concatenate(
        [
            lax.dynamic_slice_in_dim(in_low, r * OWN, OWN, 1),
            lax.dynamic_slice_in_dim(in_low, DI + r * OWN, OWN, 1),
            in_low[:, 2 * DI :],
            lax.dynamic_slice_in_dim(dt_low, r * OWN_H, OWN_H, 1),
            jnp.zeros((SHARD_IN, 2), BF16),
            dt_low,
            jnp.zeros((SHARD_IN, N - 8 - H), BF16),
        ],
        1,
    )
    from_left = move(tokens, along_x(1))
    from_right = move(tokens, along_x(-1))
    partner = move(tokens, swap_y)
    weight_pair = both(weight_block, move(weight_block, swap_y_hi), place.yh)

    from_left, from_right, weight_pair = lax.optimization_barrier((from_left, from_right, weight_pair))
    far_top = move(from_left[:half], along_x(1))
    far_low = move(from_right[half:], along_x(-1))
    partner_left = move(from_left, swap_y)
    weight_left = move(weight_pair, along_z(1))
    weight_right = move(weight_pair, along_z(-1))

    far_top, far_low, partner, weight_left, weight_right = lax.optimization_barrier(
        (far_top, far_low, partner, weight_left, weight_right)
    )
    partner_right = move(partner, along_x(-1))
    weight_far = jnp.concatenate(
        [move(weight_left[:1], along_z(1)), move(weight_right[1:], along_z(-1))], 0
    )

    partner_right, weight_far, partner_left = lax.optimization_barrier(
        (partner_right, weight_far, partner_left)
    )
    partner_far_top = move(partner_left[:half], along_x(1))
    partner_far_low = move(partner_right[half:], along_x(-1))
    weight_ring = in_ring_order([weight_pair, weight_right, weight_far, weight_left], place.z, 1)
    weight_ring = weight_ring.reshape(N_FSDP // 2, SHARD_IN, 3 * WIDE)
    weight_other = move(weight_ring, swap_core)
    token_pieces = [
        tokens, partner, from_right, partner_right, far_top, far_low,
        partner_far_top, partner_far_low, from_left, partner_left,
    ]

    offset = 0
    gain_in = vector[None, :D]
    offset = D
    gain_row = lax.dynamic_slice_in_dim(vector, offset + r * OWN, OWN, 0)[None, :]
    offset += DI
    taps = vector[offset : offset + (CONV + 1) * CHANNELS].reshape(CONV + 1, CHANNELS)
    offset += (CONV + 1) * CHANNELS
    per_head = vector[offset:].reshape(3, H)
    dt_bias, a_log, d_skip = lax.dynamic_slice_in_dim(per_head, r * OWN_H, OWN_H, 1)
    taps_bc = taps[:, DI:]
    conv_par = jnp.concatenate([lax.dynamic_slice_in_dim(taps, r * OWN, OWN, 1), taps_bc], 1)
    head_par = jnp.stack(
        [
            jnp.pad(jnp.broadcast_to(d_skip[:, None], (OWN_H, P_SIZE)).reshape(-1), (0, 2 * N)),
            jnp.pad(dt_bias, (0, 640 - OWN_H)),
            jnp.pad(-jnp.exp(a_log), (0, 640 - OWN_H)),
        ],
        0,
    )
    par = jnp.concatenate([conv_par, head_par, jnp.zeros((8, 640), F32)], 0)

    branch = (cotangent.astype(F32) * own_live).astype(BF16)
    branch = tie(branch, partner_left, partner_right)
    b_left = move(branch, along_x(1))
    b_right = move(branch, along_x(-1))
    b_partner = move(branch, swap_y)
    core_table = jnp.concatenate([ahead, place.c[None]])
    normed, proj, low_dt = run_project(core_table, token_pieces, gain_in, weight_ring, weight_other)
    b_left, b_right, b_partner, proj = lax.optimization_barrier((b_left, b_right, b_partner, proj))
    b_far_top = move(b_left[:half], along_x(1))
    b_far_low = move(b_right[half:], along_x(-1))
    b_partner_left = move(b_left, swap_y)
    b_partner_right = move(b_partner, along_x(-1))
    before = run_forward(0, seg_ends, proj, par)
    b_partner_left, b_partner_right, before = lax.optimization_barrier((b_partner_left, b_partner_right, before))
    b_partner_far_top = move(b_partner_left[:half], along_x(1))
    b_partner_far_low = move(b_partner_right[half:], along_x(-1))
    pre, mixed, states, _ = run_forward(1, seg_ends, proj, par, before)
    branch_pieces = [
        branch, b_partner, b_right, b_partner_right, b_far_top, b_far_low,
        b_partner_far_top, b_partner_far_low, b_left, b_partner_left,
    ]
    rep_table = jnp.concatenate([ahead, r[None]])
    grad_branch, grad_normed_out, sums = run_out_grad(rep_table, branch_pieces, full_out, mixed, proj, gain_row)
    sums = sum_rep(sums[:2].reshape(32, 128)).reshape(2, PACK)
    sums = jnp.concatenate([sums, jnp.zeros((6, PACK), F32)], 0)

    low_rows, grad_mixed, early, grad_gain = run_gate(
        grad_normed_out, mixed, proj, sums, gain_row, grad_branch, normed
    )

    low_rows = exchange(low_rows.reshape(N_REP, ROWS, 2 * OWN), "rep")
    early = exchange(early, "fsdp")
    before = run_backward(0, seg_ends, proj, pre, mixed, grad_mixed, states, par)
    grad_x, grad_dtraw, grad_bc, grad_sums, grad_heads, _ = run_backward(
        1, seg_ends, proj, pre, mixed, grad_mixed, states, par,
        (before[0], before[1], before[2], before[5], before[3], before[4]),
    )

    grad_bc = exchange(grad_bc, "rep")
    x_rows = exchange(grad_x.reshape(N_REP, ROWS, OWN), "rep")
    grad_x_own = contract_rows(normed, grad_x).reshape(N_FSDP, SHARD_IN, OWN)
    x_part = exchange(grad_x_own, "fsdp")
    block_out = run_block_out(low_rows, full_out, tokens, own_live)
    grad_z_rows = run_z_grad(low_rows, full_in)
    grad_bc, block_out, grad_z_rows = lax.optimization_barrier((grad_bc, block_out, grad_z_rows))
    grad_bc = grad_bc.reshape(N_REP, OWN_BC, PACK).astype(F32).sum(0)
    early = early.sum(0)
    out_part = move(
        early[:SHARD_IN],
        lambda yh, z, c, x, yl: (x // 2, (x % 2) * 2 + yl, z % 2, 2 * c + yh, z // 2),
    )
    early_parts = share_rep(jnp.concatenate([out_part, early[SHARD_IN:]], 0))
    own_taps = lax.dynamic_slice_in_dim(taps_bc, r * OWN_BC, OWN_BC, 1)
    own_pre = lax.dynamic_slice_in_dim(pre, OWN + r * OWN_BC, OWN_BC, 1).T
    own_conv = lax.dynamic_slice_in_dim(proj, 2 * OWN + r * OWN_BC, OWN_BC, 1).T
    own_conv = own_conv.astype(BF16).astype(F32)
    sig = jax.nn.sigmoid(own_pre)
    grad_pre = grad_bc * (sig * (1.0 + own_pre * (1.0 - sig)))
    positions = jnp.arange(PACK, dtype=jnp.int32)
    segments = segment_at(positions, seg_ends)
    grad_conv_bc = own_taps[CONV - 1][:, None] * grad_pre
    grad_taps_bc = [jnp.sum(own_conv * grad_pre, 1)]
    for later_by in range(1, CONV):
        same = (segment_at(positions + later_by, seg_ends) == segments) & (positions + later_by < PACK)
        later = jnp.concatenate([grad_pre[:, later_by:], jnp.zeros((OWN_BC, later_by), F32)], 1)
        later = later * same.astype(F32)[None, :]
        grad_taps_bc.insert(0, jnp.sum(own_conv * later, 1))
        grad_conv_bc = grad_conv_bc + own_taps[CONV - 1 - later_by][:, None] * later
    grad_bias_bc = jnp.sum(grad_pre, 1)
    rest = jnp.concatenate(
        [grad_conv_bc.T.astype(BF16), grad_dtraw[:, :OWN_H], jnp.zeros((PACK, N - OWN_BC - OWN_H), BF16)], 1
    )
    rest_rows = exchange(rest.reshape(N_REP, ROWS, N), "rep")

    row = lambda value: jnp.pad(value, (0, OWN - value.shape[0]))[None, :]
    head_columns = jnp.concatenate(
        [grad_gain[0:1]]
        + [grad_sums[1:6]]
        + [row(grad_heads[1, :OWN_H]), row(grad_sums[6].reshape(OWN_H, P_SIZE).sum(1))],
        0,
    )
    bc_columns = jnp.stack(
        [jnp.pad(grad_heads[0, :OWN_H], (0, OWN_BC - OWN_H))]
        + grad_taps_bc
        + [grad_bias_bc, jnp.zeros_like(grad_bias_bc), jnp.zeros_like(grad_bias_bc)],
        0,
    )
    small_own = jnp.concatenate(
        [
            head_columns[:, :N],
            head_columns[:, N : 2 * N],
            head_columns[:, 2 * N :],
            jnp.pad(bc_columns, ((0, 0), (0, N - OWN_BC))),
        ],
        0,
    )
    grad_rest = contract_rows(normed, rest).reshape(N_FSDP, SHARD_IN, N)
    grad_rest = jnp.concatenate([grad_rest, jnp.broadcast_to(small_own[None], (N_FSDP, 32, N))], 1)
    rest_part = exchange(grad_rest, "fsdp")
    x_parts = share_rep(x_part.sum(0))
    rest_parts = share_rep(rest_part.sum(0))

    def columns(parts):
        return parts.transpose(1, 0, 2).reshape(parts.shape[1], -1)

    rest_rows = jnp.concatenate(
        [
            columns(rest_rows[:, :, :OWN_BC]),
            jnp.zeros((ROWS, 8), BF16),
            columns(rest_rows[:, :, OWN_BC : OWN_BC + OWN_H]),
            jnp.zeros((ROWS, N - 8 - H), BF16),
        ],
        1,
    )
    input_grad, grad_gain_in = run_input_grad(
        grad_z_rows, x_rows, rest_rows, full_in, low_dt, tokens, cotangent, gain_in
    )
    grad_gain_in = sum_all(grad_gain_in[0].reshape(12, 128)).reshape(-1)

    small_parts = rest_parts[:, SHARD_IN:].reshape(N_REP, 4, 8, N)
    small_x = small_parts[:, :3].transpose(2, 0, 1, 3).reshape(8, DI)
    small_bc = small_parts[:, 3].transpose(1, 0, 2)

    def channels(row):
        return jnp.concatenate([small_x[row], small_bc[row, :, :OWN_BC].reshape(-1)])

    grad_small_all = jnp.concatenate(
        [grad_gain_in, small_x[0]]
        + [channels(row) for row in range(1, 6)]
        + [
            small_bc[0, :, :OWN_H].reshape(-1),
            small_parts[:, 0, 6, :OWN_H].reshape(-1),
            small_parts[:, 0, 7, :OWN_H].reshape(-1),
        ]
    )
    grad_small = lax.dynamic_slice_in_dim(grad_small_all, place.f * SHARD_SMALL, SHARD_SMALL, 0)
    grad_dt = columns(rest_parts[:, :SHARD_IN, OWN_BC : OWN_BC + OWN_H])
    rest_grad = jnp.pad(columns(rest_parts[:, :SHARD_IN, :OWN_BC]), ((0, 0), (0, 2 * WIDE - 2 * N)))
    grad_in, new_first_in, new_second_in, new_in = run_adam_in(
        early_parts, x_parts, rest_grad, w_in, first_in, second_in
    )
    grad_out, new_first_out, new_second_out, new_out = run_adam_out(early_parts, w_out, first_out, second_out)
    new_dt, new_first_dt, new_second_dt = adam_update(
        w_dt, grad_dt, first_dt, second_dt, RATE_MATRIX, WEIGHT_DECAY
    )
    new_small, new_first_small, new_second_small = adam_update(
        small, grad_small, first_small, second_small, RATE_SMALL, 0.0
    )
    return (
        block_out,
        input_grad,
        grad_in,
        grad_dt,
        grad_out,
        grad_small,
        new_first_in,
        new_first_dt,
        new_first_out,
        new_first_small,
        new_second_in,
        new_second_dt,
        new_second_out,
        new_second_small,
        new_in,
        new_dt,
        new_out,
        new_small,
    )


def solution(mesh):
    rows = P(("fsdp", "rep"), None)
    matrix = P("fsdp", None)
    vector = P("fsdp")
    group = (matrix, matrix, matrix, vector)
    return jax.shard_map(
        body,
        mesh=mesh,
        in_specs=(rows, rows, P()) + group * 3,
        out_specs=(rows, rows) + group * 4,
        check_vma=False,
    )
```

```python
from functools import partial

import jax
import jax.numpy as jnp
from jax import lax
from jax.experimental import pallas as pl
from jax.experimental.pallas import tpu as pltpu
from jax.sharding import PartitionSpec as P

D = 1536
H = 48
P_SIZE = 64
N = 128
CONV = 4
STEP = 10
DI = 3072
CHANNELS = DI + 2 * N
SMALL = 21392
N_FSDP = 16
N_REP = 8
ROWS = 256
PACK = 2048
OWN = DI // N_REP
OWN_H = H // N_REP
OWN_BC = 2 * N // N_REP
SHARD_IN = D // N_FSDP
SHARD_OUT = DI // N_FSDP
SHARD_SMALL = SMALL // N_FSDP
WIDE = 384
CHUNK = 128
CHUNKS = PACK // CHUNK
HALF = CHUNKS // 2
VMEM_LIMIT = 60 * 1024 * 1024

NORM_EPS = 1e-05
BETA_ONE = 0.9
BETA_TWO = 0.999
ADAM_EPS = 1e-08
WEIGHT_DECAY = 0.1
RATE_MATRIX = 0.04
RATE_SMALL = 0.4
PRECISE = lax.Precision.HIGHEST
BF16 = jnp.bfloat16
F32 = jnp.float32
COST = pl.CostEstimate(flops=1_000_000, bytes_accessed=100_000, transcendentals=0)


def move(value, target):
    pairs = []
    for f in range(N_FSDP):
        for r in range(N_REP):
            yh, z, c, x, yl = target(f // 8, (f // 2) % 4, f % 2, r // 2, r % 2)
            pairs.append((f * N_REP + r, ((yh % 2) * 8 + (z % 4) * 2 + c % 2) * N_REP + (x % 4) * 2 + yl % 2))
    return lax.ppermute(value, ("fsdp", "rep"), pairs)


def along_x(steps):
    return lambda yh, z, c, x, yl: (yh, z, c, x + steps, yl)


def along_z(steps):
    return lambda yh, z, c, x, yl: (yh, z + steps, c, x, yl)


def swap_y(yh, z, c, x, yl):
    return (yh, z, c, x, yl + 1)


def swap_y_hi(yh, z, c, x, yl):
    return (yh + 1, z, c, x, yl)


def swap_core(yh, z, c, x, yl):
    return (yh, z, c + 1, x, yl)


class Place:
    def __init__(self):
        f = lax.axis_index("fsdp")
        r = lax.axis_index("rep")
        self.f, self.r = f, r
        self.yh, self.z, self.c = f // 8, (f // 2) % 4, f % 2
        self.x, self.yl = r // 2, r % 2


def at(value, index, axis=0):
    return lax.dynamic_index_in_dim(value, index, axis, keepdims=False)


def tie(values, *others):
    return lax.optimization_barrier((values, others))[0]


def both(mine, other, second):
    first = jnp.where(second == 0, mine, other)
    last = jnp.where(second == 0, other, mine)
    return jnp.stack([first, last], 0)


def put(out, piece, axis, index):
    starts = [jnp.int32(0)] * out.ndim
    starts[axis] = jnp.int32(index)
    return lax.dynamic_update_slice(out, jnp.expand_dims(piece, axis), tuple(starts))


def swap_shards(value, place):
    other = move(value, lambda yh, z, c, x, yl: (yh + 1, z, c, x, yl + 1))
    return both(value, other, place.yh)


def gather_eight(pair):
    groups = [list(range(8)), list(range(8, 16))]
    out = lax.all_gather(pair, "fsdp", axis=0, tiled=True, axis_index_groups=groups)
    return out.reshape((4, 2) + pair.shape)


def scatter_ring(keep, got, extra, place):
    z_sum = at(keep, place.z, 1) + at(got, place.z, 1)
    found = []
    for step in (1, 3, 2):
        there = (place.z + step) % 4
        found.append(received(at(keep, there, 1) + at(got, there, 1), along_z(step), extra, z_sum))
    z_sum = z_sum + found[0][0] + found[1][0] + found[2][0]
    if extra is not None:
        extra = extra + found[0][1] + found[1][1] + found[2][1]
    mine = at(z_sum, place.yh)
    more, more_extra = received(at(z_sum, 1 - place.yh), swap_y_hi, extra, mine)
    return mine + more, (None if extra is None else extra + more_extra)


def scatter_fsdp(value, extra, place):
    split = value.reshape((2, 4, 2) + value.shape[1:])
    keep = at(split, place.c, 2)
    got, got_extra = received(at(split, 1 - place.c, 2), swap_core, extra, keep)
    return scatter_ring(keep, got, None if extra is None else extra + got_extra, place)


def exchange(value, axis):
    return lax.all_to_all(value, axis, 0, 0, tiled=True)


def share_rep(value):
    return exchange(jnp.broadcast_to(value[None], (N_REP,) + value.shape), "rep")


def sum_rep(value):
    value = value + move(value, swap_y)
    value = value + move(value, lambda yh, z, c, x, yl: (yh, z, c, x ^ 1, yl))
    return value + move(value, lambda yh, z, c, x, yl: (yh, z, c, x ^ 2, yl))


def sum_all(value):
    value = sum_rep(value)
    value = value + move(value, swap_core)
    value = value + move(value, lambda yh, z, c, x, yl: (yh, z ^ 1, c, x, yl))
    value = value + move(value, lambda yh, z, c, x, yl: (yh, z ^ 2, c, x, yl))
    return value + move(value, swap_y_hi)


def with_rows(block, extra):
    width = block.shape[-1]
    flat = block.reshape(-1, width)
    return flat if extra is None else jnp.concatenate([flat, extra], 0)


def received(block, target, base, add_to):
    got = move(with_rows(block, base), target)
    rows = got.shape[0] - (0 if base is None else base.shape[0])
    return got[:rows].reshape(add_to.shape), got[rows:]


def adam_update(weight, gradient, moment_one, moment_two, learn_rate, decay_rate):
    moment_one = BETA_ONE * moment_one + (1.0 - BETA_ONE) * gradient
    moment_two = BETA_TWO * moment_two + (1.0 - BETA_TWO) * gradient * gradient
    scaled = (
        moment_one
        / (1.0 - BETA_ONE**STEP)
        / (jnp.sqrt(moment_two / (1.0 - BETA_TWO**STEP)) + ADAM_EPS)
    )
    return (weight - learn_rate * (scaled + decay_rate * weight), moment_one, moment_two)


def contract_rows(left_side, right_side):
    return lax.dot_general(
        left_side, right_side, (((0,), (0,)), ((), ())), preferred_element_type=F32
    )


def contract_cols(left_side, right_side):
    return lax.dot_general(
        left_side, right_side, (((1,), (1,)), ((), ())), preferred_element_type=F32
    )


def matmul(left_side, right_side):
    return jnp.dot(left_side, right_side, preferred_element_type=F32)


def segment_at(positions, seg_ends):
    counted = jnp.sum((positions[:, None] >= seg_ends[None, :]).astype(jnp.int32), axis=1)
    return jnp.where(positions < 0, jnp.int32(-1), counted)


def split_two(value):
    high = value.astype(BF16)
    return high, (value - high.astype(F32)).astype(BF16)


def split_three(value):
    high = value.astype(BF16)
    rest = value - high.astype(F32)
    middle = rest.astype(BF16)
    return high, middle, (rest - middle.astype(F32)).astype(BF16)


def product(left, right, left_dim, right_dim):
    return lax.dot_general(
        left, right, (((left_dim,), (right_dim,)), ((), ())), preferred_element_type=F32
    )


def joined_product(left_parts, right_parts, left_dim=1, right_dim=0):
    left_high, left_low = left_parts
    right_high, right_low = right_parts
    return product(
        jnp.concatenate([left_high, left_high, left_low], left_dim),
        jnp.concatenate([right_high, right_low, right_high], right_dim),
        left_dim,
        right_dim,
    )


def precise_product(left, right, left_dim=1, right_dim=0):
    return joined_product(split_two(left), split_two(right), left_dim, right_dim)


def ones_product(ones, value):
    return product(jnp.concatenate([ones] * 3, 1), jnp.concatenate(split_three(value), 0), 1, 0)


def spread(per_head, lane):
    return jnp.concatenate(
        [
            jnp.where(lane < P_SIZE, per_head[:, 2 * k : 2 * k + 1], per_head[:, 2 * k + 1 : 2 * k + 2])
            for k in range(OWN_H // 2)
        ],
        1,
    )


def head_sums(value):
    column = lax.broadcasted_iota(jnp.int32, (OWN, N), 0)
    head = lax.broadcasted_iota(jnp.int32, (OWN, N), 1)
    members = ((column >= head * P_SIZE) & (column < (head + 1) * P_SIZE)).astype(F32).astype(BF16)
    high, low = split_two(value)
    return product(jnp.concatenate([high, low], 1), jnp.concatenate([members, members], 0), 1, 0)


def two_heads(pair, lane):
    zero = jnp.zeros_like(pair)
    return jnp.concatenate([jnp.where(lane < P_SIZE, pair, zero), jnp.where(lane < P_SIZE, zero, pair)], 0)


def chunk_facts(ends, chunk, dt_pre, par):
    column = lax.broadcasted_iota(jnp.int32, (CHUNK, 1), 0) + chunk * CHUNK
    row = lax.broadcasted_iota(jnp.int32, (1, CHUNK), 1) + chunk * CHUNK

    def segment(position):
        counted = jnp.zeros_like(position)
        for k in range(3):
            counted = counted + (position >= ends[k]).astype(jnp.int32)
        return jnp.where(position < 0, -1, counted)

    def one_segment(position):
        counted = jnp.int32(0)
        for k in range(3):
            counted = counted + (position >= ends[k]).astype(jnp.int32)
        return jnp.where(position < 0, -1, counted)

    here_column, here_row = segment(column), segment(row)
    prior = one_segment(chunk * CHUNK - 1)
    last = one_segment(chunk * CHUNK + CHUNK - 1)
    lane = lax.broadcasted_iota(jnp.int32, (CHUNK, N), 1)
    shifted = dt_pre + par[6:7, :N]
    soft = jnp.maximum(shifted, 0.0) + jnp.log1p(jnp.exp(-jnp.abs(shifted)))
    step = jnp.where(lane < OWN_H, soft, 0.0)
    decay = step * par[7:8, :N]
    tri_row = lax.broadcasted_iota(jnp.int32, (CHUNK, CHUNK), 0)
    tri_column = lax.broadcasted_iota(jnp.int32, (CHUNK, CHUNK), 1)
    lower = (tri_row >= tri_column).astype(F32).astype(BF16)
    upper = (tri_row <= tri_column).astype(F32).astype(BF16)
    total = ones_product(lower, decay)
    entering = (here_column == prior).astype(F32) * jnp.exp(total)
    end = total[CHUNK - 1 : CHUNK]
    leaving = (here_column == last).astype(F32) * jnp.exp(jnp.minimum(end - total, 0.0))
    passing = jnp.where(last == prior, 1.0, 0.0) * jnp.exp(end)
    return dict(
        column=column,
        segment=segment,
        here_column=here_column,
        here_row=here_row,
        lane=lane,
        shifted=shifted,
        step=step,
        decay=decay,
        total=total,
        entering=entering,
        leaving=leaving,
        passing=passing,
        tri_row=tri_row,
        tri_column=tri_column,
        upper=upper,
    )


def forward_kernel(part, ends, proj, par, *refs):
    if part:
        carry_in, refs = refs[3], refs[4:]
    pre_out, mixed_out, state_out, carry_out, extended, state = refs
    chunk = pl.program_id(0) + part * HALF

    @pl.when(pl.program_id(0) == 0)
    def _():
        if part:
            state[...] = carry_in[:N, :OWN]
            extended[0:8, :] = carry_in[N:, :]
        else:
            state[...] = jnp.zeros_like(state)
            extended[0:8, :] = jnp.zeros((8, 640), F32)

    facts = chunk_facts(ends, chunk, proj[:, 1024:1152], par)
    lane = facts["lane"]
    conv = proj[:, OWN:1024].astype(BF16).astype(F32)
    extended[8 : 8 + CHUNK, :] = conv
    pre = par[4:5] + par[3:4] * conv
    for back in range(1, CONV):
        same = (facts["segment"](facts["column"] - back) == facts["here_column"]).astype(F32)
        pre = pre + par[3 - back : 4 - back] * (extended[8 - back : 8 - back + CHUNK, :] * same)
    extended[0:8, :] = extended[CHUNK : CHUNK + 8, :]
    pre_out[...] = pre
    act = pre * jax.nn.sigmoid(pre)
    own_x, state_b, state_c = act[:, :OWN], act[:, OWN : OWN + N], act[:, OWN + N :]
    stepped = own_x * spread(facts["step"], lane)
    b_parts, c_parts = split_two(state_b), split_two(state_c)
    inside = (facts["tri_row"] >= facts["tri_column"]) & (facts["here_column"] == facts["here_row"])
    scores = jnp.where(inside, joined_product(c_parts, b_parts, 1, 1), 0.0)
    total_rows = facts["total"].T
    state_in = state[...]
    state_out[...] = state_in
    outs = []
    for pair in range(OWN_H // 2):
        mixing = []
        for head in (2 * pair, 2 * pair + 1):
            span = facts["total"][:, head : head + 1] - total_rows[head : head + 1, :]
            mixing.append(jnp.exp(jnp.minimum(span, 0.0)) * scores)
        inner = two_heads(stepped[:, pair * N : pair * N + N], lane)
        outs.append(precise_product(jnp.concatenate(mixing, 1), inner))
    scanned = jnp.concatenate(outs, 1) + spread(facts["entering"], lane) * joined_product(
        c_parts, split_two(state_in)
    )
    state[...] = spread(facts["passing"], lane[:1]) * state_in + precise_product(
        state_b.T, stepped * spread(facts["leaving"], lane)
    )
    mixed_out[...] = scanned + par[5:6, :OWN] * own_x

    @pl.when(pl.program_id(0) == HALF - 1)
    def _():
        carry_out[:N, :OWN] = state[...]
        carry_out[:N, OWN:] = jnp.zeros((N, 640 - OWN), F32)
        carry_out[N:, :] = extended[0:8, :]


def run_forward(part, ends, proj, par, before=()):
    here = lambda i: (i + part * HALF, 0)
    chunked = lambda width: pl.BlockSpec((CHUNK, width), here)
    fixed = lambda shape: pl.BlockSpec(shape, lambda i: (0, 0))
    carry = fixed((N + 8, 640))
    return pl.pallas_call(
        partial(forward_kernel, part),
        grid=(HALF,),
        in_specs=[pl.BlockSpec(memory_space=pltpu.SMEM), chunked(1152), fixed((16, 640))]
        + ([pl.BlockSpec(memory_space=pl.ANY)] * 3 + [carry] if part else []),
        out_specs=[chunked(640), chunked(OWN), pl.BlockSpec((N, OWN), here), carry],
        out_shape=[
            jax.ShapeDtypeStruct((PACK, 640), F32),
            jax.ShapeDtypeStruct((PACK, OWN), F32),
            jax.ShapeDtypeStruct((CHUNKS * N, OWN), F32),
            jax.ShapeDtypeStruct((N + 8, 640), F32),
        ],
        input_output_aliases={3: 0, 4: 1, 5: 2} if part else {},
        scratch_shapes=[pltpu.VMEM((CHUNK + 8, 640), F32), pltpu.VMEM((N, OWN), F32)],
        compiler_params=pltpu.CompilerParams(
            dimension_semantics=("arbitrary",), vmem_limit_bytes=VMEM_LIMIT
        ),
        cost_estimate=COST,
        name="scan_forward",
    )(ends, proj, par, *before)


def backward_kernel(part, ends, conv_in, dt_in, pre_in, mixed_in, grad_mixed, state_all, par, *refs):
    if part:
        carry_in, sums_in, head_in, refs = refs[3], refs[4], refs[5], refs[6:]
    grad_x, grad_dt, grad_bc, sums, head_acc, carry_out, carried, extended, end_dot = refs
    step_index = pl.program_id(0)
    chunk = CHUNKS - 1 - part * HALF - step_index

    @pl.when(step_index == 0)
    def _():
        if part:
            carried[...] = carry_in[:N, :]
            extended[CHUNK : CHUNK + 8, :] = carry_in[N : N + 8, :]
            end_dot[...] = carry_in[N + 8 :, :N]
            sums[...] = sums_in[...]
            head_acc[...] = head_in[...]
        else:
            carried[...] = jnp.zeros_like(carried)
            extended[CHUNK : CHUNK + 8, :] = jnp.zeros((8, OWN), F32)
            end_dot[...] = jnp.zeros_like(end_dot)
            sums[...] = jnp.zeros_like(sums)
            head_acc[...] = jnp.zeros_like(head_acc)

    facts = chunk_facts(ends, chunk, dt_in[...], par)
    lane = facts["lane"]
    pre = pre_in[...]
    sig = jax.nn.sigmoid(pre)
    act = pre * sig
    own_x, state_b, state_c = act[:, :OWN], act[:, OWN : OWN + N], act[:, OWN + N :]
    step = facts["step"]
    step_wide = spread(step, lane)
    stepped = own_x * step_wide
    skip = par[5:6, :OWN]
    scanned = mixed_in[...] - skip * own_x
    grad_m = grad_mixed[...]
    sums[6:7] += jnp.sum(grad_m * own_x, 0, keepdims=True)

    b_parts, c_parts = split_two(state_b), split_two(state_c)
    inside = (facts["tri_row"] <= facts["tri_column"]) & (facts["here_column"] == facts["here_row"])
    scores = jnp.where(inside, joined_product(b_parts, c_parts, 1, 1), 0.0)
    total_rows = facts["total"].T
    grad_scores = jnp.zeros((CHUNK, CHUNK), F32)
    grad_stepped = []
    for pair in range(OWN_H // 2):
        columns = slice(pair * N, pair * N + N)
        grad_pair = grad_m[:, columns]
        high, low = split_two(grad_pair)
        stepped_parts = split_two(two_heads(stepped[:, columns], lane))
        grad_mixing = joined_product(stepped_parts, (high, low), 1, 1)
        mixing = []
        for k in range(2):
            head = 2 * pair + k
            span = total_rows[head : head + 1, :] - facts["total"][:, head : head + 1]
            decays = jnp.exp(jnp.minimum(span, 0.0))
            mixing.append(decays * scores)
            grad_scores = grad_scores + decays * grad_mixing[k * CHUNK : (k + 1) * CHUNK]
        grad_stepped.append(
            joined_product(
                split_two(jnp.concatenate(mixing, 1)), (two_heads(high, lane), two_heads(low, lane))
            )
        )
    grad_scores = jnp.where(inside, grad_scores, 0.0)
    carry = carried[...]
    carry_parts = split_two(carry)
    leaving = spread(facts["leaving"], lane)
    grad_stepped = jnp.concatenate(grad_stepped, 1) + leaving * joined_product(b_parts, carry_parts)
    state_in = state_all[...]
    entered = spread(facts["entering"], lane) * grad_m
    entered_parts = split_two(entered)
    grad_b = precise_product(grad_scores, state_c) + joined_product(
        split_two(leaving * stepped), carry_parts, 1, 1
    )
    grad_c = precise_product(grad_scores.T, state_b) + joined_product(
        entered_parts, split_two(state_in), 1, 1
    )
    grad_bc[0:N, :] = grad_b.T.astype(BF16)
    grad_bc[N:, :] = grad_c.T.astype(BF16)
    new_carry = spread(facts["passing"], lane[:1]) * carry + joined_product(
        split_two(state_c.T), entered_parts
    )
    carried[...] = new_carry

    grad_step = head_sums(own_x * grad_stepped)
    last_row = lax.broadcasted_iota(jnp.int32, (CHUNK, N), 0) == CHUNK - 1
    grad_total = head_sums(grad_m * scanned) - step * grad_step
    grad_total = grad_total + jnp.where(last_row, end_dot[0:1, :], 0.0)
    grad_decay = ones_product(facts["upper"], grad_total)
    end_dot[...] = head_sums(
        jnp.broadcast_to(jnp.sum(new_carry * state_in, 0, keepdims=True), (8, OWN))
    )
    grad_pre_dt = (grad_step + grad_decay * par[7:8, :N]) * jax.nn.sigmoid(facts["shifted"])
    grad_pre_dt = jnp.where(lane < OWN_H, grad_pre_dt, 0.0)
    grad_dt[...] = grad_pre_dt.astype(BF16)
    head_acc[0:1] += jnp.sum(grad_pre_dt, 0, keepdims=True)
    head_acc[1:2] += jnp.sum(grad_decay * facts["decay"], 0, keepdims=True)

    sig_x, pre_x = sig[:, :OWN], pre[:, :OWN]
    grad_pre = (step_wide * grad_stepped + skip * grad_m) * (sig_x * (1.0 + pre_x * (1.0 - sig_x)))
    extended[0:CHUNK, :] = grad_pre
    conv = conv_in[...].astype(BF16).astype(F32)
    sums[5:6] += jnp.sum(grad_pre, 0, keepdims=True)
    sums[4:5] += jnp.sum(conv * grad_pre, 0, keepdims=True)
    grad_conv = par[3:4, :OWN] * grad_pre
    for ahead in range(1, CONV):
        same = (facts["segment"](facts["column"] + ahead) == facts["here_column"]).astype(F32)
        later = extended[ahead : ahead + CHUNK, :] * same
        sums[4 - ahead : 5 - ahead] += jnp.sum(conv * later, 0, keepdims=True)
        grad_conv = grad_conv + par[3 - ahead : 4 - ahead, :OWN] * later
    extended[CHUNK : CHUNK + 8, :] = extended[0:8, :]
    grad_x[...] = grad_conv.astype(BF16)

    @pl.when(step_index == HALF - 1)
    def _():
        carry_out[:N, :] = carried[...]
        carry_out[N : N + 8, :] = extended[CHUNK : CHUNK + 8, :]
        carry_out[N + 8 :, :N] = end_dot[...]
        carry_out[N + 8 :, N:] = jnp.zeros((8, OWN - N), F32)


def run_backward(part, ends, proj, pre, mixed, grad_mixed, states, par, before=()):
    last = CHUNKS - 1 - part * HALF
    chunked = lambda width, column=0: pl.BlockSpec((CHUNK, width), lambda i: (last - i, column))
    fixed = lambda shape: pl.BlockSpec(shape, lambda i: (0, 0))
    carry = [fixed((N + 16, OWN)), fixed((8, OWN)), fixed((8, N))]
    return pl.pallas_call(
        partial(backward_kernel, part),
        grid=(HALF,),
        in_specs=[
            pl.BlockSpec(memory_space=pltpu.SMEM),
            chunked(OWN, 1),
            chunked(N, 8),
            chunked(640),
            chunked(OWN),
            chunked(OWN),
            pl.BlockSpec((N, OWN), lambda i: (last - i, 0)),
            fixed((16, 640)),
        ]
        + ([pl.BlockSpec(memory_space=pl.ANY)] * 3 + carry if part else []),
        out_specs=[
            chunked(OWN),
            chunked(N),
            pl.BlockSpec((2 * N, CHUNK), lambda i: (0, last - i)),
            carry[1],
            carry[2],
            carry[0],
        ],
        out_shape=[
            jax.ShapeDtypeStruct((PACK, OWN), BF16),
            jax.ShapeDtypeStruct((PACK, N), BF16),
            jax.ShapeDtypeStruct((2 * N, PACK), BF16),
            jax.ShapeDtypeStruct((8, OWN), F32),
            jax.ShapeDtypeStruct((8, N), F32),
            jax.ShapeDtypeStruct((N + 16, OWN), F32),
        ],
        input_output_aliases={8: 0, 9: 1, 10: 2} if part else {},
        scratch_shapes=[
            pltpu.VMEM((N, OWN), F32),
            pltpu.VMEM((CHUNK + 8, OWN), F32),
            pltpu.VMEM((8, N), F32),
        ],
        compiler_params=pltpu.CompilerParams(
            dimension_semantics=("arbitrary",), vmem_limit_bytes=VMEM_LIMIT
        ),
        cost_estimate=COST,
        name="scan_backward",
    )(ends, proj, proj, pre, mixed, grad_mixed, states, par, *before)


PARTS = (1, 1, 1, 1, 2, 2, 1, 1)
PIECES = sum(PARTS)
EARLY_SLOTS = (0, 1, 2, 6)
LATE_SLOTS = (3, 4, 5, 7)


def load_block(step, groups, block):
    for slot, refs in enumerate(groups):

        @pl.when(step == slot)
        def _(refs=refs):
            if len(refs) == 1:
                block[...] = refs[0][...]
            else:
                block[: ROWS // 2, :] = refs[0][...]
                block[ROWS // 2 :, :] = refs[1][...]


def grouped(refs, slots):
    groups = []
    for slot in slots:
        groups.append(refs[: PARTS[slot]])
        refs = refs[PARTS[slot] :]
    return groups, refs


def piece_specs(slots):
    return [
        pl.BlockSpec((ROWS // PARTS[slot], D), lambda i, table: (0, 0))
        for slot in slots
        for _ in range(PARTS[slot])
    ]


def project_kernel(slots, table, *refs):
    groups, (gain, shards, *refs) = grouped(refs, slots)
    normed_out, proj, dt_out, block, weight = refs[-5:]

    @pl.when(pl.program_id(0) == 0)
    def _():
        for f in range(N_FSDP):
            weight[f * SHARD_IN : (f + 1) * SHARD_IN, :] = shards[(f // 2) % 4, f % 2, f // 8]
        dt_out[...] = weight[:, 1024:]

    load_block(pl.program_id(0), groups, block)
    values = block[...].astype(F32)
    scale = lax.rsqrt(jnp.mean(values * values, axis=1, keepdims=True) + NORM_EPS)
    normed = (values * scale * gain[...]).astype(BF16)
    normed_out[...] = normed
    proj[...] = matmul(normed, weight[...])


def run_project(slots, table, pieces, gain, shards, before=()):
    fixed = lambda shape: pl.BlockSpec(shape, lambda i, table: (0,) * len(shape))
    placed = lambda width: pl.BlockSpec((ROWS, width), lambda i, table: (table[i], 0))
    count = sum(PARTS[slot] for slot in slots)
    return pl.pallas_call(
        partial(project_kernel, slots),
        grid_spec=pltpu.PrefetchScalarGridSpec(
            num_scalar_prefetch=1,
            grid=(len(slots),),
            in_specs=piece_specs(slots)
            + [fixed((1, D)), fixed(shards.shape)]
            + [pl.BlockSpec(memory_space=pl.ANY)] * len(before),
            out_specs=[placed(D), placed(3 * WIDE), fixed((D, N))],
            scratch_shapes=[pltpu.VMEM((ROWS, D), BF16), pltpu.VMEM((D, 3 * WIDE), BF16)],
        ),
        out_shape=[
            jax.ShapeDtypeStruct((PACK, D), BF16),
            jax.ShapeDtypeStruct((PACK, 3 * WIDE), F32),
            jax.ShapeDtypeStruct((D, N), BF16),
        ],
        input_output_aliases={count + 3 + k: k for k in range(len(before))},
        compiler_params=pltpu.CompilerParams(
            dimension_semantics=("arbitrary",), vmem_limit_bytes=VMEM_LIMIT
        ),
        cost_estimate=COST,
        name="project",
    )(table, *pieces, gain, shards, *before)


def row_sums(value):
    folded = value[:, :N] + value[:, N : 2 * N] + value[:, 2 * N :]
    return jnp.sum(folded.T, 0, keepdims=True)


def out_grad_kernel(table, *refs):
    groups, refs = grouped(refs, range(N_REP))
    w_out, mixed, gate_in, gain, branch_out, grad_out, sums, block, turned = refs

    @pl.when(pl.program_id(0) == 0)
    def _():
        turned[...] = w_out[...].reshape(OWN, D).T

    load_block(pl.program_id(0), groups, block)
    branch = block[...]
    branch_out[...] = branch
    total = matmul(branch, turned[...])
    grad_out[...] = total
    gate = gate_in[...]
    gated = mixed[...] * (gate * jax.nn.sigmoid(gate))
    row = lax.broadcasted_iota(jnp.int32, (8, ROWS), 0)
    sums[...] = jnp.where(
        row == 0, row_sums(gated * gated), jnp.where(row == 1, row_sums(total * gain[...] * gated), 0.0)
    )


def run_out_grad(table, pieces, w_out, mixed, proj, gain):
    fixed = lambda shape: pl.BlockSpec(shape, lambda i, table: (0, 0))
    placed = lambda width: pl.BlockSpec((ROWS, width), lambda i, table: (table[i], 0))
    return pl.pallas_call(
        out_grad_kernel,
        grid_spec=pltpu.PrefetchScalarGridSpec(
            num_scalar_prefetch=1,
            grid=(N_REP,),
            in_specs=piece_specs(range(N_REP))
            + [
                pl.BlockSpec(
                    (1, 2, 1, SHARD_OUT, D), lambda i, table: (table[N_REP] % 4, 0, table[N_REP] // 4, 0, 0)
                )
            ]
            + [placed(OWN), placed(OWN), fixed((1, OWN))],
            out_specs=[placed(D), placed(OWN), pl.BlockSpec((8, ROWS), lambda i, table: (0, table[i]))],
            scratch_shapes=[pltpu.VMEM((ROWS, D), BF16), pltpu.VMEM((D, WIDE), BF16)],
        ),
        out_shape=[
            jax.ShapeDtypeStruct((PACK, D), BF16),
            jax.ShapeDtypeStruct((PACK, OWN), F32),
            jax.ShapeDtypeStruct((8, PACK), F32),
        ],
        compiler_params=pltpu.CompilerParams(
            dimension_semantics=("arbitrary",), vmem_limit_bytes=VMEM_LIMIT
        ),
        cost_estimate=COST,
        name="out_grad",
    )(table, *pieces, w_out, mixed, proj, gain)


def gate_kernel(
    where, grad_out, mixed_in, gate_in, sums, gain, grad_branch, normed,
    low_out, grad_mixed, keep, give, grad_gain, total,
):
    step = pl.program_id(0)
    rows = grad_out.shape[0]
    mixed, gate, grad_o = mixed_in[...], gate_in[...], grad_out[...]
    stats = jnp.concatenate([sums[...], jnp.zeros((N - 8, rows), F32)], 0).T
    out_scale = lax.rsqrt(stats[:, 0:1] * (1.0 / DI) + NORM_EPS)
    pull = out_scale * out_scale * out_scale * (stats[:, 1:2] * (1.0 / DI))
    gate_sig = jax.nn.sigmoid(gate)
    silu = gate * gate_sig
    gated = mixed * silu
    unit = gated * out_scale
    low = (unit * gain[...]).astype(BF16)
    grad_gated = out_scale * (grad_o * gain[...]) - gated * pull
    grad_mixed[...] = grad_gated * silu
    grad_z = (grad_gated * mixed * (gate_sig * (1.0 + gate * (1.0 - gate_sig)))).astype(BF16)
    low_out[:, :OWN] = low
    low_out[:, OWN:] = grad_z

    @pl.when(step == 0)
    def _():
        grad_gain[...] = jnp.zeros_like(grad_gain)
        total[...] = jnp.zeros_like(total)

    grad_gain[0:1] += jnp.sum(grad_o * unit, 0, keepdims=True)
    for k in range(4):
        part = product(low, grad_branch[:, k * WIDE : (k + 1) * WIDE], 0, 0)
        for m in range(4):
            total[4 * k + m, :SHARD_IN] += part[m * SHARD_IN : (m + 1) * SHARD_IN]
    part = product(normed[...], grad_z, 0, 0)
    for f in range(N_FSDP):
        total[f, SHARD_IN:] += part[f * SHARD_IN : (f + 1) * SHARD_IN]

    @pl.when(step == pl.num_programs(0) - 1)
    def _():
        for k in range(N_FSDP // 2):
            keep[k] = total[2 * k + where[0]]
            give[k] = total[2 * k + 1 - where[0]]


def run_gate(where, grad_out, mixed, proj, sums, gain, grad_branch, normed):
    count = 2 * ROWS
    rows = lambda width: pl.BlockSpec((count, width), lambda i: (i, 0))
    fixed = lambda shape: pl.BlockSpec(shape, lambda i: (0,) * len(shape))
    half = (N_FSDP // 2, 2 * SHARD_IN, WIDE)
    return pl.pallas_call(
        gate_kernel,
        grid=(PACK // count,),
        in_specs=[
            pl.BlockSpec(memory_space=pltpu.SMEM),
            rows(OWN),
            rows(OWN),
            rows(OWN),
            pl.BlockSpec((8, count), lambda i: (0, i)),
            fixed((1, OWN)),
            rows(D),
            rows(D),
        ],
        out_specs=[rows(2 * OWN), rows(OWN), fixed(half), fixed(half), fixed((8, OWN))],
        out_shape=[
            jax.ShapeDtypeStruct((PACK, 2 * OWN), BF16),
            jax.ShapeDtypeStruct((PACK, OWN), F32),
            jax.ShapeDtypeStruct(half, F32),
            jax.ShapeDtypeStruct(half, F32),
            jax.ShapeDtypeStruct((8, OWN), F32),
        ],
        scratch_shapes=[pltpu.VMEM((N_FSDP, 2 * SHARD_IN, WIDE), F32)],
        compiler_params=pltpu.CompilerParams(
            dimension_semantics=("arbitrary",), vmem_limit_bytes=VMEM_LIMIT
        ),
        cost_estimate=COST,
        name="gate_backward",
    )(where, grad_out, mixed, proj, sums, gain, grad_branch, normed)


def block_out_kernel(rows, weight, tokens, live, out):
    step = pl.program_id(0)
    part = matmul(rows[0], weight[...].reshape(OWN, D))

    @pl.when(step == 0)
    def _():
        out[...] = part

    @pl.when(step > 0)
    def _():
        out[...] += part

    @pl.when(step == N_REP - 1)
    def _():
        out[...] = tokens[...].astype(F32) + live[...] * out[...]


def run_block_out(rows, weight, tokens, live):
    fixed = lambda shape: pl.BlockSpec(shape, lambda i: (0, 0))
    return pl.pallas_call(
        block_out_kernel,
        grid=(N_REP,),
        in_specs=[
            pl.BlockSpec((1, ROWS, OWN), lambda i: (i, 0, 0)),
            pl.BlockSpec((1, 2, 1, SHARD_OUT, D), lambda i: (i % 4, 0, i // 4, 0, 0)),
            fixed((ROWS, D)),
            fixed((ROWS, 1)),
        ],
        out_specs=fixed((ROWS, D)),
        out_shape=jax.ShapeDtypeStruct((ROWS, D), F32),
        compiler_params=pltpu.CompilerParams(
            dimension_semantics=("arbitrary",), vmem_limit_bytes=VMEM_LIMIT
        ),
        cost_estimate=COST,
        name="block_out",
    )(rows, weight, tokens, live)


def turned_part(weight, rows):
    return product(weight[...].reshape(D, weight.shape[-1]), rows, 1, 1)


def z_grad_kernel(rows, weight, out):
    part = turned_part(weight, rows[0])

    @pl.when(pl.program_id(0) == 0)
    def _():
        out[...] = part

    @pl.when(pl.program_id(0) > 0)
    def _():
        out[...] += part


def columns_of(full_in, width, index):
    return pl.BlockSpec(full_in.shape[:-1] + (width,), lambda i: (0, 0, 0, 0, index(i)))


def run_z_grad(rows, full_in):
    return pl.pallas_call(
        z_grad_kernel,
        grid=(N_REP,),
        in_specs=[
            pl.BlockSpec((1, ROWS, OWN), lambda i: (i, 0, 1)),
            columns_of(full_in, OWN, lambda i: i),
        ],
        out_specs=pl.BlockSpec((D, ROWS), lambda i: (0, 0)),
        out_shape=jax.ShapeDtypeStruct((D, ROWS), F32),
        compiler_params=pltpu.CompilerParams(
            dimension_semantics=("arbitrary",), vmem_limit_bytes=VMEM_LIMIT
        ),
        cost_estimate=COST,
        name="z_grad",
    )(rows, full_in)


def input_grad_kernel(
    grad_z, rows, rest, w_x, w_bc, low_dt, tokens, cotangent, gain, out, gain_out, total, ordered
):
    step = pl.program_id(0)
    part = turned_part(w_x, rows[0])

    @pl.when(step == 0)
    def _():
        total[...] = grad_z[...] + part

    @pl.when(step > 0)
    def _():
        total[...] += part

    @pl.when(step == N_REP - 1)
    def _():
        total[...] += turned_part(w_bc, rest[:, : 2 * N])
        for f in range(N_FSDP):
            start = (((f // 2) % 4 * 2 + f % 2) * 2 + f // 8) * SHARD_IN
            ordered[f * SHARD_IN : (f + 1) * SHARD_IN, :] = total[start : start + SHARD_IN, :]
        grad_h = (ordered[...] + product(low_dt[...], rest[:, 2 * N :], 1, 1)).T
        values = tokens[...].astype(F32)
        scale = lax.rsqrt(jnp.mean(values * values, axis=1, keepdims=True) + NORM_EPS)
        unit = values * scale
        gain_out[...] = jnp.broadcast_to(jnp.sum(grad_h * unit, 0, keepdims=True), gain_out.shape)
        grad_unit = grad_h * gain[...]
        inner = jnp.mean(grad_unit * unit, axis=1, keepdims=True)
        out[...] = cotangent[...].astype(F32) + scale * (grad_unit - unit * inner)


def run_input_grad(grad_z, rows, rest, full_in, low_dt, tokens, cotangent, gain):
    fixed = lambda shape: pl.BlockSpec(shape, lambda i: (0, 0))
    return pl.pallas_call(
        input_grad_kernel,
        grid=(N_REP,),
        in_specs=[
            fixed((D, ROWS)),
            pl.BlockSpec((1, ROWS, OWN), lambda i: (i, 0, 0)),
            fixed((ROWS, 3 * N)),
            columns_of(full_in, OWN, lambda i: N_REP + i),
            columns_of(full_in, 2 * N, lambda i: DI // N),
            fixed((D, N)),
            fixed((ROWS, D)),
            fixed((ROWS, D)),
            fixed((1, D)),
        ],
        out_specs=[fixed((ROWS, D)), fixed((8, D))],
        out_shape=[jax.ShapeDtypeStruct((ROWS, D), F32), jax.ShapeDtypeStruct((8, D), F32)],
        scratch_shapes=[pltpu.VMEM((D, ROWS), F32), pltpu.VMEM((D, ROWS), F32)],
        compiler_params=pltpu.CompilerParams(
            dimension_semantics=("arbitrary",), vmem_limit_bytes=VMEM_LIMIT
        ),
        cost_estimate=COST,
        name="input_grad",
    )(grad_z, rows, rest, full_in, full_in, low_dt, tokens, cotangent, gain)


def adam_step(grad, weight, first, second, grad_out, first_out, second_out, weight_out):
    new_weight, new_first, new_second = adam_update(
        weight[...], grad, first[...], second[...], RATE_MATRIX, WEIGHT_DECAY
    )
    grad_out[...] = grad
    first_out[...] = new_first
    second_out[...] = new_second
    weight_out[...] = new_weight


def adam_in_kernel(early, tail, rest, *refs):
    arrays, grad = refs[:7], refs[7]
    step = pl.program_id(0)
    half = N_REP // 2

    @pl.when(step < half)
    def _():
        grad[:, :WIDE] = early[0, SHARD_IN:]
        grad[:, WIDE:] = early[1, SHARD_IN:]

    @pl.when((step >= half) & (step < 2 * half))
    def _():
        grad[:, :WIDE] = tail[0]
        grad[:, WIDE:] = tail[1]

    @pl.when(step == 2 * half)
    def _():
        grad[...] = rest[...]

    adam_step(grad[...], *arrays)


def run_adam_in(early, tail, rest, weight, first, second):
    half = N_REP // 2
    column = pl.BlockSpec((SHARD_IN, 2 * WIDE), lambda i: (0, i))
    shape = jax.ShapeDtypeStruct(weight.shape, F32)
    return pl.pallas_call(
        adam_in_kernel,
        grid=(2 * half + 1,),
        in_specs=[
            pl.BlockSpec((2, 2 * SHARD_IN, WIDE), lambda i: (jnp.minimum(i, half - 1), 0, 0)),
            pl.BlockSpec((2, SHARD_IN, WIDE), lambda i: (jnp.clip(i - half, 0, half - 1), 0, 0)),
            pl.BlockSpec((SHARD_IN, 2 * WIDE), lambda i: (0, 0)),
            column,
            column,
            column,
        ],
        out_specs=[column] * 4,
        out_shape=[shape] * 4,
        scratch_shapes=[pltpu.VMEM((SHARD_IN, 2 * WIDE), F32)],
        compiler_params=pltpu.CompilerParams(
            dimension_semantics=("arbitrary",), vmem_limit_bytes=VMEM_LIMIT
        ),
        cost_estimate=COST,
        name="adam_in",
    )(early, tail, rest, weight, first, second)


def adam_out_kernel(early, *refs):
    arrays, grad = refs[:7], refs[7]
    for k in range(4):
        grad[:, k * WIDE : (k + 1) * WIDE] = early[k, :SHARD_IN]
    adam_step(grad[...], *arrays)


def run_adam_out(early, weight, first, second):
    part = pl.BlockSpec((SHARD_IN, D), lambda i: (i, 0))
    shape = jax.ShapeDtypeStruct(weight.shape, F32)
    return pl.pallas_call(
        adam_out_kernel,
        grid=(2,),
        in_specs=[pl.BlockSpec((4, 2 * SHARD_IN, WIDE), lambda i: (i, 0, 0))] + [part] * 3,
        out_specs=[part] * 4,
        out_shape=[shape] * 4,
        scratch_shapes=[pltpu.VMEM((SHARD_IN, D), F32)],
        compiler_params=pltpu.CompilerParams(
            dimension_semantics=("arbitrary",), vmem_limit_bytes=VMEM_LIMIT
        ),
        cost_estimate=COST,
        name="adam_out",
    )(early, weight, first, second)


def body(
    tokens,
    cotangent,
    lengths,
    w_in,
    w_dt,
    w_out,
    small,
    first_in,
    first_dt,
    first_out,
    first_small,
    second_in,
    second_dt,
    second_out,
    second_small,
):
    place = Place()
    r = place.r
    zero = jnp.int32(0)
    pack_lengths = lax.dynamic_slice_in_dim(lengths, place.f, 1, 0)[0]
    seg_ends = jnp.cumsum(pack_lengths)
    own_positions = r * ROWS + jnp.arange(ROWS, dtype=jnp.int32)
    own_live = (segment_at(own_positions, seg_ends) < 3).astype(F32)[:, None]
    slots = jnp.arange(N_REP, dtype=jnp.int32)
    ahead = ((place.x + slots // 2) % 4) * 2 + (place.yl + slots) % 2
    half = ROWS // 2

    in_low = w_in.astype(BF16)
    dt_low = w_dt.astype(BF16)
    out_low = w_out.astype(BF16)

    small_block = jnp.pad(small.astype(BF16), (0, 16 * N - SHARD_SMALL)).reshape(1, 16, N)
    small_all = exchange(jnp.broadcast_to(small_block, (N_FSDP, 16, N)), "fsdp")
    vector = small_all.reshape(N_FSDP, 16 * N)[:, :SHARD_SMALL].reshape(-1).astype(F32)

    def own_columns(rep):
        return jnp.concatenate(
            [
                lax.dynamic_slice_in_dim(in_low, rep * OWN, OWN, 1),
                lax.dynamic_slice_in_dim(in_low, DI + rep * OWN, OWN, 1),
                in_low[:, 2 * DI :],
                lax.dynamic_slice_in_dim(dt_low, rep * OWN_H, OWN_H, 1),
                jnp.zeros((SHARD_IN, 2), BF16),
                dt_low,
                jnp.zeros((SHARD_IN, N - 8 - H), BF16),
            ],
            1,
        )

    other_columns = move(
        own_columns(2 * place.x + 1 - place.yl), lambda yh, z, c, x, yl: (yh + 1, z, c, x, yl + 1)
    )
    own_shards = gather_eight(both(own_columns(r), other_columns, place.yh))

    from_left = move(tokens, along_x(1))
    from_right = move(tokens, along_x(-1))
    partner = move(tokens, swap_y)

    from_left, from_right, partner, out_low = lax.optimization_barrier((from_left, from_right, partner, out_low))
    far_top = move(from_left[:half], along_x(1))
    far_low = move(from_right[half:], along_x(-1))
    partner_left = move(from_left, swap_y)
    partner_right = move(partner, along_x(-1))
    out_pair = swap_shards(out_low, place)

    far_top, far_low, partner_left, partner_right, in_low, out_pair = lax.optimization_barrier(
        (far_top, far_low, partner_left, partner_right, in_low, out_pair)
    )
    partner_far_top = move(partner_left[:half], along_x(1))
    partner_far_low = move(partner_right[half:], along_x(-1))
    in_pair = swap_shards(in_low, place)

    offset = 0
    gain_in = vector[None, :D]
    offset = D
    gain_row = lax.dynamic_slice_in_dim(vector, offset + r * OWN, OWN, 0)[None, :]
    offset += DI
    taps = vector[offset : offset + (CONV + 1) * CHANNELS].reshape(CONV + 1, CHANNELS)
    offset += (CONV + 1) * CHANNELS
    per_head = vector[offset:].reshape(3, H)
    dt_bias, a_log, d_skip = lax.dynamic_slice_in_dim(per_head, r * OWN_H, OWN_H, 1)
    taps_bc = taps[:, DI:]
    conv_par = jnp.concatenate([lax.dynamic_slice_in_dim(taps, r * OWN, OWN, 1), taps_bc], 1)
    head_par = jnp.stack(
        [
            jnp.pad(jnp.broadcast_to(d_skip[:, None], (OWN_H, P_SIZE)).reshape(-1), (0, 2 * N)),
            jnp.pad(dt_bias, (0, 640 - OWN_H)),
            jnp.pad(-jnp.exp(a_log), (0, 640 - OWN_H)),
        ],
        0,
    )
    par = jnp.concatenate([conv_par, head_par, jnp.zeros((8, 640), F32)], 0)

    branch = (cotangent.astype(F32) * own_live).astype(BF16)
    branch = tie(branch, far_top, partner_left)
    b_left = move(branch, along_x(1))
    b_right = move(branch, along_x(-1))
    b_partner = move(branch, swap_y)
    token_pieces = [
        (tokens,), (partner,), (from_right,), (partner_right,), (far_top, far_low),
        (partner_far_top, partner_far_low), (from_left,), (partner_left,),
    ]

    def chosen(slots):
        return jnp.stack([ahead[slot] for slot in slots]), [piece for slot in slots for piece in token_pieces[slot]]

    own_shards, far_top = lax.optimization_barrier((own_shards, far_top))
    full_out = gather_eight(tie(out_pair, own_shards))
    before = run_project(EARLY_SLOTS, *chosen(EARLY_SLOTS), gain_in, own_shards)
    normed, proj, low_dt = run_project(LATE_SLOTS, *chosen(LATE_SLOTS), gain_in, own_shards, before)
    b_left, b_right, b_partner, proj = lax.optimization_barrier((b_left, b_right, b_partner, proj))
    b_far_top = move(b_left[:half], along_x(1))
    b_far_low = move(b_right[half:], along_x(-1))
    b_partner_left = move(b_left, swap_y)
    b_partner_right = move(b_partner, along_x(-1))
    before = run_forward(0, seg_ends, proj, par)
    pre, mixed, states, _ = run_forward(1, seg_ends, proj, par, before)
    b_far_top, b_far_low, b_partner_left, b_partner_right, mixed = lax.optimization_barrier(
        (b_far_top, b_far_low, b_partner_left, b_partner_right, mixed)
    )
    b_partner_far_top = move(b_partner_left[:half], along_x(1))
    b_partner_far_low = move(b_partner_right[half:], along_x(-1))
    branch_pieces = [
        branch, b_partner, b_right, b_partner_right, b_far_top, b_far_low,
        b_partner_far_top, b_partner_far_low, b_left, b_partner_left,
    ]
    rep_table = jnp.concatenate([ahead, r[None]])
    grad_branch, grad_normed_out, sums = run_out_grad(rep_table, branch_pieces, full_out, mixed, proj, gain_row)
    sums = sum_rep(sums[:2].reshape(32, 128)).reshape(2, PACK)
    sums = jnp.concatenate([sums, jnp.zeros((6, PACK), F32)], 0)

    full_in = gather_eight(tie(in_pair, grad_normed_out))

    low_rows, grad_mixed, keep, give, grad_gain = run_gate(
        place.c[None], grad_normed_out, mixed, proj, sums, gain_row, grad_branch, normed
    )

    low_rows = exchange(low_rows.reshape(N_REP, ROWS, 2 * OWN), "rep")
    got = move(give, swap_core)
    before = run_backward(0, seg_ends, proj, pre, mixed, grad_mixed, states, par)
    got, before = lax.optimization_barrier((got, before))
    split = (2, 4, 2 * SHARD_IN, WIDE)
    early, _ = scatter_ring(keep.reshape(split), got.reshape(split), None, place)
    grad_x, grad_dtraw, grad_bc, grad_sums, grad_heads, _ = run_backward(
        1, seg_ends, proj, pre, mixed, grad_mixed, states, par,
        (before[0], before[1], before[2], before[5], before[3], before[4]),
    )
    low_rows, early, grad_bc, grad_x = lax.optimization_barrier((low_rows, early, grad_bc, grad_x))

    grad_bc = exchange(grad_bc, "rep")
    grad_x_own = contract_rows(normed, grad_x).reshape(N_FSDP, SHARD_IN, OWN)
    x_part, _ = scatter_fsdp(grad_x_own, None, place)
    block_out = run_block_out(low_rows, full_out, tokens, own_live)
    grad_bc, block_out, grad_x, grad_x_own = lax.optimization_barrier((grad_bc, block_out, grad_x, grad_x_own))
    x_rows = exchange(grad_x.reshape(N_REP, ROWS, OWN), "rep")
    grad_z_rows = run_z_grad(low_rows, full_in)
    grad_bc = grad_bc.reshape(N_REP, OWN_BC, PACK).astype(F32).sum(0)
    out_part = move(
        early[:SHARD_IN],
        lambda yh, z, c, x, yl: (x // 2, (x % 2) * 2 + yl, z % 2, 2 * c + yh, z // 2),
    )
    early = jnp.concatenate([out_part, early[SHARD_IN:]], 0)
    own_taps = lax.dynamic_slice_in_dim(taps_bc, r * OWN_BC, OWN_BC, 1)
    own_pre = lax.dynamic_slice_in_dim(pre, OWN + r * OWN_BC, OWN_BC, 1).T
    own_conv = lax.dynamic_slice_in_dim(proj, 2 * OWN + r * OWN_BC, OWN_BC, 1).T
    own_conv = own_conv.astype(BF16).astype(F32)
    sig = jax.nn.sigmoid(own_pre)
    grad_pre = grad_bc * (sig * (1.0 + own_pre * (1.0 - sig)))
    positions = jnp.arange(PACK, dtype=jnp.int32)
    segments = segment_at(positions, seg_ends)
    grad_conv_bc = own_taps[CONV - 1][:, None] * grad_pre
    grad_taps_bc = [jnp.sum(own_conv * grad_pre, 1)]
    for later_by in range(1, CONV):
        same = (segment_at(positions + later_by, seg_ends) == segments) & (positions + later_by < PACK)
        later = jnp.concatenate([grad_pre[:, later_by:], jnp.zeros((OWN_BC, later_by), F32)], 1)
        later = later * same.astype(F32)[None, :]
        grad_taps_bc.insert(0, jnp.sum(own_conv * later, 1))
        grad_conv_bc = grad_conv_bc + own_taps[CONV - 1 - later_by][:, None] * later
    grad_bias_bc = jnp.sum(grad_pre, 1)
    rest = jnp.concatenate(
        [grad_conv_bc.T.astype(BF16), grad_dtraw[:, :OWN_H], jnp.zeros((PACK, N - OWN_BC - OWN_H), BF16)], 1
    )
    x_rows, rest, grad_z_rows = lax.optimization_barrier((x_rows, rest, grad_z_rows))
    rest_rows = exchange(rest.reshape(N_REP, ROWS, N), "rep")

    row = lambda value: jnp.pad(value, (0, OWN - value.shape[0]))[None, :]
    head_columns = jnp.concatenate(
        [grad_gain[0:1]]
        + [grad_sums[1:6]]
        + [row(grad_heads[1, :OWN_H]), row(grad_sums[6].reshape(OWN_H, P_SIZE).sum(1))],
        0,
    )
    bc_columns = jnp.stack(
        [jnp.pad(grad_heads[0, :OWN_H], (0, OWN_BC - OWN_H))]
        + grad_taps_bc
        + [grad_bias_bc, jnp.zeros_like(grad_bias_bc), jnp.zeros_like(grad_bias_bc)],
        0,
    )
    small_own = jnp.concatenate(
        [
            head_columns[:, :N],
            head_columns[:, N : 2 * N],
            head_columns[:, 2 * N :],
            jnp.pad(bc_columns, ((0, 0), (0, N - OWN_BC))),
        ],
        0,
    )
    grad_rest = contract_rows(normed, rest).reshape(N_FSDP, SHARD_IN, N)
    rest_part, small_sum = scatter_fsdp(grad_rest, small_own, place)
    rest_rows, early = lax.optimization_barrier((rest_rows, early))
    early_parts = share_rep(early)
    def columns(parts):
        return parts.transpose(1, 0, 2).reshape(parts.shape[1], -1)

    rest_rows = jnp.concatenate(
        [
            columns(rest_rows[:, :, :OWN_BC]),
            jnp.zeros((ROWS, 8), BF16),
            columns(rest_rows[:, :, OWN_BC : OWN_BC + OWN_H]),
            jnp.zeros((ROWS, N - 8 - H), BF16),
        ],
        1,
    )
    input_grad, grad_gain_in = run_input_grad(
        grad_z_rows, x_rows, rest_rows, full_in, low_dt, tokens, cotangent, gain_in
    )
    early_parts, input_grad, x_part = lax.optimization_barrier((early_parts, input_grad, x_part))
    x_parts = share_rep(x_part)
    grad_out, new_first_out, new_second_out, new_out = run_adam_out(early_parts, w_out, first_out, second_out)
    rest_block = jnp.concatenate([rest_part, small_sum], 0)
    x_parts, rest_block = lax.optimization_barrier((x_parts, rest_block))
    rest_parts = share_rep(rest_block)
    grad_gain_in = sum_all(grad_gain_in[0].reshape(12, 128)).reshape(-1)

    small_parts = rest_parts[:, SHARD_IN:].reshape(N_REP, 4, 8, N)
    small_x = small_parts[:, :3].transpose(2, 0, 1, 3).reshape(8, DI)
    small_bc = small_parts[:, 3].transpose(1, 0, 2)

    def channels(row):
        return jnp.concatenate([small_x[row], small_bc[row, :, :OWN_BC].reshape(-1)])

    grad_small_all = jnp.concatenate(
        [grad_gain_in, small_x[0]]
        + [channels(row) for row in range(1, 6)]
        + [
            small_bc[0, :, :OWN_H].reshape(-1),
            small_parts[:, 0, 6, :OWN_H].reshape(-1),
            small_parts[:, 0, 7, :OWN_H].reshape(-1),
        ]
    )
    grad_small = lax.dynamic_slice_in_dim(grad_small_all, place.f * SHARD_SMALL, SHARD_SMALL, 0)
    grad_dt = columns(rest_parts[:, :SHARD_IN, OWN_BC : OWN_BC + OWN_H])
    rest_grad = jnp.pad(columns(rest_parts[:, :SHARD_IN, :OWN_BC]), ((0, 0), (0, 2 * WIDE - 2 * N)))
    grad_in, new_first_in, new_second_in, new_in = run_adam_in(
        early_parts, x_parts, rest_grad, w_in, first_in, second_in
    )
    new_dt, new_first_dt, new_second_dt = adam_update(
        w_dt, grad_dt, first_dt, second_dt, RATE_MATRIX, WEIGHT_DECAY
    )
    new_small, new_first_small, new_second_small = adam_update(
        small, grad_small, first_small, second_small, RATE_SMALL, 0.0
    )
    return (
        block_out,
        input_grad,
        grad_in,
        grad_dt,
        grad_out,
        grad_small,
        new_first_in,
        new_first_dt,
        new_first_out,
        new_first_small,
        new_second_in,
        new_second_dt,
        new_second_out,
        new_second_small,
        new_in,
        new_dt,
        new_out,
        new_small,
    )


def solution(mesh):
    rows = P(("fsdp", "rep"), None)
    matrix = P("fsdp", None)
    vector = P("fsdp")
    group = (matrix, matrix, matrix, vector)
    return jax.shard_map(
        body,
        mesh=mesh,
        in_specs=(rows, rows, P()) + group * 3,
        out_specs=(rows, rows) + group * 4,
        check_vma=False,
    )
```

```python
from functools import partial

import jax
import jax.numpy as jnp
from jax import lax
from jax.experimental import pallas as pl
from jax.experimental.pallas import tpu as pltpu
from jax.sharding import PartitionSpec as P

D = 1536
H = 48
P_SIZE = 64
N = 128
CONV = 4
STEP = 10
DI = 3072
CHANNELS = DI + 2 * N
SMALL = 21392
N_FSDP = 16
N_REP = 8
ROWS = 256
PACK = 2048
OWN = DI // N_REP
OWN_H = H // N_REP
OWN_BC = 2 * N // N_REP
SHARD_IN = D // N_FSDP
SHARD_OUT = DI // N_FSDP
SHARD_SMALL = SMALL // N_FSDP
WIDE = 384
CHUNK = 128
CHUNKS = PACK // CHUNK
HALF = CHUNKS // 2
VMEM_LIMIT = 60 * 1024 * 1024

NORM_EPS = 1e-05
BETA_ONE = 0.9
BETA_TWO = 0.999
ADAM_EPS = 1e-08
WEIGHT_DECAY = 0.1
RATE_MATRIX = 0.04
RATE_SMALL = 0.4
PRECISE = lax.Precision.HIGHEST
BF16 = jnp.bfloat16
F32 = jnp.float32
COST = pl.CostEstimate(flops=1_000_000, bytes_accessed=100_000, transcendentals=0)


def move(value, target):
    pairs = []
    for f in range(N_FSDP):
        for r in range(N_REP):
            yh, z, c, x, yl = target(f // 8, (f // 2) % 4, f % 2, r // 2, r % 2)
            pairs.append((f * N_REP + r, ((yh % 2) * 8 + (z % 4) * 2 + c % 2) * N_REP + (x % 4) * 2 + yl % 2))
    return lax.ppermute(value, ("fsdp", "rep"), pairs)


def along_x(steps):
    return lambda yh, z, c, x, yl: (yh, z, c, x + steps, yl)


def along_z(steps):
    return lambda yh, z, c, x, yl: (yh, z + steps, c, x, yl)


def swap_y(yh, z, c, x, yl):
    return (yh, z, c, x, yl + 1)


def swap_y_hi(yh, z, c, x, yl):
    return (yh + 1, z, c, x, yl)


def swap_core(yh, z, c, x, yl):
    return (yh, z, c + 1, x, yl)


class Place:
    def __init__(self):
        f = lax.axis_index("fsdp")
        r = lax.axis_index("rep")
        self.f, self.r = f, r
        self.yh, self.z, self.c = f // 8, (f // 2) % 4, f % 2
        self.x, self.yl = r // 2, r % 2


def at(value, index, axis=0):
    return lax.dynamic_index_in_dim(value, index, axis, keepdims=False)


def tie(values, *others):
    return lax.optimization_barrier((values, others))[0]


def both(mine, other, second):
    first = jnp.where(second == 0, mine, other)
    last = jnp.where(second == 0, other, mine)
    return jnp.stack([first, last], 0)


def put(out, piece, axis, index):
    starts = [jnp.int32(0)] * out.ndim
    starts[axis] = jnp.int32(index)
    return lax.dynamic_update_slice(out, jnp.expand_dims(piece, axis), tuple(starts))


def swap_shards(value, place):
    other = move(value, lambda yh, z, c, x, yl: (yh + 1, z, c, x, yl + 1))
    return both(value, other, place.yh)


def gather_eight(pair):
    groups = [list(range(8)), list(range(8, 16))]
    out = lax.all_gather(pair, "fsdp", axis=0, tiled=True, axis_index_groups=groups)
    return out.reshape((4, 2) + pair.shape)


def scatter_ring(keep, got, extra, place):
    z_sum = at(keep, place.z, 1) + at(got, place.z, 1)
    found = []
    for step in (1, 3, 2):
        there = (place.z + step) % 4
        found.append(received(at(keep, there, 1) + at(got, there, 1), along_z(step), extra, z_sum))
    z_sum = z_sum + found[0][0] + found[1][0] + found[2][0]
    if extra is not None:
        extra = extra + found[0][1] + found[1][1] + found[2][1]
    mine = at(z_sum, place.yh)
    more, more_extra = received(at(z_sum, 1 - place.yh), swap_y_hi, extra, mine)
    return mine + more, (None if extra is None else extra + more_extra)


def scatter_fsdp(value, extra, place):
    split = value.reshape((2, 4, 2) + value.shape[1:])
    keep = at(split, place.c, 2)
    got, got_extra = received(at(split, 1 - place.c, 2), swap_core, extra, keep)
    return scatter_ring(keep, got, None if extra is None else extra + got_extra, place)


def exchange(value, axis):
    return lax.all_to_all(value, axis, 0, 0, tiled=True)


def share_rep(value):
    return exchange(jnp.broadcast_to(value[None], (N_REP,) + value.shape), "rep")


def gather_pairs(value, place):
    pair = both(value, move(value, swap_y), place.yl)
    left = move(pair, along_x(1))
    right = move(pair, along_x(-1))
    return pair, right, move(left[:1], along_x(1)), move(right[1:], along_x(-1)), left


def sum_rep(value):
    value = value + move(value, swap_y)
    value = value + move(value, lambda yh, z, c, x, yl: (yh, z, c, x ^ 1, yl))
    return value + move(value, lambda yh, z, c, x, yl: (yh, z, c, x ^ 2, yl))


def sum_fsdp(value):
    value = value + move(value, swap_core)
    value = value + move(value, lambda yh, z, c, x, yl: (yh, z ^ 1, c, x, yl))
    value = value + move(value, lambda yh, z, c, x, yl: (yh, z ^ 2, c, x, yl))
    return value + move(value, swap_y_hi)


def with_rows(block, extra):
    width = block.shape[-1]
    flat = block.reshape(-1, width)
    return flat if extra is None else jnp.concatenate([flat, extra], 0)


def received(block, target, base, add_to):
    got = move(with_rows(block, base), target)
    rows = got.shape[0] - (0 if base is None else base.shape[0])
    return got[:rows].reshape(add_to.shape), got[rows:]


def adam_update(weight, gradient, moment_one, moment_two, learn_rate, decay_rate):
    moment_one = BETA_ONE * moment_one + (1.0 - BETA_ONE) * gradient
    moment_two = BETA_TWO * moment_two + (1.0 - BETA_TWO) * gradient * gradient
    scaled = (
        moment_one
        / (1.0 - BETA_ONE**STEP)
        / (jnp.sqrt(moment_two / (1.0 - BETA_TWO**STEP)) + ADAM_EPS)
    )
    return (weight - learn_rate * (scaled + decay_rate * weight), moment_one, moment_two)


def contract_rows(left_side, right_side):
    return lax.dot_general(
        left_side, right_side, (((0,), (0,)), ((), ())), preferred_element_type=F32
    )


def contract_cols(left_side, right_side):
    return lax.dot_general(
        left_side, right_side, (((1,), (1,)), ((), ())), preferred_element_type=F32
    )


def matmul(left_side, right_side):
    return jnp.dot(left_side, right_side, preferred_element_type=F32)


def segment_at(positions, seg_ends):
    counted = jnp.sum((positions[:, None] >= seg_ends[None, :]).astype(jnp.int32), axis=1)
    return jnp.where(positions < 0, jnp.int32(-1), counted)


def split_two(value):
    high = value.astype(BF16)
    return high, (value - high.astype(F32)).astype(BF16)


def split_three(value):
    high = value.astype(BF16)
    rest = value - high.astype(F32)
    middle = rest.astype(BF16)
    return high, middle, (rest - middle.astype(F32)).astype(BF16)


def product(left, right, left_dim, right_dim):
    return lax.dot_general(
        left, right, (((left_dim,), (right_dim,)), ((), ())), preferred_element_type=F32
    )


def joined_product(left_parts, right_parts, left_dim=1, right_dim=0):
    left_high, left_low = left_parts
    right_high, right_low = right_parts
    return product(
        jnp.concatenate([left_high, left_high, left_low], left_dim),
        jnp.concatenate([right_high, right_low, right_high], right_dim),
        left_dim,
        right_dim,
    )


def precise_product(left, right, left_dim=1, right_dim=0):
    return joined_product(split_two(left), split_two(right), left_dim, right_dim)


def ones_product(ones, value):
    return product(jnp.concatenate([ones] * 3, 1), jnp.concatenate(split_three(value), 0), 1, 0)


def spread(per_head, lane):
    return jnp.concatenate(
        [
            jnp.where(lane < P_SIZE, per_head[:, 2 * k : 2 * k + 1], per_head[:, 2 * k + 1 : 2 * k + 2])
            for k in range(OWN_H // 2)
        ],
        1,
    )


def head_sums(value):
    column = lax.broadcasted_iota(jnp.int32, (OWN, N), 0)
    head = lax.broadcasted_iota(jnp.int32, (OWN, N), 1)
    members = ((column >= head * P_SIZE) & (column < (head + 1) * P_SIZE)).astype(F32).astype(BF16)
    high, low = split_two(value)
    return product(jnp.concatenate([high, low], 1), jnp.concatenate([members, members], 0), 1, 0)


def two_heads(pair, lane):
    zero = jnp.zeros_like(pair)
    return jnp.concatenate([jnp.where(lane < P_SIZE, pair, zero), jnp.where(lane < P_SIZE, zero, pair)], 0)


def chunk_facts(ends, chunk, dt_pre, par):
    column = lax.broadcasted_iota(jnp.int32, (CHUNK, 1), 0) + chunk * CHUNK
    row = lax.broadcasted_iota(jnp.int32, (1, CHUNK), 1) + chunk * CHUNK

    def segment(position):
        counted = jnp.zeros_like(position)
        for k in range(3):
            counted = counted + (position >= ends[k]).astype(jnp.int32)
        return jnp.where(position < 0, -1, counted)

    def one_segment(position):
        counted = jnp.int32(0)
        for k in range(3):
            counted = counted + (position >= ends[k]).astype(jnp.int32)
        return jnp.where(position < 0, -1, counted)

    here_column, here_row = segment(column), segment(row)
    prior = one_segment(chunk * CHUNK - 1)
    last = one_segment(chunk * CHUNK + CHUNK - 1)
    lane = lax.broadcasted_iota(jnp.int32, (CHUNK, N), 1)
    shifted = dt_pre + par[6:7, :N]
    soft = jnp.maximum(shifted, 0.0) + jnp.log1p(jnp.exp(-jnp.abs(shifted)))
    step = jnp.where(lane < OWN_H, soft, 0.0)
    decay = step * par[7:8, :N]
    tri_row = lax.broadcasted_iota(jnp.int32, (CHUNK, CHUNK), 0)
    tri_column = lax.broadcasted_iota(jnp.int32, (CHUNK, CHUNK), 1)
    lower = (tri_row >= tri_column).astype(F32).astype(BF16)
    upper = (tri_row <= tri_column).astype(F32).astype(BF16)
    total = ones_product(lower, decay)
    entering = (here_column == prior).astype(F32) * jnp.exp(total)
    end = total[CHUNK - 1 : CHUNK]
    leaving = (here_column == last).astype(F32) * jnp.exp(jnp.minimum(end - total, 0.0))
    passing = jnp.where(last == prior, 1.0, 0.0) * jnp.exp(end)
    return dict(
        column=column,
        segment=segment,
        here_column=here_column,
        here_row=here_row,
        lane=lane,
        shifted=shifted,
        step=step,
        decay=decay,
        total=total,
        entering=entering,
        leaving=leaving,
        passing=passing,
        tri_row=tri_row,
        tri_column=tri_column,
        upper=upper,
    )


def forward_kernel(part, ends, proj, par, *refs):
    if part:
        carry_in, refs = refs[3], refs[4:]
    pre_out, mixed_out, state_out, carry_out, extended, state = refs
    chunk = pl.program_id(0) + part * HALF

    @pl.when(pl.program_id(0) == 0)
    def _():
        if part:
            state[...] = carry_in[:N, :OWN]
            extended[0:8, :] = carry_in[N:, :]
        else:
            state[...] = jnp.zeros_like(state)
            extended[0:8, :] = jnp.zeros((8, 640), F32)

    facts = chunk_facts(ends, chunk, proj[:, 1024:1152], par)
    lane = facts["lane"]
    conv = proj[:, OWN:1024].astype(BF16).astype(F32)
    extended[8 : 8 + CHUNK, :] = conv
    pre = par[4:5] + par[3:4] * conv
    for back in range(1, CONV):
        same = (facts["segment"](facts["column"] - back) == facts["here_column"]).astype(F32)
        pre = pre + par[3 - back : 4 - back] * (extended[8 - back : 8 - back + CHUNK, :] * same)
    extended[0:8, :] = extended[CHUNK : CHUNK + 8, :]
    pre_out[...] = pre
    act = pre * jax.nn.sigmoid(pre)
    own_x, state_b, state_c = act[:, :OWN], act[:, OWN : OWN + N], act[:, OWN + N :]
    stepped = own_x * spread(facts["step"], lane)
    b_parts, c_parts = split_two(state_b), split_two(state_c)
    inside = (facts["tri_row"] >= facts["tri_column"]) & (facts["here_column"] == facts["here_row"])
    scores = jnp.where(inside, joined_product(c_parts, b_parts, 1, 1), 0.0)
    total_rows = facts["total"].T
    state_in = state[...]
    state_out[...] = state_in
    outs = []
    for pair in range(OWN_H // 2):
        mixing = []
        for head in (2 * pair, 2 * pair + 1):
            span = facts["total"][:, head : head + 1] - total_rows[head : head + 1, :]
            mixing.append(jnp.exp(jnp.minimum(span, 0.0)) * scores)
        inner = two_heads(stepped[:, pair * N : pair * N + N], lane)
        outs.append(precise_product(jnp.concatenate(mixing, 1), inner))
    scanned = jnp.concatenate(outs, 1) + spread(facts["entering"], lane) * joined_product(
        c_parts, split_two(state_in)
    )
    state[...] = spread(facts["passing"], lane[:1]) * state_in + precise_product(
        state_b.T, stepped * spread(facts["leaving"], lane)
    )
    mixed_out[...] = scanned + par[5:6, :OWN] * own_x

    @pl.when(pl.program_id(0) == HALF - 1)
    def _():
        carry_out[:N, :OWN] = state[...]
        carry_out[:N, OWN:] = jnp.zeros((N, 640 - OWN), F32)
        carry_out[N:, :] = extended[0:8, :]


def run_forward(part, ends, proj, par, before=()):
    here = lambda i: (i + part * HALF, 0)
    chunked = lambda width: pl.BlockSpec((CHUNK, width), here)
    fixed = lambda shape: pl.BlockSpec(shape, lambda i: (0, 0))
    carry = fixed((N + 8, 640))
    return pl.pallas_call(
        partial(forward_kernel, part),
        grid=(HALF,),
        in_specs=[pl.BlockSpec(memory_space=pltpu.SMEM), chunked(1152), fixed((16, 640))]
        + ([pl.BlockSpec(memory_space=pl.ANY)] * 3 + [carry] if part else []),
        out_specs=[chunked(640), chunked(OWN), pl.BlockSpec((N, OWN), here), carry],
        out_shape=[
            jax.ShapeDtypeStruct((PACK, 640), F32),
            jax.ShapeDtypeStruct((PACK, OWN), F32),
            jax.ShapeDtypeStruct((CHUNKS * N, OWN), F32),
            jax.ShapeDtypeStruct((N + 8, 640), F32),
        ],
        input_output_aliases={3: 0, 4: 1, 5: 2} if part else {},
        scratch_shapes=[pltpu.VMEM((CHUNK + 8, 640), F32), pltpu.VMEM((N, OWN), F32)],
        compiler_params=pltpu.CompilerParams(
            dimension_semantics=("arbitrary",), vmem_limit_bytes=VMEM_LIMIT
        ),
        cost_estimate=COST,
        name="scan_forward",
    )(ends, proj, par, *before)


def backward_kernel(part, ends, conv_in, dt_in, pre_in, mixed_in, grad_mixed, state_all, par, *refs):
    if part:
        carry_in, sums_in, head_in, refs = refs[3], refs[4], refs[5], refs[6:]
    grad_x, grad_dt, grad_bc, sums, head_acc, carry_out, carried, extended, end_dot = refs
    step_index = pl.program_id(0)
    chunk = CHUNKS - 1 - part * HALF - step_index

    @pl.when(step_index == 0)
    def _():
        if part:
            carried[...] = carry_in[:N, :]
            extended[CHUNK : CHUNK + 8, :] = carry_in[N : N + 8, :]
            end_dot[...] = carry_in[N + 8 :, :N]
            sums[...] = sums_in[...]
            head_acc[...] = head_in[...]
        else:
            carried[...] = jnp.zeros_like(carried)
            extended[CHUNK : CHUNK + 8, :] = jnp.zeros((8, OWN), F32)
            end_dot[...] = jnp.zeros_like(end_dot)
            sums[...] = jnp.zeros_like(sums)
            head_acc[...] = jnp.zeros_like(head_acc)

    facts = chunk_facts(ends, chunk, dt_in[...], par)
    lane = facts["lane"]
    pre = pre_in[...]
    sig = jax.nn.sigmoid(pre)
    act = pre * sig
    own_x, state_b, state_c = act[:, :OWN], act[:, OWN : OWN + N], act[:, OWN + N :]
    step = facts["step"]
    step_wide = spread(step, lane)
    stepped = own_x * step_wide
    skip = par[5:6, :OWN]
    scanned = mixed_in[...] - skip * own_x
    grad_m = grad_mixed[...]
    sums[6:7] += jnp.sum(grad_m * own_x, 0, keepdims=True)

    b_parts, c_parts = split_two(state_b), split_two(state_c)
    inside = (facts["tri_row"] <= facts["tri_column"]) & (facts["here_column"] == facts["here_row"])
    scores = jnp.where(inside, joined_product(b_parts, c_parts, 1, 1), 0.0)
    total_rows = facts["total"].T
    grad_scores = jnp.zeros((CHUNK, CHUNK), F32)
    grad_stepped = []
    for pair in range(OWN_H // 2):
        columns = slice(pair * N, pair * N + N)
        grad_pair = grad_m[:, columns]
        high, low = split_two(grad_pair)
        stepped_parts = split_two(two_heads(stepped[:, columns], lane))
        grad_mixing = joined_product(stepped_parts, (high, low), 1, 1)
        mixing = []
        for k in range(2):
            head = 2 * pair + k
            span = total_rows[head : head + 1, :] - facts["total"][:, head : head + 1]
            decays = jnp.exp(jnp.minimum(span, 0.0))
            mixing.append(decays * scores)
            grad_scores = grad_scores + decays * grad_mixing[k * CHUNK : (k + 1) * CHUNK]
        grad_stepped.append(
            joined_product(
                split_two(jnp.concatenate(mixing, 1)), (two_heads(high, lane), two_heads(low, lane))
            )
        )
    grad_scores = jnp.where(inside, grad_scores, 0.0)
    carry = carried[...]
    carry_parts = split_two(carry)
    leaving = spread(facts["leaving"], lane)
    grad_stepped = jnp.concatenate(grad_stepped, 1) + leaving * joined_product(b_parts, carry_parts)
    state_in = state_all[...]
    entered = spread(facts["entering"], lane) * grad_m
    entered_parts = split_two(entered)
    grad_b = precise_product(grad_scores, state_c) + joined_product(
        split_two(leaving * stepped), carry_parts, 1, 1
    )
    grad_c = precise_product(grad_scores.T, state_b) + joined_product(
        entered_parts, split_two(state_in), 1, 1
    )
    grad_bc[0:N, :] = grad_b.T.astype(BF16)
    grad_bc[N:, :] = grad_c.T.astype(BF16)
    new_carry = spread(facts["passing"], lane[:1]) * carry + joined_product(
        split_two(state_c.T), entered_parts
    )
    carried[...] = new_carry

    grad_step = head_sums(own_x * grad_stepped)
    last_row = lax.broadcasted_iota(jnp.int32, (CHUNK, N), 0) == CHUNK - 1
    grad_total = head_sums(grad_m * scanned) - step * grad_step
    grad_total = grad_total + jnp.where(last_row, end_dot[0:1, :], 0.0)
    grad_decay = ones_product(facts["upper"], grad_total)
    end_dot[...] = head_sums(
        jnp.broadcast_to(jnp.sum(new_carry * state_in, 0, keepdims=True), (8, OWN))
    )
    grad_pre_dt = (grad_step + grad_decay * par[7:8, :N]) * jax.nn.sigmoid(facts["shifted"])
    grad_pre_dt = jnp.where(lane < OWN_H, grad_pre_dt, 0.0)
    grad_dt[...] = grad_pre_dt.astype(BF16)
    head_acc[0:1] += jnp.sum(grad_pre_dt, 0, keepdims=True)
    head_acc[1:2] += jnp.sum(grad_decay * facts["decay"], 0, keepdims=True)

    sig_x, pre_x = sig[:, :OWN], pre[:, :OWN]
    grad_pre = (step_wide * grad_stepped + skip * grad_m) * (sig_x * (1.0 + pre_x * (1.0 - sig_x)))
    extended[0:CHUNK, :] = grad_pre
    conv = conv_in[...].astype(BF16).astype(F32)
    sums[5:6] += jnp.sum(grad_pre, 0, keepdims=True)
    sums[4:5] += jnp.sum(conv * grad_pre, 0, keepdims=True)
    grad_conv = par[3:4, :OWN] * grad_pre
    for ahead in range(1, CONV):
        same = (facts["segment"](facts["column"] + ahead) == facts["here_column"]).astype(F32)
        later = extended[ahead : ahead + CHUNK, :] * same
        sums[4 - ahead : 5 - ahead] += jnp.sum(conv * later, 0, keepdims=True)
        grad_conv = grad_conv + par[3 - ahead : 4 - ahead, :OWN] * later
    extended[CHUNK : CHUNK + 8, :] = extended[0:8, :]
    grad_x[...] = grad_conv.astype(BF16)

    @pl.when(step_index == HALF - 1)
    def _():
        carry_out[:N, :] = carried[...]
        carry_out[N : N + 8, :] = extended[CHUNK : CHUNK + 8, :]
        carry_out[N + 8 :, :N] = end_dot[...]
        carry_out[N + 8 :, N:] = jnp.zeros((8, OWN - N), F32)


def run_backward(part, ends, proj, pre, mixed, grad_mixed, states, par, before=()):
    last = CHUNKS - 1 - part * HALF
    chunked = lambda width, column=0: pl.BlockSpec((CHUNK, width), lambda i: (last - i, column))
    fixed = lambda shape: pl.BlockSpec(shape, lambda i: (0, 0))
    carry = [fixed((N + 16, OWN)), fixed((8, OWN)), fixed((8, N))]
    return pl.pallas_call(
        partial(backward_kernel, part),
        grid=(HALF,),
        in_specs=[
            pl.BlockSpec(memory_space=pltpu.SMEM),
            chunked(OWN, 1),
            chunked(N, 8),
            chunked(640),
            chunked(OWN),
            chunked(OWN),
            pl.BlockSpec((N, OWN), lambda i: (last - i, 0)),
            fixed((16, 640)),
        ]
        + ([pl.BlockSpec(memory_space=pl.ANY)] * 3 + carry if part else []),
        out_specs=[
            chunked(OWN),
            chunked(N),
            pl.BlockSpec((2 * N, CHUNK), lambda i: (0, last - i)),
            carry[1],
            carry[2],
            carry[0],
        ],
        out_shape=[
            jax.ShapeDtypeStruct((PACK, OWN), BF16),
            jax.ShapeDtypeStruct((PACK, N), BF16),
            jax.ShapeDtypeStruct((2 * N, PACK), BF16),
            jax.ShapeDtypeStruct((8, OWN), F32),
            jax.ShapeDtypeStruct((8, N), F32),
            jax.ShapeDtypeStruct((N + 16, OWN), F32),
        ],
        input_output_aliases={8: 0, 9: 1, 10: 2} if part else {},
        scratch_shapes=[
            pltpu.VMEM((N, OWN), F32),
            pltpu.VMEM((CHUNK + 8, OWN), F32),
            pltpu.VMEM((8, N), F32),
        ],
        compiler_params=pltpu.CompilerParams(
            dimension_semantics=("arbitrary",), vmem_limit_bytes=VMEM_LIMIT
        ),
        cost_estimate=COST,
        name="scan_backward",
    )(ends, proj, proj, pre, mixed, grad_mixed, states, par, *before)


PARTS = (1, 1, 1, 1, 2, 2, 1, 1)
PIECES = sum(PARTS)
EARLY_SLOTS = (0, 1, 2, 6)
LATE_SLOTS = (3, 4, 5, 7)


def load_block(step, groups, block):
    for slot, refs in enumerate(groups):

        @pl.when(step == slot)
        def _(refs=refs):
            if len(refs) == 1:
                block[...] = refs[0][...]
            else:
                block[: ROWS // 2, :] = refs[0][...]
                block[ROWS // 2 :, :] = refs[1][...]


def grouped(refs, slots):
    groups = []
    for slot in slots:
        groups.append(refs[: PARTS[slot]])
        refs = refs[PARTS[slot] :]
    return groups, refs


def piece_specs(slots):
    return [
        pl.BlockSpec((ROWS // PARTS[slot], D), lambda i, table: (0, 0))
        for slot in slots
        for _ in range(PARTS[slot])
    ]


def project_kernel(slots, table, *refs):
    groups, (gain, shards, *refs) = grouped(refs, slots)
    normed_out, proj, dt_out, block, weight = refs[-5:]

    @pl.when(pl.program_id(0) == 0)
    def _():
        for f in range(N_FSDP):
            weight[f * SHARD_IN : (f + 1) * SHARD_IN, :] = shards[(f // 2) % 4, f % 2, f // 8]
        dt_out[...] = weight[:, 1024:]

    load_block(pl.program_id(0), groups, block)
    values = block[...].astype(F32)
    scale = lax.rsqrt(jnp.mean(values * values, axis=1, keepdims=True) + NORM_EPS)
    normed = (values * scale * gain[...]).astype(BF16)
    normed_out[...] = normed
    proj[...] = matmul(normed, weight[...])


def run_project(slots, table, pieces, gain, shards, before=()):
    fixed = lambda shape: pl.BlockSpec(shape, lambda i, table: (0,) * len(shape))
    placed = lambda width: pl.BlockSpec((ROWS, width), lambda i, table: (table[i], 0))
    count = sum(PARTS[slot] for slot in slots)
    return pl.pallas_call(
        partial(project_kernel, slots),
        grid_spec=pltpu.PrefetchScalarGridSpec(
            num_scalar_prefetch=1,
            grid=(len(slots),),
            in_specs=piece_specs(slots)
            + [fixed((1, D)), fixed(shards.shape)]
            + [pl.BlockSpec(memory_space=pl.ANY)] * len(before),
            out_specs=[placed(D), placed(3 * WIDE), fixed((D, N))],
            scratch_shapes=[pltpu.VMEM((ROWS, D), BF16), pltpu.VMEM((D, 3 * WIDE), BF16)],
        ),
        out_shape=[
            jax.ShapeDtypeStruct((PACK, D), BF16),
            jax.ShapeDtypeStruct((PACK, 3 * WIDE), F32),
            jax.ShapeDtypeStruct((D, N), BF16),
        ],
        input_output_aliases={count + 3 + k: k for k in range(len(before))},
        compiler_params=pltpu.CompilerParams(
            dimension_semantics=("arbitrary",), vmem_limit_bytes=VMEM_LIMIT
        ),
        cost_estimate=COST,
        name="project",
    )(table, *pieces, gain, shards, *before)


def row_sums(value):
    folded = value[:, :N] + value[:, N : 2 * N] + value[:, 2 * N :]
    return jnp.sum(folded.T, 0, keepdims=True)


def out_grad_kernel(table, *refs):
    groups, refs = grouped(refs, range(N_REP))
    w_out, mixed, gate_in, gain, branch_out, grad_out, sums, block, turned = refs

    @pl.when(pl.program_id(0) == 0)
    def _():
        turned[...] = w_out[...].reshape(OWN, D).T

    load_block(pl.program_id(0), groups, block)
    branch = block[...]
    branch_out[...] = branch
    total = matmul(branch, turned[...])
    grad_out[...] = total
    gate = gate_in[...]
    gated = mixed[...] * (gate * jax.nn.sigmoid(gate))
    row = lax.broadcasted_iota(jnp.int32, (8, ROWS), 0)
    sums[...] = jnp.where(
        row == 0, row_sums(gated * gated), jnp.where(row == 1, row_sums(total * gain[...] * gated), 0.0)
    )


def run_out_grad(table, pieces, w_out, mixed, proj, gain):
    fixed = lambda shape: pl.BlockSpec(shape, lambda i, table: (0, 0))
    placed = lambda width: pl.BlockSpec((ROWS, width), lambda i, table: (table[i], 0))
    return pl.pallas_call(
        out_grad_kernel,
        grid_spec=pltpu.PrefetchScalarGridSpec(
            num_scalar_prefetch=1,
            grid=(N_REP,),
            in_specs=piece_specs(range(N_REP))
            + [
                pl.BlockSpec(
                    (1, 2, 1, SHARD_OUT, D), lambda i, table: (table[N_REP] % 4, 0, table[N_REP] // 4, 0, 0)
                )
            ]
            + [placed(OWN), placed(OWN), fixed((1, OWN))],
            out_specs=[placed(D), placed(OWN), pl.BlockSpec((8, ROWS), lambda i, table: (0, table[i]))],
            scratch_shapes=[pltpu.VMEM((ROWS, D), BF16), pltpu.VMEM((D, WIDE), BF16)],
        ),
        out_shape=[
            jax.ShapeDtypeStruct((PACK, D), BF16),
            jax.ShapeDtypeStruct((PACK, OWN), F32),
            jax.ShapeDtypeStruct((8, PACK), F32),
        ],
        compiler_params=pltpu.CompilerParams(
            dimension_semantics=("arbitrary",), vmem_limit_bytes=VMEM_LIMIT
        ),
        cost_estimate=COST,
        name="out_grad",
    )(table, *pieces, w_out, mixed, proj, gain)


def gate_kernel(
    where, grad_out, mixed_in, gate_in, sums, gain, grad_branch, normed,
    low_out, grad_mixed, keep, give, grad_gain, total,
):
    step = pl.program_id(0)
    rows = grad_out.shape[0]
    mixed, gate, grad_o = mixed_in[...], gate_in[...], grad_out[...]
    stats = jnp.concatenate([sums[...], jnp.zeros((N - 8, rows), F32)], 0).T
    out_scale = lax.rsqrt(stats[:, 0:1] * (1.0 / DI) + NORM_EPS)
    pull = out_scale * out_scale * out_scale * (stats[:, 1:2] * (1.0 / DI))
    gate_sig = jax.nn.sigmoid(gate)
    silu = gate * gate_sig
    gated = mixed * silu
    unit = gated * out_scale
    low = (unit * gain[...]).astype(BF16)
    grad_gated = out_scale * (grad_o * gain[...]) - gated * pull
    grad_mixed[...] = grad_gated * silu
    grad_z = (grad_gated * mixed * (gate_sig * (1.0 + gate * (1.0 - gate_sig)))).astype(BF16)
    low_out[:, :OWN] = low
    low_out[:, OWN:] = grad_z

    @pl.when(step == 0)
    def _():
        grad_gain[...] = jnp.zeros_like(grad_gain)
        total[...] = jnp.zeros_like(total)

    grad_gain[0:1] += jnp.sum(grad_o * unit, 0, keepdims=True)
    for k in range(4):
        part = product(low, grad_branch[:, k * WIDE : (k + 1) * WIDE], 0, 0)
        for m in range(4):
            total[4 * k + m, :SHARD_IN] += part[m * SHARD_IN : (m + 1) * SHARD_IN]
    part = product(normed[...], grad_z, 0, 0)
    for f in range(N_FSDP):
        total[f, SHARD_IN:] += part[f * SHARD_IN : (f + 1) * SHARD_IN]

    @pl.when(step == pl.num_programs(0) - 1)
    def _():
        for k in range(N_FSDP // 2):
            keep[k] = total[2 * k + where[0]]
            give[k] = total[2 * k + 1 - where[0]]


def run_gate(where, grad_out, mixed, proj, sums, gain, grad_branch, normed):
    count = 2 * ROWS
    rows = lambda width: pl.BlockSpec((count, width), lambda i: (i, 0))
    fixed = lambda shape: pl.BlockSpec(shape, lambda i: (0,) * len(shape))
    half = (N_FSDP // 2, 2 * SHARD_IN, WIDE)
    return pl.pallas_call(
        gate_kernel,
        grid=(PACK // count,),
        in_specs=[
            pl.BlockSpec(memory_space=pltpu.SMEM),
            rows(OWN),
            rows(OWN),
            rows(OWN),
            pl.BlockSpec((8, count), lambda i: (0, i)),
            fixed((1, OWN)),
            rows(D),
            rows(D),
        ],
        out_specs=[rows(2 * OWN), rows(OWN), fixed(half), fixed(half), fixed((8, OWN))],
        out_shape=[
            jax.ShapeDtypeStruct((PACK, 2 * OWN), BF16),
            jax.ShapeDtypeStruct((PACK, OWN), F32),
            jax.ShapeDtypeStruct(half, F32),
            jax.ShapeDtypeStruct(half, F32),
            jax.ShapeDtypeStruct((8, OWN), F32),
        ],
        scratch_shapes=[pltpu.VMEM((N_FSDP, 2 * SHARD_IN, WIDE), F32)],
        compiler_params=pltpu.CompilerParams(
            dimension_semantics=("arbitrary",), vmem_limit_bytes=VMEM_LIMIT
        ),
        cost_estimate=COST,
        name="gate_backward",
    )(where, grad_out, mixed, proj, sums, gain, grad_branch, normed)


def block_out_kernel(rows, weight, tokens, live, out):
    step = pl.program_id(0)
    part = matmul(rows[0], weight[...].reshape(OWN, D))

    @pl.when(step == 0)
    def _():
        out[...] = part

    @pl.when(step > 0)
    def _():
        out[...] += part

    @pl.when(step == N_REP - 1)
    def _():
        out[...] = tokens[...].astype(F32) + live[...] * out[...]


def run_block_out(rows, weight, tokens, live):
    fixed = lambda shape: pl.BlockSpec(shape, lambda i: (0, 0))
    return pl.pallas_call(
        block_out_kernel,
        grid=(N_REP,),
        in_specs=[
            pl.BlockSpec((1, ROWS, OWN), lambda i: (i, 0, 0)),
            pl.BlockSpec((1, 2, 1, SHARD_OUT, D), lambda i: (i % 4, 0, i // 4, 0, 0)),
            fixed((ROWS, D)),
            fixed((ROWS, 1)),
        ],
        out_specs=fixed((ROWS, D)),
        out_shape=jax.ShapeDtypeStruct((ROWS, D), F32),
        compiler_params=pltpu.CompilerParams(
            dimension_semantics=("arbitrary",), vmem_limit_bytes=VMEM_LIMIT
        ),
        cost_estimate=COST,
        name="block_out",
    )(rows, weight, tokens, live)


def turned_part(weight, rows):
    return product(weight[...].reshape(D, weight.shape[-1]), rows, 1, 1)


def columns_of(full_in, width, index):
    return pl.BlockSpec(full_in.shape[:-1] + (width,), lambda i: (0, 0, 0, 0, index(i)))


def z_grad_kernel(rows, weight, out):
    part = turned_part(weight, rows[0])

    @pl.when(pl.program_id(0) == 0)
    def _():
        out[...] = part

    @pl.when(pl.program_id(0) > 0)
    def _():
        out[...] += part


def x_grad_kernel(before, rows, weight, out):
    part = turned_part(weight, rows[0])

    @pl.when(pl.program_id(0) == 0)
    def _():
        out[...] = before[...] + part

    @pl.when(pl.program_id(0) > 0)
    def _():
        out[...] += part


def run_rows_grad(rows, full_in, before=None):
    fixed = pl.BlockSpec((D, ROWS), lambda i: (0, 0))
    column = 1 if before is None else 0
    first = 0 if before is None else N_REP
    return pl.pallas_call(
        z_grad_kernel if before is None else x_grad_kernel,
        grid=(N_REP,),
        in_specs=([] if before is None else [fixed])
        + [
            pl.BlockSpec((1, ROWS, OWN), lambda i: (i, 0, column)),
            columns_of(full_in, OWN, lambda i: first + i),
        ],
        out_specs=fixed,
        out_shape=jax.ShapeDtypeStruct((D, ROWS), F32),
        compiler_params=pltpu.CompilerParams(
            dimension_semantics=("arbitrary",), vmem_limit_bytes=VMEM_LIMIT
        ),
        cost_estimate=COST,
        name="z_grad" if before is None else "x_grad",
    )(*(() if before is None else (before,)), rows, full_in)


def input_grad_kernel(total, rest_rows, w_bc, low_dt, tokens, cotangent, gain, out, gain_out, ordered):
    lane = lax.broadcasted_iota(jnp.int32, (ROWS, N), 1)
    groups = []
    for k in range(2):
        group = jnp.zeros((ROWS, N), F32)
        for m in range(4):
            value = rest_rows[4 * k + m].astype(F32)
            value = value if m == 0 else pltpu.roll(value, m * OWN_BC, 1)
            group = jnp.where((lane >= m * OWN_BC) & (lane < (m + 1) * OWN_BC), value, group)
        groups.append(group.astype(BF16))
    steps = jnp.zeros((ROWS, N), F32)
    for m in range(N_REP):
        start = 8 + m * OWN_H
        value = pltpu.roll(rest_rows[m].astype(F32), (start - OWN_BC) % N, 1)
        steps = jnp.where((lane >= start) & (lane < start + OWN_H), value, steps)
    shared = total[...] + turned_part(w_bc, jnp.concatenate(groups, 1))
    for f in range(N_FSDP):
        start = (((f // 2) % 4 * 2 + f % 2) * 2 + f // 8) * SHARD_IN
        ordered[f * SHARD_IN : (f + 1) * SHARD_IN, :] = shared[start : start + SHARD_IN, :]
    grad_h = (ordered[...] + product(low_dt[...], steps.astype(BF16), 1, 1)).T
    values = tokens[...].astype(F32)
    scale = lax.rsqrt(jnp.mean(values * values, axis=1, keepdims=True) + NORM_EPS)
    unit = values * scale
    gain_sum = jnp.sum(grad_h * unit, 0, keepdims=True)
    gain_out[...] = jnp.zeros_like(gain_out)
    for k in range(D // N):
        gain_out[k : k + 1, :] = gain_sum[:, k * N : (k + 1) * N]
    grad_unit = grad_h * gain[...]
    inner = jnp.mean(grad_unit * unit, axis=1, keepdims=True)
    out[...] = cotangent[...].astype(F32) + scale * (grad_unit - unit * inner)


def run_input_grad(total, rest_rows, full_in, low_dt, tokens, cotangent, gain):
    fixed = lambda shape: pl.BlockSpec(shape, lambda i: (0,) * len(shape))
    return pl.pallas_call(
        input_grad_kernel,
        grid=(1,),
        in_specs=[
            fixed((D, ROWS)),
            fixed((N_REP, ROWS, N)),
            columns_of(full_in, 2 * N, lambda i: DI // N),
            fixed((D, N)),
            fixed((ROWS, D)),
            fixed((ROWS, D)),
            fixed((1, D)),
        ],
        out_specs=[fixed((ROWS, D)), fixed((16, N))],
        out_shape=[jax.ShapeDtypeStruct((ROWS, D), F32), jax.ShapeDtypeStruct((16, N), F32)],
        scratch_shapes=[pltpu.VMEM((D, ROWS), F32)],
        compiler_params=pltpu.CompilerParams(
            dimension_semantics=("arbitrary",), vmem_limit_bytes=VMEM_LIMIT
        ),
        cost_estimate=COST,
        name="input_grad",
    )(total, rest_rows, full_in, low_dt, tokens, cotangent, gain)


def rest_kernel(ends, parts, pre_b, pre_c, conv_in, par, grad_dt, sums, head_acc, grad_gain, first, rest_out, small_out):
    own = lax.broadcasted_iota(jnp.int32, (OWN_BC, 2 * N), 0) + first[0]
    chosen = (lax.broadcasted_iota(jnp.int32, (OWN_BC, 2 * N), 1) == own).astype(F32).astype(BF16)

    def pick(value):
        return product(jnp.concatenate([chosen] * 3, 1), jnp.concatenate(split_three(value), 1), 1, 1)

    grad = parts[0].astype(F32)
    for k in range(1, N_REP):
        grad = grad + parts[k].astype(F32)
    own_pre = pick(jnp.concatenate([pre_b[...], pre_c[...]], 1))
    own_conv = product(chosen, conv_in[...].astype(BF16), 1, 1)
    taps = pick(par[:, OWN:])
    sig = jax.nn.sigmoid(own_pre)
    grad_pre = grad * (sig * (1.0 + own_pre * (1.0 - sig)))
    position = lax.broadcasted_iota(jnp.int32, (1, PACK), 1)

    def segment(places):
        counted = jnp.zeros_like(places)
        for k in range(3):
            counted = counted + (places >= ends[k]).astype(jnp.int32)
        return counted

    grad_conv = taps[:, CONV - 1 : CONV] * grad_pre
    column = lax.broadcasted_iota(jnp.int32, (OWN_BC, N), 1)
    found = jnp.where(column == CONV, jnp.sum(grad_pre, 1, keepdims=True), 0.0)
    found = jnp.where(column == CONV - 1, jnp.sum(own_conv * grad_pre, 1, keepdims=True), found)
    for later_by in range(1, CONV):
        same = (segment(position + later_by) == segment(position)) & (position < PACK - later_by)
        later = jnp.where(same, pltpu.roll(grad_pre, PACK - later_by, 1), 0.0)
        tap = CONV - 1 - later_by
        found = jnp.where(column == tap, jnp.sum(own_conv * later, 1, keepdims=True), found)
        grad_conv = grad_conv + taps[:, tap : tap + 1] * later
    lane = lax.broadcasted_iota(jnp.int32, (N, N), 1)
    filler = jnp.zeros((N - OWN_BC, N), F32)
    for k in range(PACK // N):
        rows = slice(k * N, (k + 1) * N)
        columns = jnp.concatenate([grad_conv[:, rows], filler], 0).T
        steps = pltpu.roll(grad_dt[rows, :].astype(F32), OWN_BC, 1)
        rest_out[rows, :] = jnp.where(
            lane < OWN_BC, columns, jnp.where(lane < OWN_BC + OWN_H, steps, 0.0)
        ).astype(BF16)
    row = lax.broadcasted_iota(jnp.int32, (8, OWN), 0)
    skip = head_sums(sums[...])
    by_head = jnp.concatenate([skip, jnp.zeros((8, OWN - N), F32)], 1)
    logs = jnp.concatenate([head_acc[...], jnp.zeros((8, OWN - N), F32)], 1)
    wide = jnp.where(row == 0, grad_gain[0:1, :], jnp.where(row < 6, sums[...], 0.0))
    wide = jnp.where(row == 6, logs[1:2, :], jnp.where(row == 7, by_head[6:7, :], wide))
    turned = jnp.concatenate([found, filler], 0).T
    first_row = lax.broadcasted_iota(jnp.int32, (8, N), 0) == 0
    for k in range(3):
        small_out[8 * k : 8 * k + 8, :] = wide[:, k * N : (k + 1) * N]
    small_out[24:32, :] = jnp.where(first_row, head_acc[0:1, :], pltpu.roll(turned[:8], 1, 0))


def run_rest(ends, parts, pre, proj, par, grad_dt, sums, head_acc, grad_gain, first):
    fixed = lambda shape: pl.BlockSpec(shape, lambda i: (0,) * len(shape))
    return pl.pallas_call(
        rest_kernel,
        grid=(1,),
        in_specs=[
            pl.BlockSpec(memory_space=pltpu.SMEM),
            fixed((N_REP, OWN_BC, PACK)),
            pl.BlockSpec((PACK, N), lambda i: (0, 3)),
            pl.BlockSpec((PACK, N), lambda i: (0, 4)),
            pl.BlockSpec((PACK, 2 * N), lambda i: (0, 3)),
            fixed((16, 640)),
            fixed((PACK, N)),
            fixed((8, OWN)),
            fixed((8, N)),
            fixed((8, OWN)),
            pl.BlockSpec(memory_space=pltpu.SMEM),
        ],
        out_specs=[fixed((PACK, N)), fixed((32, N))],
        out_shape=[jax.ShapeDtypeStruct((PACK, N), BF16), jax.ShapeDtypeStruct((32, N), F32)],
        compiler_params=pltpu.CompilerParams(
            dimension_semantics=("arbitrary",), vmem_limit_bytes=VMEM_LIMIT
        ),
        cost_estimate=COST,
        name="rest_backward",
    )(ends, parts, pre, pre, proj, par, grad_dt, sums, head_acc, grad_gain, first)


def adam_step(grad, weight, first, second, grad_out, first_out, second_out, weight_out):
    new_weight, new_first, new_second = adam_update(
        weight[...], grad, first[...], second[...], RATE_MATRIX, WEIGHT_DECAY
    )
    grad_out[...] = grad
    first_out[...] = new_first
    second_out[...] = new_second
    weight_out[...] = new_weight


def load_pair(step, pairs, rows, grad):
    pair, right, far_first, far_second, left = pairs
    for slot, (low, high) in enumerate(
        (((pair, 0), (pair, 1)), ((right, 0), (right, 1)), ((far_first, 0), (far_second, 0)), ((left, 0), (left, 1)))
    ):

        @pl.when(step == slot)
        def _(low=low, high=high):
            grad[:, :WIDE] = low[0][low[1], rows, :]
            grad[:, WIDE:] = high[0][high[1], rows, :]


def adam_pairs_kernel(rows, table, *refs):
    pairs, arrays, grad = refs[:5], refs[5:8] + refs[-5:-1], refs[-1]
    load_pair(pl.program_id(0), pairs, rows, grad)
    adam_step(grad[...], *arrays)


def run_adam_pairs(table, place_of, rows, pairs, weight, first, second, before=()):
    part = pl.BlockSpec((SHARD_IN, 2 * WIDE), lambda i, table: place_of(table[i]))
    shape = jax.ShapeDtypeStruct(weight.shape, F32)
    return pl.pallas_call(
        partial(adam_pairs_kernel, rows),
        grid_spec=pltpu.PrefetchScalarGridSpec(
            num_scalar_prefetch=1,
            grid=(4,),
            in_specs=[pl.BlockSpec(pair.shape, lambda i, table: (0, 0, 0)) for pair in pairs]
            + [part] * 3
            + [pl.BlockSpec(memory_space=pl.ANY)] * len(before),
            out_specs=[part] * 4,
            scratch_shapes=[pltpu.VMEM((SHARD_IN, 2 * WIDE), F32)],
        ),
        out_shape=[shape] * 4,
        input_output_aliases={9 + k: k for k in range(len(before))},
        compiler_params=pltpu.CompilerParams(
            dimension_semantics=("arbitrary",), vmem_limit_bytes=VMEM_LIMIT
        ),
        cost_estimate=COST,
        name="adam",
    )(table, *pairs, weight, first, second, *before)


def adam_rest_kernel(parts, weight, first, second, *refs):
    lane = lax.broadcasted_iota(jnp.int32, (SHARD_IN, N), 1)
    groups = []
    for k in range(2):
        group = jnp.zeros((SHARD_IN, N), F32)
        for m in range(4):
            value = parts[4 * k + m, :SHARD_IN]
            value = value if m == 0 else pltpu.roll(value, m * OWN_BC, 1)
            group = jnp.where((lane >= m * OWN_BC) & (lane < (m + 1) * OWN_BC), value, group)
        groups.append(group)
    adam_step(jnp.concatenate(groups, 1), weight, first, second, *refs[-4:])


def run_adam_rest(parts, weight, first, second, before):
    column = pl.BlockSpec((SHARD_IN, 2 * N), lambda i: (0, DI // N))
    shape = jax.ShapeDtypeStruct(weight.shape, F32)
    return pl.pallas_call(
        adam_rest_kernel,
        grid=(1,),
        in_specs=[pl.BlockSpec(parts.shape, lambda i: (0, 0, 0))]
        + [column] * 3
        + [pl.BlockSpec(memory_space=pl.ANY)] * 4,
        out_specs=[column] * 4,
        out_shape=[shape] * 4,
        input_output_aliases={4 + k: k for k in range(4)},
        compiler_params=pltpu.CompilerParams(
            dimension_semantics=("arbitrary",), vmem_limit_bytes=VMEM_LIMIT
        ),
        cost_estimate=COST,
        name="adam_rest",
    )(parts, weight, first, second, *before)


def body(
    tokens,
    cotangent,
    lengths,
    w_in,
    w_dt,
    w_out,
    small,
    first_in,
    first_dt,
    first_out,
    first_small,
    second_in,
    second_dt,
    second_out,
    second_small,
):
    place = Place()
    r = place.r
    zero = jnp.int32(0)
    pack_lengths = lax.dynamic_slice_in_dim(lengths, place.f, 1, 0)[0]
    seg_ends = jnp.cumsum(pack_lengths)
    own_positions = r * ROWS + jnp.arange(ROWS, dtype=jnp.int32)
    own_live = (segment_at(own_positions, seg_ends) < 3).astype(F32)[:, None]
    slots = jnp.arange(N_REP, dtype=jnp.int32)
    ahead = ((place.x + slots // 2) % 4) * 2 + (place.yl + slots) % 2
    half = ROWS // 2

    in_low = w_in.astype(BF16)
    dt_low = w_dt.astype(BF16)
    out_low = w_out.astype(BF16)

    small_block = jnp.pad(small.astype(BF16), (0, 16 * N - SHARD_SMALL)).reshape(1, 16, N)
    small_all = exchange(jnp.broadcast_to(small_block, (N_FSDP, 16, N)), "fsdp")
    vector = small_all.reshape(N_FSDP, 16 * N)[:, :SHARD_SMALL].reshape(-1).astype(F32)

    def own_columns(rep):
        return jnp.concatenate(
            [
                lax.dynamic_slice_in_dim(in_low, rep * OWN, OWN, 1),
                lax.dynamic_slice_in_dim(in_low, DI + rep * OWN, OWN, 1),
                in_low[:, 2 * DI :],
                lax.dynamic_slice_in_dim(dt_low, rep * OWN_H, OWN_H, 1),
                jnp.zeros((SHARD_IN, 2), BF16),
                dt_low,
                jnp.zeros((SHARD_IN, N - 8 - H), BF16),
            ],
            1,
        )

    other_columns = move(
        own_columns(2 * place.x + 1 - place.yl), lambda yh, z, c, x, yl: (yh + 1, z, c, x, yl + 1)
    )
    from_left = move(tokens, along_x(1))
    from_right = move(tokens, along_x(-1))
    partner = move(tokens, swap_y)

    from_left, from_right, partner, out_low, other_columns = lax.optimization_barrier(
        (from_left, from_right, partner, out_low, other_columns)
    )
    own_shards = gather_eight(both(own_columns(r), other_columns, place.yh))
    far_top = move(from_left[:half], along_x(1))
    far_low = move(from_right[half:], along_x(-1))
    partner_left = move(from_left, swap_y)
    partner_right = move(partner, along_x(-1))
    out_pair = swap_shards(out_low, place)

    far_top, far_low, partner_left, partner_right, in_low, out_pair = lax.optimization_barrier(
        (far_top, far_low, partner_left, partner_right, in_low, out_pair)
    )
    partner_far_top = move(partner_left[:half], along_x(1))
    partner_far_low = move(partner_right[half:], along_x(-1))
    in_pair = swap_shards(in_low, place)

    offset = 0
    gain_in = vector[None, :D]
    offset = D
    gain_row = lax.dynamic_slice_in_dim(vector, offset + r * OWN, OWN, 0)[None, :]
    offset += DI
    taps = vector[offset : offset + (CONV + 1) * CHANNELS].reshape(CONV + 1, CHANNELS)
    offset += (CONV + 1) * CHANNELS
    per_head = vector[offset:].reshape(3, H)
    dt_bias, a_log, d_skip = lax.dynamic_slice_in_dim(per_head, r * OWN_H, OWN_H, 1)
    taps_bc = taps[:, DI:]
    conv_par = jnp.concatenate([lax.dynamic_slice_in_dim(taps, r * OWN, OWN, 1), taps_bc], 1)
    head_par = jnp.stack(
        [
            jnp.pad(jnp.broadcast_to(d_skip[:, None], (OWN_H, P_SIZE)).reshape(-1), (0, 2 * N)),
            jnp.pad(dt_bias, (0, 640 - OWN_H)),
            jnp.pad(-jnp.exp(a_log), (0, 640 - OWN_H)),
        ],
        0,
    )
    par = jnp.concatenate([conv_par, head_par, jnp.zeros((8, 640), F32)], 0)

    branch = (cotangent.astype(F32) * own_live).astype(BF16)
    token_pieces = [
        (tokens,), (partner,), (from_right,), (partner_right,), (far_top, far_low),
        (partner_far_top, partner_far_low), (from_left,), (partner_left,),
    ]

    def chosen(slots):
        return jnp.stack([ahead[slot] for slot in slots]), [piece for slot in slots for piece in token_pieces[slot]]

    own_shards, far_top = lax.optimization_barrier((own_shards, far_top))
    full_out = gather_eight(tie(out_pair, own_shards))
    before = run_project(EARLY_SLOTS, *chosen(EARLY_SLOTS), gain_in, own_shards)
    branch, before = lax.optimization_barrier((branch, before))
    b_left = move(branch, along_x(1))
    b_right = move(branch, along_x(-1))
    b_partner = move(branch, swap_y)
    normed, proj, low_dt = run_project(LATE_SLOTS, *chosen(LATE_SLOTS), gain_in, own_shards, before)
    b_left, b_right, b_partner, proj = lax.optimization_barrier((b_left, b_right, b_partner, proj))
    full_in = gather_eight(tie(in_pair, proj))
    b_far_top = move(b_left[:half], along_x(1))
    b_far_low = move(b_right[half:], along_x(-1))
    b_partner_left = move(b_left, swap_y)
    b_partner_right = move(b_partner, along_x(-1))
    before = run_forward(0, seg_ends, proj, par)
    pre, mixed, states, _ = run_forward(1, seg_ends, proj, par, before)
    b_far_top, b_far_low, b_partner_left, b_partner_right, mixed = lax.optimization_barrier(
        (b_far_top, b_far_low, b_partner_left, b_partner_right, mixed)
    )
    b_partner_far_top = move(b_partner_left[:half], along_x(1))
    b_partner_far_low = move(b_partner_right[half:], along_x(-1))
    branch_pieces = [
        branch, b_partner, b_right, b_partner_right, b_far_top, b_far_low,
        b_partner_far_top, b_partner_far_low, b_left, b_partner_left,
    ]
    rep_table = jnp.concatenate([ahead, r[None]])
    grad_branch, grad_normed_out, sums = run_out_grad(rep_table, branch_pieces, full_out, mixed, proj, gain_row)
    sums = sum_rep(sums[:2].reshape(32, 128)).reshape(2, PACK)
    sums = jnp.concatenate([sums, jnp.zeros((6, PACK), F32)], 0)

    low_rows, grad_mixed, keep, give, grad_gain = run_gate(
        place.c[None], grad_normed_out, mixed, proj, sums, gain_row, grad_branch, normed
    )

    low_rows = exchange(low_rows.reshape(N_REP, ROWS, 2 * OWN), "rep")
    got = move(give, swap_core)
    before = run_backward(0, seg_ends, proj, pre, mixed, grad_mixed, states, par)
    got, before = lax.optimization_barrier((got, before))
    split = (2, 4, 2 * SHARD_IN, WIDE)
    early, _ = scatter_ring(keep.reshape(split), got.reshape(split), None, place)
    grad_x, grad_dtraw, grad_bc, grad_sums, grad_heads, _ = run_backward(
        1, seg_ends, proj, pre, mixed, grad_mixed, states, par,
        (before[0], before[1], before[2], before[5], before[3], before[4]),
    )
    low_rows, grad_bc, grad_x = lax.optimization_barrier((low_rows, grad_bc, grad_x))

    grad_bc = exchange(grad_bc, "rep").reshape(N_REP, OWN_BC, PACK)
    grad_x_own = contract_rows(normed, grad_x).reshape(2, 4, 2, SHARD_IN, OWN)
    x_keep, x_give = at(grad_x_own, place.c, 2), at(grad_x_own, 1 - place.c, 2)
    x_got = move(x_give, swap_core)
    block_out = run_block_out(low_rows, full_out, tokens, own_live)
    grad_bc, block_out, grad_x, x_got, early = lax.optimization_barrier((grad_bc, block_out, grad_x, x_got, early))
    x_rows = exchange(grad_x.reshape(N_REP, ROWS, OWN), "rep")
    rest, small_own = run_rest(
        seg_ends, grad_bc, pre, proj, par, grad_dtraw, grad_sums, grad_heads, grad_gain, (r * OWN_BC)[None]
    )
    grad_rest = contract_rows(normed, rest).reshape(N_FSDP, SHARD_IN, N)
    x_part, _ = scatter_ring(x_keep, x_got, None, place)
    rest_part, small_sum = scatter_fsdp(grad_rest, small_own, place)
    out_part = move(
        early[:SHARD_IN],
        lambda yh, z, c, x, yl: (x // 2, (x % 2) * 2 + yl, z % 2, 2 * c + yh, z // 2),
    )
    early_pairs = gather_pairs(jnp.concatenate([out_part, early[SHARD_IN:]], 0), place)

    grad_rows = run_rows_grad(low_rows, full_in)
    x_rows, rest, grad_rows = lax.optimization_barrier((x_rows, rest, grad_rows))
    rest_rows = exchange(rest.reshape(N_REP, ROWS, N), "rep")
    grad_rows = run_rows_grad(x_rows, full_in, grad_rows)
    input_grad, grad_gain_in = run_input_grad(
        grad_rows, rest_rows, full_in, low_dt, tokens, cotangent, gain_in
    )
    grad_gain_in = sum_fsdp(grad_gain_in)
    x_pairs = gather_pairs(x_part, place)
    rest_parts = share_rep(jnp.concatenate([rest_part, small_sum, grad_gain_in], 0))

    x_order = (place.x + jnp.arange(4, dtype=jnp.int32)) % 4
    grad_out, new_first_out, new_second_out, new_out = run_adam_pairs(
        x_order, lambda k: (k // 2, k % 2), slice(0, SHARD_IN), early_pairs, w_out, first_out, second_out
    )
    updated = run_adam_pairs(
        x_order, lambda k: (0, k), slice(SHARD_IN, 2 * SHARD_IN), early_pairs, w_in, first_in, second_in
    )
    updated = run_adam_pairs(
        x_order, lambda k: (0, 4 + k), slice(0, SHARD_IN), x_pairs, w_in, first_in, second_in, updated
    )
    grad_in, new_first_in, new_second_in, new_in = run_adam_rest(rest_parts, w_in, first_in, second_in, updated)

    def columns(parts):
        return parts.transpose(1, 0, 2).reshape(parts.shape[1], -1)

    grad_gain_in = rest_parts[:, SHARD_IN + 32 : SHARD_IN + 32 + D // N].sum(0).reshape(-1)
    small_parts = rest_parts[:, SHARD_IN : SHARD_IN + 32].reshape(N_REP, 4, 8, N)
    small_x = small_parts[:, :3].transpose(2, 0, 1, 3).reshape(8, DI)
    small_bc = small_parts[:, 3].transpose(1, 0, 2)

    def channels(row):
        return jnp.concatenate([small_x[row], small_bc[row, :, :OWN_BC].reshape(-1)])

    grad_small_all = jnp.concatenate(
        [grad_gain_in, small_x[0]]
        + [channels(row) for row in range(1, 6)]
        + [
            small_bc[0, :, :OWN_H].reshape(-1),
            small_parts[:, 0, 6, :OWN_H].reshape(-1),
            small_parts[:, 0, 7, :OWN_H].reshape(-1),
        ]
    )
    grad_small = lax.dynamic_slice_in_dim(grad_small_all, place.f * SHARD_SMALL, SHARD_SMALL, 0)
    grad_dt = columns(rest_parts[:, :SHARD_IN, OWN_BC : OWN_BC + OWN_H])
    new_dt, new_first_dt, new_second_dt = adam_update(
        w_dt, grad_dt, first_dt, second_dt, RATE_MATRIX, WEIGHT_DECAY
    )
    new_small, new_first_small, new_second_small = adam_update(
        small, grad_small, first_small, second_small, RATE_SMALL, 0.0
    )
    return (
        block_out,
        input_grad,
        grad_in,
        grad_dt,
        grad_out,
        grad_small,
        new_first_in,
        new_first_dt,
        new_first_out,
        new_first_small,
        new_second_in,
        new_second_dt,
        new_second_out,
        new_second_small,
        new_in,
        new_dt,
        new_out,
        new_small,
    )


def solution(mesh):
    rows = P(("fsdp", "rep"), None)
    matrix = P("fsdp", None)
    vector = P("fsdp")
    group = (matrix, matrix, matrix, vector)
    return jax.shard_map(
        body,
        mesh=mesh,
        in_specs=(rows, rows, P()) + group * 3,
        out_specs=(rows, rows) + group * 4,
        check_vma=False,
    )
```

```python
from functools import partial

import jax
import jax.numpy as jnp
from jax import lax
from jax.experimental import pallas as pl
from jax.experimental.pallas import tpu as pltpu
from jax.sharding import PartitionSpec as P

D = 1536
H = 48
P_SIZE = 64
N = 128
CONV = 4
STEP = 10
DI = 3072
CHANNELS = DI + 2 * N
SMALL = 21392
N_FSDP = 16
N_REP = 8
ROWS = 256
PACK = 2048
OWN = DI // N_REP
OWN_H = H // N_REP
OWN_BC = 2 * N // N_REP
SHARD_IN = D // N_FSDP
SHARD_OUT = DI // N_FSDP
SHARD_SMALL = SMALL // N_FSDP
WIDE = 384
CHUNK = 128
CHUNKS = PACK // CHUNK
HALF = CHUNKS // 2
VMEM_LIMIT = 60 * 1024 * 1024

NORM_EPS = 1e-05
BETA_ONE = 0.9
BETA_TWO = 0.999
ADAM_EPS = 1e-08
WEIGHT_DECAY = 0.1
RATE_MATRIX = 0.04
RATE_SMALL = 0.4
PRECISE = lax.Precision.HIGHEST
BF16 = jnp.bfloat16
F32 = jnp.float32
COST = pl.CostEstimate(flops=1_000_000, bytes_accessed=100_000, transcendentals=0)


def move(value, target):
    pairs = []
    for f in range(N_FSDP):
        for r in range(N_REP):
            yh, z, c, x, yl = target(f // 8, (f // 2) % 4, f % 2, r // 2, r % 2)
            pairs.append((f * N_REP + r, ((yh % 2) * 8 + (z % 4) * 2 + c % 2) * N_REP + (x % 4) * 2 + yl % 2))
    return lax.ppermute(value, ("fsdp", "rep"), pairs)


def along_x(steps):
    return lambda yh, z, c, x, yl: (yh, z, c, x + steps, yl)


def along_z(steps):
    return lambda yh, z, c, x, yl: (yh, z + steps, c, x, yl)


def swap_y(yh, z, c, x, yl):
    return (yh, z, c, x, yl + 1)


def swap_y_hi(yh, z, c, x, yl):
    return (yh + 1, z, c, x, yl)


def swap_core(yh, z, c, x, yl):
    return (yh, z, c + 1, x, yl)


class Place:
    def __init__(self):
        f = lax.axis_index("fsdp")
        r = lax.axis_index("rep")
        self.f, self.r = f, r
        self.yh, self.z, self.c = f // 8, (f // 2) % 4, f % 2
        self.x, self.yl = r // 2, r % 2


def at(value, index, axis=0):
    return lax.dynamic_index_in_dim(value, index, axis, keepdims=False)


def tie(values, *others):
    return lax.optimization_barrier((values, others))[0]


def both(mine, other, second):
    first = jnp.where(second == 0, mine, other)
    last = jnp.where(second == 0, other, mine)
    return jnp.stack([first, last], 0)


def put(out, piece, axis, index):
    starts = [jnp.int32(0)] * out.ndim
    starts[axis] = jnp.int32(index)
    return lax.dynamic_update_slice(out, jnp.expand_dims(piece, axis), tuple(starts))


def swap_shards(value, place):
    other = move(value, lambda yh, z, c, x, yl: (yh + 1, z, c, x, yl + 1))
    return both(value, other, place.yh)


def gather_eight(pair):
    groups = [list(range(8)), list(range(8, 16))]
    out = lax.all_gather(pair, "fsdp", axis=0, tiled=True, axis_index_groups=groups)
    return out.reshape((4, 2) + pair.shape)


def scatter_ring(keep, got, extra, place):
    z_sum = at(keep, place.z, 1) + at(got, place.z, 1)
    found = []
    for step in (1, 3, 2):
        there = (place.z + step) % 4
        found.append(received(at(keep, there, 1) + at(got, there, 1), along_z(step), extra, z_sum))
    z_sum = z_sum + found[0][0] + found[1][0] + found[2][0]
    if extra is not None:
        extra = extra + found[0][1] + found[1][1] + found[2][1]
    mine = at(z_sum, place.yh)
    more, more_extra = received(at(z_sum, 1 - place.yh), swap_y_hi, extra, mine)
    return mine + more, (None if extra is None else extra + more_extra)


def scatter_fsdp(value, extra, place):
    split = value.reshape((2, 4, 2) + value.shape[1:])
    keep = at(split, place.c, 2)
    got, got_extra = received(at(split, 1 - place.c, 2), swap_core, extra, keep)
    return scatter_ring(keep, got, None if extra is None else extra + got_extra, place)


def exchange(value, axis):
    return lax.all_to_all(value, axis, 0, 0, tiled=True)


def share_rep(value):
    return exchange(jnp.broadcast_to(value[None], (N_REP,) + value.shape), "rep")


def gather_pairs(pair):
    left = move(pair, along_x(1))
    right = move(pair, along_x(-1))
    return pair, right, move(left[:1], along_x(1)), move(right[1:], along_x(-1)), left


def sum_rep(value):
    value = value + move(value, swap_y)
    value = value + move(value, lambda yh, z, c, x, yl: (yh, z, c, x ^ 1, yl))
    return value + move(value, lambda yh, z, c, x, yl: (yh, z, c, x ^ 2, yl))


def sum_fsdp(value):
    value = value + move(value, swap_core)
    value = value + move(value, lambda yh, z, c, x, yl: (yh, z ^ 1, c, x, yl))
    value = value + move(value, lambda yh, z, c, x, yl: (yh, z ^ 2, c, x, yl))
    return value + move(value, swap_y_hi)


def with_rows(block, extra):
    width = block.shape[-1]
    flat = block.reshape(-1, width)
    return flat if extra is None else jnp.concatenate([flat, extra], 0)


def received(block, target, base, add_to):
    got = move(with_rows(block, base), target)
    rows = got.shape[0] - (0 if base is None else base.shape[0])
    return got[:rows].reshape(add_to.shape), got[rows:]


def adam_update(weight, gradient, moment_one, moment_two, learn_rate, decay_rate):
    moment_one = BETA_ONE * moment_one + (1.0 - BETA_ONE) * gradient
    moment_two = BETA_TWO * moment_two + (1.0 - BETA_TWO) * gradient * gradient
    scaled = (
        moment_one
        / (1.0 - BETA_ONE**STEP)
        / (jnp.sqrt(moment_two / (1.0 - BETA_TWO**STEP)) + ADAM_EPS)
    )
    return (weight - learn_rate * (scaled + decay_rate * weight), moment_one, moment_two)


def contract_rows(left_side, right_side):
    return lax.dot_general(
        left_side, right_side, (((0,), (0,)), ((), ())), preferred_element_type=F32
    )


def contract_cols(left_side, right_side):
    return lax.dot_general(
        left_side, right_side, (((1,), (1,)), ((), ())), preferred_element_type=F32
    )


def matmul(left_side, right_side):
    return jnp.dot(left_side, right_side, preferred_element_type=F32)


def segment_at(positions, seg_ends):
    counted = jnp.sum((positions[:, None] >= seg_ends[None, :]).astype(jnp.int32), axis=1)
    return jnp.where(positions < 0, jnp.int32(-1), counted)


def split_two(value):
    high = value.astype(BF16)
    return high, (value - high.astype(F32)).astype(BF16)


def split_three(value):
    high = value.astype(BF16)
    rest = value - high.astype(F32)
    middle = rest.astype(BF16)
    return high, middle, (rest - middle.astype(F32)).astype(BF16)


def product(left, right, left_dim, right_dim):
    return lax.dot_general(
        left, right, (((left_dim,), (right_dim,)), ((), ())), preferred_element_type=F32
    )


def joined_product(left_parts, right_parts, left_dim=1, right_dim=0):
    left_high, left_low = left_parts
    right_high, right_low = right_parts
    return product(
        jnp.concatenate([left_high, left_high, left_low], left_dim),
        jnp.concatenate([right_high, right_low, right_high], right_dim),
        left_dim,
        right_dim,
    )


def precise_product(left, right, left_dim=1, right_dim=0):
    return joined_product(split_two(left), split_two(right), left_dim, right_dim)


def ones_product(ones, value):
    return product(jnp.concatenate([ones] * 3, 1), jnp.concatenate(split_three(value), 0), 1, 0)


def spread(per_head, lane):
    return jnp.concatenate(
        [
            jnp.where(lane < P_SIZE, per_head[:, 2 * k : 2 * k + 1], per_head[:, 2 * k + 1 : 2 * k + 2])
            for k in range(OWN_H // 2)
        ],
        1,
    )


def head_sums(value):
    column = lax.broadcasted_iota(jnp.int32, (OWN, N), 0)
    head = lax.broadcasted_iota(jnp.int32, (OWN, N), 1)
    members = ((column >= head * P_SIZE) & (column < (head + 1) * P_SIZE)).astype(F32).astype(BF16)
    high, low = split_two(value)
    return product(jnp.concatenate([high, low], 1), jnp.concatenate([members, members], 0), 1, 0)


def two_heads(pair, lane):
    zero = jnp.zeros_like(pair)
    return jnp.concatenate([jnp.where(lane < P_SIZE, pair, zero), jnp.where(lane < P_SIZE, zero, pair)], 0)


def chunk_facts(ends, chunk, dt_pre, par):
    column = lax.broadcasted_iota(jnp.int32, (CHUNK, 1), 0) + chunk * CHUNK
    row = lax.broadcasted_iota(jnp.int32, (1, CHUNK), 1) + chunk * CHUNK

    def segment(position):
        counted = jnp.zeros_like(position)
        for k in range(3):
            counted = counted + (position >= ends[k]).astype(jnp.int32)
        return jnp.where(position < 0, -1, counted)

    def one_segment(position):
        counted = jnp.int32(0)
        for k in range(3):
            counted = counted + (position >= ends[k]).astype(jnp.int32)
        return jnp.where(position < 0, -1, counted)

    here_column, here_row = segment(column), segment(row)
    prior = one_segment(chunk * CHUNK - 1)
    last = one_segment(chunk * CHUNK + CHUNK - 1)
    lane = lax.broadcasted_iota(jnp.int32, (CHUNK, N), 1)
    shifted = dt_pre + par[6:7, :N]
    soft = jnp.maximum(shifted, 0.0) + jnp.log1p(jnp.exp(-jnp.abs(shifted)))
    step = jnp.where(lane < OWN_H, soft, 0.0)
    decay = step * par[7:8, :N]
    tri_row = lax.broadcasted_iota(jnp.int32, (CHUNK, CHUNK), 0)
    tri_column = lax.broadcasted_iota(jnp.int32, (CHUNK, CHUNK), 1)
    lower = (tri_row >= tri_column).astype(F32).astype(BF16)
    upper = (tri_row <= tri_column).astype(F32).astype(BF16)
    total = ones_product(lower, decay)
    entering = (here_column == prior).astype(F32) * jnp.exp(total)
    end = total[CHUNK - 1 : CHUNK]
    leaving = (here_column == last).astype(F32) * jnp.exp(jnp.minimum(end - total, 0.0))
    passing = jnp.where(last == prior, 1.0, 0.0) * jnp.exp(end)
    return dict(
        column=column,
        segment=segment,
        here_column=here_column,
        here_row=here_row,
        lane=lane,
        shifted=shifted,
        step=step,
        decay=decay,
        total=total,
        entering=entering,
        leaving=leaving,
        passing=passing,
        tri_row=tri_row,
        tri_column=tri_column,
        upper=upper,
    )


def forward_kernel(part, ends, proj, par, *refs):
    if part:
        carry_in, refs = refs[3], refs[4:]
    pre_out, mixed_out, state_out, carry_out, extended, state = refs
    chunk = pl.program_id(0) + part * HALF

    @pl.when(pl.program_id(0) == 0)
    def _():
        if part:
            state[...] = carry_in[:N, :OWN]
            extended[0:8, :] = carry_in[N:, :]
        else:
            state[...] = jnp.zeros_like(state)
            extended[0:8, :] = jnp.zeros((8, 640), F32)

    facts = chunk_facts(ends, chunk, proj[:, 1024:1152], par)
    lane = facts["lane"]
    conv = proj[:, OWN:1024].astype(BF16).astype(F32)
    extended[8 : 8 + CHUNK, :] = conv
    pre = par[4:5] + par[3:4] * conv
    for back in range(1, CONV):
        same = (facts["segment"](facts["column"] - back) == facts["here_column"]).astype(F32)
        pre = pre + par[3 - back : 4 - back] * (extended[8 - back : 8 - back + CHUNK, :] * same)
    extended[0:8, :] = extended[CHUNK : CHUNK + 8, :]
    pre_out[...] = pre
    act = pre * jax.nn.sigmoid(pre)
    own_x, state_b, state_c = act[:, :OWN], act[:, OWN : OWN + N], act[:, OWN + N :]
    stepped = own_x * spread(facts["step"], lane)
    b_parts, c_parts = split_two(state_b), split_two(state_c)
    inside = (facts["tri_row"] >= facts["tri_column"]) & (facts["here_column"] == facts["here_row"])
    scores = jnp.where(inside, joined_product(c_parts, b_parts, 1, 1), 0.0)
    total_rows = facts["total"].T
    state_in = state[...]
    state_out[...] = state_in
    outs = []
    for pair in range(OWN_H // 2):
        mixing = []
        for head in (2 * pair, 2 * pair + 1):
            span = facts["total"][:, head : head + 1] - total_rows[head : head + 1, :]
            mixing.append(jnp.exp(jnp.minimum(span, 0.0)) * scores)
        inner = two_heads(stepped[:, pair * N : pair * N + N], lane)
        outs.append(precise_product(jnp.concatenate(mixing, 1), inner))
    scanned = jnp.concatenate(outs, 1) + spread(facts["entering"], lane) * joined_product(
        c_parts, split_two(state_in)
    )
    state[...] = spread(facts["passing"], lane[:1]) * state_in + precise_product(
        state_b.T, stepped * spread(facts["leaving"], lane)
    )
    mixed_out[...] = scanned + par[5:6, :OWN] * own_x

    @pl.when(pl.program_id(0) == HALF - 1)
    def _():
        carry_out[:N, :OWN] = state[...]
        carry_out[:N, OWN:] = jnp.zeros((N, 640 - OWN), F32)
        carry_out[N:, :] = extended[0:8, :]


def run_forward(part, ends, proj, par, before=()):
    here = lambda i: (i + part * HALF, 0)
    chunked = lambda width: pl.BlockSpec((CHUNK, width), here)
    fixed = lambda shape: pl.BlockSpec(shape, lambda i: (0, 0))
    carry = fixed((N + 8, 640))
    return pl.pallas_call(
        partial(forward_kernel, part),
        grid=(HALF,),
        in_specs=[pl.BlockSpec(memory_space=pltpu.SMEM), chunked(1152), fixed((16, 640))]
        + ([pl.BlockSpec(memory_space=pl.ANY)] * 3 + [carry] if part else []),
        out_specs=[chunked(640), chunked(OWN), pl.BlockSpec((N, OWN), here), carry],
        out_shape=[
            jax.ShapeDtypeStruct((PACK, 640), F32),
            jax.ShapeDtypeStruct((PACK, OWN), F32),
            jax.ShapeDtypeStruct((CHUNKS * N, OWN), F32),
            jax.ShapeDtypeStruct((N + 8, 640), F32),
        ],
        input_output_aliases={3: 0, 4: 1, 5: 2} if part else {},
        scratch_shapes=[pltpu.VMEM((CHUNK + 8, 640), F32), pltpu.VMEM((N, OWN), F32)],
        compiler_params=pltpu.CompilerParams(
            dimension_semantics=("arbitrary",), vmem_limit_bytes=VMEM_LIMIT
        ),
        cost_estimate=COST,
        name="scan_forward",
    )(ends, proj, par, *before)


def backward_kernel(part, ends, conv_in, dt_in, pre_in, mixed_in, grad_mixed, state_all, par, *refs):
    if part:
        carry_in, sums_in, head_in, refs = refs[3], refs[4], refs[5], refs[6:]
    grad_x, grad_dt, grad_bc, sums, head_acc, carry_out, carried, extended, end_dot = refs
    step_index = pl.program_id(0)
    chunk = CHUNKS - 1 - part * HALF - step_index

    @pl.when(step_index == 0)
    def _():
        if part:
            carried[...] = carry_in[:N, :]
            extended[CHUNK : CHUNK + 8, :] = carry_in[N : N + 8, :]
            end_dot[...] = carry_in[N + 8 :, :N]
            sums[...] = sums_in[...]
            head_acc[...] = head_in[...]
        else:
            carried[...] = jnp.zeros_like(carried)
            extended[CHUNK : CHUNK + 8, :] = jnp.zeros((8, OWN), F32)
            end_dot[...] = jnp.zeros_like(end_dot)
            sums[...] = jnp.zeros_like(sums)
            head_acc[...] = jnp.zeros_like(head_acc)

    facts = chunk_facts(ends, chunk, dt_in[...], par)
    lane = facts["lane"]
    pre = pre_in[...]
    sig = jax.nn.sigmoid(pre)
    act = pre * sig
    own_x, state_b, state_c = act[:, :OWN], act[:, OWN : OWN + N], act[:, OWN + N :]
    step = facts["step"]
    step_wide = spread(step, lane)
    stepped = own_x * step_wide
    skip = par[5:6, :OWN]
    scanned = mixed_in[...] - skip * own_x
    grad_m = grad_mixed[...]
    sums[6:7] += jnp.sum(grad_m * own_x, 0, keepdims=True)

    b_parts, c_parts = split_two(state_b), split_two(state_c)
    inside = (facts["tri_row"] <= facts["tri_column"]) & (facts["here_column"] == facts["here_row"])
    scores = jnp.where(inside, joined_product(b_parts, c_parts, 1, 1), 0.0)
    total_rows = facts["total"].T
    grad_scores = jnp.zeros((CHUNK, CHUNK), F32)
    grad_stepped = []
    for pair in range(OWN_H // 2):
        columns = slice(pair * N, pair * N + N)
        grad_pair = grad_m[:, columns]
        high, low = split_two(grad_pair)
        stepped_parts = split_two(two_heads(stepped[:, columns], lane))
        grad_mixing = joined_product(stepped_parts, (high, low), 1, 1)
        mixing = []
        for k in range(2):
            head = 2 * pair + k
            span = total_rows[head : head + 1, :] - facts["total"][:, head : head + 1]
            decays = jnp.exp(jnp.minimum(span, 0.0))
            mixing.append(decays * scores)
            grad_scores = grad_scores + decays * grad_mixing[k * CHUNK : (k + 1) * CHUNK]
        grad_stepped.append(
            joined_product(
                split_two(jnp.concatenate(mixing, 1)), (two_heads(high, lane), two_heads(low, lane))
            )
        )
    grad_scores = jnp.where(inside, grad_scores, 0.0)
    carry = carried[...]
    carry_parts = split_two(carry)
    leaving = spread(facts["leaving"], lane)
    grad_stepped = jnp.concatenate(grad_stepped, 1) + leaving * joined_product(b_parts, carry_parts)
    state_in = state_all[...]
    entered = spread(facts["entering"], lane) * grad_m
    entered_parts = split_two(entered)
    grad_b = precise_product(grad_scores, state_c) + joined_product(
        split_two(leaving * stepped), carry_parts, 1, 1
    )
    grad_c = precise_product(grad_scores.T, state_b) + joined_product(
        entered_parts, split_two(state_in), 1, 1
    )
    grad_bc[0:N, :] = grad_b.T.astype(BF16)
    grad_bc[N:, :] = grad_c.T.astype(BF16)
    new_carry = spread(facts["passing"], lane[:1]) * carry + joined_product(
        split_two(state_c.T), entered_parts
    )
    carried[...] = new_carry

    grad_step = head_sums(own_x * grad_stepped)
    last_row = lax.broadcasted_iota(jnp.int32, (CHUNK, N), 0) == CHUNK - 1
    grad_total = head_sums(grad_m * scanned) - step * grad_step
    grad_total = grad_total + jnp.where(last_row, end_dot[0:1, :], 0.0)
    grad_decay = ones_product(facts["upper"], grad_total)
    end_dot[...] = head_sums(
        jnp.broadcast_to(jnp.sum(new_carry * state_in, 0, keepdims=True), (8, OWN))
    )
    grad_pre_dt = (grad_step + grad_decay * par[7:8, :N]) * jax.nn.sigmoid(facts["shifted"])
    grad_pre_dt = jnp.where(lane < OWN_H, grad_pre_dt, 0.0)
    grad_dt[...] = grad_pre_dt.astype(BF16)
    head_acc[0:1] += jnp.sum(grad_pre_dt, 0, keepdims=True)
    head_acc[1:2] += jnp.sum(grad_decay * facts["decay"], 0, keepdims=True)

    sig_x, pre_x = sig[:, :OWN], pre[:, :OWN]
    grad_pre = (step_wide * grad_stepped + skip * grad_m) * (sig_x * (1.0 + pre_x * (1.0 - sig_x)))
    extended[0:CHUNK, :] = grad_pre
    conv = conv_in[...].astype(BF16).astype(F32)
    sums[5:6] += jnp.sum(grad_pre, 0, keepdims=True)
    sums[4:5] += jnp.sum(conv * grad_pre, 0, keepdims=True)
    grad_conv = par[3:4, :OWN] * grad_pre
    for ahead in range(1, CONV):
        same = (facts["segment"](facts["column"] + ahead) == facts["here_column"]).astype(F32)
        later = extended[ahead : ahead + CHUNK, :] * same
        sums[4 - ahead : 5 - ahead] += jnp.sum(conv * later, 0, keepdims=True)
        grad_conv = grad_conv + par[3 - ahead : 4 - ahead, :OWN] * later
    extended[CHUNK : CHUNK + 8, :] = extended[0:8, :]
    grad_x[...] = grad_conv.astype(BF16)

    @pl.when(step_index == HALF - 1)
    def _():
        carry_out[:N, :] = carried[...]
        carry_out[N : N + 8, :] = extended[CHUNK : CHUNK + 8, :]
        carry_out[N + 8 :, :N] = end_dot[...]
        carry_out[N + 8 :, N:] = jnp.zeros((8, OWN - N), F32)


def run_backward(part, ends, proj, pre, mixed, grad_mixed, states, par, before=()):
    last = CHUNKS - 1 - part * HALF
    chunked = lambda width, column=0: pl.BlockSpec((CHUNK, width), lambda i: (last - i, column))
    fixed = lambda shape: pl.BlockSpec(shape, lambda i: (0, 0))
    carry = [fixed((N + 16, OWN)), fixed((8, OWN)), fixed((8, N))]
    return pl.pallas_call(
        partial(backward_kernel, part),
        grid=(HALF,),
        in_specs=[
            pl.BlockSpec(memory_space=pltpu.SMEM),
            chunked(OWN, 1),
            chunked(N, 8),
            chunked(640),
            chunked(OWN),
            chunked(OWN),
            pl.BlockSpec((N, OWN), lambda i: (last - i, 0)),
            fixed((16, 640)),
        ]
        + ([pl.BlockSpec(memory_space=pl.ANY)] * 3 + carry if part else []),
        out_specs=[
            chunked(OWN),
            chunked(N),
            pl.BlockSpec((2 * N, CHUNK), lambda i: (0, last - i)),
            carry[1],
            carry[2],
            carry[0],
        ],
        out_shape=[
            jax.ShapeDtypeStruct((PACK, OWN), BF16),
            jax.ShapeDtypeStruct((PACK, N), BF16),
            jax.ShapeDtypeStruct((2 * N, PACK), BF16),
            jax.ShapeDtypeStruct((8, OWN), F32),
            jax.ShapeDtypeStruct((8, N), F32),
            jax.ShapeDtypeStruct((N + 16, OWN), F32),
        ],
        input_output_aliases={8: 0, 9: 1, 10: 2} if part else {},
        scratch_shapes=[
            pltpu.VMEM((N, OWN), F32),
            pltpu.VMEM((CHUNK + 8, OWN), F32),
            pltpu.VMEM((8, N), F32),
        ],
        compiler_params=pltpu.CompilerParams(
            dimension_semantics=("arbitrary",), vmem_limit_bytes=VMEM_LIMIT
        ),
        cost_estimate=COST,
        name="scan_backward",
    )(ends, proj, proj, pre, mixed, grad_mixed, states, par, *before)


PARTS = (1, 1, 1, 1, 1, 2, 1, 1)
WHOLE = (1,) * N_REP
EARLY_SLOTS = (0, 1, 2, 6)
LATE_SLOTS = (3, 4, 5, 7)


def load_block(step, groups, block):
    for slot, refs in enumerate(groups):

        @pl.when(step == slot)
        def _(refs=refs):
            if len(refs) == 1:
                block[...] = refs[0][...]
            else:
                block[: ROWS // 2, :] = refs[0][...]
                block[ROWS // 2 :, :] = refs[1][...]


def grouped(refs, parts):
    groups = []
    for count in parts:
        groups.append(refs[:count])
        refs = refs[count:]
    return groups, refs


def piece_specs(parts):
    return [pl.BlockSpec((ROWS // count, D), lambda i, table: (0, 0)) for count in parts for _ in range(count)]


def project_kernel(parts, table, *refs):
    groups, (gain, shards, *refs) = grouped(refs, parts)
    normed_out, proj, dt_out, block, weight = refs[-5:]

    @pl.when(pl.program_id(0) == 0)
    def _():
        for f in range(N_FSDP):
            weight[f * SHARD_IN : (f + 1) * SHARD_IN, :] = shards[(f // 2) % 4, f % 2, f // 8]
        dt_out[...] = weight[:, 1024:]

    load_block(pl.program_id(0), groups, block)
    values = block[...].astype(F32)
    scale = lax.rsqrt(jnp.mean(values * values, axis=1, keepdims=True) + NORM_EPS)
    normed = (values * scale * gain[...]).astype(BF16)
    normed_out[...] = normed
    proj[...] = matmul(normed, weight[...])


def run_project(slots, table, pieces, gain, shards, before=()):
    fixed = lambda shape: pl.BlockSpec(shape, lambda i, table: (0,) * len(shape))
    placed = lambda width: pl.BlockSpec((ROWS, width), lambda i, table: (table[i], 0))
    parts = [PARTS[slot] for slot in slots]
    count = sum(parts)
    return pl.pallas_call(
        partial(project_kernel, parts),
        grid_spec=pltpu.PrefetchScalarGridSpec(
            num_scalar_prefetch=1,
            grid=(len(slots),),
            in_specs=piece_specs(parts)
            + [fixed((1, D)), fixed(shards.shape)]
            + [pl.BlockSpec(memory_space=pl.ANY)] * len(before),
            out_specs=[placed(D), placed(3 * WIDE), fixed((D, N))],
            scratch_shapes=[pltpu.VMEM((ROWS, D), BF16), pltpu.VMEM((D, 3 * WIDE), BF16)],
        ),
        out_shape=[
            jax.ShapeDtypeStruct((PACK, D), BF16),
            jax.ShapeDtypeStruct((PACK, 3 * WIDE), F32),
            jax.ShapeDtypeStruct((D, N), BF16),
        ],
        input_output_aliases={count + 3 + k: k for k in range(len(before))},
        compiler_params=pltpu.CompilerParams(
            dimension_semantics=("arbitrary",), vmem_limit_bytes=VMEM_LIMIT
        ),
        cost_estimate=COST,
        name="project",
    )(table, *pieces, gain, shards, *before)


def row_sums(value):
    folded = value[:, :N] + value[:, N : 2 * N] + value[:, 2 * N :]
    return jnp.sum(folded.T, 0, keepdims=True)


def out_grad_kernel(table, *refs):
    groups, refs = grouped(refs, WHOLE)
    w_out, mixed, gate_in, gain, branch_out, grad_out, sums, block, turned = refs

    @pl.when(pl.program_id(0) == 0)
    def _():
        turned[...] = w_out[...].reshape(OWN, D).T

    load_block(pl.program_id(0), groups, block)
    branch = block[...]
    branch_out[...] = branch
    total = matmul(branch, turned[...])
    grad_out[...] = total
    gate = gate_in[...]
    gated = mixed[...] * (gate * jax.nn.sigmoid(gate))
    row = lax.broadcasted_iota(jnp.int32, (8, ROWS), 0)
    sums[...] = jnp.where(
        row == 0, row_sums(gated * gated), jnp.where(row == 1, row_sums(total * gain[...] * gated), 0.0)
    )


def run_out_grad(table, pieces, w_out, mixed, proj, gain):
    fixed = lambda shape: pl.BlockSpec(shape, lambda i, table: (0, 0))
    placed = lambda width: pl.BlockSpec((ROWS, width), lambda i, table: (table[i], 0))
    return pl.pallas_call(
        out_grad_kernel,
        grid_spec=pltpu.PrefetchScalarGridSpec(
            num_scalar_prefetch=1,
            grid=(N_REP,),
            in_specs=piece_specs(WHOLE)
            + [
                pl.BlockSpec(
                    (1, 2, 1, SHARD_OUT, D), lambda i, table: (table[N_REP] % 4, 0, table[N_REP] // 4, 0, 0)
                )
            ]
            + [placed(OWN), placed(OWN), fixed((1, OWN))],
            out_specs=[placed(D), placed(OWN), pl.BlockSpec((8, ROWS), lambda i, table: (0, table[i]))],
            scratch_shapes=[pltpu.VMEM((ROWS, D), BF16), pltpu.VMEM((D, WIDE), BF16)],
        ),
        out_shape=[
            jax.ShapeDtypeStruct((PACK, D), BF16),
            jax.ShapeDtypeStruct((PACK, OWN), F32),
            jax.ShapeDtypeStruct((8, PACK), F32),
        ],
        compiler_params=pltpu.CompilerParams(
            dimension_semantics=("arbitrary",), vmem_limit_bytes=VMEM_LIMIT
        ),
        cost_estimate=COST,
        name="out_grad",
    )(table, *pieces, w_out, mixed, proj, gain)


def gate_kernel(
    where, grad_out, mixed_in, gate_in, sums, gain, grad_branch, normed,
    low_out, grad_mixed, keep, give, grad_gain, total,
):
    step = pl.program_id(0)
    rows = grad_out.shape[0]
    mixed, gate, grad_o = mixed_in[...], gate_in[...], grad_out[...]
    stats = jnp.concatenate([sums[...], jnp.zeros((N - 8, rows), F32)], 0).T
    out_scale = lax.rsqrt(stats[:, 0:1] * (1.0 / DI) + NORM_EPS)
    pull = out_scale * out_scale * out_scale * (stats[:, 1:2] * (1.0 / DI))
    gate_sig = jax.nn.sigmoid(gate)
    silu = gate * gate_sig
    gated = mixed * silu
    unit = gated * out_scale
    low = (unit * gain[...]).astype(BF16)
    grad_gated = out_scale * (grad_o * gain[...]) - gated * pull
    grad_mixed[...] = grad_gated * silu
    grad_z = (grad_gated * mixed * (gate_sig * (1.0 + gate * (1.0 - gate_sig)))).astype(BF16)
    low_out[:, :OWN] = low
    low_out[:, OWN:] = grad_z

    @pl.when(step == 0)
    def _():
        grad_gain[...] = jnp.zeros_like(grad_gain)
        total[...] = jnp.zeros_like(total)

    grad_gain[0:1] += jnp.sum(grad_o * unit, 0, keepdims=True)
    for k in range(4):
        part = product(low, grad_branch[:, k * WIDE : (k + 1) * WIDE], 0, 0)
        for m in range(4):
            total[4 * k + m, :SHARD_IN] += part[m * SHARD_IN : (m + 1) * SHARD_IN]
    part = product(normed[...], grad_z, 0, 0)
    for f in range(N_FSDP):
        total[f, SHARD_IN:] += part[f * SHARD_IN : (f + 1) * SHARD_IN]

    @pl.when(step == pl.num_programs(0) - 1)
    def _():
        for k in range(N_FSDP // 2):
            keep[k] = total[2 * k + where[0]]
            give[k] = total[2 * k + 1 - where[0]]


def run_gate(where, grad_out, mixed, proj, sums, gain, grad_branch, normed):
    count = 2 * ROWS
    rows = lambda width: pl.BlockSpec((count, width), lambda i: (i, 0))
    fixed = lambda shape: pl.BlockSpec(shape, lambda i: (0,) * len(shape))
    half = (N_FSDP // 2, 2 * SHARD_IN, WIDE)
    return pl.pallas_call(
        gate_kernel,
        grid=(PACK // count,),
        in_specs=[
            pl.BlockSpec(memory_space=pltpu.SMEM),
            rows(OWN),
            rows(OWN),
            rows(OWN),
            pl.BlockSpec((8, count), lambda i: (0, i)),
            fixed((1, OWN)),
            rows(D),
            rows(D),
        ],
        out_specs=[rows(2 * OWN), rows(OWN), fixed(half), fixed(half), fixed((8, OWN))],
        out_shape=[
            jax.ShapeDtypeStruct((PACK, 2 * OWN), BF16),
            jax.ShapeDtypeStruct((PACK, OWN), F32),
            jax.ShapeDtypeStruct(half, F32),
            jax.ShapeDtypeStruct(half, F32),
            jax.ShapeDtypeStruct((8, OWN), F32),
        ],
        scratch_shapes=[pltpu.VMEM((N_FSDP, 2 * SHARD_IN, WIDE), F32)],
        compiler_params=pltpu.CompilerParams(
            dimension_semantics=("arbitrary",), vmem_limit_bytes=VMEM_LIMIT
        ),
        cost_estimate=COST,
        name="gate_backward",
    )(where, grad_out, mixed, proj, sums, gain, grad_branch, normed)


def block_out_kernel(rows, weight, tokens, live, out):
    step = pl.program_id(0)
    part = matmul(jnp.concatenate([rows[0], rows[1]], 1), weight[...].reshape(2 * OWN, D))

    @pl.when(step == 0)
    def _():
        out[...] = part

    @pl.when(step > 0)
    def _():
        out[...] += part

    @pl.when(step == N_REP // 2 - 1)
    def _():
        out[...] = tokens[...].astype(F32) + live[...] * out[...]


def run_block_out(rows, weight, tokens, live):
    fixed = lambda shape: pl.BlockSpec(shape, lambda i: (0, 0))
    return pl.pallas_call(
        block_out_kernel,
        grid=(N_REP // 2,),
        in_specs=[
            pl.BlockSpec((2, ROWS, OWN), lambda i: (i, 0, 0)),
            pl.BlockSpec((2, 2, 1, SHARD_OUT, D), lambda i: (i % 2, 0, i // 2, 0, 0)),
            fixed((ROWS, D)),
            fixed((ROWS, 1)),
        ],
        out_specs=fixed((ROWS, D)),
        out_shape=jax.ShapeDtypeStruct((ROWS, D), F32),
        compiler_params=pltpu.CompilerParams(
            dimension_semantics=("arbitrary",), vmem_limit_bytes=VMEM_LIMIT
        ),
        cost_estimate=COST,
        name="block_out",
    )(rows, weight, tokens, live)


def turned_part(weight, rows):
    return product(weight[...].reshape(D, weight.shape[-1]), rows, 1, 1)


def columns_of(full_in, width, index):
    return pl.BlockSpec(full_in.shape[:-1] + (width,), lambda i: (0, 0, 0, 0, index(i)))


def z_grad_kernel(rows, weight, out):
    part = turned_part(weight, jnp.concatenate([rows[0], rows[1]], 1))

    @pl.when(pl.program_id(0) == 0)
    def _():
        out[...] = part

    @pl.when(pl.program_id(0) > 0)
    def _():
        out[...] += part


def x_grad_kernel(before, rows, weight, out):
    part = turned_part(weight, jnp.concatenate([rows[0], rows[1]], 1))

    @pl.when(pl.program_id(0) == 0)
    def _():
        out[...] = before[...] + part

    @pl.when(pl.program_id(0) > 0)
    def _():
        out[...] += part


def run_rows_grad(rows, full_in, before=None):
    fixed = pl.BlockSpec((D, ROWS), lambda i: (0, 0))
    column = 1 if before is None else 0
    first = 0 if before is None else N_REP // 2
    return pl.pallas_call(
        z_grad_kernel if before is None else x_grad_kernel,
        grid=(N_REP // 2,),
        in_specs=([] if before is None else [fixed])
        + [
            pl.BlockSpec((2, ROWS, OWN), lambda i: (i, 0, column)),
            columns_of(full_in, 2 * OWN, lambda i: first + i),
        ],
        out_specs=fixed,
        out_shape=jax.ShapeDtypeStruct((D, ROWS), F32),
        compiler_params=pltpu.CompilerParams(
            dimension_semantics=("arbitrary",), vmem_limit_bytes=VMEM_LIMIT
        ),
        cost_estimate=COST,
        name="z_grad" if before is None else "x_grad",
    )(*(() if before is None else (before,)), rows, full_in)


def input_grad_kernel(total, rest_rows, w_bc, low_dt, tokens, cotangent, gain, out, gain_out, ordered):
    lane = lax.broadcasted_iota(jnp.int32, (ROWS, N), 1)
    groups = []
    for k in range(2):
        group = jnp.zeros((ROWS, N), F32)
        for m in range(4):
            value = rest_rows[4 * k + m].astype(F32)
            value = value if m == 0 else pltpu.roll(value, m * OWN_BC, 1)
            group = jnp.where((lane >= m * OWN_BC) & (lane < (m + 1) * OWN_BC), value, group)
        groups.append(group.astype(BF16))
    steps = jnp.zeros((ROWS, N), F32)
    for m in range(N_REP):
        start = 8 + m * OWN_H
        value = pltpu.roll(rest_rows[m].astype(F32), (start - OWN_BC) % N, 1)
        steps = jnp.where((lane >= start) & (lane < start + OWN_H), value, steps)
    shared = total[...] + turned_part(w_bc, jnp.concatenate(groups, 1))
    for f in range(N_FSDP):
        start = (((f // 2) % 4 * 2 + f % 2) * 2 + f // 8) * SHARD_IN
        ordered[f * SHARD_IN : (f + 1) * SHARD_IN, :] = shared[start : start + SHARD_IN, :]
    grad_h = (ordered[...] + product(low_dt[...], steps.astype(BF16), 1, 1)).T
    values = tokens[...].astype(F32)
    scale = lax.rsqrt(jnp.mean(values * values, axis=1, keepdims=True) + NORM_EPS)
    unit = values * scale
    gain_sum = jnp.sum(grad_h * unit, 0, keepdims=True)
    gain_out[...] = jnp.zeros_like(gain_out)
    for k in range(D // N):
        gain_out[k : k + 1, :] = gain_sum[:, k * N : (k + 1) * N]
    grad_unit = grad_h * gain[...]
    inner = jnp.mean(grad_unit * unit, axis=1, keepdims=True)
    out[...] = cotangent[...].astype(F32) + scale * (grad_unit - unit * inner)


def run_input_grad(total, rest_rows, full_in, low_dt, tokens, cotangent, gain):
    fixed = lambda shape: pl.BlockSpec(shape, lambda i: (0,) * len(shape))
    return pl.pallas_call(
        input_grad_kernel,
        grid=(1,),
        in_specs=[
            fixed((D, ROWS)),
            fixed((N_REP, ROWS, N)),
            columns_of(full_in, 2 * N, lambda i: DI // N),
            fixed((D, N)),
            fixed((ROWS, D)),
            fixed((ROWS, D)),
            fixed((1, D)),
        ],
        out_specs=[fixed((ROWS, D)), fixed((16, N))],
        out_shape=[jax.ShapeDtypeStruct((ROWS, D), F32), jax.ShapeDtypeStruct((16, N), F32)],
        scratch_shapes=[pltpu.VMEM((D, ROWS), F32)],
        compiler_params=pltpu.CompilerParams(
            dimension_semantics=("arbitrary",), vmem_limit_bytes=VMEM_LIMIT
        ),
        cost_estimate=COST,
        name="input_grad",
    )(total, rest_rows, full_in, low_dt, tokens, cotangent, gain)


def rest_kernel(ends, parts, pre_b, pre_c, conv_in, par, grad_dt, sums, head_acc, grad_gain, first, rest_out, small_out):
    own = lax.broadcasted_iota(jnp.int32, (OWN_BC, 2 * N), 0) + first[0]
    chosen = (lax.broadcasted_iota(jnp.int32, (OWN_BC, 2 * N), 1) == own).astype(F32).astype(BF16)

    def pick(value):
        return product(jnp.concatenate([chosen] * 3, 1), jnp.concatenate(split_three(value), 1), 1, 1)

    grad = parts[0].astype(F32)
    for k in range(1, N_REP):
        grad = grad + parts[k].astype(F32)
    own_pre = pick(jnp.concatenate([pre_b[...], pre_c[...]], 1))
    own_conv = product(chosen, conv_in[...].astype(BF16), 1, 1)
    taps = pick(par[:, OWN:])
    sig = jax.nn.sigmoid(own_pre)
    grad_pre = grad * (sig * (1.0 + own_pre * (1.0 - sig)))
    position = lax.broadcasted_iota(jnp.int32, (1, PACK), 1)

    def segment(places):
        counted = jnp.zeros_like(places)
        for k in range(3):
            counted = counted + (places >= ends[k]).astype(jnp.int32)
        return counted

    grad_conv = taps[:, CONV - 1 : CONV] * grad_pre
    column = lax.broadcasted_iota(jnp.int32, (OWN_BC, N), 1)
    found = jnp.where(column == CONV, jnp.sum(grad_pre, 1, keepdims=True), 0.0)
    found = jnp.where(column == CONV - 1, jnp.sum(own_conv * grad_pre, 1, keepdims=True), found)
    for later_by in range(1, CONV):
        same = (segment(position + later_by) == segment(position)) & (position < PACK - later_by)
        later = jnp.where(same, pltpu.roll(grad_pre, PACK - later_by, 1), 0.0)
        tap = CONV - 1 - later_by
        found = jnp.where(column == tap, jnp.sum(own_conv * later, 1, keepdims=True), found)
        grad_conv = grad_conv + taps[:, tap : tap + 1] * later
    lane = lax.broadcasted_iota(jnp.int32, (N, N), 1)
    filler = jnp.zeros((N - OWN_BC, N), F32)
    for k in range(PACK // N):
        rows = slice(k * N, (k + 1) * N)
        columns = jnp.concatenate([grad_conv[:, rows], filler], 0).T
        steps = pltpu.roll(grad_dt[rows, :].astype(F32), OWN_BC, 1)
        rest_out[rows, :] = jnp.where(
            lane < OWN_BC, columns, jnp.where(lane < OWN_BC + OWN_H, steps, 0.0)
        ).astype(BF16)
    row = lax.broadcasted_iota(jnp.int32, (8, OWN), 0)
    skip = head_sums(sums[...])
    by_head = jnp.concatenate([skip, jnp.zeros((8, OWN - N), F32)], 1)
    logs = jnp.concatenate([head_acc[...], jnp.zeros((8, OWN - N), F32)], 1)
    wide = jnp.where(row == 0, grad_gain[0:1, :], jnp.where(row < 6, sums[...], 0.0))
    wide = jnp.where(row == 6, logs[1:2, :], jnp.where(row == 7, by_head[6:7, :], wide))
    turned = jnp.concatenate([found, filler], 0).T
    first_row = lax.broadcasted_iota(jnp.int32, (8, N), 0) == 0
    for k in range(3):
        small_out[8 * k : 8 * k + 8, :] = wide[:, k * N : (k + 1) * N]
    small_out[24:32, :] = jnp.where(first_row, head_acc[0:1, :], pltpu.roll(turned[:8], 1, 0))


def run_rest(ends, parts, pre, proj, par, grad_dt, sums, head_acc, grad_gain, first):
    fixed = lambda shape: pl.BlockSpec(shape, lambda i: (0,) * len(shape))
    return pl.pallas_call(
        rest_kernel,
        grid=(1,),
        in_specs=[
            pl.BlockSpec(memory_space=pltpu.SMEM),
            fixed((N_REP, OWN_BC, PACK)),
            pl.BlockSpec((PACK, N), lambda i: (0, 3)),
            pl.BlockSpec((PACK, N), lambda i: (0, 4)),
            pl.BlockSpec((PACK, 2 * N), lambda i: (0, 3)),
            fixed((16, 640)),
            fixed((PACK, N)),
            fixed((8, OWN)),
            fixed((8, N)),
            fixed((8, OWN)),
            pl.BlockSpec(memory_space=pltpu.SMEM),
        ],
        out_specs=[fixed((PACK, N)), fixed((32, N))],
        out_shape=[jax.ShapeDtypeStruct((PACK, N), BF16), jax.ShapeDtypeStruct((32, N), F32)],
        compiler_params=pltpu.CompilerParams(
            dimension_semantics=("arbitrary",), vmem_limit_bytes=VMEM_LIMIT
        ),
        cost_estimate=COST,
        name="rest_backward",
    )(ends, parts, pre, pre, proj, par, grad_dt, sums, head_acc, grad_gain, first)


def adam_step(grad, weight, first, second, grad_out, first_out, second_out, weight_out):
    new_weight, new_first, new_second = adam_update(
        weight[...], grad, first[...], second[...], RATE_MATRIX, WEIGHT_DECAY
    )
    grad_out[...] = grad
    first_out[...] = new_first
    second_out[...] = new_second
    weight_out[...] = new_weight


def load_pair(step, pairs, rows, grad):
    pair, right, far_first, far_second, left = pairs
    for slot, (low, high) in enumerate(
        (((pair, 0), (pair, 1)), ((right, 0), (right, 1)), ((far_first, 0), (far_second, 0)), ((left, 0), (left, 1)))
    ):

        @pl.when(step == slot)
        def _(low=low, high=high):
            grad[:, :WIDE] = low[0][low[1], rows, :]
            grad[:, WIDE:] = high[0][high[1], rows, :]


def adam_pairs_kernel(rows, table, *refs):
    pairs, arrays, grad = refs[:5], refs[5:8] + refs[-5:-1], refs[-1]
    load_pair(pl.program_id(0), pairs, rows, grad)
    adam_step(grad[...], *arrays)


def run_adam_pairs(table, place_of, rows, pairs, weight, first, second, before=()):
    part = pl.BlockSpec((SHARD_IN, 2 * WIDE), lambda i, table: place_of(table[i]))
    shape = jax.ShapeDtypeStruct(weight.shape, F32)
    return pl.pallas_call(
        partial(adam_pairs_kernel, rows),
        grid_spec=pltpu.PrefetchScalarGridSpec(
            num_scalar_prefetch=1,
            grid=(4,),
            in_specs=[pl.BlockSpec(pair.shape, lambda i, table: (0, 0, 0)) for pair in pairs]
            + [part] * 3
            + [pl.BlockSpec(memory_space=pl.ANY)] * len(before),
            out_specs=[part] * 4,
            scratch_shapes=[pltpu.VMEM((SHARD_IN, 2 * WIDE), F32)],
        ),
        out_shape=[shape] * 4,
        input_output_aliases={9 + k: k for k in range(len(before))},
        compiler_params=pltpu.CompilerParams(
            dimension_semantics=("arbitrary",), vmem_limit_bytes=VMEM_LIMIT
        ),
        cost_estimate=COST,
        name="adam",
    )(table, *pairs, weight, first, second, *before)


def adam_rest_kernel(parts, weight, first, second, *refs):
    lane = lax.broadcasted_iota(jnp.int32, (SHARD_IN, N), 1)
    groups = []
    for k in range(2):
        group = jnp.zeros((SHARD_IN, N), F32)
        for m in range(4):
            value = parts[4 * k + m, :SHARD_IN]
            value = value if m == 0 else pltpu.roll(value, m * OWN_BC, 1)
            group = jnp.where((lane >= m * OWN_BC) & (lane < (m + 1) * OWN_BC), value, group)
        groups.append(group)
    adam_step(jnp.concatenate(groups, 1), weight, first, second, *refs[-4:])


def run_adam_rest(parts, weight, first, second, before):
    column = pl.BlockSpec((SHARD_IN, 2 * N), lambda i: (0, DI // N))
    shape = jax.ShapeDtypeStruct(weight.shape, F32)
    return pl.pallas_call(
        adam_rest_kernel,
        grid=(1,),
        in_specs=[pl.BlockSpec(parts.shape, lambda i: (0, 0, 0))]
        + [column] * 3
        + [pl.BlockSpec(memory_space=pl.ANY)] * 4,
        out_specs=[column] * 4,
        out_shape=[shape] * 4,
        input_output_aliases={4 + k: k for k in range(4)},
        compiler_params=pltpu.CompilerParams(
            dimension_semantics=("arbitrary",), vmem_limit_bytes=VMEM_LIMIT
        ),
        cost_estimate=COST,
        name="adam_rest",
    )(parts, weight, first, second, *before)


def body(
    tokens,
    cotangent,
    lengths,
    w_in,
    w_dt,
    w_out,
    small,
    first_in,
    first_dt,
    first_out,
    first_small,
    second_in,
    second_dt,
    second_out,
    second_small,
):
    place = Place()
    r = place.r
    zero = jnp.int32(0)
    pack_lengths = lax.dynamic_slice_in_dim(lengths, place.f, 1, 0)[0]
    seg_ends = jnp.cumsum(pack_lengths)
    own_positions = r * ROWS + jnp.arange(ROWS, dtype=jnp.int32)
    own_live = (segment_at(own_positions, seg_ends) < 3).astype(F32)[:, None]
    slots = jnp.arange(N_REP, dtype=jnp.int32)
    ahead = ((place.x + slots // 2) % 4) * 2 + (place.yl + slots) % 2
    half = ROWS // 2

    in_low = w_in.astype(BF16)
    dt_low = w_dt.astype(BF16)
    out_low = w_out.astype(BF16)

    small_block = jnp.pad(small.astype(BF16), (0, 16 * N - SHARD_SMALL)).reshape(1, 16, N)
    small_all = exchange(jnp.broadcast_to(small_block, (N_FSDP, 16, N)), "fsdp")

    def own_columns(rep):
        return jnp.concatenate(
            [
                lax.dynamic_slice_in_dim(in_low, rep * OWN, OWN, 1),
                lax.dynamic_slice_in_dim(in_low, DI + rep * OWN, OWN, 1),
                in_low[:, 2 * DI :],
                lax.dynamic_slice_in_dim(dt_low, rep * OWN_H, OWN_H, 1),
                jnp.zeros((SHARD_IN, 2), BF16),
                dt_low,
                jnp.zeros((SHARD_IN, N - 8 - H), BF16),
            ],
            1,
        )

    other_columns = move(
        own_columns(2 * place.x + 1 - place.yl), lambda yh, z, c, x, yl: (yh + 1, z, c, x, yl + 1)
    )
    from_left = move(tokens, along_x(1))
    from_right = move(tokens, along_x(-1))
    partner = move(tokens, swap_y)

    from_left, from_right, partner, out_low, other_columns, small_all = lax.optimization_barrier(
        (from_left, from_right, partner, out_low, other_columns, small_all)
    )
    own_shards = gather_eight(both(own_columns(r), other_columns, place.yh))
    far = move(from_left, along_x(1))
    partner_left = move(from_left, swap_y)
    partner_right = move(partner, along_x(-1))
    out_pair = swap_shards(out_low, place)

    far, partner_left, partner_right, out_pair = lax.optimization_barrier(
        (far, partner_left, partner_right, out_pair)
    )
    partner_far_top = move(partner_left[:half], along_x(1))
    partner_far_low = move(partner_right[half:], along_x(-1))

    vector = small_all.reshape(N_FSDP, 16 * N)[:, :SHARD_SMALL].reshape(-1).astype(F32)
    offset = 0
    gain_in = vector[None, :D]
    offset = D
    gain_row = lax.dynamic_slice_in_dim(vector, offset + r * OWN, OWN, 0)[None, :]
    offset += DI
    taps = vector[offset : offset + (CONV + 1) * CHANNELS].reshape(CONV + 1, CHANNELS)
    offset += (CONV + 1) * CHANNELS
    per_head = vector[offset:].reshape(3, H)
    dt_bias, a_log, d_skip = lax.dynamic_slice_in_dim(per_head, r * OWN_H, OWN_H, 1)
    taps_bc = taps[:, DI:]
    conv_par = jnp.concatenate([lax.dynamic_slice_in_dim(taps, r * OWN, OWN, 1), taps_bc], 1)
    head_par = jnp.stack(
        [
            jnp.pad(jnp.broadcast_to(d_skip[:, None], (OWN_H, P_SIZE)).reshape(-1), (0, 2 * N)),
            jnp.pad(dt_bias, (0, 640 - OWN_H)),
            jnp.pad(-jnp.exp(a_log), (0, 640 - OWN_H)),
        ],
        0,
    )
    par = jnp.concatenate([conv_par, head_par, jnp.zeros((8, 640), F32)], 0)

    branch = (cotangent.astype(F32) * own_live).astype(BF16)
    token_pieces = [
        (tokens,), (partner,), (from_right,), (partner_right,), (far,),
        (partner_far_top, partner_far_low), (from_left,), (partner_left,),
    ]

    def chosen(slots):
        return jnp.stack([ahead[slot] for slot in slots]), [piece for slot in slots for piece in token_pieces[slot]]

    own_shards, far = lax.optimization_barrier((own_shards, far))
    full_out = gather_eight(tie(out_pair, own_shards))
    before = run_project(EARLY_SLOTS, *chosen(EARLY_SLOTS), gain_in, own_shards)
    branch, in_low, before = lax.optimization_barrier((branch, in_low, before))
    in_other = move(in_low, lambda yh, z, c, x, yl: (yh + 1, z, c, x, yl + 1))
    b_left = move(branch, along_x(1))
    b_right = move(branch, along_x(-1))
    b_partner = move(branch, swap_y)
    normed, proj, low_dt = run_project(LATE_SLOTS, *chosen(LATE_SLOTS), gain_in, own_shards, before)
    b_left, b_right, b_partner, proj, in_other, in_low = lax.optimization_barrier(
        (b_left, b_right, b_partner, proj, in_other, in_low)
    )
    full_in = gather_eight(both(in_low, in_other, place.yh))
    b_far = move(b_left, along_x(1))
    b_partner_left = move(b_left, swap_y)
    b_partner_right = move(b_partner, along_x(-1))
    before = run_forward(0, seg_ends, proj, par)
    b_partner_left, before = lax.optimization_barrier((b_partner_left, before))
    b_partner_far = move(b_partner_left, along_x(1))
    pre, mixed, states, _ = run_forward(1, seg_ends, proj, par, before)
    branch_pieces = [branch, b_partner, b_right, b_partner_right, b_far, b_partner_far, b_left, b_partner_left]
    rep_table = jnp.concatenate([ahead, r[None]])
    grad_branch, grad_normed_out, sums = run_out_grad(rep_table, branch_pieces, full_out, mixed, proj, gain_row)
    sums = sum_rep(sums[:2].reshape(32, 128)).reshape(2, PACK)
    sums = jnp.concatenate([sums, jnp.zeros((6, PACK), F32)], 0)

    low_rows, grad_mixed, keep, give, grad_gain = run_gate(
        place.c[None], grad_normed_out, mixed, proj, sums, gain_row, grad_branch, normed
    )

    low_rows = exchange(low_rows.reshape(N_REP, ROWS, 2 * OWN), "rep")
    got = move(give, swap_core)
    before = run_backward(0, seg_ends, proj, pre, mixed, grad_mixed, states, par)
    got, before = lax.optimization_barrier((got, before))
    split = (2, 4, 2 * SHARD_IN, WIDE)
    early, _ = scatter_ring(keep.reshape(split), got.reshape(split), None, place)
    grad_x, grad_dtraw, grad_bc, grad_sums, grad_heads, _ = run_backward(
        1, seg_ends, proj, pre, mixed, grad_mixed, states, par,
        (before[0], before[1], before[2], before[5], before[3], before[4]),
    )
    low_rows, grad_bc, grad_x = lax.optimization_barrier((low_rows, grad_bc, grad_x))

    grad_bc = exchange(grad_bc, "rep").reshape(N_REP, OWN_BC, PACK)
    block_out = run_block_out(low_rows, full_out, tokens, own_live)
    grad_x, block_out = lax.optimization_barrier((grad_x, block_out))
    grad_x_own = contract_rows(normed, grad_x).reshape(2, 4, 2, SHARD_IN, OWN)
    x_keep, x_give = at(grad_x_own, place.c, 2), at(grad_x_own, 1 - place.c, 2)
    grad_rows = run_rows_grad(low_rows, full_in)
    grad_bc, x_give, grad_x, early, grad_rows = lax.optimization_barrier(
        (grad_bc, x_give, grad_x, early, grad_rows)
    )

    x_rows = exchange(grad_x.reshape(N_REP, ROWS, OWN), "rep")
    x_got = move(x_give, swap_core)
    out_part = move(
        early[:SHARD_IN],
        lambda yh, z, c, x, yl: (x // 2, (x % 2) * 2 + yl, z % 2, 2 * c + yh, z // 2),
    )
    rest, small_own = run_rest(
        seg_ends, grad_bc, pre, proj, par, grad_dtraw, grad_sums, grad_heads, grad_gain, (r * OWN_BC)[None]
    )
    grad_rest = contract_rows(normed, rest).reshape(2, 4, 2, SHARD_IN, N)
    rest_keep = at(grad_rest, place.c, 2)
    rest_give = with_rows(at(grad_rest, 1 - place.c, 2), small_own)
    x_rows, rest, rest_give, x_got, out_part = lax.optimization_barrier((x_rows, rest, rest_give, x_got, out_part))

    rest_rows = exchange(rest.reshape(N_REP, ROWS, N), "rep")
    rest_got = move(rest_give, swap_core)
    x_part, _ = scatter_ring(x_keep, x_got, None, place)
    early = jnp.concatenate([out_part, early[SHARD_IN:]], 0)
    early_other = move(early, swap_y)
    grad_rows = run_rows_grad(x_rows, full_in, grad_rows)
    rest_rows, grad_rows, rest_got, early_other = lax.optimization_barrier(
        (rest_rows, grad_rows, rest_got, early_other)
    )

    rest_part, small_sum = scatter_ring(
        rest_keep, rest_got[: -small_own.shape[0]].reshape(rest_keep.shape),
        small_own + rest_got[-small_own.shape[0] :], place,
    )
    early_pairs = gather_pairs(both(early, early_other, place.yl))
    input_grad, grad_gain_in = run_input_grad(
        grad_rows, rest_rows, full_in, low_dt, tokens, cotangent, gain_in
    )
    grad_gain_in = sum_fsdp(grad_gain_in)
    x_pairs = gather_pairs(both(x_part, move(x_part, swap_y), place.yl))
    rest_block = jnp.concatenate([rest_part, small_sum, grad_gain_in], 0)
    rest_block, *early_pairs = lax.optimization_barrier((rest_block, *early_pairs))
    rest_parts = share_rep(rest_block)

    x_order = (place.x + jnp.arange(4, dtype=jnp.int32)) % 4
    grad_out, new_first_out, new_second_out, new_out = run_adam_pairs(
        x_order, lambda k: (k // 2, k % 2), slice(0, SHARD_IN), early_pairs, w_out, first_out, second_out
    )
    updated = run_adam_pairs(
        x_order, lambda k: (0, k), slice(SHARD_IN, 2 * SHARD_IN), early_pairs, w_in, first_in, second_in
    )
    updated = run_adam_pairs(
        x_order, lambda k: (0, 4 + k), slice(0, SHARD_IN), x_pairs, w_in, first_in, second_in, updated
    )
    grad_in, new_first_in, new_second_in, new_in = run_adam_rest(rest_parts, w_in, first_in, second_in, updated)

    def columns(parts):
        return parts.transpose(1, 0, 2).reshape(parts.shape[1], -1)

    grad_gain_in = rest_parts[:, SHARD_IN + 32 : SHARD_IN + 32 + D // N].sum(0).reshape(-1)
    small_parts = rest_parts[:, SHARD_IN : SHARD_IN + 32].reshape(N_REP, 4, 8, N)
    small_x = small_parts[:, :3].transpose(2, 0, 1, 3).reshape(8, DI)
    small_bc = small_parts[:, 3].transpose(1, 0, 2)

    def channels(row):
        return jnp.concatenate([small_x[row], small_bc[row, :, :OWN_BC].reshape(-1)])

    grad_small_all = jnp.concatenate(
        [grad_gain_in, small_x[0]]
        + [channels(row) for row in range(1, 6)]
        + [
            small_bc[0, :, :OWN_H].reshape(-1),
            small_parts[:, 0, 6, :OWN_H].reshape(-1),
            small_parts[:, 0, 7, :OWN_H].reshape(-1),
        ]
    )
    grad_small = lax.dynamic_slice_in_dim(grad_small_all, place.f * SHARD_SMALL, SHARD_SMALL, 0)
    grad_dt = columns(rest_parts[:, :SHARD_IN, OWN_BC : OWN_BC + OWN_H])
    new_dt, new_first_dt, new_second_dt = adam_update(
        w_dt, grad_dt, first_dt, second_dt, RATE_MATRIX, WEIGHT_DECAY
    )
    new_small, new_first_small, new_second_small = adam_update(
        small, grad_small, first_small, second_small, RATE_SMALL, 0.0
    )
    return (
        block_out,
        input_grad,
        grad_in,
        grad_dt,
        grad_out,
        grad_small,
        new_first_in,
        new_first_dt,
        new_first_out,
        new_first_small,
        new_second_in,
        new_second_dt,
        new_second_out,
        new_second_small,
        new_in,
        new_dt,
        new_out,
        new_small,
    )


def solution(mesh):
    rows = P(("fsdp", "rep"), None)
    matrix = P("fsdp", None)
    vector = P("fsdp")
    group = (matrix, matrix, matrix, vector)
    return jax.shard_map(
        body,
        mesh=mesh,
        in_specs=(rows, rows, P()) + group * 3,
        out_specs=(rows, rows) + group * 4,
        check_vma=False,
    )
```

```python
from functools import partial

import jax
import jax.numpy as jnp
from jax import lax
from jax.experimental import pallas as pl
from jax.experimental.pallas import tpu as pltpu
from jax.sharding import PartitionSpec as P

D = 1536
H = 48
P_SIZE = 64
N = 128
CONV = 4
STEP = 10
DI = 3072
CHANNELS = DI + 2 * N
SMALL = 21392
N_FSDP = 16
N_REP = 8
ROWS = 256
PACK = 2048
OWN = DI // N_REP
OWN_H = H // N_REP
OWN_BC = 2 * N // N_REP
SHARD_IN = D // N_FSDP
SHARD_OUT = DI // N_FSDP
SHARD_SMALL = SMALL // N_FSDP
WIDE = 384
CHUNK = 128
CHUNKS = PACK // CHUNK
HALF = CHUNKS // 2
TAIL = 512
VMEM_LIMIT = 60 * 1024 * 1024

NORM_EPS = 1e-05
BETA_ONE = 0.9
BETA_TWO = 0.999
ADAM_EPS = 1e-08
WEIGHT_DECAY = 0.1
RATE_MATRIX = 0.04
RATE_SMALL = 0.4
PRECISE = lax.Precision.HIGHEST
BF16 = jnp.bfloat16
F32 = jnp.float32
COST = pl.CostEstimate(flops=1_000_000, bytes_accessed=100_000, transcendentals=0)
FILL = pl.CostEstimate(flops=2_400_000_000, bytes_accessed=20_000_000, transcendentals=0)


def move(value, target):
    pairs = []
    for f in range(N_FSDP):
        for r in range(N_REP):
            yh, z, c, x, yl = target(f // 8, (f // 2) % 4, f % 2, r // 2, r % 2)
            pairs.append((f * N_REP + r, ((yh % 2) * 8 + (z % 4) * 2 + c % 2) * N_REP + (x % 4) * 2 + yl % 2))
    return lax.ppermute(value, ("fsdp", "rep"), pairs)


def along_x(steps):
    return lambda yh, z, c, x, yl: (yh, z, c, x + steps, yl)


def along_z(steps):
    return lambda yh, z, c, x, yl: (yh, z + steps, c, x, yl)


def swap_y(yh, z, c, x, yl):
    return (yh, z, c, x, yl + 1)


def swap_y_hi(yh, z, c, x, yl):
    return (yh + 1, z, c, x, yl)


def swap_core(yh, z, c, x, yl):
    return (yh, z, c + 1, x, yl)


class Place:
    def __init__(self):
        f = lax.axis_index("fsdp")
        r = lax.axis_index("rep")
        self.f, self.r = f, r
        self.yh, self.z, self.c = f // 8, (f // 2) % 4, f % 2
        self.x, self.yl = r // 2, r % 2


def at(value, index, axis=0):
    return lax.dynamic_index_in_dim(value, index, axis, keepdims=False)


def tie(values, *others):
    return lax.optimization_barrier((values, others))[0]


def both(mine, other, second):
    first = jnp.where(second == 0, mine, other)
    last = jnp.where(second == 0, other, mine)
    return jnp.stack([first, last], 0)


def put(out, piece, axis, index):
    starts = [jnp.int32(0)] * out.ndim
    starts[axis] = jnp.int32(index)
    return lax.dynamic_update_slice(out, jnp.expand_dims(piece, axis), tuple(starts))


def swap_shards(value, place):
    other = move(value, lambda yh, z, c, x, yl: (yh + 1, z, c, x, yl + 1))
    return both(value, other, place.yh)


def gather_eight(pair):
    groups = [list(range(8)), list(range(8, 16))]
    out = lax.all_gather(pair, "fsdp", axis=0, tiled=True, axis_index_groups=groups)
    return out.reshape((4, 2) + pair.shape)


def start_ring(keep, got, extra, place):
    own = at(keep, place.z, 1) + at(got, place.z, 1)
    found = []
    for step in (1, 3, 2):
        there = (place.z + step) % 4
        found.append(move(with_rows(at(keep, there, 1) + at(got, there, 1), extra), along_z(step)))
    return own, found


def end_ring(own, found, extra):
    rows = own.shape[0] * own.shape[1]
    total = own
    for part in found:
        total = total + part[:rows].reshape(own.shape)
        extra = None if extra is None else extra + part[rows:]
    return total, extra


def start_half(total, extra, place):
    return at(total, place.yh), move(with_rows(at(total, 1 - place.yh), extra), swap_y_hi)


def end_half(mine, other, extra):
    rows = mine.shape[0]
    return mine + other[:rows], None if extra is None else extra + other[rows:]


def exchange(value, axis):
    return lax.all_to_all(value, axis, 0, 0, tiled=True)


def share_rep(value):
    return exchange(jnp.broadcast_to(value[None], (N_REP,) + value.shape), "rep")


def sum_rep(value):
    value = value + move(value, swap_y)
    value = value + move(value, lambda yh, z, c, x, yl: (yh, z, c, x ^ 1, yl))
    return value + move(value, lambda yh, z, c, x, yl: (yh, z, c, x ^ 2, yl))


def sum_all(value):
    value = sum_rep(value)
    value = value + move(value, swap_core)
    value = value + move(value, lambda yh, z, c, x, yl: (yh, z ^ 1, c, x, yl))
    value = value + move(value, lambda yh, z, c, x, yl: (yh, z ^ 2, c, x, yl))
    return value + move(value, swap_y_hi)


def with_rows(block, extra):
    width = block.shape[-1]
    flat = block.reshape(-1, width)
    return flat if extra is None else jnp.concatenate([flat, extra], 0)


def adam_update(weight, gradient, moment_one, moment_two, learn_rate, decay_rate):
    moment_one = BETA_ONE * moment_one + (1.0 - BETA_ONE) * gradient
    moment_two = BETA_TWO * moment_two + (1.0 - BETA_TWO) * gradient * gradient
    scaled = (
        moment_one
        / (1.0 - BETA_ONE**STEP)
        / (jnp.sqrt(moment_two / (1.0 - BETA_TWO**STEP)) + ADAM_EPS)
    )
    return (weight - learn_rate * (scaled + decay_rate * weight), moment_one, moment_two)


def contract_rows(left_side, right_side):
    return lax.dot_general(
        left_side, right_side, (((0,), (0,)), ((), ())), preferred_element_type=F32
    )


def contract_cols(left_side, right_side):
    return lax.dot_general(
        left_side, right_side, (((1,), (1,)), ((), ())), preferred_element_type=F32
    )


def matmul(left_side, right_side):
    return jnp.dot(left_side, right_side, preferred_element_type=F32)


def segment_at(positions, seg_ends):
    counted = jnp.sum((positions[:, None] >= seg_ends[None, :]).astype(jnp.int32), axis=1)
    return jnp.where(positions < 0, jnp.int32(-1), counted)


def split_two(value):
    high = value.astype(BF16)
    return high, (value - high.astype(F32)).astype(BF16)


def split_three(value):
    high = value.astype(BF16)
    rest = value - high.astype(F32)
    middle = rest.astype(BF16)
    return high, middle, (rest - middle.astype(F32)).astype(BF16)


def product(left, right, left_dim, right_dim):
    return lax.dot_general(
        left, right, (((left_dim,), (right_dim,)), ((), ())), preferred_element_type=F32
    )


def joined_product(left_parts, right_parts, left_dim=1, right_dim=0):
    left_high, left_low = left_parts
    right_high, right_low = right_parts
    return product(
        jnp.concatenate([left_high, left_high, left_low], left_dim),
        jnp.concatenate([right_high, right_low, right_high], right_dim),
        left_dim,
        right_dim,
    )


def precise_product(left, right, left_dim=1, right_dim=0):
    return joined_product(split_two(left), split_two(right), left_dim, right_dim)


def ones_product(ones, value):
    return product(jnp.concatenate([ones] * 3, 1), jnp.concatenate(split_three(value), 0), 1, 0)


def spread(per_head, lane):
    return jnp.concatenate(
        [
            jnp.where(lane < P_SIZE, per_head[:, 2 * k : 2 * k + 1], per_head[:, 2 * k + 1 : 2 * k + 2])
            for k in range(OWN_H // 2)
        ],
        1,
    )


def head_sums(value):
    column = lax.broadcasted_iota(jnp.int32, (OWN, N), 0)
    head = lax.broadcasted_iota(jnp.int32, (OWN, N), 1)
    members = ((column >= head * P_SIZE) & (column < (head + 1) * P_SIZE)).astype(F32).astype(BF16)
    high, low = split_two(value)
    return product(jnp.concatenate([high, low], 1), jnp.concatenate([members, members], 0), 1, 0)


def two_heads(pair, lane):
    zero = jnp.zeros_like(pair)
    return jnp.concatenate([jnp.where(lane < P_SIZE, pair, zero), jnp.where(lane < P_SIZE, zero, pair)], 0)


def chunk_facts(ends, chunk, dt_pre, par):
    column = lax.broadcasted_iota(jnp.int32, (CHUNK, 1), 0) + chunk * CHUNK
    row = lax.broadcasted_iota(jnp.int32, (1, CHUNK), 1) + chunk * CHUNK

    def segment(position):
        counted = jnp.zeros_like(position)
        for k in range(3):
            counted = counted + (position >= ends[k]).astype(jnp.int32)
        return jnp.where(position < 0, -1, counted)

    def one_segment(position):
        counted = jnp.int32(0)
        for k in range(3):
            counted = counted + (position >= ends[k]).astype(jnp.int32)
        return jnp.where(position < 0, -1, counted)

    here_column, here_row = segment(column), segment(row)
    prior = one_segment(chunk * CHUNK - 1)
    last = one_segment(chunk * CHUNK + CHUNK - 1)
    lane = lax.broadcasted_iota(jnp.int32, (CHUNK, N), 1)
    shifted = dt_pre + par[6:7, :N]
    soft = jnp.maximum(shifted, 0.0) + jnp.log1p(jnp.exp(-jnp.abs(shifted)))
    step = jnp.where(lane < OWN_H, soft, 0.0)
    decay = step * par[7:8, :N]
    tri_row = lax.broadcasted_iota(jnp.int32, (CHUNK, CHUNK), 0)
    tri_column = lax.broadcasted_iota(jnp.int32, (CHUNK, CHUNK), 1)
    lower = (tri_row >= tri_column).astype(F32).astype(BF16)
    upper = (tri_row <= tri_column).astype(F32).astype(BF16)
    total = ones_product(lower, decay)
    entering = (here_column == prior).astype(F32) * jnp.exp(total)
    end = total[CHUNK - 1 : CHUNK]
    leaving = (here_column == last).astype(F32) * jnp.exp(jnp.minimum(end - total, 0.0))
    passing = jnp.where(last == prior, 1.0, 0.0) * jnp.exp(end)
    return dict(
        column=column,
        segment=segment,
        here_column=here_column,
        here_row=here_row,
        lane=lane,
        shifted=shifted,
        step=step,
        decay=decay,
        total=total,
        entering=entering,
        leaving=leaving,
        passing=passing,
        tri_row=tri_row,
        tri_column=tri_column,
        upper=upper,
    )


def forward_kernel(part, ends, proj, par, *refs):
    if part:
        carry_in, refs = refs[3], refs[4:]
    pre_out, mixed_out, state_out, carry_out, extended, state = refs
    chunk = pl.program_id(0) + part * HALF

    @pl.when(pl.program_id(0) == 0)
    def _():
        if part:
            state[...] = carry_in[:N, :OWN]
            extended[0:8, :] = carry_in[N:, :]
        else:
            state[...] = jnp.zeros_like(state)
            extended[0:8, :] = jnp.zeros((8, 640), F32)

    facts = chunk_facts(ends, chunk, proj[:, 1024:1152], par)
    lane = facts["lane"]
    conv = proj[:, OWN:1024].astype(BF16).astype(F32)
    extended[8 : 8 + CHUNK, :] = conv
    pre = par[4:5] + par[3:4] * conv
    for back in range(1, CONV):
        same = (facts["segment"](facts["column"] - back) == facts["here_column"]).astype(F32)
        pre = pre + par[3 - back : 4 - back] * (extended[8 - back : 8 - back + CHUNK, :] * same)
    extended[0:8, :] = extended[CHUNK : CHUNK + 8, :]
    pre_out[...] = pre
    act = pre * jax.nn.sigmoid(pre)
    own_x, state_b, state_c = act[:, :OWN], act[:, OWN : OWN + N], act[:, OWN + N :]
    stepped = own_x * spread(facts["step"], lane)
    b_parts, c_parts = split_two(state_b), split_two(state_c)
    inside = (facts["tri_row"] >= facts["tri_column"]) & (facts["here_column"] == facts["here_row"])
    scores = jnp.where(inside, joined_product(c_parts, b_parts, 1, 1), 0.0)
    total_rows = facts["total"].T
    state_in = state[...]
    state_out[...] = state_in
    outs = []
    for pair in range(OWN_H // 2):
        mixing = []
        for head in (2 * pair, 2 * pair + 1):
            span = facts["total"][:, head : head + 1] - total_rows[head : head + 1, :]
            mixing.append(jnp.exp(jnp.minimum(span, 0.0)) * scores)
        inner = two_heads(stepped[:, pair * N : pair * N + N], lane)
        outs.append(precise_product(jnp.concatenate(mixing, 1), inner))
    scanned = jnp.concatenate(outs, 1) + spread(facts["entering"], lane) * joined_product(
        c_parts, split_two(state_in)
    )
    state[...] = spread(facts["passing"], lane[:1]) * state_in + precise_product(
        state_b.T, stepped * spread(facts["leaving"], lane)
    )
    mixed_out[...] = scanned + par[5:6, :OWN] * own_x

    @pl.when(pl.program_id(0) == HALF - 1)
    def _():
        carry_out[:N, :OWN] = state[...]
        carry_out[:N, OWN:] = jnp.zeros((N, 640 - OWN), F32)
        carry_out[N:, :] = extended[0:8, :]


def run_forward(part, ends, proj, par, before=()):
    here = lambda i: (i + part * HALF, 0)
    chunked = lambda width: pl.BlockSpec((CHUNK, width), here)
    fixed = lambda shape: pl.BlockSpec(shape, lambda i: (0, 0))
    carry = fixed((N + 8, 640))
    return pl.pallas_call(
        partial(forward_kernel, part),
        grid=(HALF,),
        in_specs=[pl.BlockSpec(memory_space=pltpu.SMEM), chunked(1152), fixed((16, 640))]
        + ([pl.BlockSpec(memory_space=pl.ANY)] * 3 + [carry] if part else []),
        out_specs=[chunked(640), chunked(OWN), pl.BlockSpec((N, OWN), here), carry],
        out_shape=[
            jax.ShapeDtypeStruct((PACK, 640), F32),
            jax.ShapeDtypeStruct((PACK, OWN), F32),
            jax.ShapeDtypeStruct((CHUNKS * N, OWN), F32),
            jax.ShapeDtypeStruct((N + 8, 640), F32),
        ],
        input_output_aliases={3: 0, 4: 1, 5: 2} if part else {},
        scratch_shapes=[pltpu.VMEM((CHUNK + 8, 640), F32), pltpu.VMEM((N, OWN), F32)],
        compiler_params=pltpu.CompilerParams(
            dimension_semantics=("arbitrary",), vmem_limit_bytes=VMEM_LIMIT
        ),
        cost_estimate=COST,
        name="scan_forward",
    )(ends, proj, par, *before)


def backward_kernel(ends, conv_in, dt_in, pre_in, mixed_in, grad_mixed, state_all, par, *refs):
    grad_x, grad_dt, grad_bc, sums, head_acc, carried, extended, end_dot = refs
    step_index = pl.program_id(0)
    chunk = CHUNKS - 1 - step_index

    @pl.when(step_index == 0)
    def _():
        carried[...] = jnp.zeros_like(carried)
        extended[CHUNK : CHUNK + 8, :] = jnp.zeros((8, OWN), F32)
        end_dot[...] = jnp.zeros_like(end_dot)
        sums[...] = jnp.zeros_like(sums)
        head_acc[...] = jnp.zeros_like(head_acc)

    facts = chunk_facts(ends, chunk, dt_in[...], par)
    lane = facts["lane"]
    pre = pre_in[...]
    sig = jax.nn.sigmoid(pre)
    act = pre * sig
    own_x, state_b, state_c = act[:, :OWN], act[:, OWN : OWN + N], act[:, OWN + N :]
    step = facts["step"]
    step_wide = spread(step, lane)
    stepped = own_x * step_wide
    skip = par[5:6, :OWN]
    scanned = mixed_in[...] - skip * own_x
    grad_m = grad_mixed[...]
    sums[6:7] += jnp.sum(grad_m * own_x, 0, keepdims=True)

    b_parts, c_parts = split_two(state_b), split_two(state_c)
    inside = (facts["tri_row"] <= facts["tri_column"]) & (facts["here_column"] == facts["here_row"])
    scores = jnp.where(inside, joined_product(b_parts, c_parts, 1, 1), 0.0)
    total_rows = facts["total"].T
    grad_scores = jnp.zeros((CHUNK, CHUNK), F32)
    grad_stepped = []
    for pair in range(OWN_H // 2):
        columns = slice(pair * N, pair * N + N)
        grad_pair = grad_m[:, columns]
        high, low = split_two(grad_pair)
        stepped_parts = split_two(two_heads(stepped[:, columns], lane))
        grad_mixing = joined_product(stepped_parts, (high, low), 1, 1)
        mixing = []
        for k in range(2):
            head = 2 * pair + k
            span = total_rows[head : head + 1, :] - facts["total"][:, head : head + 1]
            decays = jnp.exp(jnp.minimum(span, 0.0))
            mixing.append(decays * scores)
            grad_scores = grad_scores + decays * grad_mixing[k * CHUNK : (k + 1) * CHUNK]
        grad_stepped.append(
            joined_product(
                split_two(jnp.concatenate(mixing, 1)), (two_heads(high, lane), two_heads(low, lane))
            )
        )
    grad_scores = jnp.where(inside, grad_scores, 0.0)
    carry = carried[...]
    carry_parts = split_two(carry)
    leaving = spread(facts["leaving"], lane)
    grad_stepped = jnp.concatenate(grad_stepped, 1) + leaving * joined_product(b_parts, carry_parts)
    state_in = state_all[...]
    entered = spread(facts["entering"], lane) * grad_m
    entered_parts = split_two(entered)
    grad_b = precise_product(grad_scores, state_c) + joined_product(
        split_two(leaving * stepped), carry_parts, 1, 1
    )
    grad_c = precise_product(grad_scores.T, state_b) + joined_product(
        entered_parts, split_two(state_in), 1, 1
    )
    grad_bc[0:N, :] = grad_b.T.astype(BF16)
    grad_bc[N:, :] = grad_c.T.astype(BF16)
    new_carry = spread(facts["passing"], lane[:1]) * carry + joined_product(
        split_two(state_c.T), entered_parts
    )
    carried[...] = new_carry

    grad_step = head_sums(own_x * grad_stepped)
    last_row = lax.broadcasted_iota(jnp.int32, (CHUNK, N), 0) == CHUNK - 1
    grad_total = head_sums(grad_m * scanned) - step * grad_step
    grad_total = grad_total + jnp.where(last_row, end_dot[0:1, :], 0.0)
    grad_decay = ones_product(facts["upper"], grad_total)
    end_dot[...] = head_sums(
        jnp.broadcast_to(jnp.sum(new_carry * state_in, 0, keepdims=True), (8, OWN))
    )
    grad_pre_dt = (grad_step + grad_decay * par[7:8, :N]) * jax.nn.sigmoid(facts["shifted"])
    grad_pre_dt = jnp.where(lane < OWN_H, grad_pre_dt, 0.0)
    grad_dt[...] = grad_pre_dt.astype(BF16)
    head_acc[0:1] += jnp.sum(grad_pre_dt, 0, keepdims=True)
    head_acc[1:2] += jnp.sum(grad_decay * facts["decay"], 0, keepdims=True)

    sig_x, pre_x = sig[:, :OWN], pre[:, :OWN]
    grad_pre = (step_wide * grad_stepped + skip * grad_m) * (sig_x * (1.0 + pre_x * (1.0 - sig_x)))
    extended[0:CHUNK, :] = grad_pre
    conv = conv_in[...].astype(BF16).astype(F32)
    sums[5:6] += jnp.sum(grad_pre, 0, keepdims=True)
    sums[4:5] += jnp.sum(conv * grad_pre, 0, keepdims=True)
    grad_conv = par[3:4, :OWN] * grad_pre
    for ahead in range(1, CONV):
        same = (facts["segment"](facts["column"] + ahead) == facts["here_column"]).astype(F32)
        later = extended[ahead : ahead + CHUNK, :] * same
        sums[4 - ahead : 5 - ahead] += jnp.sum(conv * later, 0, keepdims=True)
        grad_conv = grad_conv + par[3 - ahead : 4 - ahead, :OWN] * later
    extended[CHUNK : CHUNK + 8, :] = extended[0:8, :]
    grad_x[...] = grad_conv.astype(BF16)


def run_backward(ends, proj, pre, mixed, grad_mixed, states, par):
    last = CHUNKS - 1
    chunked = lambda width, column=0: pl.BlockSpec((CHUNK, width), lambda i: (last - i, column))
    fixed = lambda shape: pl.BlockSpec(shape, lambda i: (0, 0))
    return pl.pallas_call(
        backward_kernel,
        grid=(CHUNKS,),
        in_specs=[
            pl.BlockSpec(memory_space=pltpu.SMEM),
            chunked(OWN, 1),
            chunked(N, 8),
            chunked(640),
            chunked(OWN),
            chunked(OWN),
            pl.BlockSpec((N, OWN), lambda i: (last - i, 0)),
            fixed((16, 640)),
        ],
        out_specs=[
            chunked(OWN),
            chunked(N),
            pl.BlockSpec((2 * N, CHUNK), lambda i: (0, last - i)),
            fixed((8, OWN)),
            fixed((8, N)),
        ],
        out_shape=[
            jax.ShapeDtypeStruct((PACK, OWN), BF16),
            jax.ShapeDtypeStruct((PACK, N), BF16),
            jax.ShapeDtypeStruct((2 * N, PACK), BF16),
            jax.ShapeDtypeStruct((8, OWN), F32),
            jax.ShapeDtypeStruct((8, N), F32),
        ],
        scratch_shapes=[
            pltpu.VMEM((N, OWN), F32),
            pltpu.VMEM((CHUNK + 8, OWN), F32),
            pltpu.VMEM((8, N), F32),
        ],
        compiler_params=pltpu.CompilerParams(
            dimension_semantics=("arbitrary",), vmem_limit_bytes=VMEM_LIMIT
        ),
        cost_estimate=COST,
        name="scan_backward",
    )(ends, proj, proj, pre, mixed, grad_mixed, states, par)


PARTS = (1, 1, 1, 1, 1, 2, 1, 1)
WHOLE = (1,) * N_REP


def load_block(step, groups, block):
    for slot, refs in enumerate(groups):

        @pl.when(step == slot)
        def _(refs=refs):
            if len(refs) == 1:
                block[...] = refs[0][...]
            else:
                block[: ROWS // 2, :] = refs[0][...]
                block[ROWS // 2 :, :] = refs[1][...]


def grouped(refs, parts):
    groups = []
    for count in parts:
        groups.append(refs[:count])
        refs = refs[count:]
    return groups, refs


def piece_specs(parts):
    return [pl.BlockSpec((ROWS // count, D), lambda i, table: (0, 0)) for count in parts for _ in range(count)]


def project_kernel(parts, table, *refs):
    groups, (gain, shards, *refs) = grouped(refs, parts)
    normed_out, proj, dt_out, block, weight = refs[-5:]

    @pl.when(pl.program_id(0) == 0)
    def _():
        for f in range(N_FSDP):
            weight[f * SHARD_IN : (f + 1) * SHARD_IN, :] = shards[(f // 2) % 4, f % 2, f // 8]
        dt_out[...] = weight[:, 1024:]

    load_block(pl.program_id(0), groups, block)
    values = block[...].astype(F32)
    scale = lax.rsqrt(jnp.mean(values * values, axis=1, keepdims=True) + NORM_EPS)
    normed = (values * scale * gain[...]).astype(BF16)
    normed_out[...] = normed
    proj[...] = matmul(normed, weight[...])


def run_project(table, pieces, gain, shards):
    fixed = lambda shape: pl.BlockSpec(shape, lambda i, table: (0,) * len(shape))
    placed = lambda width: pl.BlockSpec((ROWS, width), lambda i, table: (table[i], 0))
    return pl.pallas_call(
        partial(project_kernel, PARTS),
        grid_spec=pltpu.PrefetchScalarGridSpec(
            num_scalar_prefetch=1,
            grid=(N_REP,),
            in_specs=piece_specs(PARTS) + [fixed((1, D)), fixed(shards.shape)],
            out_specs=[placed(D), placed(3 * WIDE), fixed((D, N))],
            scratch_shapes=[pltpu.VMEM((ROWS, D), BF16), pltpu.VMEM((D, 3 * WIDE), BF16)],
        ),
        out_shape=[
            jax.ShapeDtypeStruct((PACK, D), BF16),
            jax.ShapeDtypeStruct((PACK, 3 * WIDE), F32),
            jax.ShapeDtypeStruct((D, N), BF16),
        ],
        compiler_params=pltpu.CompilerParams(
            dimension_semantics=("arbitrary",), vmem_limit_bytes=VMEM_LIMIT
        ),
        cost_estimate=COST,
        name="project",
    )(table, *pieces, gain, shards)


def row_sums(value):
    folded = value[:, :N] + value[:, N : 2 * N] + value[:, 2 * N :]
    return jnp.sum(folded.T, 0, keepdims=True)


def out_grad_kernel(table, *refs):
    groups, refs = grouped(refs, WHOLE)
    w_out, mixed, gate_in, gain, branch_out, grad_out, sums, block, turned = refs

    @pl.when(pl.program_id(0) == 0)
    def _():
        turned[...] = w_out[...].reshape(OWN, D).T

    load_block(pl.program_id(0), groups, block)
    branch = block[...]
    branch_out[...] = branch
    total = matmul(branch, turned[...])
    grad_out[...] = total
    gate = gate_in[...]
    gated = mixed[...] * (gate * jax.nn.sigmoid(gate))
    row = lax.broadcasted_iota(jnp.int32, (8, ROWS), 0)
    sums[...] = jnp.where(
        row == 0, row_sums(gated * gated), jnp.where(row == 1, row_sums(total * gain[...] * gated), 0.0)
    )


def run_out_grad(table, pieces, w_out, mixed, proj, gain):
    fixed = lambda shape: pl.BlockSpec(shape, lambda i, table: (0, 0))
    placed = lambda width: pl.BlockSpec((ROWS, width), lambda i, table: (table[i], 0))
    return pl.pallas_call(
        out_grad_kernel,
        grid_spec=pltpu.PrefetchScalarGridSpec(
            num_scalar_prefetch=1,
            grid=(N_REP,),
            in_specs=piece_specs(WHOLE)
            + [
                pl.BlockSpec(
                    (1, 2, 1, SHARD_OUT, D), lambda i, table: (table[N_REP] % 4, 0, table[N_REP] // 4, 0, 0)
                )
            ]
            + [placed(OWN), placed(OWN), fixed((1, OWN))],
            out_specs=[placed(D), placed(OWN), pl.BlockSpec((8, ROWS), lambda i, table: (0, table[i]))],
            scratch_shapes=[pltpu.VMEM((ROWS, D), BF16), pltpu.VMEM((D, WIDE), BF16)],
        ),
        out_shape=[
            jax.ShapeDtypeStruct((PACK, D), BF16),
            jax.ShapeDtypeStruct((PACK, OWN), F32),
            jax.ShapeDtypeStruct((8, PACK), F32),
        ],
        compiler_params=pltpu.CompilerParams(
            dimension_semantics=("arbitrary",), vmem_limit_bytes=VMEM_LIMIT
        ),
        cost_estimate=COST,
        name="out_grad",
    )(table, *pieces, w_out, mixed, proj, gain)


def gate_kernel(
    where, grad_out, mixed_in, gate_in, sums, gain, grad_branch, normed,
    low_out, grad_mixed, keep, give, grad_gain, total,
):
    step = pl.program_id(0)
    rows = grad_out.shape[0]
    mixed, gate, grad_o = mixed_in[...], gate_in[...], grad_out[...]
    stats = jnp.concatenate([sums[...], jnp.zeros((N - 8, rows), F32)], 0).T
    out_scale = lax.rsqrt(stats[:, 0:1] * (1.0 / DI) + NORM_EPS)
    pull = out_scale * out_scale * out_scale * (stats[:, 1:2] * (1.0 / DI))
    gate_sig = jax.nn.sigmoid(gate)
    silu = gate * gate_sig
    gated = mixed * silu
    unit = gated * out_scale
    low = (unit * gain[...]).astype(BF16)
    grad_gated = out_scale * (grad_o * gain[...]) - gated * pull
    grad_mixed[...] = grad_gated * silu
    grad_z = (grad_gated * mixed * (gate_sig * (1.0 + gate * (1.0 - gate_sig)))).astype(BF16)
    low_out[:, :OWN] = low
    low_out[:, OWN:] = grad_z

    @pl.when(step == 0)
    def _():
        grad_gain[...] = jnp.zeros_like(grad_gain)
        total[...] = jnp.zeros_like(total)

    grad_gain[0:1] += jnp.sum(grad_o * unit, 0, keepdims=True)
    for k in range(4):
        part = product(low, grad_branch[:, k * WIDE : (k + 1) * WIDE], 0, 0)
        for m in range(4):
            total[4 * k + m, :SHARD_IN] += part[m * SHARD_IN : (m + 1) * SHARD_IN]
    part = product(normed[...], grad_z, 0, 0)
    for f in range(N_FSDP):
        total[f, SHARD_IN:] += part[f * SHARD_IN : (f + 1) * SHARD_IN]

    @pl.when(step == pl.num_programs(0) - 1)
    def _():
        for k in range(N_FSDP // 2):
            keep[k] = total[2 * k + where[0]]
            give[k] = total[2 * k + 1 - where[0]]


def run_gate(where, grad_out, mixed, proj, sums, gain, grad_branch, normed):
    count = 2 * ROWS
    rows = lambda width: pl.BlockSpec((count, width), lambda i: (i, 0))
    fixed = lambda shape: pl.BlockSpec(shape, lambda i: (0,) * len(shape))
    half = (N_FSDP // 2, 2 * SHARD_IN, WIDE)
    return pl.pallas_call(
        gate_kernel,
        grid=(PACK // count,),
        in_specs=[
            pl.BlockSpec(memory_space=pltpu.SMEM),
            rows(OWN),
            rows(OWN),
            rows(OWN),
            pl.BlockSpec((8, count), lambda i: (0, i)),
            fixed((1, OWN)),
            rows(D),
            rows(D),
        ],
        out_specs=[rows(2 * OWN), rows(OWN), fixed(half), fixed(half), fixed((8, OWN))],
        out_shape=[
            jax.ShapeDtypeStruct((PACK, 2 * OWN), BF16),
            jax.ShapeDtypeStruct((PACK, OWN), F32),
            jax.ShapeDtypeStruct(half, F32),
            jax.ShapeDtypeStruct(half, F32),
            jax.ShapeDtypeStruct((8, OWN), F32),
        ],
        scratch_shapes=[pltpu.VMEM((N_FSDP, 2 * SHARD_IN, WIDE), F32)],
        compiler_params=pltpu.CompilerParams(
            dimension_semantics=("arbitrary",), vmem_limit_bytes=VMEM_LIMIT
        ),
        cost_estimate=COST,
        name="gate_backward",
    )(where, grad_out, mixed, proj, sums, gain, grad_branch, normed)


def block_out_kernel(rows, weight, tokens, live, out):
    step = pl.program_id(0)
    part = matmul(jnp.concatenate([rows[0], rows[1]], 1), weight[...].reshape(2 * OWN, D))

    @pl.when(step == 0)
    def _():
        out[...] = part

    @pl.when(step > 0)
    def _():
        out[...] += part

    @pl.when(step == N_REP // 2 - 1)
    def _():
        out[...] = tokens[...].astype(F32) + live[...] * out[...]


def run_block_out(rows, weight, tokens, live):
    fixed = lambda shape: pl.BlockSpec(shape, lambda i: (0, 0))
    return pl.pallas_call(
        block_out_kernel,
        grid=(N_REP // 2,),
        in_specs=[
            pl.BlockSpec((2, ROWS, OWN), lambda i: (i, 0, 0)),
            pl.BlockSpec((2, 2, 1, SHARD_OUT, D), lambda i: (i % 2, 0, i // 2, 0, 0)),
            fixed((ROWS, D)),
            fixed((ROWS, 1)),
        ],
        out_specs=fixed((ROWS, D)),
        out_shape=jax.ShapeDtypeStruct((ROWS, D), F32),
        compiler_params=pltpu.CompilerParams(
            dimension_semantics=("arbitrary",), vmem_limit_bytes=VMEM_LIMIT
        ),
        cost_estimate=FILL,
        name="block_out",
    )(rows, weight, tokens, live)


def turned_part(weight, rows):
    return product(weight[...].reshape(D, weight.shape[-1]), rows, 1, 1)


def columns_of(full_in, width, index):
    return pl.BlockSpec(full_in.shape[:-1] + (width,), lambda i: (0, 0, 0, 0, index(i)))


def z_grad_kernel(rows, weight, out):
    part = turned_part(weight, jnp.concatenate([rows[0], rows[1]], 1))

    @pl.when(pl.program_id(0) == 0)
    def _():
        out[...] = part

    @pl.when(pl.program_id(0) > 0)
    def _():
        out[...] += part


def run_z_grad(rows, full_in):
    return pl.pallas_call(
        z_grad_kernel,
        grid=(N_REP // 2,),
        in_specs=[
            pl.BlockSpec((2, ROWS, OWN), lambda i: (i, 0, 1)),
            columns_of(full_in, 2 * OWN, lambda i: i),
        ],
        out_specs=pl.BlockSpec((D, ROWS), lambda i: (0, 0)),
        out_shape=jax.ShapeDtypeStruct((D, ROWS), F32),
        compiler_params=pltpu.CompilerParams(
            dimension_semantics=("arbitrary",), vmem_limit_bytes=VMEM_LIMIT
        ),
        cost_estimate=FILL,
        name="z_grad",
    )(rows, full_in)


def input_grad_kernel(
    grad_z, x_rows, rest_rows, w_x, w_bc, low_dt, tokens, cotangent, gain, out, gain_out, total, ordered
):
    step = pl.program_id(0)
    part = turned_part(w_x, jnp.concatenate([x_rows[0], x_rows[1]], 1))

    @pl.when(step == 0)
    def _():
        total[...] = grad_z[...] + part

    @pl.when(step > 0)
    def _():
        total[...] += part

    @pl.when(step == N_REP // 2 - 1)
    def _():
        lane = lax.broadcasted_iota(jnp.int32, (ROWS, N), 1)
        groups = []
        for k in range(2):
            group = jnp.zeros((ROWS, N), F32)
            for m in range(4):
                value = rest_rows[4 * k + m].astype(F32)
                value = value if m == 0 else pltpu.roll(value, m * OWN_BC, 1)
                group = jnp.where((lane >= m * OWN_BC) & (lane < (m + 1) * OWN_BC), value, group)
            groups.append(group.astype(BF16))
        steps = jnp.zeros((ROWS, N), F32)
        for m in range(N_REP):
            start = 8 + m * OWN_H
            value = pltpu.roll(rest_rows[m].astype(F32), (start - OWN_BC) % N, 1)
            steps = jnp.where((lane >= start) & (lane < start + OWN_H), value, steps)
        shared = total[...] + turned_part(w_bc, jnp.concatenate(groups, 1))
        for f in range(N_FSDP):
            start = (((f // 2) % 4 * 2 + f % 2) * 2 + f // 8) * SHARD_IN
            ordered[f * SHARD_IN : (f + 1) * SHARD_IN, :] = shared[start : start + SHARD_IN, :]
        grad_h = (ordered[...] + product(low_dt[...], steps.astype(BF16), 1, 1)).T
        values = tokens[...].astype(F32)
        scale = lax.rsqrt(jnp.mean(values * values, axis=1, keepdims=True) + NORM_EPS)
        unit = values * scale
        gain_sum = jnp.sum(grad_h * unit, 0, keepdims=True)
        gain_out[...] = jnp.zeros_like(gain_out)
        for k in range(D // N):
            gain_out[k : k + 1, :] = gain_sum[:, k * N : (k + 1) * N]
        grad_unit = grad_h * gain[...]
        inner = jnp.mean(grad_unit * unit, axis=1, keepdims=True)
        out[...] = cotangent[...].astype(F32) + scale * (grad_unit - unit * inner)


def run_input_grad(grad_z, tail_rows, full_in, low_dt, tokens, cotangent, gain):
    fixed = lambda shape: pl.BlockSpec(shape, lambda i: (0,) * len(shape))
    return pl.pallas_call(
        input_grad_kernel,
        grid=(N_REP // 2,),
        in_specs=[
            fixed((D, ROWS)),
            pl.BlockSpec((2, ROWS, OWN), lambda i: (i, 0, 0)),
            pl.BlockSpec((N_REP, ROWS, N), lambda i: (0, 0, OWN // N)),
            columns_of(full_in, 2 * OWN, lambda i: N_REP // 2 + i),
            columns_of(full_in, 2 * N, lambda i: DI // N),
            fixed((D, N)),
            fixed((ROWS, D)),
            fixed((ROWS, D)),
            fixed((1, D)),
        ],
        out_specs=[fixed((ROWS, D)), fixed((16, N))],
        out_shape=[jax.ShapeDtypeStruct((ROWS, D), F32), jax.ShapeDtypeStruct((16, N), F32)],
        scratch_shapes=[pltpu.VMEM((D, ROWS), F32), pltpu.VMEM((D, ROWS), F32)],
        compiler_params=pltpu.CompilerParams(
            dimension_semantics=("arbitrary",), vmem_limit_bytes=VMEM_LIMIT
        ),
        cost_estimate=COST,
        name="input_grad",
    )(grad_z, tail_rows, tail_rows, full_in, full_in, low_dt, tokens, cotangent, gain)


def rest_kernel(
    ends, parts, pre_b, pre_c, conv_in, par, grad_x, grad_dt, sums, head_acc, grad_gain, first, tail_out, small_out
):
    own = lax.broadcasted_iota(jnp.int32, (OWN_BC, 2 * N), 0) + first[0]
    chosen = (lax.broadcasted_iota(jnp.int32, (OWN_BC, 2 * N), 1) == own).astype(F32).astype(BF16)

    def pick(value):
        return product(jnp.concatenate([chosen] * 3, 1), jnp.concatenate(split_three(value), 1), 1, 1)

    grad = parts[0].astype(F32)
    for k in range(1, N_REP):
        grad = grad + parts[k].astype(F32)
    own_pre = pick(jnp.concatenate([pre_b[...], pre_c[...]], 1))
    own_conv = product(chosen, conv_in[...].astype(BF16), 1, 1)
    taps = pick(par[:, OWN:])
    sig = jax.nn.sigmoid(own_pre)
    grad_pre = grad * (sig * (1.0 + own_pre * (1.0 - sig)))
    position = lax.broadcasted_iota(jnp.int32, (1, PACK), 1)

    def segment(places):
        counted = jnp.zeros_like(places)
        for k in range(3):
            counted = counted + (places >= ends[k]).astype(jnp.int32)
        return counted

    grad_conv = taps[:, CONV - 1 : CONV] * grad_pre
    column = lax.broadcasted_iota(jnp.int32, (OWN_BC, N), 1)
    found = jnp.where(column == CONV, jnp.sum(grad_pre, 1, keepdims=True), 0.0)
    found = jnp.where(column == CONV - 1, jnp.sum(own_conv * grad_pre, 1, keepdims=True), found)
    for later_by in range(1, CONV):
        same = (segment(position + later_by) == segment(position)) & (position < PACK - later_by)
        later = jnp.where(same, pltpu.roll(grad_pre, PACK - later_by, 1), 0.0)
        tap = CONV - 1 - later_by
        found = jnp.where(column == tap, jnp.sum(own_conv * later, 1, keepdims=True), found)
        grad_conv = grad_conv + taps[:, tap : tap + 1] * later
    lane = lax.broadcasted_iota(jnp.int32, (N, N), 1)
    filler = jnp.zeros((N - OWN_BC, N), F32)
    for k in range(PACK // N):
        rows = slice(k * N, (k + 1) * N)
        columns = jnp.concatenate([grad_conv[:, rows], filler], 0).T
        steps = pltpu.roll(grad_dt[rows, :].astype(F32), OWN_BC, 1)
        tail_out[rows, :OWN] = grad_x[rows, :]
        tail_out[rows, OWN:] = jnp.where(
            lane < OWN_BC, columns, jnp.where(lane < OWN_BC + OWN_H, steps, 0.0)
        ).astype(BF16)
    row = lax.broadcasted_iota(jnp.int32, (8, OWN), 0)
    skip = head_sums(sums[...])
    by_head = jnp.concatenate([skip, jnp.zeros((8, OWN - N), F32)], 1)
    logs = jnp.concatenate([head_acc[...], jnp.zeros((8, OWN - N), F32)], 1)
    wide = jnp.where(row == 0, grad_gain[0:1, :], jnp.where(row < 6, sums[...], 0.0))
    wide = jnp.where(row == 6, logs[1:2, :], jnp.where(row == 7, by_head[6:7, :], wide))
    turned = jnp.concatenate([found, filler], 0).T
    first_row = lax.broadcasted_iota(jnp.int32, (8, N), 0) == 0
    small_out[:, :OWN] = wide
    small_out[:, OWN:] = jnp.where(first_row, head_acc[0:1, :], pltpu.roll(turned[:8], 1, 0))


def run_rest(ends, parts, pre, proj, par, grad_x, grad_dt, sums, head_acc, grad_gain, first):
    fixed = lambda shape: pl.BlockSpec(shape, lambda i: (0,) * len(shape))
    return pl.pallas_call(
        rest_kernel,
        grid=(1,),
        in_specs=[
            pl.BlockSpec(memory_space=pltpu.SMEM),
            fixed((N_REP, OWN_BC, PACK)),
            pl.BlockSpec((PACK, N), lambda i: (0, 3)),
            pl.BlockSpec((PACK, N), lambda i: (0, 4)),
            pl.BlockSpec((PACK, 2 * N), lambda i: (0, 3)),
            fixed((16, 640)),
            fixed((PACK, OWN)),
            fixed((PACK, N)),
            fixed((8, OWN)),
            fixed((8, N)),
            fixed((8, OWN)),
            pl.BlockSpec(memory_space=pltpu.SMEM),
        ],
        out_specs=[fixed((PACK, TAIL)), fixed((8, TAIL))],
        out_shape=[jax.ShapeDtypeStruct((PACK, TAIL), BF16), jax.ShapeDtypeStruct((8, TAIL), F32)],
        compiler_params=pltpu.CompilerParams(
            dimension_semantics=("arbitrary",), vmem_limit_bytes=VMEM_LIMIT
        ),
        cost_estimate=COST,
        name="rest_backward",
    )(ends, parts, pre, pre, proj, par, grad_x, grad_dt, sums, head_acc, grad_gain, first)


def adam_step(grad, weight, first, second, grad_out, first_out, second_out, weight_out):
    new_weight, new_first, new_second = adam_update(
        weight[...], grad, first[...], second[...], RATE_MATRIX, WEIGHT_DECAY
    )
    grad_out[...] = grad
    first_out[...] = new_first
    second_out[...] = new_second
    weight_out[...] = new_weight


def load_pair(step, pairs, rows, grad):
    pair, right, far_first, far_second, left = pairs
    for slot, (low, high) in enumerate(
        (((pair, 0), (pair, 1)), ((right, 0), (right, 1)), ((far_first, 0), (far_second, 0)), ((left, 0), (left, 1)))
    ):

        @pl.when(step == slot)
        def _(low=low, high=high):
            grad[:, :WIDE] = low[0][low[1], rows, :]
            grad[:, WIDE:] = high[0][high[1], rows, :]


def adam_pairs_kernel(rows, table, *refs):
    pairs, arrays, grad = refs[:5], refs[5:8] + refs[-5:-1], refs[-1]
    load_pair(pl.program_id(0), pairs, rows, grad)
    adam_step(grad[...], *arrays)


def run_adam_pairs(table, place_of, rows, pairs, weight, first, second):
    part = pl.BlockSpec((SHARD_IN, 2 * WIDE), lambda i, table: place_of(table[i]))
    shape = jax.ShapeDtypeStruct(weight.shape, F32)
    return pl.pallas_call(
        partial(adam_pairs_kernel, rows),
        grid_spec=pltpu.PrefetchScalarGridSpec(
            num_scalar_prefetch=1,
            grid=(4,),
            in_specs=[pl.BlockSpec(pair.shape, lambda i, table: (0, 0, 0)) for pair in pairs]
            + [part] * 3,
            out_specs=[part] * 4,
            scratch_shapes=[pltpu.VMEM((SHARD_IN, 2 * WIDE), F32)],
        ),
        out_shape=[shape] * 4,
        compiler_params=pltpu.CompilerParams(
            dimension_semantics=("arbitrary",), vmem_limit_bytes=VMEM_LIMIT
        ),
        cost_estimate=FILL,
        name="adam",
    )(table, *pairs, weight, first, second)


def adam_tail_kernel(pair, rest, *refs):
    arrays, grad = refs[:3] + refs[-5:-1], refs[-1]
    step = pl.program_id(0)

    @pl.when(step < N_REP // 2)
    def _():
        grad[:, :WIDE] = pair[0, :SHARD_IN]
        grad[:, WIDE:] = pair[1, :SHARD_IN]

    @pl.when(step == N_REP // 2)
    def _():
        lane = lax.broadcasted_iota(jnp.int32, (SHARD_IN, N), 1)
        for k in range(2):
            group = jnp.zeros((SHARD_IN, N), F32)
            for m in range(4):
                value = rest[4 * k + m, :SHARD_IN]
                value = value if m == 0 else pltpu.roll(value, m * OWN_BC, 1)
                group = jnp.where((lane >= m * OWN_BC) & (lane < (m + 1) * OWN_BC), value, group)
            grad[:, k * N : (k + 1) * N] = group

    adam_step(grad[...], *arrays)


def run_adam_tail(parts, weight, first, second, before):
    half = N_REP // 2
    rows = parts.shape[1]
    column = pl.BlockSpec((SHARD_IN, 2 * WIDE), lambda i: (0, half + i))
    shape = jax.ShapeDtypeStruct(weight.shape, F32)
    return pl.pallas_call(
        adam_tail_kernel,
        grid=(half + 1,),
        in_specs=[
            pl.BlockSpec((2, rows, OWN), lambda i: (jnp.minimum(i, half - 1), 0, 0)),
            pl.BlockSpec((N_REP, rows, N), lambda i: (0, 0, OWN // N)),
        ]
        + [column] * 3
        + [pl.BlockSpec(memory_space=pl.ANY)] * 4,
        out_specs=[column] * 4,
        out_shape=[shape] * 4,
        input_output_aliases={5 + k: k for k in range(4)},
        scratch_shapes=[pltpu.VMEM((SHARD_IN, 2 * WIDE), F32)],
        compiler_params=pltpu.CompilerParams(
            dimension_semantics=("arbitrary",), vmem_limit_bytes=VMEM_LIMIT
        ),
        cost_estimate=COST,
        name="adam_tail",
    )(parts, parts, weight, first, second, *before)


def body(
    tokens,
    cotangent,
    lengths,
    w_in,
    w_dt,
    w_out,
    small,
    first_in,
    first_dt,
    first_out,
    first_small,
    second_in,
    second_dt,
    second_out,
    second_small,
):
    place = Place()
    r = place.r
    zero = jnp.int32(0)
    pack_lengths = lax.dynamic_slice_in_dim(lengths, place.f, 1, 0)[0]
    seg_ends = jnp.cumsum(pack_lengths)
    own_positions = r * ROWS + jnp.arange(ROWS, dtype=jnp.int32)
    own_live = (segment_at(own_positions, seg_ends) < 3).astype(F32)[:, None]
    slots = jnp.arange(N_REP, dtype=jnp.int32)
    ahead = ((place.x + slots // 2) % 4) * 2 + (place.yl + slots) % 2
    half = ROWS // 2

    in_low = w_in.astype(BF16)
    dt_low = w_dt.astype(BF16)
    out_low = w_out.astype(BF16)

    small_block = jnp.pad(small.astype(BF16), (0, 16 * N - SHARD_SMALL)).reshape(1, 16, N)
    small_all = exchange(jnp.broadcast_to(small_block, (N_FSDP, 16, N)), "fsdp")

    def own_columns(rep):
        return jnp.concatenate(
            [
                lax.dynamic_slice_in_dim(in_low, rep * OWN, OWN, 1),
                lax.dynamic_slice_in_dim(in_low, DI + rep * OWN, OWN, 1),
                in_low[:, 2 * DI :],
                lax.dynamic_slice_in_dim(dt_low, rep * OWN_H, OWN_H, 1),
                jnp.zeros((SHARD_IN, 2), BF16),
                dt_low,
                jnp.zeros((SHARD_IN, N - 8 - H), BF16),
            ],
            1,
        )

    other_columns = move(
        own_columns(2 * place.x + 1 - place.yl), lambda yh, z, c, x, yl: (yh + 1, z, c, x, yl + 1)
    )
    from_left = move(tokens, along_x(1))
    from_right = move(tokens, along_x(-1))
    partner = move(tokens, swap_y)

    from_left, from_right, partner, out_low, other_columns = lax.optimization_barrier(
        (from_left, from_right, partner, out_low, other_columns)
    )
    own_shards = gather_eight(both(own_columns(r), other_columns, place.yh))
    far = move(from_left, along_x(1))
    partner_left = move(from_left, swap_y)
    partner_right = move(partner, along_x(-1))
    out_pair = swap_shards(out_low, place)

    far, partner_left, partner_right, out_pair, small_all = lax.optimization_barrier(
        (far, partner_left, partner_right, out_pair, small_all)
    )
    partner_far_top = move(partner_left[:half], along_x(1))
    partner_far_low = move(partner_right[half:], along_x(-1))

    vector = small_all.reshape(N_FSDP, 16 * N)[:, :SHARD_SMALL].reshape(-1).astype(F32)
    offset = 0
    gain_in = vector[None, :D]
    offset = D
    gain_row = lax.dynamic_slice_in_dim(vector, offset + r * OWN, OWN, 0)[None, :]
    offset += DI
    taps = vector[offset : offset + (CONV + 1) * CHANNELS].reshape(CONV + 1, CHANNELS)
    offset += (CONV + 1) * CHANNELS
    per_head = vector[offset:].reshape(3, H)
    dt_bias, a_log, d_skip = lax.dynamic_slice_in_dim(per_head, r * OWN_H, OWN_H, 1)
    taps_bc = taps[:, DI:]
    conv_par = jnp.concatenate([lax.dynamic_slice_in_dim(taps, r * OWN, OWN, 1), taps_bc], 1)
    head_par = jnp.stack(
        [
            jnp.pad(jnp.broadcast_to(d_skip[:, None], (OWN_H, P_SIZE)).reshape(-1), (0, 2 * N)),
            jnp.pad(dt_bias, (0, 640 - OWN_H)),
            jnp.pad(-jnp.exp(a_log), (0, 640 - OWN_H)),
        ],
        0,
    )
    par = jnp.concatenate([conv_par, head_par, jnp.zeros((8, 640), F32)], 0)

    branch = (cotangent.astype(F32) * own_live).astype(BF16)
    branch, in_low, partner_far_top, partner_far_low, own_shards = lax.optimization_barrier(
        (branch, in_low, partner_far_top, partner_far_low, own_shards)
    )
    full_out = gather_eight(tie(out_pair, own_shards))
    in_other = move(in_low, lambda yh, z, c, x, yl: (yh + 1, z, c, x, yl + 1))
    b_left = move(branch, along_x(1))
    b_right = move(branch, along_x(-1))
    b_partner = move(branch, swap_y)
    token_pieces = [
        tokens, partner, from_right, partner_right, far,
        partner_far_top, partner_far_low, from_left, partner_left,
    ]
    normed, proj, low_dt = run_project(ahead, token_pieces, gain_in, own_shards)
    b_left, b_right, b_partner, proj, in_other, in_low = lax.optimization_barrier(
        (b_left, b_right, b_partner, proj, in_other, in_low)
    )
    full_in = gather_eight(both(in_low, in_other, place.yh))
    b_far = move(b_left, along_x(1))
    b_partner_left = move(b_left, swap_y)
    b_partner_right = move(b_partner, along_x(-1))
    before = run_forward(0, seg_ends, proj, par)
    b_partner_left, before = lax.optimization_barrier((b_partner_left, before))
    b_partner_far = move(b_partner_left, along_x(1))
    pre, mixed, states, _ = run_forward(1, seg_ends, proj, par, before)
    branch_pieces = [branch, b_partner, b_right, b_partner_right, b_far, b_partner_far, b_left, b_partner_left]
    rep_table = jnp.concatenate([ahead, r[None]])
    grad_branch, grad_normed_out, sums = run_out_grad(rep_table, branch_pieces, full_out, mixed, proj, gain_row)
    sums = sum_rep(sums[:2].reshape(32, 128)).reshape(2, PACK)
    sums = jnp.concatenate([sums, jnp.zeros((6, PACK), F32)], 0)

    low_rows, grad_mixed, keep, give, grad_gain = run_gate(
        place.c[None], grad_normed_out, mixed, proj, sums, gain_row, grad_branch, normed
    )

    low_rows = exchange(low_rows.reshape(N_REP, ROWS, 2 * OWN), "rep")
    got = move(give, swap_core)
    grad_x, grad_dtraw, grad_bc, grad_sums, grad_heads = run_backward(
        seg_ends, proj, pre, mixed, grad_mixed, states, par
    )
    low_rows, got, grad_bc, grad_x = lax.optimization_barrier((low_rows, got, grad_bc, grad_x))

    grad_bc = exchange(grad_bc, "rep").reshape(N_REP, OWN_BC, PACK)
    split = (2, 4, 2 * SHARD_IN, WIDE)
    early, early_found = start_ring(keep.reshape(split), got.reshape(split), None, place)
    grad_rows = run_z_grad(low_rows, full_in)
    block_out = run_block_out(low_rows, full_out, tokens, own_live)
    grad_bc, grad_rows, block_out, early_found = lax.optimization_barrier(
        (grad_bc, grad_rows, block_out, early_found)
    )

    early, _ = end_ring(early, early_found, None)
    early, early_half = start_half(early, None, place)
    tail, small_own = run_rest(
        seg_ends, grad_bc, pre, proj, par, grad_x, grad_dtraw, grad_sums, grad_heads, grad_gain, (r * OWN_BC)[None]
    )
    tail_rows = exchange(tail.reshape(N_REP, ROWS, TAIL), "rep")
    grad_tail = contract_rows(normed, tail).reshape(2, 4, 2, SHARD_IN, TAIL)
    tail_keep = at(grad_tail, place.c, 2)
    tail_got = move(with_rows(at(grad_tail, 1 - place.c, 2), small_own), swap_core)
    early, _ = end_half(early, early_half, None)
    out_part = move(
        early[:SHARD_IN],
        lambda yh, z, c, x, yl: (x // 2, (x % 2) * 2 + yl, z % 2, 2 * c + yh, z // 2),
    )
    early = jnp.concatenate([out_part, early[SHARD_IN:]], 0)
    early_other = move(early, swap_y)
    tail_rows, tail_got, early_other = lax.optimization_barrier((tail_rows, tail_got, early_other))

    small_sum = small_own + tail_got[-8:]
    tail_part, tail_found = start_ring(tail_keep, tail_got[:-8].reshape(tail_keep.shape), small_sum, place)
    early_pair = both(early, early_other, place.yl)
    early_left, early_right = move(early_pair, along_x(1)), move(early_pair, along_x(-1))
    input_grad, grad_gain_in = run_input_grad(
        grad_rows, tail_rows, full_in, low_dt, tokens, cotangent, gain_in
    )
    tail_found, early_left, early_right, input_grad, grad_gain_in = lax.optimization_barrier(
        (tail_found, early_left, early_right, input_grad, grad_gain_in)
    )

    tail_part, small_sum = end_ring(tail_part, tail_found, small_sum)
    tail_part, tail_half = start_half(tail_part, small_sum, place)
    early_far = move(early_left[:1], along_x(1)), move(early_right[1:], along_x(-1))
    tail_half, early_far, grad_gain_in = lax.optimization_barrier((tail_half, early_far, grad_gain_in))
    early_pairs = (early_pair, early_right, *early_far, early_left)

    tail_part, small_sum = end_half(tail_part, tail_half, small_sum)
    tail_parts = share_rep(jnp.concatenate([tail_part, small_sum], 0))
    grad_gain_in = sum_all(grad_gain_in)

    x_order = (place.x + jnp.arange(4, dtype=jnp.int32)) % 4
    grad_out, new_first_out, new_second_out, new_out = run_adam_pairs(
        x_order, lambda k: (k // 2, k % 2), slice(0, SHARD_IN), early_pairs, w_out, first_out, second_out
    )
    updated = run_adam_pairs(
        x_order, lambda k: (0, k), slice(SHARD_IN, 2 * SHARD_IN), early_pairs, w_in, first_in, second_in
    )
    grad_in, new_first_in, new_second_in, new_in = run_adam_tail(tail_parts, w_in, first_in, second_in, updated)

    def columns(parts):
        return parts.transpose(1, 0, 2).reshape(parts.shape[1], -1)

    grad_gain_in = grad_gain_in[: D // N].reshape(-1)
    small_parts = tail_parts[:, SHARD_IN:]
    small_x = small_parts[:, :, :OWN].transpose(1, 0, 2).reshape(8, DI)
    small_bc = small_parts[:, :, OWN:].transpose(1, 0, 2)

    def channels(row):
        return jnp.concatenate([small_x[row], small_bc[row, :, :OWN_BC].reshape(-1)])

    grad_small_all = jnp.concatenate(
        [grad_gain_in, small_x[0]]
        + [channels(row) for row in range(1, 6)]
        + [
            small_bc[0, :, :OWN_H].reshape(-1),
            small_parts[:, 6, :OWN_H].reshape(-1),
            small_parts[:, 7, :OWN_H].reshape(-1),
        ]
    )
    grad_small = lax.dynamic_slice_in_dim(grad_small_all, place.f * SHARD_SMALL, SHARD_SMALL, 0)
    grad_dt = columns(tail_parts[:, :SHARD_IN, OWN + OWN_BC : OWN + OWN_BC + OWN_H])
    new_dt, new_first_dt, new_second_dt = adam_update(
        w_dt, grad_dt, first_dt, second_dt, RATE_MATRIX, WEIGHT_DECAY
    )
    new_small, new_first_small, new_second_small = adam_update(
        small, grad_small, first_small, second_small, RATE_SMALL, 0.0
    )
    return (
        block_out,
        input_grad,
        grad_in,
        grad_dt,
        grad_out,
        grad_small,
        new_first_in,
        new_first_dt,
        new_first_out,
        new_first_small,
        new_second_in,
        new_second_dt,
        new_second_out,
        new_second_small,
        new_in,
        new_dt,
        new_out,
        new_small,
    )


def solution(mesh):
    rows = P(("fsdp", "rep"), None)
    matrix = P("fsdp", None)
    vector = P("fsdp")
    group = (matrix, matrix, matrix, vector)
    return jax.shard_map(
        body,
        mesh=mesh,
        in_specs=(rows, rows, P()) + group * 3,
        out_specs=(rows, rows) + group * 4,
        check_vma=False,
    )
```

```python
from functools import partial

import jax
import jax.numpy as jnp
from jax import lax
from jax.experimental import pallas as pl
from jax.experimental.pallas import tpu as pltpu
from jax.sharding import PartitionSpec as P

D = 1536
H = 48
P_SIZE = 64
N = 128
CONV = 4
STEP = 10
DI = 3072
CHANNELS = DI + 2 * N
SMALL = 21392
N_FSDP = 16
N_REP = 8
ROWS = 256
PACK = 2048
OWN = DI // N_REP
OWN_H = H // N_REP
OWN_BC = 2 * N // N_REP
SHARD_IN = D // N_FSDP
SHARD_OUT = DI // N_FSDP
SHARD_SMALL = SMALL // N_FSDP
WIDE = 384
CHUNK = 128
CHUNKS = PACK // CHUNK
HALF = CHUNKS // 2
TAIL = 512
VMEM_LIMIT = 60 * 1024 * 1024

NORM_EPS = 1e-05
BETA_ONE = 0.9
BETA_TWO = 0.999
ADAM_EPS = 1e-08
WEIGHT_DECAY = 0.1
RATE_MATRIX = 0.04
RATE_SMALL = 0.4
PRECISE = lax.Precision.HIGHEST
BF16 = jnp.bfloat16
F32 = jnp.float32
COST = pl.CostEstimate(flops=1_000_000, bytes_accessed=100_000, transcendentals=0)
FILL = pl.CostEstimate(flops=2_400_000_000, bytes_accessed=20_000_000, transcendentals=0)


def move(value, target):
    pairs = []
    for f in range(N_FSDP):
        for r in range(N_REP):
            yh, z, c, x, yl = target(f // 8, (f // 2) % 4, f % 2, r // 2, r % 2)
            pairs.append((f * N_REP + r, ((yh % 2) * 8 + (z % 4) * 2 + c % 2) * N_REP + (x % 4) * 2 + yl % 2))
    return lax.ppermute(value, ("fsdp", "rep"), pairs)


def along_x(steps):
    return lambda yh, z, c, x, yl: (yh, z, c, x + steps, yl)


def along_z(steps):
    return lambda yh, z, c, x, yl: (yh, z + steps, c, x, yl)


def swap_y(yh, z, c, x, yl):
    return (yh, z, c, x, yl + 1)


def swap_y_hi(yh, z, c, x, yl):
    return (yh + 1, z, c, x, yl)


def swap_core(yh, z, c, x, yl):
    return (yh, z, c + 1, x, yl)


class Place:
    def __init__(self):
        f = lax.axis_index("fsdp")
        r = lax.axis_index("rep")
        self.f, self.r = f, r
        self.yh, self.z, self.c = f // 8, (f // 2) % 4, f % 2
        self.x, self.yl = r // 2, r % 2


def at(value, index, axis=0):
    return lax.dynamic_index_in_dim(value, index, axis, keepdims=False)


def tie(values, *others):
    return lax.optimization_barrier((values, others))[0]


def both(mine, other, second):
    first = jnp.where(second == 0, mine, other)
    last = jnp.where(second == 0, other, mine)
    return jnp.stack([first, last], 0)


def put(out, piece, axis, index):
    starts = [jnp.int32(0)] * out.ndim
    starts[axis] = jnp.int32(index)
    return lax.dynamic_update_slice(out, jnp.expand_dims(piece, axis), tuple(starts))


def swap_shards(value, place):
    other = move(value, lambda yh, z, c, x, yl: (yh + 1, z, c, x, yl + 1))
    return both(value, other, place.yh)


def gather_eight(pair):
    groups = [list(range(8)), list(range(8, 16))]
    out = lax.all_gather(pair, "fsdp", axis=0, tiled=True, axis_index_groups=groups)
    return out.reshape((4, 2) + pair.shape)


def start_ring(keep, got, extra, place):
    own = at(keep, place.z, 1) + at(got, place.z, 1)
    found = []
    for step in (1, 3, 2):
        there = (place.z + step) % 4
        found.append(move(with_rows(at(keep, there, 1) + at(got, there, 1), extra), along_z(step)))
    return own, found


def end_ring(own, found, extra):
    rows = own.shape[0] * own.shape[1]
    total = own
    for part in found:
        total = total + part[:rows].reshape(own.shape)
        extra = None if extra is None else extra + part[rows:]
    return total, extra


def start_half(total, extra, place):
    return at(total, place.yh), move(with_rows(at(total, 1 - place.yh), extra), swap_y_hi)


def end_half(mine, other, extra):
    rows = mine.shape[0]
    return mine + other[:rows], None if extra is None else extra + other[rows:]


def exchange(value, axis):
    return lax.all_to_all(value, axis, 0, 0, tiled=True)


def share_rep(value):
    return exchange(jnp.broadcast_to(value[None], (N_REP,) + value.shape), "rep")


def sum_rep(value):
    value = value + move(value, swap_y)
    steps = [move(value, along_x(step)) for step in (1, 3, 2)]
    return value + steps[0] + steps[1] + steps[2]


def sum_all(value):
    value = sum_rep(value)
    value = value + move(value, swap_core)
    steps = [move(value, along_z(step)) for step in (1, 3, 2)]
    value = value + steps[0] + steps[1] + steps[2]
    return value + move(value, swap_y_hi)


def scatter_eight(value):
    groups = [list(range(8)), list(range(8, 16))]
    flat = value.reshape(-1, value.shape[-1])
    out = lax.psum_scatter(flat, "fsdp", scatter_dimension=0, tiled=True, axis_index_groups=groups)
    return out.reshape((2,) + value.shape[1:])


def eight_order(f):
    return ((f // 2) % 4 * 2 + f % 2) * 2 + f // 8


def with_rows(block, extra):
    width = block.shape[-1]
    flat = block.reshape(-1, width)
    return flat if extra is None else jnp.concatenate([flat, extra], 0)


def adam_update(weight, gradient, moment_one, moment_two, learn_rate, decay_rate):
    moment_one = BETA_ONE * moment_one + (1.0 - BETA_ONE) * gradient
    moment_two = BETA_TWO * moment_two + (1.0 - BETA_TWO) * gradient * gradient
    scaled = (
        moment_one
        / (1.0 - BETA_ONE**STEP)
        / (jnp.sqrt(moment_two / (1.0 - BETA_TWO**STEP)) + ADAM_EPS)
    )
    return (weight - learn_rate * (scaled + decay_rate * weight), moment_one, moment_two)


def contract_rows(left_side, right_side):
    return lax.dot_general(
        left_side, right_side, (((0,), (0,)), ((), ())), preferred_element_type=F32
    )


def contract_cols(left_side, right_side):
    return lax.dot_general(
        left_side, right_side, (((1,), (1,)), ((), ())), preferred_element_type=F32
    )


def matmul(left_side, right_side):
    return jnp.dot(left_side, right_side, preferred_element_type=F32)


def segment_at(positions, seg_ends):
    counted = jnp.sum((positions[:, None] >= seg_ends[None, :]).astype(jnp.int32), axis=1)
    return jnp.where(positions < 0, jnp.int32(-1), counted)


def split_two(value):
    high = value.astype(BF16)
    return high, (value - high.astype(F32)).astype(BF16)


def split_three(value):
    high = value.astype(BF16)
    rest = value - high.astype(F32)
    middle = rest.astype(BF16)
    return high, middle, (rest - middle.astype(F32)).astype(BF16)


def product(left, right, left_dim, right_dim):
    return lax.dot_general(
        left, right, (((left_dim,), (right_dim,)), ((), ())), preferred_element_type=F32
    )


def joined_product(left_parts, right_parts, left_dim=1, right_dim=0):
    left_high, left_low = left_parts
    right_high, right_low = right_parts
    return product(
        jnp.concatenate([left_high, left_high, left_low], left_dim),
        jnp.concatenate([right_high, right_low, right_high], right_dim),
        left_dim,
        right_dim,
    )


def precise_product(left, right, left_dim=1, right_dim=0):
    return joined_product(split_two(left), split_two(right), left_dim, right_dim)


def ones_product(ones, value):
    return product(jnp.concatenate([ones] * 3, 1), jnp.concatenate(split_three(value), 0), 1, 0)


def spread(per_head, lane):
    return jnp.concatenate(
        [
            jnp.where(lane < P_SIZE, per_head[:, 2 * k : 2 * k + 1], per_head[:, 2 * k + 1 : 2 * k + 2])
            for k in range(OWN_H // 2)
        ],
        1,
    )


def head_sums(value):
    column = lax.broadcasted_iota(jnp.int32, (OWN, N), 0)
    head = lax.broadcasted_iota(jnp.int32, (OWN, N), 1)
    members = ((column >= head * P_SIZE) & (column < (head + 1) * P_SIZE)).astype(F32).astype(BF16)
    high, low = split_two(value)
    return product(jnp.concatenate([high, low], 1), jnp.concatenate([members, members], 0), 1, 0)


def two_heads(pair, lane):
    zero = jnp.zeros_like(pair)
    return jnp.concatenate([jnp.where(lane < P_SIZE, pair, zero), jnp.where(lane < P_SIZE, zero, pair)], 0)


def chunk_facts(ends, chunk, dt_pre, par):
    column = lax.broadcasted_iota(jnp.int32, (CHUNK, 1), 0) + chunk * CHUNK
    row = lax.broadcasted_iota(jnp.int32, (1, CHUNK), 1) + chunk * CHUNK

    def segment(position):
        counted = jnp.zeros_like(position)
        for k in range(3):
            counted = counted + (position >= ends[k]).astype(jnp.int32)
        return jnp.where(position < 0, -1, counted)

    def one_segment(position):
        counted = jnp.int32(0)
        for k in range(3):
            counted = counted + (position >= ends[k]).astype(jnp.int32)
        return jnp.where(position < 0, -1, counted)

    here_column, here_row = segment(column), segment(row)
    prior = one_segment(chunk * CHUNK - 1)
    last = one_segment(chunk * CHUNK + CHUNK - 1)
    lane = lax.broadcasted_iota(jnp.int32, (CHUNK, N), 1)
    shifted = dt_pre + par[6:7, :N]
    soft = jnp.maximum(shifted, 0.0) + jnp.log1p(jnp.exp(-jnp.abs(shifted)))
    step = jnp.where(lane < OWN_H, soft, 0.0)
    decay = step * par[7:8, :N]
    tri_row = lax.broadcasted_iota(jnp.int32, (CHUNK, CHUNK), 0)
    tri_column = lax.broadcasted_iota(jnp.int32, (CHUNK, CHUNK), 1)
    lower = (tri_row >= tri_column).astype(F32).astype(BF16)
    upper = (tri_row <= tri_column).astype(F32).astype(BF16)
    total = ones_product(lower, decay)
    entering = (here_column == prior).astype(F32) * jnp.exp(total)
    end = total[CHUNK - 1 : CHUNK]
    leaving = (here_column == last).astype(F32) * jnp.exp(jnp.minimum(end - total, 0.0))
    passing = jnp.where(last == prior, 1.0, 0.0) * jnp.exp(end)
    return dict(
        column=column,
        segment=segment,
        here_column=here_column,
        here_row=here_row,
        lane=lane,
        shifted=shifted,
        step=step,
        decay=decay,
        total=total,
        entering=entering,
        leaving=leaving,
        passing=passing,
        tri_row=tri_row,
        tri_column=tri_column,
        upper=upper,
    )


def forward_kernel(part, ends, proj, par, *refs):
    if part:
        carry_in, refs = refs[3], refs[4:]
    pre_out, mixed_out, state_out, carry_out, extended, state = refs
    chunk = pl.program_id(0) + part * HALF

    @pl.when(pl.program_id(0) == 0)
    def _():
        if part:
            state[...] = carry_in[:N, :OWN]
            extended[0:8, :] = carry_in[N:, :]
        else:
            state[...] = jnp.zeros_like(state)
            extended[0:8, :] = jnp.zeros((8, 640), F32)

    facts = chunk_facts(ends, chunk, proj[:, 1024:1152], par)
    lane = facts["lane"]
    conv = proj[:, OWN:1024].astype(BF16).astype(F32)
    extended[8 : 8 + CHUNK, :] = conv
    pre = par[4:5] + par[3:4] * conv
    for back in range(1, CONV):
        same = (facts["segment"](facts["column"] - back) == facts["here_column"]).astype(F32)
        pre = pre + par[3 - back : 4 - back] * (extended[8 - back : 8 - back + CHUNK, :] * same)
    extended[0:8, :] = extended[CHUNK : CHUNK + 8, :]
    pre_out[...] = pre
    act = pre * jax.nn.sigmoid(pre)
    own_x, state_b, state_c = act[:, :OWN], act[:, OWN : OWN + N], act[:, OWN + N :]
    stepped = own_x * spread(facts["step"], lane)
    b_parts, c_parts = split_two(state_b), split_two(state_c)
    inside = (facts["tri_row"] >= facts["tri_column"]) & (facts["here_column"] == facts["here_row"])
    scores = jnp.where(inside, joined_product(c_parts, b_parts, 1, 1), 0.0)
    total_rows = facts["total"].T
    state_in = state[...]
    state_out[...] = state_in
    outs = []
    for pair in range(OWN_H // 2):
        mixing = []
        for head in (2 * pair, 2 * pair + 1):
            span = facts["total"][:, head : head + 1] - total_rows[head : head + 1, :]
            mixing.append(jnp.exp(jnp.minimum(span, 0.0)) * scores)
        inner = two_heads(stepped[:, pair * N : pair * N + N], lane)
        outs.append(precise_product(jnp.concatenate(mixing, 1), inner))
    scanned = jnp.concatenate(outs, 1) + spread(facts["entering"], lane) * joined_product(
        c_parts, split_two(state_in)
    )
    state[...] = spread(facts["passing"], lane[:1]) * state_in + precise_product(
        state_b.T, stepped * spread(facts["leaving"], lane)
    )
    mixed_out[...] = scanned + par[5:6, :OWN] * own_x

    @pl.when(pl.program_id(0) == HALF - 1)
    def _():
        carry_out[:N, :OWN] = state[...]
        carry_out[:N, OWN:] = jnp.zeros((N, 640 - OWN), F32)
        carry_out[N:, :] = extended[0:8, :]


def run_forward(part, ends, proj, par, before=()):
    here = lambda i: (i + part * HALF, 0)
    chunked = lambda width: pl.BlockSpec((CHUNK, width), here)
    fixed = lambda shape: pl.BlockSpec(shape, lambda i: (0, 0))
    carry = fixed((N + 8, 640))
    return pl.pallas_call(
        partial(forward_kernel, part),
        grid=(HALF,),
        in_specs=[pl.BlockSpec(memory_space=pltpu.SMEM), chunked(1152), fixed((16, 640))]
        + ([pl.BlockSpec(memory_space=pl.ANY)] * 3 + [carry] if part else []),
        out_specs=[chunked(640), chunked(OWN), pl.BlockSpec((N, OWN), here), carry],
        out_shape=[
            jax.ShapeDtypeStruct((PACK, 640), F32),
            jax.ShapeDtypeStruct((PACK, OWN), F32),
            jax.ShapeDtypeStruct((CHUNKS * N, OWN), F32),
            jax.ShapeDtypeStruct((N + 8, 640), F32),
        ],
        input_output_aliases={3: 0, 4: 1, 5: 2} if part else {},
        scratch_shapes=[pltpu.VMEM((CHUNK + 8, 640), F32), pltpu.VMEM((N, OWN), F32)],
        compiler_params=pltpu.CompilerParams(
            dimension_semantics=("arbitrary",), vmem_limit_bytes=VMEM_LIMIT
        ),
        cost_estimate=COST,
        name="scan_forward",
    )(ends, proj, par, *before)


def backward_kernel(ends, conv_in, dt_in, pre_in, mixed_in, grad_mixed, state_all, par, *refs):
    grad_x, grad_dt, grad_bc, sums, head_acc, carried, extended, end_dot = refs
    step_index = pl.program_id(0)
    chunk = CHUNKS - 1 - step_index

    @pl.when(step_index == 0)
    def _():
        carried[...] = jnp.zeros_like(carried)
        extended[CHUNK : CHUNK + 8, :] = jnp.zeros((8, OWN), F32)
        end_dot[...] = jnp.zeros_like(end_dot)
        sums[...] = jnp.zeros_like(sums)
        head_acc[...] = jnp.zeros_like(head_acc)

    facts = chunk_facts(ends, chunk, dt_in[...], par)
    lane = facts["lane"]
    pre = pre_in[...]
    sig = jax.nn.sigmoid(pre)
    act = pre * sig
    own_x, state_b, state_c = act[:, :OWN], act[:, OWN : OWN + N], act[:, OWN + N :]
    step = facts["step"]
    step_wide = spread(step, lane)
    stepped = own_x * step_wide
    skip = par[5:6, :OWN]
    scanned = mixed_in[...] - skip * own_x
    grad_m = grad_mixed[...]
    sums[6:7] += jnp.sum(grad_m * own_x, 0, keepdims=True)

    b_parts, c_parts = split_two(state_b), split_two(state_c)
    inside = (facts["tri_row"] <= facts["tri_column"]) & (facts["here_column"] == facts["here_row"])
    scores = jnp.where(inside, joined_product(b_parts, c_parts, 1, 1), 0.0)
    total_rows = facts["total"].T
    grad_scores = jnp.zeros((CHUNK, CHUNK), F32)
    grad_stepped = []
    for pair in range(OWN_H // 2):
        columns = slice(pair * N, pair * N + N)
        grad_pair = grad_m[:, columns]
        high, low = split_two(grad_pair)
        stepped_parts = split_two(two_heads(stepped[:, columns], lane))
        grad_mixing = joined_product(stepped_parts, (high, low), 1, 1)
        mixing = []
        for k in range(2):
            head = 2 * pair + k
            span = total_rows[head : head + 1, :] - facts["total"][:, head : head + 1]
            decays = jnp.exp(jnp.minimum(span, 0.0))
            mixing.append(decays * scores)
            grad_scores = grad_scores + decays * grad_mixing[k * CHUNK : (k + 1) * CHUNK]
        grad_stepped.append(
            joined_product(
                split_two(jnp.concatenate(mixing, 1)), (two_heads(high, lane), two_heads(low, lane))
            )
        )
    grad_scores = jnp.where(inside, grad_scores, 0.0)
    carry = carried[...]
    carry_parts = split_two(carry)
    leaving = spread(facts["leaving"], lane)
    grad_stepped = jnp.concatenate(grad_stepped, 1) + leaving * joined_product(b_parts, carry_parts)
    state_in = state_all[...]
    entered = spread(facts["entering"], lane) * grad_m
    entered_parts = split_two(entered)
    grad_b = precise_product(grad_scores, state_c) + joined_product(
        split_two(leaving * stepped), carry_parts, 1, 1
    )
    grad_c = precise_product(grad_scores.T, state_b) + joined_product(
        entered_parts, split_two(state_in), 1, 1
    )
    grad_bc[0:N, :] = grad_b.T.astype(BF16)
    grad_bc[N:, :] = grad_c.T.astype(BF16)
    new_carry = spread(facts["passing"], lane[:1]) * carry + joined_product(
        split_two(state_c.T), entered_parts
    )
    carried[...] = new_carry

    grad_step = head_sums(own_x * grad_stepped)
    last_row = lax.broadcasted_iota(jnp.int32, (CHUNK, N), 0) == CHUNK - 1
    grad_total = head_sums(grad_m * scanned) - step * grad_step
    grad_total = grad_total + jnp.where(last_row, end_dot[0:1, :], 0.0)
    grad_decay = ones_product(facts["upper"], grad_total)
    end_dot[...] = head_sums(
        jnp.broadcast_to(jnp.sum(new_carry * state_in, 0, keepdims=True), (8, OWN))
    )
    grad_pre_dt = (grad_step + grad_decay * par[7:8, :N]) * jax.nn.sigmoid(facts["shifted"])
    grad_pre_dt = jnp.where(lane < OWN_H, grad_pre_dt, 0.0)
    grad_dt[...] = grad_pre_dt.astype(BF16)
    head_acc[0:1] += jnp.sum(grad_pre_dt, 0, keepdims=True)
    head_acc[1:2] += jnp.sum(grad_decay * facts["decay"], 0, keepdims=True)

    sig_x, pre_x = sig[:, :OWN], pre[:, :OWN]
    grad_pre = (step_wide * grad_stepped + skip * grad_m) * (sig_x * (1.0 + pre_x * (1.0 - sig_x)))
    extended[0:CHUNK, :] = grad_pre
    conv = conv_in[...].astype(BF16).astype(F32)
    sums[5:6] += jnp.sum(grad_pre, 0, keepdims=True)
    sums[4:5] += jnp.sum(conv * grad_pre, 0, keepdims=True)
    grad_conv = par[3:4, :OWN] * grad_pre
    for ahead in range(1, CONV):
        same = (facts["segment"](facts["column"] + ahead) == facts["here_column"]).astype(F32)
        later = extended[ahead : ahead + CHUNK, :] * same
        sums[4 - ahead : 5 - ahead] += jnp.sum(conv * later, 0, keepdims=True)
        grad_conv = grad_conv + par[3 - ahead : 4 - ahead, :OWN] * later
    extended[CHUNK : CHUNK + 8, :] = extended[0:8, :]
    grad_x[...] = grad_conv.astype(BF16)


def run_backward(ends, proj, pre, mixed, grad_mixed, states, par):
    last = CHUNKS - 1
    chunked = lambda width, column=0: pl.BlockSpec((CHUNK, width), lambda i: (last - i, column))
    fixed = lambda shape: pl.BlockSpec(shape, lambda i: (0, 0))
    return pl.pallas_call(
        backward_kernel,
        grid=(CHUNKS,),
        in_specs=[
            pl.BlockSpec(memory_space=pltpu.SMEM),
            chunked(OWN, 1),
            chunked(N, 8),
            chunked(640),
            chunked(OWN),
            chunked(OWN),
            pl.BlockSpec((N, OWN), lambda i: (last - i, 0)),
            fixed((16, 640)),
        ],
        out_specs=[
            chunked(OWN),
            chunked(N),
            pl.BlockSpec((2 * N, CHUNK), lambda i: (0, last - i)),
            fixed((8, OWN)),
            fixed((8, N)),
        ],
        out_shape=[
            jax.ShapeDtypeStruct((PACK, OWN), BF16),
            jax.ShapeDtypeStruct((PACK, N), BF16),
            jax.ShapeDtypeStruct((2 * N, PACK), BF16),
            jax.ShapeDtypeStruct((8, OWN), F32),
            jax.ShapeDtypeStruct((8, N), F32),
        ],
        scratch_shapes=[
            pltpu.VMEM((N, OWN), F32),
            pltpu.VMEM((CHUNK + 8, OWN), F32),
            pltpu.VMEM((8, N), F32),
        ],
        compiler_params=pltpu.CompilerParams(
            dimension_semantics=("arbitrary",), vmem_limit_bytes=VMEM_LIMIT
        ),
        cost_estimate=COST,
        name="scan_backward",
    )(ends, proj, proj, pre, mixed, grad_mixed, states, par)


PARTS = (1, 1, 1, 1, 1, 2, 1, 1)
WHOLE = (1,) * N_REP


def load_block(step, groups, block):
    for slot, refs in enumerate(groups):

        @pl.when(step == slot)
        def _(refs=refs):
            if len(refs) == 1:
                block[...] = refs[0][...]
            else:
                block[: ROWS // 2, :] = refs[0][...]
                block[ROWS // 2 :, :] = refs[1][...]


def grouped(refs, parts):
    groups = []
    for count in parts:
        groups.append(refs[:count])
        refs = refs[count:]
    return groups, refs


def piece_specs(parts):
    return [pl.BlockSpec((ROWS // count, D), lambda i, table: (0, 0)) for count in parts for _ in range(count)]


def project_kernel(parts, table, *refs):
    groups, (gain, shards, *refs) = grouped(refs, parts)
    normed_out, proj, dt_out, block, weight = refs[-5:]

    @pl.when(pl.program_id(0) == 0)
    def _():
        for f in range(N_FSDP):
            weight[f * SHARD_IN : (f + 1) * SHARD_IN, :] = shards[(f // 2) % 4, f % 2, f // 8, :SHARD_IN]
        dt_out[...] = weight[:, 1024:]

    load_block(pl.program_id(0), groups, block)
    values = block[...].astype(F32)
    scale = lax.rsqrt(jnp.mean(values * values, axis=1, keepdims=True) + NORM_EPS)
    normed = (values * scale * gain[...]).astype(BF16)
    normed_out[...] = normed
    proj[...] = matmul(normed, weight[...])


def run_project(table, pieces, gain, shards):
    fixed = lambda shape: pl.BlockSpec(shape, lambda i, table: (0,) * len(shape))
    placed = lambda width: pl.BlockSpec((ROWS, width), lambda i, table: (table[i], 0))
    return pl.pallas_call(
        partial(project_kernel, PARTS),
        grid_spec=pltpu.PrefetchScalarGridSpec(
            num_scalar_prefetch=1,
            grid=(N_REP,),
            in_specs=piece_specs(PARTS) + [fixed((1, D)), fixed(shards.shape)],
            out_specs=[placed(D), placed(3 * WIDE), fixed((D, N))],
            scratch_shapes=[pltpu.VMEM((ROWS, D), BF16), pltpu.VMEM((D, 3 * WIDE), BF16)],
        ),
        out_shape=[
            jax.ShapeDtypeStruct((PACK, D), BF16),
            jax.ShapeDtypeStruct((PACK, 3 * WIDE), F32),
            jax.ShapeDtypeStruct((D, N), BF16),
        ],
        compiler_params=pltpu.CompilerParams(
            dimension_semantics=("arbitrary",), vmem_limit_bytes=VMEM_LIMIT
        ),
        cost_estimate=COST,
        name="project",
    )(table, *pieces, gain, shards)


def row_sums(value):
    folded = value[:, :N] + value[:, N : 2 * N] + value[:, 2 * N :]
    return jnp.sum(folded.T, 0, keepdims=True)


def out_grad_kernel(table, *refs):
    groups, refs = grouped(refs, WHOLE)
    w_out, mixed, gate_in, gain, branch_out, grad_out, sums, block, turned = refs

    @pl.when(pl.program_id(0) == 0)
    def _():
        turned[...] = w_out[...].reshape(OWN, D).T

    load_block(pl.program_id(0), groups, block)
    branch = block[...]
    branch_out[...] = branch
    total = matmul(branch, turned[...])
    grad_out[...] = total
    gate = gate_in[...]
    gated = mixed[...] * (gate * jax.nn.sigmoid(gate))
    row = lax.broadcasted_iota(jnp.int32, (8, ROWS), 0)
    sums[...] = jnp.where(
        row == 0, row_sums(gated * gated), jnp.where(row == 1, row_sums(total * gain[...] * gated), 0.0)
    )


def run_out_grad(table, pieces, w_out, mixed, proj, gain):
    fixed = lambda shape: pl.BlockSpec(shape, lambda i, table: (0, 0))
    placed = lambda width: pl.BlockSpec((ROWS, width), lambda i, table: (table[i], 0))
    return pl.pallas_call(
        out_grad_kernel,
        grid_spec=pltpu.PrefetchScalarGridSpec(
            num_scalar_prefetch=1,
            grid=(N_REP,),
            in_specs=piece_specs(WHOLE)
            + [
                pl.BlockSpec(
                    (1, 2, 1, SHARD_OUT, D), lambda i, table: (table[N_REP] % 4, 0, table[N_REP] // 4, 0, 0)
                )
            ]
            + [placed(OWN), placed(OWN), fixed((1, OWN))],
            out_specs=[placed(D), placed(OWN), pl.BlockSpec((8, ROWS), lambda i, table: (0, table[i]))],
            scratch_shapes=[pltpu.VMEM((ROWS, D), BF16), pltpu.VMEM((D, WIDE), BF16)],
        ),
        out_shape=[
            jax.ShapeDtypeStruct((PACK, D), BF16),
            jax.ShapeDtypeStruct((PACK, OWN), F32),
            jax.ShapeDtypeStruct((8, PACK), F32),
        ],
        compiler_params=pltpu.CompilerParams(
            dimension_semantics=("arbitrary",), vmem_limit_bytes=VMEM_LIMIT
        ),
        cost_estimate=COST,
        name="out_grad",
    )(table, *pieces, w_out, mixed, proj, gain)


def gate_kernel(
    where, grad_out, mixed_in, gate_in, sums, gain, grad_branch, normed,
    low_out, grad_mixed, keep, give, grad_gain, total,
):
    step = pl.program_id(0)
    rows = grad_out.shape[0]
    mixed, gate, grad_o = mixed_in[...], gate_in[...], grad_out[...]
    stats = jnp.concatenate([sums[...], jnp.zeros((N - 8, rows), F32)], 0).T
    out_scale = lax.rsqrt(stats[:, 0:1] * (1.0 / DI) + NORM_EPS)
    pull = out_scale * out_scale * out_scale * (stats[:, 1:2] * (1.0 / DI))
    gate_sig = jax.nn.sigmoid(gate)
    silu = gate * gate_sig
    gated = mixed * silu
    unit = gated * out_scale
    low = (unit * gain[...]).astype(BF16)
    grad_gated = out_scale * (grad_o * gain[...]) - gated * pull
    grad_mixed[...] = grad_gated * silu
    grad_z = (grad_gated * mixed * (gate_sig * (1.0 + gate * (1.0 - gate_sig)))).astype(BF16)
    low_out[:, :OWN] = low
    low_out[:, OWN:] = grad_z

    @pl.when(step == 0)
    def _():
        grad_gain[...] = jnp.zeros_like(grad_gain)
        total[...] = jnp.zeros_like(total)

    grad_gain[0:1] += jnp.sum(grad_o * unit, 0, keepdims=True)
    for k in range(4):
        part = product(low, grad_branch[:, k * WIDE : (k + 1) * WIDE], 0, 0)
        for m in range(4):
            total[4 * k + m, :SHARD_IN] += part[m * SHARD_IN : (m + 1) * SHARD_IN]
    part = product(normed[...], grad_z, 0, 0)
    for f in range(N_FSDP):
        total[f, SHARD_IN:] += part[f * SHARD_IN : (f + 1) * SHARD_IN]

    @pl.when(step == pl.num_programs(0) - 1)
    def _():
        for k in range(N_FSDP // 2):
            keep[k] = total[2 * k + where[0]]
            give[k] = total[2 * k + 1 - where[0]]


def run_gate(where, grad_out, mixed, proj, sums, gain, grad_branch, normed):
    count = 2 * ROWS
    rows = lambda width: pl.BlockSpec((count, width), lambda i: (i, 0))
    fixed = lambda shape: pl.BlockSpec(shape, lambda i: (0,) * len(shape))
    half = (N_FSDP // 2, 2 * SHARD_IN, WIDE)
    return pl.pallas_call(
        gate_kernel,
        grid=(PACK // count,),
        in_specs=[
            pl.BlockSpec(memory_space=pltpu.SMEM),
            rows(OWN),
            rows(OWN),
            rows(OWN),
            pl.BlockSpec((8, count), lambda i: (0, i)),
            fixed((1, OWN)),
            rows(D),
            rows(D),
        ],
        out_specs=[rows(2 * OWN), rows(OWN), fixed(half), fixed(half), fixed((8, OWN))],
        out_shape=[
            jax.ShapeDtypeStruct((PACK, 2 * OWN), BF16),
            jax.ShapeDtypeStruct((PACK, OWN), F32),
            jax.ShapeDtypeStruct(half, F32),
            jax.ShapeDtypeStruct(half, F32),
            jax.ShapeDtypeStruct((8, OWN), F32),
        ],
        scratch_shapes=[pltpu.VMEM((N_FSDP, 2 * SHARD_IN, WIDE), F32)],
        compiler_params=pltpu.CompilerParams(
            dimension_semantics=("arbitrary",), vmem_limit_bytes=VMEM_LIMIT
        ),
        cost_estimate=COST,
        name="gate_backward",
    )(where, grad_out, mixed, proj, sums, gain, grad_branch, normed)


def block_out_kernel(rows, weight, tokens, live, out):
    step = pl.program_id(0)
    part = matmul(jnp.concatenate([rows[0], rows[1]], 1), weight[...].reshape(2 * OWN, D))

    @pl.when(step == 0)
    def _():
        out[...] = part

    @pl.when(step > 0)
    def _():
        out[...] += part

    @pl.when(step == N_REP // 2 - 1)
    def _():
        out[...] = tokens[...].astype(F32) + live[...] * out[...]


def run_block_out(rows, weight, tokens, live):
    fixed = lambda shape: pl.BlockSpec(shape, lambda i: (0, 0))
    return pl.pallas_call(
        block_out_kernel,
        grid=(N_REP // 2,),
        in_specs=[
            pl.BlockSpec((2, ROWS, OWN), lambda i: (i, 0, 0)),
            pl.BlockSpec((2, 2, 1, SHARD_OUT, D), lambda i: (i % 2, 0, i // 2, 0, 0)),
            fixed((ROWS, D)),
            fixed((ROWS, 1)),
        ],
        out_specs=fixed((ROWS, D)),
        out_shape=jax.ShapeDtypeStruct((ROWS, D), F32),
        compiler_params=pltpu.CompilerParams(
            dimension_semantics=("arbitrary",), vmem_limit_bytes=VMEM_LIMIT
        ),
        cost_estimate=FILL,
        name="block_out",
    )(rows, weight, tokens, live)


def turned_part(weight, rows):
    return product(weight[...].reshape(D, weight.shape[-1]), rows, 1, 1)


def columns_of(full_in, width, index):
    return pl.BlockSpec(full_in.shape[:-1] + (width,), lambda i: (0, 0, 0, 0, index(i)))


def z_grad_kernel(rows, weight, out):
    part = turned_part(weight, jnp.concatenate([rows[0], rows[1]], 1))

    @pl.when(pl.program_id(0) == 0)
    def _():
        out[...] = part

    @pl.when(pl.program_id(0) > 0)
    def _():
        out[...] += part


def run_z_grad(rows, full_in):
    return pl.pallas_call(
        z_grad_kernel,
        grid=(N_REP // 2,),
        in_specs=[
            pl.BlockSpec((2, ROWS, OWN), lambda i: (i, 0, 1)),
            columns_of(full_in, 2 * OWN, lambda i: i),
        ],
        out_specs=pl.BlockSpec((D, ROWS), lambda i: (0, 0)),
        out_shape=jax.ShapeDtypeStruct((D, ROWS), F32),
        compiler_params=pltpu.CompilerParams(
            dimension_semantics=("arbitrary",), vmem_limit_bytes=VMEM_LIMIT
        ),
        cost_estimate=FILL,
        name="z_grad",
    )(rows, full_in)


def input_grad_kernel(
    grad_z, x_rows, rest_rows, w_x, w_bc, low_dt, tokens, cotangent, gain, out, gain_out, total, ordered
):
    step = pl.program_id(0)
    part = turned_part(w_x, jnp.concatenate([x_rows[0], x_rows[1]], 1))

    @pl.when(step == 0)
    def _():
        total[...] = grad_z[...] + part

    @pl.when(step > 0)
    def _():
        total[...] += part

    @pl.when(step == N_REP // 2 - 1)
    def _():
        lane = lax.broadcasted_iota(jnp.int32, (ROWS, N), 1)
        groups = []
        for k in range(2):
            group = jnp.zeros((ROWS, N), F32)
            for m in range(4):
                value = rest_rows[4 * k + m].astype(F32)
                value = value if m == 0 else pltpu.roll(value, m * OWN_BC, 1)
                group = jnp.where((lane >= m * OWN_BC) & (lane < (m + 1) * OWN_BC), value, group)
            groups.append(group.astype(BF16))
        steps = jnp.zeros((ROWS, N), F32)
        for m in range(N_REP):
            start = 8 + m * OWN_H
            value = pltpu.roll(rest_rows[m].astype(F32), (start - OWN_BC) % N, 1)
            steps = jnp.where((lane >= start) & (lane < start + OWN_H), value, steps)
        shared = total[...] + turned_part(w_bc, jnp.concatenate(groups, 1))
        for f in range(N_FSDP):
            start = eight_order(f) * SHARD_IN
            ordered[f * SHARD_IN : (f + 1) * SHARD_IN, :] = shared[start : start + SHARD_IN, :]
        grad_h = (ordered[...] + product(low_dt[...], steps.astype(BF16), 1, 1)).T
        values = tokens[...].astype(F32)
        scale = lax.rsqrt(jnp.mean(values * values, axis=1, keepdims=True) + NORM_EPS)
        unit = values * scale
        gain_sum = jnp.sum(grad_h * unit, 0, keepdims=True)
        gain_out[...] = jnp.zeros_like(gain_out)
        for k in range(D // N):
            gain_out[k : k + 1, :] = gain_sum[:, k * N : (k + 1) * N]
        grad_unit = grad_h * gain[...]
        inner = jnp.mean(grad_unit * unit, axis=1, keepdims=True)
        out[...] = cotangent[...].astype(F32) + scale * (grad_unit - unit * inner)


def run_input_grad(grad_z, tail_rows, full_in, low_dt, tokens, cotangent, gain):
    fixed = lambda shape: pl.BlockSpec(shape, lambda i: (0,) * len(shape))
    return pl.pallas_call(
        input_grad_kernel,
        grid=(N_REP // 2,),
        in_specs=[
            fixed((D, ROWS)),
            pl.BlockSpec((2, ROWS, OWN), lambda i: (i, 0, 0)),
            pl.BlockSpec((N_REP, ROWS, N), lambda i: (0, 0, OWN // N)),
            columns_of(full_in, 2 * OWN, lambda i: N_REP // 2 + i),
            columns_of(full_in, 2 * N, lambda i: DI // N),
            fixed((D, N)),
            fixed((ROWS, D)),
            fixed((ROWS, D)),
            fixed((1, D)),
        ],
        out_specs=[fixed((ROWS, D)), fixed((16, N))],
        out_shape=[jax.ShapeDtypeStruct((ROWS, D), F32), jax.ShapeDtypeStruct((16, N), F32)],
        scratch_shapes=[pltpu.VMEM((D, ROWS), F32), pltpu.VMEM((D, ROWS), F32)],
        compiler_params=pltpu.CompilerParams(
            dimension_semantics=("arbitrary",), vmem_limit_bytes=VMEM_LIMIT
        ),
        cost_estimate=COST,
        name="input_grad",
    )(grad_z, tail_rows, tail_rows, full_in, full_in, low_dt, tokens, cotangent, gain)


def rest_kernel(
    ends, parts, pre_b, pre_c, conv_in, par, grad_x, grad_dt, sums, head_acc, grad_gain, first, tail_out, small_out
):
    own = lax.broadcasted_iota(jnp.int32, (OWN_BC, 2 * N), 0) + first[0]
    chosen = (lax.broadcasted_iota(jnp.int32, (OWN_BC, 2 * N), 1) == own).astype(F32).astype(BF16)

    def pick(value):
        return product(jnp.concatenate([chosen] * 3, 1), jnp.concatenate(split_three(value), 1), 1, 1)

    grad = parts[0].astype(F32)
    for k in range(1, N_REP):
        grad = grad + parts[k].astype(F32)
    own_pre = pick(jnp.concatenate([pre_b[...], pre_c[...]], 1))
    own_conv = product(chosen, conv_in[...].astype(BF16), 1, 1)
    taps = pick(par[:, OWN:])
    sig = jax.nn.sigmoid(own_pre)
    grad_pre = grad * (sig * (1.0 + own_pre * (1.0 - sig)))
    position = lax.broadcasted_iota(jnp.int32, (1, PACK), 1)

    def segment(places):
        counted = jnp.zeros_like(places)
        for k in range(3):
            counted = counted + (places >= ends[k]).astype(jnp.int32)
        return counted

    grad_conv = taps[:, CONV - 1 : CONV] * grad_pre
    column = lax.broadcasted_iota(jnp.int32, (OWN_BC, N), 1)
    found = jnp.where(column == CONV, jnp.sum(grad_pre, 1, keepdims=True), 0.0)
    found = jnp.where(column == CONV - 1, jnp.sum(own_conv * grad_pre, 1, keepdims=True), found)
    for later_by in range(1, CONV):
        same = (segment(position + later_by) == segment(position)) & (position < PACK - later_by)
        later = jnp.where(same, pltpu.roll(grad_pre, PACK - later_by, 1), 0.0)
        tap = CONV - 1 - later_by
        found = jnp.where(column == tap, jnp.sum(own_conv * later, 1, keepdims=True), found)
        grad_conv = grad_conv + taps[:, tap : tap + 1] * later
    lane = lax.broadcasted_iota(jnp.int32, (N, N), 1)
    filler = jnp.zeros((N - OWN_BC, N), F32)
    for k in range(PACK // N):
        rows = slice(k * N, (k + 1) * N)
        columns = jnp.concatenate([grad_conv[:, rows], filler], 0).T
        steps = pltpu.roll(grad_dt[rows, :].astype(F32), OWN_BC, 1)
        tail_out[rows, :OWN] = grad_x[rows, :]
        tail_out[rows, OWN:] = jnp.where(
            lane < OWN_BC, columns, jnp.where(lane < OWN_BC + OWN_H, steps, 0.0)
        ).astype(BF16)
    row = lax.broadcasted_iota(jnp.int32, (8, OWN), 0)
    skip = head_sums(sums[...])
    by_head = jnp.concatenate([skip, jnp.zeros((8, OWN - N), F32)], 1)
    logs = jnp.concatenate([head_acc[...], jnp.zeros((8, OWN - N), F32)], 1)
    wide = jnp.where(row == 0, grad_gain[0:1, :], jnp.where(row < 6, sums[...], 0.0))
    wide = jnp.where(row == 6, logs[1:2, :], jnp.where(row == 7, by_head[6:7, :], wide))
    turned = jnp.concatenate([found, filler], 0).T
    first_row = lax.broadcasted_iota(jnp.int32, (8, N), 0) == 0
    small_out[:, :OWN] = wide
    small_out[:, OWN:] = jnp.where(first_row, head_acc[0:1, :], pltpu.roll(turned[:8], 1, 0))


def run_rest(ends, parts, pre, proj, par, grad_x, grad_dt, sums, head_acc, grad_gain, first):
    fixed = lambda shape: pl.BlockSpec(shape, lambda i: (0,) * len(shape))
    return pl.pallas_call(
        rest_kernel,
        grid=(1,),
        in_specs=[
            pl.BlockSpec(memory_space=pltpu.SMEM),
            fixed((N_REP, OWN_BC, PACK)),
            pl.BlockSpec((PACK, N), lambda i: (0, 3)),
            pl.BlockSpec((PACK, N), lambda i: (0, 4)),
            pl.BlockSpec((PACK, 2 * N), lambda i: (0, 3)),
            fixed((16, 640)),
            fixed((PACK, OWN)),
            fixed((PACK, N)),
            fixed((8, OWN)),
            fixed((8, N)),
            fixed((8, OWN)),
            pl.BlockSpec(memory_space=pltpu.SMEM),
        ],
        out_specs=[fixed((PACK, TAIL)), fixed((8, TAIL))],
        out_shape=[jax.ShapeDtypeStruct((PACK, TAIL), BF16), jax.ShapeDtypeStruct((8, TAIL), F32)],
        compiler_params=pltpu.CompilerParams(
            dimension_semantics=("arbitrary",), vmem_limit_bytes=VMEM_LIMIT
        ),
        cost_estimate=COST,
        name="rest_backward",
    )(ends, parts, pre, pre, proj, par, grad_x, grad_dt, sums, head_acc, grad_gain, first)


def tail_grad_kernel(normed, tail, small, out):
    step = pl.program_id(0)
    part = product(normed[...], tail[...], 0, 0)
    for f in range(N_FSDP):
        rows = part[f * SHARD_IN : (f + 1) * SHARD_IN]

        @pl.when(step == 0)
        def _(f=f, rows=rows):
            out[eight_order(f), :SHARD_IN] = rows
            out[eight_order(f), SHARD_IN:] = small[...]

        @pl.when(step > 0)
        def _(f=f, rows=rows):
            out[eight_order(f), :SHARD_IN] += rows


def run_tail_grad(normed, tail, small):
    count = 2 * ROWS
    shape = (N_FSDP, SHARD_IN + 8, TAIL)
    return pl.pallas_call(
        tail_grad_kernel,
        grid=(PACK // count,),
        in_specs=[
            pl.BlockSpec((count, D), lambda i: (i, 0)),
            pl.BlockSpec((count, TAIL), lambda i: (i, 0)),
            pl.BlockSpec((8, TAIL), lambda i: (0, 0)),
        ],
        out_specs=pl.BlockSpec(shape, lambda i: (0, 0, 0)),
        out_shape=jax.ShapeDtypeStruct(shape, F32),
        compiler_params=pltpu.CompilerParams(
            dimension_semantics=("arbitrary",), vmem_limit_bytes=VMEM_LIMIT
        ),
        cost_estimate=COST,
        name="tail_grad",
    )(normed, tail, small)


def adam_step(grad, weight, first, second, grad_out, first_out, second_out, weight_out):
    new_weight, new_first, new_second = adam_update(
        weight[...], grad, first[...], second[...], RATE_MATRIX, WEIGHT_DECAY
    )
    grad_out[...] = grad
    first_out[...] = new_first
    second_out[...] = new_second
    weight_out[...] = new_weight


def load_pair(step, pairs, rows, grad):
    pair, right, far_first, far_second, left = pairs
    for slot, (low, high) in enumerate(
        (((pair, 0), (pair, 1)), ((right, 0), (right, 1)), ((far_first, 0), (far_second, 0)), ((left, 0), (left, 1)))
    ):

        @pl.when(step == slot)
        def _(low=low, high=high):
            grad[:, :WIDE] = low[0][low[1], rows, :]
            grad[:, WIDE:] = high[0][high[1], rows, :]


def adam_pairs_kernel(rows, table, *refs):
    pairs, arrays, grad = refs[:5], refs[5:8] + refs[-5:-1], refs[-1]
    load_pair(pl.program_id(0), pairs, rows, grad)
    adam_step(grad[...], *arrays)


def run_adam_pairs(table, place_of, rows, pairs, weight, first, second):
    part = pl.BlockSpec((SHARD_IN, 2 * WIDE), lambda i, table: place_of(table[i]))
    shape = jax.ShapeDtypeStruct(weight.shape, F32)
    return pl.pallas_call(
        partial(adam_pairs_kernel, rows),
        grid_spec=pltpu.PrefetchScalarGridSpec(
            num_scalar_prefetch=1,
            grid=(4,),
            in_specs=[pl.BlockSpec(pair.shape, lambda i, table: (0, 0, 0)) for pair in pairs]
            + [part] * 3,
            out_specs=[part] * 4,
            scratch_shapes=[pltpu.VMEM((SHARD_IN, 2 * WIDE), F32)],
        ),
        out_shape=[shape] * 4,
        compiler_params=pltpu.CompilerParams(
            dimension_semantics=("arbitrary",), vmem_limit_bytes=VMEM_LIMIT
        ),
        cost_estimate=FILL,
        name="adam",
    )(table, *pairs, weight, first, second)


def adam_tail_kernel(pair, rest, *refs):
    arrays, grad = refs[:3] + refs[-5:-1], refs[-1]
    step = pl.program_id(0)

    @pl.when(step < N_REP // 2)
    def _():
        grad[:, :WIDE] = pair[0, :SHARD_IN]
        grad[:, WIDE:] = pair[1, :SHARD_IN]

    @pl.when(step == N_REP // 2)
    def _():
        lane = lax.broadcasted_iota(jnp.int32, (SHARD_IN, N), 1)
        for k in range(2):
            group = jnp.zeros((SHARD_IN, N), F32)
            for m in range(4):
                value = rest[4 * k + m, :SHARD_IN]
                value = value if m == 0 else pltpu.roll(value, m * OWN_BC, 1)
                group = jnp.where((lane >= m * OWN_BC) & (lane < (m + 1) * OWN_BC), value, group)
            grad[:, k * N : (k + 1) * N] = group

    adam_step(grad[...], *arrays)


def run_adam_tail(parts, weight, first, second, before):
    half = N_REP // 2
    rows = parts.shape[1]
    column = pl.BlockSpec((SHARD_IN, 2 * WIDE), lambda i: (0, half + i))
    shape = jax.ShapeDtypeStruct(weight.shape, F32)
    return pl.pallas_call(
        adam_tail_kernel,
        grid=(half + 1,),
        in_specs=[
            pl.BlockSpec((2, rows, OWN), lambda i: (jnp.minimum(i, half - 1), 0, 0)),
            pl.BlockSpec((N_REP, rows, N), lambda i: (0, 0, OWN // N)),
        ]
        + [column] * 3
        + [pl.BlockSpec(memory_space=pl.ANY)] * 4,
        out_specs=[column] * 4,
        out_shape=[shape] * 4,
        input_output_aliases={5 + k: k for k in range(4)},
        scratch_shapes=[pltpu.VMEM((SHARD_IN, 2 * WIDE), F32)],
        compiler_params=pltpu.CompilerParams(
            dimension_semantics=("arbitrary",), vmem_limit_bytes=VMEM_LIMIT
        ),
        cost_estimate=COST,
        name="adam_tail",
    )(parts, parts, weight, first, second, *before)


def body(
    tokens,
    cotangent,
    lengths,
    w_in,
    w_dt,
    w_out,
    small,
    first_in,
    first_dt,
    first_out,
    first_small,
    second_in,
    second_dt,
    second_out,
    second_small,
):
    place = Place()
    r = place.r
    zero = jnp.int32(0)
    pack_lengths = lax.dynamic_slice_in_dim(lengths, place.f, 1, 0)[0]
    seg_ends = jnp.cumsum(pack_lengths)
    own_positions = r * ROWS + jnp.arange(ROWS, dtype=jnp.int32)
    own_live = (segment_at(own_positions, seg_ends) < 3).astype(F32)[:, None]
    slots = jnp.arange(N_REP, dtype=jnp.int32)
    ahead = ((place.x + slots // 2) % 4) * 2 + (place.yl + slots) % 2
    half = ROWS // 2

    in_low = w_in.astype(BF16)
    dt_low = w_dt.astype(BF16)
    out_low = w_out.astype(BF16)

    small_rows = jnp.pad(small.astype(BF16), (0, 16 * 3 * WIDE - SHARD_SMALL)).reshape(16, 3 * WIDE)

    def own_columns(rep):
        columns = jnp.concatenate(
            [
                lax.dynamic_slice_in_dim(in_low, rep * OWN, OWN, 1),
                lax.dynamic_slice_in_dim(in_low, DI + rep * OWN, OWN, 1),
                in_low[:, 2 * DI :],
                lax.dynamic_slice_in_dim(dt_low, rep * OWN_H, OWN_H, 1),
                jnp.zeros((SHARD_IN, 2), BF16),
                dt_low,
                jnp.zeros((SHARD_IN, N - 8 - H), BF16),
            ],
            1,
        )
        return jnp.concatenate([columns, small_rows], 0)

    other_columns = move(
        own_columns(2 * place.x + 1 - place.yl), lambda yh, z, c, x, yl: (yh + 1, z, c, x, yl + 1)
    )
    from_left = move(tokens, along_x(1))
    from_right = move(tokens, along_x(-1))
    partner = move(tokens, swap_y)

    out_other = move(out_low, lambda yh, z, c, x, yl: (yh + 1, z, c, x, yl + 1))
    from_left, from_right, partner, out_low, out_other, other_columns = lax.optimization_barrier(
        (from_left, from_right, partner, out_low, out_other, other_columns)
    )
    own_shards = gather_eight(both(own_columns(r), other_columns, place.yh))
    far = move(from_left, along_x(1))
    partner_left = move(from_left, swap_y)
    partner_right = move(partner, along_x(-1))
    out_pair = both(out_low, out_other, place.yh)

    far, partner_left, partner_right, out_pair = lax.optimization_barrier(
        (far, partner_left, partner_right, out_pair)
    )
    partner_far_top = move(partner_left[:half], along_x(1))
    partner_far_low = move(partner_right[half:], along_x(-1))

    vector = own_shards[:, :, :, SHARD_IN : SHARD_IN + 2].transpose(2, 0, 1, 3, 4)
    vector = vector.reshape(N_FSDP, 6 * WIDE)[:, :SHARD_SMALL].reshape(-1).astype(F32)
    offset = 0
    gain_in = vector[None, :D]
    offset = D
    gain_row = lax.dynamic_slice_in_dim(vector, offset + r * OWN, OWN, 0)[None, :]
    offset += DI
    taps = vector[offset : offset + (CONV + 1) * CHANNELS].reshape(CONV + 1, CHANNELS)
    offset += (CONV + 1) * CHANNELS
    per_head = vector[offset:].reshape(3, H)
    dt_bias, a_log, d_skip = lax.dynamic_slice_in_dim(per_head, r * OWN_H, OWN_H, 1)
    taps_bc = taps[:, DI:]
    conv_par = jnp.concatenate([lax.dynamic_slice_in_dim(taps, r * OWN, OWN, 1), taps_bc], 1)
    head_par = jnp.stack(
        [
            jnp.pad(jnp.broadcast_to(d_skip[:, None], (OWN_H, P_SIZE)).reshape(-1), (0, 2 * N)),
            jnp.pad(dt_bias, (0, 640 - OWN_H)),
            jnp.pad(-jnp.exp(a_log), (0, 640 - OWN_H)),
        ],
        0,
    )
    par = jnp.concatenate([conv_par, head_par, jnp.zeros((8, 640), F32)], 0)

    branch = (cotangent.astype(F32) * own_live).astype(BF16)
    branch, in_low, partner_far_top, partner_far_low, own_shards = lax.optimization_barrier(
        (branch, in_low, partner_far_top, partner_far_low, own_shards)
    )
    full_out = gather_eight(tie(out_pair, own_shards))
    in_other = move(in_low, lambda yh, z, c, x, yl: (yh + 1, z, c, x, yl + 1))
    b_left = move(branch, along_x(1))
    b_right = move(branch, along_x(-1))
    b_partner = move(branch, swap_y)
    token_pieces = [
        tokens, partner, from_right, partner_right, far,
        partner_far_top, partner_far_low, from_left, partner_left,
    ]
    normed, proj, low_dt = run_project(ahead, token_pieces, gain_in, own_shards)
    b_left, b_right, b_partner, proj = lax.optimization_barrier((b_left, b_right, b_partner, proj))
    b_far = move(b_left, along_x(1))
    b_partner_left = move(b_left, swap_y)
    b_partner_right = move(b_partner, along_x(-1))
    before = run_forward(0, seg_ends, proj, par)
    b_far, b_partner_left, b_partner_right, in_other, in_low, before = lax.optimization_barrier(
        (b_far, b_partner_left, b_partner_right, in_other, in_low, before)
    )
    full_in = gather_eight(both(in_low, in_other, place.yh))
    b_partner_far = move(b_partner_left, along_x(1))
    pre, mixed, states, _ = run_forward(1, seg_ends, proj, par, before)
    branch_pieces = [branch, b_partner, b_right, b_partner_right, b_far, b_partner_far, b_left, b_partner_left]
    rep_table = jnp.concatenate([ahead, r[None]])
    grad_branch, grad_normed_out, sums = run_out_grad(rep_table, branch_pieces, full_out, mixed, proj, gain_row)
    sums = sum_rep(sums[:2].reshape(32, 128)).reshape(2, PACK)
    sums = jnp.concatenate([sums, jnp.zeros((6, PACK), F32)], 0)

    low_rows, grad_mixed, keep, give, grad_gain = run_gate(
        place.c[None], grad_normed_out, mixed, proj, sums, gain_row, grad_branch, normed
    )

    low_rows = exchange(low_rows.reshape(N_REP, ROWS, 2 * OWN), "rep")
    got = move(give, swap_core)
    grad_x, grad_dtraw, grad_bc, grad_sums, grad_heads = run_backward(
        seg_ends, proj, pre, mixed, grad_mixed, states, par
    )
    low_rows, got, grad_bc, grad_x = lax.optimization_barrier((low_rows, got, grad_bc, grad_x))

    grad_bc = exchange(grad_bc, "rep").reshape(N_REP, OWN_BC, PACK)
    split = (2, 4, 2 * SHARD_IN, WIDE)
    early, early_found = start_ring(keep.reshape(split), got.reshape(split), None, place)
    grad_rows = run_z_grad(low_rows, full_in)
    block_out = run_block_out(low_rows, full_out, tokens, own_live)
    grad_bc, grad_rows, block_out, early_found = lax.optimization_barrier(
        (grad_bc, grad_rows, block_out, early_found)
    )

    early, _ = end_ring(early, early_found, None)
    early, early_half = start_half(early, None, place)
    tail, small_own = run_rest(
        seg_ends, grad_bc, pre, proj, par, grad_x, grad_dtraw, grad_sums, grad_heads, grad_gain, (r * OWN_BC)[None]
    )
    tail_rows = exchange(tail.reshape(N_REP, ROWS, TAIL), "rep")
    tail_part = scatter_eight(run_tail_grad(normed, tail, small_own))
    early, _ = end_half(early, early_half, None)
    out_part = move(
        early[:SHARD_IN],
        lambda yh, z, c, x, yl: (x // 2, (x % 2) * 2 + yl, z % 2, 2 * c + yh, z // 2),
    )
    tail_rows, out_part = lax.optimization_barrier((tail_rows, out_part))

    early = jnp.concatenate([out_part, early[SHARD_IN:]], 0)
    early_other = move(early, swap_y)
    input_grad, grad_gain_in = run_input_grad(
        grad_rows, tail_rows, full_in, low_dt, tokens, cotangent, gain_in
    )
    tail_part, early_other, input_grad, grad_gain_in = lax.optimization_barrier(
        (tail_part, early_other, input_grad, grad_gain_in)
    )

    tail_part, tail_half = start_half(tail_part, None, place)
    early_pair = both(early, early_other, place.yl)
    early_left, early_right = move(early_pair, along_x(1)), move(early_pair, along_x(-1))
    tail_half, grad_gain_in = lax.optimization_barrier((tail_half, grad_gain_in))

    tail_part, _ = end_half(tail_part, tail_half, None)
    tail_parts = share_rep(tail_part)
    grad_gain_in = sum_all(grad_gain_in)
    early_far = move(early_left[:1], along_x(1)), move(early_right[1:], along_x(-1))
    early_pairs = (early_pair, early_right, *early_far, early_left)

    x_order = (place.x + jnp.arange(4, dtype=jnp.int32)) % 4
    grad_out, new_first_out, new_second_out, new_out = run_adam_pairs(
        x_order, lambda k: (k // 2, k % 2), slice(0, SHARD_IN), early_pairs, w_out, first_out, second_out
    )
    updated = run_adam_pairs(
        x_order, lambda k: (0, k), slice(SHARD_IN, 2 * SHARD_IN), early_pairs, w_in, first_in, second_in
    )
    grad_in, new_first_in, new_second_in, new_in = run_adam_tail(tail_parts, w_in, first_in, second_in, updated)

    def columns(parts):
        return parts.transpose(1, 0, 2).reshape(parts.shape[1], -1)

    grad_gain_in = grad_gain_in[: D // N].reshape(-1)
    small_parts = tail_parts[:, SHARD_IN:]
    small_x = small_parts[:, :, :OWN].transpose(1, 0, 2).reshape(8, DI)
    small_bc = small_parts[:, :, OWN:].transpose(1, 0, 2)

    def channels(row):
        return jnp.concatenate([small_x[row], small_bc[row, :, :OWN_BC].reshape(-1)])

    grad_small_all = jnp.concatenate(
        [grad_gain_in, small_x[0]]
        + [channels(row) for row in range(1, 6)]
        + [
            small_bc[0, :, :OWN_H].reshape(-1),
            small_parts[:, 6, :OWN_H].reshape(-1),
            small_parts[:, 7, :OWN_H].reshape(-1),
        ]
    )
    grad_small = lax.dynamic_slice_in_dim(grad_small_all, place.f * SHARD_SMALL, SHARD_SMALL, 0)
    grad_dt = columns(tail_parts[:, :SHARD_IN, OWN + OWN_BC : OWN + OWN_BC + OWN_H])
    new_dt, new_first_dt, new_second_dt = adam_update(
        w_dt, grad_dt, first_dt, second_dt, RATE_MATRIX, WEIGHT_DECAY
    )
    new_small, new_first_small, new_second_small = adam_update(
        small, grad_small, first_small, second_small, RATE_SMALL, 0.0
    )
    return (
        block_out,
        input_grad,
        grad_in,
        grad_dt,
        grad_out,
        grad_small,
        new_first_in,
        new_first_dt,
        new_first_out,
        new_first_small,
        new_second_in,
        new_second_dt,
        new_second_out,
        new_second_small,
        new_in,
        new_dt,
        new_out,
        new_small,
    )


def solution(mesh):
    rows = P(("fsdp", "rep"), None)
    matrix = P("fsdp", None)
    vector = P("fsdp")
    group = (matrix, matrix, matrix, vector)
    return jax.shard_map(
        body,
        mesh=mesh,
        in_specs=(rows, rows, P()) + group * 3,
        out_specs=(rows, rows) + group * 4,
        check_vma=False,
    )
```

```python
from functools import partial

import jax
import jax.numpy as jnp
from jax import lax
from jax.experimental import pallas as pl
from jax.experimental.pallas import tpu as pltpu
from jax.sharding import PartitionSpec as P

D = 1536
H = 48
P_SIZE = 64
N = 128
CONV = 4
STEP = 10
DI = 3072
CHANNELS = DI + 2 * N
SMALL = 21392
N_FSDP = 16
N_REP = 8
ROWS = 256
PACK = 2048
OWN = DI // N_REP
OWN_H = H // N_REP
OWN_BC = 2 * N // N_REP
SHARD_IN = D // N_FSDP
SHARD_OUT = DI // N_FSDP
SHARD_SMALL = SMALL // N_FSDP
WIDE = 384
CHUNK = 128
CHUNKS = PACK // CHUNK
HALF = CHUNKS // 2
TAIL = 512
VMEM_LIMIT = 60 * 1024 * 1024

NORM_EPS = 1e-05
BETA_ONE = 0.9
BETA_TWO = 0.999
ADAM_EPS = 1e-08
WEIGHT_DECAY = 0.1
RATE_MATRIX = 0.04
RATE_SMALL = 0.4
PRECISE = lax.Precision.HIGHEST
BF16 = jnp.bfloat16
F32 = jnp.float32
COST = pl.CostEstimate(flops=1_000_000, bytes_accessed=100_000, transcendentals=0)
FILL = pl.CostEstimate(flops=2_400_000_000, bytes_accessed=20_000_000, transcendentals=0)


def move(value, target):
    pairs = []
    for f in range(N_FSDP):
        for r in range(N_REP):
            yh, z, c, x, yl = target(f // 8, (f // 2) % 4, f % 2, r // 2, r % 2)
            pairs.append((f * N_REP + r, ((yh % 2) * 8 + (z % 4) * 2 + c % 2) * N_REP + (x % 4) * 2 + yl % 2))
    return lax.ppermute(value, ("fsdp", "rep"), pairs)


def along_x(steps):
    return lambda yh, z, c, x, yl: (yh, z, c, x + steps, yl)


def along_z(steps):
    return lambda yh, z, c, x, yl: (yh, z + steps, c, x, yl)


def swap_y(yh, z, c, x, yl):
    return (yh, z, c, x, yl + 1)


def swap_y_hi(yh, z, c, x, yl):
    return (yh + 1, z, c, x, yl)


def swap_core(yh, z, c, x, yl):
    return (yh, z, c + 1, x, yl)


class Place:
    def __init__(self):
        f = lax.axis_index("fsdp")
        r = lax.axis_index("rep")
        self.f, self.r = f, r
        self.yh, self.z, self.c = f // 8, (f // 2) % 4, f % 2
        self.x, self.yl = r // 2, r % 2


def at(value, index, axis=0):
    return lax.dynamic_index_in_dim(value, index, axis, keepdims=False)


def tie(values, *others):
    return lax.optimization_barrier((values, others))[0]


def both(mine, other, second):
    first = jnp.where(second == 0, mine, other)
    last = jnp.where(second == 0, other, mine)
    return jnp.stack([first, last], 0)


def put(out, piece, axis, index):
    starts = [jnp.int32(0)] * out.ndim
    starts[axis] = jnp.int32(index)
    return lax.dynamic_update_slice(out, jnp.expand_dims(piece, axis), tuple(starts))


def swap_shards(value, place):
    other = move(value, lambda yh, z, c, x, yl: (yh + 1, z, c, x, yl + 1))
    return both(value, other, place.yh)


def gather_eight(pair):
    groups = [list(range(8)), list(range(8, 16))]
    out = lax.all_gather(pair, "fsdp", axis=0, tiled=True, axis_index_groups=groups)
    return out.reshape((4, 2) + pair.shape)


def start_ring(keep, got, extra, place):
    own = at(keep, place.z, 1) + at(got, place.z, 1)
    found = []
    for step in (1, 3, 2):
        there = (place.z + step) % 4
        found.append(move(with_rows(at(keep, there, 1) + at(got, there, 1), extra), along_z(step)))
    return own, found


def end_ring(own, found, extra):
    rows = own.shape[0] * own.shape[1]
    total = own
    for part in found:
        total = total + part[:rows].reshape(own.shape)
        extra = None if extra is None else extra + part[rows:]
    return total, extra


def start_half(total, extra, place):
    return at(total, place.yh), move(with_rows(at(total, 1 - place.yh), extra), swap_y_hi)


def end_half(mine, other, extra):
    rows = mine.shape[0]
    return mine + other[:rows], None if extra is None else extra + other[rows:]


def exchange(value, axis):
    return lax.all_to_all(value, axis, 0, 0, tiled=True)


def share_rep(value):
    return exchange(jnp.broadcast_to(value[None], (N_REP,) + value.shape), "rep")


def sum_rep(value):
    value = value + move(value, swap_y)
    steps = [move(value, along_x(step)) for step in (1, 3, 2)]
    return value + steps[0] + steps[1] + steps[2]


def sum_all(value):
    value = value + move(value, swap_core)
    steps = [move(value, along_z(step)) for step in (1, 3, 2)]
    value = value + steps[0] + steps[1] + steps[2]
    return sum_rep(value + move(value, swap_y_hi))


def scatter_eight(value):
    groups = [list(range(8)), list(range(8, 16))]
    flat = value.reshape(-1, value.shape[-1])
    out = lax.psum_scatter(flat, "fsdp", scatter_dimension=0, tiled=True, axis_index_groups=groups)
    return out.reshape((2,) + value.shape[1:])


def eight_order(f):
    return ((f // 2) % 4 * 2 + f % 2) * 2 + f // 8


def with_rows(block, extra):
    width = block.shape[-1]
    flat = block.reshape(-1, width)
    return flat if extra is None else jnp.concatenate([flat, extra], 0)


def adam_update(weight, gradient, moment_one, moment_two, learn_rate, decay_rate):
    moment_one = BETA_ONE * moment_one + (1.0 - BETA_ONE) * gradient
    moment_two = BETA_TWO * moment_two + (1.0 - BETA_TWO) * gradient * gradient
    scaled = (
        moment_one
        / (1.0 - BETA_ONE**STEP)
        / (jnp.sqrt(moment_two / (1.0 - BETA_TWO**STEP)) + ADAM_EPS)
    )
    return (weight - learn_rate * (scaled + decay_rate * weight), moment_one, moment_two)


def contract_rows(left_side, right_side):
    return lax.dot_general(
        left_side, right_side, (((0,), (0,)), ((), ())), preferred_element_type=F32
    )


def contract_cols(left_side, right_side):
    return lax.dot_general(
        left_side, right_side, (((1,), (1,)), ((), ())), preferred_element_type=F32
    )


def matmul(left_side, right_side):
    return jnp.dot(left_side, right_side, preferred_element_type=F32)


def segment_at(positions, seg_ends):
    counted = jnp.sum((positions[:, None] >= seg_ends[None, :]).astype(jnp.int32), axis=1)
    return jnp.where(positions < 0, jnp.int32(-1), counted)


def split_two(value):
    high = value.astype(BF16)
    return high, (value - high.astype(F32)).astype(BF16)


def split_three(value):
    high = value.astype(BF16)
    rest = value - high.astype(F32)
    middle = rest.astype(BF16)
    return high, middle, (rest - middle.astype(F32)).astype(BF16)


def product(left, right, left_dim, right_dim):
    return lax.dot_general(
        left, right, (((left_dim,), (right_dim,)), ((), ())), preferred_element_type=F32
    )


def joined_product(left_parts, right_parts, left_dim=1, right_dim=0):
    left_high, left_low = left_parts
    right_high, right_low = right_parts
    return product(
        jnp.concatenate([left_high, left_high, left_low], left_dim),
        jnp.concatenate([right_high, right_low, right_high], right_dim),
        left_dim,
        right_dim,
    )


def precise_product(left, right, left_dim=1, right_dim=0):
    return joined_product(split_two(left), split_two(right), left_dim, right_dim)


def ones_product(ones, value):
    return product(jnp.concatenate([ones] * 3, 1), jnp.concatenate(split_three(value), 0), 1, 0)


def spread(per_head, lane):
    return jnp.concatenate(
        [
            jnp.where(lane < P_SIZE, per_head[:, 2 * k : 2 * k + 1], per_head[:, 2 * k + 1 : 2 * k + 2])
            for k in range(OWN_H // 2)
        ],
        1,
    )


def head_sums(value):
    column = lax.broadcasted_iota(jnp.int32, (OWN, N), 0)
    head = lax.broadcasted_iota(jnp.int32, (OWN, N), 1)
    members = ((column >= head * P_SIZE) & (column < (head + 1) * P_SIZE)).astype(F32).astype(BF16)
    high, low = split_two(value)
    return product(jnp.concatenate([high, low], 1), jnp.concatenate([members, members], 0), 1, 0)


def two_heads(pair, lane):
    zero = jnp.zeros_like(pair)
    return jnp.concatenate([jnp.where(lane < P_SIZE, pair, zero), jnp.where(lane < P_SIZE, zero, pair)], 0)


def chunk_facts(ends, chunk, dt_pre, par):
    column = lax.broadcasted_iota(jnp.int32, (CHUNK, 1), 0) + chunk * CHUNK
    row = lax.broadcasted_iota(jnp.int32, (1, CHUNK), 1) + chunk * CHUNK

    def segment(position):
        counted = jnp.zeros_like(position)
        for k in range(3):
            counted = counted + (position >= ends[k]).astype(jnp.int32)
        return jnp.where(position < 0, -1, counted)

    def one_segment(position):
        counted = jnp.int32(0)
        for k in range(3):
            counted = counted + (position >= ends[k]).astype(jnp.int32)
        return jnp.where(position < 0, -1, counted)

    here_column, here_row = segment(column), segment(row)
    prior = one_segment(chunk * CHUNK - 1)
    last = one_segment(chunk * CHUNK + CHUNK - 1)
    lane = lax.broadcasted_iota(jnp.int32, (CHUNK, N), 1)
    shifted = dt_pre + par[6:7, :N]
    soft = jnp.maximum(shifted, 0.0) + jnp.log1p(jnp.exp(-jnp.abs(shifted)))
    step = jnp.where(lane < OWN_H, soft, 0.0)
    decay = step * par[7:8, :N]
    tri_row = lax.broadcasted_iota(jnp.int32, (CHUNK, CHUNK), 0)
    tri_column = lax.broadcasted_iota(jnp.int32, (CHUNK, CHUNK), 1)
    lower = (tri_row >= tri_column).astype(F32).astype(BF16)
    upper = (tri_row <= tri_column).astype(F32).astype(BF16)
    total = ones_product(lower, decay)
    entering = (here_column == prior).astype(F32) * jnp.exp(total)
    end = total[CHUNK - 1 : CHUNK]
    leaving = (here_column == last).astype(F32) * jnp.exp(jnp.minimum(end - total, 0.0))
    passing = jnp.where(last == prior, 1.0, 0.0) * jnp.exp(end)
    return dict(
        column=column,
        segment=segment,
        here_column=here_column,
        here_row=here_row,
        lane=lane,
        shifted=shifted,
        step=step,
        decay=decay,
        total=total,
        entering=entering,
        leaving=leaving,
        passing=passing,
        tri_row=tri_row,
        tri_column=tri_column,
        upper=upper,
    )


def forward_kernel(part, ends, proj, par, *refs):
    if part:
        carry_in, refs = refs[3], refs[4:]
    pre_out, mixed_out, state_out, carry_out, extended, state = refs
    chunk = pl.program_id(0) + part * HALF

    @pl.when(pl.program_id(0) == 0)
    def _():
        if part:
            state[...] = carry_in[:N, :OWN]
            extended[0:8, :] = carry_in[N:, :]
        else:
            state[...] = jnp.zeros_like(state)
            extended[0:8, :] = jnp.zeros((8, 640), F32)

    facts = chunk_facts(ends, chunk, proj[:, 1024:1152], par)
    lane = facts["lane"]
    conv = proj[:, OWN:1024].astype(BF16).astype(F32)
    extended[8 : 8 + CHUNK, :] = conv
    pre = par[4:5] + par[3:4] * conv
    for back in range(1, CONV):
        same = (facts["segment"](facts["column"] - back) == facts["here_column"]).astype(F32)
        pre = pre + par[3 - back : 4 - back] * (extended[8 - back : 8 - back + CHUNK, :] * same)
    extended[0:8, :] = extended[CHUNK : CHUNK + 8, :]
    pre_out[...] = pre
    act = pre * jax.nn.sigmoid(pre)
    own_x, state_b, state_c = act[:, :OWN], act[:, OWN : OWN + N], act[:, OWN + N :]
    stepped = own_x * spread(facts["step"], lane)
    b_parts, c_parts = split_two(state_b), split_two(state_c)
    inside = (facts["tri_row"] >= facts["tri_column"]) & (facts["here_column"] == facts["here_row"])
    scores = jnp.where(inside, joined_product(c_parts, b_parts, 1, 1), 0.0)
    total_rows = facts["total"].T
    state_in = state[...]
    state_out[...] = state_in
    outs = []
    for pair in range(OWN_H // 2):
        mixing = []
        for head in (2 * pair, 2 * pair + 1):
            span = facts["total"][:, head : head + 1] - total_rows[head : head + 1, :]
            mixing.append(jnp.exp(jnp.minimum(span, 0.0)) * scores)
        inner = two_heads(stepped[:, pair * N : pair * N + N], lane)
        outs.append(precise_product(jnp.concatenate(mixing, 1), inner))
    scanned = jnp.concatenate(outs, 1) + spread(facts["entering"], lane) * joined_product(
        c_parts, split_two(state_in)
    )
    state[...] = spread(facts["passing"], lane[:1]) * state_in + precise_product(
        state_b.T, stepped * spread(facts["leaving"], lane)
    )
    mixed_out[...] = scanned + par[5:6, :OWN] * own_x

    @pl.when(pl.program_id(0) == HALF - 1)
    def _():
        carry_out[:N, :OWN] = state[...]
        carry_out[:N, OWN:] = jnp.zeros((N, 640 - OWN), F32)
        carry_out[N:, :] = extended[0:8, :]


def run_forward(part, ends, proj, par, before=()):
    here = lambda i: (i + part * HALF, 0)
    chunked = lambda width: pl.BlockSpec((CHUNK, width), here)
    fixed = lambda shape: pl.BlockSpec(shape, lambda i: (0, 0))
    carry = fixed((N + 8, 640))
    return pl.pallas_call(
        partial(forward_kernel, part),
        grid=(HALF,),
        in_specs=[pl.BlockSpec(memory_space=pltpu.SMEM), chunked(1152), fixed((16, 640))]
        + ([pl.BlockSpec(memory_space=pl.ANY)] * 3 + [carry] if part else []),
        out_specs=[chunked(640), chunked(OWN), pl.BlockSpec((N, OWN), here), carry],
        out_shape=[
            jax.ShapeDtypeStruct((PACK, 640), F32),
            jax.ShapeDtypeStruct((PACK, OWN), F32),
            jax.ShapeDtypeStruct((CHUNKS * N, OWN), F32),
            jax.ShapeDtypeStruct((N + 8, 640), F32),
        ],
        input_output_aliases={3: 0, 4: 1, 5: 2} if part else {},
        scratch_shapes=[pltpu.VMEM((CHUNK + 8, 640), F32), pltpu.VMEM((N, OWN), F32)],
        compiler_params=pltpu.CompilerParams(
            dimension_semantics=("arbitrary",), vmem_limit_bytes=VMEM_LIMIT
        ),
        cost_estimate=COST,
        name="scan_forward",
    )(ends, proj, par, *before)


def backward_kernel(ends, conv_in, dt_in, pre_in, mixed_in, grad_mixed, state_all, par, *refs):
    grad_x, grad_dt, grad_bc, sums, head_acc, carried, extended, end_dot = refs
    step_index = pl.program_id(0)
    chunk = CHUNKS - 1 - step_index

    @pl.when(step_index == 0)
    def _():
        carried[...] = jnp.zeros_like(carried)
        extended[CHUNK : CHUNK + 8, :] = jnp.zeros((8, OWN), F32)
        end_dot[...] = jnp.zeros_like(end_dot)
        sums[...] = jnp.zeros_like(sums)
        head_acc[...] = jnp.zeros_like(head_acc)

    facts = chunk_facts(ends, chunk, dt_in[...], par)
    lane = facts["lane"]
    pre = pre_in[...]
    sig = jax.nn.sigmoid(pre)
    act = pre * sig
    own_x, state_b, state_c = act[:, :OWN], act[:, OWN : OWN + N], act[:, OWN + N :]
    step = facts["step"]
    step_wide = spread(step, lane)
    stepped = own_x * step_wide
    skip = par[5:6, :OWN]
    scanned = mixed_in[...] - skip * own_x
    grad_m = grad_mixed[...]
    sums[6:7] += jnp.sum(grad_m * own_x, 0, keepdims=True)

    b_parts, c_parts = split_two(state_b), split_two(state_c)
    inside = (facts["tri_row"] <= facts["tri_column"]) & (facts["here_column"] == facts["here_row"])
    scores = jnp.where(inside, joined_product(b_parts, c_parts, 1, 1), 0.0)
    total_rows = facts["total"].T
    grad_scores = jnp.zeros((CHUNK, CHUNK), F32)
    grad_stepped = []
    for pair in range(OWN_H // 2):
        columns = slice(pair * N, pair * N + N)
        grad_pair = grad_m[:, columns]
        high, low = split_two(grad_pair)
        stepped_parts = split_two(two_heads(stepped[:, columns], lane))
        grad_mixing = joined_product(stepped_parts, (high, low), 1, 1)
        mixing = []
        for k in range(2):
            head = 2 * pair + k
            span = total_rows[head : head + 1, :] - facts["total"][:, head : head + 1]
            decays = jnp.exp(jnp.minimum(span, 0.0))
            mixing.append(decays * scores)
            grad_scores = grad_scores + decays * grad_mixing[k * CHUNK : (k + 1) * CHUNK]
        grad_stepped.append(
            joined_product(
                split_two(jnp.concatenate(mixing, 1)), (two_heads(high, lane), two_heads(low, lane))
            )
        )
    grad_scores = jnp.where(inside, grad_scores, 0.0)
    carry = carried[...]
    carry_parts = split_two(carry)
    leaving = spread(facts["leaving"], lane)
    grad_stepped = jnp.concatenate(grad_stepped, 1) + leaving * joined_product(b_parts, carry_parts)
    state_in = state_all[...]
    entered = spread(facts["entering"], lane) * grad_m
    entered_parts = split_two(entered)
    grad_b = precise_product(grad_scores, state_c) + joined_product(
        split_two(leaving * stepped), carry_parts, 1, 1
    )
    grad_c = precise_product(grad_scores.T, state_b) + joined_product(
        entered_parts, split_two(state_in), 1, 1
    )
    grad_bc[0:N, :] = grad_b.T.astype(BF16)
    grad_bc[N:, :] = grad_c.T.astype(BF16)
    new_carry = spread(facts["passing"], lane[:1]) * carry + joined_product(
        split_two(state_c.T), entered_parts
    )
    carried[...] = new_carry

    grad_step = head_sums(own_x * grad_stepped)
    last_row = lax.broadcasted_iota(jnp.int32, (CHUNK, N), 0) == CHUNK - 1
    grad_total = head_sums(grad_m * scanned) - step * grad_step
    grad_total = grad_total + jnp.where(last_row, end_dot[0:1, :], 0.0)
    grad_decay = ones_product(facts["upper"], grad_total)
    end_dot[...] = head_sums(
        jnp.broadcast_to(jnp.sum(new_carry * state_in, 0, keepdims=True), (8, OWN))
    )
    grad_pre_dt = (grad_step + grad_decay * par[7:8, :N]) * jax.nn.sigmoid(facts["shifted"])
    grad_pre_dt = jnp.where(lane < OWN_H, grad_pre_dt, 0.0)
    grad_dt[...] = grad_pre_dt.astype(BF16)
    head_acc[0:1] += jnp.sum(grad_pre_dt, 0, keepdims=True)
    head_acc[1:2] += jnp.sum(grad_decay * facts["decay"], 0, keepdims=True)

    sig_x, pre_x = sig[:, :OWN], pre[:, :OWN]
    grad_pre = (step_wide * grad_stepped + skip * grad_m) * (sig_x * (1.0 + pre_x * (1.0 - sig_x)))
    extended[0:CHUNK, :] = grad_pre
    conv = conv_in[...].astype(BF16).astype(F32)
    sums[5:6] += jnp.sum(grad_pre, 0, keepdims=True)
    sums[4:5] += jnp.sum(conv * grad_pre, 0, keepdims=True)
    grad_conv = par[3:4, :OWN] * grad_pre
    for ahead in range(1, CONV):
        same = (facts["segment"](facts["column"] + ahead) == facts["here_column"]).astype(F32)
        later = extended[ahead : ahead + CHUNK, :] * same
        sums[4 - ahead : 5 - ahead] += jnp.sum(conv * later, 0, keepdims=True)
        grad_conv = grad_conv + par[3 - ahead : 4 - ahead, :OWN] * later
    extended[CHUNK : CHUNK + 8, :] = extended[0:8, :]
    grad_x[...] = grad_conv.astype(BF16)


def run_backward(ends, proj, pre, mixed, grad_mixed, states, par):
    last = CHUNKS - 1
    chunked = lambda width, column=0: pl.BlockSpec((CHUNK, width), lambda i: (last - i, column))
    fixed = lambda shape: pl.BlockSpec(shape, lambda i: (0, 0))
    return pl.pallas_call(
        backward_kernel,
        grid=(CHUNKS,),
        in_specs=[
            pl.BlockSpec(memory_space=pltpu.SMEM),
            chunked(OWN, 1),
            chunked(N, 8),
            chunked(640),
            chunked(OWN),
            chunked(OWN),
            pl.BlockSpec((N, OWN), lambda i: (last - i, 0)),
            fixed((16, 640)),
        ],
        out_specs=[
            chunked(OWN),
            chunked(N),
            pl.BlockSpec((2 * N, CHUNK), lambda i: (0, last - i)),
            fixed((8, OWN)),
            fixed((8, N)),
        ],
        out_shape=[
            jax.ShapeDtypeStruct((PACK, OWN), BF16),
            jax.ShapeDtypeStruct((PACK, N), BF16),
            jax.ShapeDtypeStruct((2 * N, PACK), BF16),
            jax.ShapeDtypeStruct((8, OWN), F32),
            jax.ShapeDtypeStruct((8, N), F32),
        ],
        scratch_shapes=[
            pltpu.VMEM((N, OWN), F32),
            pltpu.VMEM((CHUNK + 8, OWN), F32),
            pltpu.VMEM((8, N), F32),
        ],
        compiler_params=pltpu.CompilerParams(
            dimension_semantics=("arbitrary",), vmem_limit_bytes=VMEM_LIMIT
        ),
        cost_estimate=COST,
        name="scan_backward",
    )(ends, proj, proj, pre, mixed, grad_mixed, states, par)


PARTS = (1, 1, 1, 1, 1, 2, 1, 1)
WHOLE = (1,) * N_REP


def piece_copies(pieces, parts, blocks, sems):
    copies = []
    taken = 0
    for slot, count in enumerate(parts):
        rows = ROWS // count
        copies.append(
            [
                pltpu.make_async_copy(
                    pieces[taken + k], blocks.at[slot, pl.ds(k * rows, rows)], sems.at[taken + k]
                )
                for k in range(count)
            ]
        )
        taken += count
    return copies


def fetch_block(pieces, parts, blocks, sems):
    copies = piece_copies(pieces, parts, blocks, sems)
    step = pl.program_id(0)

    @pl.when(step == 0)
    def _():
        for group in copies:
            for copy in group:
                copy.start()

    for slot, group in enumerate(copies):

        @pl.when(step == slot)
        def _(group=group):
            for copy in group:
                copy.wait()

    return blocks[step]


def project_kernel(parts, table, *refs):
    pieces = refs[: sum(parts)]
    gain, shards, normed_out, proj, dt_out, blocks, weight, sems = refs[sum(parts) :]
    block = fetch_block(pieces, parts, blocks, sems)

    @pl.when(pl.program_id(0) == 0)
    def _():
        for f in range(N_FSDP):
            weight[f * SHARD_IN : (f + 1) * SHARD_IN, :] = shards[(f // 2) % 4, f % 2, f // 8, :SHARD_IN]
        dt_out[...] = weight[:, 1024:]

    values = block.astype(F32)
    scale = lax.rsqrt(jnp.mean(values * values, axis=1, keepdims=True) + NORM_EPS)
    normed = (values * scale * gain[...]).astype(BF16)
    normed_out[...] = normed
    proj[...] = matmul(normed, weight[...])


def run_project(table, pieces, gain, shards):
    fixed = lambda shape: pl.BlockSpec(shape, lambda i, table: (0,) * len(shape))
    placed = lambda width: pl.BlockSpec((ROWS, width), lambda i, table: (table[i], 0))
    return pl.pallas_call(
        partial(project_kernel, PARTS),
        grid_spec=pltpu.PrefetchScalarGridSpec(
            num_scalar_prefetch=1,
            grid=(N_REP,),
            in_specs=[pl.BlockSpec(memory_space=pl.ANY)] * len(pieces) + [fixed((1, D)), fixed(shards.shape)],
            out_specs=[placed(D), placed(3 * WIDE), fixed((D, N))],
            scratch_shapes=[
                pltpu.VMEM((N_REP, ROWS, D), BF16),
                pltpu.VMEM((D, 3 * WIDE), BF16),
                pltpu.SemaphoreType.DMA((len(pieces),)),
            ],
        ),
        out_shape=[
            jax.ShapeDtypeStruct((PACK, D), BF16),
            jax.ShapeDtypeStruct((PACK, 3 * WIDE), F32),
            jax.ShapeDtypeStruct((D, N), BF16),
        ],
        compiler_params=pltpu.CompilerParams(
            dimension_semantics=("arbitrary",), vmem_limit_bytes=VMEM_LIMIT
        ),
        cost_estimate=COST,
        name="project",
    )(table, *pieces, gain, shards)


def row_sums(value):
    folded = value[:, :N] + value[:, N : 2 * N] + value[:, 2 * N :]
    return jnp.sum(folded.T, 0, keepdims=True)


def out_grad_kernel(table, *refs):
    pieces = refs[:N_REP]
    w_out, mixed, gate_in, gain, branch_out, grad_out, sums, blocks, turned, sems = refs[N_REP:]
    branch = fetch_block(pieces, WHOLE, blocks, sems)

    @pl.when(pl.program_id(0) == 0)
    def _():
        turned[...] = w_out[...].reshape(OWN, D).T

    branch_out[...] = branch
    total = matmul(branch, turned[...])
    grad_out[...] = total
    gate = gate_in[...]
    gated = mixed[...] * (gate * jax.nn.sigmoid(gate))
    row = lax.broadcasted_iota(jnp.int32, (8, ROWS), 0)
    sums[...] = jnp.where(
        row == 0, row_sums(gated * gated), jnp.where(row == 1, row_sums(total * gain[...] * gated), 0.0)
    )


def run_out_grad(table, pieces, w_out, mixed, proj, gain):
    fixed = lambda shape: pl.BlockSpec(shape, lambda i, table: (0, 0))
    placed = lambda width: pl.BlockSpec((ROWS, width), lambda i, table: (table[i], 0))
    own = pl.BlockSpec(
        (1, 2, 1, SHARD_OUT, D), lambda i, table: (table[N_REP] % 4, 0, table[N_REP] // 4, 0, 0)
    )
    return pl.pallas_call(
        out_grad_kernel,
        grid_spec=pltpu.PrefetchScalarGridSpec(
            num_scalar_prefetch=1,
            grid=(N_REP,),
            in_specs=[pl.BlockSpec(memory_space=pl.ANY)] * N_REP
            + [own, placed(OWN), placed(OWN), fixed((1, OWN))],
            out_specs=[placed(D), placed(OWN), pl.BlockSpec((8, ROWS), lambda i, table: (0, table[i]))],
            scratch_shapes=[
                pltpu.VMEM((N_REP, ROWS, D), BF16),
                pltpu.VMEM((D, WIDE), BF16),
                pltpu.SemaphoreType.DMA((N_REP,)),
            ],
        ),
        out_shape=[
            jax.ShapeDtypeStruct((PACK, D), BF16),
            jax.ShapeDtypeStruct((PACK, OWN), F32),
            jax.ShapeDtypeStruct((8, PACK), F32),
        ],
        compiler_params=pltpu.CompilerParams(
            dimension_semantics=("arbitrary",), vmem_limit_bytes=VMEM_LIMIT
        ),
        cost_estimate=COST,
        name="out_grad",
    )(table, *pieces, w_out, mixed, proj, gain)


def gate_kernel(
    where, grad_out, mixed_in, gate_in, sums, gain, grad_branch, normed,
    low_out, grad_mixed, keep, give, grad_gain, total,
):
    step = pl.program_id(0)
    rows = grad_out.shape[0]
    mixed, gate, grad_o = mixed_in[...], gate_in[...], grad_out[...]
    stats = jnp.concatenate([sums[...], jnp.zeros((N - 8, rows), F32)], 0).T
    out_scale = lax.rsqrt(stats[:, 0:1] * (1.0 / DI) + NORM_EPS)
    pull = out_scale * out_scale * out_scale * (stats[:, 1:2] * (1.0 / DI))
    gate_sig = jax.nn.sigmoid(gate)
    silu = gate * gate_sig
    gated = mixed * silu
    unit = gated * out_scale
    low = (unit * gain[...]).astype(BF16)
    grad_gated = out_scale * (grad_o * gain[...]) - gated * pull
    grad_mixed[...] = grad_gated * silu
    grad_z = (grad_gated * mixed * (gate_sig * (1.0 + gate * (1.0 - gate_sig)))).astype(BF16)
    low_out[:, :OWN] = low
    low_out[:, OWN:] = grad_z

    @pl.when(step == 0)
    def _():
        grad_gain[...] = jnp.zeros_like(grad_gain)
        total[...] = jnp.zeros_like(total)

    grad_gain[0:1] += jnp.sum(grad_o * unit, 0, keepdims=True)
    for k in range(4):
        part = product(low, grad_branch[:, k * WIDE : (k + 1) * WIDE], 0, 0)
        for m in range(4):
            total[4 * k + m, :SHARD_IN] += part[m * SHARD_IN : (m + 1) * SHARD_IN]
    part = product(normed[...], grad_z, 0, 0)
    for f in range(N_FSDP):
        total[f, SHARD_IN:] += part[f * SHARD_IN : (f + 1) * SHARD_IN]

    @pl.when(step == pl.num_programs(0) - 1)
    def _():
        for k in range(N_FSDP // 2):
            keep[k] = total[2 * k + where[0]]
            give[k] = total[2 * k + 1 - where[0]]


def run_gate(where, grad_out, mixed, proj, sums, gain, grad_branch, normed):
    count = 2 * ROWS
    rows = lambda width: pl.BlockSpec((count, width), lambda i: (i, 0))
    fixed = lambda shape: pl.BlockSpec(shape, lambda i: (0,) * len(shape))
    half = (N_FSDP // 2, 2 * SHARD_IN, WIDE)
    return pl.pallas_call(
        gate_kernel,
        grid=(PACK // count,),
        in_specs=[
            pl.BlockSpec(memory_space=pltpu.SMEM),
            rows(OWN),
            rows(OWN),
            rows(OWN),
            pl.BlockSpec((8, count), lambda i: (0, i)),
            fixed((1, OWN)),
            rows(D),
            rows(D),
        ],
        out_specs=[rows(2 * OWN), rows(OWN), fixed(half), fixed(half), fixed((8, OWN))],
        out_shape=[
            jax.ShapeDtypeStruct((PACK, 2 * OWN), BF16),
            jax.ShapeDtypeStruct((PACK, OWN), F32),
            jax.ShapeDtypeStruct(half, F32),
            jax.ShapeDtypeStruct(half, F32),
            jax.ShapeDtypeStruct((8, OWN), F32),
        ],
        scratch_shapes=[pltpu.VMEM((N_FSDP, 2 * SHARD_IN, WIDE), F32)],
        compiler_params=pltpu.CompilerParams(
            dimension_semantics=("arbitrary",), vmem_limit_bytes=VMEM_LIMIT
        ),
        cost_estimate=COST,
        name="gate_backward",
    )(where, grad_out, mixed, proj, sums, gain, grad_branch, normed)


def block_out_kernel(rows, weight, tokens, live, out):
    step = pl.program_id(0)
    part = matmul(jnp.concatenate([rows[0], rows[1]], 1), weight[...].reshape(2 * OWN, D))

    @pl.when(step == 0)
    def _():
        out[...] = part

    @pl.when(step > 0)
    def _():
        out[...] += part

    @pl.when(step == N_REP // 2 - 1)
    def _():
        out[...] = tokens[...].astype(F32) + live[...] * out[...]


def run_block_out(rows, weight, tokens, live):
    fixed = lambda shape: pl.BlockSpec(shape, lambda i: (0, 0))
    return pl.pallas_call(
        block_out_kernel,
        grid=(N_REP // 2,),
        in_specs=[
            pl.BlockSpec((2, ROWS, OWN), lambda i: (i, 0, 0)),
            pl.BlockSpec((2, 2, 1, SHARD_OUT, D), lambda i: (i % 2, 0, i // 2, 0, 0)),
            fixed((ROWS, D)),
            fixed((ROWS, 1)),
        ],
        out_specs=fixed((ROWS, D)),
        out_shape=jax.ShapeDtypeStruct((ROWS, D), F32),
        compiler_params=pltpu.CompilerParams(
            dimension_semantics=("arbitrary",), vmem_limit_bytes=VMEM_LIMIT
        ),
        cost_estimate=FILL,
        name="block_out",
    )(rows, weight, tokens, live)


def turned_part(weight, rows):
    return product(weight[...].reshape(D, weight.shape[-1]), rows, 1, 1)


def columns_of(full_in, width, index):
    return pl.BlockSpec(full_in.shape[:-1] + (width,), lambda i: (0, 0, 0, 0, index(i)))


def z_grad_kernel(rows, weight, out):
    part = turned_part(weight, jnp.concatenate([rows[0], rows[1]], 1))

    @pl.when(pl.program_id(0) == 0)
    def _():
        out[...] = part

    @pl.when(pl.program_id(0) > 0)
    def _():
        out[...] += part


def run_z_grad(rows, full_in):
    return pl.pallas_call(
        z_grad_kernel,
        grid=(N_REP // 2,),
        in_specs=[
            pl.BlockSpec((2, ROWS, OWN), lambda i: (i, 0, 1)),
            columns_of(full_in, 2 * OWN, lambda i: i),
        ],
        out_specs=pl.BlockSpec((D, ROWS), lambda i: (0, 0)),
        out_shape=jax.ShapeDtypeStruct((D, ROWS), F32),
        compiler_params=pltpu.CompilerParams(
            dimension_semantics=("arbitrary",), vmem_limit_bytes=VMEM_LIMIT
        ),
        cost_estimate=FILL,
        name="z_grad",
    )(rows, full_in)


def input_grad_kernel(
    grad_z, x_rows, rest_rows, w_x, w_bc, low_dt, tokens, cotangent, gain, out, gain_out, total, ordered
):
    step = pl.program_id(0)
    part = turned_part(w_x, jnp.concatenate([x_rows[0], x_rows[1]], 1))

    @pl.when(step == 0)
    def _():
        total[...] = grad_z[...] + part

    @pl.when(step > 0)
    def _():
        total[...] += part

    @pl.when(step == N_REP // 2 - 1)
    def _():
        lane = lax.broadcasted_iota(jnp.int32, (ROWS, N), 1)
        groups = []
        for k in range(2):
            group = jnp.zeros((ROWS, N), F32)
            for m in range(4):
                value = rest_rows[4 * k + m].astype(F32)
                value = value if m == 0 else pltpu.roll(value, m * OWN_BC, 1)
                group = jnp.where((lane >= m * OWN_BC) & (lane < (m + 1) * OWN_BC), value, group)
            groups.append(group.astype(BF16))
        steps = jnp.zeros((ROWS, N), F32)
        for m in range(N_REP):
            start = 8 + m * OWN_H
            value = pltpu.roll(rest_rows[m].astype(F32), (start - OWN_BC) % N, 1)
            steps = jnp.where((lane >= start) & (lane < start + OWN_H), value, steps)
        shared = total[...] + turned_part(w_bc, jnp.concatenate(groups, 1))
        for f in range(N_FSDP):
            start = eight_order(f) * SHARD_IN
            ordered[f * SHARD_IN : (f + 1) * SHARD_IN, :] = shared[start : start + SHARD_IN, :]
        grad_h = (ordered[...] + product(low_dt[...], steps.astype(BF16), 1, 1)).T
        values = tokens[...].astype(F32)
        scale = lax.rsqrt(jnp.mean(values * values, axis=1, keepdims=True) + NORM_EPS)
        unit = values * scale
        gain_sum = jnp.sum(grad_h * unit, 0, keepdims=True)
        gain_out[...] = jnp.zeros_like(gain_out)
        for k in range(D // N):
            gain_out[k : k + 1, :] = gain_sum[:, k * N : (k + 1) * N]
        grad_unit = grad_h * gain[...]
        inner = jnp.mean(grad_unit * unit, axis=1, keepdims=True)
        out[...] = cotangent[...].astype(F32) + scale * (grad_unit - unit * inner)


def run_input_grad(grad_z, tail_rows, full_in, low_dt, tokens, cotangent, gain):
    fixed = lambda shape: pl.BlockSpec(shape, lambda i: (0,) * len(shape))
    return pl.pallas_call(
        input_grad_kernel,
        grid=(N_REP // 2,),
        in_specs=[
            fixed((D, ROWS)),
            pl.BlockSpec((2, ROWS, OWN), lambda i: (i, 0, 0)),
            pl.BlockSpec((N_REP, ROWS, N), lambda i: (0, 0, OWN // N)),
            columns_of(full_in, 2 * OWN, lambda i: N_REP // 2 + i),
            columns_of(full_in, 2 * N, lambda i: DI // N),
            fixed((D, N)),
            fixed((ROWS, D)),
            fixed((ROWS, D)),
            fixed((1, D)),
        ],
        out_specs=[fixed((ROWS, D)), fixed((16, N))],
        out_shape=[jax.ShapeDtypeStruct((ROWS, D), F32), jax.ShapeDtypeStruct((16, N), F32)],
        scratch_shapes=[pltpu.VMEM((D, ROWS), F32), pltpu.VMEM((D, ROWS), F32)],
        compiler_params=pltpu.CompilerParams(
            dimension_semantics=("arbitrary",), vmem_limit_bytes=VMEM_LIMIT
        ),
        cost_estimate=COST,
        name="input_grad",
    )(grad_z, tail_rows, tail_rows, full_in, full_in, low_dt, tokens, cotangent, gain)


def rest_kernel(
    ends, parts, pre_b, pre_c, conv_in, par, grad_x, grad_dt, sums, head_acc, grad_gain, first, tail_out, small_out
):
    own = lax.broadcasted_iota(jnp.int32, (OWN_BC, 2 * N), 0) + first[0]
    chosen = (lax.broadcasted_iota(jnp.int32, (OWN_BC, 2 * N), 1) == own).astype(F32).astype(BF16)

    def pick(value):
        return product(jnp.concatenate([chosen] * 3, 1), jnp.concatenate(split_three(value), 1), 1, 1)

    grad = parts[0].astype(F32)
    for k in range(1, N_REP):
        grad = grad + parts[k].astype(F32)
    own_pre = pick(jnp.concatenate([pre_b[...], pre_c[...]], 1))
    own_conv = product(chosen, conv_in[...].astype(BF16), 1, 1)
    taps = pick(par[:, OWN:])
    sig = jax.nn.sigmoid(own_pre)
    grad_pre = grad * (sig * (1.0 + own_pre * (1.0 - sig)))
    position = lax.broadcasted_iota(jnp.int32, (1, PACK), 1)

    def segment(places):
        counted = jnp.zeros_like(places)
        for k in range(3):
            counted = counted + (places >= ends[k]).astype(jnp.int32)
        return counted

    grad_conv = taps[:, CONV - 1 : CONV] * grad_pre
    column = lax.broadcasted_iota(jnp.int32, (OWN_BC, N), 1)
    found = jnp.where(column == CONV, jnp.sum(grad_pre, 1, keepdims=True), 0.0)
    found = jnp.where(column == CONV - 1, jnp.sum(own_conv * grad_pre, 1, keepdims=True), found)
    for later_by in range(1, CONV):
        same = (segment(position + later_by) == segment(position)) & (position < PACK - later_by)
        later = jnp.where(same, pltpu.roll(grad_pre, PACK - later_by, 1), 0.0)
        tap = CONV - 1 - later_by
        found = jnp.where(column == tap, jnp.sum(own_conv * later, 1, keepdims=True), found)
        grad_conv = grad_conv + taps[:, tap : tap + 1] * later
    lane = lax.broadcasted_iota(jnp.int32, (N, N), 1)
    filler = jnp.zeros((N - OWN_BC, N), F32)
    for k in range(PACK // N):
        rows = slice(k * N, (k + 1) * N)
        columns = jnp.concatenate([grad_conv[:, rows], filler], 0).T
        steps = pltpu.roll(grad_dt[rows, :].astype(F32), OWN_BC, 1)
        tail_out[rows, :OWN] = grad_x[rows, :]
        tail_out[rows, OWN:] = jnp.where(
            lane < OWN_BC, columns, jnp.where(lane < OWN_BC + OWN_H, steps, 0.0)
        ).astype(BF16)
    row = lax.broadcasted_iota(jnp.int32, (8, OWN), 0)
    skip = head_sums(sums[...])
    by_head = jnp.concatenate([skip, jnp.zeros((8, OWN - N), F32)], 1)
    logs = jnp.concatenate([head_acc[...], jnp.zeros((8, OWN - N), F32)], 1)
    wide = jnp.where(row == 0, grad_gain[0:1, :], jnp.where(row < 6, sums[...], 0.0))
    wide = jnp.where(row == 6, logs[1:2, :], jnp.where(row == 7, by_head[6:7, :], wide))
    turned = jnp.concatenate([found, filler], 0).T
    first_row = lax.broadcasted_iota(jnp.int32, (8, N), 0) == 0
    small_out[:, :OWN] = wide
    small_out[:, OWN:] = jnp.where(first_row, head_acc[0:1, :], pltpu.roll(turned[:8], 1, 0))


def run_rest(ends, parts, pre, proj, par, grad_x, grad_dt, sums, head_acc, grad_gain, first):
    fixed = lambda shape: pl.BlockSpec(shape, lambda i: (0,) * len(shape))
    return pl.pallas_call(
        rest_kernel,
        grid=(1,),
        in_specs=[
            pl.BlockSpec(memory_space=pltpu.SMEM),
            fixed((N_REP, OWN_BC, PACK)),
            pl.BlockSpec((PACK, N), lambda i: (0, 3)),
            pl.BlockSpec((PACK, N), lambda i: (0, 4)),
            pl.BlockSpec((PACK, 2 * N), lambda i: (0, 3)),
            fixed((16, 640)),
            fixed((PACK, OWN)),
            fixed((PACK, N)),
            fixed((8, OWN)),
            fixed((8, N)),
            fixed((8, OWN)),
            pl.BlockSpec(memory_space=pltpu.SMEM),
        ],
        out_specs=[fixed((PACK, TAIL)), fixed((8, TAIL))],
        out_shape=[jax.ShapeDtypeStruct((PACK, TAIL), BF16), jax.ShapeDtypeStruct((8, TAIL), F32)],
        compiler_params=pltpu.CompilerParams(
            dimension_semantics=("arbitrary",), vmem_limit_bytes=VMEM_LIMIT
        ),
        cost_estimate=COST,
        name="rest_backward",
    )(ends, parts, pre, pre, proj, par, grad_x, grad_dt, sums, head_acc, grad_gain, first)


def tail_grad_kernel(normed, tail, small, out):
    step = pl.program_id(0)
    part = product(normed[...], tail[...], 0, 0)
    for f in range(N_FSDP):
        rows = part[f * SHARD_IN : (f + 1) * SHARD_IN]

        @pl.when(step == 0)
        def _(f=f, rows=rows):
            out[eight_order(f), :SHARD_IN] = rows
            out[eight_order(f), SHARD_IN:] = small[...]

        @pl.when(step > 0)
        def _(f=f, rows=rows):
            out[eight_order(f), :SHARD_IN] += rows


def run_tail_grad(normed, tail, small):
    count = 2 * ROWS
    shape = (N_FSDP, SHARD_IN + 8, TAIL)
    return pl.pallas_call(
        tail_grad_kernel,
        grid=(PACK // count,),
        in_specs=[
            pl.BlockSpec((count, D), lambda i: (i, 0)),
            pl.BlockSpec((count, TAIL), lambda i: (i, 0)),
            pl.BlockSpec((8, TAIL), lambda i: (0, 0)),
        ],
        out_specs=pl.BlockSpec(shape, lambda i: (0, 0, 0)),
        out_shape=jax.ShapeDtypeStruct(shape, F32),
        compiler_params=pltpu.CompilerParams(
            dimension_semantics=("arbitrary",), vmem_limit_bytes=VMEM_LIMIT
        ),
        cost_estimate=COST,
        name="tail_grad",
    )(normed, tail, small)


def adam_step(grad, weight, first, second, grad_out, first_out, second_out, weight_out):
    new_weight, new_first, new_second = adam_update(
        weight[...], grad, first[...], second[...], RATE_MATRIX, WEIGHT_DECAY
    )
    grad_out[...] = grad
    first_out[...] = new_first
    second_out[...] = new_second
    weight_out[...] = new_weight


def load_pair(step, pairs, rows, grad):
    pair, right, far_first, far_second, left = pairs
    for slot, (low, high) in enumerate(
        (((pair, 0), (pair, 1)), ((right, 0), (right, 1)), ((far_first, 0), (far_second, 0)), ((left, 0), (left, 1)))
    ):

        @pl.when(step == slot)
        def _(low=low, high=high):
            grad[:, :WIDE] = low[0][low[1], rows, :]
            grad[:, WIDE:] = high[0][high[1], rows, :]


def adam_pairs_kernel(rows, table, *refs):
    pairs, arrays, grad = refs[:5], refs[5:8] + refs[-5:-1], refs[-1]
    load_pair(pl.program_id(0), pairs, rows, grad)
    adam_step(grad[...], *arrays)


def run_adam_pairs(table, place_of, rows, pairs, weight, first, second):
    part = pl.BlockSpec((SHARD_IN, 2 * WIDE), lambda i, table: place_of(table[i]))
    shape = jax.ShapeDtypeStruct(weight.shape, F32)
    return pl.pallas_call(
        partial(adam_pairs_kernel, rows),
        grid_spec=pltpu.PrefetchScalarGridSpec(
            num_scalar_prefetch=1,
            grid=(4,),
            in_specs=[pl.BlockSpec(pair.shape, lambda i, table: (0, 0, 0)) for pair in pairs]
            + [part] * 3,
            out_specs=[part] * 4,
            scratch_shapes=[pltpu.VMEM((SHARD_IN, 2 * WIDE), F32)],
        ),
        out_shape=[shape] * 4,
        compiler_params=pltpu.CompilerParams(
            dimension_semantics=("arbitrary",), vmem_limit_bytes=VMEM_LIMIT
        ),
        cost_estimate=FILL,
        name="adam",
    )(table, *pairs, weight, first, second)


def adam_tail_kernel(pair, rest, *refs):
    arrays, grad = refs[:3] + refs[-5:-1], refs[-1]
    step = pl.program_id(0)

    @pl.when(step < N_REP // 2)
    def _():
        grad[:, :WIDE] = pair[0, :SHARD_IN]
        grad[:, WIDE:] = pair[1, :SHARD_IN]

    @pl.when(step == N_REP // 2)
    def _():
        lane = lax.broadcasted_iota(jnp.int32, (SHARD_IN, N), 1)
        for k in range(2):
            group = jnp.zeros((SHARD_IN, N), F32)
            for m in range(4):
                value = rest[4 * k + m, :SHARD_IN]
                value = value if m == 0 else pltpu.roll(value, m * OWN_BC, 1)
                group = jnp.where((lane >= m * OWN_BC) & (lane < (m + 1) * OWN_BC), value, group)
            grad[:, k * N : (k + 1) * N] = group

    adam_step(grad[...], *arrays)


def run_adam_tail(parts, weight, first, second, before):
    half = N_REP // 2
    rows = parts.shape[1]
    column = pl.BlockSpec((SHARD_IN, 2 * WIDE), lambda i: (0, half + i))
    shape = jax.ShapeDtypeStruct(weight.shape, F32)
    return pl.pallas_call(
        adam_tail_kernel,
        grid=(half + 1,),
        in_specs=[
            pl.BlockSpec((2, rows, OWN), lambda i: (jnp.minimum(i, half - 1), 0, 0)),
            pl.BlockSpec((N_REP, rows, N), lambda i: (0, 0, OWN // N)),
        ]
        + [column] * 3
        + [pl.BlockSpec(memory_space=pl.ANY)] * 4,
        out_specs=[column] * 4,
        out_shape=[shape] * 4,
        input_output_aliases={5 + k: k for k in range(4)},
        scratch_shapes=[pltpu.VMEM((SHARD_IN, 2 * WIDE), F32)],
        compiler_params=pltpu.CompilerParams(
            dimension_semantics=("arbitrary",), vmem_limit_bytes=VMEM_LIMIT
        ),
        cost_estimate=COST,
        name="adam_tail",
    )(parts, parts, weight, first, second, *before)


def body(
    tokens,
    cotangent,
    lengths,
    w_in,
    w_dt,
    w_out,
    small,
    first_in,
    first_dt,
    first_out,
    first_small,
    second_in,
    second_dt,
    second_out,
    second_small,
):
    place = Place()
    r = place.r
    zero = jnp.int32(0)
    pack_lengths = lax.dynamic_slice_in_dim(lengths, place.f, 1, 0)[0]
    seg_ends = jnp.cumsum(pack_lengths)
    own_positions = r * ROWS + jnp.arange(ROWS, dtype=jnp.int32)
    own_live = (segment_at(own_positions, seg_ends) < 3).astype(F32)[:, None]
    slots = jnp.arange(N_REP, dtype=jnp.int32)
    ahead = ((place.x + slots // 2) % 4) * 2 + (place.yl + slots) % 2
    half = ROWS // 2

    in_low = w_in.astype(BF16)
    dt_low = w_dt.astype(BF16)
    out_low = w_out.astype(BF16)

    small_rows = jnp.pad(small.astype(BF16), (0, 16 * 3 * WIDE - SHARD_SMALL)).reshape(16, 3 * WIDE)

    def own_columns(rep):
        columns = jnp.concatenate(
            [
                lax.dynamic_slice_in_dim(in_low, rep * OWN, OWN, 1),
                lax.dynamic_slice_in_dim(in_low, DI + rep * OWN, OWN, 1),
                in_low[:, 2 * DI :],
                lax.dynamic_slice_in_dim(dt_low, rep * OWN_H, OWN_H, 1),
                jnp.zeros((SHARD_IN, 2), BF16),
                dt_low,
                jnp.zeros((SHARD_IN, N - 8 - H), BF16),
            ],
            1,
        )
        return jnp.concatenate([columns, small_rows], 0)

    other_columns = move(
        own_columns(2 * place.x + 1 - place.yl), lambda yh, z, c, x, yl: (yh + 1, z, c, x, yl + 1)
    )
    from_left = move(tokens, along_x(1))
    from_right = move(tokens, along_x(-1))
    partner = move(tokens, swap_y)

    out_low, other_columns = lax.optimization_barrier((out_low, other_columns))
    out_other = move(out_low, lambda yh, z, c, x, yl: (yh + 1, z, c, x, yl + 1))
    from_left, from_right, partner, other_columns = lax.optimization_barrier(
        (from_left, from_right, partner, other_columns)
    )
    own_shards = gather_eight(both(own_columns(r), other_columns, place.yh))
    far = move(from_left, along_x(1))
    partner_left = move(from_left, swap_y)
    partner_right = move(partner, along_x(-1))

    far, partner_left, partner_right, out_other = lax.optimization_barrier(
        (far, partner_left, partner_right, out_other)
    )
    out_pair = both(out_low, out_other, place.yh)
    partner_far_top = move(partner_left[:half], along_x(1))
    partner_far_low = move(partner_right[half:], along_x(-1))

    vector = own_shards[:, :, :, SHARD_IN : SHARD_IN + 2].transpose(2, 0, 1, 3, 4)
    vector = vector.reshape(N_FSDP, 6 * WIDE)[:, :SHARD_SMALL].reshape(-1).astype(F32)
    offset = 0
    gain_in = vector[None, :D]
    offset = D
    gain_row = lax.dynamic_slice_in_dim(vector, offset + r * OWN, OWN, 0)[None, :]
    offset += DI
    taps = vector[offset : offset + (CONV + 1) * CHANNELS].reshape(CONV + 1, CHANNELS)
    offset += (CONV + 1) * CHANNELS
    per_head = vector[offset:].reshape(3, H)
    dt_bias, a_log, d_skip = lax.dynamic_slice_in_dim(per_head, r * OWN_H, OWN_H, 1)
    taps_bc = taps[:, DI:]
    conv_par = jnp.concatenate([lax.dynamic_slice_in_dim(taps, r * OWN, OWN, 1), taps_bc], 1)
    head_par = jnp.stack(
        [
            jnp.pad(jnp.broadcast_to(d_skip[:, None], (OWN_H, P_SIZE)).reshape(-1), (0, 2 * N)),
            jnp.pad(dt_bias, (0, 640 - OWN_H)),
            jnp.pad(-jnp.exp(a_log), (0, 640 - OWN_H)),
        ],
        0,
    )
    par = jnp.concatenate([conv_par, head_par, jnp.zeros((8, 640), F32)], 0)

    branch = (cotangent.astype(F32) * own_live).astype(BF16)
    branch, in_low, partner_far_top, partner_far_low, own_shards = lax.optimization_barrier(
        (branch, in_low, partner_far_top, partner_far_low, own_shards)
    )
    full_out = gather_eight(tie(out_pair, own_shards))
    in_other = move(in_low, lambda yh, z, c, x, yl: (yh + 1, z, c, x, yl + 1))
    b_left = move(branch, along_x(1))
    b_right = move(branch, along_x(-1))
    b_partner = move(branch, swap_y)
    token_pieces = [
        tokens, partner, from_right, partner_right, far,
        partner_far_top, partner_far_low, from_left, partner_left,
    ]
    normed, proj, low_dt = run_project(ahead, token_pieces, gain_in, own_shards)
    b_left, b_right, b_partner, proj = lax.optimization_barrier((b_left, b_right, b_partner, proj))
    b_far = move(b_left, along_x(1))
    b_partner_left = move(b_left, swap_y)
    b_partner_right = move(b_partner, along_x(-1))
    before = run_forward(0, seg_ends, proj, par)
    b_far, b_partner_left, b_partner_right, before = lax.optimization_barrier(
        (b_far, b_partner_left, b_partner_right, before)
    )
    b_partner_far = move(b_partner_left, along_x(1))
    pre, mixed, states, _ = run_forward(1, seg_ends, proj, par, before)
    mixed, in_low, in_other, b_partner_far = lax.optimization_barrier((mixed, in_low, in_other, b_partner_far))
    full_in = gather_eight(both(in_low, in_other, place.yh))
    branch_pieces = [branch, b_partner, b_right, b_partner_right, b_far, b_partner_far, b_left, b_partner_left]
    rep_table = jnp.concatenate([ahead, r[None]])
    grad_branch, grad_normed_out, sums = run_out_grad(rep_table, branch_pieces, full_out, mixed, proj, gain_row)
    sums = sum_rep(sums[:2].reshape(32, 128)).reshape(2, PACK)
    sums = jnp.concatenate([sums, jnp.zeros((6, PACK), F32)], 0)

    low_rows, grad_mixed, keep, give, grad_gain = run_gate(
        place.c[None], grad_normed_out, mixed, proj, sums, gain_row, grad_branch, normed
    )

    low_rows = exchange(low_rows.reshape(N_REP, ROWS, 2 * OWN), "rep")
    got = move(give, swap_core)
    grad_x, grad_dtraw, grad_bc, grad_sums, grad_heads = run_backward(
        seg_ends, proj, pre, mixed, grad_mixed, states, par
    )
    low_rows, got, grad_bc, grad_x = lax.optimization_barrier((low_rows, got, grad_bc, grad_x))

    grad_bc = exchange(grad_bc, "rep").reshape(N_REP, OWN_BC, PACK)
    split = (2, 4, 2 * SHARD_IN, WIDE)
    early, early_found = start_ring(keep.reshape(split), got.reshape(split), None, place)
    grad_rows = run_z_grad(low_rows, full_in)
    block_out = run_block_out(low_rows, full_out, tokens, own_live)
    grad_bc, grad_rows, block_out = lax.optimization_barrier((grad_bc, grad_rows, block_out))

    tail, small_own = run_rest(
        seg_ends, grad_bc, pre, proj, par, grad_x, grad_dtraw, grad_sums, grad_heads, grad_gain, (r * OWN_BC)[None]
    )
    tail, small_own, early_found = lax.optimization_barrier((tail, small_own, early_found))
    early, _ = end_ring(early, early_found, None)
    early, early_half = start_half(early, None, place)
    grad_tail = run_tail_grad(normed, tail, small_own)
    tail, grad_tail, early_half = lax.optimization_barrier((tail, grad_tail, early_half))
    tail_rows = exchange(tail.reshape(N_REP, ROWS, TAIL), "rep")
    tail_part = scatter_eight(grad_tail)
    early, _ = end_half(early, early_half, None)
    out_part = move(
        early[:SHARD_IN],
        lambda yh, z, c, x, yl: (x // 2, (x % 2) * 2 + yl, z % 2, 2 * c + yh, z // 2),
    )
    tail_rows, tail_part = lax.optimization_barrier((tail_rows, tail_part))

    tail_part, tail_half = start_half(tail_part, None, place)
    input_grad, grad_gain_in = run_input_grad(
        grad_rows, tail_rows, full_in, low_dt, tokens, cotangent, gain_in
    )
    early = jnp.concatenate([out_part, early[SHARD_IN:]], 0)
    tail_half, early, input_grad, grad_gain_in = lax.optimization_barrier(
        (tail_half, early, input_grad, grad_gain_in)
    )

    tail_part, _ = end_half(tail_part, tail_half, None)
    tail_parts = share_rep(tail_part)
    grad_gain_in = sum_all(grad_gain_in)
    early_pair = both(early, move(early, swap_y), place.yl)
    early_left, early_right = move(early_pair, along_x(1)), move(early_pair, along_x(-1))
    early_far = move(early_left[:1], along_x(1)), move(early_right[1:], along_x(-1))
    early_pairs = (early_pair, early_right, *early_far, early_left)

    x_order = (place.x + jnp.arange(4, dtype=jnp.int32)) % 4
    grad_out, new_first_out, new_second_out, new_out = run_adam_pairs(
        x_order, lambda k: (k // 2, k % 2), slice(0, SHARD_IN), early_pairs, w_out, first_out, second_out
    )
    updated = run_adam_pairs(
        x_order, lambda k: (0, k), slice(SHARD_IN, 2 * SHARD_IN), early_pairs, w_in, first_in, second_in
    )
    grad_in, new_first_in, new_second_in, new_in = run_adam_tail(tail_parts, w_in, first_in, second_in, updated)

    def columns(parts):
        return parts.transpose(1, 0, 2).reshape(parts.shape[1], -1)

    grad_gain_in = grad_gain_in[: D // N].reshape(-1)
    small_parts = tail_parts[:, SHARD_IN:]
    small_x = small_parts[:, :, :OWN].transpose(1, 0, 2).reshape(8, DI)
    small_bc = small_parts[:, :, OWN:].transpose(1, 0, 2)

    def channels(row):
        return jnp.concatenate([small_x[row], small_bc[row, :, :OWN_BC].reshape(-1)])

    grad_small_all = jnp.concatenate(
        [grad_gain_in, small_x[0]]
        + [channels(row) for row in range(1, 6)]
        + [
            small_bc[0, :, :OWN_H].reshape(-1),
            small_parts[:, 6, :OWN_H].reshape(-1),
            small_parts[:, 7, :OWN_H].reshape(-1),
        ]
    )
    grad_small = lax.dynamic_slice_in_dim(grad_small_all, place.f * SHARD_SMALL, SHARD_SMALL, 0)
    grad_dt = columns(tail_parts[:, :SHARD_IN, OWN + OWN_BC : OWN + OWN_BC + OWN_H])
    new_dt, new_first_dt, new_second_dt = adam_update(
        w_dt, grad_dt, first_dt, second_dt, RATE_MATRIX, WEIGHT_DECAY
    )
    new_small, new_first_small, new_second_small = adam_update(
        small, grad_small, first_small, second_small, RATE_SMALL, 0.0
    )
    return (
        block_out,
        input_grad,
        grad_in,
        grad_dt,
        grad_out,
        grad_small,
        new_first_in,
        new_first_dt,
        new_first_out,
        new_first_small,
        new_second_in,
        new_second_dt,
        new_second_out,
        new_second_small,
        new_in,
        new_dt,
        new_out,
        new_small,
    )


def solution(mesh):
    rows = P(("fsdp", "rep"), None)
    matrix = P("fsdp", None)
    vector = P("fsdp")
    group = (matrix, matrix, matrix, vector)
    return jax.shard_map(
        body,
        mesh=mesh,
        in_specs=(rows, rows, P()) + group * 3,
        out_specs=(rows, rows) + group * 4,
        check_vma=False,
    )
```

```python
from functools import partial

import jax
import jax.numpy as jnp
from jax import lax
from jax.experimental import pallas as pl
from jax.experimental.pallas import tpu as pltpu
from jax.sharding import PartitionSpec as P

D = 1536
H = 48
P_SIZE = 64
N = 128
CONV = 4
STEP = 10
DI = 3072
CHANNELS = DI + 2 * N
SMALL = 21392
N_FSDP = 16
N_REP = 8
ROWS = 256
PACK = 2048
OWN = DI // N_REP
OWN_H = H // N_REP
OWN_BC = 2 * N // N_REP
SHARD_IN = D // N_FSDP
SHARD_OUT = DI // N_FSDP
SHARD_SMALL = SMALL // N_FSDP
WIDE = 384
CHUNK = 128
CHUNKS = PACK // CHUNK
HALF = CHUNKS // 2
TAIL = 512
VMEM_LIMIT = 60 * 1024 * 1024

NORM_EPS = 1e-05
BETA_ONE = 0.9
BETA_TWO = 0.999
ADAM_EPS = 1e-08
WEIGHT_DECAY = 0.1
RATE_MATRIX = 0.04
RATE_SMALL = 0.4
PRECISE = lax.Precision.HIGHEST
BF16 = jnp.bfloat16
F32 = jnp.float32
COST = pl.CostEstimate(flops=1_000_000, bytes_accessed=100_000, transcendentals=0)
FILL = pl.CostEstimate(flops=2_400_000_000, bytes_accessed=20_000_000, transcendentals=0)


def move(value, target):
    pairs = []
    for f in range(N_FSDP):
        for r in range(N_REP):
            yh, z, c, x, yl = target(f // 8, (f // 2) % 4, f % 2, r // 2, r % 2)
            pairs.append((f * N_REP + r, ((yh % 2) * 8 + (z % 4) * 2 + c % 2) * N_REP + (x % 4) * 2 + yl % 2))
    return lax.ppermute(value, ("fsdp", "rep"), pairs)


def along_x(steps):
    return lambda yh, z, c, x, yl: (yh, z, c, x + steps, yl)


def along_z(steps):
    return lambda yh, z, c, x, yl: (yh, z + steps, c, x, yl)


def swap_y(yh, z, c, x, yl):
    return (yh, z, c, x, yl + 1)


def swap_y_hi(yh, z, c, x, yl):
    return (yh + 1, z, c, x, yl)


def swap_core(yh, z, c, x, yl):
    return (yh, z, c + 1, x, yl)


class Place:
    def __init__(self):
        f = lax.axis_index("fsdp")
        r = lax.axis_index("rep")
        self.f, self.r = f, r
        self.yh, self.z, self.c = f // 8, (f // 2) % 4, f % 2
        self.x, self.yl = r // 2, r % 2


def at(value, index, axis=0):
    return lax.dynamic_index_in_dim(value, index, axis, keepdims=False)


def tie(values, *others):
    return lax.optimization_barrier((values, others))[0]


def both(mine, other, second):
    first = jnp.where(second == 0, mine, other)
    last = jnp.where(second == 0, other, mine)
    return jnp.stack([first, last], 0)


def put(out, piece, axis, index):
    starts = [jnp.int32(0)] * out.ndim
    starts[axis] = jnp.int32(index)
    return lax.dynamic_update_slice(out, jnp.expand_dims(piece, axis), tuple(starts))


def swap_shards(value, place):
    other = move(value, lambda yh, z, c, x, yl: (yh + 1, z, c, x, yl + 1))
    return both(value, other, place.yh)


def gather_eight(pair):
    groups = [list(range(8)), list(range(8, 16))]
    out = lax.all_gather(pair, "fsdp", axis=0, tiled=True, axis_index_groups=groups)
    return out.reshape((4, 2) + pair.shape)


def start_half(total, extra, place):
    return at(total, place.yh), move(with_rows(at(total, 1 - place.yh), extra), swap_y_hi)


def end_half(mine, other, extra):
    rows = mine.shape[0]
    return mine + other[:rows], None if extra is None else extra + other[rows:]


def exchange(value, axis):
    return lax.all_to_all(value, axis, 0, 0, tiled=True)


def share_rep(value):
    return exchange(jnp.broadcast_to(value[None], (N_REP,) + value.shape), "rep")


def sum_rep(value):
    value = value + move(value, swap_y)
    steps = [move(value, along_x(step)) for step in (1, 3, 2)]
    return value + steps[0] + steps[1] + steps[2]


def sum_most(value):
    steps = [move(value, along_z(step)) for step in (1, 3, 2)]
    value = value + steps[0] + steps[1] + steps[2]
    return sum_rep(value + move(value, swap_y_hi))


def scatter_eight(value):
    groups = [list(range(8)), list(range(8, 16))]
    flat = value.reshape(-1, value.shape[-1])
    out = lax.psum_scatter(flat, "fsdp", scatter_dimension=0, tiled=True, axis_index_groups=groups)
    return out.reshape((2,) + value.shape[1:])


def eight_order(f):
    return ((f // 2) % 4 * 2 + f % 2) * 2 + f // 8


def with_rows(block, extra):
    width = block.shape[-1]
    flat = block.reshape(-1, width)
    return flat if extra is None else jnp.concatenate([flat, extra], 0)


def adam_update(weight, gradient, moment_one, moment_two, learn_rate, decay_rate):
    moment_one = BETA_ONE * moment_one + (1.0 - BETA_ONE) * gradient
    moment_two = BETA_TWO * moment_two + (1.0 - BETA_TWO) * gradient * gradient
    scaled = (
        moment_one
        / (1.0 - BETA_ONE**STEP)
        / (jnp.sqrt(moment_two / (1.0 - BETA_TWO**STEP)) + ADAM_EPS)
    )
    return (weight - learn_rate * (scaled + decay_rate * weight), moment_one, moment_two)


def contract_rows(left_side, right_side):
    return lax.dot_general(
        left_side, right_side, (((0,), (0,)), ((), ())), preferred_element_type=F32
    )


def contract_cols(left_side, right_side):
    return lax.dot_general(
        left_side, right_side, (((1,), (1,)), ((), ())), preferred_element_type=F32
    )


def matmul(left_side, right_side):
    return jnp.dot(left_side, right_side, preferred_element_type=F32)


def segment_at(positions, seg_ends):
    counted = jnp.sum((positions[:, None] >= seg_ends[None, :]).astype(jnp.int32), axis=1)
    return jnp.where(positions < 0, jnp.int32(-1), counted)


def split_two(value):
    high = value.astype(BF16)
    return high, (value - high.astype(F32)).astype(BF16)


def split_three(value):
    high = value.astype(BF16)
    rest = value - high.astype(F32)
    middle = rest.astype(BF16)
    return high, middle, (rest - middle.astype(F32)).astype(BF16)


def product(left, right, left_dim, right_dim):
    return lax.dot_general(
        left, right, (((left_dim,), (right_dim,)), ((), ())), preferred_element_type=F32
    )


def joined_product(left_parts, right_parts, left_dim=1, right_dim=0):
    left_high, left_low = left_parts
    right_high, right_low = right_parts
    return product(
        jnp.concatenate([left_high, left_high, left_low], left_dim),
        jnp.concatenate([right_high, right_low, right_high], right_dim),
        left_dim,
        right_dim,
    )


def precise_product(left, right, left_dim=1, right_dim=0):
    return joined_product(split_two(left), split_two(right), left_dim, right_dim)


def ones_product(ones, value):
    return product(jnp.concatenate([ones] * 3, 1), jnp.concatenate(split_three(value), 0), 1, 0)


def spread(per_head, lane):
    return jnp.concatenate(
        [
            jnp.where(lane < P_SIZE, per_head[:, 2 * k : 2 * k + 1], per_head[:, 2 * k + 1 : 2 * k + 2])
            for k in range(OWN_H // 2)
        ],
        1,
    )


def head_sums(value):
    column = lax.broadcasted_iota(jnp.int32, (OWN, N), 0)
    head = lax.broadcasted_iota(jnp.int32, (OWN, N), 1)
    members = ((column >= head * P_SIZE) & (column < (head + 1) * P_SIZE)).astype(F32).astype(BF16)
    high, low = split_two(value)
    return product(jnp.concatenate([high, low], 1), jnp.concatenate([members, members], 0), 1, 0)


def two_heads(pair, lane):
    zero = jnp.zeros_like(pair)
    return jnp.concatenate([jnp.where(lane < P_SIZE, pair, zero), jnp.where(lane < P_SIZE, zero, pair)], 0)


def chunk_facts(ends, chunk, dt_pre, par):
    column = lax.broadcasted_iota(jnp.int32, (CHUNK, 1), 0) + chunk * CHUNK
    row = lax.broadcasted_iota(jnp.int32, (1, CHUNK), 1) + chunk * CHUNK

    def segment(position):
        counted = jnp.zeros_like(position)
        for k in range(3):
            counted = counted + (position >= ends[k]).astype(jnp.int32)
        return jnp.where(position < 0, -1, counted)

    def one_segment(position):
        counted = jnp.int32(0)
        for k in range(3):
            counted = counted + (position >= ends[k]).astype(jnp.int32)
        return jnp.where(position < 0, -1, counted)

    here_column, here_row = segment(column), segment(row)
    prior = one_segment(chunk * CHUNK - 1)
    last = one_segment(chunk * CHUNK + CHUNK - 1)
    lane = lax.broadcasted_iota(jnp.int32, (CHUNK, N), 1)
    shifted = dt_pre + par[6:7, :N]
    soft = jnp.maximum(shifted, 0.0) + jnp.log1p(jnp.exp(-jnp.abs(shifted)))
    step = jnp.where(lane < OWN_H, soft, 0.0)
    decay = step * par[7:8, :N]
    tri_row = lax.broadcasted_iota(jnp.int32, (CHUNK, CHUNK), 0)
    tri_column = lax.broadcasted_iota(jnp.int32, (CHUNK, CHUNK), 1)
    lower = (tri_row >= tri_column).astype(F32).astype(BF16)
    upper = (tri_row <= tri_column).astype(F32).astype(BF16)
    total = ones_product(lower, decay)
    entering = (here_column == prior).astype(F32) * jnp.exp(total)
    end = total[CHUNK - 1 : CHUNK]
    leaving = (here_column == last).astype(F32) * jnp.exp(jnp.minimum(end - total, 0.0))
    passing = jnp.where(last == prior, 1.0, 0.0) * jnp.exp(end)
    return dict(
        column=column,
        segment=segment,
        here_column=here_column,
        here_row=here_row,
        lane=lane,
        shifted=shifted,
        step=step,
        decay=decay,
        total=total,
        entering=entering,
        leaving=leaving,
        passing=passing,
        tri_row=tri_row,
        tri_column=tri_column,
        upper=upper,
    )


def forward_kernel(part, ends, proj, par, *refs):
    if part:
        carry_in, refs = refs[3], refs[4:]
    pre_out, mixed_out, state_out, carry_out, extended, state = refs
    chunk = pl.program_id(0) + part * HALF

    @pl.when(pl.program_id(0) == 0)
    def _():
        if part:
            state[...] = carry_in[:N, :OWN]
            extended[0:8, :] = carry_in[N:, :]
        else:
            state[...] = jnp.zeros_like(state)
            extended[0:8, :] = jnp.zeros((8, 640), F32)

    facts = chunk_facts(ends, chunk, proj[:, 1024:1152], par)
    lane = facts["lane"]
    conv = proj[:, OWN:1024].astype(BF16).astype(F32)
    extended[8 : 8 + CHUNK, :] = conv
    pre = par[4:5] + par[3:4] * conv
    for back in range(1, CONV):
        same = (facts["segment"](facts["column"] - back) == facts["here_column"]).astype(F32)
        pre = pre + par[3 - back : 4 - back] * (extended[8 - back : 8 - back + CHUNK, :] * same)
    extended[0:8, :] = extended[CHUNK : CHUNK + 8, :]
    pre_out[...] = pre
    act = pre * jax.nn.sigmoid(pre)
    own_x, state_b, state_c = act[:, :OWN], act[:, OWN : OWN + N], act[:, OWN + N :]
    stepped = own_x * spread(facts["step"], lane)
    b_parts, c_parts = split_two(state_b), split_two(state_c)
    inside = (facts["tri_row"] >= facts["tri_column"]) & (facts["here_column"] == facts["here_row"])
    scores = jnp.where(inside, joined_product(c_parts, b_parts, 1, 1), 0.0)
    total_rows = facts["total"].T
    state_in = state[...]
    state_out[...] = state_in
    outs = []
    for pair in range(OWN_H // 2):
        mixing = []
        for head in (2 * pair, 2 * pair + 1):
            span = facts["total"][:, head : head + 1] - total_rows[head : head + 1, :]
            mixing.append(jnp.exp(jnp.minimum(span, 0.0)) * scores)
        inner = two_heads(stepped[:, pair * N : pair * N + N], lane)
        outs.append(precise_product(jnp.concatenate(mixing, 1), inner))
    scanned = jnp.concatenate(outs, 1) + spread(facts["entering"], lane) * joined_product(
        c_parts, split_two(state_in)
    )
    state[...] = spread(facts["passing"], lane[:1]) * state_in + precise_product(
        state_b.T, stepped * spread(facts["leaving"], lane)
    )
    mixed_out[...] = scanned + par[5:6, :OWN] * own_x

    @pl.when(pl.program_id(0) == HALF - 1)
    def _():
        carry_out[:N, :OWN] = state[...]
        carry_out[:N, OWN:] = jnp.zeros((N, 640 - OWN), F32)
        carry_out[N:, :] = extended[0:8, :]


def run_forward(part, ends, proj, par, before=()):
    here = lambda i: (i + part * HALF, 0)
    chunked = lambda width: pl.BlockSpec((CHUNK, width), here)
    fixed = lambda shape: pl.BlockSpec(shape, lambda i: (0, 0))
    carry = fixed((N + 8, 640))
    return pl.pallas_call(
        partial(forward_kernel, part),
        grid=(HALF,),
        in_specs=[pl.BlockSpec(memory_space=pltpu.SMEM), chunked(1152), fixed((16, 640))]
        + ([pl.BlockSpec(memory_space=pl.ANY)] * 3 + [carry] if part else []),
        out_specs=[chunked(640), chunked(OWN), pl.BlockSpec((N, OWN), here), carry],
        out_shape=[
            jax.ShapeDtypeStruct((PACK, 640), F32),
            jax.ShapeDtypeStruct((PACK, OWN), F32),
            jax.ShapeDtypeStruct((CHUNKS * N, OWN), F32),
            jax.ShapeDtypeStruct((N + 8, 640), F32),
        ],
        input_output_aliases={3: 0, 4: 1, 5: 2} if part else {},
        scratch_shapes=[pltpu.VMEM((CHUNK + 8, 640), F32), pltpu.VMEM((N, OWN), F32)],
        compiler_params=pltpu.CompilerParams(
            dimension_semantics=("arbitrary",), vmem_limit_bytes=VMEM_LIMIT
        ),
        cost_estimate=COST,
        name="scan_forward",
    )(ends, proj, par, *before)


def backward_kernel(ends, conv_in, dt_in, pre_in, mixed_in, grad_mixed, state_all, par, *refs):
    grad_x, grad_dt, grad_bc, sums, head_acc, carried, extended, end_dot = refs
    step_index = pl.program_id(0)
    chunk = CHUNKS - 1 - step_index

    @pl.when(step_index == 0)
    def _():
        carried[...] = jnp.zeros_like(carried)
        extended[CHUNK : CHUNK + 8, :] = jnp.zeros((8, OWN), F32)
        end_dot[...] = jnp.zeros_like(end_dot)
        sums[...] = jnp.zeros_like(sums)
        head_acc[...] = jnp.zeros_like(head_acc)

    facts = chunk_facts(ends, chunk, dt_in[...], par)
    lane = facts["lane"]
    pre = pre_in[...]
    sig = jax.nn.sigmoid(pre)
    act = pre * sig
    own_x, state_b, state_c = act[:, :OWN], act[:, OWN : OWN + N], act[:, OWN + N :]
    step = facts["step"]
    step_wide = spread(step, lane)
    stepped = own_x * step_wide
    skip = par[5:6, :OWN]
    scanned = mixed_in[...] - skip * own_x
    grad_m = grad_mixed[...]
    sums[6:7] += jnp.sum(grad_m * own_x, 0, keepdims=True)

    b_parts, c_parts = split_two(state_b), split_two(state_c)
    inside = (facts["tri_row"] <= facts["tri_column"]) & (facts["here_column"] == facts["here_row"])
    scores = jnp.where(inside, joined_product(b_parts, c_parts, 1, 1), 0.0)
    total_rows = facts["total"].T
    grad_scores = jnp.zeros((CHUNK, CHUNK), F32)
    grad_stepped = []
    for pair in range(OWN_H // 2):
        columns = slice(pair * N, pair * N + N)
        grad_pair = grad_m[:, columns]
        high, low = split_two(grad_pair)
        stepped_parts = split_two(two_heads(stepped[:, columns], lane))
        grad_mixing = joined_product(stepped_parts, (high, low), 1, 1)
        mixing = []
        for k in range(2):
            head = 2 * pair + k
            span = total_rows[head : head + 1, :] - facts["total"][:, head : head + 1]
            decays = jnp.exp(jnp.minimum(span, 0.0))
            mixing.append(decays * scores)
            grad_scores = grad_scores + decays * grad_mixing[k * CHUNK : (k + 1) * CHUNK]
        grad_stepped.append(
            joined_product(
                split_two(jnp.concatenate(mixing, 1)), (two_heads(high, lane), two_heads(low, lane))
            )
        )
    grad_scores = jnp.where(inside, grad_scores, 0.0)
    carry = carried[...]
    carry_parts = split_two(carry)
    leaving = spread(facts["leaving"], lane)
    grad_stepped = jnp.concatenate(grad_stepped, 1) + leaving * joined_product(b_parts, carry_parts)
    state_in = state_all[...]
    entered = spread(facts["entering"], lane) * grad_m
    entered_parts = split_two(entered)
    grad_b = precise_product(grad_scores, state_c) + joined_product(
        split_two(leaving * stepped), carry_parts, 1, 1
    )
    grad_c = precise_product(grad_scores.T, state_b) + joined_product(
        entered_parts, split_two(state_in), 1, 1
    )
    grad_bc[0:N, :] = grad_b.T.astype(BF16)
    grad_bc[N:, :] = grad_c.T.astype(BF16)
    new_carry = spread(facts["passing"], lane[:1]) * carry + joined_product(
        split_two(state_c.T), entered_parts
    )
    carried[...] = new_carry

    grad_step = head_sums(own_x * grad_stepped)
    last_row = lax.broadcasted_iota(jnp.int32, (CHUNK, N), 0) == CHUNK - 1
    grad_total = head_sums(grad_m * scanned) - step * grad_step
    grad_total = grad_total + jnp.where(last_row, end_dot[0:1, :], 0.0)
    grad_decay = ones_product(facts["upper"], grad_total)
    end_dot[...] = head_sums(
        jnp.broadcast_to(jnp.sum(new_carry * state_in, 0, keepdims=True), (8, OWN))
    )
    grad_pre_dt = (grad_step + grad_decay * par[7:8, :N]) * jax.nn.sigmoid(facts["shifted"])
    grad_pre_dt = jnp.where(lane < OWN_H, grad_pre_dt, 0.0)
    grad_dt[...] = grad_pre_dt.astype(BF16)
    head_acc[0:1] += jnp.sum(grad_pre_dt, 0, keepdims=True)
    head_acc[1:2] += jnp.sum(grad_decay * facts["decay"], 0, keepdims=True)

    sig_x, pre_x = sig[:, :OWN], pre[:, :OWN]
    grad_pre = (step_wide * grad_stepped + skip * grad_m) * (sig_x * (1.0 + pre_x * (1.0 - sig_x)))
    extended[0:CHUNK, :] = grad_pre
    conv = conv_in[...].astype(BF16).astype(F32)
    sums[5:6] += jnp.sum(grad_pre, 0, keepdims=True)
    sums[4:5] += jnp.sum(conv * grad_pre, 0, keepdims=True)
    grad_conv = par[3:4, :OWN] * grad_pre
    for ahead in range(1, CONV):
        same = (facts["segment"](facts["column"] + ahead) == facts["here_column"]).astype(F32)
        later = extended[ahead : ahead + CHUNK, :] * same
        sums[4 - ahead : 5 - ahead] += jnp.sum(conv * later, 0, keepdims=True)
        grad_conv = grad_conv + par[3 - ahead : 4 - ahead, :OWN] * later
    extended[CHUNK : CHUNK + 8, :] = extended[0:8, :]
    grad_x[...] = grad_conv.astype(BF16)


def run_backward(ends, proj, pre, mixed, grad_mixed, states, par):
    last = CHUNKS - 1
    chunked = lambda width, column=0: pl.BlockSpec((CHUNK, width), lambda i: (last - i, column))
    fixed = lambda shape: pl.BlockSpec(shape, lambda i: (0, 0))
    return pl.pallas_call(
        backward_kernel,
        grid=(CHUNKS,),
        in_specs=[
            pl.BlockSpec(memory_space=pltpu.SMEM),
            chunked(OWN, 1),
            chunked(N, 8),
            chunked(640),
            chunked(OWN),
            chunked(OWN),
            pl.BlockSpec((N, OWN), lambda i: (last - i, 0)),
            fixed((16, 640)),
        ],
        out_specs=[
            chunked(OWN),
            chunked(N),
            pl.BlockSpec((2 * N, CHUNK), lambda i: (0, last - i)),
            fixed((8, OWN)),
            fixed((8, N)),
        ],
        out_shape=[
            jax.ShapeDtypeStruct((PACK, OWN), BF16),
            jax.ShapeDtypeStruct((PACK, N), BF16),
            jax.ShapeDtypeStruct((2 * N, PACK), BF16),
            jax.ShapeDtypeStruct((8, OWN), F32),
            jax.ShapeDtypeStruct((8, N), F32),
        ],
        scratch_shapes=[
            pltpu.VMEM((N, OWN), F32),
            pltpu.VMEM((CHUNK + 8, OWN), F32),
            pltpu.VMEM((8, N), F32),
        ],
        compiler_params=pltpu.CompilerParams(
            dimension_semantics=("arbitrary",), vmem_limit_bytes=VMEM_LIMIT
        ),
        cost_estimate=COST,
        name="scan_backward",
    )(ends, proj, proj, pre, mixed, grad_mixed, states, par)


PARTS = (1, 1, 1, 1, 1, 2, 1, 1)


def piece_copies(pieces, parts, blocks, sems):
    copies = []
    taken = 0
    for slot, count in enumerate(parts):
        rows = ROWS // count
        copies.append(
            [
                pltpu.make_async_copy(
                    pieces[taken + k], blocks.at[slot, pl.ds(k * rows, rows)], sems.at[taken + k]
                )
                for k in range(count)
            ]
        )
        taken += count
    return copies


def fetch_block(pieces, parts, blocks, sems):
    copies = piece_copies(pieces, parts, blocks, sems)
    step = pl.program_id(0)

    @pl.when(step == 0)
    def _():
        for group in copies:
            for copy in group:
                copy.start()

    for slot, group in enumerate(copies):

        @pl.when(step == slot)
        def _(group=group):
            for copy in group:
                copy.wait()

    return blocks[step]


def project_kernel(parts, table, *refs):
    pieces = refs[: sum(parts)]
    gain, shards, normed_out, proj, dt_out, blocks, weight, sems = refs[sum(parts) :]
    block = fetch_block(pieces, parts, blocks, sems)

    @pl.when(pl.program_id(0) == 0)
    def _():
        for f in range(N_FSDP):
            weight[f * SHARD_IN : (f + 1) * SHARD_IN, :] = shards[(f // 2) % 4, f % 2, f // 8, :SHARD_IN]
        dt_out[...] = weight[:, 1024:]

    values = block.astype(F32)
    scale = lax.rsqrt(jnp.mean(values * values, axis=1, keepdims=True) + NORM_EPS)
    normed = (values * scale * gain[...]).astype(BF16)
    normed_out[...] = normed
    proj[...] = matmul(normed, weight[...])


def run_project(table, pieces, gain, shards):
    fixed = lambda shape: pl.BlockSpec(shape, lambda i, table: (0,) * len(shape))
    placed = lambda width: pl.BlockSpec((ROWS, width), lambda i, table: (table[i], 0))
    return pl.pallas_call(
        partial(project_kernel, PARTS),
        grid_spec=pltpu.PrefetchScalarGridSpec(
            num_scalar_prefetch=1,
            grid=(N_REP,),
            in_specs=[pl.BlockSpec(memory_space=pl.ANY)] * len(pieces) + [fixed((1, D)), fixed(shards.shape)],
            out_specs=[placed(D), placed(3 * WIDE), fixed((D, N))],
            scratch_shapes=[
                pltpu.VMEM((N_REP, ROWS, D), BF16),
                pltpu.VMEM((D, 3 * WIDE), BF16),
                pltpu.SemaphoreType.DMA((len(pieces),)),
            ],
        ),
        out_shape=[
            jax.ShapeDtypeStruct((PACK, D), BF16),
            jax.ShapeDtypeStruct((PACK, 3 * WIDE), F32),
            jax.ShapeDtypeStruct((D, N), BF16),
        ],
        compiler_params=pltpu.CompilerParams(
            dimension_semantics=("arbitrary",), vmem_limit_bytes=VMEM_LIMIT
        ),
        cost_estimate=COST,
        name="project",
    )(table, *pieces, gain, shards)


def row_sums(value):
    folded = value[:, :N] + value[:, N : 2 * N] + value[:, 2 * N :]
    return jnp.sum(folded.T, 0, keepdims=True)


def out_grad_kernel(table, *refs):
    pieces = refs[: sum(PARTS)]
    w_out, mixed, gate_in, gain, branch_out, grad_out, sums, blocks, turned, sems = refs[sum(PARTS) :]
    branch = fetch_block(pieces, PARTS, blocks, sems)

    @pl.when(pl.program_id(0) == 0)
    def _():
        turned[...] = w_out[...].reshape(OWN, D).T

    branch_out[...] = branch
    total = matmul(branch, turned[...])
    grad_out[...] = total
    gate = gate_in[...]
    gated = mixed[...] * (gate * jax.nn.sigmoid(gate))
    row = lax.broadcasted_iota(jnp.int32, (8, ROWS), 0)
    sums[...] = jnp.where(
        row == 0, row_sums(gated * gated), jnp.where(row == 1, row_sums(total * gain[...] * gated), 0.0)
    )


def run_out_grad(table, pieces, w_out, mixed, proj, gain):
    fixed = lambda shape: pl.BlockSpec(shape, lambda i, table: (0, 0))
    placed = lambda width: pl.BlockSpec((ROWS, width), lambda i, table: (table[i], 0))
    own = pl.BlockSpec(
        (1, 2, 1, SHARD_OUT, D), lambda i, table: (table[N_REP] % 4, 0, table[N_REP] // 4, 0, 0)
    )
    return pl.pallas_call(
        out_grad_kernel,
        grid_spec=pltpu.PrefetchScalarGridSpec(
            num_scalar_prefetch=1,
            grid=(N_REP,),
            in_specs=[pl.BlockSpec(memory_space=pl.ANY)] * len(pieces)
            + [own, placed(OWN), placed(OWN), fixed((1, OWN))],
            out_specs=[placed(D), placed(OWN), pl.BlockSpec((8, ROWS), lambda i, table: (0, table[i]))],
            scratch_shapes=[
                pltpu.VMEM((N_REP, ROWS, D), BF16),
                pltpu.VMEM((D, WIDE), BF16),
                pltpu.SemaphoreType.DMA((len(pieces),)),
            ],
        ),
        out_shape=[
            jax.ShapeDtypeStruct((PACK, D), BF16),
            jax.ShapeDtypeStruct((PACK, OWN), F32),
            jax.ShapeDtypeStruct((8, PACK), F32),
        ],
        compiler_params=pltpu.CompilerParams(
            dimension_semantics=("arbitrary",), vmem_limit_bytes=VMEM_LIMIT
        ),
        cost_estimate=COST,
        name="out_grad",
    )(table, *pieces, w_out, mixed, proj, gain)


def gate_kernel(grad_out, mixed_in, gate_in, sums, gain, low_out, grad_mixed, grad_gain):
    rows = grad_out.shape[0]
    mixed, gate, grad_o = mixed_in[...], gate_in[...], grad_out[...]
    stats = jnp.concatenate([sums[...], jnp.zeros((N - 8, rows), F32)], 0).T
    out_scale = lax.rsqrt(stats[:, 0:1] * (1.0 / DI) + NORM_EPS)
    pull = out_scale * out_scale * out_scale * (stats[:, 1:2] * (1.0 / DI))
    gate_sig = jax.nn.sigmoid(gate)
    silu = gate * gate_sig
    gated = mixed * silu
    unit = gated * out_scale
    grad_gated = out_scale * (grad_o * gain[...]) - gated * pull
    grad_mixed[...] = grad_gated * silu
    low_out[:, :OWN] = (unit * gain[...]).astype(BF16)
    low_out[:, OWN:] = (grad_gated * mixed * (gate_sig * (1.0 + gate * (1.0 - gate_sig)))).astype(BF16)
    gain_part = jnp.sum(grad_o * unit, 0, keepdims=True)

    @pl.when(pl.program_id(0) == 0)
    def _():
        grad_gain[...] = jnp.broadcast_to(gain_part, grad_gain.shape)

    @pl.when(pl.program_id(0) > 0)
    def _():
        grad_gain[...] += gain_part


def run_gate(grad_out, mixed, proj, sums, gain):
    rows = lambda width: pl.BlockSpec((ROWS, width), lambda i: (i, 0))
    fixed = lambda shape: pl.BlockSpec(shape, lambda i: (0, 0))
    return pl.pallas_call(
        gate_kernel,
        grid=(PACK // ROWS,),
        in_specs=[
            rows(OWN),
            rows(OWN),
            rows(OWN),
            pl.BlockSpec((8, ROWS), lambda i: (0, i)),
            fixed((1, OWN)),
        ],
        out_specs=[rows(2 * OWN), rows(OWN), fixed((8, OWN))],
        out_shape=[
            jax.ShapeDtypeStruct((PACK, 2 * OWN), BF16),
            jax.ShapeDtypeStruct((PACK, OWN), F32),
            jax.ShapeDtypeStruct((8, OWN), F32),
        ],
        compiler_params=pltpu.CompilerParams(
            dimension_semantics=("arbitrary",), vmem_limit_bytes=VMEM_LIMIT
        ),
        cost_estimate=COST,
        name="gate_backward",
    )(grad_out, mixed, proj, sums, gain)


def early_grad_kernel(low, grad_branch, normed, out):
    step = pl.program_id(0)

    @pl.when(step == 0)
    def _():
        out[...] = jnp.zeros_like(out)

    for k in range(4):
        part = product(low[:, :OWN], grad_branch[:, k * WIDE : (k + 1) * WIDE], 0, 0)
        for m in range(4):
            out[eight_order(4 * k + m), :SHARD_IN] += part[m * SHARD_IN : (m + 1) * SHARD_IN]
    part = product(normed[...], low[:, OWN:], 0, 0)
    for f in range(N_FSDP):
        out[eight_order(f), SHARD_IN:] += part[f * SHARD_IN : (f + 1) * SHARD_IN]


def run_early_grad(low, grad_branch, normed):
    count = 2 * ROWS
    rows = lambda width: pl.BlockSpec((count, width), lambda i: (i, 0))
    shape = (N_FSDP, 2 * SHARD_IN, WIDE)
    return pl.pallas_call(
        early_grad_kernel,
        grid=(PACK // count,),
        in_specs=[rows(2 * OWN), rows(D), rows(D)],
        out_specs=pl.BlockSpec(shape, lambda i: (0, 0, 0)),
        out_shape=jax.ShapeDtypeStruct(shape, F32),
        compiler_params=pltpu.CompilerParams(
            dimension_semantics=("arbitrary",), vmem_limit_bytes=VMEM_LIMIT
        ),
        cost_estimate=COST,
        name="early_grad",
    )(low, grad_branch, normed)


def block_out_kernel(rows, weight, tokens, live, out):
    step = pl.program_id(0)
    part = matmul(jnp.concatenate([rows[0], rows[1]], 1), weight[...].reshape(2 * OWN, D))

    @pl.when(step == 0)
    def _():
        out[...] = part

    @pl.when(step > 0)
    def _():
        out[...] += part

    @pl.when(step == N_REP // 2 - 1)
    def _():
        out[...] = tokens[...].astype(F32) + live[...] * out[...]


def run_block_out(rows, weight, tokens, live):
    fixed = lambda shape: pl.BlockSpec(shape, lambda i: (0, 0))
    return pl.pallas_call(
        block_out_kernel,
        grid=(N_REP // 2,),
        in_specs=[
            pl.BlockSpec((2, ROWS, OWN), lambda i: (i, 0, 0)),
            pl.BlockSpec((2, 2, 1, SHARD_OUT, D), lambda i: (i % 2, 0, i // 2, 0, 0)),
            fixed((ROWS, D)),
            fixed((ROWS, 1)),
        ],
        out_specs=fixed((ROWS, D)),
        out_shape=jax.ShapeDtypeStruct((ROWS, D), F32),
        compiler_params=pltpu.CompilerParams(
            dimension_semantics=("arbitrary",), vmem_limit_bytes=VMEM_LIMIT
        ),
        cost_estimate=FILL,
        name="block_out",
    )(rows, weight, tokens, live)


def turned_part(weight, rows):
    return product(weight[...].reshape(D, weight.shape[-1]), rows, 1, 1)


def columns_of(full_in, width, index):
    return pl.BlockSpec(full_in.shape[:-1] + (width,), lambda i: (0, 0, 0, 0, index(i)))


def z_grad_kernel(rows, weight, out):
    part = turned_part(weight, jnp.concatenate([rows[0], rows[1]], 1))

    @pl.when(pl.program_id(0) == 0)
    def _():
        out[...] = part

    @pl.when(pl.program_id(0) > 0)
    def _():
        out[...] += part


def run_z_grad(rows, full_in):
    return pl.pallas_call(
        z_grad_kernel,
        grid=(N_REP // 2,),
        in_specs=[
            pl.BlockSpec((2, ROWS, OWN), lambda i: (i, 0, 1)),
            columns_of(full_in, 2 * OWN, lambda i: i),
        ],
        out_specs=pl.BlockSpec((D, ROWS), lambda i: (0, 0)),
        out_shape=jax.ShapeDtypeStruct((D, ROWS), F32),
        compiler_params=pltpu.CompilerParams(
            dimension_semantics=("arbitrary",), vmem_limit_bytes=VMEM_LIMIT
        ),
        cost_estimate=FILL,
        name="z_grad",
    )(rows, full_in)


def input_grad_kernel(
    grad_z, x_rows, rest_rows, w_x, w_bc, low_dt, tokens, cotangent, gain, out, gain_out, total, ordered
):
    step = pl.program_id(0)
    part = turned_part(w_x, jnp.concatenate([x_rows[0], x_rows[1]], 1))

    @pl.when(step == 0)
    def _():
        total[...] = grad_z[...] + part

    @pl.when(step > 0)
    def _():
        total[...] += part

    @pl.when(step == N_REP // 2 - 1)
    def _():
        lane = lax.broadcasted_iota(jnp.int32, (ROWS, N), 1)
        groups = []
        for k in range(2):
            group = jnp.zeros((ROWS, N), F32)
            for m in range(4):
                value = rest_rows[4 * k + m].astype(F32)
                value = value if m == 0 else pltpu.roll(value, m * OWN_BC, 1)
                group = jnp.where((lane >= m * OWN_BC) & (lane < (m + 1) * OWN_BC), value, group)
            groups.append(group.astype(BF16))
        steps = jnp.zeros((ROWS, N), F32)
        for m in range(N_REP):
            start = 8 + m * OWN_H
            value = pltpu.roll(rest_rows[m].astype(F32), (start - OWN_BC) % N, 1)
            steps = jnp.where((lane >= start) & (lane < start + OWN_H), value, steps)
        shared = total[...] + turned_part(w_bc, jnp.concatenate(groups, 1))
        for f in range(N_FSDP):
            start = eight_order(f) * SHARD_IN
            ordered[f * SHARD_IN : (f + 1) * SHARD_IN, :] = shared[start : start + SHARD_IN, :]
        grad_h = (ordered[...] + product(low_dt[...], steps.astype(BF16), 1, 1)).T
        values = tokens[...].astype(F32)
        scale = lax.rsqrt(jnp.mean(values * values, axis=1, keepdims=True) + NORM_EPS)
        unit = values * scale
        gain_sum = jnp.sum(grad_h * unit, 0, keepdims=True)
        gain_out[...] = jnp.zeros_like(gain_out)
        for k in range(D // N):
            gain_out[k : k + 1, :] = gain_sum[:, k * N : (k + 1) * N]
        grad_unit = grad_h * gain[...]
        inner = jnp.mean(grad_unit * unit, axis=1, keepdims=True)
        out[...] = cotangent[...].astype(F32) + scale * (grad_unit - unit * inner)


def run_input_grad(grad_z, tail_rows, full_in, low_dt, tokens, cotangent, gain):
    fixed = lambda shape: pl.BlockSpec(shape, lambda i: (0,) * len(shape))
    return pl.pallas_call(
        input_grad_kernel,
        grid=(N_REP // 2,),
        in_specs=[
            fixed((D, ROWS)),
            pl.BlockSpec((2, ROWS, OWN), lambda i: (i, 0, 0)),
            pl.BlockSpec((N_REP, ROWS, N), lambda i: (0, 0, OWN // N)),
            columns_of(full_in, 2 * OWN, lambda i: N_REP // 2 + i),
            columns_of(full_in, 2 * N, lambda i: DI // N),
            fixed((D, N)),
            fixed((ROWS, D)),
            fixed((ROWS, D)),
            fixed((1, D)),
        ],
        out_specs=[fixed((ROWS, D)), fixed((16, N))],
        out_shape=[jax.ShapeDtypeStruct((ROWS, D), F32), jax.ShapeDtypeStruct((16, N), F32)],
        scratch_shapes=[pltpu.VMEM((D, ROWS), F32), pltpu.VMEM((D, ROWS), F32)],
        compiler_params=pltpu.CompilerParams(
            dimension_semantics=("arbitrary",), vmem_limit_bytes=VMEM_LIMIT
        ),
        cost_estimate=COST,
        name="input_grad",
    )(grad_z, tail_rows, tail_rows, full_in, full_in, low_dt, tokens, cotangent, gain)


def rest_kernel(
    ends, parts, pre_b, pre_c, conv_in, par, grad_x, grad_dt, sums, head_acc, grad_gain, first, tail_out, small_out
):
    own = lax.broadcasted_iota(jnp.int32, (OWN_BC, 2 * N), 0) + first[0]
    chosen = (lax.broadcasted_iota(jnp.int32, (OWN_BC, 2 * N), 1) == own).astype(F32).astype(BF16)

    def pick(value):
        return product(jnp.concatenate([chosen] * 3, 1), jnp.concatenate(split_three(value), 1), 1, 1)

    grad = parts[0].astype(F32)
    for k in range(1, N_REP):
        grad = grad + parts[k].astype(F32)
    own_pre = pick(jnp.concatenate([pre_b[...], pre_c[...]], 1))
    own_conv = product(chosen, conv_in[...].astype(BF16), 1, 1)
    taps = pick(par[:, OWN:])
    sig = jax.nn.sigmoid(own_pre)
    grad_pre = grad * (sig * (1.0 + own_pre * (1.0 - sig)))
    position = lax.broadcasted_iota(jnp.int32, (1, PACK), 1)

    def segment(places):
        counted = jnp.zeros_like(places)
        for k in range(3):
            counted = counted + (places >= ends[k]).astype(jnp.int32)
        return counted

    grad_conv = taps[:, CONV - 1 : CONV] * grad_pre
    column = lax.broadcasted_iota(jnp.int32, (OWN_BC, N), 1)
    found = jnp.where(column == CONV, jnp.sum(grad_pre, 1, keepdims=True), 0.0)
    found = jnp.where(column == CONV - 1, jnp.sum(own_conv * grad_pre, 1, keepdims=True), found)
    for later_by in range(1, CONV):
        same = (segment(position + later_by) == segment(position)) & (position < PACK - later_by)
        later = jnp.where(same, pltpu.roll(grad_pre, PACK - later_by, 1), 0.0)
        tap = CONV - 1 - later_by
        found = jnp.where(column == tap, jnp.sum(own_conv * later, 1, keepdims=True), found)
        grad_conv = grad_conv + taps[:, tap : tap + 1] * later
    lane = lax.broadcasted_iota(jnp.int32, (N, N), 1)
    filler = jnp.zeros((N - OWN_BC, N), F32)
    for k in range(PACK // N):
        rows = slice(k * N, (k + 1) * N)
        columns = jnp.concatenate([grad_conv[:, rows], filler], 0).T
        steps = pltpu.roll(grad_dt[rows, :].astype(F32), OWN_BC, 1)
        tail_out[rows, :OWN] = grad_x[rows, :]
        tail_out[rows, OWN:] = jnp.where(
            lane < OWN_BC, columns, jnp.where(lane < OWN_BC + OWN_H, steps, 0.0)
        ).astype(BF16)
    row = lax.broadcasted_iota(jnp.int32, (8, OWN), 0)
    skip = head_sums(sums[...])
    by_head = jnp.concatenate([skip, jnp.zeros((8, OWN - N), F32)], 1)
    logs = jnp.concatenate([head_acc[...], jnp.zeros((8, OWN - N), F32)], 1)
    wide = jnp.where(row == 0, grad_gain[0:1, :], jnp.where(row < 6, sums[...], 0.0))
    wide = jnp.where(row == 6, logs[1:2, :], jnp.where(row == 7, by_head[6:7, :], wide))
    turned = jnp.concatenate([found, filler], 0).T
    first_row = lax.broadcasted_iota(jnp.int32, (8, N), 0) == 0
    small_out[:, :OWN] = wide
    small_out[:, OWN:] = jnp.where(first_row, head_acc[0:1, :], pltpu.roll(turned[:8], 1, 0))


def run_rest(ends, parts, pre, proj, par, grad_x, grad_dt, sums, head_acc, grad_gain, first):
    fixed = lambda shape: pl.BlockSpec(shape, lambda i: (0,) * len(shape))
    return pl.pallas_call(
        rest_kernel,
        grid=(1,),
        in_specs=[
            pl.BlockSpec(memory_space=pltpu.SMEM),
            fixed((N_REP, OWN_BC, PACK)),
            pl.BlockSpec((PACK, N), lambda i: (0, 3)),
            pl.BlockSpec((PACK, N), lambda i: (0, 4)),
            pl.BlockSpec((PACK, 2 * N), lambda i: (0, 3)),
            fixed((16, 640)),
            fixed((PACK, OWN)),
            fixed((PACK, N)),
            fixed((8, OWN)),
            fixed((8, N)),
            fixed((8, OWN)),
            pl.BlockSpec(memory_space=pltpu.SMEM),
        ],
        out_specs=[fixed((PACK, TAIL)), fixed((8, TAIL))],
        out_shape=[jax.ShapeDtypeStruct((PACK, TAIL), BF16), jax.ShapeDtypeStruct((8, TAIL), F32)],
        compiler_params=pltpu.CompilerParams(
            dimension_semantics=("arbitrary",), vmem_limit_bytes=VMEM_LIMIT
        ),
        cost_estimate=COST,
        name="rest_backward",
    )(ends, parts, pre, pre, proj, par, grad_x, grad_dt, sums, head_acc, grad_gain, first)


def tail_grad_kernel(normed, tail, small, out):
    step = pl.program_id(0)
    part = product(normed[...], tail[...], 0, 0)
    for f in range(N_FSDP):
        rows = part[f * SHARD_IN : (f + 1) * SHARD_IN]

        @pl.when(step == 0)
        def _(f=f, rows=rows):
            out[eight_order(f), :SHARD_IN] = rows
            out[eight_order(f), SHARD_IN:] = small[...]

        @pl.when(step > 0)
        def _(f=f, rows=rows):
            out[eight_order(f), :SHARD_IN] += rows


def run_tail_grad(normed, tail, small):
    count = 2 * ROWS
    shape = (N_FSDP, SHARD_IN + 8, TAIL)
    return pl.pallas_call(
        tail_grad_kernel,
        grid=(PACK // count,),
        in_specs=[
            pl.BlockSpec((count, D), lambda i: (i, 0)),
            pl.BlockSpec((count, TAIL), lambda i: (i, 0)),
            pl.BlockSpec((8, TAIL), lambda i: (0, 0)),
        ],
        out_specs=pl.BlockSpec(shape, lambda i: (0, 0, 0)),
        out_shape=jax.ShapeDtypeStruct(shape, F32),
        compiler_params=pltpu.CompilerParams(
            dimension_semantics=("arbitrary",), vmem_limit_bytes=VMEM_LIMIT
        ),
        cost_estimate=COST,
        name="tail_grad",
    )(normed, tail, small)


def adam_step(grad, weight, first, second, grad_out, first_out, second_out, weight_out):
    new_weight, new_first, new_second = adam_update(
        weight[...], grad, first[...], second[...], RATE_MATRIX, WEIGHT_DECAY
    )
    grad_out[...] = grad
    first_out[...] = new_first
    second_out[...] = new_second
    weight_out[...] = new_weight


def load_pair(step, pairs, rows, grad):
    pair, right, far_first, far_second, left = pairs
    for slot, (low, high) in enumerate(
        (((pair, 0), (pair, 1)), ((right, 0), (right, 1)), ((far_first, 0), (far_second, 0)), ((left, 0), (left, 1)))
    ):

        @pl.when(step == slot)
        def _(low=low, high=high):
            grad[:, :WIDE] = low[0][low[1], rows, :]
            grad[:, WIDE:] = high[0][high[1], rows, :]


def adam_pairs_kernel(rows, table, *refs):
    pairs, arrays, grad = refs[:5], refs[5:8] + refs[-5:-1], refs[-1]
    load_pair(pl.program_id(0), pairs, rows, grad)
    adam_step(grad[...], *arrays)


def run_adam_pairs(table, place_of, rows, pairs, weight, first, second):
    part = pl.BlockSpec((SHARD_IN, 2 * WIDE), lambda i, table: place_of(table[i]))
    shape = jax.ShapeDtypeStruct(weight.shape, F32)
    return pl.pallas_call(
        partial(adam_pairs_kernel, rows),
        grid_spec=pltpu.PrefetchScalarGridSpec(
            num_scalar_prefetch=1,
            grid=(4,),
            in_specs=[pl.BlockSpec(pair.shape, lambda i, table: (0, 0, 0)) for pair in pairs]
            + [part] * 3,
            out_specs=[part] * 4,
            scratch_shapes=[pltpu.VMEM((SHARD_IN, 2 * WIDE), F32)],
        ),
        out_shape=[shape] * 4,
        compiler_params=pltpu.CompilerParams(
            dimension_semantics=("arbitrary",), vmem_limit_bytes=VMEM_LIMIT
        ),
        cost_estimate=FILL,
        name="adam",
    )(table, *pairs, weight, first, second)


def adam_tail_kernel(pair, rest, *refs):
    arrays, grad = refs[:3] + refs[-5:-1], refs[-1]
    step = pl.program_id(0)

    @pl.when(step < N_REP // 2)
    def _():
        grad[:, :WIDE] = pair[0, :SHARD_IN]
        grad[:, WIDE:] = pair[1, :SHARD_IN]

    @pl.when(step == N_REP // 2)
    def _():
        lane = lax.broadcasted_iota(jnp.int32, (SHARD_IN, N), 1)
        for k in range(2):
            group = jnp.zeros((SHARD_IN, N), F32)
            for m in range(4):
                value = rest[4 * k + m, :SHARD_IN]
                value = value if m == 0 else pltpu.roll(value, m * OWN_BC, 1)
                group = jnp.where((lane >= m * OWN_BC) & (lane < (m + 1) * OWN_BC), value, group)
            grad[:, k * N : (k + 1) * N] = group

    adam_step(grad[...], *arrays)


def run_adam_tail(parts, weight, first, second, before):
    half = N_REP // 2
    rows = parts.shape[1]
    column = pl.BlockSpec((SHARD_IN, 2 * WIDE), lambda i: (0, half + i))
    shape = jax.ShapeDtypeStruct(weight.shape, F32)
    return pl.pallas_call(
        adam_tail_kernel,
        grid=(half + 1,),
        in_specs=[
            pl.BlockSpec((2, rows, OWN), lambda i: (jnp.minimum(i, half - 1), 0, 0)),
            pl.BlockSpec((N_REP, rows, N), lambda i: (0, 0, OWN // N)),
        ]
        + [column] * 3
        + [pl.BlockSpec(memory_space=pl.ANY)] * 4,
        out_specs=[column] * 4,
        out_shape=[shape] * 4,
        input_output_aliases={5 + k: k for k in range(4)},
        scratch_shapes=[pltpu.VMEM((SHARD_IN, 2 * WIDE), F32)],
        compiler_params=pltpu.CompilerParams(
            dimension_semantics=("arbitrary",), vmem_limit_bytes=VMEM_LIMIT
        ),
        cost_estimate=COST,
        name="adam_tail",
    )(parts, parts, weight, first, second, *before)


def body(
    tokens,
    cotangent,
    lengths,
    w_in,
    w_dt,
    w_out,
    small,
    first_in,
    first_dt,
    first_out,
    first_small,
    second_in,
    second_dt,
    second_out,
    second_small,
):
    place = Place()
    r = place.r
    zero = jnp.int32(0)
    pack_lengths = lax.dynamic_slice_in_dim(lengths, place.f, 1, 0)[0]
    seg_ends = jnp.cumsum(pack_lengths)
    own_positions = r * ROWS + jnp.arange(ROWS, dtype=jnp.int32)
    own_live = (segment_at(own_positions, seg_ends) < 3).astype(F32)[:, None]
    slots = jnp.arange(N_REP, dtype=jnp.int32)
    ahead = ((place.x + slots // 2) % 4) * 2 + (place.yl + slots) % 2
    half = ROWS // 2

    in_low = w_in.astype(BF16)
    dt_low = w_dt.astype(BF16)
    out_low = w_out.astype(BF16)

    small_rows = jnp.pad(small.astype(BF16), (0, 16 * 3 * WIDE - SHARD_SMALL)).reshape(16, 3 * WIDE)

    def own_columns(rep):
        columns = jnp.concatenate(
            [
                lax.dynamic_slice_in_dim(in_low, rep * OWN, OWN, 1),
                lax.dynamic_slice_in_dim(in_low, DI + rep * OWN, OWN, 1),
                in_low[:, 2 * DI :],
                lax.dynamic_slice_in_dim(dt_low, rep * OWN_H, OWN_H, 1),
                jnp.zeros((SHARD_IN, 2), BF16),
                dt_low,
                jnp.zeros((SHARD_IN, N - 8 - H), BF16),
            ],
            1,
        )
        return jnp.concatenate([columns, small_rows], 0)

    other_columns = move(
        own_columns(2 * place.x + 1 - place.yl), lambda yh, z, c, x, yl: (yh + 1, z, c, x, yl + 1)
    )
    from_left = move(tokens, along_x(1))
    from_right = move(tokens, along_x(-1))
    partner = move(tokens, swap_y)

    out_low, other_columns = lax.optimization_barrier((out_low, other_columns))
    out_other = move(out_low, lambda yh, z, c, x, yl: (yh + 1, z, c, x, yl + 1))
    from_left, from_right, partner, other_columns = lax.optimization_barrier(
        (from_left, from_right, partner, other_columns)
    )
    own_shards = gather_eight(both(own_columns(r), other_columns, place.yh))
    far = move(from_left, along_x(1))
    partner_left = move(from_left, swap_y)
    partner_right = move(partner, along_x(-1))

    branch = (cotangent.astype(F32) * own_live).astype(BF16)
    far, partner_left, partner_right, out_other, branch = lax.optimization_barrier(
        (far, partner_left, partner_right, out_other, branch)
    )
    out_pair = both(out_low, out_other, place.yh)
    partner_far_top = move(partner_left[:half], along_x(1))
    partner_far_low = move(partner_right[half:], along_x(-1))

    vector = own_shards[:, :, :, SHARD_IN : SHARD_IN + 2].transpose(2, 0, 1, 3, 4)
    vector = vector.reshape(N_FSDP, 6 * WIDE)[:, :SHARD_SMALL].reshape(-1).astype(F32)
    offset = 0
    gain_in = vector[None, :D]
    offset = D
    gain_row = lax.dynamic_slice_in_dim(vector, offset + r * OWN, OWN, 0)[None, :]
    offset += DI
    taps = vector[offset : offset + (CONV + 1) * CHANNELS].reshape(CONV + 1, CHANNELS)
    offset += (CONV + 1) * CHANNELS
    per_head = vector[offset:].reshape(3, H)
    dt_bias, a_log, d_skip = lax.dynamic_slice_in_dim(per_head, r * OWN_H, OWN_H, 1)
    taps_bc = taps[:, DI:]
    conv_par = jnp.concatenate([lax.dynamic_slice_in_dim(taps, r * OWN, OWN, 1), taps_bc], 1)
    head_par = jnp.stack(
        [
            jnp.pad(jnp.broadcast_to(d_skip[:, None], (OWN_H, P_SIZE)).reshape(-1), (0, 2 * N)),
            jnp.pad(dt_bias, (0, 640 - OWN_H)),
            jnp.pad(-jnp.exp(a_log), (0, 640 - OWN_H)),
        ],
        0,
    )
    par = jnp.concatenate([conv_par, head_par, jnp.zeros((8, 640), F32)], 0)

    in_low, partner_far_top, partner_far_low, own_shards = lax.optimization_barrier(
        (in_low, partner_far_top, partner_far_low, own_shards)
    )
    full_out = gather_eight(tie(out_pair, own_shards))
    in_other = move(in_low, lambda yh, z, c, x, yl: (yh + 1, z, c, x, yl + 1))
    b_left = move(branch, along_x(1))
    b_right = move(branch, along_x(-1))
    b_partner = move(branch, swap_y)
    token_pieces = [
        tokens, partner, from_right, partner_right, far,
        partner_far_top, partner_far_low, from_left, partner_left,
    ]
    normed, proj, low_dt = run_project(ahead, token_pieces, gain_in, own_shards)
    b_left, b_right, b_partner, proj = lax.optimization_barrier((b_left, b_right, b_partner, proj))
    b_far = move(b_left, along_x(1))
    b_partner_left = move(b_left, swap_y)
    b_partner_right = move(b_partner, along_x(-1))
    before = run_forward(0, seg_ends, proj, par)
    b_far, b_partner_left, b_partner_right, before = lax.optimization_barrier(
        (b_far, b_partner_left, b_partner_right, before)
    )
    b_partner_far_top = move(b_partner_left[:half], along_x(1))
    b_partner_far_low = move(b_partner_right[half:], along_x(-1))
    pre, mixed, states, _ = run_forward(1, seg_ends, proj, par, before)
    mixed, in_low, in_other, b_partner_far_top, b_partner_far_low = lax.optimization_barrier(
        (mixed, in_low, in_other, b_partner_far_top, b_partner_far_low)
    )
    full_in = gather_eight(both(in_low, in_other, place.yh))
    branch_pieces = [
        branch, b_partner, b_right, b_partner_right, b_far,
        b_partner_far_top, b_partner_far_low, b_left, b_partner_left,
    ]
    rep_table = jnp.concatenate([ahead, r[None]])
    grad_branch, grad_normed_out, sums = run_out_grad(rep_table, branch_pieces, full_out, mixed, proj, gain_row)
    sums = share_rep(sums[:2].reshape(32, 128)).sum(0).reshape(2, PACK)
    sums = jnp.concatenate([sums, jnp.zeros((6, PACK), F32)], 0)

    low, grad_mixed, grad_gain = run_gate(grad_normed_out, mixed, proj, sums, gain_row)

    low_rows = exchange(low.reshape(N_REP, ROWS, 2 * OWN), "rep")
    grad_x, grad_dtraw, grad_bc, grad_sums, grad_heads = run_backward(
        seg_ends, proj, pre, mixed, grad_mixed, states, par
    )
    low_rows, low, grad_bc, grad_x = lax.optimization_barrier((low_rows, low, grad_bc, grad_x))

    grad_bc = exchange(grad_bc, "rep").reshape(N_REP, OWN_BC, PACK)
    early_grad = run_early_grad(low, grad_branch, normed)
    early_grad, low_rows = lax.optimization_barrier((early_grad, low_rows))
    early = scatter_eight(early_grad)
    grad_rows = run_z_grad(low_rows, full_in)
    grad_bc, grad_rows = lax.optimization_barrier((grad_bc, grad_rows))

    tail, small_own = run_rest(
        seg_ends, grad_bc, pre, proj, par, grad_x, grad_dtraw, grad_sums, grad_heads, grad_gain, (r * OWN_BC)[None]
    )
    grad_tail = run_tail_grad(normed, tail, small_own)
    tail, grad_tail, low_rows = lax.optimization_barrier((tail, grad_tail, low_rows))
    tail_rows = exchange(tail.reshape(N_REP, ROWS, TAIL), "rep")
    tail_part = scatter_eight(grad_tail)
    block_out = run_block_out(low_rows, full_out, tokens, own_live)
    early, block_out = lax.optimization_barrier((early, block_out))
    early, early_half = start_half(early, None, place)
    early, _ = end_half(early, early_half, None)
    out_part = move(
        early[:SHARD_IN],
        lambda yh, z, c, x, yl: (x // 2, (x % 2) * 2 + yl, z % 2, 2 * c + yh, z // 2),
    )
    early = jnp.concatenate([out_part, early[SHARD_IN:]], 0)
    tail_rows, early = lax.optimization_barrier((tail_rows, early))

    early_pair = both(early, move(early, swap_y), place.yl)
    input_grad, grad_gain_in = run_input_grad(
        grad_rows, tail_rows, full_in, low_dt, tokens, cotangent, gain_in
    )
    tail_part, input_grad, grad_gain_in, early_pair = lax.optimization_barrier(
        (tail_part, input_grad, grad_gain_in, early_pair)
    )

    tail_part, tail_half = start_half(tail_part, None, place)
    early_left, early_right = move(early_pair, along_x(1)), move(early_pair, along_x(-1))
    grad_gain_in = grad_gain_in + move(grad_gain_in, swap_core)
    tail_half, grad_gain_in, early_left, early_right = lax.optimization_barrier(
        (tail_half, grad_gain_in, early_left, early_right)
    )

    tail_part, _ = end_half(tail_part, tail_half, None)
    tail_parts = share_rep(tail_part)
    early_far = move(early_left[:1], along_x(1)), move(early_right[1:], along_x(-1))
    early_pairs = (early_pair, early_right, *early_far, early_left)
    grad_gain_in = sum_most(grad_gain_in)

    x_order = (place.x + jnp.arange(4, dtype=jnp.int32)) % 4
    grad_out, new_first_out, new_second_out, new_out = run_adam_pairs(
        x_order, lambda k: (k // 2, k % 2), slice(0, SHARD_IN), early_pairs, w_out, first_out, second_out
    )
    updated = run_adam_pairs(
        x_order, lambda k: (0, k), slice(SHARD_IN, 2 * SHARD_IN), early_pairs, w_in, first_in, second_in
    )
    grad_in, new_first_in, new_second_in, new_in = run_adam_tail(tail_parts, w_in, first_in, second_in, updated)

    def columns(parts):
        return parts.transpose(1, 0, 2).reshape(parts.shape[1], -1)

    grad_gain_in = grad_gain_in[: D // N].reshape(-1)
    small_parts = tail_parts[:, SHARD_IN:]
    small_x = small_parts[:, :, :OWN].transpose(1, 0, 2).reshape(8, DI)
    small_bc = small_parts[:, :, OWN:].transpose(1, 0, 2)

    def channels(row):
        return jnp.concatenate([small_x[row], small_bc[row, :, :OWN_BC].reshape(-1)])

    grad_small_all = jnp.concatenate(
        [grad_gain_in, small_x[0]]
        + [channels(row) for row in range(1, 6)]
        + [
            small_bc[0, :, :OWN_H].reshape(-1),
            small_parts[:, 6, :OWN_H].reshape(-1),
            small_parts[:, 7, :OWN_H].reshape(-1),
        ]
    )
    grad_small = lax.dynamic_slice_in_dim(grad_small_all, place.f * SHARD_SMALL, SHARD_SMALL, 0)
    grad_dt = columns(tail_parts[:, :SHARD_IN, OWN + OWN_BC : OWN + OWN_BC + OWN_H])
    new_dt, new_first_dt, new_second_dt = adam_update(
        w_dt, grad_dt, first_dt, second_dt, RATE_MATRIX, WEIGHT_DECAY
    )
    new_small, new_first_small, new_second_small = adam_update(
        small, grad_small, first_small, second_small, RATE_SMALL, 0.0
    )
    return (
        block_out,
        input_grad,
        grad_in,
        grad_dt,
        grad_out,
        grad_small,
        new_first_in,
        new_first_dt,
        new_first_out,
        new_first_small,
        new_second_in,
        new_second_dt,
        new_second_out,
        new_second_small,
        new_in,
        new_dt,
        new_out,
        new_small,
    )


def solution(mesh):
    rows = P(("fsdp", "rep"), None)
    matrix = P("fsdp", None)
    vector = P("fsdp")
    group = (matrix, matrix, matrix, vector)
    return jax.shard_map(
        body,
        mesh=mesh,
        in_specs=(rows, rows, P()) + group * 3,
        out_specs=(rows, rows) + group * 4,
        check_vma=False,
    )
```

```python
from functools import partial

import jax
import jax.numpy as jnp
from jax import lax
from jax.experimental import pallas as pl
from jax.experimental.pallas import tpu as pltpu
from jax.sharding import PartitionSpec as P

D = 1536
H = 48
P_SIZE = 64
N = 128
CONV = 4
STEP = 10
DI = 3072
CHANNELS = DI + 2 * N
SMALL = 21392
N_FSDP = 16
N_REP = 8
ROWS = 256
PACK = 2048
OWN = DI // N_REP
OWN_H = H // N_REP
OWN_BC = 2 * N // N_REP
SHARD_IN = D // N_FSDP
SHARD_OUT = DI // N_FSDP
SHARD_SMALL = SMALL // N_FSDP
WIDE = 384
CHUNK = 128
CHUNKS = PACK // CHUNK
HALF = CHUNKS // 2
TAIL = 512
VMEM_LIMIT = 60 * 1024 * 1024

NORM_EPS = 1e-05
BETA_ONE = 0.9
BETA_TWO = 0.999
ADAM_EPS = 1e-08
WEIGHT_DECAY = 0.1
RATE_MATRIX = 0.04
RATE_SMALL = 0.4
PRECISE = lax.Precision.HIGHEST
BF16 = jnp.bfloat16
F32 = jnp.float32
COST = pl.CostEstimate(flops=1_000_000, bytes_accessed=100_000, transcendentals=0)
FILL = pl.CostEstimate(flops=2_400_000_000, bytes_accessed=20_000_000, transcendentals=0)


def move(value, target):
    pairs = []
    for f in range(N_FSDP):
        for r in range(N_REP):
            yh, z, c, x, yl = target(f // 8, (f // 2) % 4, f % 2, r // 2, r % 2)
            pairs.append((f * N_REP + r, ((yh % 2) * 8 + (z % 4) * 2 + c % 2) * N_REP + (x % 4) * 2 + yl % 2))
    return lax.ppermute(value, ("fsdp", "rep"), pairs)


def along_x(steps):
    return lambda yh, z, c, x, yl: (yh, z, c, x + steps, yl)


def along_z(steps):
    return lambda yh, z, c, x, yl: (yh, z + steps, c, x, yl)


def swap_y(yh, z, c, x, yl):
    return (yh, z, c, x, yl + 1)


def swap_y_hi(yh, z, c, x, yl):
    return (yh + 1, z, c, x, yl)


def swap_core(yh, z, c, x, yl):
    return (yh, z, c + 1, x, yl)


class Place:
    def __init__(self):
        f = lax.axis_index("fsdp")
        r = lax.axis_index("rep")
        self.f, self.r = f, r
        self.yh, self.z, self.c = f // 8, (f // 2) % 4, f % 2
        self.x, self.yl = r // 2, r % 2


def at(value, index, axis=0):
    return lax.dynamic_index_in_dim(value, index, axis, keepdims=False)


def tie(values, *others):
    return lax.optimization_barrier((values, others))[0]


def both(mine, other, second):
    first = jnp.where(second == 0, mine, other)
    last = jnp.where(second == 0, other, mine)
    return jnp.stack([first, last], 0)


def put(out, piece, axis, index):
    starts = [jnp.int32(0)] * out.ndim
    starts[axis] = jnp.int32(index)
    return lax.dynamic_update_slice(out, jnp.expand_dims(piece, axis), tuple(starts))


def swap_shards(value, place):
    other = move(value, lambda yh, z, c, x, yl: (yh + 1, z, c, x, yl + 1))
    return both(value, other, place.yh)


def gather_eight(pair):
    groups = [list(range(8)), list(range(8, 16))]
    out = lax.all_gather(pair, "fsdp", axis=0, tiled=True, axis_index_groups=groups)
    return out.reshape((4, 2) + pair.shape)


def start_half(total, extra, place):
    return at(total, place.yh), move(with_rows(at(total, 1 - place.yh), extra), swap_y_hi)


def end_half(mine, other, extra):
    rows = mine.shape[0]
    return mine + other[:rows], None if extra is None else extra + other[rows:]


def exchange(value, axis):
    return lax.all_to_all(value, axis, 0, 0, tiled=True)


def share_rep(value):
    return exchange(jnp.broadcast_to(value[None], (N_REP,) + value.shape), "rep")


def sum_rep(value):
    value = value + move(value, swap_y)
    steps = [move(value, along_x(step)) for step in (1, 3, 2)]
    return value + steps[0] + steps[1] + steps[2]


def sum_z(value):
    steps = [move(value, along_z(step)) for step in (1, 3, 2)]
    return value + steps[0] + steps[1] + steps[2]


def scatter_eight(value):
    groups = [list(range(8)), list(range(8, 16))]
    flat = value.reshape(-1, value.shape[-1])
    out = lax.psum_scatter(flat, "fsdp", scatter_dimension=0, tiled=True, axis_index_groups=groups)
    return out.reshape((2,) + value.shape[1:])


def eight_order(f):
    return ((f // 2) % 4 * 2 + f % 2) * 2 + f // 8


def with_rows(block, extra):
    width = block.shape[-1]
    flat = block.reshape(-1, width)
    return flat if extra is None else jnp.concatenate([flat, extra], 0)


def adam_update(weight, gradient, moment_one, moment_two, learn_rate, decay_rate):
    moment_one = BETA_ONE * moment_one + (1.0 - BETA_ONE) * gradient
    moment_two = BETA_TWO * moment_two + (1.0 - BETA_TWO) * gradient * gradient
    scaled = (
        moment_one
        / (1.0 - BETA_ONE**STEP)
        / (jnp.sqrt(moment_two / (1.0 - BETA_TWO**STEP)) + ADAM_EPS)
    )
    return (weight - learn_rate * (scaled + decay_rate * weight), moment_one, moment_two)


def contract_rows(left_side, right_side):
    return lax.dot_general(
        left_side, right_side, (((0,), (0,)), ((), ())), preferred_element_type=F32
    )


def contract_cols(left_side, right_side):
    return lax.dot_general(
        left_side, right_side, (((1,), (1,)), ((), ())), preferred_element_type=F32
    )


def matmul(left_side, right_side):
    return jnp.dot(left_side, right_side, preferred_element_type=F32)


def segment_at(positions, seg_ends):
    counted = jnp.sum((positions[:, None] >= seg_ends[None, :]).astype(jnp.int32), axis=1)
    return jnp.where(positions < 0, jnp.int32(-1), counted)


def split_two(value):
    high = value.astype(BF16)
    return high, (value - high.astype(F32)).astype(BF16)


def split_three(value):
    high = value.astype(BF16)
    rest = value - high.astype(F32)
    middle = rest.astype(BF16)
    return high, middle, (rest - middle.astype(F32)).astype(BF16)


def product(left, right, left_dim, right_dim):
    return lax.dot_general(
        left, right, (((left_dim,), (right_dim,)), ((), ())), preferred_element_type=F32
    )


def joined_product(left_parts, right_parts, left_dim=1, right_dim=0):
    left_high, left_low = left_parts
    right_high, right_low = right_parts
    return product(
        jnp.concatenate([left_high, left_high, left_low], left_dim),
        jnp.concatenate([right_high, right_low, right_high], right_dim),
        left_dim,
        right_dim,
    )


def precise_product(left, right, left_dim=1, right_dim=0):
    return joined_product(split_two(left), split_two(right), left_dim, right_dim)


def ones_product(ones, value):
    return product(jnp.concatenate([ones] * 3, 1), jnp.concatenate(split_three(value), 0), 1, 0)


def spread(per_head, lane):
    return jnp.concatenate(
        [
            jnp.where(lane < P_SIZE, per_head[:, 2 * k : 2 * k + 1], per_head[:, 2 * k + 1 : 2 * k + 2])
            for k in range(OWN_H // 2)
        ],
        1,
    )


def head_sums(value):
    column = lax.broadcasted_iota(jnp.int32, (OWN, N), 0)
    head = lax.broadcasted_iota(jnp.int32, (OWN, N), 1)
    members = ((column >= head * P_SIZE) & (column < (head + 1) * P_SIZE)).astype(F32).astype(BF16)
    high, low = split_two(value)
    return product(jnp.concatenate([high, low], 1), jnp.concatenate([members, members], 0), 1, 0)


def two_heads(pair, lane):
    zero = jnp.zeros_like(pair)
    return jnp.concatenate([jnp.where(lane < P_SIZE, pair, zero), jnp.where(lane < P_SIZE, zero, pair)], 0)


def chunk_facts(ends, chunk, dt_pre, par):
    column = lax.broadcasted_iota(jnp.int32, (CHUNK, 1), 0) + chunk * CHUNK
    row = lax.broadcasted_iota(jnp.int32, (1, CHUNK), 1) + chunk * CHUNK

    def segment(position):
        counted = jnp.zeros_like(position)
        for k in range(3):
            counted = counted + (position >= ends[k]).astype(jnp.int32)
        return jnp.where(position < 0, -1, counted)

    def one_segment(position):
        counted = jnp.int32(0)
        for k in range(3):
            counted = counted + (position >= ends[k]).astype(jnp.int32)
        return jnp.where(position < 0, -1, counted)

    here_column, here_row = segment(column), segment(row)
    prior = one_segment(chunk * CHUNK - 1)
    last = one_segment(chunk * CHUNK + CHUNK - 1)
    lane = lax.broadcasted_iota(jnp.int32, (CHUNK, N), 1)
    shifted = dt_pre + par[6:7, :N]
    soft = jnp.maximum(shifted, 0.0) + jnp.log1p(jnp.exp(-jnp.abs(shifted)))
    step = jnp.where(lane < OWN_H, soft, 0.0)
    decay = step * par[7:8, :N]
    tri_row = lax.broadcasted_iota(jnp.int32, (CHUNK, CHUNK), 0)
    tri_column = lax.broadcasted_iota(jnp.int32, (CHUNK, CHUNK), 1)
    lower = (tri_row >= tri_column).astype(F32).astype(BF16)
    upper = (tri_row <= tri_column).astype(F32).astype(BF16)
    total = ones_product(lower, decay)
    entering = (here_column == prior).astype(F32) * jnp.exp(total)
    end = total[CHUNK - 1 : CHUNK]
    leaving = (here_column == last).astype(F32) * jnp.exp(jnp.minimum(end - total, 0.0))
    passing = jnp.where(last == prior, 1.0, 0.0) * jnp.exp(end)
    return dict(
        column=column,
        segment=segment,
        here_column=here_column,
        here_row=here_row,
        lane=lane,
        shifted=shifted,
        step=step,
        decay=decay,
        total=total,
        entering=entering,
        leaving=leaving,
        passing=passing,
        tri_row=tri_row,
        tri_column=tri_column,
        upper=upper,
    )


def forward_kernel(part, ends, proj, par, *refs):
    if part:
        carry_in, refs = refs[3], refs[4:]
    pre_out, mixed_out, state_out, carry_out, extended, state = refs
    chunk = pl.program_id(0) + part * HALF

    @pl.when(pl.program_id(0) == 0)
    def _():
        if part:
            state[...] = carry_in[:N, :OWN]
            extended[0:8, :] = carry_in[N:, :]
        else:
            state[...] = jnp.zeros_like(state)
            extended[0:8, :] = jnp.zeros((8, 640), F32)

    facts = chunk_facts(ends, chunk, proj[:, 1024:1152], par)
    lane = facts["lane"]
    conv = proj[:, OWN:1024].astype(BF16).astype(F32)
    extended[8 : 8 + CHUNK, :] = conv
    pre = par[4:5] + par[3:4] * conv
    for back in range(1, CONV):
        same = (facts["segment"](facts["column"] - back) == facts["here_column"]).astype(F32)
        pre = pre + par[3 - back : 4 - back] * (extended[8 - back : 8 - back + CHUNK, :] * same)
    extended[0:8, :] = extended[CHUNK : CHUNK + 8, :]
    pre_out[...] = pre
    act = pre * jax.nn.sigmoid(pre)
    own_x, state_b, state_c = act[:, :OWN], act[:, OWN : OWN + N], act[:, OWN + N :]
    stepped = own_x * spread(facts["step"], lane)
    b_parts, c_parts = split_two(state_b), split_two(state_c)
    inside = (facts["tri_row"] >= facts["tri_column"]) & (facts["here_column"] == facts["here_row"])
    scores = jnp.where(inside, joined_product(c_parts, b_parts, 1, 1), 0.0)
    total_rows = facts["total"].T
    state_in = state[...]
    state_out[...] = state_in
    outs = []
    for pair in range(OWN_H // 2):
        mixing = []
        for head in (2 * pair, 2 * pair + 1):
            span = facts["total"][:, head : head + 1] - total_rows[head : head + 1, :]
            mixing.append(jnp.exp(jnp.minimum(span, 0.0)) * scores)
        inner = two_heads(stepped[:, pair * N : pair * N + N], lane)
        outs.append(precise_product(jnp.concatenate(mixing, 1), inner))
    scanned = jnp.concatenate(outs, 1) + spread(facts["entering"], lane) * joined_product(
        c_parts, split_two(state_in)
    )
    state[...] = spread(facts["passing"], lane[:1]) * state_in + precise_product(
        state_b.T, stepped * spread(facts["leaving"], lane)
    )
    mixed_out[...] = scanned + par[5:6, :OWN] * own_x

    @pl.when(pl.program_id(0) == HALF - 1)
    def _():
        carry_out[:N, :OWN] = state[...]
        carry_out[:N, OWN:] = jnp.zeros((N, 640 - OWN), F32)
        carry_out[N:, :] = extended[0:8, :]


def run_forward(part, ends, proj, par, before=()):
    here = lambda i: (i + part * HALF, 0)
    chunked = lambda width: pl.BlockSpec((CHUNK, width), here)
    fixed = lambda shape: pl.BlockSpec(shape, lambda i: (0, 0))
    carry = fixed((N + 8, 640))
    return pl.pallas_call(
        partial(forward_kernel, part),
        grid=(HALF,),
        in_specs=[pl.BlockSpec(memory_space=pltpu.SMEM), chunked(1152), fixed((16, 640))]
        + ([pl.BlockSpec(memory_space=pl.ANY)] * 3 + [carry] if part else []),
        out_specs=[chunked(640), chunked(OWN), pl.BlockSpec((N, OWN), here), carry],
        out_shape=[
            jax.ShapeDtypeStruct((PACK, 640), F32),
            jax.ShapeDtypeStruct((PACK, OWN), F32),
            jax.ShapeDtypeStruct((CHUNKS * N, OWN), F32),
            jax.ShapeDtypeStruct((N + 8, 640), F32),
        ],
        input_output_aliases={3: 0, 4: 1, 5: 2} if part else {},
        scratch_shapes=[pltpu.VMEM((CHUNK + 8, 640), F32), pltpu.VMEM((N, OWN), F32)],
        compiler_params=pltpu.CompilerParams(
            dimension_semantics=("arbitrary",), vmem_limit_bytes=VMEM_LIMIT
        ),
        cost_estimate=COST,
        name="scan_forward",
    )(ends, proj, par, *before)


def backward_kernel(ends, conv_in, dt_in, pre_in, mixed_in, grad_mixed, state_all, par, *refs):
    grad_x, grad_dt, grad_bc, sums, head_acc, carried, extended, end_dot = refs
    step_index = pl.program_id(0)
    chunk = CHUNKS - 1 - step_index

    @pl.when(step_index == 0)
    def _():
        carried[...] = jnp.zeros_like(carried)
        extended[CHUNK : CHUNK + 8, :] = jnp.zeros((8, OWN), F32)
        end_dot[...] = jnp.zeros_like(end_dot)
        sums[...] = jnp.zeros_like(sums)
        head_acc[...] = jnp.zeros_like(head_acc)

    facts = chunk_facts(ends, chunk, dt_in[...], par)
    lane = facts["lane"]
    pre = pre_in[...]
    sig = jax.nn.sigmoid(pre)
    act = pre * sig
    own_x, state_b, state_c = act[:, :OWN], act[:, OWN : OWN + N], act[:, OWN + N :]
    step = facts["step"]
    step_wide = spread(step, lane)
    stepped = own_x * step_wide
    skip = par[5:6, :OWN]
    scanned = mixed_in[...] - skip * own_x
    grad_m = grad_mixed[...]
    sums[6:7] += jnp.sum(grad_m * own_x, 0, keepdims=True)

    b_parts, c_parts = split_two(state_b), split_two(state_c)
    inside = (facts["tri_row"] <= facts["tri_column"]) & (facts["here_column"] == facts["here_row"])
    scores = jnp.where(inside, joined_product(b_parts, c_parts, 1, 1), 0.0)
    total_rows = facts["total"].T
    grad_scores = jnp.zeros((CHUNK, CHUNK), F32)
    grad_stepped = []
    for pair in range(OWN_H // 2):
        columns = slice(pair * N, pair * N + N)
        grad_pair = grad_m[:, columns]
        high, low = split_two(grad_pair)
        stepped_parts = split_two(two_heads(stepped[:, columns], lane))
        grad_mixing = joined_product(stepped_parts, (high, low), 1, 1)
        mixing = []
        for k in range(2):
            head = 2 * pair + k
            span = total_rows[head : head + 1, :] - facts["total"][:, head : head + 1]
            decays = jnp.exp(jnp.minimum(span, 0.0))
            mixing.append(decays * scores)
            grad_scores = grad_scores + decays * grad_mixing[k * CHUNK : (k + 1) * CHUNK]
        grad_stepped.append(
            joined_product(
                split_two(jnp.concatenate(mixing, 1)), (two_heads(high, lane), two_heads(low, lane))
            )
        )
    grad_scores = jnp.where(inside, grad_scores, 0.0)
    carry = carried[...]
    carry_parts = split_two(carry)
    leaving = spread(facts["leaving"], lane)
    grad_stepped = jnp.concatenate(grad_stepped, 1) + leaving * joined_product(b_parts, carry_parts)
    state_in = state_all[...]
    entered = spread(facts["entering"], lane) * grad_m
    entered_parts = split_two(entered)
    grad_b = precise_product(grad_scores, state_c) + joined_product(
        split_two(leaving * stepped), carry_parts, 1, 1
    )
    grad_c = precise_product(grad_scores.T, state_b) + joined_product(
        entered_parts, split_two(state_in), 1, 1
    )
    grad_bc[0:N, :] = grad_b.T.astype(BF16)
    grad_bc[N:, :] = grad_c.T.astype(BF16)
    new_carry = spread(facts["passing"], lane[:1]) * carry + joined_product(
        split_two(state_c.T), entered_parts
    )
    carried[...] = new_carry

    grad_step = head_sums(own_x * grad_stepped)
    last_row = lax.broadcasted_iota(jnp.int32, (CHUNK, N), 0) == CHUNK - 1
    grad_total = head_sums(grad_m * scanned) - step * grad_step
    grad_total = grad_total + jnp.where(last_row, end_dot[0:1, :], 0.0)
    grad_decay = ones_product(facts["upper"], grad_total)
    end_dot[...] = head_sums(
        jnp.broadcast_to(jnp.sum(new_carry * state_in, 0, keepdims=True), (8, OWN))
    )
    grad_pre_dt = (grad_step + grad_decay * par[7:8, :N]) * jax.nn.sigmoid(facts["shifted"])
    grad_pre_dt = jnp.where(lane < OWN_H, grad_pre_dt, 0.0)
    grad_dt[...] = grad_pre_dt.astype(BF16)
    head_acc[0:1] += jnp.sum(grad_pre_dt, 0, keepdims=True)
    head_acc[1:2] += jnp.sum(grad_decay * facts["decay"], 0, keepdims=True)

    sig_x, pre_x = sig[:, :OWN], pre[:, :OWN]
    grad_pre = (step_wide * grad_stepped + skip * grad_m) * (sig_x * (1.0 + pre_x * (1.0 - sig_x)))
    extended[0:CHUNK, :] = grad_pre
    conv = conv_in[...].astype(BF16).astype(F32)
    sums[5:6] += jnp.sum(grad_pre, 0, keepdims=True)
    sums[4:5] += jnp.sum(conv * grad_pre, 0, keepdims=True)
    grad_conv = par[3:4, :OWN] * grad_pre
    for ahead in range(1, CONV):
        same = (facts["segment"](facts["column"] + ahead) == facts["here_column"]).astype(F32)
        later = extended[ahead : ahead + CHUNK, :] * same
        sums[4 - ahead : 5 - ahead] += jnp.sum(conv * later, 0, keepdims=True)
        grad_conv = grad_conv + par[3 - ahead : 4 - ahead, :OWN] * later
    extended[CHUNK : CHUNK + 8, :] = extended[0:8, :]
    grad_x[...] = grad_conv.astype(BF16)


def run_backward(ends, proj, pre, mixed, grad_mixed, states, par):
    last = CHUNKS - 1
    chunked = lambda width, column=0: pl.BlockSpec((CHUNK, width), lambda i: (last - i, column))
    fixed = lambda shape: pl.BlockSpec(shape, lambda i: (0, 0))
    return pl.pallas_call(
        backward_kernel,
        grid=(CHUNKS,),
        in_specs=[
            pl.BlockSpec(memory_space=pltpu.SMEM),
            chunked(OWN, 1),
            chunked(N, 8),
            chunked(640),
            chunked(OWN),
            chunked(OWN),
            pl.BlockSpec((N, OWN), lambda i: (last - i, 0)),
            fixed((16, 640)),
        ],
        out_specs=[
            chunked(OWN),
            chunked(N),
            pl.BlockSpec((2 * N, CHUNK), lambda i: (0, last - i)),
            fixed((8, OWN)),
            fixed((8, N)),
        ],
        out_shape=[
            jax.ShapeDtypeStruct((PACK, OWN), BF16),
            jax.ShapeDtypeStruct((PACK, N), BF16),
            jax.ShapeDtypeStruct((2 * N, PACK), BF16),
            jax.ShapeDtypeStruct((8, OWN), F32),
            jax.ShapeDtypeStruct((8, N), F32),
        ],
        scratch_shapes=[
            pltpu.VMEM((N, OWN), F32),
            pltpu.VMEM((CHUNK + 8, OWN), F32),
            pltpu.VMEM((8, N), F32),
        ],
        compiler_params=pltpu.CompilerParams(
            dimension_semantics=("arbitrary",), vmem_limit_bytes=VMEM_LIMIT
        ),
        cost_estimate=COST,
        name="scan_backward",
    )(ends, proj, proj, pre, mixed, grad_mixed, states, par)


PARTS = (1, 1, 1, 1, 1, 2, 1, 1)


def piece_copies(pieces, parts, blocks, sems):
    copies = []
    taken = 0
    for slot, count in enumerate(parts):
        rows = ROWS // count
        copies.append(
            [
                pltpu.make_async_copy(
                    pieces[taken + k], blocks.at[slot, pl.ds(k * rows, rows)], sems.at[taken + k]
                )
                for k in range(count)
            ]
        )
        taken += count
    return copies


def fetch_block(pieces, parts, blocks, sems):
    copies = piece_copies(pieces, parts, blocks, sems)
    step = pl.program_id(0)

    @pl.when(step == 0)
    def _():
        for group in copies:
            for copy in group:
                copy.start()

    for slot, group in enumerate(copies):

        @pl.when(step == slot)
        def _(group=group):
            for copy in group:
                copy.wait()

    return blocks[step]


def project_kernel(parts, table, *refs):
    pieces = refs[: sum(parts)]
    gain, shards, normed_out, proj, dt_out, blocks, weight, sems = refs[sum(parts) :]
    block = fetch_block(pieces, parts, blocks, sems)

    @pl.when(pl.program_id(0) == 0)
    def _():
        for f in range(N_FSDP):
            weight[f * SHARD_IN : (f + 1) * SHARD_IN, :] = shards[(f // 2) % 4, f % 2, f // 8, :SHARD_IN]
        dt_out[...] = weight[:, 1024:]

    values = block.astype(F32)
    scale = lax.rsqrt(jnp.mean(values * values, axis=1, keepdims=True) + NORM_EPS)
    normed = (values * scale * gain[...]).astype(BF16)
    normed_out[...] = normed
    proj[...] = matmul(normed, weight[...])


def run_project(table, pieces, gain, shards):
    fixed = lambda shape: pl.BlockSpec(shape, lambda i, table: (0,) * len(shape))
    placed = lambda width: pl.BlockSpec((ROWS, width), lambda i, table: (table[i], 0))
    return pl.pallas_call(
        partial(project_kernel, PARTS),
        grid_spec=pltpu.PrefetchScalarGridSpec(
            num_scalar_prefetch=1,
            grid=(N_REP,),
            in_specs=[pl.BlockSpec(memory_space=pl.ANY)] * len(pieces) + [fixed((1, D)), fixed(shards.shape)],
            out_specs=[placed(D), placed(3 * WIDE), fixed((D, N))],
            scratch_shapes=[
                pltpu.VMEM((N_REP, ROWS, D), BF16),
                pltpu.VMEM((D, 3 * WIDE), BF16),
                pltpu.SemaphoreType.DMA((len(pieces),)),
            ],
        ),
        out_shape=[
            jax.ShapeDtypeStruct((PACK, D), BF16),
            jax.ShapeDtypeStruct((PACK, 3 * WIDE), F32),
            jax.ShapeDtypeStruct((D, N), BF16),
        ],
        compiler_params=pltpu.CompilerParams(
            dimension_semantics=("arbitrary",), vmem_limit_bytes=VMEM_LIMIT
        ),
        cost_estimate=COST,
        name="project",
    )(table, *pieces, gain, shards)


def row_sums(value):
    folded = value[:, :N] + value[:, N : 2 * N] + value[:, 2 * N :]
    return jnp.sum(folded.T, 0, keepdims=True)


def out_grad_kernel(table, *refs):
    pieces = refs[: sum(PARTS)]
    w_out, mixed, gate_in, gain, branch_out, grad_out, sums, blocks, turned, sems = refs[sum(PARTS) :]
    branch = fetch_block(pieces, PARTS, blocks, sems)

    @pl.when(pl.program_id(0) == 0)
    def _():
        turned[...] = w_out[...].reshape(OWN, D).T

    branch_out[...] = branch
    total = matmul(branch, turned[...])
    grad_out[...] = total
    gate = gate_in[...]
    gated = mixed[...] * (gate * jax.nn.sigmoid(gate))
    row = lax.broadcasted_iota(jnp.int32, (8, ROWS), 0)
    sums[...] = jnp.where(
        row == 0, row_sums(gated * gated), jnp.where(row == 1, row_sums(total * gain[...] * gated), 0.0)
    )


def run_out_grad(table, pieces, w_out, mixed, proj, gain):
    fixed = lambda shape: pl.BlockSpec(shape, lambda i, table: (0, 0))
    placed = lambda width: pl.BlockSpec((ROWS, width), lambda i, table: (table[i], 0))
    own = pl.BlockSpec(
        (1, 2, 1, SHARD_OUT, D), lambda i, table: (table[N_REP] % 4, 0, table[N_REP] // 4, 0, 0)
    )
    return pl.pallas_call(
        out_grad_kernel,
        grid_spec=pltpu.PrefetchScalarGridSpec(
            num_scalar_prefetch=1,
            grid=(N_REP,),
            in_specs=[pl.BlockSpec(memory_space=pl.ANY)] * len(pieces)
            + [own, placed(OWN), placed(OWN), fixed((1, OWN))],
            out_specs=[placed(D), placed(OWN), pl.BlockSpec((8, ROWS), lambda i, table: (0, table[i]))],
            scratch_shapes=[
                pltpu.VMEM((N_REP, ROWS, D), BF16),
                pltpu.VMEM((D, WIDE), BF16),
                pltpu.SemaphoreType.DMA((len(pieces),)),
            ],
        ),
        out_shape=[
            jax.ShapeDtypeStruct((PACK, D), BF16),
            jax.ShapeDtypeStruct((PACK, OWN), F32),
            jax.ShapeDtypeStruct((8, PACK), F32),
        ],
        compiler_params=pltpu.CompilerParams(
            dimension_semantics=("arbitrary",), vmem_limit_bytes=VMEM_LIMIT
        ),
        cost_estimate=COST,
        name="out_grad",
    )(table, *pieces, w_out, mixed, proj, gain)


def gate_kernel(grad_out, mixed_in, gate_in, sums, gain, low_out, grad_mixed, grad_gain):
    rows = grad_out.shape[0]
    mixed, gate, grad_o = mixed_in[...], gate_in[...], grad_out[...]
    stats = jnp.concatenate([sums[...], jnp.zeros((N - 8, rows), F32)], 0).T
    out_scale = lax.rsqrt(stats[:, 0:1] * (1.0 / DI) + NORM_EPS)
    pull = out_scale * out_scale * out_scale * (stats[:, 1:2] * (1.0 / DI))
    gate_sig = jax.nn.sigmoid(gate)
    silu = gate * gate_sig
    gated = mixed * silu
    unit = gated * out_scale
    grad_gated = out_scale * (grad_o * gain[...]) - gated * pull
    grad_mixed[...] = grad_gated * silu
    low_out[:, :OWN] = (unit * gain[...]).astype(BF16)
    low_out[:, OWN:] = (grad_gated * mixed * (gate_sig * (1.0 + gate * (1.0 - gate_sig)))).astype(BF16)
    gain_part = jnp.sum(grad_o * unit, 0, keepdims=True)

    @pl.when(pl.program_id(0) == 0)
    def _():
        grad_gain[...] = jnp.broadcast_to(gain_part, grad_gain.shape)

    @pl.when(pl.program_id(0) > 0)
    def _():
        grad_gain[...] += gain_part


def run_gate(grad_out, mixed, proj, sums, gain):
    rows = lambda width: pl.BlockSpec((ROWS, width), lambda i: (i, 0))
    fixed = lambda shape: pl.BlockSpec(shape, lambda i: (0, 0))
    return pl.pallas_call(
        gate_kernel,
        grid=(PACK // ROWS,),
        in_specs=[
            rows(OWN),
            rows(OWN),
            rows(OWN),
            pl.BlockSpec((8, ROWS), lambda i: (0, i)),
            fixed((1, OWN)),
        ],
        out_specs=[rows(2 * OWN), rows(OWN), fixed((8, OWN))],
        out_shape=[
            jax.ShapeDtypeStruct((PACK, 2 * OWN), BF16),
            jax.ShapeDtypeStruct((PACK, OWN), F32),
            jax.ShapeDtypeStruct((8, OWN), F32),
        ],
        compiler_params=pltpu.CompilerParams(
            dimension_semantics=("arbitrary",), vmem_limit_bytes=VMEM_LIMIT
        ),
        cost_estimate=COST,
        name="gate_backward",
    )(grad_out, mixed, proj, sums, gain)


def early_grad_kernel(low, grad_branch, normed, out):
    step = pl.program_id(0)

    @pl.when(step == 0)
    def _():
        out[...] = jnp.zeros_like(out)

    for k in range(4):
        part = product(low[:, :OWN], grad_branch[:, k * WIDE : (k + 1) * WIDE], 0, 0)
        for m in range(4):
            out[eight_order(4 * k + m), :SHARD_IN] += part[m * SHARD_IN : (m + 1) * SHARD_IN]
    part = product(normed[...], low[:, OWN:], 0, 0)
    for f in range(N_FSDP):
        out[eight_order(f), SHARD_IN:] += part[f * SHARD_IN : (f + 1) * SHARD_IN]


def run_early_grad(low, grad_branch, normed):
    count = 2 * ROWS
    rows = lambda width: pl.BlockSpec((count, width), lambda i: (i, 0))
    shape = (N_FSDP, 2 * SHARD_IN, WIDE)
    return pl.pallas_call(
        early_grad_kernel,
        grid=(PACK // count,),
        in_specs=[rows(2 * OWN), rows(D), rows(D)],
        out_specs=pl.BlockSpec(shape, lambda i: (0, 0, 0)),
        out_shape=jax.ShapeDtypeStruct(shape, F32),
        compiler_params=pltpu.CompilerParams(
            dimension_semantics=("arbitrary",), vmem_limit_bytes=VMEM_LIMIT
        ),
        cost_estimate=COST,
        name="early_grad",
    )(low, grad_branch, normed)


def block_out_kernel(rows, weight, tokens, live, out):
    step = pl.program_id(0)
    part = matmul(jnp.concatenate([rows[0], rows[1]], 1), weight[...].reshape(2 * OWN, D))

    @pl.when(step == 0)
    def _():
        out[...] = part

    @pl.when(step > 0)
    def _():
        out[...] += part

    @pl.when(step == N_REP // 2 - 1)
    def _():
        out[...] = tokens[...].astype(F32) + live[...] * out[...]


def run_block_out(rows, weight, tokens, live):
    fixed = lambda shape: pl.BlockSpec(shape, lambda i: (0, 0))
    return pl.pallas_call(
        block_out_kernel,
        grid=(N_REP // 2,),
        in_specs=[
            pl.BlockSpec((2, ROWS, OWN), lambda i: (i, 0, 0)),
            pl.BlockSpec((2, 2, 1, SHARD_OUT, D), lambda i: (i % 2, 0, i // 2, 0, 0)),
            fixed((ROWS, D)),
            fixed((ROWS, 1)),
        ],
        out_specs=fixed((ROWS, D)),
        out_shape=jax.ShapeDtypeStruct((ROWS, D), F32),
        compiler_params=pltpu.CompilerParams(
            dimension_semantics=("arbitrary",), vmem_limit_bytes=VMEM_LIMIT
        ),
        cost_estimate=FILL,
        name="block_out",
    )(rows, weight, tokens, live)


def turned_part(weight, rows):
    return product(weight[...].reshape(D, weight.shape[-1]), rows, 1, 1)


def columns_of(full_in, width, index):
    return pl.BlockSpec(full_in.shape[:-1] + (width,), lambda i: (0, 0, 0, 0, index(i)))


def z_grad_kernel(rows, weight, out):
    part = turned_part(weight, jnp.concatenate([rows[0], rows[1]], 1))

    @pl.when(pl.program_id(0) == 0)
    def _():
        out[...] = part

    @pl.when(pl.program_id(0) > 0)
    def _():
        out[...] += part


def run_z_grad(rows, full_in):
    return pl.pallas_call(
        z_grad_kernel,
        grid=(N_REP // 2,),
        in_specs=[
            pl.BlockSpec((2, ROWS, OWN), lambda i: (i, 0, 1)),
            columns_of(full_in, 2 * OWN, lambda i: i),
        ],
        out_specs=pl.BlockSpec((D, ROWS), lambda i: (0, 0)),
        out_shape=jax.ShapeDtypeStruct((D, ROWS), F32),
        compiler_params=pltpu.CompilerParams(
            dimension_semantics=("arbitrary",), vmem_limit_bytes=VMEM_LIMIT
        ),
        cost_estimate=FILL,
        name="z_grad",
    )(rows, full_in)


def input_grad_kernel(
    grad_z, x_rows, rest_rows, w_x, w_bc, low_dt, tokens, cotangent, gain, out, gain_out, total, ordered
):
    step = pl.program_id(0)
    part = turned_part(w_x, jnp.concatenate([x_rows[0], x_rows[1]], 1))

    @pl.when(step == 0)
    def _():
        total[...] = grad_z[...] + part

    @pl.when(step > 0)
    def _():
        total[...] += part

    @pl.when(step == N_REP // 2 - 1)
    def _():
        lane = lax.broadcasted_iota(jnp.int32, (ROWS, N), 1)
        groups = []
        for k in range(2):
            group = jnp.zeros((ROWS, N), F32)
            for m in range(4):
                value = rest_rows[4 * k + m].astype(F32)
                value = value if m == 0 else pltpu.roll(value, m * OWN_BC, 1)
                group = jnp.where((lane >= m * OWN_BC) & (lane < (m + 1) * OWN_BC), value, group)
            groups.append(group.astype(BF16))
        steps = jnp.zeros((ROWS, N), F32)
        for m in range(N_REP):
            start = 8 + m * OWN_H
            value = pltpu.roll(rest_rows[m].astype(F32), (start - OWN_BC) % N, 1)
            steps = jnp.where((lane >= start) & (lane < start + OWN_H), value, steps)
        shared = total[...] + turned_part(w_bc, jnp.concatenate(groups, 1))
        for f in range(N_FSDP):
            start = eight_order(f) * SHARD_IN
            ordered[f * SHARD_IN : (f + 1) * SHARD_IN, :] = shared[start : start + SHARD_IN, :]
        grad_h = (ordered[...] + product(low_dt[...], steps.astype(BF16), 1, 1)).T
        values = tokens[...].astype(F32)
        scale = lax.rsqrt(jnp.mean(values * values, axis=1, keepdims=True) + NORM_EPS)
        unit = values * scale
        gain_sum = jnp.sum(grad_h * unit, 0, keepdims=True)
        gain_out[...] = jnp.zeros_like(gain_out)
        for k in range(D // N):
            gain_out[k : k + 1, :] = gain_sum[:, k * N : (k + 1) * N]
        grad_unit = grad_h * gain[...]
        inner = jnp.mean(grad_unit * unit, axis=1, keepdims=True)
        out[...] = cotangent[...].astype(F32) + scale * (grad_unit - unit * inner)


def run_input_grad(grad_z, tail_rows, full_in, low_dt, tokens, cotangent, gain):
    fixed = lambda shape: pl.BlockSpec(shape, lambda i: (0,) * len(shape))
    return pl.pallas_call(
        input_grad_kernel,
        grid=(N_REP // 2,),
        in_specs=[
            fixed((D, ROWS)),
            pl.BlockSpec((2, ROWS, OWN), lambda i: (i, 0, 0)),
            pl.BlockSpec((N_REP, ROWS, N), lambda i: (0, 0, OWN // N)),
            columns_of(full_in, 2 * OWN, lambda i: N_REP // 2 + i),
            columns_of(full_in, 2 * N, lambda i: DI // N),
            fixed((D, N)),
            fixed((ROWS, D)),
            fixed((ROWS, D)),
            fixed((1, D)),
        ],
        out_specs=[fixed((ROWS, D)), fixed((16, N))],
        out_shape=[jax.ShapeDtypeStruct((ROWS, D), F32), jax.ShapeDtypeStruct((16, N), F32)],
        scratch_shapes=[pltpu.VMEM((D, ROWS), F32), pltpu.VMEM((D, ROWS), F32)],
        compiler_params=pltpu.CompilerParams(
            dimension_semantics=("arbitrary",), vmem_limit_bytes=VMEM_LIMIT
        ),
        cost_estimate=COST,
        name="input_grad",
    )(grad_z, tail_rows, tail_rows, full_in, full_in, low_dt, tokens, cotangent, gain)


def rest_kernel(
    ends, parts, pre_b, pre_c, conv_in, par, grad_x, grad_dt, sums, head_acc, grad_gain, first, tail_out, small_out
):
    own = lax.broadcasted_iota(jnp.int32, (OWN_BC, 2 * N), 0) + first[0]
    chosen = (lax.broadcasted_iota(jnp.int32, (OWN_BC, 2 * N), 1) == own).astype(F32).astype(BF16)

    def pick(value):
        return product(jnp.concatenate([chosen] * 3, 1), jnp.concatenate(split_three(value), 1), 1, 1)

    grad = parts[0].astype(F32)
    for k in range(1, N_REP):
        grad = grad + parts[k].astype(F32)
    own_pre = pick(jnp.concatenate([pre_b[...], pre_c[...]], 1))
    own_conv = product(chosen, conv_in[...].astype(BF16), 1, 1)
    taps = pick(par[:, OWN:])
    sig = jax.nn.sigmoid(own_pre)
    grad_pre = grad * (sig * (1.0 + own_pre * (1.0 - sig)))
    position = lax.broadcasted_iota(jnp.int32, (1, PACK), 1)

    def segment(places):
        counted = jnp.zeros_like(places)
        for k in range(3):
            counted = counted + (places >= ends[k]).astype(jnp.int32)
        return counted

    grad_conv = taps[:, CONV - 1 : CONV] * grad_pre
    column = lax.broadcasted_iota(jnp.int32, (OWN_BC, N), 1)
    found = jnp.where(column == CONV, jnp.sum(grad_pre, 1, keepdims=True), 0.0)
    found = jnp.where(column == CONV - 1, jnp.sum(own_conv * grad_pre, 1, keepdims=True), found)
    for later_by in range(1, CONV):
        same = (segment(position + later_by) == segment(position)) & (position < PACK - later_by)
        later = jnp.where(same, pltpu.roll(grad_pre, PACK - later_by, 1), 0.0)
        tap = CONV - 1 - later_by
        found = jnp.where(column == tap, jnp.sum(own_conv * later, 1, keepdims=True), found)
        grad_conv = grad_conv + taps[:, tap : tap + 1] * later
    lane = lax.broadcasted_iota(jnp.int32, (N, N), 1)
    filler = jnp.zeros((N - OWN_BC, N), F32)
    for k in range(PACK // N):
        rows = slice(k * N, (k + 1) * N)
        columns = jnp.concatenate([grad_conv[:, rows], filler], 0).T
        steps = pltpu.roll(grad_dt[rows, :].astype(F32), OWN_BC, 1)
        tail_out[rows, :OWN] = grad_x[rows, :]
        tail_out[rows, OWN:] = jnp.where(
            lane < OWN_BC, columns, jnp.where(lane < OWN_BC + OWN_H, steps, 0.0)
        ).astype(BF16)
    row = lax.broadcasted_iota(jnp.int32, (8, OWN), 0)
    skip = head_sums(sums[...])
    by_head = jnp.concatenate([skip, jnp.zeros((8, OWN - N), F32)], 1)
    logs = jnp.concatenate([head_acc[...], jnp.zeros((8, OWN - N), F32)], 1)
    wide = jnp.where(row == 0, grad_gain[0:1, :], jnp.where(row < 6, sums[...], 0.0))
    wide = jnp.where(row == 6, logs[1:2, :], jnp.where(row == 7, by_head[6:7, :], wide))
    turned = jnp.concatenate([found, filler], 0).T
    first_row = lax.broadcasted_iota(jnp.int32, (8, N), 0) == 0
    small_out[:, :OWN] = wide
    small_out[:, OWN:] = jnp.where(first_row, head_acc[0:1, :], pltpu.roll(turned[:8], 1, 0))


def run_rest(ends, parts, pre, proj, par, grad_x, grad_dt, sums, head_acc, grad_gain, first):
    fixed = lambda shape: pl.BlockSpec(shape, lambda i: (0,) * len(shape))
    return pl.pallas_call(
        rest_kernel,
        grid=(1,),
        in_specs=[
            pl.BlockSpec(memory_space=pltpu.SMEM),
            fixed((N_REP, OWN_BC, PACK)),
            pl.BlockSpec((PACK, N), lambda i: (0, 3)),
            pl.BlockSpec((PACK, N), lambda i: (0, 4)),
            pl.BlockSpec((PACK, 2 * N), lambda i: (0, 3)),
            fixed((16, 640)),
            fixed((PACK, OWN)),
            fixed((PACK, N)),
            fixed((8, OWN)),
            fixed((8, N)),
            fixed((8, OWN)),
            pl.BlockSpec(memory_space=pltpu.SMEM),
        ],
        out_specs=[fixed((PACK, TAIL)), fixed((8, TAIL))],
        out_shape=[jax.ShapeDtypeStruct((PACK, TAIL), BF16), jax.ShapeDtypeStruct((8, TAIL), F32)],
        compiler_params=pltpu.CompilerParams(
            dimension_semantics=("arbitrary",), vmem_limit_bytes=VMEM_LIMIT
        ),
        cost_estimate=COST,
        name="rest_backward",
    )(ends, parts, pre, pre, proj, par, grad_x, grad_dt, sums, head_acc, grad_gain, first)


def tail_grad_kernel(normed, tail, small, out):
    step = pl.program_id(0)
    part = product(normed[...], tail[...], 0, 0)
    for f in range(N_FSDP):
        rows = part[f * SHARD_IN : (f + 1) * SHARD_IN]

        @pl.when(step == 0)
        def _(f=f, rows=rows):
            out[eight_order(f), :SHARD_IN] = rows
            out[eight_order(f), SHARD_IN:] = small[...]

        @pl.when(step > 0)
        def _(f=f, rows=rows):
            out[eight_order(f), :SHARD_IN] += rows


def run_tail_grad(normed, tail, small):
    count = 2 * ROWS
    shape = (N_FSDP, SHARD_IN + 8, TAIL)
    return pl.pallas_call(
        tail_grad_kernel,
        grid=(PACK // count,),
        in_specs=[
            pl.BlockSpec((count, D), lambda i: (i, 0)),
            pl.BlockSpec((count, TAIL), lambda i: (i, 0)),
            pl.BlockSpec((8, TAIL), lambda i: (0, 0)),
        ],
        out_specs=pl.BlockSpec(shape, lambda i: (0, 0, 0)),
        out_shape=jax.ShapeDtypeStruct(shape, F32),
        compiler_params=pltpu.CompilerParams(
            dimension_semantics=("arbitrary",), vmem_limit_bytes=VMEM_LIMIT
        ),
        cost_estimate=COST,
        name="tail_grad",
    )(normed, tail, small)


def adam_step(grad, weight, first, second, grad_out, first_out, second_out, weight_out):
    new_weight, new_first, new_second = adam_update(
        weight[...], grad, first[...], second[...], RATE_MATRIX, WEIGHT_DECAY
    )
    grad_out[...] = grad
    first_out[...] = new_first
    second_out[...] = new_second
    weight_out[...] = new_weight


def load_pair(step, pairs, rows, grad):
    pair, right, far_first, far_second, left = pairs
    for slot, (low, high) in enumerate(
        (((pair, 0), (pair, 1)), ((right, 0), (right, 1)), ((far_first, 0), (far_second, 0)), ((left, 0), (left, 1)))
    ):

        @pl.when(step == slot)
        def _(low=low, high=high):
            grad[:, :WIDE] = low[0][low[1], rows, :]
            grad[:, WIDE:] = high[0][high[1], rows, :]


def adam_pairs_kernel(rows, table, *refs):
    pairs, arrays, grad = refs[:5], refs[5:8] + refs[-5:-1], refs[-1]
    load_pair(pl.program_id(0), pairs, rows, grad)
    adam_step(grad[...], *arrays)


def run_adam_pairs(table, place_of, rows, pairs, weight, first, second):
    part = pl.BlockSpec((SHARD_IN, 2 * WIDE), lambda i, table: place_of(table[i]))
    shape = jax.ShapeDtypeStruct(weight.shape, F32)
    return pl.pallas_call(
        partial(adam_pairs_kernel, rows),
        grid_spec=pltpu.PrefetchScalarGridSpec(
            num_scalar_prefetch=1,
            grid=(4,),
            in_specs=[pl.BlockSpec(pair.shape, lambda i, table: (0, 0, 0)) for pair in pairs]
            + [part] * 3,
            out_specs=[part] * 4,
            scratch_shapes=[pltpu.VMEM((SHARD_IN, 2 * WIDE), F32)],
        ),
        out_shape=[shape] * 4,
        compiler_params=pltpu.CompilerParams(
            dimension_semantics=("arbitrary",), vmem_limit_bytes=VMEM_LIMIT
        ),
        cost_estimate=FILL,
        name="adam",
    )(table, *pairs, weight, first, second)


def adam_tail_kernel(pair, rest, *refs):
    arrays, grad = refs[:3] + refs[-5:-1], refs[-1]
    step = pl.program_id(0)

    @pl.when(step < N_REP // 2)
    def _():
        grad[:, :WIDE] = pair[0, :SHARD_IN]
        grad[:, WIDE:] = pair[1, :SHARD_IN]

    @pl.when(step == N_REP // 2)
    def _():
        lane = lax.broadcasted_iota(jnp.int32, (SHARD_IN, N), 1)
        for k in range(2):
            group = jnp.zeros((SHARD_IN, N), F32)
            for m in range(4):
                value = rest[4 * k + m, :SHARD_IN]
                value = value if m == 0 else pltpu.roll(value, m * OWN_BC, 1)
                group = jnp.where((lane >= m * OWN_BC) & (lane < (m + 1) * OWN_BC), value, group)
            grad[:, k * N : (k + 1) * N] = group

    adam_step(grad[...], *arrays)


def run_adam_tail(parts, weight, first, second, before):
    half = N_REP // 2
    rows = parts.shape[1]
    column = pl.BlockSpec((SHARD_IN, 2 * WIDE), lambda i: (0, half + i))
    shape = jax.ShapeDtypeStruct(weight.shape, F32)
    return pl.pallas_call(
        adam_tail_kernel,
        grid=(half + 1,),
        in_specs=[
            pl.BlockSpec((2, rows, OWN), lambda i: (jnp.minimum(i, half - 1), 0, 0)),
            pl.BlockSpec((N_REP, rows, N), lambda i: (0, 0, OWN // N)),
        ]
        + [column] * 3
        + [pl.BlockSpec(memory_space=pl.ANY)] * 4,
        out_specs=[column] * 4,
        out_shape=[shape] * 4,
        input_output_aliases={5 + k: k for k in range(4)},
        scratch_shapes=[pltpu.VMEM((SHARD_IN, 2 * WIDE), F32)],
        compiler_params=pltpu.CompilerParams(
            dimension_semantics=("arbitrary",), vmem_limit_bytes=VMEM_LIMIT
        ),
        cost_estimate=COST,
        name="adam_tail",
    )(parts, parts, weight, first, second, *before)


def body(
    tokens,
    cotangent,
    lengths,
    w_in,
    w_dt,
    w_out,
    small,
    first_in,
    first_dt,
    first_out,
    first_small,
    second_in,
    second_dt,
    second_out,
    second_small,
):
    place = Place()
    r = place.r
    zero = jnp.int32(0)
    pack_lengths = lax.dynamic_slice_in_dim(lengths, place.f, 1, 0)[0]
    seg_ends = jnp.cumsum(pack_lengths)
    own_positions = r * ROWS + jnp.arange(ROWS, dtype=jnp.int32)
    own_live = (segment_at(own_positions, seg_ends) < 3).astype(F32)[:, None]
    slots = jnp.arange(N_REP, dtype=jnp.int32)
    ahead = ((place.x + slots // 2) % 4) * 2 + (place.yl + slots) % 2
    half = ROWS // 2

    in_low = w_in.astype(BF16)
    dt_low = w_dt.astype(BF16)
    out_low = w_out.astype(BF16)

    small_rows = jnp.pad(small.astype(BF16), (0, 16 * 3 * WIDE - SHARD_SMALL)).reshape(16, 3 * WIDE)

    def own_columns(rep):
        columns = jnp.concatenate(
            [
                lax.dynamic_slice_in_dim(in_low, rep * OWN, OWN, 1),
                lax.dynamic_slice_in_dim(in_low, DI + rep * OWN, OWN, 1),
                in_low[:, 2 * DI :],
                lax.dynamic_slice_in_dim(dt_low, rep * OWN_H, OWN_H, 1),
                jnp.zeros((SHARD_IN, 2), BF16),
                dt_low,
                jnp.zeros((SHARD_IN, N - 8 - H), BF16),
            ],
            1,
        )
        return jnp.concatenate([columns, small_rows], 0)

    other_columns = move(
        own_columns(2 * place.x + 1 - place.yl), lambda yh, z, c, x, yl: (yh + 1, z, c, x, yl + 1)
    )
    from_left = move(tokens, along_x(1))
    from_right = move(tokens, along_x(-1))
    partner = move(tokens, swap_y)

    out_low, other_columns = lax.optimization_barrier((out_low, other_columns))
    out_other = move(out_low, lambda yh, z, c, x, yl: (yh + 1, z, c, x, yl + 1))
    from_left, from_right, partner, other_columns = lax.optimization_barrier(
        (from_left, from_right, partner, other_columns)
    )
    own_shards = gather_eight(both(own_columns(r), other_columns, place.yh))
    far = move(from_left, along_x(1))
    partner_left = move(from_left, swap_y)
    partner_right = move(partner, along_x(-1))

    branch = (cotangent.astype(F32) * own_live).astype(BF16)
    far, partner_left, partner_right, out_other, branch = lax.optimization_barrier(
        (far, partner_left, partner_right, out_other, branch)
    )
    out_pair = both(out_low, out_other, place.yh)
    partner_far_top = move(partner_left[:half], along_x(1))
    partner_far_low = move(partner_right[half:], along_x(-1))

    vector = own_shards[:, :, :, SHARD_IN : SHARD_IN + 2].transpose(2, 0, 1, 3, 4)
    vector = vector.reshape(N_FSDP, 6 * WIDE)[:, :SHARD_SMALL].reshape(-1).astype(F32)
    offset = 0
    gain_in = vector[None, :D]
    offset = D
    gain_row = lax.dynamic_slice_in_dim(vector, offset + r * OWN, OWN, 0)[None, :]
    offset += DI
    taps = vector[offset : offset + (CONV + 1) * CHANNELS].reshape(CONV + 1, CHANNELS)
    offset += (CONV + 1) * CHANNELS
    per_head = vector[offset:].reshape(3, H)
    dt_bias, a_log, d_skip = lax.dynamic_slice_in_dim(per_head, r * OWN_H, OWN_H, 1)
    taps_bc = taps[:, DI:]
    conv_par = jnp.concatenate([lax.dynamic_slice_in_dim(taps, r * OWN, OWN, 1), taps_bc], 1)
    head_par = jnp.stack(
        [
            jnp.pad(jnp.broadcast_to(d_skip[:, None], (OWN_H, P_SIZE)).reshape(-1), (0, 2 * N)),
            jnp.pad(dt_bias, (0, 640 - OWN_H)),
            jnp.pad(-jnp.exp(a_log), (0, 640 - OWN_H)),
        ],
        0,
    )
    par = jnp.concatenate([conv_par, head_par, jnp.zeros((8, 640), F32)], 0)

    in_low, partner_far_top, partner_far_low, own_shards = lax.optimization_barrier(
        (in_low, partner_far_top, partner_far_low, own_shards)
    )
    full_out = gather_eight(tie(out_pair, own_shards))
    in_other = move(in_low, lambda yh, z, c, x, yl: (yh + 1, z, c, x, yl + 1))
    b_left = move(branch, along_x(1))
    b_right = move(branch, along_x(-1))
    b_partner = move(branch, swap_y)
    token_pieces = [
        tokens, partner, from_right, partner_right, far,
        partner_far_top, partner_far_low, from_left, partner_left,
    ]
    normed, proj, low_dt = run_project(ahead, token_pieces, gain_in, own_shards)
    b_left, b_right, b_partner, proj = lax.optimization_barrier((b_left, b_right, b_partner, proj))
    b_far = move(b_left, along_x(1))
    b_partner_left = move(b_left, swap_y)
    b_partner_right = move(b_partner, along_x(-1))
    before = run_forward(0, seg_ends, proj, par)
    b_far, b_partner_left, b_partner_right, before = lax.optimization_barrier(
        (b_far, b_partner_left, b_partner_right, before)
    )
    b_partner_far_top = move(b_partner_left[:half], along_x(1))
    b_partner_far_low = move(b_partner_right[half:], along_x(-1))
    pre, mixed, states, _ = run_forward(1, seg_ends, proj, par, before)
    mixed, in_low, in_other, b_partner_far_top, b_partner_far_low = lax.optimization_barrier(
        (mixed, in_low, in_other, b_partner_far_top, b_partner_far_low)
    )
    full_in = gather_eight(both(in_low, in_other, place.yh))
    branch_pieces = [
        branch, b_partner, b_right, b_partner_right, b_far,
        b_partner_far_top, b_partner_far_low, b_left, b_partner_left,
    ]
    rep_table = jnp.concatenate([ahead, r[None]])
    grad_branch, grad_normed_out, sums = run_out_grad(rep_table, branch_pieces, full_out, mixed, proj, gain_row)
    sums = share_rep(sums[:2].reshape(32, 128)).sum(0).reshape(2, PACK)
    sums = jnp.concatenate([sums, jnp.zeros((6, PACK), F32)], 0)

    low, grad_mixed, grad_gain = run_gate(grad_normed_out, mixed, proj, sums, gain_row)

    low_rows = exchange(low.reshape(N_REP, ROWS, 2 * OWN), "rep")
    grad_x, grad_dtraw, grad_bc, grad_sums, grad_heads = run_backward(
        seg_ends, proj, pre, mixed, grad_mixed, states, par
    )
    low, grad_x = lax.optimization_barrier((low, grad_x))
    early_grad = run_early_grad(low, grad_branch, normed)
    low_rows, early_grad, grad_bc, grad_x = lax.optimization_barrier((low_rows, early_grad, grad_bc, grad_x))

    grad_bc = exchange(grad_bc, "rep").reshape(N_REP, OWN_BC, PACK)
    early = scatter_eight(early_grad)
    grad_rows = run_z_grad(low_rows, full_in)
    grad_bc, grad_rows = lax.optimization_barrier((grad_bc, grad_rows))

    tail, small_own = run_rest(
        seg_ends, grad_bc, pre, proj, par, grad_x, grad_dtraw, grad_sums, grad_heads, grad_gain, (r * OWN_BC)[None]
    )
    grad_tail = run_tail_grad(normed, tail, small_own)
    tail, grad_tail, low_rows = lax.optimization_barrier((tail, grad_tail, low_rows))
    tail_rows = exchange(tail.reshape(N_REP, ROWS, TAIL), "rep")
    block_out = run_block_out(low_rows, full_out, tokens, own_live)
    block_out, early, grad_tail = lax.optimization_barrier((block_out, early, grad_tail))
    tail_part = scatter_eight(grad_tail)
    tail_rows, early = lax.optimization_barrier((tail_rows, early))

    early, early_half = start_half(early, None, place)
    input_grad, grad_gain_in = run_input_grad(
        grad_rows, tail_rows, full_in, low_dt, tokens, cotangent, gain_in
    )
    input_grad, grad_gain_in, early_half = lax.optimization_barrier((input_grad, grad_gain_in, early_half))

    early, _ = end_half(early, early_half, None)
    out_part = move(
        early[:SHARD_IN],
        lambda yh, z, c, x, yl: (x // 2, (x % 2) * 2 + yl, z % 2, 2 * c + yh, z // 2),
    )
    grad_gain_in = grad_gain_in + move(grad_gain_in, swap_core)
    out_part, grad_gain_in = lax.optimization_barrier((out_part, grad_gain_in))
    early = jnp.concatenate([out_part, early[SHARD_IN:]], 0)
    early_pair = both(early, move(early, swap_y), place.yl)
    grad_gain_in = sum_z(grad_gain_in)
    tail_part, early_pair, grad_gain_in = lax.optimization_barrier((tail_part, early_pair, grad_gain_in))

    tail_part, tail_half = start_half(tail_part, None, place)
    early_left, early_right = move(early_pair, along_x(1)), move(early_pair, along_x(-1))
    grad_gain_in = grad_gain_in + move(grad_gain_in, swap_y_hi)
    tail_half, grad_gain_in = lax.optimization_barrier((tail_half, grad_gain_in))

    tail_part, _ = end_half(tail_part, tail_half, None)
    tail_parts = share_rep(tail_part)
    early_far = move(early_left[:1], along_x(1)), move(early_right[1:], along_x(-1))
    early_pairs = (early_pair, early_right, *early_far, early_left)
    grad_gain_in = sum_rep(grad_gain_in)

    x_order = (place.x + jnp.arange(4, dtype=jnp.int32)) % 4
    grad_out, new_first_out, new_second_out, new_out = run_adam_pairs(
        x_order, lambda k: (k // 2, k % 2), slice(0, SHARD_IN), early_pairs, w_out, first_out, second_out
    )
    updated = run_adam_pairs(
        x_order, lambda k: (0, k), slice(SHARD_IN, 2 * SHARD_IN), early_pairs, w_in, first_in, second_in
    )
    grad_in, new_first_in, new_second_in, new_in = run_adam_tail(tail_parts, w_in, first_in, second_in, updated)

    def columns(parts):
        return parts.transpose(1, 0, 2).reshape(parts.shape[1], -1)

    grad_gain_in = grad_gain_in[: D // N].reshape(-1)
    small_parts = tail_parts[:, SHARD_IN:]
    small_x = small_parts[:, :, :OWN].transpose(1, 0, 2).reshape(8, DI)
    small_bc = small_parts[:, :, OWN:].transpose(1, 0, 2)

    def channels(row):
        return jnp.concatenate([small_x[row], small_bc[row, :, :OWN_BC].reshape(-1)])

    grad_small_all = jnp.concatenate(
        [grad_gain_in, small_x[0]]
        + [channels(row) for row in range(1, 6)]
        + [
            small_bc[0, :, :OWN_H].reshape(-1),
            small_parts[:, 6, :OWN_H].reshape(-1),
            small_parts[:, 7, :OWN_H].reshape(-1),
        ]
    )
    grad_small = lax.dynamic_slice_in_dim(grad_small_all, place.f * SHARD_SMALL, SHARD_SMALL, 0)
    grad_dt = columns(tail_parts[:, :SHARD_IN, OWN + OWN_BC : OWN + OWN_BC + OWN_H])
    new_dt, new_first_dt, new_second_dt = adam_update(
        w_dt, grad_dt, first_dt, second_dt, RATE_MATRIX, WEIGHT_DECAY
    )
    new_small, new_first_small, new_second_small = adam_update(
        small, grad_small, first_small, second_small, RATE_SMALL, 0.0
    )
    return (
        block_out,
        input_grad,
        grad_in,
        grad_dt,
        grad_out,
        grad_small,
        new_first_in,
        new_first_dt,
        new_first_out,
        new_first_small,
        new_second_in,
        new_second_dt,
        new_second_out,
        new_second_small,
        new_in,
        new_dt,
        new_out,
        new_small,
    )


def solution(mesh):
    rows = P(("fsdp", "rep"), None)
    matrix = P("fsdp", None)
    vector = P("fsdp")
    group = (matrix, matrix, matrix, vector)
    return jax.shard_map(
        body,
        mesh=mesh,
        in_specs=(rows, rows, P()) + group * 3,
        out_specs=(rows, rows) + group * 4,
        check_vma=False,
    )
```

```python
from functools import partial

import jax
import jax.numpy as jnp
from jax import lax
from jax.experimental import pallas as pl
from jax.experimental.pallas import tpu as pltpu
from jax.sharding import PartitionSpec as P

D = 1536
H = 48
P_SIZE = 64
N = 128
CONV = 4
STEP = 10
DI = 3072
CHANNELS = DI + 2 * N
SMALL = 21392
N_FSDP = 16
N_REP = 8
ROWS = 256
PACK = 2048
OWN = DI // N_REP
OWN_H = H // N_REP
OWN_BC = 2 * N // N_REP
SHARD_IN = D // N_FSDP
SHARD_OUT = DI // N_FSDP
SHARD_SMALL = SMALL // N_FSDP
WIDE = 384
CHUNK = 128
CHUNKS = PACK // CHUNK
HALF = CHUNKS // 2
TAIL = 512
VMEM_LIMIT = 60 * 1024 * 1024

NORM_EPS = 1e-05
BETA_ONE = 0.9
BETA_TWO = 0.999
ADAM_EPS = 1e-08
WEIGHT_DECAY = 0.1
RATE_MATRIX = 0.04
RATE_SMALL = 0.4
PRECISE = lax.Precision.HIGHEST
BF16 = jnp.bfloat16
F32 = jnp.float32
COST = pl.CostEstimate(flops=1_000_000, bytes_accessed=100_000, transcendentals=0)
FILL = pl.CostEstimate(flops=2_400_000_000, bytes_accessed=20_000_000, transcendentals=0)


def move(value, target):
    pairs = []
    for f in range(N_FSDP):
        for r in range(N_REP):
            yh, z, c, x, yl = target(f // 8, (f // 2) % 4, f % 2, r // 2, r % 2)
            pairs.append((f * N_REP + r, ((yh % 2) * 8 + (z % 4) * 2 + c % 2) * N_REP + (x % 4) * 2 + yl % 2))
    return lax.ppermute(value, ("fsdp", "rep"), pairs)


def along_x(steps):
    return lambda yh, z, c, x, yl: (yh, z, c, x + steps, yl)


def along_z(steps):
    return lambda yh, z, c, x, yl: (yh, z + steps, c, x, yl)


def swap_y(yh, z, c, x, yl):
    return (yh, z, c, x, yl + 1)


def swap_y_hi(yh, z, c, x, yl):
    return (yh + 1, z, c, x, yl)


def swap_core(yh, z, c, x, yl):
    return (yh, z, c + 1, x, yl)


class Place:
    def __init__(self):
        f = lax.axis_index("fsdp")
        r = lax.axis_index("rep")
        self.f, self.r = f, r
        self.yh, self.z, self.c = f // 8, (f // 2) % 4, f % 2
        self.x, self.yl = r // 2, r % 2


def at(value, index, axis=0):
    return lax.dynamic_index_in_dim(value, index, axis, keepdims=False)


def tie(values, *others):
    return lax.optimization_barrier((values, others))[0]


def both(mine, other, second):
    first = jnp.where(second == 0, mine, other)
    last = jnp.where(second == 0, other, mine)
    return jnp.stack([first, last], 0)


def put(out, piece, axis, index):
    starts = [jnp.int32(0)] * out.ndim
    starts[axis] = jnp.int32(index)
    return lax.dynamic_update_slice(out, jnp.expand_dims(piece, axis), tuple(starts))


def swap_shards(value, place):
    other = move(value, lambda yh, z, c, x, yl: (yh + 1, z, c, x, yl + 1))
    return both(value, other, place.yh)


def gather_eight(pair):
    groups = [list(range(8)), list(range(8, 16))]
    out = lax.all_gather(pair, "fsdp", axis=0, tiled=True, axis_index_groups=groups)
    return out.reshape((4, 2) + pair.shape)


def exchange(value, axis):
    return lax.all_to_all(value, axis, 0, 0, tiled=True)


def share_rep(value):
    return exchange(jnp.broadcast_to(value[None], (N_REP,) + value.shape), "rep")


def sum_z(value):
    steps = [move(value, along_z(step)) for step in (1, 3, 2)]
    return value + steps[0] + steps[1] + steps[2]


def scatter_eight(value):
    groups = [list(range(8)), list(range(8, 16))]
    flat = value.reshape(-1, value.shape[-1])
    out = lax.psum_scatter(flat, "fsdp", scatter_dimension=0, tiled=True, axis_index_groups=groups)
    return out.reshape((2,) + value.shape[1:])


def eight_order(f):
    return ((f // 2) % 4 * 2 + f % 2) * 2 + f // 8


def with_rows(block, extra):
    width = block.shape[-1]
    flat = block.reshape(-1, width)
    return flat if extra is None else jnp.concatenate([flat, extra], 0)


def adam_update(weight, gradient, moment_one, moment_two, learn_rate, decay_rate):
    moment_one = BETA_ONE * moment_one + (1.0 - BETA_ONE) * gradient
    moment_two = BETA_TWO * moment_two + (1.0 - BETA_TWO) * gradient * gradient
    scaled = (
        moment_one
        / (1.0 - BETA_ONE**STEP)
        / (jnp.sqrt(moment_two / (1.0 - BETA_TWO**STEP)) + ADAM_EPS)
    )
    return (weight - learn_rate * (scaled + decay_rate * weight), moment_one, moment_two)


def contract_rows(left_side, right_side):
    return lax.dot_general(
        left_side, right_side, (((0,), (0,)), ((), ())), preferred_element_type=F32
    )


def contract_cols(left_side, right_side):
    return lax.dot_general(
        left_side, right_side, (((1,), (1,)), ((), ())), preferred_element_type=F32
    )


def matmul(left_side, right_side):
    return jnp.dot(left_side, right_side, preferred_element_type=F32)


def segment_at(positions, seg_ends):
    counted = jnp.sum((positions[:, None] >= seg_ends[None, :]).astype(jnp.int32), axis=1)
    return jnp.where(positions < 0, jnp.int32(-1), counted)


def split_two(value):
    high = value.astype(BF16)
    return high, (value - high.astype(F32)).astype(BF16)


def split_three(value):
    high = value.astype(BF16)
    rest = value - high.astype(F32)
    middle = rest.astype(BF16)
    return high, middle, (rest - middle.astype(F32)).astype(BF16)


def product(left, right, left_dim, right_dim):
    return lax.dot_general(
        left, right, (((left_dim,), (right_dim,)), ((), ())), preferred_element_type=F32
    )


def joined_product(left_parts, right_parts, left_dim=1, right_dim=0):
    left_high, left_low = left_parts
    right_high, right_low = right_parts
    return product(
        jnp.concatenate([left_high, left_high, left_low], left_dim),
        jnp.concatenate([right_high, right_low, right_high], right_dim),
        left_dim,
        right_dim,
    )


def precise_product(left, right, left_dim=1, right_dim=0):
    return joined_product(split_two(left), split_two(right), left_dim, right_dim)


def ones_product(ones, value):
    return product(jnp.concatenate([ones] * 3, 1), jnp.concatenate(split_three(value), 0), 1, 0)


def spread(per_head, lane):
    return jnp.concatenate(
        [
            jnp.where(lane < P_SIZE, per_head[:, 2 * k : 2 * k + 1], per_head[:, 2 * k + 1 : 2 * k + 2])
            for k in range(OWN_H // 2)
        ],
        1,
    )


def head_sums(value):
    column = lax.broadcasted_iota(jnp.int32, (OWN, N), 0)
    head = lax.broadcasted_iota(jnp.int32, (OWN, N), 1)
    members = ((column >= head * P_SIZE) & (column < (head + 1) * P_SIZE)).astype(F32).astype(BF16)
    high, low = split_two(value)
    return product(jnp.concatenate([high, low], 1), jnp.concatenate([members, members], 0), 1, 0)


def two_heads(pair, lane):
    zero = jnp.zeros_like(pair)
    return jnp.concatenate([jnp.where(lane < P_SIZE, pair, zero), jnp.where(lane < P_SIZE, zero, pair)], 0)


def chunk_facts(ends, chunk, dt_pre, par):
    column = lax.broadcasted_iota(jnp.int32, (CHUNK, 1), 0) + chunk * CHUNK
    row = lax.broadcasted_iota(jnp.int32, (1, CHUNK), 1) + chunk * CHUNK

    def segment(position):
        counted = jnp.zeros_like(position)
        for k in range(3):
            counted = counted + (position >= ends[k]).astype(jnp.int32)
        return jnp.where(position < 0, -1, counted)

    def one_segment(position):
        counted = jnp.int32(0)
        for k in range(3):
            counted = counted + (position >= ends[k]).astype(jnp.int32)
        return jnp.where(position < 0, -1, counted)

    here_column, here_row = segment(column), segment(row)
    prior = one_segment(chunk * CHUNK - 1)
    last = one_segment(chunk * CHUNK + CHUNK - 1)
    lane = lax.broadcasted_iota(jnp.int32, (CHUNK, N), 1)
    shifted = dt_pre + par[6:7, :N]
    soft = jnp.maximum(shifted, 0.0) + jnp.log1p(jnp.exp(-jnp.abs(shifted)))
    step = jnp.where(lane < OWN_H, soft, 0.0)
    decay = step * par[7:8, :N]
    tri_row = lax.broadcasted_iota(jnp.int32, (CHUNK, CHUNK), 0)
    tri_column = lax.broadcasted_iota(jnp.int32, (CHUNK, CHUNK), 1)
    lower = (tri_row >= tri_column).astype(F32).astype(BF16)
    upper = (tri_row <= tri_column).astype(F32).astype(BF16)
    total = ones_product(lower, decay)
    entering = (here_column == prior).astype(F32) * jnp.exp(total)
    end = total[CHUNK - 1 : CHUNK]
    leaving = (here_column == last).astype(F32) * jnp.exp(jnp.minimum(end - total, 0.0))
    passing = jnp.where(last == prior, 1.0, 0.0) * jnp.exp(end)
    return dict(
        column=column,
        segment=segment,
        here_column=here_column,
        here_row=here_row,
        lane=lane,
        shifted=shifted,
        step=step,
        decay=decay,
        total=total,
        entering=entering,
        leaving=leaving,
        passing=passing,
        tri_row=tri_row,
        tri_column=tri_column,
        upper=upper,
    )


def forward_kernel(part, ends, proj, par, *refs):
    if part:
        carry_in, refs = refs[3], refs[4:]
    pre_out, mixed_out, state_out, carry_out, extended, state = refs
    chunk = pl.program_id(0) + part * HALF

    @pl.when(pl.program_id(0) == 0)
    def _():
        if part:
            state[...] = carry_in[:N, :OWN]
            extended[0:8, :] = carry_in[N:, :]
        else:
            state[...] = jnp.zeros_like(state)
            extended[0:8, :] = jnp.zeros((8, 640), F32)

    facts = chunk_facts(ends, chunk, proj[:, 1024:1152], par)
    lane = facts["lane"]
    conv = proj[:, OWN:1024].astype(BF16).astype(F32)
    extended[8 : 8 + CHUNK, :] = conv
    pre = par[4:5] + par[3:4] * conv
    for back in range(1, CONV):
        same = (facts["segment"](facts["column"] - back) == facts["here_column"]).astype(F32)
        pre = pre + par[3 - back : 4 - back] * (extended[8 - back : 8 - back + CHUNK, :] * same)
    extended[0:8, :] = extended[CHUNK : CHUNK + 8, :]
    pre_out[...] = pre
    act = pre * jax.nn.sigmoid(pre)
    own_x, state_b, state_c = act[:, :OWN], act[:, OWN : OWN + N], act[:, OWN + N :]
    stepped = own_x * spread(facts["step"], lane)
    b_parts, c_parts = split_two(state_b), split_two(state_c)
    inside = (facts["tri_row"] >= facts["tri_column"]) & (facts["here_column"] == facts["here_row"])
    scores = jnp.where(inside, joined_product(c_parts, b_parts, 1, 1), 0.0)
    total_rows = facts["total"].T
    state_in = state[...]
    state_out[...] = state_in
    outs = []
    for pair in range(OWN_H // 2):
        mixing = []
        for head in (2 * pair, 2 * pair + 1):
            span = facts["total"][:, head : head + 1] - total_rows[head : head + 1, :]
            mixing.append(jnp.exp(jnp.minimum(span, 0.0)) * scores)
        inner = two_heads(stepped[:, pair * N : pair * N + N], lane)
        outs.append(precise_product(jnp.concatenate(mixing, 1), inner))
    scanned = jnp.concatenate(outs, 1) + spread(facts["entering"], lane) * joined_product(
        c_parts, split_two(state_in)
    )
    state[...] = spread(facts["passing"], lane[:1]) * state_in + precise_product(
        state_b.T, stepped * spread(facts["leaving"], lane)
    )
    mixed_out[...] = scanned + par[5:6, :OWN] * own_x

    @pl.when(pl.program_id(0) == HALF - 1)
    def _():
        carry_out[:N, :OWN] = state[...]
        carry_out[:N, OWN:] = jnp.zeros((N, 640 - OWN), F32)
        carry_out[N:, :] = extended[0:8, :]


def run_forward(part, ends, proj, par, before=()):
    here = lambda i: (i + part * HALF, 0)
    chunked = lambda width: pl.BlockSpec((CHUNK, width), here)
    fixed = lambda shape: pl.BlockSpec(shape, lambda i: (0, 0))
    carry = fixed((N + 8, 640))
    return pl.pallas_call(
        partial(forward_kernel, part),
        grid=(HALF,),
        in_specs=[pl.BlockSpec(memory_space=pltpu.SMEM), chunked(1152), fixed((16, 640))]
        + ([pl.BlockSpec(memory_space=pl.ANY)] * 3 + [carry] if part else []),
        out_specs=[chunked(640), chunked(OWN), pl.BlockSpec((N, OWN), here), carry],
        out_shape=[
            jax.ShapeDtypeStruct((PACK, 640), F32),
            jax.ShapeDtypeStruct((PACK, OWN), F32),
            jax.ShapeDtypeStruct((CHUNKS * N, OWN), F32),
            jax.ShapeDtypeStruct((N + 8, 640), F32),
        ],
        input_output_aliases={3: 0, 4: 1, 5: 2} if part else {},
        scratch_shapes=[pltpu.VMEM((CHUNK + 8, 640), F32), pltpu.VMEM((N, OWN), F32)],
        compiler_params=pltpu.CompilerParams(
            dimension_semantics=("arbitrary",), vmem_limit_bytes=VMEM_LIMIT
        ),
        cost_estimate=COST,
        name="scan_forward",
    )(ends, proj, par, *before)


def backward_kernel(ends, conv_in, dt_in, pre_in, mixed_in, grad_mixed, state_all, par, *refs):
    grad_x, grad_dt, grad_bc, sums, head_acc, carried, extended, end_dot = refs
    step_index = pl.program_id(0)
    chunk = CHUNKS - 1 - step_index

    @pl.when(step_index == 0)
    def _():
        carried[...] = jnp.zeros_like(carried)
        extended[CHUNK : CHUNK + 8, :] = jnp.zeros((8, OWN), F32)
        end_dot[...] = jnp.zeros_like(end_dot)
        sums[...] = jnp.zeros_like(sums)
        head_acc[...] = jnp.zeros_like(head_acc)

    facts = chunk_facts(ends, chunk, dt_in[...], par)
    lane = facts["lane"]
    pre = pre_in[...]
    sig = jax.nn.sigmoid(pre)
    act = pre * sig
    own_x, state_b, state_c = act[:, :OWN], act[:, OWN : OWN + N], act[:, OWN + N :]
    step = facts["step"]
    step_wide = spread(step, lane)
    stepped = own_x * step_wide
    skip = par[5:6, :OWN]
    scanned = mixed_in[...] - skip * own_x
    grad_m = grad_mixed[...]
    sums[6:7] += jnp.sum(grad_m * own_x, 0, keepdims=True)

    b_parts, c_parts = split_two(state_b), split_two(state_c)
    inside = (facts["tri_row"] <= facts["tri_column"]) & (facts["here_column"] == facts["here_row"])
    scores = jnp.where(inside, joined_product(b_parts, c_parts, 1, 1), 0.0)
    total_rows = facts["total"].T
    grad_scores = jnp.zeros((CHUNK, CHUNK), F32)
    grad_stepped = []
    for pair in range(OWN_H // 2):
        columns = slice(pair * N, pair * N + N)
        grad_pair = grad_m[:, columns]
        high, low = split_two(grad_pair)
        stepped_parts = split_two(two_heads(stepped[:, columns], lane))
        grad_mixing = joined_product(stepped_parts, (high, low), 1, 1)
        mixing = []
        for k in range(2):
            head = 2 * pair + k
            span = total_rows[head : head + 1, :] - facts["total"][:, head : head + 1]
            decays = jnp.exp(jnp.minimum(span, 0.0))
            mixing.append(decays * scores)
            grad_scores = grad_scores + decays * grad_mixing[k * CHUNK : (k + 1) * CHUNK]
        grad_stepped.append(
            joined_product(
                split_two(jnp.concatenate(mixing, 1)), (two_heads(high, lane), two_heads(low, lane))
            )
        )
    grad_scores = jnp.where(inside, grad_scores, 0.0)
    carry = carried[...]
    carry_parts = split_two(carry)
    leaving = spread(facts["leaving"], lane)
    grad_stepped = jnp.concatenate(grad_stepped, 1) + leaving * joined_product(b_parts, carry_parts)
    state_in = state_all[...]
    entered = spread(facts["entering"], lane) * grad_m
    entered_parts = split_two(entered)
    grad_b = precise_product(grad_scores, state_c) + joined_product(
        split_two(leaving * stepped), carry_parts, 1, 1
    )
    grad_c = precise_product(grad_scores.T, state_b) + joined_product(
        entered_parts, split_two(state_in), 1, 1
    )
    grad_bc[0:N, :] = grad_b.T.astype(BF16)
    grad_bc[N:, :] = grad_c.T.astype(BF16)
    new_carry = spread(facts["passing"], lane[:1]) * carry + joined_product(
        split_two(state_c.T), entered_parts
    )
    carried[...] = new_carry

    grad_step = head_sums(own_x * grad_stepped)
    last_row = lax.broadcasted_iota(jnp.int32, (CHUNK, N), 0) == CHUNK - 1
    grad_total = head_sums(grad_m * scanned) - step * grad_step
    grad_total = grad_total + jnp.where(last_row, end_dot[0:1, :], 0.0)
    grad_decay = ones_product(facts["upper"], grad_total)
    end_dot[...] = head_sums(
        jnp.broadcast_to(jnp.sum(new_carry * state_in, 0, keepdims=True), (8, OWN))
    )
    grad_pre_dt = (grad_step + grad_decay * par[7:8, :N]) * jax.nn.sigmoid(facts["shifted"])
    grad_pre_dt = jnp.where(lane < OWN_H, grad_pre_dt, 0.0)
    grad_dt[...] = grad_pre_dt.astype(BF16)
    head_acc[0:1] += jnp.sum(grad_pre_dt, 0, keepdims=True)
    head_acc[1:2] += jnp.sum(grad_decay * facts["decay"], 0, keepdims=True)

    sig_x, pre_x = sig[:, :OWN], pre[:, :OWN]
    grad_pre = (step_wide * grad_stepped + skip * grad_m) * (sig_x * (1.0 + pre_x * (1.0 - sig_x)))
    extended[0:CHUNK, :] = grad_pre
    conv = conv_in[...].astype(BF16).astype(F32)
    sums[5:6] += jnp.sum(grad_pre, 0, keepdims=True)
    sums[4:5] += jnp.sum(conv * grad_pre, 0, keepdims=True)
    grad_conv = par[3:4, :OWN] * grad_pre
    for ahead in range(1, CONV):
        same = (facts["segment"](facts["column"] + ahead) == facts["here_column"]).astype(F32)
        later = extended[ahead : ahead + CHUNK, :] * same
        sums[4 - ahead : 5 - ahead] += jnp.sum(conv * later, 0, keepdims=True)
        grad_conv = grad_conv + par[3 - ahead : 4 - ahead, :OWN] * later
    extended[CHUNK : CHUNK + 8, :] = extended[0:8, :]
    grad_x[...] = grad_conv.astype(BF16)


def run_backward(ends, proj, pre, mixed, grad_mixed, states, par):
    last = CHUNKS - 1
    chunked = lambda width, column=0: pl.BlockSpec((CHUNK, width), lambda i: (last - i, column))
    fixed = lambda shape: pl.BlockSpec(shape, lambda i: (0, 0))
    return pl.pallas_call(
        backward_kernel,
        grid=(CHUNKS,),
        in_specs=[
            pl.BlockSpec(memory_space=pltpu.SMEM),
            chunked(OWN, 1),
            chunked(N, 8),
            chunked(640),
            chunked(OWN),
            chunked(OWN),
            pl.BlockSpec((N, OWN), lambda i: (last - i, 0)),
            fixed((16, 640)),
        ],
        out_specs=[
            chunked(OWN),
            chunked(N),
            pl.BlockSpec((2 * N, CHUNK), lambda i: (0, last - i)),
            fixed((8, OWN)),
            fixed((8, N)),
        ],
        out_shape=[
            jax.ShapeDtypeStruct((PACK, OWN), BF16),
            jax.ShapeDtypeStruct((PACK, N), BF16),
            jax.ShapeDtypeStruct((2 * N, PACK), BF16),
            jax.ShapeDtypeStruct((8, OWN), F32),
            jax.ShapeDtypeStruct((8, N), F32),
        ],
        scratch_shapes=[
            pltpu.VMEM((N, OWN), F32),
            pltpu.VMEM((CHUNK + 8, OWN), F32),
            pltpu.VMEM((8, N), F32),
        ],
        compiler_params=pltpu.CompilerParams(
            dimension_semantics=("arbitrary",), vmem_limit_bytes=VMEM_LIMIT
        ),
        cost_estimate=COST,
        name="scan_backward",
    )(ends, proj, proj, pre, mixed, grad_mixed, states, par)


PARTS = (1, 1, 1, 1, 1, 2, 1, 1)


def piece_copies(pieces, parts, blocks, sems):
    copies = []
    taken = 0
    for slot, count in enumerate(parts):
        rows = ROWS // count
        copies.append(
            [
                pltpu.make_async_copy(
                    pieces[taken + k], blocks.at[slot, pl.ds(k * rows, rows)], sems.at[taken + k]
                )
                for k in range(count)
            ]
        )
        taken += count
    return copies


def fetch_block(pieces, parts, blocks, sems):
    copies = piece_copies(pieces, parts, blocks, sems)
    step = pl.program_id(0)

    @pl.when(step == 0)
    def _():
        for group in copies:
            for copy in group:
                copy.start()

    for slot, group in enumerate(copies):

        @pl.when(step == slot)
        def _(group=group):
            for copy in group:
                copy.wait()

    return blocks[step]


def project_kernel(parts, table, *refs):
    pieces = refs[: sum(parts)]
    gain, shards, normed_out, proj, dt_out, blocks, weight, sems = refs[sum(parts) :]
    block = fetch_block(pieces, parts, blocks, sems)

    @pl.when(pl.program_id(0) == 0)
    def _():
        for f in range(N_FSDP):
            weight[f * SHARD_IN : (f + 1) * SHARD_IN, :] = shards[(f // 2) % 4, f % 2, f // 8, :SHARD_IN]
        dt_out[...] = weight[:, 1024:]

    values = block.astype(F32)
    scale = lax.rsqrt(jnp.mean(values * values, axis=1, keepdims=True) + NORM_EPS)
    normed = (values * scale * gain[...]).astype(BF16)
    normed_out[...] = normed
    proj[...] = matmul(normed, weight[...])


def run_project(table, pieces, gain, shards):
    fixed = lambda shape: pl.BlockSpec(shape, lambda i, table: (0,) * len(shape))
    placed = lambda width: pl.BlockSpec((ROWS, width), lambda i, table: (table[i], 0))
    return pl.pallas_call(
        partial(project_kernel, PARTS),
        grid_spec=pltpu.PrefetchScalarGridSpec(
            num_scalar_prefetch=1,
            grid=(N_REP,),
            in_specs=[pl.BlockSpec(memory_space=pl.ANY)] * len(pieces) + [fixed((1, D)), fixed(shards.shape)],
            out_specs=[placed(D), placed(3 * WIDE), fixed((D, N))],
            scratch_shapes=[
                pltpu.VMEM((N_REP, ROWS, D), BF16),
                pltpu.VMEM((D, 3 * WIDE), BF16),
                pltpu.SemaphoreType.DMA((len(pieces),)),
            ],
        ),
        out_shape=[
            jax.ShapeDtypeStruct((PACK, D), BF16),
            jax.ShapeDtypeStruct((PACK, 3 * WIDE), F32),
            jax.ShapeDtypeStruct((D, N), BF16),
        ],
        compiler_params=pltpu.CompilerParams(
            dimension_semantics=("arbitrary",), vmem_limit_bytes=VMEM_LIMIT
        ),
        cost_estimate=COST,
        name="project",
    )(table, *pieces, gain, shards)


def row_sums(value):
    folded = value[:, :N] + value[:, N : 2 * N] + value[:, 2 * N :]
    return jnp.sum(folded.T, 0, keepdims=True)


def out_grad_kernel(table, *refs):
    pieces = refs[: sum(PARTS)]
    w_out, mixed, gate_in, gain, branch_out, grad_out, sums, blocks, turned, sems = refs[sum(PARTS) :]
    branch = fetch_block(pieces, PARTS, blocks, sems)

    @pl.when(pl.program_id(0) == 0)
    def _():
        turned[...] = w_out[...].reshape(OWN, D).T

    branch_out[...] = branch
    total = matmul(branch, turned[...])
    grad_out[...] = total
    gate = gate_in[...]
    gated = mixed[...] * (gate * jax.nn.sigmoid(gate))
    row = lax.broadcasted_iota(jnp.int32, (8, ROWS), 0)
    sums[...] = jnp.where(
        row == 0, row_sums(gated * gated), jnp.where(row == 1, row_sums(total * gain[...] * gated), 0.0)
    )


def run_out_grad(table, pieces, w_out, mixed, proj, gain):
    fixed = lambda shape: pl.BlockSpec(shape, lambda i, table: (0, 0))
    placed = lambda width: pl.BlockSpec((ROWS, width), lambda i, table: (table[i], 0))
    own = pl.BlockSpec(
        (1, 2, 1, SHARD_OUT, D), lambda i, table: (table[N_REP] % 4, 0, table[N_REP] // 4, 0, 0)
    )
    return pl.pallas_call(
        out_grad_kernel,
        grid_spec=pltpu.PrefetchScalarGridSpec(
            num_scalar_prefetch=1,
            grid=(N_REP,),
            in_specs=[pl.BlockSpec(memory_space=pl.ANY)] * len(pieces)
            + [own, placed(OWN), placed(OWN), fixed((1, OWN))],
            out_specs=[placed(D), placed(OWN), pl.BlockSpec((8, ROWS), lambda i, table: (0, table[i]))],
            scratch_shapes=[
                pltpu.VMEM((N_REP, ROWS, D), BF16),
                pltpu.VMEM((D, WIDE), BF16),
                pltpu.SemaphoreType.DMA((len(pieces),)),
            ],
        ),
        out_shape=[
            jax.ShapeDtypeStruct((PACK, D), BF16),
            jax.ShapeDtypeStruct((PACK, OWN), F32),
            jax.ShapeDtypeStruct((8, PACK), F32),
        ],
        compiler_params=pltpu.CompilerParams(
            dimension_semantics=("arbitrary",), vmem_limit_bytes=VMEM_LIMIT
        ),
        cost_estimate=COST,
        name="out_grad",
    )(table, *pieces, w_out, mixed, proj, gain)


def gate_kernel(grad_out, mixed_in, gate_in, sums, gain, low_out, grad_mixed, grad_gain):
    rows = grad_out.shape[0]
    mixed, gate, grad_o = mixed_in[...], gate_in[...], grad_out[...]
    stats = jnp.concatenate([sums[...], jnp.zeros((N - 8, rows), F32)], 0).T
    out_scale = lax.rsqrt(stats[:, 0:1] * (1.0 / DI) + NORM_EPS)
    pull = out_scale * out_scale * out_scale * (stats[:, 1:2] * (1.0 / DI))
    gate_sig = jax.nn.sigmoid(gate)
    silu = gate * gate_sig
    gated = mixed * silu
    unit = gated * out_scale
    grad_gated = out_scale * (grad_o * gain[...]) - gated * pull
    grad_mixed[...] = grad_gated * silu
    low_out[:, :OWN] = (unit * gain[...]).astype(BF16)
    low_out[:, OWN:] = (grad_gated * mixed * (gate_sig * (1.0 + gate * (1.0 - gate_sig)))).astype(BF16)
    gain_part = jnp.sum(grad_o * unit, 0, keepdims=True)

    @pl.when(pl.program_id(0) == 0)
    def _():
        grad_gain[...] = jnp.broadcast_to(gain_part, grad_gain.shape)

    @pl.when(pl.program_id(0) > 0)
    def _():
        grad_gain[...] += gain_part


def run_gate(grad_out, mixed, proj, sums, gain):
    rows = lambda width: pl.BlockSpec((ROWS, width), lambda i: (i, 0))
    fixed = lambda shape: pl.BlockSpec(shape, lambda i: (0, 0))
    return pl.pallas_call(
        gate_kernel,
        grid=(PACK // ROWS,),
        in_specs=[
            rows(OWN),
            rows(OWN),
            rows(OWN),
            pl.BlockSpec((8, ROWS), lambda i: (0, i)),
            fixed((1, OWN)),
        ],
        out_specs=[rows(2 * OWN), rows(OWN), fixed((8, OWN))],
        out_shape=[
            jax.ShapeDtypeStruct((PACK, 2 * OWN), BF16),
            jax.ShapeDtypeStruct((PACK, OWN), F32),
            jax.ShapeDtypeStruct((8, OWN), F32),
        ],
        compiler_params=pltpu.CompilerParams(
            dimension_semantics=("arbitrary",), vmem_limit_bytes=VMEM_LIMIT
        ),
        cost_estimate=COST,
        name="gate_backward",
    )(grad_out, mixed, proj, sums, gain)


def early_grad_kernel(low, grad_branch, normed, out):
    step = pl.program_id(0)

    @pl.when(step == 0)
    def _():
        out[...] = jnp.zeros_like(out)

    for k in range(4):
        part = product(low[:, :OWN], grad_branch[:, k * WIDE : (k + 1) * WIDE], 0, 0)
        for m in range(4):
            out[eight_order(4 * k + m), :SHARD_IN] += part[m * SHARD_IN : (m + 1) * SHARD_IN]
    part = product(normed[...], low[:, OWN:], 0, 0)
    for f in range(N_FSDP):
        out[eight_order(f), SHARD_IN:] += part[f * SHARD_IN : (f + 1) * SHARD_IN]


def run_early_grad(low, grad_branch, normed):
    count = 2 * ROWS
    rows = lambda width: pl.BlockSpec((count, width), lambda i: (i, 0))
    shape = (N_FSDP, 2 * SHARD_IN, WIDE)
    return pl.pallas_call(
        early_grad_kernel,
        grid=(PACK // count,),
        in_specs=[rows(2 * OWN), rows(D), rows(D)],
        out_specs=pl.BlockSpec(shape, lambda i: (0, 0, 0)),
        out_shape=jax.ShapeDtypeStruct(shape, F32),
        compiler_params=pltpu.CompilerParams(
            dimension_semantics=("arbitrary",), vmem_limit_bytes=VMEM_LIMIT
        ),
        cost_estimate=COST,
        name="early_grad",
    )(low, grad_branch, normed)


def block_out_kernel(rows, weight, tokens, live, out):
    step = pl.program_id(0)
    part = matmul(jnp.concatenate([rows[0], rows[1]], 1), weight[...].reshape(2 * OWN, D))

    @pl.when(step == 0)
    def _():
        out[...] = part

    @pl.when(step > 0)
    def _():
        out[...] += part

    @pl.when(step == N_REP // 2 - 1)
    def _():
        out[...] = tokens[...].astype(F32) + live[...] * out[...]


def run_block_out(rows, weight, tokens, live):
    fixed = lambda shape: pl.BlockSpec(shape, lambda i: (0, 0))
    return pl.pallas_call(
        block_out_kernel,
        grid=(N_REP // 2,),
        in_specs=[
            pl.BlockSpec((2, ROWS, OWN), lambda i: (i, 0, 0)),
            pl.BlockSpec((2, 2, 1, SHARD_OUT, D), lambda i: (i % 2, 0, i // 2, 0, 0)),
            fixed((ROWS, D)),
            fixed((ROWS, 1)),
        ],
        out_specs=fixed((ROWS, D)),
        out_shape=jax.ShapeDtypeStruct((ROWS, D), F32),
        compiler_params=pltpu.CompilerParams(
            dimension_semantics=("arbitrary",), vmem_limit_bytes=VMEM_LIMIT
        ),
        cost_estimate=FILL,
        name="block_out",
    )(rows, weight, tokens, live)


def turned_part(weight, rows):
    return product(weight[...].reshape(D, weight.shape[-1]), rows, 1, 1)


def columns_of(full_in, width, index):
    return pl.BlockSpec(full_in.shape[:-1] + (width,), lambda i: (0, 0, 0, 0, index(i)))


def z_grad_kernel(rows, weight, out):
    part = turned_part(weight, jnp.concatenate([rows[0], rows[1]], 1))

    @pl.when(pl.program_id(0) == 0)
    def _():
        out[...] = part

    @pl.when(pl.program_id(0) > 0)
    def _():
        out[...] += part


def run_z_grad(rows, full_in):
    return pl.pallas_call(
        z_grad_kernel,
        grid=(N_REP // 2,),
        in_specs=[
            pl.BlockSpec((2, ROWS, OWN), lambda i: (i, 0, 1)),
            columns_of(full_in, 2 * OWN, lambda i: i),
        ],
        out_specs=pl.BlockSpec((D, ROWS), lambda i: (0, 0)),
        out_shape=jax.ShapeDtypeStruct((D, ROWS), F32),
        compiler_params=pltpu.CompilerParams(
            dimension_semantics=("arbitrary",), vmem_limit_bytes=VMEM_LIMIT
        ),
        cost_estimate=FILL,
        name="z_grad",
    )(rows, full_in)


def input_grad_kernel(
    grad_z, x_rows, rest_rows, w_x, w_bc, low_dt, tokens, cotangent, gain, out, gain_out, total, ordered
):
    step = pl.program_id(0)
    part = turned_part(w_x, jnp.concatenate([x_rows[0], x_rows[1]], 1))

    @pl.when(step == 0)
    def _():
        total[...] = grad_z[...] + part

    @pl.when(step > 0)
    def _():
        total[...] += part

    @pl.when(step == N_REP // 2 - 1)
    def _():
        lane = lax.broadcasted_iota(jnp.int32, (ROWS, N), 1)
        groups = []
        for k in range(2):
            group = jnp.zeros((ROWS, N), F32)
            for m in range(4):
                value = rest_rows[4 * k + m].astype(F32)
                value = value if m == 0 else pltpu.roll(value, m * OWN_BC, 1)
                group = jnp.where((lane >= m * OWN_BC) & (lane < (m + 1) * OWN_BC), value, group)
            groups.append(group.astype(BF16))
        steps = jnp.zeros((ROWS, N), F32)
        for m in range(N_REP):
            start = 8 + m * OWN_H
            value = pltpu.roll(rest_rows[m].astype(F32), (start - OWN_BC) % N, 1)
            steps = jnp.where((lane >= start) & (lane < start + OWN_H), value, steps)
        shared = total[...] + turned_part(w_bc, jnp.concatenate(groups, 1))
        for f in range(N_FSDP):
            start = eight_order(f) * SHARD_IN
            ordered[f * SHARD_IN : (f + 1) * SHARD_IN, :] = shared[start : start + SHARD_IN, :]
        grad_h = (ordered[...] + product(low_dt[...], steps.astype(BF16), 1, 1)).T
        values = tokens[...].astype(F32)
        scale = lax.rsqrt(jnp.mean(values * values, axis=1, keepdims=True) + NORM_EPS)
        unit = values * scale
        gain_sum = jnp.sum(grad_h * unit, 0, keepdims=True)
        gain_out[...] = jnp.zeros_like(gain_out)
        for k in range(D // TAIL):
            gain_out[k : k + 1, :] = gain_sum[:, k * TAIL : (k + 1) * TAIL]
        grad_unit = grad_h * gain[...]
        inner = jnp.mean(grad_unit * unit, axis=1, keepdims=True)
        out[...] = cotangent[...].astype(F32) + scale * (grad_unit - unit * inner)


def run_input_grad(grad_z, tail_rows, full_in, low_dt, tokens, cotangent, gain):
    fixed = lambda shape: pl.BlockSpec(shape, lambda i: (0,) * len(shape))
    return pl.pallas_call(
        input_grad_kernel,
        grid=(N_REP // 2,),
        in_specs=[
            fixed((D, ROWS)),
            pl.BlockSpec((2, ROWS, OWN), lambda i: (i, 0, 0)),
            pl.BlockSpec((N_REP, ROWS, N), lambda i: (0, 0, OWN // N)),
            columns_of(full_in, 2 * OWN, lambda i: N_REP // 2 + i),
            columns_of(full_in, 2 * N, lambda i: DI // N),
            fixed((D, N)),
            fixed((ROWS, D)),
            fixed((ROWS, D)),
            fixed((1, D)),
        ],
        out_specs=[fixed((ROWS, D)), fixed((8, TAIL))],
        out_shape=[jax.ShapeDtypeStruct((ROWS, D), F32), jax.ShapeDtypeStruct((8, TAIL), F32)],
        scratch_shapes=[pltpu.VMEM((D, ROWS), F32), pltpu.VMEM((D, ROWS), F32)],
        compiler_params=pltpu.CompilerParams(
            dimension_semantics=("arbitrary",), vmem_limit_bytes=VMEM_LIMIT
        ),
        cost_estimate=COST,
        name="input_grad",
    )(grad_z, tail_rows, tail_rows, full_in, full_in, low_dt, tokens, cotangent, gain)


def rest_kernel(
    ends, parts, pre_b, pre_c, conv_in, par, grad_x, grad_dt, sums, head_acc, grad_gain, first, tail_out, small_out
):
    own = lax.broadcasted_iota(jnp.int32, (OWN_BC, 2 * N), 0) + first[0]
    chosen = (lax.broadcasted_iota(jnp.int32, (OWN_BC, 2 * N), 1) == own).astype(F32).astype(BF16)

    def pick(value):
        return product(jnp.concatenate([chosen] * 3, 1), jnp.concatenate(split_three(value), 1), 1, 1)

    grad = parts[0].astype(F32)
    for k in range(1, N_REP):
        grad = grad + parts[k].astype(F32)
    own_pre = pick(jnp.concatenate([pre_b[...], pre_c[...]], 1))
    own_conv = product(chosen, conv_in[...].astype(BF16), 1, 1)
    taps = pick(par[:, OWN:])
    sig = jax.nn.sigmoid(own_pre)
    grad_pre = grad * (sig * (1.0 + own_pre * (1.0 - sig)))
    position = lax.broadcasted_iota(jnp.int32, (1, PACK), 1)

    def segment(places):
        counted = jnp.zeros_like(places)
        for k in range(3):
            counted = counted + (places >= ends[k]).astype(jnp.int32)
        return counted

    grad_conv = taps[:, CONV - 1 : CONV] * grad_pre
    column = lax.broadcasted_iota(jnp.int32, (OWN_BC, N), 1)
    found = jnp.where(column == CONV, jnp.sum(grad_pre, 1, keepdims=True), 0.0)
    found = jnp.where(column == CONV - 1, jnp.sum(own_conv * grad_pre, 1, keepdims=True), found)
    for later_by in range(1, CONV):
        same = (segment(position + later_by) == segment(position)) & (position < PACK - later_by)
        later = jnp.where(same, pltpu.roll(grad_pre, PACK - later_by, 1), 0.0)
        tap = CONV - 1 - later_by
        found = jnp.where(column == tap, jnp.sum(own_conv * later, 1, keepdims=True), found)
        grad_conv = grad_conv + taps[:, tap : tap + 1] * later
    lane = lax.broadcasted_iota(jnp.int32, (N, N), 1)
    filler = jnp.zeros((N - OWN_BC, N), F32)
    for k in range(PACK // N):
        rows = slice(k * N, (k + 1) * N)
        columns = jnp.concatenate([grad_conv[:, rows], filler], 0).T
        steps = pltpu.roll(grad_dt[rows, :].astype(F32), OWN_BC, 1)
        tail_out[rows, :OWN] = grad_x[rows, :]
        tail_out[rows, OWN:] = jnp.where(
            lane < OWN_BC, columns, jnp.where(lane < OWN_BC + OWN_H, steps, 0.0)
        ).astype(BF16)
    row = lax.broadcasted_iota(jnp.int32, (8, OWN), 0)
    skip = head_sums(sums[...])
    by_head = jnp.concatenate([skip, jnp.zeros((8, OWN - N), F32)], 1)
    logs = jnp.concatenate([head_acc[...], jnp.zeros((8, OWN - N), F32)], 1)
    wide = jnp.where(row == 0, grad_gain[0:1, :], jnp.where(row < 6, sums[...], 0.0))
    wide = jnp.where(row == 6, logs[1:2, :], jnp.where(row == 7, by_head[6:7, :], wide))
    turned = jnp.concatenate([found, filler], 0).T
    first_row = lax.broadcasted_iota(jnp.int32, (8, N), 0) == 0
    small_out[:, :OWN] = wide
    small_out[:, OWN:] = jnp.where(first_row, head_acc[0:1, :], pltpu.roll(turned[:8], 1, 0))


def run_rest(ends, parts, pre, proj, par, grad_x, grad_dt, sums, head_acc, grad_gain, first):
    fixed = lambda shape: pl.BlockSpec(shape, lambda i: (0,) * len(shape))
    return pl.pallas_call(
        rest_kernel,
        grid=(1,),
        in_specs=[
            pl.BlockSpec(memory_space=pltpu.SMEM),
            fixed((N_REP, OWN_BC, PACK)),
            pl.BlockSpec((PACK, N), lambda i: (0, 3)),
            pl.BlockSpec((PACK, N), lambda i: (0, 4)),
            pl.BlockSpec((PACK, 2 * N), lambda i: (0, 3)),
            fixed((16, 640)),
            fixed((PACK, OWN)),
            fixed((PACK, N)),
            fixed((8, OWN)),
            fixed((8, N)),
            fixed((8, OWN)),
            pl.BlockSpec(memory_space=pltpu.SMEM),
        ],
        out_specs=[fixed((PACK, TAIL)), fixed((8, TAIL))],
        out_shape=[jax.ShapeDtypeStruct((PACK, TAIL), BF16), jax.ShapeDtypeStruct((8, TAIL), F32)],
        compiler_params=pltpu.CompilerParams(
            dimension_semantics=("arbitrary",), vmem_limit_bytes=VMEM_LIMIT
        ),
        cost_estimate=COST,
        name="rest_backward",
    )(ends, parts, pre, pre, proj, par, grad_x, grad_dt, sums, head_acc, grad_gain, first)


def tail_grad_kernel(normed, tail, small, out):
    step = pl.program_id(0)
    part = product(normed[...], tail[...], 0, 0)
    for f in range(N_FSDP):
        rows = part[f * SHARD_IN : (f + 1) * SHARD_IN]

        @pl.when(step == 0)
        def _(f=f, rows=rows):
            out[eight_order(f), :SHARD_IN] = rows
            out[eight_order(f), SHARD_IN:] = small[...]

        @pl.when(step > 0)
        def _(f=f, rows=rows):
            out[eight_order(f), :SHARD_IN] += rows


def run_tail_grad(normed, tail, small):
    count = 2 * ROWS
    shape = (N_FSDP, SHARD_IN + 8, TAIL)
    return pl.pallas_call(
        tail_grad_kernel,
        grid=(PACK // count,),
        in_specs=[
            pl.BlockSpec((count, D), lambda i: (i, 0)),
            pl.BlockSpec((count, TAIL), lambda i: (i, 0)),
            pl.BlockSpec((8, TAIL), lambda i: (0, 0)),
        ],
        out_specs=pl.BlockSpec(shape, lambda i: (0, 0, 0)),
        out_shape=jax.ShapeDtypeStruct(shape, F32),
        compiler_params=pltpu.CompilerParams(
            dimension_semantics=("arbitrary",), vmem_limit_bytes=VMEM_LIMIT
        ),
        cost_estimate=COST,
        name="tail_grad",
    )(normed, tail, small)


def adam_step(grad, weight, first, second, grad_out, first_out, second_out, weight_out):
    new_weight, new_first, new_second = adam_update(
        weight[...], grad, first[...], second[...], RATE_MATRIX, WEIGHT_DECAY
    )
    grad_out[...] = grad
    first_out[...] = new_first
    second_out[...] = new_second
    weight_out[...] = new_weight


def adam_early_kernel(rows, pair, *refs):
    arrays, grad = refs[:-1], refs[-1]
    grad[:, :WIDE] = pair[0, rows, :]
    grad[:, WIDE:] = pair[1, rows, :]
    adam_step(grad[...], *arrays)


def run_adam_early(place_of, rows, parts, weight, first, second):
    part = pl.BlockSpec((SHARD_IN, 2 * WIDE), place_of)
    shape = jax.ShapeDtypeStruct(weight.shape, F32)
    return pl.pallas_call(
        partial(adam_early_kernel, rows),
        grid=(N_REP // 2,),
        in_specs=[pl.BlockSpec((2,) + parts.shape[1:], lambda i: (i, 0, 0))] + [part] * 3,
        out_specs=[part] * 4,
        out_shape=[shape] * 4,
        scratch_shapes=[pltpu.VMEM((SHARD_IN, 2 * WIDE), F32)],
        compiler_params=pltpu.CompilerParams(
            dimension_semantics=("arbitrary",), vmem_limit_bytes=VMEM_LIMIT
        ),
        cost_estimate=FILL,
        name="adam",
    )(parts, weight, first, second)


def adam_tail_kernel(pair, rest, *refs):
    arrays, grad = refs[:3] + refs[-5:-1], refs[-1]
    step = pl.program_id(0)

    @pl.when(step < N_REP // 2)
    def _():
        grad[:, :WIDE] = pair[0, :SHARD_IN]
        grad[:, WIDE:] = pair[1, :SHARD_IN]

    @pl.when(step == N_REP // 2)
    def _():
        lane = lax.broadcasted_iota(jnp.int32, (SHARD_IN, N), 1)
        for k in range(2):
            group = jnp.zeros((SHARD_IN, N), F32)
            for m in range(4):
                value = rest[4 * k + m, :SHARD_IN]
                value = value if m == 0 else pltpu.roll(value, m * OWN_BC, 1)
                group = jnp.where((lane >= m * OWN_BC) & (lane < (m + 1) * OWN_BC), value, group)
            grad[:, k * N : (k + 1) * N] = group

    adam_step(grad[...], *arrays)


def run_adam_tail(parts, weight, first, second, before):
    half = N_REP // 2
    rows = parts.shape[1]
    column = pl.BlockSpec((SHARD_IN, 2 * WIDE), lambda i: (0, half + i))
    shape = jax.ShapeDtypeStruct(weight.shape, F32)
    return pl.pallas_call(
        adam_tail_kernel,
        grid=(half + 1,),
        in_specs=[
            pl.BlockSpec((2, rows, OWN), lambda i: (jnp.minimum(i, half - 1), 0, 0)),
            pl.BlockSpec((N_REP, rows, N), lambda i: (0, 0, OWN // N)),
        ]
        + [column] * 3
        + [pl.BlockSpec(memory_space=pl.ANY)] * 4,
        out_specs=[column] * 4,
        out_shape=[shape] * 4,
        input_output_aliases={5 + k: k for k in range(4)},
        scratch_shapes=[pltpu.VMEM((SHARD_IN, 2 * WIDE), F32)],
        compiler_params=pltpu.CompilerParams(
            dimension_semantics=("arbitrary",), vmem_limit_bytes=VMEM_LIMIT
        ),
        cost_estimate=COST,
        name="adam_tail",
    )(parts, parts, weight, first, second, *before)


def body(
    tokens,
    cotangent,
    lengths,
    w_in,
    w_dt,
    w_out,
    small,
    first_in,
    first_dt,
    first_out,
    first_small,
    second_in,
    second_dt,
    second_out,
    second_small,
):
    place = Place()
    r = place.r
    zero = jnp.int32(0)
    pack_lengths = lax.dynamic_slice_in_dim(lengths, place.f, 1, 0)[0]
    seg_ends = jnp.cumsum(pack_lengths)
    own_positions = r * ROWS + jnp.arange(ROWS, dtype=jnp.int32)
    own_live = (segment_at(own_positions, seg_ends) < 3).astype(F32)[:, None]
    slots = jnp.arange(N_REP, dtype=jnp.int32)
    ahead = ((place.x + slots // 2) % 4) * 2 + (place.yl + slots) % 2
    half = ROWS // 2

    in_low = w_in.astype(BF16)
    dt_low = w_dt.astype(BF16)
    out_low = w_out.astype(BF16)

    small_rows = jnp.pad(small.astype(BF16), (0, 16 * 3 * WIDE - SHARD_SMALL)).reshape(16, 3 * WIDE)

    def own_columns(rep):
        columns = jnp.concatenate(
            [
                lax.dynamic_slice_in_dim(in_low, rep * OWN, OWN, 1),
                lax.dynamic_slice_in_dim(in_low, DI + rep * OWN, OWN, 1),
                in_low[:, 2 * DI :],
                lax.dynamic_slice_in_dim(dt_low, rep * OWN_H, OWN_H, 1),
                jnp.zeros((SHARD_IN, 2), BF16),
                dt_low,
                jnp.zeros((SHARD_IN, N - 8 - H), BF16),
            ],
            1,
        )
        return jnp.concatenate([columns, small_rows], 0)

    other_columns = move(
        own_columns(2 * place.x + 1 - place.yl), lambda yh, z, c, x, yl: (yh + 1, z, c, x, yl + 1)
    )
    from_left = move(tokens, along_x(1))
    from_right = move(tokens, along_x(-1))
    partner = move(tokens, swap_y)

    out_low, other_columns = lax.optimization_barrier((out_low, other_columns))
    out_other = move(out_low, lambda yh, z, c, x, yl: (yh + 1, z, c, x, yl + 1))
    from_left, from_right, partner, other_columns = lax.optimization_barrier(
        (from_left, from_right, partner, other_columns)
    )
    own_shards = gather_eight(both(own_columns(r), other_columns, place.yh))
    far = move(from_left, along_x(1))
    partner_left = move(from_left, swap_y)
    partner_right = move(partner, along_x(-1))

    branch = (cotangent.astype(F32) * own_live).astype(BF16)
    far, partner_left, partner_right, out_other, branch = lax.optimization_barrier(
        (far, partner_left, partner_right, out_other, branch)
    )
    out_pair = both(out_low, out_other, place.yh)
    partner_far_top = move(partner_left[:half], along_x(1))
    partner_far_low = move(partner_right[half:], along_x(-1))

    vector = own_shards[:, :, :, SHARD_IN : SHARD_IN + 2].transpose(2, 0, 1, 3, 4)
    vector = vector.reshape(N_FSDP, 6 * WIDE)[:, :SHARD_SMALL].reshape(-1).astype(F32)
    offset = 0
    gain_in = vector[None, :D]
    offset = D
    gain_row = lax.dynamic_slice_in_dim(vector, offset + r * OWN, OWN, 0)[None, :]
    offset += DI
    taps = vector[offset : offset + (CONV + 1) * CHANNELS].reshape(CONV + 1, CHANNELS)
    offset += (CONV + 1) * CHANNELS
    per_head = vector[offset:].reshape(3, H)
    dt_bias, a_log, d_skip = lax.dynamic_slice_in_dim(per_head, r * OWN_H, OWN_H, 1)
    taps_bc = taps[:, DI:]
    conv_par = jnp.concatenate([lax.dynamic_slice_in_dim(taps, r * OWN, OWN, 1), taps_bc], 1)
    head_par = jnp.stack(
        [
            jnp.pad(jnp.broadcast_to(d_skip[:, None], (OWN_H, P_SIZE)).reshape(-1), (0, 2 * N)),
            jnp.pad(dt_bias, (0, 640 - OWN_H)),
            jnp.pad(-jnp.exp(a_log), (0, 640 - OWN_H)),
        ],
        0,
    )
    par = jnp.concatenate([conv_par, head_par, jnp.zeros((8, 640), F32)], 0)

    in_low, partner_far_top, partner_far_low, own_shards = lax.optimization_barrier(
        (in_low, partner_far_top, partner_far_low, own_shards)
    )
    full_out = gather_eight(tie(out_pair, own_shards))
    in_other = move(in_low, lambda yh, z, c, x, yl: (yh + 1, z, c, x, yl + 1))
    b_left = move(branch, along_x(1))
    b_right = move(branch, along_x(-1))
    b_partner = move(branch, swap_y)
    token_pieces = [
        tokens, partner, from_right, partner_right, far,
        partner_far_top, partner_far_low, from_left, partner_left,
    ]
    normed, proj, low_dt = run_project(ahead, token_pieces, gain_in, own_shards)
    b_left, b_right, b_partner, proj = lax.optimization_barrier((b_left, b_right, b_partner, proj))
    b_far = move(b_left, along_x(1))
    b_partner_left = move(b_left, swap_y)
    b_partner_right = move(b_partner, along_x(-1))
    before = run_forward(0, seg_ends, proj, par)
    b_far, b_partner_left, b_partner_right, before = lax.optimization_barrier(
        (b_far, b_partner_left, b_partner_right, before)
    )
    b_partner_far_top = move(b_partner_left[:half], along_x(1))
    b_partner_far_low = move(b_partner_right[half:], along_x(-1))
    pre, mixed, states, _ = run_forward(1, seg_ends, proj, par, before)
    mixed, in_low, in_other, b_partner_far_top, b_partner_far_low = lax.optimization_barrier(
        (mixed, in_low, in_other, b_partner_far_top, b_partner_far_low)
    )
    full_in = gather_eight(both(in_low, in_other, place.yh))
    branch_pieces = [
        branch, b_partner, b_right, b_partner_right, b_far,
        b_partner_far_top, b_partner_far_low, b_left, b_partner_left,
    ]
    rep_table = jnp.concatenate([ahead, r[None]])
    grad_branch, grad_normed_out, sums = run_out_grad(rep_table, branch_pieces, full_out, mixed, proj, gain_row)
    sums = share_rep(sums[:2].reshape(32, 128)).sum(0).reshape(2, PACK)
    sums = jnp.concatenate([sums, jnp.zeros((6, PACK), F32)], 0)

    low, grad_mixed, grad_gain = run_gate(grad_normed_out, mixed, proj, sums, gain_row)

    low_rows = exchange(low.reshape(N_REP, ROWS, 2 * OWN), "rep")
    grad_x, grad_dtraw, grad_bc, grad_sums, grad_heads = run_backward(
        seg_ends, proj, pre, mixed, grad_mixed, states, par
    )
    low, grad_x = lax.optimization_barrier((low, grad_x))
    early_grad = run_early_grad(low, grad_branch, normed)
    low_rows, early_grad, grad_bc, grad_x = lax.optimization_barrier((low_rows, early_grad, grad_bc, grad_x))

    grad_bc = exchange(grad_bc, "rep").reshape(N_REP, OWN_BC, PACK)
    early = scatter_eight(early_grad)
    grad_rows = run_z_grad(low_rows, full_in)
    grad_bc, grad_rows = lax.optimization_barrier((grad_bc, grad_rows))

    tail, small_own = run_rest(
        seg_ends, grad_bc, pre, proj, par, grad_x, grad_dtraw, grad_sums, grad_heads, grad_gain, (r * OWN_BC)[None]
    )
    grad_tail = run_tail_grad(normed, tail, small_own)
    tail, grad_tail, low_rows = lax.optimization_barrier((tail, grad_tail, low_rows))
    tail_rows = exchange(tail.reshape(N_REP, ROWS, TAIL), "rep")
    tail_part = scatter_eight(grad_tail)
    block_out = run_block_out(low_rows, full_out, tokens, own_live)
    early, block_out = lax.optimization_barrier((early, block_out))
    mine, other = at(early, place.yh), at(early, 1 - place.yh)
    out_mine = move(
        mine[:SHARD_IN], lambda yh, z, c, x, yl: (x // 2, (x % 2) * 2 + yl, z % 2, 2 * c + yh, z // 2)
    )
    out_other = move(
        other[:SHARD_IN], lambda yh, z, c, x, yl: (x // 2, (x % 2) * 2 + yl, z % 2, 2 * c + 1 - yh, z // 2)
    )
    z_other = move(other[SHARD_IN:], swap_y_hi)
    tail_rows, out_mine, out_other, z_other = lax.optimization_barrier((tail_rows, out_mine, out_other, z_other))

    early_parts = share_rep(jnp.concatenate([out_mine + out_other, mine[SHARD_IN:] + z_other], 0))
    input_grad, grad_gain_in = run_input_grad(
        grad_rows, tail_rows, full_in, low_dt, tokens, cotangent, gain_in
    )

    grad_gain_in = sum_z(grad_gain_in + move(grad_gain_in, swap_core))
    tail_part, grad_gain_in = lax.optimization_barrier((tail_part, grad_gain_in))
    gain_rows = grad_gain_in.shape[0]
    tail_other = move(with_rows(at(tail_part, 1 - place.yh), grad_gain_in), swap_y_hi)
    tail_part = with_rows(at(tail_part, place.yh), grad_gain_in) + tail_other

    tail_part, early_parts = lax.optimization_barrier((tail_part, early_parts))
    tail_parts = share_rep(tail_part)

    grad_out, new_first_out, new_second_out, new_out = run_adam_early(
        lambda i: (i // 2, i % 2), slice(0, SHARD_IN), early_parts, w_out, first_out, second_out
    )
    updated = run_adam_early(
        lambda i: (0, i), slice(SHARD_IN, 2 * SHARD_IN), early_parts, w_in, first_in, second_in
    )
    grad_in, new_first_in, new_second_in, new_in = run_adam_tail(tail_parts, w_in, first_in, second_in, updated)

    def columns(parts):
        return parts.transpose(1, 0, 2).reshape(parts.shape[1], -1)

    grad_gain_in = tail_parts[:, -gain_rows : D // TAIL - gain_rows].sum(0).reshape(-1)
    small_parts = tail_parts[:, SHARD_IN:-gain_rows]
    small_x = small_parts[:, :, :OWN].transpose(1, 0, 2).reshape(8, DI)
    small_bc = small_parts[:, :, OWN:].transpose(1, 0, 2)

    def channels(row):
        return jnp.concatenate([small_x[row], small_bc[row, :, :OWN_BC].reshape(-1)])

    grad_small_all = jnp.concatenate(
        [grad_gain_in, small_x[0]]
        + [channels(row) for row in range(1, 6)]
        + [
            small_bc[0, :, :OWN_H].reshape(-1),
            small_parts[:, 6, :OWN_H].reshape(-1),
            small_parts[:, 7, :OWN_H].reshape(-1),
        ]
    )
    grad_small = lax.dynamic_slice_in_dim(grad_small_all, place.f * SHARD_SMALL, SHARD_SMALL, 0)
    grad_dt = columns(tail_parts[:, :SHARD_IN, OWN + OWN_BC : OWN + OWN_BC + OWN_H])
    new_dt, new_first_dt, new_second_dt = adam_update(
        w_dt, grad_dt, first_dt, second_dt, RATE_MATRIX, WEIGHT_DECAY
    )
    new_small, new_first_small, new_second_small = adam_update(
        small, grad_small, first_small, second_small, RATE_SMALL, 0.0
    )
    return (
        block_out,
        input_grad,
        grad_in,
        grad_dt,
        grad_out,
        grad_small,
        new_first_in,
        new_first_dt,
        new_first_out,
        new_first_small,
        new_second_in,
        new_second_dt,
        new_second_out,
        new_second_small,
        new_in,
        new_dt,
        new_out,
        new_small,
    )


def solution(mesh):
    rows = P(("fsdp", "rep"), None)
    matrix = P("fsdp", None)
    vector = P("fsdp")
    group = (matrix, matrix, matrix, vector)
    return jax.shard_map(
        body,
        mesh=mesh,
        in_specs=(rows, rows, P()) + group * 3,
        out_specs=(rows, rows) + group * 4,
        check_vma=False,
    )
```

```python
from functools import partial

import jax
import jax.numpy as jnp
from jax import lax
from jax.experimental import pallas as pl
from jax.experimental.pallas import tpu as pltpu
from jax.sharding import PartitionSpec as P

D = 1536
H = 48
P_SIZE = 64
N = 128
CONV = 4
STEP = 10
DI = 3072
CHANNELS = DI + 2 * N
SMALL = 21392
N_FSDP = 16
N_REP = 8
ROWS = 256
PACK = 2048
OWN = DI // N_REP
OWN_H = H // N_REP
OWN_BC = 2 * N // N_REP
SHARD_IN = D // N_FSDP
SHARD_OUT = DI // N_FSDP
SHARD_SMALL = SMALL // N_FSDP
WIDE = 384
CHUNK = 128
CHUNKS = PACK // CHUNK
HALF = CHUNKS // 2
TAIL = 512
VMEM_LIMIT = 60 * 1024 * 1024

NORM_EPS = 1e-05
BETA_ONE = 0.9
BETA_TWO = 0.999
ADAM_EPS = 1e-08
WEIGHT_DECAY = 0.1
RATE_MATRIX = 0.04
RATE_SMALL = 0.4
PRECISE = lax.Precision.HIGHEST
BF16 = jnp.bfloat16
F32 = jnp.float32
COST = pl.CostEstimate(flops=1_000_000, bytes_accessed=100_000, transcendentals=0)
FILL = pl.CostEstimate(flops=2_400_000_000, bytes_accessed=20_000_000, transcendentals=0)


def move(value, target):
    pairs = []
    for f in range(N_FSDP):
        for r in range(N_REP):
            yh, z, c, x, yl = target(f // 8, (f // 2) % 4, f % 2, r // 2, r % 2)
            pairs.append((f * N_REP + r, ((yh % 2) * 8 + (z % 4) * 2 + c % 2) * N_REP + (x % 4) * 2 + yl % 2))
    return lax.ppermute(value, ("fsdp", "rep"), pairs)


def along_x(steps):
    return lambda yh, z, c, x, yl: (yh, z, c, x + steps, yl)


def along_z(steps):
    return lambda yh, z, c, x, yl: (yh, z + steps, c, x, yl)


def swap_y(yh, z, c, x, yl):
    return (yh, z, c, x, yl + 1)


def swap_y_hi(yh, z, c, x, yl):
    return (yh + 1, z, c, x, yl)


def swap_core(yh, z, c, x, yl):
    return (yh, z, c + 1, x, yl)


class Place:
    def __init__(self):
        f = lax.axis_index("fsdp")
        r = lax.axis_index("rep")
        self.f, self.r = f, r
        self.yh, self.z, self.c = f // 8, (f // 2) % 4, f % 2
        self.x, self.yl = r // 2, r % 2


def at(value, index, axis=0):
    return lax.dynamic_index_in_dim(value, index, axis, keepdims=False)


def tie(values, *others):
    return lax.optimization_barrier((values, others))[0]


def both(mine, other, second):
    first = jnp.where(second == 0, mine, other)
    last = jnp.where(second == 0, other, mine)
    return jnp.stack([first, last], 0)


def put(out, piece, axis, index):
    starts = [jnp.int32(0)] * out.ndim
    starts[axis] = jnp.int32(index)
    return lax.dynamic_update_slice(out, jnp.expand_dims(piece, axis), tuple(starts))


def swap_shards(value, place):
    other = move(value, lambda yh, z, c, x, yl: (yh + 1, z, c, x, yl + 1))
    return both(value, other, place.yh)


def gather_eight(pair):
    groups = [list(range(8)), list(range(8, 16))]
    out = lax.all_gather(pair, "fsdp", axis=0, tiled=True, axis_index_groups=groups)
    return out.reshape((4, 2) + pair.shape)


def exchange(value, axis):
    return lax.all_to_all(value, axis, 0, 0, tiled=True)


def share_rep(value):
    return exchange(jnp.broadcast_to(value[None], (N_REP,) + value.shape), "rep")


def sum_z(value):
    steps = [move(value, along_z(step)) for step in (1, 3, 2)]
    return value + steps[0] + steps[1] + steps[2]


def scatter_eight(value):
    groups = [list(range(8)), list(range(8, 16))]
    flat = value.reshape(-1, value.shape[-1])
    out = lax.psum_scatter(flat, "fsdp", scatter_dimension=0, tiled=True, axis_index_groups=groups)
    return out.reshape((2,) + value.shape[1:])


def eight_order(f):
    return ((f // 2) % 4 * 2 + f % 2) * 2 + f // 8


def with_rows(block, extra):
    width = block.shape[-1]
    flat = block.reshape(-1, width)
    return flat if extra is None else jnp.concatenate([flat, extra], 0)


def adam_update(weight, gradient, moment_one, moment_two, learn_rate, decay_rate):
    moment_one = BETA_ONE * moment_one + (1.0 - BETA_ONE) * gradient
    moment_two = BETA_TWO * moment_two + (1.0 - BETA_TWO) * gradient * gradient
    scaled = (
        moment_one
        / (1.0 - BETA_ONE**STEP)
        / (jnp.sqrt(moment_two / (1.0 - BETA_TWO**STEP)) + ADAM_EPS)
    )
    return (weight - learn_rate * (scaled + decay_rate * weight), moment_one, moment_two)


def contract_rows(left_side, right_side):
    return lax.dot_general(
        left_side, right_side, (((0,), (0,)), ((), ())), preferred_element_type=F32
    )


def contract_cols(left_side, right_side):
    return lax.dot_general(
        left_side, right_side, (((1,), (1,)), ((), ())), preferred_element_type=F32
    )


def matmul(left_side, right_side):
    return jnp.dot(left_side, right_side, preferred_element_type=F32)


def segment_at(positions, seg_ends):
    counted = jnp.sum((positions[:, None] >= seg_ends[None, :]).astype(jnp.int32), axis=1)
    return jnp.where(positions < 0, jnp.int32(-1), counted)


def split_two(value):
    high = value.astype(BF16)
    return high, (value - high.astype(F32)).astype(BF16)


def split_three(value):
    high = value.astype(BF16)
    rest = value - high.astype(F32)
    middle = rest.astype(BF16)
    return high, middle, (rest - middle.astype(F32)).astype(BF16)


def product(left, right, left_dim, right_dim):
    return lax.dot_general(
        left, right, (((left_dim,), (right_dim,)), ((), ())), preferred_element_type=F32
    )


def joined_product(left_parts, right_parts, left_dim=1, right_dim=0):
    left_high, left_low = left_parts
    right_high, right_low = right_parts
    return product(
        jnp.concatenate([left_high, left_high, left_low], left_dim),
        jnp.concatenate([right_high, right_low, right_high], right_dim),
        left_dim,
        right_dim,
    )


def precise_product(left, right, left_dim=1, right_dim=0):
    return joined_product(split_two(left), split_two(right), left_dim, right_dim)


def ones_product(ones, value):
    return product(jnp.concatenate([ones] * 3, 1), jnp.concatenate(split_three(value), 0), 1, 0)


def spread(per_head, lane):
    return jnp.concatenate(
        [
            jnp.where(lane < P_SIZE, per_head[:, 2 * k : 2 * k + 1], per_head[:, 2 * k + 1 : 2 * k + 2])
            for k in range(OWN_H // 2)
        ],
        1,
    )


def head_sums(value):
    column = lax.broadcasted_iota(jnp.int32, (OWN, N), 0)
    head = lax.broadcasted_iota(jnp.int32, (OWN, N), 1)
    members = ((column >= head * P_SIZE) & (column < (head + 1) * P_SIZE)).astype(F32).astype(BF16)
    high, low = split_two(value)
    return product(jnp.concatenate([high, low], 1), jnp.concatenate([members, members], 0), 1, 0)


def two_heads(pair, lane):
    zero = jnp.zeros_like(pair)
    return jnp.concatenate([jnp.where(lane < P_SIZE, pair, zero), jnp.where(lane < P_SIZE, zero, pair)], 0)


def chunk_facts(ends, chunk, dt_pre, par):
    column = lax.broadcasted_iota(jnp.int32, (CHUNK, 1), 0) + chunk * CHUNK
    row = lax.broadcasted_iota(jnp.int32, (1, CHUNK), 1) + chunk * CHUNK

    def segment(position):
        counted = jnp.zeros_like(position)
        for k in range(3):
            counted = counted + (position >= ends[k]).astype(jnp.int32)
        return jnp.where(position < 0, -1, counted)

    def one_segment(position):
        counted = jnp.int32(0)
        for k in range(3):
            counted = counted + (position >= ends[k]).astype(jnp.int32)
        return jnp.where(position < 0, -1, counted)

    here_column, here_row = segment(column), segment(row)
    prior = one_segment(chunk * CHUNK - 1)
    last = one_segment(chunk * CHUNK + CHUNK - 1)
    lane = lax.broadcasted_iota(jnp.int32, (CHUNK, N), 1)
    shifted = dt_pre + par[6:7, :N]
    soft = jnp.maximum(shifted, 0.0) + jnp.log1p(jnp.exp(-jnp.abs(shifted)))
    step = jnp.where(lane < OWN_H, soft, 0.0)
    decay = step * par[7:8, :N]
    tri_row = lax.broadcasted_iota(jnp.int32, (CHUNK, CHUNK), 0)
    tri_column = lax.broadcasted_iota(jnp.int32, (CHUNK, CHUNK), 1)
    lower = (tri_row >= tri_column).astype(F32).astype(BF16)
    upper = (tri_row <= tri_column).astype(F32).astype(BF16)
    total = ones_product(lower, decay)
    entering = (here_column == prior).astype(F32) * jnp.exp(total)
    end = total[CHUNK - 1 : CHUNK]
    leaving = (here_column == last).astype(F32) * jnp.exp(jnp.minimum(end - total, 0.0))
    passing = jnp.where(last == prior, 1.0, 0.0) * jnp.exp(end)
    return dict(
        column=column,
        segment=segment,
        here_column=here_column,
        here_row=here_row,
        lane=lane,
        shifted=shifted,
        step=step,
        decay=decay,
        total=total,
        entering=entering,
        leaving=leaving,
        passing=passing,
        tri_row=tri_row,
        tri_column=tri_column,
        upper=upper,
    )


def forward_kernel(part, ends, proj, par, *refs):
    if part:
        carry_in, refs = refs[3], refs[4:]
    pre_out, mixed_out, state_out, carry_out, extended, state = refs
    chunk = pl.program_id(0) + part * HALF

    @pl.when(pl.program_id(0) == 0)
    def _():
        if part:
            state[...] = carry_in[:N, :OWN]
            extended[0:8, :] = carry_in[N:, :]
        else:
            state[...] = jnp.zeros_like(state)
            extended[0:8, :] = jnp.zeros((8, 640), F32)

    facts = chunk_facts(ends, chunk, proj[:, 1024:1152], par)
    lane = facts["lane"]
    conv = proj[:, OWN:1024].astype(BF16).astype(F32)
    extended[8 : 8 + CHUNK, :] = conv
    pre = par[4:5] + par[3:4] * conv
    for back in range(1, CONV):
        same = (facts["segment"](facts["column"] - back) == facts["here_column"]).astype(F32)
        pre = pre + par[3 - back : 4 - back] * (extended[8 - back : 8 - back + CHUNK, :] * same)
    extended[0:8, :] = extended[CHUNK : CHUNK + 8, :]
    pre_out[...] = pre
    act = pre * jax.nn.sigmoid(pre)
    own_x, state_b, state_c = act[:, :OWN], act[:, OWN : OWN + N], act[:, OWN + N :]
    stepped = own_x * spread(facts["step"], lane)
    b_parts, c_parts = split_two(state_b), split_two(state_c)
    inside = (facts["tri_row"] >= facts["tri_column"]) & (facts["here_column"] == facts["here_row"])
    scores = jnp.where(inside, joined_product(c_parts, b_parts, 1, 1), 0.0)
    total_rows = facts["total"].T
    state_in = state[...]
    state_out[...] = state_in
    outs = []
    for pair in range(OWN_H // 2):
        mixing = []
        for head in (2 * pair, 2 * pair + 1):
            span = facts["total"][:, head : head + 1] - total_rows[head : head + 1, :]
            mixing.append(jnp.exp(jnp.minimum(span, 0.0)) * scores)
        inner = two_heads(stepped[:, pair * N : pair * N + N], lane)
        outs.append(precise_product(jnp.concatenate(mixing, 1), inner))
    scanned = jnp.concatenate(outs, 1) + spread(facts["entering"], lane) * joined_product(
        c_parts, split_two(state_in)
    )
    state[...] = spread(facts["passing"], lane[:1]) * state_in + precise_product(
        state_b.T, stepped * spread(facts["leaving"], lane)
    )
    mixed_out[...] = scanned + par[5:6, :OWN] * own_x

    @pl.when(pl.program_id(0) == HALF - 1)
    def _():
        carry_out[:N, :OWN] = state[...]
        carry_out[:N, OWN:] = jnp.zeros((N, 640 - OWN), F32)
        carry_out[N:, :] = extended[0:8, :]


def run_forward(part, ends, proj, par, before=()):
    here = lambda i: (i + part * HALF, 0)
    chunked = lambda width: pl.BlockSpec((CHUNK, width), here)
    fixed = lambda shape: pl.BlockSpec(shape, lambda i: (0, 0))
    carry = fixed((N + 8, 640))
    return pl.pallas_call(
        partial(forward_kernel, part),
        grid=(HALF,),
        in_specs=[pl.BlockSpec(memory_space=pltpu.SMEM), chunked(1152), fixed((16, 640))]
        + ([pl.BlockSpec(memory_space=pl.ANY)] * 3 + [carry] if part else []),
        out_specs=[chunked(640), chunked(OWN), pl.BlockSpec((N, OWN), here), carry],
        out_shape=[
            jax.ShapeDtypeStruct((PACK, 640), F32),
            jax.ShapeDtypeStruct((PACK, OWN), F32),
            jax.ShapeDtypeStruct((CHUNKS * N, OWN), F32),
            jax.ShapeDtypeStruct((N + 8, 640), F32),
        ],
        input_output_aliases={3: 0, 4: 1, 5: 2} if part else {},
        scratch_shapes=[pltpu.VMEM((CHUNK + 8, 640), F32), pltpu.VMEM((N, OWN), F32)],
        compiler_params=pltpu.CompilerParams(
            dimension_semantics=("arbitrary",), vmem_limit_bytes=VMEM_LIMIT
        ),
        cost_estimate=COST,
        name="scan_forward",
    )(ends, proj, par, *before)


def backward_kernel(ends, conv_in, dt_in, pre_in, mixed_in, grad_mixed, state_all, par, *refs):
    grad_x, grad_dt, grad_bc, sums, head_acc, carried, extended, end_dot = refs
    step_index = pl.program_id(0)
    chunk = CHUNKS - 1 - step_index

    @pl.when(step_index == 0)
    def _():
        carried[...] = jnp.zeros_like(carried)
        extended[CHUNK : CHUNK + 8, :] = jnp.zeros((8, OWN), F32)
        end_dot[...] = jnp.zeros_like(end_dot)
        sums[...] = jnp.zeros_like(sums)
        head_acc[...] = jnp.zeros_like(head_acc)

    facts = chunk_facts(ends, chunk, dt_in[...], par)
    lane = facts["lane"]
    pre = pre_in[...]
    sig = jax.nn.sigmoid(pre)
    act = pre * sig
    own_x, state_b, state_c = act[:, :OWN], act[:, OWN : OWN + N], act[:, OWN + N :]
    step = facts["step"]
    step_wide = spread(step, lane)
    stepped = own_x * step_wide
    skip = par[5:6, :OWN]
    scanned = mixed_in[...] - skip * own_x
    grad_m = grad_mixed[...]
    sums[6:7] += jnp.sum(grad_m * own_x, 0, keepdims=True)

    b_parts, c_parts = split_two(state_b), split_two(state_c)
    inside = (facts["tri_row"] <= facts["tri_column"]) & (facts["here_column"] == facts["here_row"])
    scores = jnp.where(inside, joined_product(b_parts, c_parts, 1, 1), 0.0)
    total_rows = facts["total"].T
    grad_scores = jnp.zeros((CHUNK, CHUNK), F32)
    grad_stepped = []
    for pair in range(OWN_H // 2):
        columns = slice(pair * N, pair * N + N)
        grad_pair = grad_m[:, columns]
        high, low = split_two(grad_pair)
        stepped_parts = split_two(two_heads(stepped[:, columns], lane))
        grad_mixing = joined_product(stepped_parts, (high, low), 1, 1)
        mixing = []
        for k in range(2):
            head = 2 * pair + k
            span = total_rows[head : head + 1, :] - facts["total"][:, head : head + 1]
            decays = jnp.exp(jnp.minimum(span, 0.0))
            mixing.append(decays * scores)
            grad_scores = grad_scores + decays * grad_mixing[k * CHUNK : (k + 1) * CHUNK]
        grad_stepped.append(
            joined_product(
                split_two(jnp.concatenate(mixing, 1)), (two_heads(high, lane), two_heads(low, lane))
            )
        )
    grad_scores = jnp.where(inside, grad_scores, 0.0)
    carry = carried[...]
    carry_parts = split_two(carry)
    leaving = spread(facts["leaving"], lane)
    grad_stepped = jnp.concatenate(grad_stepped, 1) + leaving * joined_product(b_parts, carry_parts)
    state_in = state_all[...]
    entered = spread(facts["entering"], lane) * grad_m
    entered_parts = split_two(entered)
    grad_b = precise_product(grad_scores, state_c) + joined_product(
        split_two(leaving * stepped), carry_parts, 1, 1
    )
    grad_c = precise_product(grad_scores.T, state_b) + joined_product(
        entered_parts, split_two(state_in), 1, 1
    )
    grad_bc[0:N, :] = grad_b.T
    grad_bc[N:, :] = grad_c.T
    new_carry = spread(facts["passing"], lane[:1]) * carry + joined_product(
        split_two(state_c.T), entered_parts
    )
    carried[...] = new_carry

    grad_step = head_sums(own_x * grad_stepped)
    last_row = lax.broadcasted_iota(jnp.int32, (CHUNK, N), 0) == CHUNK - 1
    grad_total = head_sums(grad_m * scanned) - step * grad_step
    grad_total = grad_total + jnp.where(last_row, end_dot[0:1, :], 0.0)
    grad_decay = ones_product(facts["upper"], grad_total)
    end_dot[...] = head_sums(
        jnp.broadcast_to(jnp.sum(new_carry * state_in, 0, keepdims=True), (8, OWN))
    )
    grad_pre_dt = (grad_step + grad_decay * par[7:8, :N]) * jax.nn.sigmoid(facts["shifted"])
    grad_pre_dt = jnp.where(lane < OWN_H, grad_pre_dt, 0.0)
    grad_dt[...] = grad_pre_dt.astype(BF16)
    head_acc[0:1] += jnp.sum(grad_pre_dt, 0, keepdims=True)
    head_acc[1:2] += jnp.sum(grad_decay * facts["decay"], 0, keepdims=True)

    sig_x, pre_x = sig[:, :OWN], pre[:, :OWN]
    grad_pre = (step_wide * grad_stepped + skip * grad_m) * (sig_x * (1.0 + pre_x * (1.0 - sig_x)))
    extended[0:CHUNK, :] = grad_pre
    conv = conv_in[...].astype(BF16).astype(F32)
    sums[5:6] += jnp.sum(grad_pre, 0, keepdims=True)
    sums[4:5] += jnp.sum(conv * grad_pre, 0, keepdims=True)
    grad_conv = par[3:4, :OWN] * grad_pre
    for ahead in range(1, CONV):
        same = (facts["segment"](facts["column"] + ahead) == facts["here_column"]).astype(F32)
        later = extended[ahead : ahead + CHUNK, :] * same
        sums[4 - ahead : 5 - ahead] += jnp.sum(conv * later, 0, keepdims=True)
        grad_conv = grad_conv + par[3 - ahead : 4 - ahead, :OWN] * later
    extended[CHUNK : CHUNK + 8, :] = extended[0:8, :]
    grad_x[...] = grad_conv.astype(BF16)


def run_backward(ends, proj, pre, mixed, grad_mixed, states, par):
    last = CHUNKS - 1
    chunked = lambda width, column=0: pl.BlockSpec((CHUNK, width), lambda i: (last - i, column))
    fixed = lambda shape: pl.BlockSpec(shape, lambda i: (0, 0))
    return pl.pallas_call(
        backward_kernel,
        grid=(CHUNKS,),
        in_specs=[
            pl.BlockSpec(memory_space=pltpu.SMEM),
            chunked(OWN, 1),
            chunked(N, 8),
            chunked(640),
            chunked(OWN),
            chunked(OWN),
            pl.BlockSpec((N, OWN), lambda i: (last - i, 0)),
            fixed((16, 640)),
        ],
        out_specs=[
            chunked(OWN),
            chunked(N),
            pl.BlockSpec((2 * N, CHUNK), lambda i: (0, last - i)),
            fixed((8, OWN)),
            fixed((8, N)),
        ],
        out_shape=[
            jax.ShapeDtypeStruct((PACK, OWN), BF16),
            jax.ShapeDtypeStruct((PACK, N), BF16),
            jax.ShapeDtypeStruct((2 * N, PACK), F32),
            jax.ShapeDtypeStruct((8, OWN), F32),
            jax.ShapeDtypeStruct((8, N), F32),
        ],
        scratch_shapes=[
            pltpu.VMEM((N, OWN), F32),
            pltpu.VMEM((CHUNK + 8, OWN), F32),
            pltpu.VMEM((8, N), F32),
        ],
        compiler_params=pltpu.CompilerParams(
            dimension_semantics=("arbitrary",), vmem_limit_bytes=VMEM_LIMIT
        ),
        cost_estimate=COST,
        name="scan_backward",
    )(ends, proj, proj, pre, mixed, grad_mixed, states, par)


PARTS = (1, 1, 1, 1, 1, 2, 1, 1)


def piece_copies(pieces, parts, blocks, sems):
    copies = []
    taken = 0
    for slot, count in enumerate(parts):
        rows = ROWS // count
        copies.append(
            [
                pltpu.make_async_copy(
                    pieces[taken + k], blocks.at[slot, pl.ds(k * rows, rows)], sems.at[taken + k]
                )
                for k in range(count)
            ]
        )
        taken += count
    return copies


def fetch_block(pieces, parts, blocks, sems):
    copies = piece_copies(pieces, parts, blocks, sems)
    step = pl.program_id(0)

    @pl.when(step == 0)
    def _():
        for group in copies:
            for copy in group:
                copy.start()

    for slot, group in enumerate(copies):

        @pl.when(step == slot)
        def _(group=group):
            for copy in group:
                copy.wait()

    return blocks[step]


def project_kernel(parts, table, *refs):
    pieces = refs[: sum(parts)]
    gain, shards, normed_out, proj, dt_out, blocks, weight, sems = refs[sum(parts) :]
    block = fetch_block(pieces, parts, blocks, sems)

    @pl.when(pl.program_id(0) == 0)
    def _():
        for f in range(N_FSDP):
            weight[f * SHARD_IN : (f + 1) * SHARD_IN, :] = shards[(f // 2) % 4, f % 2, f // 8, :SHARD_IN]
        dt_out[...] = weight[:, 1024:]

    values = block.astype(F32)
    scale = lax.rsqrt(jnp.mean(values * values, axis=1, keepdims=True) + NORM_EPS)
    normed = (values * scale * gain[...]).astype(BF16)
    normed_out[...] = normed
    proj[...] = matmul(normed, weight[...])


def run_project(table, pieces, gain, shards):
    fixed = lambda shape: pl.BlockSpec(shape, lambda i, table: (0,) * len(shape))
    placed = lambda width: pl.BlockSpec((ROWS, width), lambda i, table: (table[i], 0))
    return pl.pallas_call(
        partial(project_kernel, PARTS),
        grid_spec=pltpu.PrefetchScalarGridSpec(
            num_scalar_prefetch=1,
            grid=(N_REP,),
            in_specs=[pl.BlockSpec(memory_space=pl.ANY)] * len(pieces) + [fixed((1, D)), fixed(shards.shape)],
            out_specs=[placed(D), placed(3 * WIDE), fixed((D, N))],
            scratch_shapes=[
                pltpu.VMEM((N_REP, ROWS, D), BF16),
                pltpu.VMEM((D, 3 * WIDE), BF16),
                pltpu.SemaphoreType.DMA((len(pieces),)),
            ],
        ),
        out_shape=[
            jax.ShapeDtypeStruct((PACK, D), BF16),
            jax.ShapeDtypeStruct((PACK, 3 * WIDE), F32),
            jax.ShapeDtypeStruct((D, N), BF16),
        ],
        compiler_params=pltpu.CompilerParams(
            dimension_semantics=("arbitrary",), vmem_limit_bytes=VMEM_LIMIT
        ),
        cost_estimate=COST,
        name="project",
    )(table, *pieces, gain, shards)


def row_sums(value):
    folded = value[:, :N] + value[:, N : 2 * N] + value[:, 2 * N :]
    return jnp.sum(folded.T, 0, keepdims=True)


def out_grad_kernel(table, *refs):
    pieces = refs[: sum(PARTS)]
    w_out, mixed, gate_in, gain, branch_out, grad_out, sums, blocks, turned, sems = refs[sum(PARTS) :]
    branch = fetch_block(pieces, PARTS, blocks, sems)

    @pl.when(pl.program_id(0) == 0)
    def _():
        turned[...] = w_out[...].reshape(OWN, D).T

    branch_out[...] = branch
    total = matmul(branch, turned[...])
    grad_out[...] = total
    gate = gate_in[...]
    gated = mixed[...] * (gate * jax.nn.sigmoid(gate))
    row = lax.broadcasted_iota(jnp.int32, (8, ROWS), 0)
    sums[...] = jnp.where(
        row == 0, row_sums(gated * gated), jnp.where(row == 1, row_sums(total * gain[...] * gated), 0.0)
    )


def run_out_grad(table, pieces, w_out, mixed, proj, gain):
    fixed = lambda shape: pl.BlockSpec(shape, lambda i, table: (0, 0))
    placed = lambda width: pl.BlockSpec((ROWS, width), lambda i, table: (table[i], 0))
    own = pl.BlockSpec(
        (1, 2, 1, SHARD_OUT, D), lambda i, table: (table[N_REP] % 4, 0, table[N_REP] // 4, 0, 0)
    )
    return pl.pallas_call(
        out_grad_kernel,
        grid_spec=pltpu.PrefetchScalarGridSpec(
            num_scalar_prefetch=1,
            grid=(N_REP,),
            in_specs=[pl.BlockSpec(memory_space=pl.ANY)] * len(pieces)
            + [own, placed(OWN), placed(OWN), fixed((1, OWN))],
            out_specs=[placed(D), placed(OWN), pl.BlockSpec((8, ROWS), lambda i, table: (0, table[i]))],
            scratch_shapes=[
                pltpu.VMEM((N_REP, ROWS, D), BF16),
                pltpu.VMEM((D, WIDE), BF16),
                pltpu.SemaphoreType.DMA((len(pieces),)),
            ],
        ),
        out_shape=[
            jax.ShapeDtypeStruct((PACK, D), BF16),
            jax.ShapeDtypeStruct((PACK, OWN), F32),
            jax.ShapeDtypeStruct((8, PACK), F32),
        ],
        compiler_params=pltpu.CompilerParams(
            dimension_semantics=("arbitrary",), vmem_limit_bytes=VMEM_LIMIT
        ),
        cost_estimate=COST,
        name="out_grad",
    )(table, *pieces, w_out, mixed, proj, gain)


def gate_kernel(grad_out, mixed_in, gate_in, sums, gain, low_out, grad_mixed, grad_gain):
    rows = grad_out.shape[0]
    mixed, gate, grad_o = mixed_in[...], gate_in[...], grad_out[...]
    stats = jnp.concatenate([sums[...], jnp.zeros((N - 8, rows), F32)], 0).T
    out_scale = lax.rsqrt(stats[:, 0:1] * (1.0 / DI) + NORM_EPS)
    pull = out_scale * out_scale * out_scale * (stats[:, 1:2] * (1.0 / DI))
    gate_sig = jax.nn.sigmoid(gate)
    silu = gate * gate_sig
    gated = mixed * silu
    unit = gated * out_scale
    grad_gated = out_scale * (grad_o * gain[...]) - gated * pull
    grad_mixed[...] = grad_gated * silu
    low_out[:, :OWN] = (unit * gain[...]).astype(BF16)
    low_out[:, OWN:] = (grad_gated * mixed * (gate_sig * (1.0 + gate * (1.0 - gate_sig)))).astype(BF16)
    gain_part = jnp.sum(grad_o * unit, 0, keepdims=True)

    @pl.when(pl.program_id(0) == 0)
    def _():
        grad_gain[...] = jnp.broadcast_to(gain_part, grad_gain.shape)

    @pl.when(pl.program_id(0) > 0)
    def _():
        grad_gain[...] += gain_part


def run_gate(grad_out, mixed, proj, sums, gain):
    rows = lambda width: pl.BlockSpec((ROWS, width), lambda i: (i, 0))
    fixed = lambda shape: pl.BlockSpec(shape, lambda i: (0, 0))
    return pl.pallas_call(
        gate_kernel,
        grid=(PACK // ROWS,),
        in_specs=[
            rows(OWN),
            rows(OWN),
            rows(OWN),
            pl.BlockSpec((8, ROWS), lambda i: (0, i)),
            fixed((1, OWN)),
        ],
        out_specs=[rows(2 * OWN), rows(OWN), fixed((8, OWN))],
        out_shape=[
            jax.ShapeDtypeStruct((PACK, 2 * OWN), BF16),
            jax.ShapeDtypeStruct((PACK, OWN), F32),
            jax.ShapeDtypeStruct((8, OWN), F32),
        ],
        compiler_params=pltpu.CompilerParams(
            dimension_semantics=("arbitrary",), vmem_limit_bytes=VMEM_LIMIT
        ),
        cost_estimate=COST,
        name="gate_backward",
    )(grad_out, mixed, proj, sums, gain)


def early_grad_kernel(low, grad_branch, normed, out):
    step = pl.program_id(0)

    @pl.when(step == 0)
    def _():
        out[...] = jnp.zeros_like(out)

    for k in range(4):
        part = product(low[:, :OWN], grad_branch[:, k * WIDE : (k + 1) * WIDE], 0, 0)
        for m in range(4):
            out[eight_order(4 * k + m), :SHARD_IN] += part[m * SHARD_IN : (m + 1) * SHARD_IN]
    part = product(normed[...], low[:, OWN:], 0, 0)
    for f in range(N_FSDP):
        out[eight_order(f), SHARD_IN:] += part[f * SHARD_IN : (f + 1) * SHARD_IN]


def run_early_grad(low, grad_branch, normed):
    count = 2 * ROWS
    rows = lambda width: pl.BlockSpec((count, width), lambda i: (i, 0))
    shape = (N_FSDP, 2 * SHARD_IN, WIDE)
    return pl.pallas_call(
        early_grad_kernel,
        grid=(PACK // count,),
        in_specs=[rows(2 * OWN), rows(D), rows(D)],
        out_specs=pl.BlockSpec(shape, lambda i: (0, 0, 0)),
        out_shape=jax.ShapeDtypeStruct(shape, F32),
        compiler_params=pltpu.CompilerParams(
            dimension_semantics=("arbitrary",), vmem_limit_bytes=VMEM_LIMIT
        ),
        cost_estimate=COST,
        name="early_grad",
    )(low, grad_branch, normed)


def block_out_kernel(rows, weight, tokens, live, out):
    step = pl.program_id(0)
    part = matmul(jnp.concatenate([rows[0], rows[1]], 1), weight[...].reshape(2 * OWN, D))

    @pl.when(step == 0)
    def _():
        out[...] = part

    @pl.when(step > 0)
    def _():
        out[...] += part

    @pl.when(step == N_REP // 2 - 1)
    def _():
        out[...] = tokens[...].astype(F32) + live[...] * out[...]


def run_block_out(rows, weight, tokens, live):
    fixed = lambda shape: pl.BlockSpec(shape, lambda i: (0, 0))
    return pl.pallas_call(
        block_out_kernel,
        grid=(N_REP // 2,),
        in_specs=[
            pl.BlockSpec((2, ROWS, OWN), lambda i: (i, 0, 0)),
            pl.BlockSpec((2, 2, 1, SHARD_OUT, D), lambda i: (i % 2, 0, i // 2, 0, 0)),
            fixed((ROWS, D)),
            fixed((ROWS, 1)),
        ],
        out_specs=fixed((ROWS, D)),
        out_shape=jax.ShapeDtypeStruct((ROWS, D), F32),
        compiler_params=pltpu.CompilerParams(
            dimension_semantics=("arbitrary",), vmem_limit_bytes=VMEM_LIMIT
        ),
        cost_estimate=FILL,
        name="block_out",
    )(rows, weight, tokens, live)


def turned_part(weight, rows):
    return product(weight[...].reshape(D, weight.shape[-1]), rows, 1, 1)


def columns_of(full_in, width, index):
    return pl.BlockSpec(full_in.shape[:-1] + (width,), lambda i: (0, 0, 0, 0, index(i)))


def z_grad_kernel(rows, weight, out):
    part = turned_part(weight, jnp.concatenate([rows[0], rows[1]], 1))

    @pl.when(pl.program_id(0) == 0)
    def _():
        out[...] = part

    @pl.when(pl.program_id(0) > 0)
    def _():
        out[...] += part


def run_z_grad(rows, full_in):
    return pl.pallas_call(
        z_grad_kernel,
        grid=(N_REP // 2,),
        in_specs=[
            pl.BlockSpec((2, ROWS, OWN), lambda i: (i, 0, 1)),
            columns_of(full_in, 2 * OWN, lambda i: i),
        ],
        out_specs=pl.BlockSpec((D, ROWS), lambda i: (0, 0)),
        out_shape=jax.ShapeDtypeStruct((D, ROWS), F32),
        compiler_params=pltpu.CompilerParams(
            dimension_semantics=("arbitrary",), vmem_limit_bytes=VMEM_LIMIT
        ),
        cost_estimate=FILL,
        name="z_grad",
    )(rows, full_in)


def input_grad_kernel(
    own_half, grad_z, x_rows, rest_rows, w_x, w_bc, low_dt, tokens, cotangent, gain, out, gain_out, total, ordered
):
    step = pl.program_id(0)
    part = turned_part(w_x, jnp.concatenate([x_rows[0], x_rows[1]], 1))

    @pl.when(step == 0)
    def _():
        total[...] = grad_z[...] + part

    @pl.when(step > 0)
    def _():
        total[...] += part

    @pl.when(step == N_REP // 2 - 1)
    def _():
        lane = lax.broadcasted_iota(jnp.int32, (ROWS, N), 1)
        groups = []
        for k in range(2):
            group = jnp.zeros((ROWS, N), F32)
            for m in range(4):
                value = rest_rows[4 * k + m].astype(F32)
                value = value if m == 0 else pltpu.roll(value, m * OWN_BC, 1)
                group = jnp.where((lane >= m * OWN_BC) & (lane < (m + 1) * OWN_BC), value, group)
            groups.append(group.astype(BF16))
        steps = jnp.zeros((ROWS, N), F32)
        for m in range(N_REP):
            start = 8 + m * OWN_H
            value = pltpu.roll(rest_rows[m].astype(F32), (start - OWN_BC) % N, 1)
            steps = jnp.where((lane >= start) & (lane < start + OWN_H), value, steps)
        total[...] += turned_part(w_bc, jnp.concatenate(groups, 1))
        for f in range(N_FSDP):
            place = eight_order(f) - f // 8 + (f // 8 + own_half[0]) % 2
            start = pl.multiple_of(place * SHARD_IN, SHARD_IN)
            ordered[f * SHARD_IN : (f + 1) * SHARD_IN, :] = total[pl.ds(start, SHARD_IN), :]
        grad_h = (ordered[...] + product(low_dt[...], steps.astype(BF16), 1, 1)).T
        values = tokens[...].astype(F32)
        scale = lax.rsqrt(jnp.mean(values * values, axis=1, keepdims=True) + NORM_EPS)
        unit = values * scale
        gain_sum = jnp.sum(grad_h * unit, 0, keepdims=True)
        gain_out[...] = jnp.zeros_like(gain_out)
        for k in range(D // TAIL):
            gain_out[k : k + 1, :] = gain_sum[:, k * TAIL : (k + 1) * TAIL]
        grad_unit = grad_h * gain[...]
        inner = jnp.mean(grad_unit * unit, axis=1, keepdims=True)
        out[...] = cotangent[...].astype(F32) + scale * (grad_unit - unit * inner)


def run_input_grad(own_half, grad_z, tail_rows, full_in, low_dt, tokens, cotangent, gain):
    fixed = lambda shape: pl.BlockSpec(shape, lambda i: (0,) * len(shape))
    return pl.pallas_call(
        input_grad_kernel,
        grid=(N_REP // 2,),
        in_specs=[
            pl.BlockSpec(memory_space=pltpu.SMEM),
            fixed((D, ROWS)),
            pl.BlockSpec((2, ROWS, OWN), lambda i: (i, 0, 0)),
            pl.BlockSpec((N_REP, ROWS, N), lambda i: (0, 0, OWN // N)),
            columns_of(full_in, 2 * OWN, lambda i: N_REP // 2 + i),
            columns_of(full_in, 2 * N, lambda i: DI // N),
            fixed((D, N)),
            fixed((ROWS, D)),
            fixed((ROWS, D)),
            fixed((1, D)),
        ],
        out_specs=[fixed((ROWS, D)), fixed((8, TAIL))],
        out_shape=[jax.ShapeDtypeStruct((ROWS, D), F32), jax.ShapeDtypeStruct((8, TAIL), F32)],
        scratch_shapes=[pltpu.VMEM((D, ROWS), F32), pltpu.VMEM((D, ROWS), F32)],
        compiler_params=pltpu.CompilerParams(
            dimension_semantics=("arbitrary",), vmem_limit_bytes=VMEM_LIMIT
        ),
        cost_estimate=COST,
        name="input_grad",
    )(own_half, grad_z, tail_rows, tail_rows, full_in, full_in, low_dt, tokens, cotangent, gain)


def rest_kernel(
    ends, parts, pre_b, pre_c, conv_in, par, grad_x, grad_dt, sums, head_acc, grad_gain, first, tail_out, small_out
):
    own = lax.broadcasted_iota(jnp.int32, (OWN_BC, 2 * N), 0) + first[0]
    chosen = (lax.broadcasted_iota(jnp.int32, (OWN_BC, 2 * N), 1) == own).astype(F32).astype(BF16)

    def pick(value):
        return product(jnp.concatenate([chosen] * 3, 1), jnp.concatenate(split_three(value), 1), 1, 1)

    grad = parts[0]
    for k in range(1, N_REP):
        grad = grad + parts[k]
    own_pre = pick(jnp.concatenate([pre_b[...], pre_c[...]], 1))
    own_conv = product(chosen, conv_in[...].astype(BF16), 1, 1)
    taps = pick(par[:, OWN:])
    sig = jax.nn.sigmoid(own_pre)
    grad_pre = grad * (sig * (1.0 + own_pre * (1.0 - sig)))
    position = lax.broadcasted_iota(jnp.int32, (1, PACK), 1)

    def segment(places):
        counted = jnp.zeros_like(places)
        for k in range(3):
            counted = counted + (places >= ends[k]).astype(jnp.int32)
        return counted

    grad_conv = taps[:, CONV - 1 : CONV] * grad_pre
    column = lax.broadcasted_iota(jnp.int32, (OWN_BC, N), 1)
    found = jnp.where(column == CONV, jnp.sum(grad_pre, 1, keepdims=True), 0.0)
    found = jnp.where(column == CONV - 1, jnp.sum(own_conv * grad_pre, 1, keepdims=True), found)
    for later_by in range(1, CONV):
        same = (segment(position + later_by) == segment(position)) & (position < PACK - later_by)
        later = jnp.where(same, pltpu.roll(grad_pre, PACK - later_by, 1), 0.0)
        tap = CONV - 1 - later_by
        found = jnp.where(column == tap, jnp.sum(own_conv * later, 1, keepdims=True), found)
        grad_conv = grad_conv + taps[:, tap : tap + 1] * later
    lane = lax.broadcasted_iota(jnp.int32, (N, N), 1)
    filler = jnp.zeros((N - OWN_BC, N), F32)
    for k in range(PACK // N):
        rows = slice(k * N, (k + 1) * N)
        columns = jnp.concatenate([grad_conv[:, rows], filler], 0).T
        steps = pltpu.roll(grad_dt[rows, :].astype(F32), OWN_BC, 1)
        tail_out[rows, :OWN] = grad_x[rows, :]
        tail_out[rows, OWN:] = jnp.where(
            lane < OWN_BC, columns, jnp.where(lane < OWN_BC + OWN_H, steps, 0.0)
        ).astype(BF16)
    row = lax.broadcasted_iota(jnp.int32, (8, OWN), 0)
    skip = head_sums(sums[...])
    by_head = jnp.concatenate([skip, jnp.zeros((8, OWN - N), F32)], 1)
    logs = jnp.concatenate([head_acc[...], jnp.zeros((8, OWN - N), F32)], 1)
    wide = jnp.where(row == 0, grad_gain[0:1, :], jnp.where(row < 6, sums[...], 0.0))
    wide = jnp.where(row == 6, logs[1:2, :], jnp.where(row == 7, by_head[6:7, :], wide))
    turned = jnp.concatenate([found, filler], 0).T
    first_row = lax.broadcasted_iota(jnp.int32, (8, N), 0) == 0
    small_out[:, :OWN] = wide
    small_out[:, OWN:] = jnp.where(first_row, head_acc[0:1, :], pltpu.roll(turned[:8], 1, 0))


def run_rest(ends, parts, pre, proj, par, grad_x, grad_dt, sums, head_acc, grad_gain, first):
    fixed = lambda shape: pl.BlockSpec(shape, lambda i: (0,) * len(shape))
    return pl.pallas_call(
        rest_kernel,
        grid=(1,),
        in_specs=[
            pl.BlockSpec(memory_space=pltpu.SMEM),
            fixed((N_REP, OWN_BC, PACK)),
            pl.BlockSpec((PACK, N), lambda i: (0, 3)),
            pl.BlockSpec((PACK, N), lambda i: (0, 4)),
            pl.BlockSpec((PACK, 2 * N), lambda i: (0, 3)),
            fixed((16, 640)),
            fixed((PACK, OWN)),
            fixed((PACK, N)),
            fixed((8, OWN)),
            fixed((8, N)),
            fixed((8, OWN)),
            pl.BlockSpec(memory_space=pltpu.SMEM),
        ],
        out_specs=[fixed((PACK, TAIL)), fixed((8, TAIL))],
        out_shape=[jax.ShapeDtypeStruct((PACK, TAIL), BF16), jax.ShapeDtypeStruct((8, TAIL), F32)],
        compiler_params=pltpu.CompilerParams(
            dimension_semantics=("arbitrary",), vmem_limit_bytes=VMEM_LIMIT
        ),
        cost_estimate=COST,
        name="rest_backward",
    )(ends, parts, pre, pre, proj, par, grad_x, grad_dt, sums, head_acc, grad_gain, first)


def tail_grad_kernel(normed, tail, small, out):
    step = pl.program_id(0)
    part = product(normed[...], tail[...], 0, 0)
    for f in range(N_FSDP):
        rows = part[f * SHARD_IN : (f + 1) * SHARD_IN]

        @pl.when(step == 0)
        def _(f=f, rows=rows):
            out[eight_order(f), :SHARD_IN] = rows
            out[eight_order(f), SHARD_IN:] = small[...]

        @pl.when(step > 0)
        def _(f=f, rows=rows):
            out[eight_order(f), :SHARD_IN] += rows


def run_tail_grad(normed, tail, small):
    count = 2 * ROWS
    shape = (N_FSDP, SHARD_IN + 8, TAIL)
    return pl.pallas_call(
        tail_grad_kernel,
        grid=(PACK // count,),
        in_specs=[
            pl.BlockSpec((count, D), lambda i: (i, 0)),
            pl.BlockSpec((count, TAIL), lambda i: (i, 0)),
            pl.BlockSpec((8, TAIL), lambda i: (0, 0)),
        ],
        out_specs=pl.BlockSpec(shape, lambda i: (0, 0, 0)),
        out_shape=jax.ShapeDtypeStruct(shape, F32),
        compiler_params=pltpu.CompilerParams(
            dimension_semantics=("arbitrary",), vmem_limit_bytes=VMEM_LIMIT
        ),
        cost_estimate=COST,
        name="tail_grad",
    )(normed, tail, small)


def adam_step(grad, weight, first, second, grad_out, first_out, second_out, weight_out):
    new_weight, new_first, new_second = adam_update(
        weight[...], grad, first[...], second[...], RATE_MATRIX, WEIGHT_DECAY
    )
    grad_out[...] = grad
    first_out[...] = new_first
    second_out[...] = new_second
    weight_out[...] = new_weight


def adam_early_kernel(rows, pair, *refs):
    arrays, grad = refs[:-1], refs[-1]
    grad[:, :WIDE] = pair[0, rows, :]
    grad[:, WIDE:] = pair[1, rows, :]
    adam_step(grad[...], *arrays)


def run_adam_early(place_of, rows, parts, weight, first, second):
    part = pl.BlockSpec((SHARD_IN, 2 * WIDE), place_of)
    shape = jax.ShapeDtypeStruct(weight.shape, F32)
    return pl.pallas_call(
        partial(adam_early_kernel, rows),
        grid=(N_REP // 2,),
        in_specs=[pl.BlockSpec((2,) + parts.shape[1:], lambda i: (i, 0, 0))] + [part] * 3,
        out_specs=[part] * 4,
        out_shape=[shape] * 4,
        scratch_shapes=[pltpu.VMEM((SHARD_IN, 2 * WIDE), F32)],
        compiler_params=pltpu.CompilerParams(
            dimension_semantics=("arbitrary",), vmem_limit_bytes=VMEM_LIMIT
        ),
        cost_estimate=FILL,
        name="adam",
    )(parts, weight, first, second)


def adam_tail_kernel(pair, rest, *refs):
    arrays, grad = refs[:3] + refs[-5:-1], refs[-1]
    step = pl.program_id(0)

    @pl.when(step < N_REP // 2)
    def _():
        grad[:, :WIDE] = pair[0, :SHARD_IN]
        grad[:, WIDE:] = pair[1, :SHARD_IN]

    @pl.when(step == N_REP // 2)
    def _():
        lane = lax.broadcasted_iota(jnp.int32, (SHARD_IN, N), 1)
        for k in range(2):
            group = jnp.zeros((SHARD_IN, N), F32)
            for m in range(4):
                value = rest[4 * k + m, :SHARD_IN]
                value = value if m == 0 else pltpu.roll(value, m * OWN_BC, 1)
                group = jnp.where((lane >= m * OWN_BC) & (lane < (m + 1) * OWN_BC), value, group)
            grad[:, k * N : (k + 1) * N] = group

    adam_step(grad[...], *arrays)


def run_adam_tail(parts, weight, first, second, before):
    half = N_REP // 2
    rows = parts.shape[1]
    column = pl.BlockSpec((SHARD_IN, 2 * WIDE), lambda i: (0, half + i))
    shape = jax.ShapeDtypeStruct(weight.shape, F32)
    return pl.pallas_call(
        adam_tail_kernel,
        grid=(half + 1,),
        in_specs=[
            pl.BlockSpec((2, rows, OWN), lambda i: (jnp.minimum(i, half - 1), 0, 0)),
            pl.BlockSpec((N_REP, rows, N), lambda i: (0, 0, OWN // N)),
        ]
        + [column] * 3
        + [pl.BlockSpec(memory_space=pl.ANY)] * 4,
        out_specs=[column] * 4,
        out_shape=[shape] * 4,
        input_output_aliases={5 + k: k for k in range(4)},
        scratch_shapes=[pltpu.VMEM((SHARD_IN, 2 * WIDE), F32)],
        compiler_params=pltpu.CompilerParams(
            dimension_semantics=("arbitrary",), vmem_limit_bytes=VMEM_LIMIT
        ),
        cost_estimate=COST,
        name="adam_tail",
    )(parts, parts, weight, first, second, *before)


def body(
    tokens,
    cotangent,
    lengths,
    w_in,
    w_dt,
    w_out,
    small,
    first_in,
    first_dt,
    first_out,
    first_small,
    second_in,
    second_dt,
    second_out,
    second_small,
):
    place = Place()
    r = place.r
    zero = jnp.int32(0)
    pack_lengths = lax.dynamic_slice_in_dim(lengths, place.f, 1, 0)[0]
    seg_ends = jnp.cumsum(pack_lengths)
    own_positions = r * ROWS + jnp.arange(ROWS, dtype=jnp.int32)
    own_live = (segment_at(own_positions, seg_ends) < 3).astype(F32)[:, None]
    slots = jnp.arange(N_REP, dtype=jnp.int32)
    ahead = ((place.x + slots // 2) % 4) * 2 + (place.yl + slots) % 2
    half = ROWS // 2

    in_low = w_in.astype(BF16)
    dt_low = w_dt.astype(BF16)
    out_low = w_out.astype(BF16)

    small_rows = jnp.pad(small.astype(BF16), (0, 16 * 3 * WIDE - SHARD_SMALL)).reshape(16, 3 * WIDE)

    def own_columns(rep):
        columns = jnp.concatenate(
            [
                lax.dynamic_slice_in_dim(in_low, rep * OWN, OWN, 1),
                lax.dynamic_slice_in_dim(in_low, DI + rep * OWN, OWN, 1),
                in_low[:, 2 * DI :],
                lax.dynamic_slice_in_dim(dt_low, rep * OWN_H, OWN_H, 1),
                jnp.zeros((SHARD_IN, 2), BF16),
                dt_low,
                jnp.zeros((SHARD_IN, N - 8 - H), BF16),
            ],
            1,
        )
        return jnp.concatenate([columns, small_rows], 0)

    other_columns = move(
        own_columns(2 * place.x + 1 - place.yl), lambda yh, z, c, x, yl: (yh + 1, z, c, x, yl + 1)
    )
    from_left = move(tokens, along_x(1))
    from_right = move(tokens, along_x(-1))
    partner = move(tokens, swap_y)

    out_low, other_columns = lax.optimization_barrier((out_low, other_columns))
    out_other = move(out_low, lambda yh, z, c, x, yl: (yh + 1, z, c, x, yl + 1))
    branch = (cotangent.astype(F32) * own_live).astype(BF16)
    from_left, from_right, partner, other_columns, branch = lax.optimization_barrier(
        (from_left, from_right, partner, other_columns, branch)
    )
    own_shards = gather_eight(both(own_columns(r), other_columns, place.yh))
    far = move(from_left, along_x(1))
    partner_left = move(from_left, swap_y)
    partner_right = move(partner, along_x(-1))

    b_partner = move(branch, swap_y)
    far, partner_left, partner_right, out_other, branch, in_low = lax.optimization_barrier(
        (far, partner_left, partner_right, out_other, branch, in_low)
    )
    in_other = move(in_low, lambda yh, z, c, x, yl: (yh + 1, z, c, x, yl + 1))
    out_pair = both(out_low, out_other, place.yh)
    partner_far_top = move(partner_left[:half], along_x(1))
    partner_far_low = move(partner_right[half:], along_x(-1))

    vector = own_shards[:, :, :, SHARD_IN : SHARD_IN + 2].transpose(2, 0, 1, 3, 4)
    vector = vector.reshape(N_FSDP, 6 * WIDE)[:, :SHARD_SMALL].reshape(-1).astype(F32)
    offset = 0
    gain_in = vector[None, :D]
    offset = D
    gain_row = lax.dynamic_slice_in_dim(vector, offset + r * OWN, OWN, 0)[None, :]
    offset += DI
    taps = vector[offset : offset + (CONV + 1) * CHANNELS].reshape(CONV + 1, CHANNELS)
    offset += (CONV + 1) * CHANNELS
    per_head = vector[offset:].reshape(3, H)
    dt_bias, a_log, d_skip = lax.dynamic_slice_in_dim(per_head, r * OWN_H, OWN_H, 1)
    taps_bc = taps[:, DI:]
    conv_par = jnp.concatenate([lax.dynamic_slice_in_dim(taps, r * OWN, OWN, 1), taps_bc], 1)
    head_par = jnp.stack(
        [
            jnp.pad(jnp.broadcast_to(d_skip[:, None], (OWN_H, P_SIZE)).reshape(-1), (0, 2 * N)),
            jnp.pad(dt_bias, (0, 640 - OWN_H)),
            jnp.pad(-jnp.exp(a_log), (0, 640 - OWN_H)),
        ],
        0,
    )
    par = jnp.concatenate([conv_par, head_par, jnp.zeros((8, 640), F32)], 0)

    partner_far_top, partner_far_low, own_shards, b_partner = lax.optimization_barrier(
        (partner_far_top, partner_far_low, own_shards, b_partner)
    )
    full_out = gather_eight(tie(out_pair, own_shards))
    b_left = move(branch, along_x(1))
    b_right = move(branch, along_x(-1))
    token_pieces = [
        tokens, partner, from_right, partner_right, far,
        partner_far_top, partner_far_low, from_left, partner_left,
    ]
    normed, proj, low_dt = run_project(ahead, token_pieces, gain_in, own_shards)
    b_left, b_right, b_partner, proj = lax.optimization_barrier((b_left, b_right, b_partner, proj))
    b_far = move(b_left, along_x(1))
    b_partner_left = move(b_left, swap_y)
    b_partner_right = move(b_partner, along_x(-1))
    before = run_forward(0, seg_ends, proj, par)
    b_far, b_partner_left, b_partner_right, before = lax.optimization_barrier(
        (b_far, b_partner_left, b_partner_right, before)
    )
    b_partner_far_top = move(b_partner_left[:half], along_x(1))
    b_partner_far_low = move(b_partner_right[half:], along_x(-1))
    pre, mixed, states, _ = run_forward(1, seg_ends, proj, par, before)
    mixed, in_low, in_other, b_partner_far_top, b_partner_far_low = lax.optimization_barrier(
        (mixed, in_low, in_other, b_partner_far_top, b_partner_far_low)
    )
    full_in = gather_eight(jnp.stack([in_low, in_other], 0))
    branch_pieces = [
        branch, b_partner, b_right, b_partner_right, b_far,
        b_partner_far_top, b_partner_far_low, b_left, b_partner_left,
    ]
    rep_table = jnp.concatenate([ahead, r[None]])
    grad_branch, grad_normed_out, sums = run_out_grad(rep_table, branch_pieces, full_out, mixed, proj, gain_row)
    sums = share_rep(sums[:2].reshape(32, 128)).sum(0).reshape(2, PACK)
    sums = jnp.concatenate([sums, jnp.zeros((6, PACK), F32)], 0)

    low, grad_mixed, grad_gain = run_gate(grad_normed_out, mixed, proj, sums, gain_row)

    low_rows = exchange(low.reshape(N_REP, ROWS, 2 * OWN), "rep")
    grad_x, grad_dtraw, grad_bc, grad_sums, grad_heads = run_backward(
        seg_ends, proj, pre, mixed, grad_mixed, states, par
    )
    low, grad_x = lax.optimization_barrier((low, grad_x))
    early_grad = run_early_grad(low, grad_branch, normed)
    low_rows, early_grad, grad_bc, grad_x = lax.optimization_barrier((low_rows, early_grad, grad_bc, grad_x))

    grad_bc = exchange(grad_bc, "rep").reshape(N_REP, OWN_BC, PACK)
    early = scatter_eight(early_grad)
    grad_rows = run_z_grad(low_rows, full_in)
    grad_bc, grad_rows = lax.optimization_barrier((grad_bc, grad_rows))

    tail, small_own = run_rest(
        seg_ends, grad_bc, pre, proj, par, grad_x, grad_dtraw, grad_sums, grad_heads, grad_gain, (r * OWN_BC)[None]
    )
    grad_tail = run_tail_grad(normed, tail, small_own)
    tail, grad_tail, low_rows = lax.optimization_barrier((tail, grad_tail, low_rows))
    tail_rows = exchange(tail.reshape(N_REP, ROWS, TAIL), "rep")
    tail_part = scatter_eight(grad_tail)
    block_out = run_block_out(low_rows, full_out, tokens, own_live)
    early, block_out = lax.optimization_barrier((early, block_out))
    mine, other = at(early, place.yh), at(early, 1 - place.yh)
    out_mine = move(
        mine[:SHARD_IN], lambda yh, z, c, x, yl: (x // 2, (x % 2) * 2 + yl, z % 2, 2 * c + yh, z // 2)
    )
    out_other = move(
        other[:SHARD_IN], lambda yh, z, c, x, yl: (x // 2, (x % 2) * 2 + yl, z % 2, 2 * c + 1 - yh, z // 2)
    )
    z_other = move(other[SHARD_IN:], swap_y_hi)
    tail_rows, out_mine, out_other, z_other = lax.optimization_barrier((tail_rows, out_mine, out_other, z_other))

    input_grad, grad_gain_in = run_input_grad(
        place.yh[None], grad_rows, tail_rows, full_in, low_dt, tokens, cotangent, gain_in
    )
    early = jnp.concatenate([out_mine + out_other, mine[SHARD_IN:] + z_other], 0)
    early, grad_gain_in = lax.optimization_barrier((early, grad_gain_in))

    early_parts = share_rep(early)
    grad_gain_in = sum_z(grad_gain_in + move(grad_gain_in, swap_core))
    tail_part, grad_gain_in = lax.optimization_barrier((tail_part, grad_gain_in))
    tail_other = move(with_rows(at(tail_part, 1 - place.yh), grad_gain_in), swap_y_hi)
    tail_part = with_rows(at(tail_part, place.yh), grad_gain_in) + tail_other

    tail_part, early_parts = lax.optimization_barrier((tail_part, early_parts))
    tail_parts = share_rep(tail_part)

    grad_out, new_first_out, new_second_out, new_out = run_adam_early(
        lambda i: (i // 2, i % 2), slice(0, SHARD_IN), early_parts, w_out, first_out, second_out
    )
    updated = run_adam_early(
        lambda i: (0, i), slice(SHARD_IN, 2 * SHARD_IN), early_parts, w_in, first_in, second_in
    )
    grad_in, new_first_in, new_second_in, new_in = run_adam_tail(tail_parts, w_in, first_in, second_in, updated)

    def columns(parts):
        return parts.transpose(1, 0, 2).reshape(parts.shape[1], -1)

    small_parts = tail_parts[:, SHARD_IN : SHARD_IN + 8]
    grad_gain_in = tail_parts[:, SHARD_IN + 8 : SHARD_IN + 8 + D // TAIL].sum(0).reshape(-1)
    small_x = small_parts[:, :, :OWN].transpose(1, 0, 2).reshape(8, DI)
    small_bc = small_parts[:, :, OWN:].transpose(1, 0, 2)

    def channels(row):
        return jnp.concatenate([small_x[row], small_bc[row, :, :OWN_BC].reshape(-1)])

    grad_small_all = jnp.concatenate(
        [grad_gain_in, small_x[0]]
        + [channels(row) for row in range(1, 6)]
        + [
            small_bc[0, :, :OWN_H].reshape(-1),
            small_parts[:, 6, :OWN_H].reshape(-1),
            small_parts[:, 7, :OWN_H].reshape(-1),
        ]
    )
    grad_small = lax.dynamic_slice_in_dim(grad_small_all, place.f * SHARD_SMALL, SHARD_SMALL, 0)
    grad_dt = columns(tail_parts[:, :SHARD_IN, OWN + OWN_BC : OWN + OWN_BC + OWN_H])
    new_dt, new_first_dt, new_second_dt = adam_update(
        w_dt, grad_dt, first_dt, second_dt, RATE_MATRIX, WEIGHT_DECAY
    )
    new_small, new_first_small, new_second_small = adam_update(
        small, grad_small, first_small, second_small, RATE_SMALL, 0.0
    )
    return (
        block_out,
        input_grad,
        grad_in,
        grad_dt,
        grad_out,
        grad_small,
        new_first_in,
        new_first_dt,
        new_first_out,
        new_first_small,
        new_second_in,
        new_second_dt,
        new_second_out,
        new_second_small,
        new_in,
        new_dt,
        new_out,
        new_small,
    )


def solution(mesh):
    rows = P(("fsdp", "rep"), None)
    matrix = P("fsdp", None)
    vector = P("fsdp")
    group = (matrix, matrix, matrix, vector)
    return jax.shard_map(
        body,
        mesh=mesh,
        in_specs=(rows, rows, P()) + group * 3,
        out_specs=(rows, rows) + group * 4,
        check_vma=False,
    )
```

```python
from functools import partial

import jax
import jax.numpy as jnp
from jax import lax
from jax.experimental import pallas as pl
from jax.experimental.pallas import tpu as pltpu
from jax.sharding import PartitionSpec as P

D = 1536
H = 48
P_SIZE = 64
N = 128
CONV = 4
STEP = 10
DI = 3072
CHANNELS = DI + 2 * N
SMALL = 21392
N_FSDP = 16
N_REP = 8
ROWS = 256
PACK = 2048
OWN = DI // N_REP
OWN_H = H // N_REP
OWN_BC = 2 * N // N_REP
SHARD_IN = D // N_FSDP
SHARD_OUT = DI // N_FSDP
SHARD_SMALL = SMALL // N_FSDP
WIDE = 384
CHUNK = 128
CHUNKS = PACK // CHUNK
HALF = CHUNKS // 2
TAIL = 512
VMEM_LIMIT = 60 * 1024 * 1024

NORM_EPS = 1e-05
BETA_ONE = 0.9
BETA_TWO = 0.999
ADAM_EPS = 1e-08
WEIGHT_DECAY = 0.1
RATE_MATRIX = 0.04
RATE_SMALL = 0.4
PRECISE = lax.Precision.HIGHEST
BF16 = jnp.bfloat16
F32 = jnp.float32
COST = pl.CostEstimate(flops=1_000_000, bytes_accessed=100_000, transcendentals=0)
FILL = pl.CostEstimate(flops=2_400_000_000, bytes_accessed=20_000_000, transcendentals=0)


def move(value, target):
    pairs = []
    for f in range(N_FSDP):
        for r in range(N_REP):
            yh, z, c, x, yl = target(f // 8, (f // 2) % 4, f % 2, r // 2, r % 2)
            pairs.append((f * N_REP + r, ((yh % 2) * 8 + (z % 4) * 2 + c % 2) * N_REP + (x % 4) * 2 + yl % 2))
    return lax.ppermute(value, ("fsdp", "rep"), pairs)


def along_x(steps):
    return lambda yh, z, c, x, yl: (yh, z, c, x + steps, yl)


def along_z(steps):
    return lambda yh, z, c, x, yl: (yh, z + steps, c, x, yl)


def swap_y(yh, z, c, x, yl):
    return (yh, z, c, x, yl + 1)


def swap_y_hi(yh, z, c, x, yl):
    return (yh + 1, z, c, x, yl)


def swap_core(yh, z, c, x, yl):
    return (yh, z, c + 1, x, yl)


class Place:
    def __init__(self):
        f = lax.axis_index("fsdp")
        r = lax.axis_index("rep")
        self.f, self.r = f, r
        self.yh, self.z, self.c = f // 8, (f // 2) % 4, f % 2
        self.x, self.yl = r // 2, r % 2


def at(value, index, axis=0):
    return lax.dynamic_index_in_dim(value, index, axis, keepdims=False)


def tie(values, *others):
    return lax.optimization_barrier((values, others))[0]


def both(mine, other, second):
    first = jnp.where(second == 0, mine, other)
    last = jnp.where(second == 0, other, mine)
    return jnp.stack([first, last], 0)


def put(out, piece, axis, index):
    starts = [jnp.int32(0)] * out.ndim
    starts[axis] = jnp.int32(index)
    return lax.dynamic_update_slice(out, jnp.expand_dims(piece, axis), tuple(starts))


def swap_shards(value, place):
    other = move(value, lambda yh, z, c, x, yl: (yh + 1, z, c, x, yl + 1))
    return both(value, other, place.yh)


def gather_eight(pair):
    groups = [list(range(8)), list(range(8, 16))]
    out = lax.all_gather(pair, "fsdp", axis=0, tiled=True, axis_index_groups=groups)
    return out.reshape((4, 2) + pair.shape)


def exchange(value, axis):
    return lax.all_to_all(value, axis, 0, 0, tiled=True)


def share_rep(value):
    return exchange(jnp.broadcast_to(value[None], (N_REP,) + value.shape), "rep")


def sum_z(value):
    steps = [move(value, along_z(step)) for step in (1, 3, 2)]
    return value + steps[0] + steps[1] + steps[2]


def scatter_eight(value):
    groups = [list(range(8)), list(range(8, 16))]
    flat = value.reshape(-1, value.shape[-1])
    out = lax.psum_scatter(flat, "fsdp", scatter_dimension=0, tiled=True, axis_index_groups=groups)
    return out.reshape((2,) + value.shape[1:])


def eight_order(f):
    return ((f // 2) % 4 * 2 + f % 2) * 2 + f // 8


def with_rows(block, extra):
    width = block.shape[-1]
    flat = block.reshape(-1, width)
    return flat if extra is None else jnp.concatenate([flat, extra], 0)


def adam_update(weight, gradient, moment_one, moment_two, learn_rate, decay_rate):
    moment_one = BETA_ONE * moment_one + (1.0 - BETA_ONE) * gradient
    moment_two = BETA_TWO * moment_two + (1.0 - BETA_TWO) * gradient * gradient
    scaled = (
        moment_one
        / (1.0 - BETA_ONE**STEP)
        / (jnp.sqrt(moment_two / (1.0 - BETA_TWO**STEP)) + ADAM_EPS)
    )
    return (weight - learn_rate * (scaled + decay_rate * weight), moment_one, moment_two)


def contract_rows(left_side, right_side):
    return lax.dot_general(
        left_side, right_side, (((0,), (0,)), ((), ())), preferred_element_type=F32
    )


def contract_cols(left_side, right_side):
    return lax.dot_general(
        left_side, right_side, (((1,), (1,)), ((), ())), preferred_element_type=F32
    )


def matmul(left_side, right_side):
    return jnp.dot(left_side, right_side, preferred_element_type=F32)


def segment_at(positions, seg_ends):
    counted = jnp.sum((positions[:, None] >= seg_ends[None, :]).astype(jnp.int32), axis=1)
    return jnp.where(positions < 0, jnp.int32(-1), counted)


def split_two(value):
    high = value.astype(BF16)
    return high, (value - high.astype(F32)).astype(BF16)


def split_three(value):
    high = value.astype(BF16)
    rest = value - high.astype(F32)
    middle = rest.astype(BF16)
    return high, middle, (rest - middle.astype(F32)).astype(BF16)


def product(left, right, left_dim, right_dim):
    return lax.dot_general(
        left, right, (((left_dim,), (right_dim,)), ((), ())), preferred_element_type=F32
    )


def joined_product(left_parts, right_parts, left_dim=1, right_dim=0):
    left_high, left_low = left_parts
    right_high, right_low = right_parts
    return product(
        jnp.concatenate([left_high, left_high, left_low], left_dim),
        jnp.concatenate([right_high, right_low, right_high], right_dim),
        left_dim,
        right_dim,
    )


def precise_product(left, right, left_dim=1, right_dim=0):
    return joined_product(split_two(left), split_two(right), left_dim, right_dim)


def ones_product(ones, value):
    return product(jnp.concatenate([ones] * 3, 1), jnp.concatenate(split_three(value), 0), 1, 0)


def spread(per_head, lane):
    return jnp.concatenate(
        [
            jnp.where(lane < P_SIZE, per_head[:, 2 * k : 2 * k + 1], per_head[:, 2 * k + 1 : 2 * k + 2])
            for k in range(OWN_H // 2)
        ],
        1,
    )


def head_sums(value):
    column = lax.broadcasted_iota(jnp.int32, (OWN, N), 0)
    head = lax.broadcasted_iota(jnp.int32, (OWN, N), 1)
    members = ((column >= head * P_SIZE) & (column < (head + 1) * P_SIZE)).astype(F32).astype(BF16)
    high, low = split_two(value)
    return product(jnp.concatenate([high, low], 1), jnp.concatenate([members, members], 0), 1, 0)


def two_heads(pair, lane):
    zero = jnp.zeros_like(pair)
    return jnp.concatenate([jnp.where(lane < P_SIZE, pair, zero), jnp.where(lane < P_SIZE, zero, pair)], 0)


def chunk_facts(ends, chunk, dt_pre, par):
    column = lax.broadcasted_iota(jnp.int32, (CHUNK, 1), 0) + chunk * CHUNK
    row = lax.broadcasted_iota(jnp.int32, (1, CHUNK), 1) + chunk * CHUNK

    def segment(position):
        counted = jnp.zeros_like(position)
        for k in range(3):
            counted = counted + (position >= ends[k]).astype(jnp.int32)
        return jnp.where(position < 0, -1, counted)

    def one_segment(position):
        counted = jnp.int32(0)
        for k in range(3):
            counted = counted + (position >= ends[k]).astype(jnp.int32)
        return jnp.where(position < 0, -1, counted)

    here_column, here_row = segment(column), segment(row)
    prior = one_segment(chunk * CHUNK - 1)
    last = one_segment(chunk * CHUNK + CHUNK - 1)
    lane = lax.broadcasted_iota(jnp.int32, (CHUNK, N), 1)
    shifted = dt_pre + par[6:7, :N]
    soft = jnp.maximum(shifted, 0.0) + jnp.log1p(jnp.exp(-jnp.abs(shifted)))
    step = jnp.where(lane < OWN_H, soft, 0.0)
    decay = step * par[7:8, :N]
    tri_row = lax.broadcasted_iota(jnp.int32, (CHUNK, CHUNK), 0)
    tri_column = lax.broadcasted_iota(jnp.int32, (CHUNK, CHUNK), 1)
    lower = (tri_row >= tri_column).astype(F32).astype(BF16)
    upper = (tri_row <= tri_column).astype(F32).astype(BF16)
    total = ones_product(lower, decay)
    entering = (here_column == prior).astype(F32) * jnp.exp(total)
    end = total[CHUNK - 1 : CHUNK]
    leaving = (here_column == last).astype(F32) * jnp.exp(jnp.minimum(end - total, 0.0))
    passing = jnp.where(last == prior, 1.0, 0.0) * jnp.exp(end)
    return dict(
        column=column,
        segment=segment,
        here_column=here_column,
        here_row=here_row,
        lane=lane,
        shifted=shifted,
        step=step,
        decay=decay,
        total=total,
        entering=entering,
        leaving=leaving,
        passing=passing,
        tri_row=tri_row,
        tri_column=tri_column,
        upper=upper,
    )


def forward_kernel(part, ends, proj, par, *refs):
    if part:
        carry_in, refs = refs[3], refs[4:]
    pre_out, mixed_out, state_out, carry_out, extended, state = refs
    chunk = pl.program_id(0) + part * HALF

    @pl.when(pl.program_id(0) == 0)
    def _():
        if part:
            state[...] = carry_in[:N, :OWN]
            extended[0:8, :] = carry_in[N:, :]
        else:
            state[...] = jnp.zeros_like(state)
            extended[0:8, :] = jnp.zeros((8, 640), F32)

    facts = chunk_facts(ends, chunk, proj[:, 1024:1152], par)
    lane = facts["lane"]
    conv = proj[:, OWN:1024].astype(BF16).astype(F32)
    extended[8 : 8 + CHUNK, :] = conv
    pre = par[4:5] + par[3:4] * conv
    for back in range(1, CONV):
        same = (facts["segment"](facts["column"] - back) == facts["here_column"]).astype(F32)
        pre = pre + par[3 - back : 4 - back] * (extended[8 - back : 8 - back + CHUNK, :] * same)
    extended[0:8, :] = extended[CHUNK : CHUNK + 8, :]
    pre_out[...] = pre
    act = pre * jax.nn.sigmoid(pre)
    own_x, state_b, state_c = act[:, :OWN], act[:, OWN : OWN + N], act[:, OWN + N :]
    stepped = own_x * spread(facts["step"], lane)
    b_parts, c_parts = split_two(state_b), split_two(state_c)
    inside = (facts["tri_row"] >= facts["tri_column"]) & (facts["here_column"] == facts["here_row"])
    scores = jnp.where(inside, joined_product(c_parts, b_parts, 1, 1), 0.0)
    total_rows = facts["total"].T
    state_in = state[...]
    state_out[...] = state_in
    outs = []
    for pair in range(OWN_H // 2):
        mixing = []
        for head in (2 * pair, 2 * pair + 1):
            span = facts["total"][:, head : head + 1] - total_rows[head : head + 1, :]
            mixing.append(jnp.exp(jnp.minimum(span, 0.0)) * scores)
        inner = two_heads(stepped[:, pair * N : pair * N + N], lane)
        outs.append(precise_product(jnp.concatenate(mixing, 1), inner))
    scanned = jnp.concatenate(outs, 1) + spread(facts["entering"], lane) * joined_product(
        c_parts, split_two(state_in)
    )
    state[...] = spread(facts["passing"], lane[:1]) * state_in + precise_product(
        state_b.T, stepped * spread(facts["leaving"], lane)
    )
    mixed_out[...] = scanned + par[5:6, :OWN] * own_x

    @pl.when(pl.program_id(0) == HALF - 1)
    def _():
        carry_out[:N, :OWN] = state[...]
        carry_out[:N, OWN:] = jnp.zeros((N, 640 - OWN), F32)
        carry_out[N:, :] = extended[0:8, :]


def run_forward(part, ends, proj, par, before=()):
    here = lambda i: (i + part * HALF, 0)
    chunked = lambda width: pl.BlockSpec((CHUNK, width), here)
    fixed = lambda shape: pl.BlockSpec(shape, lambda i: (0, 0))
    carry = fixed((N + 8, 640))
    return pl.pallas_call(
        partial(forward_kernel, part),
        grid=(HALF,),
        in_specs=[pl.BlockSpec(memory_space=pltpu.SMEM), chunked(1152), fixed((16, 640))]
        + ([pl.BlockSpec(memory_space=pl.ANY)] * 3 + [carry] if part else []),
        out_specs=[chunked(640), chunked(OWN), pl.BlockSpec((N, OWN), here), carry],
        out_shape=[
            jax.ShapeDtypeStruct((PACK, 640), F32),
            jax.ShapeDtypeStruct((PACK, OWN), F32),
            jax.ShapeDtypeStruct((CHUNKS * N, OWN), F32),
            jax.ShapeDtypeStruct((N + 8, 640), F32),
        ],
        input_output_aliases={3: 0, 4: 1, 5: 2} if part else {},
        scratch_shapes=[pltpu.VMEM((CHUNK + 8, 640), F32), pltpu.VMEM((N, OWN), F32)],
        compiler_params=pltpu.CompilerParams(
            dimension_semantics=("arbitrary",), vmem_limit_bytes=VMEM_LIMIT
        ),
        cost_estimate=COST,
        name="scan_forward",
    )(ends, proj, par, *before)


def backward_kernel(ends, conv_in, dt_in, pre_in, mixed_in, grad_mixed, state_all, par, *refs):
    grad_x, grad_dt, grad_bc, sums, head_acc, carried, extended, end_dot = refs
    step_index = pl.program_id(0)
    chunk = CHUNKS - 1 - step_index

    @pl.when(step_index == 0)
    def _():
        carried[...] = jnp.zeros_like(carried)
        extended[CHUNK : CHUNK + 8, :] = jnp.zeros((8, OWN), F32)
        end_dot[...] = jnp.zeros_like(end_dot)
        sums[...] = jnp.zeros_like(sums)
        head_acc[...] = jnp.zeros_like(head_acc)

    facts = chunk_facts(ends, chunk, dt_in[...], par)
    lane = facts["lane"]
    pre = pre_in[...]
    sig = jax.nn.sigmoid(pre)
    act = pre * sig
    own_x, state_b, state_c = act[:, :OWN], act[:, OWN : OWN + N], act[:, OWN + N :]
    step = facts["step"]
    step_wide = spread(step, lane)
    stepped = own_x * step_wide
    skip = par[5:6, :OWN]
    scanned = mixed_in[...] - skip * own_x
    grad_m = grad_mixed[...]
    sums[6:7] += jnp.sum(grad_m * own_x, 0, keepdims=True)

    b_parts, c_parts = split_two(state_b), split_two(state_c)
    inside = (facts["tri_row"] <= facts["tri_column"]) & (facts["here_column"] == facts["here_row"])
    scores = jnp.where(inside, joined_product(b_parts, c_parts, 1, 1), 0.0)
    total_rows = facts["total"].T
    grad_scores = jnp.zeros((CHUNK, CHUNK), F32)
    grad_stepped = []
    for pair in range(OWN_H // 2):
        columns = slice(pair * N, pair * N + N)
        grad_pair = grad_m[:, columns]
        high, low = split_two(grad_pair)
        stepped_parts = split_two(two_heads(stepped[:, columns], lane))
        grad_mixing = joined_product(stepped_parts, (high, low), 1, 1)
        mixing = []
        for k in range(2):
            head = 2 * pair + k
            span = total_rows[head : head + 1, :] - facts["total"][:, head : head + 1]
            decays = jnp.exp(jnp.minimum(span, 0.0))
            mixing.append(decays * scores)
            grad_scores = grad_scores + decays * grad_mixing[k * CHUNK : (k + 1) * CHUNK]
        grad_stepped.append(
            joined_product(
                split_two(jnp.concatenate(mixing, 1)), (two_heads(high, lane), two_heads(low, lane))
            )
        )
    grad_scores = jnp.where(inside, grad_scores, 0.0)
    carry = carried[...]
    carry_parts = split_two(carry)
    leaving = spread(facts["leaving"], lane)
    grad_stepped = jnp.concatenate(grad_stepped, 1) + leaving * joined_product(b_parts, carry_parts)
    state_in = state_all[...]
    entered = spread(facts["entering"], lane) * grad_m
    entered_parts = split_two(entered)
    grad_b = precise_product(grad_scores, state_c) + joined_product(
        split_two(leaving * stepped), carry_parts, 1, 1
    )
    grad_c = precise_product(grad_scores.T, state_b) + joined_product(
        entered_parts, split_two(state_in), 1, 1
    )
    grad_bc[0:N, :] = grad_b.T
    grad_bc[N:, :] = grad_c.T
    new_carry = spread(facts["passing"], lane[:1]) * carry + joined_product(
        split_two(state_c.T), entered_parts
    )
    carried[...] = new_carry

    grad_step = head_sums(own_x * grad_stepped)
    last_row = lax.broadcasted_iota(jnp.int32, (CHUNK, N), 0) == CHUNK - 1
    grad_total = head_sums(grad_m * scanned) - step * grad_step
    grad_total = grad_total + jnp.where(last_row, end_dot[0:1, :], 0.0)
    grad_decay = ones_product(facts["upper"], grad_total)
    end_dot[...] = head_sums(
        jnp.broadcast_to(jnp.sum(new_carry * state_in, 0, keepdims=True), (8, OWN))
    )
    grad_pre_dt = (grad_step + grad_decay * par[7:8, :N]) * jax.nn.sigmoid(facts["shifted"])
    grad_pre_dt = jnp.where(lane < OWN_H, grad_pre_dt, 0.0)
    grad_dt[...] = grad_pre_dt.astype(BF16)
    head_acc[0:1] += jnp.sum(grad_pre_dt, 0, keepdims=True)
    head_acc[1:2] += jnp.sum(grad_decay * facts["decay"], 0, keepdims=True)

    sig_x, pre_x = sig[:, :OWN], pre[:, :OWN]
    grad_pre = (step_wide * grad_stepped + skip * grad_m) * (sig_x * (1.0 + pre_x * (1.0 - sig_x)))
    extended[0:CHUNK, :] = grad_pre
    conv = conv_in[...].astype(BF16).astype(F32)
    sums[5:6] += jnp.sum(grad_pre, 0, keepdims=True)
    sums[4:5] += jnp.sum(conv * grad_pre, 0, keepdims=True)
    grad_conv = par[3:4, :OWN] * grad_pre
    for ahead in range(1, CONV):
        same = (facts["segment"](facts["column"] + ahead) == facts["here_column"]).astype(F32)
        later = extended[ahead : ahead + CHUNK, :] * same
        sums[4 - ahead : 5 - ahead] += jnp.sum(conv * later, 0, keepdims=True)
        grad_conv = grad_conv + par[3 - ahead : 4 - ahead, :OWN] * later
    extended[CHUNK : CHUNK + 8, :] = extended[0:8, :]
    grad_x[...] = grad_conv.astype(BF16)


def run_backward(ends, proj, pre, mixed, grad_mixed, states, par):
    last = CHUNKS - 1
    chunked = lambda width, column=0: pl.BlockSpec((CHUNK, width), lambda i: (last - i, column))
    fixed = lambda shape: pl.BlockSpec(shape, lambda i: (0, 0))
    return pl.pallas_call(
        backward_kernel,
        grid=(CHUNKS,),
        in_specs=[
            pl.BlockSpec(memory_space=pltpu.SMEM),
            chunked(OWN, 1),
            chunked(N, 8),
            chunked(640),
            chunked(OWN),
            chunked(OWN),
            pl.BlockSpec((N, OWN), lambda i: (last - i, 0)),
            fixed((16, 640)),
        ],
        out_specs=[
            chunked(OWN),
            chunked(N),
            pl.BlockSpec((2 * N, CHUNK), lambda i: (0, last - i)),
            fixed((8, OWN)),
            fixed((8, N)),
        ],
        out_shape=[
            jax.ShapeDtypeStruct((PACK, OWN), BF16),
            jax.ShapeDtypeStruct((PACK, N), BF16),
            jax.ShapeDtypeStruct((2 * N, PACK), F32),
            jax.ShapeDtypeStruct((8, OWN), F32),
            jax.ShapeDtypeStruct((8, N), F32),
        ],
        scratch_shapes=[
            pltpu.VMEM((N, OWN), F32),
            pltpu.VMEM((CHUNK + 8, OWN), F32),
            pltpu.VMEM((8, N), F32),
        ],
        compiler_params=pltpu.CompilerParams(
            dimension_semantics=("arbitrary",), vmem_limit_bytes=VMEM_LIMIT
        ),
        cost_estimate=COST,
        name="scan_backward",
    )(ends, proj, proj, pre, mixed, grad_mixed, states, par)


PARTS = (1, 1, 1, 1, 1, 2, 1, 1)


def piece_copies(pieces, parts, blocks, sems):
    copies = []
    taken = 0
    for slot, count in enumerate(parts):
        rows = ROWS // count
        copies.append(
            [
                pltpu.make_async_copy(
                    pieces[taken + k], blocks.at[slot, pl.ds(k * rows, rows)], sems.at[taken + k]
                )
                for k in range(count)
            ]
        )
        taken += count
    return copies


def fetch_block(pieces, parts, blocks, sems):
    copies = piece_copies(pieces, parts, blocks, sems)
    step = pl.program_id(0)

    @pl.when(step == 0)
    def _():
        for group in copies:
            for copy in group:
                copy.start()

    for slot, group in enumerate(copies):

        @pl.when(step == slot)
        def _(group=group):
            for copy in group:
                copy.wait()

    return blocks[step]


def project_kernel(parts, table, *refs):
    pieces = refs[: sum(parts)]
    gain, shards, normed_out, proj, dt_out, blocks, weight, sems = refs[sum(parts) :]
    block = fetch_block(pieces, parts, blocks, sems)

    @pl.when(pl.program_id(0) == 0)
    def _():
        for f in range(N_FSDP):
            weight[f * SHARD_IN : (f + 1) * SHARD_IN, :] = shards[(f // 2) % 4, f % 2, f // 8, :SHARD_IN]
        dt_out[...] = weight[:, 1024:]

    values = block.astype(F32)
    scale = lax.rsqrt(jnp.mean(values * values, axis=1, keepdims=True) + NORM_EPS)
    normed = (values * scale * gain[...]).astype(BF16)
    normed_out[...] = normed
    proj[...] = matmul(normed, weight[...])


def run_project(table, pieces, gain, shards):
    fixed = lambda shape: pl.BlockSpec(shape, lambda i, table: (0,) * len(shape))
    placed = lambda width: pl.BlockSpec((ROWS, width), lambda i, table: (table[i], 0))
    return pl.pallas_call(
        partial(project_kernel, PARTS),
        grid_spec=pltpu.PrefetchScalarGridSpec(
            num_scalar_prefetch=1,
            grid=(N_REP,),
            in_specs=[pl.BlockSpec(memory_space=pl.ANY)] * len(pieces) + [fixed((1, D)), fixed(shards.shape)],
            out_specs=[placed(D), placed(3 * WIDE), fixed((D, N))],
            scratch_shapes=[
                pltpu.VMEM((N_REP, ROWS, D), BF16),
                pltpu.VMEM((D, 3 * WIDE), BF16),
                pltpu.SemaphoreType.DMA((len(pieces),)),
            ],
        ),
        out_shape=[
            jax.ShapeDtypeStruct((PACK, D), BF16),
            jax.ShapeDtypeStruct((PACK, 3 * WIDE), F32),
            jax.ShapeDtypeStruct((D, N), BF16),
        ],
        compiler_params=pltpu.CompilerParams(
            dimension_semantics=("arbitrary",), vmem_limit_bytes=VMEM_LIMIT
        ),
        cost_estimate=COST,
        name="project",
    )(table, *pieces, gain, shards)


def row_sums(value):
    folded = value[:, :N] + value[:, N : 2 * N] + value[:, 2 * N :]
    return jnp.sum(folded.T, 0, keepdims=True)


def out_grad_kernel(table, *refs):
    pieces = refs[: sum(PARTS)]
    w_out, mixed, gate_in, gain, branch_out, grad_out, sums, blocks, turned, sems = refs[sum(PARTS) :]
    branch = fetch_block(pieces, PARTS, blocks, sems)

    @pl.when(pl.program_id(0) == 0)
    def _():
        turned[...] = w_out[...].reshape(OWN, D).T

    branch_out[...] = branch
    total = matmul(branch, turned[...])
    grad_out[...] = total
    gate = gate_in[...]
    gated = mixed[...] * (gate * jax.nn.sigmoid(gate))
    row = lax.broadcasted_iota(jnp.int32, (8, ROWS), 0)
    sums[...] = jnp.where(
        row == 0, row_sums(gated * gated), jnp.where(row == 1, row_sums(total * gain[...] * gated), 0.0)
    )


def run_out_grad(table, pieces, w_out, mixed, proj, gain):
    fixed = lambda shape: pl.BlockSpec(shape, lambda i, table: (0, 0))
    placed = lambda width: pl.BlockSpec((ROWS, width), lambda i, table: (table[i], 0))
    own = pl.BlockSpec(
        (1, 2, 1, SHARD_OUT, D), lambda i, table: (table[N_REP] % 4, 0, table[N_REP] // 4, 0, 0)
    )
    return pl.pallas_call(
        out_grad_kernel,
        grid_spec=pltpu.PrefetchScalarGridSpec(
            num_scalar_prefetch=1,
            grid=(N_REP,),
            in_specs=[pl.BlockSpec(memory_space=pl.ANY)] * len(pieces)
            + [own, placed(OWN), placed(OWN), fixed((1, OWN))],
            out_specs=[placed(D), placed(OWN), pl.BlockSpec((8, ROWS), lambda i, table: (0, table[i]))],
            scratch_shapes=[
                pltpu.VMEM((N_REP, ROWS, D), BF16),
                pltpu.VMEM((D, WIDE), BF16),
                pltpu.SemaphoreType.DMA((len(pieces),)),
            ],
        ),
        out_shape=[
            jax.ShapeDtypeStruct((PACK, D), BF16),
            jax.ShapeDtypeStruct((PACK, OWN), F32),
            jax.ShapeDtypeStruct((8, PACK), F32),
        ],
        compiler_params=pltpu.CompilerParams(
            dimension_semantics=("arbitrary",), vmem_limit_bytes=VMEM_LIMIT
        ),
        cost_estimate=COST,
        name="out_grad",
    )(table, *pieces, w_out, mixed, proj, gain)


def gate_kernel(grad_out, mixed_in, gate_in, sums, gain, low_out, grad_mixed, grad_gain):
    rows = grad_out.shape[0]
    mixed, gate, grad_o = mixed_in[...], gate_in[...], grad_out[...]
    stats = jnp.concatenate([sums[...], jnp.zeros((N - 8, rows), F32)], 0).T
    out_scale = lax.rsqrt(stats[:, 0:1] * (1.0 / DI) + NORM_EPS)
    pull = out_scale * out_scale * out_scale * (stats[:, 1:2] * (1.0 / DI))
    gate_sig = jax.nn.sigmoid(gate)
    silu = gate * gate_sig
    gated = mixed * silu
    unit = gated * out_scale
    grad_gated = out_scale * (grad_o * gain[...]) - gated * pull
    grad_mixed[...] = grad_gated * silu
    low_out[:, :OWN] = (unit * gain[...]).astype(BF16)
    low_out[:, OWN:] = (grad_gated * mixed * (gate_sig * (1.0 + gate * (1.0 - gate_sig)))).astype(BF16)
    gain_part = jnp.sum(grad_o * unit, 0, keepdims=True)

    @pl.when(pl.program_id(0) == 0)
    def _():
        grad_gain[...] = jnp.broadcast_to(gain_part, grad_gain.shape)

    @pl.when(pl.program_id(0) > 0)
    def _():
        grad_gain[...] += gain_part


def run_gate(grad_out, mixed, proj, sums, gain):
    rows = lambda width: pl.BlockSpec((ROWS, width), lambda i: (i, 0))
    fixed = lambda shape: pl.BlockSpec(shape, lambda i: (0, 0))
    return pl.pallas_call(
        gate_kernel,
        grid=(PACK // ROWS,),
        in_specs=[
            rows(OWN),
            rows(OWN),
            rows(OWN),
            pl.BlockSpec((8, ROWS), lambda i: (0, i)),
            fixed((1, OWN)),
        ],
        out_specs=[rows(2 * OWN), rows(OWN), fixed((8, OWN))],
        out_shape=[
            jax.ShapeDtypeStruct((PACK, 2 * OWN), BF16),
            jax.ShapeDtypeStruct((PACK, OWN), F32),
            jax.ShapeDtypeStruct((8, OWN), F32),
        ],
        compiler_params=pltpu.CompilerParams(
            dimension_semantics=("arbitrary",), vmem_limit_bytes=VMEM_LIMIT
        ),
        cost_estimate=COST,
        name="gate_backward",
    )(grad_out, mixed, proj, sums, gain)


def early_grad_kernel(low, grad_x, grad_branch, normed, out):
    step = pl.program_id(0)

    @pl.when(step == 0)
    def _():
        out[...] = jnp.zeros_like(out)

    for k in range(4):
        part = product(low[:, :OWN], grad_branch[:, k * WIDE : (k + 1) * WIDE], 0, 0)
        for m in range(4):
            out[eight_order(4 * k + m), :SHARD_IN] += part[m * SHARD_IN : (m + 1) * SHARD_IN]
    part = product(normed[...], jnp.concatenate([low[:, OWN:], grad_x[...]], 1), 0, 0)
    for f in range(N_FSDP):
        rows = part[f * SHARD_IN : (f + 1) * SHARD_IN]
        out[eight_order(f), SHARD_IN : 2 * SHARD_IN] += rows[:, :OWN]
        out[eight_order(f), 2 * SHARD_IN :] += rows[:, OWN:]


def run_early_grad(low, grad_x, grad_branch, normed):
    count = 2 * ROWS
    rows = lambda width: pl.BlockSpec((count, width), lambda i: (i, 0))
    shape = (N_FSDP, 3 * SHARD_IN, WIDE)
    return pl.pallas_call(
        early_grad_kernel,
        grid=(PACK // count,),
        in_specs=[rows(2 * OWN), rows(OWN), rows(D), rows(D)],
        out_specs=pl.BlockSpec(shape, lambda i: (0, 0, 0)),
        out_shape=jax.ShapeDtypeStruct(shape, F32),
        compiler_params=pltpu.CompilerParams(
            dimension_semantics=("arbitrary",), vmem_limit_bytes=VMEM_LIMIT
        ),
        cost_estimate=COST,
        name="early_grad",
    )(low, grad_x, grad_branch, normed)


def block_out_kernel(rows, weight, tokens, live, out):
    step = pl.program_id(0)
    part = matmul(jnp.concatenate([rows[0], rows[1]], 1), weight[...].reshape(2 * OWN, D))

    @pl.when(step == 0)
    def _():
        out[...] = part

    @pl.when(step > 0)
    def _():
        out[...] += part

    @pl.when(step == N_REP // 2 - 1)
    def _():
        out[...] = tokens[...].astype(F32) + live[...] * out[...]


def run_block_out(rows, weight, tokens, live):
    fixed = lambda shape: pl.BlockSpec(shape, lambda i: (0, 0))
    return pl.pallas_call(
        block_out_kernel,
        grid=(N_REP // 2,),
        in_specs=[
            pl.BlockSpec((2, ROWS, OWN), lambda i: (i, 0, 0)),
            pl.BlockSpec((2, 2, 1, SHARD_OUT, D), lambda i: (i % 2, 0, i // 2, 0, 0)),
            fixed((ROWS, D)),
            fixed((ROWS, 1)),
        ],
        out_specs=fixed((ROWS, D)),
        out_shape=jax.ShapeDtypeStruct((ROWS, D), F32),
        compiler_params=pltpu.CompilerParams(
            dimension_semantics=("arbitrary",), vmem_limit_bytes=VMEM_LIMIT
        ),
        cost_estimate=FILL,
        name="block_out",
    )(rows, weight, tokens, live)


def turned_part(weight, rows):
    return product(weight[...].reshape(D, weight.shape[-1]), rows, 1, 1)


def columns_of(full_in, width, index):
    return pl.BlockSpec(full_in.shape[:-1] + (width,), lambda i: (0, 0, 0, 0, index(i)))


def z_grad_kernel(rows, weight, out):
    part = turned_part(weight, jnp.concatenate([rows[0], rows[1]], 1))

    @pl.when(pl.program_id(0) == 0)
    def _():
        out[...] = part

    @pl.when(pl.program_id(0) > 0)
    def _():
        out[...] += part


def run_z_grad(rows, full_in):
    return pl.pallas_call(
        z_grad_kernel,
        grid=(N_REP // 2,),
        in_specs=[
            pl.BlockSpec((2, ROWS, OWN), lambda i: (i, 0, 1)),
            columns_of(full_in, 2 * OWN, lambda i: i),
        ],
        out_specs=pl.BlockSpec((D, ROWS), lambda i: (0, 0)),
        out_shape=jax.ShapeDtypeStruct((D, ROWS), F32),
        compiler_params=pltpu.CompilerParams(
            dimension_semantics=("arbitrary",), vmem_limit_bytes=VMEM_LIMIT
        ),
        cost_estimate=FILL,
        name="z_grad",
    )(rows, full_in)


def input_grad_kernel(
    own_half, grad_z, x_rows, rest_rows, w_x, w_bc, low_dt, tokens, cotangent, gain, out, gain_out, total, ordered
):
    step = pl.program_id(0)
    part = turned_part(w_x, jnp.concatenate([x_rows[0], x_rows[1]], 1))

    @pl.when(step == 0)
    def _():
        total[...] = grad_z[...] + part

    @pl.when(step > 0)
    def _():
        total[...] += part

    @pl.when(step == N_REP // 2 - 1)
    def _():
        lane = lax.broadcasted_iota(jnp.int32, (ROWS, N), 1)
        groups = []
        for k in range(2):
            group = jnp.zeros((ROWS, N), F32)
            for m in range(4):
                value = rest_rows[4 * k + m].astype(F32)
                value = value if m == 0 else pltpu.roll(value, m * OWN_BC, 1)
                group = jnp.where((lane >= m * OWN_BC) & (lane < (m + 1) * OWN_BC), value, group)
            groups.append(group.astype(BF16))
        steps = jnp.zeros((ROWS, N), F32)
        for m in range(N_REP):
            start = 8 + m * OWN_H
            value = pltpu.roll(rest_rows[m].astype(F32), (start - OWN_BC) % N, 1)
            steps = jnp.where((lane >= start) & (lane < start + OWN_H), value, steps)
        total[...] += turned_part(w_bc, jnp.concatenate(groups, 1))
        for f in range(N_FSDP):
            place = eight_order(f) - f // 8 + (f // 8 + own_half[0]) % 2
            start = pl.multiple_of(place * SHARD_IN, SHARD_IN)
            ordered[f * SHARD_IN : (f + 1) * SHARD_IN, :] = total[pl.ds(start, SHARD_IN), :]
        grad_h = (ordered[...] + product(low_dt[...], steps.astype(BF16), 1, 1)).T
        values = tokens[...].astype(F32)
        scale = lax.rsqrt(jnp.mean(values * values, axis=1, keepdims=True) + NORM_EPS)
        unit = values * scale
        gain_sum = jnp.sum(grad_h * unit, 0, keepdims=True)
        gain_out[...] = jnp.zeros_like(gain_out)
        for k in range(D // N):
            gain_out[k : k + 1, :] = gain_sum[:, k * N : (k + 1) * N]
        grad_unit = grad_h * gain[...]
        inner = jnp.mean(grad_unit * unit, axis=1, keepdims=True)
        out[...] = cotangent[...].astype(F32) + scale * (grad_unit - unit * inner)


def run_input_grad(own_half, grad_z, tail_rows, full_in, low_dt, tokens, cotangent, gain):
    fixed = lambda shape: pl.BlockSpec(shape, lambda i: (0,) * len(shape))
    return pl.pallas_call(
        input_grad_kernel,
        grid=(N_REP // 2,),
        in_specs=[
            pl.BlockSpec(memory_space=pltpu.SMEM),
            fixed((D, ROWS)),
            pl.BlockSpec((2, ROWS, OWN), lambda i: (i, 0, 0)),
            pl.BlockSpec((N_REP, ROWS, N), lambda i: (0, 0, OWN // N)),
            columns_of(full_in, 2 * OWN, lambda i: N_REP // 2 + i),
            columns_of(full_in, 2 * N, lambda i: DI // N),
            fixed((D, N)),
            fixed((ROWS, D)),
            fixed((ROWS, D)),
            fixed((1, D)),
        ],
        out_specs=[fixed((ROWS, D)), fixed((16, N))],
        out_shape=[jax.ShapeDtypeStruct((ROWS, D), F32), jax.ShapeDtypeStruct((16, N), F32)],
        scratch_shapes=[pltpu.VMEM((D, ROWS), F32), pltpu.VMEM((D, ROWS), F32)],
        compiler_params=pltpu.CompilerParams(
            dimension_semantics=("arbitrary",), vmem_limit_bytes=VMEM_LIMIT
        ),
        cost_estimate=COST,
        name="input_grad",
    )(own_half, grad_z, tail_rows, tail_rows, full_in, full_in, low_dt, tokens, cotangent, gain)


def rest_kernel(
    ends, parts, pre_b, pre_c, conv_in, par, grad_x, grad_dt, sums, head_acc, grad_gain, first, tail_out, small_out
):
    own = lax.broadcasted_iota(jnp.int32, (OWN_BC, 2 * N), 0) + first[0]
    chosen = (lax.broadcasted_iota(jnp.int32, (OWN_BC, 2 * N), 1) == own).astype(F32).astype(BF16)

    def pick(value):
        return product(jnp.concatenate([chosen] * 3, 1), jnp.concatenate(split_three(value), 1), 1, 1)

    grad = parts[0]
    for k in range(1, N_REP):
        grad = grad + parts[k]
    own_pre = pick(jnp.concatenate([pre_b[...], pre_c[...]], 1))
    own_conv = product(chosen, conv_in[...].astype(BF16), 1, 1)
    taps = pick(par[:, OWN:])
    sig = jax.nn.sigmoid(own_pre)
    grad_pre = grad * (sig * (1.0 + own_pre * (1.0 - sig)))
    position = lax.broadcasted_iota(jnp.int32, (1, PACK), 1)

    def segment(places):
        counted = jnp.zeros_like(places)
        for k in range(3):
            counted = counted + (places >= ends[k]).astype(jnp.int32)
        return counted

    grad_conv = taps[:, CONV - 1 : CONV] * grad_pre
    column = lax.broadcasted_iota(jnp.int32, (OWN_BC, N), 1)
    found = jnp.where(column == CONV, jnp.sum(grad_pre, 1, keepdims=True), 0.0)
    found = jnp.where(column == CONV - 1, jnp.sum(own_conv * grad_pre, 1, keepdims=True), found)
    for later_by in range(1, CONV):
        same = (segment(position + later_by) == segment(position)) & (position < PACK - later_by)
        later = jnp.where(same, pltpu.roll(grad_pre, PACK - later_by, 1), 0.0)
        tap = CONV - 1 - later_by
        found = jnp.where(column == tap, jnp.sum(own_conv * later, 1, keepdims=True), found)
        grad_conv = grad_conv + taps[:, tap : tap + 1] * later
    lane = lax.broadcasted_iota(jnp.int32, (N, N), 1)
    filler = jnp.zeros((N - OWN_BC, N), F32)
    for k in range(PACK // N):
        rows = slice(k * N, (k + 1) * N)
        columns = jnp.concatenate([grad_conv[:, rows], filler], 0).T
        steps = pltpu.roll(grad_dt[rows, :].astype(F32), OWN_BC, 1)
        tail_out[rows, :OWN] = grad_x[rows, :]
        tail_out[rows, OWN:] = jnp.where(
            lane < OWN_BC, columns, jnp.where(lane < OWN_BC + OWN_H, steps, 0.0)
        ).astype(BF16)
    row = lax.broadcasted_iota(jnp.int32, (8, OWN), 0)
    skip = head_sums(sums[...])
    by_head = jnp.concatenate([skip, jnp.zeros((8, OWN - N), F32)], 1)
    logs = jnp.concatenate([head_acc[...], jnp.zeros((8, OWN - N), F32)], 1)
    wide = jnp.where(row == 0, grad_gain[0:1, :], jnp.where(row < 6, sums[...], 0.0))
    wide = jnp.where(row == 6, logs[1:2, :], jnp.where(row == 7, by_head[6:7, :], wide))
    turned = jnp.concatenate([found, filler], 0).T
    first_row = lax.broadcasted_iota(jnp.int32, (8, N), 0) == 0
    for k in range(3):
        small_out[8 * k : 8 * k + 8, :] = wide[:, k * N : (k + 1) * N]
    small_out[24:, :] = jnp.where(first_row, head_acc[0:1, :], pltpu.roll(turned[:8], 1, 0))


def run_rest(ends, parts, pre, proj, par, grad_x, grad_dt, sums, head_acc, grad_gain, first):
    fixed = lambda shape: pl.BlockSpec(shape, lambda i: (0,) * len(shape))
    return pl.pallas_call(
        rest_kernel,
        grid=(1,),
        in_specs=[
            pl.BlockSpec(memory_space=pltpu.SMEM),
            fixed((N_REP, OWN_BC, PACK)),
            pl.BlockSpec((PACK, N), lambda i: (0, 3)),
            pl.BlockSpec((PACK, N), lambda i: (0, 4)),
            pl.BlockSpec((PACK, 2 * N), lambda i: (0, 3)),
            fixed((16, 640)),
            fixed((PACK, OWN)),
            fixed((PACK, N)),
            fixed((8, OWN)),
            fixed((8, N)),
            fixed((8, OWN)),
            pl.BlockSpec(memory_space=pltpu.SMEM),
        ],
        out_specs=[fixed((PACK, TAIL)), fixed((32, N))],
        out_shape=[jax.ShapeDtypeStruct((PACK, TAIL), BF16), jax.ShapeDtypeStruct((32, N), F32)],
        compiler_params=pltpu.CompilerParams(
            dimension_semantics=("arbitrary",), vmem_limit_bytes=VMEM_LIMIT
        ),
        cost_estimate=COST,
        name="rest_backward",
    )(ends, parts, pre, pre, proj, par, grad_x, grad_dt, sums, head_acc, grad_gain, first)


def tail_grad_kernel(normed, tail, small, out):
    step = pl.program_id(0)
    part = product(normed[...], tail[...], 0, 0)
    for f in range(N_FSDP):
        rows = part[f * SHARD_IN : (f + 1) * SHARD_IN]

        @pl.when(step == 0)
        def _(f=f, rows=rows):
            out[eight_order(f), :SHARD_IN] = rows
            out[eight_order(f), SHARD_IN:] = small[...]

        @pl.when(step > 0)
        def _(f=f, rows=rows):
            out[eight_order(f), :SHARD_IN] += rows


def run_tail_grad(normed, tail, small):
    count = 2 * ROWS
    shape = (N_FSDP, SHARD_IN + 32, N)
    return pl.pallas_call(
        tail_grad_kernel,
        grid=(PACK // count,),
        in_specs=[
            pl.BlockSpec((count, D), lambda i: (i, 0)),
            pl.BlockSpec((count, N), lambda i: (i, OWN // N)),
            pl.BlockSpec((32, N), lambda i: (0, 0)),
        ],
        out_specs=pl.BlockSpec(shape, lambda i: (0, 0, 0)),
        out_shape=jax.ShapeDtypeStruct(shape, F32),
        compiler_params=pltpu.CompilerParams(
            dimension_semantics=("arbitrary",), vmem_limit_bytes=VMEM_LIMIT
        ),
        cost_estimate=COST,
        name="tail_grad",
    )(normed, tail, small)


def adam_step(grad, weight, first, second, grad_out, first_out, second_out, weight_out):
    new_weight, new_first, new_second = adam_update(
        weight[...], grad, first[...], second[...], RATE_MATRIX, WEIGHT_DECAY
    )
    grad_out[...] = grad
    first_out[...] = new_first
    second_out[...] = new_second
    weight_out[...] = new_weight


def adam_early_kernel(rows, pair, *refs):
    arrays, grad = refs[:3] + refs[-5:-1], refs[-1]
    grad[:, :WIDE] = pair[0, rows, :]
    grad[:, WIDE:] = pair[1, rows, :]
    adam_step(grad[...], *arrays)


def run_adam_early(place_of, rows, parts, weight, first, second, before=()):
    part = pl.BlockSpec((SHARD_IN, 2 * WIDE), place_of)
    shape = jax.ShapeDtypeStruct(weight.shape, F32)
    return pl.pallas_call(
        partial(adam_early_kernel, rows),
        grid=(N_REP // 2,),
        in_specs=[pl.BlockSpec((2,) + parts.shape[1:], lambda i: (i, 0, 0))]
        + [part] * 3
        + [pl.BlockSpec(memory_space=pl.ANY)] * len(before),
        out_specs=[part] * 4,
        out_shape=[shape] * 4,
        input_output_aliases={4 + k: k for k in range(len(before))},
        scratch_shapes=[pltpu.VMEM((SHARD_IN, 2 * WIDE), F32)],
        compiler_params=pltpu.CompilerParams(
            dimension_semantics=("arbitrary",), vmem_limit_bytes=VMEM_LIMIT
        ),
        cost_estimate=FILL,
        name="adam",
    )(parts, weight, first, second, *before)


def adam_rest_kernel(parts, weight, first, second, *refs):
    lane = lax.broadcasted_iota(jnp.int32, (SHARD_IN, N), 1)
    groups = []
    for k in range(2):
        group = jnp.zeros((SHARD_IN, N), F32)
        for m in range(4):
            value = parts[4 * k + m, :SHARD_IN]
            value = value if m == 0 else pltpu.roll(value, m * OWN_BC, 1)
            group = jnp.where((lane >= m * OWN_BC) & (lane < (m + 1) * OWN_BC), value, group)
        groups.append(group)
    adam_step(jnp.concatenate(groups, 1), weight, first, second, *refs[-4:])


def run_adam_rest(parts, weight, first, second, before):
    column = pl.BlockSpec((SHARD_IN, 2 * N), lambda i: (0, DI // N))
    shape = jax.ShapeDtypeStruct(weight.shape, F32)
    return pl.pallas_call(
        adam_rest_kernel,
        grid=(1,),
        in_specs=[pl.BlockSpec(parts.shape, lambda i: (0, 0, 0))]
        + [column] * 3
        + [pl.BlockSpec(memory_space=pl.ANY)] * 4,
        out_specs=[column] * 4,
        out_shape=[shape] * 4,
        input_output_aliases={4 + k: k for k in range(4)},
        compiler_params=pltpu.CompilerParams(
            dimension_semantics=("arbitrary",), vmem_limit_bytes=VMEM_LIMIT
        ),
        cost_estimate=COST,
        name="adam_rest",
    )(parts, weight, first, second, *before)


def body(
    tokens,
    cotangent,
    lengths,
    w_in,
    w_dt,
    w_out,
    small,
    first_in,
    first_dt,
    first_out,
    first_small,
    second_in,
    second_dt,
    second_out,
    second_small,
):
    place = Place()
    r = place.r
    zero = jnp.int32(0)
    pack_lengths = lax.dynamic_slice_in_dim(lengths, place.f, 1, 0)[0]
    seg_ends = jnp.cumsum(pack_lengths)
    own_positions = r * ROWS + jnp.arange(ROWS, dtype=jnp.int32)
    own_live = (segment_at(own_positions, seg_ends) < 3).astype(F32)[:, None]
    slots = jnp.arange(N_REP, dtype=jnp.int32)
    ahead = ((place.x + slots // 2) % 4) * 2 + (place.yl + slots) % 2
    half = ROWS // 2

    in_low = w_in.astype(BF16)
    dt_low = w_dt.astype(BF16)
    out_low = w_out.astype(BF16)

    small_rows = jnp.pad(small.astype(BF16), (0, 16 * 3 * WIDE - SHARD_SMALL)).reshape(16, 3 * WIDE)

    def own_columns(rep):
        columns = jnp.concatenate(
            [
                lax.dynamic_slice_in_dim(in_low, rep * OWN, OWN, 1),
                lax.dynamic_slice_in_dim(in_low, DI + rep * OWN, OWN, 1),
                in_low[:, 2 * DI :],
                lax.dynamic_slice_in_dim(dt_low, rep * OWN_H, OWN_H, 1),
                jnp.zeros((SHARD_IN, 2), BF16),
                dt_low,
                jnp.zeros((SHARD_IN, N - 8 - H), BF16),
            ],
            1,
        )
        return jnp.concatenate([columns, small_rows], 0)

    other_columns = move(
        own_columns(2 * place.x + 1 - place.yl), lambda yh, z, c, x, yl: (yh + 1, z, c, x, yl + 1)
    )
    from_left = move(tokens, along_x(1))
    from_right = move(tokens, along_x(-1))
    partner = move(tokens, swap_y)

    out_low, other_columns = lax.optimization_barrier((out_low, other_columns))
    out_other = move(out_low, lambda yh, z, c, x, yl: (yh + 1, z, c, x, yl + 1))
    branch = (cotangent.astype(F32) * own_live).astype(BF16)
    from_left, from_right, partner, other_columns, branch = lax.optimization_barrier(
        (from_left, from_right, partner, other_columns, branch)
    )
    own_shards = gather_eight(both(own_columns(r), other_columns, place.yh))
    far = move(from_left, along_x(1))
    partner_left = move(from_left, swap_y)
    partner_right = move(partner, along_x(-1))

    b_partner = move(branch, swap_y)
    far, partner_left, partner_right, out_other, branch, in_low = lax.optimization_barrier(
        (far, partner_left, partner_right, out_other, branch, in_low)
    )
    in_other = move(in_low, lambda yh, z, c, x, yl: (yh + 1, z, c, x, yl + 1))
    out_pair = both(out_low, out_other, place.yh)
    partner_far_top = move(partner_left[:half], along_x(1))
    partner_far_low = move(partner_right[half:], along_x(-1))

    vector = own_shards[:, :, :, SHARD_IN : SHARD_IN + 2].transpose(2, 0, 1, 3, 4)
    vector = vector.reshape(N_FSDP, 6 * WIDE)[:, :SHARD_SMALL].reshape(-1).astype(F32)
    offset = 0
    gain_in = vector[None, :D]
    offset = D
    gain_row = lax.dynamic_slice_in_dim(vector, offset + r * OWN, OWN, 0)[None, :]
    offset += DI
    taps = vector[offset : offset + (CONV + 1) * CHANNELS].reshape(CONV + 1, CHANNELS)
    offset += (CONV + 1) * CHANNELS
    per_head = vector[offset:].reshape(3, H)
    dt_bias, a_log, d_skip = lax.dynamic_slice_in_dim(per_head, r * OWN_H, OWN_H, 1)
    taps_bc = taps[:, DI:]
    conv_par = jnp.concatenate([lax.dynamic_slice_in_dim(taps, r * OWN, OWN, 1), taps_bc], 1)
    head_par = jnp.stack(
        [
            jnp.pad(jnp.broadcast_to(d_skip[:, None], (OWN_H, P_SIZE)).reshape(-1), (0, 2 * N)),
            jnp.pad(dt_bias, (0, 640 - OWN_H)),
            jnp.pad(-jnp.exp(a_log), (0, 640 - OWN_H)),
        ],
        0,
    )
    par = jnp.concatenate([conv_par, head_par, jnp.zeros((8, 640), F32)], 0)

    partner_far_top, partner_far_low, own_shards, b_partner = lax.optimization_barrier(
        (partner_far_top, partner_far_low, own_shards, b_partner)
    )
    full_out = gather_eight(tie(out_pair, own_shards))
    b_left = move(branch, along_x(1))
    b_right = move(branch, along_x(-1))
    token_pieces = [
        tokens, partner, from_right, partner_right, far,
        partner_far_top, partner_far_low, from_left, partner_left,
    ]
    normed, proj, low_dt = run_project(ahead, token_pieces, gain_in, own_shards)
    b_left, b_right, b_partner, proj = lax.optimization_barrier((b_left, b_right, b_partner, proj))
    b_far = move(b_left, along_x(1))
    b_partner_left = move(b_left, swap_y)
    b_partner_right = move(b_partner, along_x(-1))
    before = run_forward(0, seg_ends, proj, par)
    b_far, b_partner_left, b_partner_right, before = lax.optimization_barrier(
        (b_far, b_partner_left, b_partner_right, before)
    )
    b_partner_far_top = move(b_partner_left[:half], along_x(1))
    b_partner_far_low = move(b_partner_right[half:], along_x(-1))
    pre, mixed, states, _ = run_forward(1, seg_ends, proj, par, before)
    mixed, in_low, in_other, b_partner_far_top, b_partner_far_low = lax.optimization_barrier(
        (mixed, in_low, in_other, b_partner_far_top, b_partner_far_low)
    )
    full_in = gather_eight(jnp.stack([in_low, in_other], 0))
    branch_pieces = [
        branch, b_partner, b_right, b_partner_right, b_far,
        b_partner_far_top, b_partner_far_low, b_left, b_partner_left,
    ]
    rep_table = jnp.concatenate([ahead, r[None]])
    grad_branch, grad_normed_out, sums = run_out_grad(rep_table, branch_pieces, full_out, mixed, proj, gain_row)
    sums = share_rep(sums[:2].reshape(32, 128)).sum(0).reshape(2, PACK)
    sums = jnp.concatenate([sums, jnp.zeros((6, PACK), F32)], 0)

    low, grad_mixed, grad_gain = run_gate(grad_normed_out, mixed, proj, sums, gain_row)

    low_rows = exchange(low.reshape(N_REP, ROWS, 2 * OWN), "rep")
    grad_x, grad_dtraw, grad_bc, grad_sums, grad_heads = run_backward(
        seg_ends, proj, pre, mixed, grad_mixed, states, par
    )
    low, grad_x = lax.optimization_barrier((low, grad_x))
    early_grad = run_early_grad(low, grad_x, grad_branch, normed)
    low_rows, early_grad, grad_bc, grad_x = lax.optimization_barrier((low_rows, early_grad, grad_bc, grad_x))

    grad_bc = exchange(grad_bc, "rep").reshape(N_REP, OWN_BC, PACK)
    early = scatter_eight(early_grad)
    grad_rows = run_z_grad(low_rows, full_in)
    grad_bc, grad_rows = lax.optimization_barrier((grad_bc, grad_rows))

    tail, small_own = run_rest(
        seg_ends, grad_bc, pre, proj, par, grad_x, grad_dtraw, grad_sums, grad_heads, grad_gain, (r * OWN_BC)[None]
    )
    grad_tail = run_tail_grad(normed, tail, small_own)
    tail, grad_tail = lax.optimization_barrier((tail, grad_tail))
    tail_rows = exchange(tail.reshape(N_REP, ROWS, TAIL), "rep")
    early, grad_tail = lax.optimization_barrier((early, grad_tail))
    tail_part = scatter_eight(grad_tail)
    mine, other = at(early, place.yh), at(early, 1 - place.yh)
    out_mine = move(
        mine[:SHARD_IN], lambda yh, z, c, x, yl: (x // 2, (x % 2) * 2 + yl, z % 2, 2 * c + yh, z // 2)
    )
    out_other = move(
        other[:SHARD_IN], lambda yh, z, c, x, yl: (x // 2, (x % 2) * 2 + yl, z % 2, 2 * c + 1 - yh, z // 2)
    )
    in_other = move(other[SHARD_IN:], swap_y_hi)
    tail_rows, out_mine, out_other, in_other = lax.optimization_barrier((tail_rows, out_mine, out_other, in_other))

    early_parts = share_rep(jnp.concatenate([out_mine + out_other, mine[SHARD_IN:] + in_other], 0))
    input_grad, grad_gain_in = run_input_grad(
        place.yh[None], grad_rows, tail_rows, full_in, low_dt, tokens, cotangent, gain_in
    )

    grad_gain_in = sum_z(grad_gain_in + move(grad_gain_in, swap_core))
    tail_part, grad_gain_in = lax.optimization_barrier((tail_part, grad_gain_in))
    tail_other = move(with_rows(at(tail_part, 1 - place.yh), grad_gain_in), swap_y_hi)
    tail_part = with_rows(at(tail_part, place.yh), grad_gain_in) + tail_other

    tail_part, early_parts, low_rows = lax.optimization_barrier((tail_part, early_parts, low_rows))
    tail_parts = share_rep(tail_part)
    block_out = run_block_out(low_rows, full_out, tokens, own_live)

    grad_out, new_first_out, new_second_out, new_out = run_adam_early(
        lambda i: (i // 2, i % 2), slice(0, SHARD_IN), early_parts, w_out, first_out, second_out
    )
    updated = run_adam_early(
        lambda i: (0, i), slice(SHARD_IN, 2 * SHARD_IN), early_parts, w_in, first_in, second_in
    )
    updated = run_adam_early(
        lambda i: (0, 4 + i), slice(2 * SHARD_IN, 3 * SHARD_IN), early_parts, w_in, first_in, second_in, updated
    )
    grad_in, new_first_in, new_second_in, new_in = run_adam_rest(tail_parts, w_in, first_in, second_in, updated)

    def columns(parts):
        return parts.transpose(1, 0, 2).reshape(parts.shape[1], -1)

    grad_gain_in = tail_parts[:, SHARD_IN + 32 : SHARD_IN + 32 + D // N].sum(0).reshape(-1)
    small_parts = tail_parts[:, SHARD_IN : SHARD_IN + 32].reshape(N_REP, 4, 8, N)
    small_x = small_parts[:, :3].transpose(2, 0, 1, 3).reshape(8, DI)
    small_bc = small_parts[:, 3].transpose(1, 0, 2)

    def channels(row):
        return jnp.concatenate([small_x[row], small_bc[row, :, :OWN_BC].reshape(-1)])

    grad_small_all = jnp.concatenate(
        [grad_gain_in, small_x[0]]
        + [channels(row) for row in range(1, 6)]
        + [
            small_bc[0, :, :OWN_H].reshape(-1),
            small_parts[:, 0, 6, :OWN_H].reshape(-1),
            small_parts[:, 0, 7, :OWN_H].reshape(-1),
        ]
    )
    grad_small = lax.dynamic_slice_in_dim(grad_small_all, place.f * SHARD_SMALL, SHARD_SMALL, 0)
    grad_dt = columns(tail_parts[:, :SHARD_IN, OWN_BC : OWN_BC + OWN_H])
    new_dt, new_first_dt, new_second_dt = adam_update(
        w_dt, grad_dt, first_dt, second_dt, RATE_MATRIX, WEIGHT_DECAY
    )
    new_small, new_first_small, new_second_small = adam_update(
        small, grad_small, first_small, second_small, RATE_SMALL, 0.0
    )
    return (
        block_out,
        input_grad,
        grad_in,
        grad_dt,
        grad_out,
        grad_small,
        new_first_in,
        new_first_dt,
        new_first_out,
        new_first_small,
        new_second_in,
        new_second_dt,
        new_second_out,
        new_second_small,
        new_in,
        new_dt,
        new_out,
        new_small,
    )


def solution(mesh):
    rows = P(("fsdp", "rep"), None)
    matrix = P("fsdp", None)
    vector = P("fsdp")
    group = (matrix, matrix, matrix, vector)
    return jax.shard_map(
        body,
        mesh=mesh,
        in_specs=(rows, rows, P()) + group * 3,
        out_specs=(rows, rows) + group * 4,
        check_vma=False,
    )
```

```python
from functools import partial

import jax
import jax.numpy as jnp
from jax import lax
from jax.experimental import pallas as pl
from jax.experimental.pallas import tpu as pltpu
from jax.sharding import PartitionSpec as P

D = 1536
H = 48
P_SIZE = 64
N = 128
CONV = 4
STEP = 10
DI = 3072
CHANNELS = DI + 2 * N
SMALL = 21392
N_FSDP = 16
N_REP = 8
ROWS = 256
PACK = 2048
OWN = DI // N_REP
OWN_H = H // N_REP
OWN_BC = 2 * N // N_REP
SHARD_IN = D // N_FSDP
SHARD_OUT = DI // N_FSDP
SHARD_SMALL = SMALL // N_FSDP
WIDE = 384
CHUNK = 128
CHUNKS = PACK // CHUNK
HALF = CHUNKS // 2
TAIL = 512
VMEM_LIMIT = 60 * 1024 * 1024

NORM_EPS = 1e-05
BETA_ONE = 0.9
BETA_TWO = 0.999
ADAM_EPS = 1e-08
WEIGHT_DECAY = 0.1
RATE_MATRIX = 0.04
RATE_SMALL = 0.4
PRECISE = lax.Precision.HIGHEST
BF16 = jnp.bfloat16
F32 = jnp.float32
COST = pl.CostEstimate(flops=1_000_000, bytes_accessed=100_000, transcendentals=0)
FILL = pl.CostEstimate(flops=2_400_000_000, bytes_accessed=20_000_000, transcendentals=0)


def move(value, target):
    pairs = []
    for f in range(N_FSDP):
        for r in range(N_REP):
            yh, z, c, x, yl = target(f // 8, (f // 2) % 4, f % 2, r // 2, r % 2)
            pairs.append((f * N_REP + r, ((yh % 2) * 8 + (z % 4) * 2 + c % 2) * N_REP + (x % 4) * 2 + yl % 2))
    return lax.ppermute(value, ("fsdp", "rep"), pairs)


def along_x(steps):
    return lambda yh, z, c, x, yl: (yh, z, c, x + steps, yl)


def along_z(steps):
    return lambda yh, z, c, x, yl: (yh, z + steps, c, x, yl)


def swap_y(yh, z, c, x, yl):
    return (yh, z, c, x, yl + 1)


def swap_y_hi(yh, z, c, x, yl):
    return (yh + 1, z, c, x, yl)


def swap_core(yh, z, c, x, yl):
    return (yh, z, c + 1, x, yl)


class Place:
    def __init__(self):
        f = lax.axis_index("fsdp")
        r = lax.axis_index("rep")
        self.f, self.r = f, r
        self.yh, self.z, self.c = f // 8, (f // 2) % 4, f % 2
        self.x, self.yl = r // 2, r % 2


def at(value, index, axis=0):
    return lax.dynamic_index_in_dim(value, index, axis, keepdims=False)


def tie(values, *others):
    return lax.optimization_barrier((values, others))[0]


def both(mine, other, second):
    first = jnp.where(second == 0, mine, other)
    last = jnp.where(second == 0, other, mine)
    return jnp.stack([first, last], 0)


def put(out, piece, axis, index):
    starts = [jnp.int32(0)] * out.ndim
    starts[axis] = jnp.int32(index)
    return lax.dynamic_update_slice(out, jnp.expand_dims(piece, axis), tuple(starts))


def swap_shards(value, place):
    other = move(value, lambda yh, z, c, x, yl: (yh + 1, z, c, x, yl + 1))
    return both(value, other, place.yh)


def gather_eight(pair):
    groups = [list(range(8)), list(range(8, 16))]
    out = lax.all_gather(pair, "fsdp", axis=0, tiled=True, axis_index_groups=groups)
    return out.reshape((4, 2) + pair.shape)


def exchange(value, axis):
    return lax.all_to_all(value, axis, 0, 0, tiled=True)


def share_rep(value):
    return exchange(jnp.broadcast_to(value[None], (N_REP,) + value.shape), "rep")


def sum_z(value):
    steps = [move(value, along_z(step)) for step in (1, 3, 2)]
    return value + steps[0] + steps[1] + steps[2]


def scatter_eight(value):
    groups = [list(range(8)), list(range(8, 16))]
    flat = value.reshape(-1, value.shape[-1])
    out = lax.psum_scatter(flat, "fsdp", scatter_dimension=0, tiled=True, axis_index_groups=groups)
    return out.reshape((2,) + value.shape[1:])


def eight_order(f):
    return ((f // 2) % 4 * 2 + f % 2) * 2 + f // 8


def adam_update(weight, gradient, moment_one, moment_two, learn_rate, decay_rate):
    moment_one = BETA_ONE * moment_one + (1.0 - BETA_ONE) * gradient
    moment_two = BETA_TWO * moment_two + (1.0 - BETA_TWO) * gradient * gradient
    scaled = (
        moment_one
        / (1.0 - BETA_ONE**STEP)
        / (jnp.sqrt(moment_two / (1.0 - BETA_TWO**STEP)) + ADAM_EPS)
    )
    return (weight - learn_rate * (scaled + decay_rate * weight), moment_one, moment_two)


def contract_rows(left_side, right_side):
    return lax.dot_general(
        left_side, right_side, (((0,), (0,)), ((), ())), preferred_element_type=F32
    )


def contract_cols(left_side, right_side):
    return lax.dot_general(
        left_side, right_side, (((1,), (1,)), ((), ())), preferred_element_type=F32
    )


def matmul(left_side, right_side):
    return jnp.dot(left_side, right_side, preferred_element_type=F32)


def segment_at(positions, seg_ends):
    counted = jnp.sum((positions[:, None] >= seg_ends[None, :]).astype(jnp.int32), axis=1)
    return jnp.where(positions < 0, jnp.int32(-1), counted)


def split_two(value):
    high = value.astype(BF16)
    return high, (value - high.astype(F32)).astype(BF16)


def split_three(value):
    high = value.astype(BF16)
    rest = value - high.astype(F32)
    middle = rest.astype(BF16)
    return high, middle, (rest - middle.astype(F32)).astype(BF16)


def product(left, right, left_dim, right_dim):
    return lax.dot_general(
        left, right, (((left_dim,), (right_dim,)), ((), ())), preferred_element_type=F32
    )


def joined_product(left_parts, right_parts, left_dim=1, right_dim=0):
    left_high, left_low = left_parts
    right_high, right_low = right_parts
    return product(
        jnp.concatenate([left_high, left_high, left_low], left_dim),
        jnp.concatenate([right_high, right_low, right_high], right_dim),
        left_dim,
        right_dim,
    )


def precise_product(left, right, left_dim=1, right_dim=0):
    return joined_product(split_two(left), split_two(right), left_dim, right_dim)


def ones_product(ones, value):
    return product(jnp.concatenate([ones] * 3, 1), jnp.concatenate(split_three(value), 0), 1, 0)


def spread(per_head, lane):
    return jnp.concatenate(
        [
            jnp.where(lane < P_SIZE, per_head[:, 2 * k : 2 * k + 1], per_head[:, 2 * k + 1 : 2 * k + 2])
            for k in range(OWN_H // 2)
        ],
        1,
    )


def head_sums(value):
    column = lax.broadcasted_iota(jnp.int32, (OWN, N), 0)
    head = lax.broadcasted_iota(jnp.int32, (OWN, N), 1)
    members = ((column >= head * P_SIZE) & (column < (head + 1) * P_SIZE)).astype(F32).astype(BF16)
    high, low = split_two(value)
    return product(jnp.concatenate([high, low], 1), jnp.concatenate([members, members], 0), 1, 0)


def two_heads(pair, lane):
    zero = jnp.zeros_like(pair)
    return jnp.concatenate([jnp.where(lane < P_SIZE, pair, zero), jnp.where(lane < P_SIZE, zero, pair)], 0)


def chunk_facts(ends, chunk, dt_pre, par):
    column = lax.broadcasted_iota(jnp.int32, (CHUNK, 1), 0) + chunk * CHUNK
    row = lax.broadcasted_iota(jnp.int32, (1, CHUNK), 1) + chunk * CHUNK

    def segment(position):
        counted = jnp.zeros_like(position)
        for k in range(3):
            counted = counted + (position >= ends[k]).astype(jnp.int32)
        return jnp.where(position < 0, -1, counted)

    def one_segment(position):
        counted = jnp.int32(0)
        for k in range(3):
            counted = counted + (position >= ends[k]).astype(jnp.int32)
        return jnp.where(position < 0, -1, counted)

    here_column, here_row = segment(column), segment(row)
    prior = one_segment(chunk * CHUNK - 1)
    last = one_segment(chunk * CHUNK + CHUNK - 1)
    lane = lax.broadcasted_iota(jnp.int32, (CHUNK, N), 1)
    shifted = dt_pre + par[6:7, :N]
    soft = jnp.maximum(shifted, 0.0) + jnp.log1p(jnp.exp(-jnp.abs(shifted)))
    step = jnp.where(lane < OWN_H, soft, 0.0)
    decay = step * par[7:8, :N]
    tri_row = lax.broadcasted_iota(jnp.int32, (CHUNK, CHUNK), 0)
    tri_column = lax.broadcasted_iota(jnp.int32, (CHUNK, CHUNK), 1)
    lower = (tri_row >= tri_column).astype(F32).astype(BF16)
    upper = (tri_row <= tri_column).astype(F32).astype(BF16)
    total = ones_product(lower, decay)
    entering = (here_column == prior).astype(F32) * jnp.exp(total)
    end = total[CHUNK - 1 : CHUNK]
    leaving = (here_column == last).astype(F32) * jnp.exp(jnp.minimum(end - total, 0.0))
    passing = jnp.where(last == prior, 1.0, 0.0) * jnp.exp(end)
    return dict(
        column=column,
        segment=segment,
        here_column=here_column,
        here_row=here_row,
        lane=lane,
        shifted=shifted,
        step=step,
        decay=decay,
        total=total,
        entering=entering,
        leaving=leaving,
        passing=passing,
        tri_row=tri_row,
        tri_column=tri_column,
        upper=upper,
    )


def forward_kernel(part, ends, proj, par, *refs):
    if part:
        carry_in, refs = refs[3], refs[4:]
    pre_out, mixed_out, state_out, carry_out, extended, state = refs
    chunk = pl.program_id(0) + part * HALF

    @pl.when(pl.program_id(0) == 0)
    def _():
        if part:
            state[...] = carry_in[:N, :OWN]
            extended[0:8, :] = carry_in[N:, :]
        else:
            state[...] = jnp.zeros_like(state)
            extended[0:8, :] = jnp.zeros((8, 640), F32)

    facts = chunk_facts(ends, chunk, proj[:, 1024:1152], par)
    lane = facts["lane"]
    conv = proj[:, OWN:1024].astype(BF16).astype(F32)
    extended[8 : 8 + CHUNK, :] = conv
    pre = par[4:5] + par[3:4] * conv
    for back in range(1, CONV):
        same = (facts["segment"](facts["column"] - back) == facts["here_column"]).astype(F32)
        pre = pre + par[3 - back : 4 - back] * (extended[8 - back : 8 - back + CHUNK, :] * same)
    extended[0:8, :] = extended[CHUNK : CHUNK + 8, :]
    pre_out[...] = pre
    act = pre * jax.nn.sigmoid(pre)
    own_x, state_b, state_c = act[:, :OWN], act[:, OWN : OWN + N], act[:, OWN + N :]
    stepped = own_x * spread(facts["step"], lane)
    b_parts, c_parts = split_two(state_b), split_two(state_c)
    inside = (facts["tri_row"] >= facts["tri_column"]) & (facts["here_column"] == facts["here_row"])
    scores = jnp.where(inside, joined_product(c_parts, b_parts, 1, 1), 0.0)
    total_rows = facts["total"].T
    state_in = state[...]
    state_out[...] = state_in
    outs = []
    for pair in range(OWN_H // 2):
        mixing = []
        for head in (2 * pair, 2 * pair + 1):
            span = facts["total"][:, head : head + 1] - total_rows[head : head + 1, :]
            mixing.append(jnp.exp(jnp.minimum(span, 0.0)) * scores)
        inner = two_heads(stepped[:, pair * N : pair * N + N], lane)
        outs.append(precise_product(jnp.concatenate(mixing, 1), inner))
    scanned = jnp.concatenate(outs, 1) + spread(facts["entering"], lane) * joined_product(
        c_parts, split_two(state_in)
    )
    state[...] = spread(facts["passing"], lane[:1]) * state_in + precise_product(
        state_b.T, stepped * spread(facts["leaving"], lane)
    )
    mixed_out[...] = scanned + par[5:6, :OWN] * own_x

    @pl.when(pl.program_id(0) == HALF - 1)
    def _():
        carry_out[:N, :OWN] = state[...]
        carry_out[:N, OWN:] = jnp.zeros((N, 640 - OWN), F32)
        carry_out[N:, :] = extended[0:8, :]


def run_forward(part, ends, proj, par, before=()):
    here = lambda i: (i + part * HALF, 0)
    chunked = lambda width: pl.BlockSpec((CHUNK, width), here)
    fixed = lambda shape: pl.BlockSpec(shape, lambda i: (0, 0))
    carry = fixed((N + 8, 640))
    return pl.pallas_call(
        partial(forward_kernel, part),
        grid=(HALF,),
        in_specs=[pl.BlockSpec(memory_space=pltpu.SMEM), chunked(1152), fixed((16, 640))]
        + ([pl.BlockSpec(memory_space=pl.ANY)] * 3 + [carry] if part else []),
        out_specs=[chunked(640), chunked(OWN), pl.BlockSpec((N, OWN), here), carry],
        out_shape=[
            jax.ShapeDtypeStruct((PACK, 640), F32),
            jax.ShapeDtypeStruct((PACK, OWN), F32),
            jax.ShapeDtypeStruct((CHUNKS * N, OWN), F32),
            jax.ShapeDtypeStruct((N + 8, 640), F32),
        ],
        input_output_aliases={3: 0, 4: 1, 5: 2} if part else {},
        scratch_shapes=[pltpu.VMEM((CHUNK + 8, 640), F32), pltpu.VMEM((N, OWN), F32)],
        compiler_params=pltpu.CompilerParams(
            dimension_semantics=("arbitrary",), vmem_limit_bytes=VMEM_LIMIT
        ),
        cost_estimate=COST,
        name="scan_forward",
    )(ends, proj, par, *before)


def backward_kernel(ends, conv_in, dt_in, pre_in, mixed_in, grad_mixed, state_all, par, *refs):
    grad_x, grad_dt, grad_bc, sums, head_acc, carried, extended, end_dot = refs
    step_index = pl.program_id(0)
    chunk = CHUNKS - 1 - step_index

    @pl.when(step_index == 0)
    def _():
        carried[...] = jnp.zeros_like(carried)
        extended[CHUNK : CHUNK + 8, :] = jnp.zeros((8, OWN), F32)
        end_dot[...] = jnp.zeros_like(end_dot)
        sums[...] = jnp.zeros_like(sums)
        head_acc[...] = jnp.zeros_like(head_acc)

    facts = chunk_facts(ends, chunk, dt_in[...], par)
    lane = facts["lane"]
    pre = pre_in[...]
    sig = jax.nn.sigmoid(pre)
    act = pre * sig
    own_x, state_b, state_c = act[:, :OWN], act[:, OWN : OWN + N], act[:, OWN + N :]
    step = facts["step"]
    step_wide = spread(step, lane)
    stepped = own_x * step_wide
    skip = par[5:6, :OWN]
    scanned = mixed_in[...] - skip * own_x
    grad_m = grad_mixed[...]
    sums[6:7] += jnp.sum(grad_m * own_x, 0, keepdims=True)

    b_parts, c_parts = split_two(state_b), split_two(state_c)
    inside = (facts["tri_row"] <= facts["tri_column"]) & (facts["here_column"] == facts["here_row"])
    scores = jnp.where(inside, joined_product(b_parts, c_parts, 1, 1), 0.0)
    total_rows = facts["total"].T
    grad_scores = jnp.zeros((CHUNK, CHUNK), F32)
    grad_stepped = []
    for pair in range(OWN_H // 2):
        columns = slice(pair * N, pair * N + N)
        grad_pair = grad_m[:, columns]
        high, low = split_two(grad_pair)
        stepped_parts = split_two(two_heads(stepped[:, columns], lane))
        grad_mixing = joined_product(stepped_parts, (high, low), 1, 1)
        mixing = []
        for k in range(2):
            head = 2 * pair + k
            span = total_rows[head : head + 1, :] - facts["total"][:, head : head + 1]
            decays = jnp.exp(jnp.minimum(span, 0.0))
            mixing.append(decays * scores)
            grad_scores = grad_scores + decays * grad_mixing[k * CHUNK : (k + 1) * CHUNK]
        grad_stepped.append(
            joined_product(
                split_two(jnp.concatenate(mixing, 1)), (two_heads(high, lane), two_heads(low, lane))
            )
        )
    grad_scores = jnp.where(inside, grad_scores, 0.0)
    carry = carried[...]
    carry_parts = split_two(carry)
    leaving = spread(facts["leaving"], lane)
    grad_stepped = jnp.concatenate(grad_stepped, 1) + leaving * joined_product(b_parts, carry_parts)
    state_in = state_all[...]
    entered = spread(facts["entering"], lane) * grad_m
    entered_parts = split_two(entered)
    grad_b = precise_product(grad_scores, state_c) + joined_product(
        split_two(leaving * stepped), carry_parts, 1, 1
    )
    grad_c = precise_product(grad_scores.T, state_b) + joined_product(
        entered_parts, split_two(state_in), 1, 1
    )
    grad_bc[0:N, :] = grad_b.T
    grad_bc[N:, :] = grad_c.T
    new_carry = spread(facts["passing"], lane[:1]) * carry + joined_product(
        split_two(state_c.T), entered_parts
    )
    carried[...] = new_carry

    grad_step = head_sums(own_x * grad_stepped)
    last_row = lax.broadcasted_iota(jnp.int32, (CHUNK, N), 0) == CHUNK - 1
    grad_total = head_sums(grad_m * scanned) - step * grad_step
    grad_total = grad_total + jnp.where(last_row, end_dot[0:1, :], 0.0)
    grad_decay = ones_product(facts["upper"], grad_total)
    end_dot[...] = head_sums(
        jnp.broadcast_to(jnp.sum(new_carry * state_in, 0, keepdims=True), (8, OWN))
    )
    grad_pre_dt = (grad_step + grad_decay * par[7:8, :N]) * jax.nn.sigmoid(facts["shifted"])
    grad_pre_dt = jnp.where(lane < OWN_H, grad_pre_dt, 0.0)
    grad_dt[...] = grad_pre_dt.astype(BF16)
    head_acc[0:1] += jnp.sum(grad_pre_dt, 0, keepdims=True)
    head_acc[1:2] += jnp.sum(grad_decay * facts["decay"], 0, keepdims=True)

    sig_x, pre_x = sig[:, :OWN], pre[:, :OWN]
    grad_pre = (step_wide * grad_stepped + skip * grad_m) * (sig_x * (1.0 + pre_x * (1.0 - sig_x)))
    extended[0:CHUNK, :] = grad_pre
    conv = conv_in[...].astype(BF16).astype(F32)
    sums[5:6] += jnp.sum(grad_pre, 0, keepdims=True)
    sums[4:5] += jnp.sum(conv * grad_pre, 0, keepdims=True)
    grad_conv = par[3:4, :OWN] * grad_pre
    for ahead in range(1, CONV):
        same = (facts["segment"](facts["column"] + ahead) == facts["here_column"]).astype(F32)
        later = extended[ahead : ahead + CHUNK, :] * same
        sums[4 - ahead : 5 - ahead] += jnp.sum(conv * later, 0, keepdims=True)
        grad_conv = grad_conv + par[3 - ahead : 4 - ahead, :OWN] * later
    extended[CHUNK : CHUNK + 8, :] = extended[0:8, :]
    grad_x[...] = grad_conv.astype(BF16)


def run_backward(ends, proj, pre, mixed, grad_mixed, states, par):
    last = CHUNKS - 1
    chunked = lambda width, column=0: pl.BlockSpec((CHUNK, width), lambda i: (last - i, column))
    fixed = lambda shape: pl.BlockSpec(shape, lambda i: (0, 0))
    return pl.pallas_call(
        backward_kernel,
        grid=(CHUNKS,),
        in_specs=[
            pl.BlockSpec(memory_space=pltpu.SMEM),
            chunked(OWN, 1),
            chunked(N, 8),
            chunked(640),
            chunked(OWN),
            chunked(OWN),
            pl.BlockSpec((N, OWN), lambda i: (last - i, 0)),
            fixed((16, 640)),
        ],
        out_specs=[
            chunked(OWN),
            chunked(N),
            pl.BlockSpec((2 * N, CHUNK), lambda i: (0, last - i)),
            fixed((8, OWN)),
            fixed((8, N)),
        ],
        out_shape=[
            jax.ShapeDtypeStruct((PACK, OWN), BF16),
            jax.ShapeDtypeStruct((PACK, N), BF16),
            jax.ShapeDtypeStruct((2 * N, PACK), F32),
            jax.ShapeDtypeStruct((8, OWN), F32),
            jax.ShapeDtypeStruct((8, N), F32),
        ],
        scratch_shapes=[
            pltpu.VMEM((N, OWN), F32),
            pltpu.VMEM((CHUNK + 8, OWN), F32),
            pltpu.VMEM((8, N), F32),
        ],
        compiler_params=pltpu.CompilerParams(
            dimension_semantics=("arbitrary",), vmem_limit_bytes=VMEM_LIMIT
        ),
        cost_estimate=COST,
        name="scan_backward",
    )(ends, proj, proj, pre, mixed, grad_mixed, states, par)


PARTS = (1, 1, 1, 1, 1, 2, 1, 1)


def piece_copies(pieces, parts, blocks, sems):
    copies = []
    taken = 0
    for slot, count in enumerate(parts):
        rows = ROWS // count
        copies.append(
            [
                pltpu.make_async_copy(
                    pieces[taken + k], blocks.at[slot, pl.ds(k * rows, rows)], sems.at[taken + k]
                )
                for k in range(count)
            ]
        )
        taken += count
    return copies


def fetch_block(pieces, parts, blocks, sems):
    copies = piece_copies(pieces, parts, blocks, sems)
    step = pl.program_id(0)

    @pl.when(step == 0)
    def _():
        for group in copies:
            for copy in group:
                copy.start()

    for slot, group in enumerate(copies):

        @pl.when(step == slot)
        def _(group=group):
            for copy in group:
                copy.wait()

    return blocks[step]


def project_kernel(parts, table, *refs):
    pieces = refs[: sum(parts)]
    gain, shards, normed_out, proj, dt_out, blocks, weight, sems = refs[sum(parts) :]
    block = fetch_block(pieces, parts, blocks, sems)

    @pl.when(pl.program_id(0) == 0)
    def _():
        for f in range(N_FSDP):
            weight[f * SHARD_IN : (f + 1) * SHARD_IN, :] = shards[(f // 2) % 4, f % 2, f // 8, :SHARD_IN]
        dt_out[...] = weight[:, 1024:]

    values = block.astype(F32)
    scale = lax.rsqrt(jnp.mean(values * values, axis=1, keepdims=True) + NORM_EPS)
    normed = (values * scale * gain[...]).astype(BF16)
    normed_out[...] = normed
    proj[...] = matmul(normed, weight[...])


def run_project(table, pieces, gain, shards):
    fixed = lambda shape: pl.BlockSpec(shape, lambda i, table: (0,) * len(shape))
    placed = lambda width: pl.BlockSpec((ROWS, width), lambda i, table: (table[i], 0))
    return pl.pallas_call(
        partial(project_kernel, PARTS),
        grid_spec=pltpu.PrefetchScalarGridSpec(
            num_scalar_prefetch=1,
            grid=(N_REP,),
            in_specs=[pl.BlockSpec(memory_space=pl.ANY)] * len(pieces) + [fixed((1, D)), fixed(shards.shape)],
            out_specs=[placed(D), placed(3 * WIDE), fixed((D, N))],
            scratch_shapes=[
                pltpu.VMEM((N_REP, ROWS, D), BF16),
                pltpu.VMEM((D, 3 * WIDE), BF16),
                pltpu.SemaphoreType.DMA((len(pieces),)),
            ],
        ),
        out_shape=[
            jax.ShapeDtypeStruct((PACK, D), BF16),
            jax.ShapeDtypeStruct((PACK, 3 * WIDE), F32),
            jax.ShapeDtypeStruct((D, N), BF16),
        ],
        compiler_params=pltpu.CompilerParams(
            dimension_semantics=("arbitrary",), vmem_limit_bytes=VMEM_LIMIT
        ),
        cost_estimate=COST,
        name="project",
    )(table, *pieces, gain, shards)


def row_sums(value):
    folded = value[:, :N] + value[:, N : 2 * N] + value[:, 2 * N :]
    return jnp.sum(folded.T, 0, keepdims=True)


def out_grad_kernel(table, *refs):
    pieces = refs[: sum(PARTS)]
    w_out, mixed, gate_in, gain, branch_out, grad_out, sums, blocks, turned, sems = refs[sum(PARTS) :]
    branch = fetch_block(pieces, PARTS, blocks, sems)

    @pl.when(pl.program_id(0) == 0)
    def _():
        turned[...] = w_out[...].reshape(OWN, D).T

    branch_out[...] = branch
    total = matmul(branch, turned[...])
    grad_out[...] = total
    gate = gate_in[...]
    gated = mixed[...] * (gate * jax.nn.sigmoid(gate))
    row = lax.broadcasted_iota(jnp.int32, (8, ROWS), 0)
    sums[...] = jnp.where(
        row == 0, row_sums(gated * gated), jnp.where(row == 1, row_sums(total * gain[...] * gated), 0.0)
    )


def run_out_grad(table, pieces, w_out, mixed, proj, gain):
    fixed = lambda shape: pl.BlockSpec(shape, lambda i, table: (0, 0))
    placed = lambda width: pl.BlockSpec((ROWS, width), lambda i, table: (table[i], 0))
    own = pl.BlockSpec(
        (1, 2, 1, SHARD_OUT, D), lambda i, table: (table[N_REP] % 4, 0, table[N_REP] // 4, 0, 0)
    )
    return pl.pallas_call(
        out_grad_kernel,
        grid_spec=pltpu.PrefetchScalarGridSpec(
            num_scalar_prefetch=1,
            grid=(N_REP,),
            in_specs=[pl.BlockSpec(memory_space=pl.ANY)] * len(pieces)
            + [own, placed(OWN), placed(OWN), fixed((1, OWN))],
            out_specs=[placed(D), placed(OWN), pl.BlockSpec((8, ROWS), lambda i, table: (0, table[i]))],
            scratch_shapes=[
                pltpu.VMEM((N_REP, ROWS, D), BF16),
                pltpu.VMEM((D, WIDE), BF16),
                pltpu.SemaphoreType.DMA((len(pieces),)),
            ],
        ),
        out_shape=[
            jax.ShapeDtypeStruct((PACK, D), BF16),
            jax.ShapeDtypeStruct((PACK, OWN), F32),
            jax.ShapeDtypeStruct((8, PACK), F32),
        ],
        compiler_params=pltpu.CompilerParams(
            dimension_semantics=("arbitrary",), vmem_limit_bytes=VMEM_LIMIT
        ),
        cost_estimate=COST,
        name="out_grad",
    )(table, *pieces, w_out, mixed, proj, gain)


def gate_kernel(grad_out, mixed_in, gate_in, sums, gain, low_out, grad_mixed, grad_gain):
    rows = grad_out.shape[0]
    mixed, gate, grad_o = mixed_in[...], gate_in[...], grad_out[...]
    stats = jnp.concatenate([sums[...], jnp.zeros((N - 8, rows), F32)], 0).T
    out_scale = lax.rsqrt(stats[:, 0:1] * (1.0 / DI) + NORM_EPS)
    pull = out_scale * out_scale * out_scale * (stats[:, 1:2] * (1.0 / DI))
    gate_sig = jax.nn.sigmoid(gate)
    silu = gate * gate_sig
    gated = mixed * silu
    unit = gated * out_scale
    grad_gated = out_scale * (grad_o * gain[...]) - gated * pull
    grad_mixed[...] = grad_gated * silu
    low_out[:, :OWN] = (unit * gain[...]).astype(BF16)
    low_out[:, OWN:] = (grad_gated * mixed * (gate_sig * (1.0 + gate * (1.0 - gate_sig)))).astype(BF16)
    gain_part = jnp.sum(grad_o * unit, 0, keepdims=True)

    @pl.when(pl.program_id(0) == 0)
    def _():
        grad_gain[...] = jnp.broadcast_to(gain_part, grad_gain.shape)

    @pl.when(pl.program_id(0) > 0)
    def _():
        grad_gain[...] += gain_part


def run_gate(grad_out, mixed, proj, sums, gain):
    rows = lambda width: pl.BlockSpec((ROWS, width), lambda i: (i, 0))
    fixed = lambda shape: pl.BlockSpec(shape, lambda i: (0, 0))
    return pl.pallas_call(
        gate_kernel,
        grid=(PACK // ROWS,),
        in_specs=[
            rows(OWN),
            rows(OWN),
            rows(OWN),
            pl.BlockSpec((8, ROWS), lambda i: (0, i)),
            fixed((1, OWN)),
        ],
        out_specs=[rows(2 * OWN), rows(OWN), fixed((8, OWN))],
        out_shape=[
            jax.ShapeDtypeStruct((PACK, 2 * OWN), BF16),
            jax.ShapeDtypeStruct((PACK, OWN), F32),
            jax.ShapeDtypeStruct((8, OWN), F32),
        ],
        compiler_params=pltpu.CompilerParams(
            dimension_semantics=("arbitrary",), vmem_limit_bytes=VMEM_LIMIT
        ),
        cost_estimate=COST,
        name="gate_backward",
    )(grad_out, mixed, proj, sums, gain)


def early_grad_kernel(low, grad_branch, normed, out):
    step = pl.program_id(0)

    @pl.when(step == 0)
    def _():
        out[...] = jnp.zeros_like(out)

    for k in range(4):
        part = product(low[:, :OWN], grad_branch[:, k * WIDE : (k + 1) * WIDE], 0, 0)
        for m in range(4):
            out[eight_order(4 * k + m), :SHARD_IN] += part[m * SHARD_IN : (m + 1) * SHARD_IN]
    part = product(normed[...], low[:, OWN:], 0, 0)
    for f in range(N_FSDP):
        out[eight_order(f), SHARD_IN:] += part[f * SHARD_IN : (f + 1) * SHARD_IN]


def run_early_grad(low, grad_branch, normed):
    count = 2 * ROWS
    rows = lambda width: pl.BlockSpec((count, width), lambda i: (i, 0))
    shape = (N_FSDP, 2 * SHARD_IN, WIDE)
    return pl.pallas_call(
        early_grad_kernel,
        grid=(PACK // count,),
        in_specs=[rows(2 * OWN), rows(D), rows(D)],
        out_specs=pl.BlockSpec(shape, lambda i: (0, 0, 0)),
        out_shape=jax.ShapeDtypeStruct(shape, F32),
        compiler_params=pltpu.CompilerParams(
            dimension_semantics=("arbitrary",), vmem_limit_bytes=VMEM_LIMIT
        ),
        cost_estimate=COST,
        name="early_grad",
    )(low, grad_branch, normed)


def block_out_kernel(rows, weight, tokens, live, out):
    step = pl.program_id(0)
    part = matmul(jnp.concatenate([rows[0], rows[1]], 1), weight[...].reshape(2 * OWN, D))

    @pl.when(step == 0)
    def _():
        out[...] = part

    @pl.when(step > 0)
    def _():
        out[...] += part

    @pl.when(step == N_REP // 2 - 1)
    def _():
        out[...] = tokens[...].astype(F32) + live[...] * out[...]


def run_block_out(rows, weight, tokens, live):
    fixed = lambda shape: pl.BlockSpec(shape, lambda i: (0, 0))
    return pl.pallas_call(
        block_out_kernel,
        grid=(N_REP // 2,),
        in_specs=[
            pl.BlockSpec((2, ROWS, OWN), lambda i: (i, 0, 0)),
            pl.BlockSpec((2, 2, 1, SHARD_OUT, D), lambda i: (i % 2, 0, i // 2, 0, 0)),
            fixed((ROWS, D)),
            fixed((ROWS, 1)),
        ],
        out_specs=fixed((ROWS, D)),
        out_shape=jax.ShapeDtypeStruct((ROWS, D), F32),
        compiler_params=pltpu.CompilerParams(
            dimension_semantics=("arbitrary",), vmem_limit_bytes=VMEM_LIMIT
        ),
        cost_estimate=FILL,
        name="block_out",
    )(rows, weight, tokens, live)


def turned_part(weight, rows):
    return product(weight[...].reshape(D, weight.shape[-1]), rows, 1, 1)


def columns_of(full_in, width, index):
    return pl.BlockSpec(full_in.shape[:-1] + (width,), lambda i: (0, 0, 0, 0, index(i)))


def z_grad_kernel(rows, weight, out):
    part = turned_part(weight, jnp.concatenate([rows[0], rows[1]], 1))

    @pl.when(pl.program_id(0) == 0)
    def _():
        out[...] = part

    @pl.when(pl.program_id(0) > 0)
    def _():
        out[...] += part


def run_z_grad(rows, full_in):
    return pl.pallas_call(
        z_grad_kernel,
        grid=(N_REP // 2,),
        in_specs=[
            pl.BlockSpec((2, ROWS, OWN), lambda i: (i, 0, 1)),
            columns_of(full_in, 2 * OWN, lambda i: i),
        ],
        out_specs=pl.BlockSpec((D, ROWS), lambda i: (0, 0)),
        out_shape=jax.ShapeDtypeStruct((D, ROWS), F32),
        compiler_params=pltpu.CompilerParams(
            dimension_semantics=("arbitrary",), vmem_limit_bytes=VMEM_LIMIT
        ),
        cost_estimate=FILL,
        name="z_grad",
    )(rows, full_in)


def input_grad_kernel(
    own_half, grad_z, x_rows, rest_rows, w_x, w_bc, low_dt, tokens, cotangent, gain, out, gain_out, total, ordered
):
    step = pl.program_id(0)
    part = turned_part(w_x, jnp.concatenate([x_rows[0], x_rows[1]], 1))

    @pl.when(step == 0)
    def _():
        total[...] = grad_z[...] + part

    @pl.when(step > 0)
    def _():
        total[...] += part

    @pl.when(step == N_REP // 2 - 1)
    def _():
        lane = lax.broadcasted_iota(jnp.int32, (ROWS, N), 1)
        groups = []
        for k in range(2):
            group = jnp.zeros((ROWS, N), F32)
            for m in range(4):
                value = rest_rows[4 * k + m].astype(F32)
                value = value if m == 0 else pltpu.roll(value, m * OWN_BC, 1)
                group = jnp.where((lane >= m * OWN_BC) & (lane < (m + 1) * OWN_BC), value, group)
            groups.append(group.astype(BF16))
        steps = jnp.zeros((ROWS, N), F32)
        for m in range(N_REP):
            start = 8 + m * OWN_H
            value = pltpu.roll(rest_rows[m].astype(F32), (start - OWN_BC) % N, 1)
            steps = jnp.where((lane >= start) & (lane < start + OWN_H), value, steps)
        total[...] += turned_part(w_bc, jnp.concatenate(groups, 1))
        for f in range(N_FSDP):
            place = eight_order(f) - f // 8 + (f // 8 + own_half[0]) % 2
            start = pl.multiple_of(place * SHARD_IN, SHARD_IN)
            ordered[f * SHARD_IN : (f + 1) * SHARD_IN, :] = total[pl.ds(start, SHARD_IN), :]
        grad_h = (ordered[...] + product(low_dt[...], steps.astype(BF16), 1, 1)).T
        values = tokens[...].astype(F32)
        scale = lax.rsqrt(jnp.mean(values * values, axis=1, keepdims=True) + NORM_EPS)
        unit = values * scale
        gain_sum = jnp.sum(grad_h * unit, 0, keepdims=True)
        gain_out[...] = jnp.zeros_like(gain_out)
        for k in range(D // TAIL):
            gain_out[k : k + 1, :] = gain_sum[:, k * TAIL : (k + 1) * TAIL]
        grad_unit = grad_h * gain[...]
        inner = jnp.mean(grad_unit * unit, axis=1, keepdims=True)
        out[...] = cotangent[...].astype(F32) + scale * (grad_unit - unit * inner)


def run_input_grad(own_half, grad_z, tail_rows, full_in, low_dt, tokens, cotangent, gain):
    fixed = lambda shape: pl.BlockSpec(shape, lambda i: (0,) * len(shape))
    return pl.pallas_call(
        input_grad_kernel,
        grid=(N_REP // 2,),
        in_specs=[
            pl.BlockSpec(memory_space=pltpu.SMEM),
            fixed((D, ROWS)),
            pl.BlockSpec((2, ROWS, OWN), lambda i: (i, 0, 0)),
            pl.BlockSpec((N_REP, ROWS, N), lambda i: (0, 0, OWN // N)),
            columns_of(full_in, 2 * OWN, lambda i: N_REP // 2 + i),
            columns_of(full_in, 2 * N, lambda i: DI // N),
            fixed((D, N)),
            fixed((ROWS, D)),
            fixed((ROWS, D)),
            fixed((1, D)),
        ],
        out_specs=[fixed((ROWS, D)), fixed((8, TAIL))],
        out_shape=[jax.ShapeDtypeStruct((ROWS, D), F32), jax.ShapeDtypeStruct((8, TAIL), F32)],
        scratch_shapes=[pltpu.VMEM((D, ROWS), F32), pltpu.VMEM((D, ROWS), F32)],
        compiler_params=pltpu.CompilerParams(
            dimension_semantics=("arbitrary",), vmem_limit_bytes=VMEM_LIMIT
        ),
        cost_estimate=COST,
        name="input_grad",
    )(own_half, grad_z, tail_rows, tail_rows, full_in, full_in, low_dt, tokens, cotangent, gain)


def rest_kernel(
    ends, parts, pre_b, pre_c, conv_in, par, grad_x, grad_dt, sums, head_acc, grad_gain, first, tail_out, small_out
):
    own = lax.broadcasted_iota(jnp.int32, (OWN_BC, 2 * N), 0) + first[0]
    chosen = (lax.broadcasted_iota(jnp.int32, (OWN_BC, 2 * N), 1) == own).astype(F32).astype(BF16)

    def pick(value):
        return product(jnp.concatenate([chosen] * 3, 1), jnp.concatenate(split_three(value), 1), 1, 1)

    grad = parts[0]
    for k in range(1, N_REP):
        grad = grad + parts[k]
    own_pre = pick(jnp.concatenate([pre_b[...], pre_c[...]], 1))
    own_conv = product(chosen, conv_in[...].astype(BF16), 1, 1)
    taps = pick(par[:, OWN:])
    sig = jax.nn.sigmoid(own_pre)
    grad_pre = grad * (sig * (1.0 + own_pre * (1.0 - sig)))
    position = lax.broadcasted_iota(jnp.int32, (1, PACK), 1)

    def segment(places):
        counted = jnp.zeros_like(places)
        for k in range(3):
            counted = counted + (places >= ends[k]).astype(jnp.int32)
        return counted

    grad_conv = taps[:, CONV - 1 : CONV] * grad_pre
    column = lax.broadcasted_iota(jnp.int32, (OWN_BC, N), 1)
    found = jnp.where(column == CONV, jnp.sum(grad_pre, 1, keepdims=True), 0.0)
    found = jnp.where(column == CONV - 1, jnp.sum(own_conv * grad_pre, 1, keepdims=True), found)
    for later_by in range(1, CONV):
        same = (segment(position + later_by) == segment(position)) & (position < PACK - later_by)
        later = jnp.where(same, pltpu.roll(grad_pre, PACK - later_by, 1), 0.0)
        tap = CONV - 1 - later_by
        found = jnp.where(column == tap, jnp.sum(own_conv * later, 1, keepdims=True), found)
        grad_conv = grad_conv + taps[:, tap : tap + 1] * later
    lane = lax.broadcasted_iota(jnp.int32, (N, N), 1)
    filler = jnp.zeros((N - OWN_BC, N), F32)
    for k in range(PACK // N):
        rows = slice(k * N, (k + 1) * N)
        columns = jnp.concatenate([grad_conv[:, rows], filler], 0).T
        steps = pltpu.roll(grad_dt[rows, :].astype(F32), OWN_BC, 1)
        tail_out[rows, :OWN] = grad_x[rows, :]
        tail_out[rows, OWN:] = jnp.where(
            lane < OWN_BC, columns, jnp.where(lane < OWN_BC + OWN_H, steps, 0.0)
        ).astype(BF16)
    row = lax.broadcasted_iota(jnp.int32, (8, OWN), 0)
    skip = head_sums(sums[...])
    by_head = jnp.concatenate([skip, jnp.zeros((8, OWN - N), F32)], 1)
    logs = jnp.concatenate([head_acc[...], jnp.zeros((8, OWN - N), F32)], 1)
    wide = jnp.where(row == 0, grad_gain[0:1, :], jnp.where(row < 6, sums[...], 0.0))
    wide = jnp.where(row == 6, logs[1:2, :], jnp.where(row == 7, by_head[6:7, :], wide))
    turned = jnp.concatenate([found, filler], 0).T
    first_row = lax.broadcasted_iota(jnp.int32, (8, N), 0) == 0
    small_out[:, :OWN] = wide
    small_out[:, OWN:] = jnp.where(first_row, head_acc[0:1, :], pltpu.roll(turned[:8], 1, 0))


def run_rest(ends, parts, pre, proj, par, grad_x, grad_dt, sums, head_acc, grad_gain, first):
    fixed = lambda shape: pl.BlockSpec(shape, lambda i: (0,) * len(shape))
    return pl.pallas_call(
        rest_kernel,
        grid=(1,),
        in_specs=[
            pl.BlockSpec(memory_space=pltpu.SMEM),
            fixed((N_REP, OWN_BC, PACK)),
            pl.BlockSpec((PACK, N), lambda i: (0, 3)),
            pl.BlockSpec((PACK, N), lambda i: (0, 4)),
            pl.BlockSpec((PACK, 2 * N), lambda i: (0, 3)),
            fixed((16, 640)),
            fixed((PACK, OWN)),
            fixed((PACK, N)),
            fixed((8, OWN)),
            fixed((8, N)),
            fixed((8, OWN)),
            pl.BlockSpec(memory_space=pltpu.SMEM),
        ],
        out_specs=[fixed((PACK, TAIL)), fixed((8, TAIL))],
        out_shape=[jax.ShapeDtypeStruct((PACK, TAIL), BF16), jax.ShapeDtypeStruct((8, TAIL), F32)],
        compiler_params=pltpu.CompilerParams(
            dimension_semantics=("arbitrary",), vmem_limit_bytes=VMEM_LIMIT
        ),
        cost_estimate=COST,
        name="rest_backward",
    )(ends, parts, pre, pre, proj, par, grad_x, grad_dt, sums, head_acc, grad_gain, first)


def tail_grad_kernel(normed, tail, small, out):
    step = pl.program_id(0)
    part = product(normed[...], tail[...], 0, 0)
    for f in range(N_FSDP):
        rows = part[f * SHARD_IN : (f + 1) * SHARD_IN]

        @pl.when(step == 0)
        def _(f=f, rows=rows):
            out[eight_order(f), :SHARD_IN] = rows
            out[eight_order(f), SHARD_IN:] = small[...]

        @pl.when(step > 0)
        def _(f=f, rows=rows):
            out[eight_order(f), :SHARD_IN] += rows


def run_tail_grad(normed, tail, small):
    count = 2 * ROWS
    shape = (N_FSDP, SHARD_IN + 8, TAIL)
    return pl.pallas_call(
        tail_grad_kernel,
        grid=(PACK // count,),
        in_specs=[
            pl.BlockSpec((count, D), lambda i: (i, 0)),
            pl.BlockSpec((count, TAIL), lambda i: (i, 0)),
            pl.BlockSpec((8, TAIL), lambda i: (0, 0)),
        ],
        out_specs=pl.BlockSpec(shape, lambda i: (0, 0, 0)),
        out_shape=jax.ShapeDtypeStruct(shape, F32),
        compiler_params=pltpu.CompilerParams(
            dimension_semantics=("arbitrary",), vmem_limit_bytes=VMEM_LIMIT
        ),
        cost_estimate=COST,
        name="tail_grad",
    )(normed, tail, small)


def adam_step(grad, weight, first, second, grad_out, first_out, second_out, weight_out):
    new_weight, new_first, new_second = adam_update(
        weight[...], grad, first[...], second[...], RATE_MATRIX, WEIGHT_DECAY
    )
    grad_out[...] = grad
    first_out[...] = new_first
    second_out[...] = new_second
    weight_out[...] = new_weight


def adam_early_kernel(rows, pair, *refs):
    arrays, grad = refs[:-1], refs[-1]
    grad[:, :WIDE] = pair[0, rows, :]
    grad[:, WIDE:] = pair[1, rows, :]
    adam_step(grad[...], *arrays)


def run_adam_early(place_of, rows, parts, weight, first, second):
    part = pl.BlockSpec((SHARD_IN, 2 * WIDE), place_of)
    shape = jax.ShapeDtypeStruct(weight.shape, F32)
    return pl.pallas_call(
        partial(adam_early_kernel, rows),
        grid=(N_REP // 2,),
        in_specs=[pl.BlockSpec((2,) + parts.shape[1:], lambda i: (i, 0, 0))] + [part] * 3,
        out_specs=[part] * 4,
        out_shape=[shape] * 4,
        scratch_shapes=[pltpu.VMEM((SHARD_IN, 2 * WIDE), F32)],
        compiler_params=pltpu.CompilerParams(
            dimension_semantics=("arbitrary",), vmem_limit_bytes=VMEM_LIMIT
        ),
        cost_estimate=FILL,
        name="adam",
    )(parts, weight, first, second)


def adam_tail_kernel(pair, rest, *refs):
    arrays, grad = refs[:3] + refs[-5:-1], refs[-1]
    step = pl.program_id(0)

    @pl.when(step < N_REP // 2)
    def _():
        grad[:, :WIDE] = pair[0, :SHARD_IN]
        grad[:, WIDE:] = pair[1, :SHARD_IN]

    @pl.when(step == N_REP // 2)
    def _():
        lane = lax.broadcasted_iota(jnp.int32, (SHARD_IN, N), 1)
        for k in range(2):
            group = jnp.zeros((SHARD_IN, N), F32)
            for m in range(4):
                value = rest[4 * k + m, :SHARD_IN]
                value = value if m == 0 else pltpu.roll(value, m * OWN_BC, 1)
                group = jnp.where((lane >= m * OWN_BC) & (lane < (m + 1) * OWN_BC), value, group)
            grad[:, k * N : (k + 1) * N] = group

    adam_step(grad[...], *arrays)


def run_adam_tail(parts, weight, first, second, before):
    half = N_REP // 2
    rows = parts.shape[1]
    column = pl.BlockSpec((SHARD_IN, 2 * WIDE), lambda i: (0, half + i))
    shape = jax.ShapeDtypeStruct(weight.shape, F32)
    return pl.pallas_call(
        adam_tail_kernel,
        grid=(half + 1,),
        in_specs=[
            pl.BlockSpec((2, rows, OWN), lambda i: (jnp.minimum(i, half - 1), 0, 0)),
            pl.BlockSpec((N_REP, rows, N), lambda i: (0, 0, OWN // N)),
        ]
        + [column] * 3
        + [pl.BlockSpec(memory_space=pl.ANY)] * 4,
        out_specs=[column] * 4,
        out_shape=[shape] * 4,
        input_output_aliases={5 + k: k for k in range(4)},
        scratch_shapes=[pltpu.VMEM((SHARD_IN, 2 * WIDE), F32)],
        compiler_params=pltpu.CompilerParams(
            dimension_semantics=("arbitrary",), vmem_limit_bytes=VMEM_LIMIT
        ),
        cost_estimate=COST,
        name="adam_tail",
    )(parts, parts, weight, first, second, *before)


def body(
    tokens,
    cotangent,
    lengths,
    w_in,
    w_dt,
    w_out,
    small,
    first_in,
    first_dt,
    first_out,
    first_small,
    second_in,
    second_dt,
    second_out,
    second_small,
):
    place = Place()
    r = place.r
    zero = jnp.int32(0)
    pack_lengths = lax.dynamic_slice_in_dim(lengths, place.f, 1, 0)[0]
    seg_ends = jnp.cumsum(pack_lengths)
    own_positions = r * ROWS + jnp.arange(ROWS, dtype=jnp.int32)
    own_live = (segment_at(own_positions, seg_ends) < 3).astype(F32)[:, None]
    slots = jnp.arange(N_REP, dtype=jnp.int32)
    ahead = ((place.x + slots // 2) % 4) * 2 + (place.yl + slots) % 2
    half = ROWS // 2

    in_low = w_in.astype(BF16)
    dt_low = w_dt.astype(BF16)
    out_low = w_out.astype(BF16)

    small_rows = jnp.pad(small.astype(BF16), (0, 16 * 3 * WIDE - SHARD_SMALL)).reshape(16, 3 * WIDE)

    def own_columns(rep):
        columns = jnp.concatenate(
            [
                lax.dynamic_slice_in_dim(in_low, rep * OWN, OWN, 1),
                lax.dynamic_slice_in_dim(in_low, DI + rep * OWN, OWN, 1),
                in_low[:, 2 * DI :],
                lax.dynamic_slice_in_dim(dt_low, rep * OWN_H, OWN_H, 1),
                jnp.zeros((SHARD_IN, 2), BF16),
                dt_low,
                jnp.zeros((SHARD_IN, N - 8 - H), BF16),
            ],
            1,
        )
        return jnp.concatenate([columns, small_rows], 0)

    other_columns = move(
        own_columns(2 * place.x + 1 - place.yl), lambda yh, z, c, x, yl: (yh + 1, z, c, x, yl + 1)
    )
    from_left = move(tokens, along_x(1))
    from_right = move(tokens, along_x(-1))
    partner = move(tokens, swap_y)

    out_low, other_columns = lax.optimization_barrier((out_low, other_columns))
    out_other = move(out_low, lambda yh, z, c, x, yl: (yh + 1, z, c, x, yl + 1))
    branch = (cotangent.astype(F32) * own_live).astype(BF16)
    from_left, from_right, partner, other_columns, branch = lax.optimization_barrier(
        (from_left, from_right, partner, other_columns, branch)
    )
    own_shards = gather_eight(both(own_columns(r), other_columns, place.yh))
    far = move(from_left, along_x(1))
    partner_left = move(from_left, swap_y)
    partner_right = move(partner, along_x(-1))

    far, partner_left, partner_right, out_other, branch, in_low = lax.optimization_barrier(
        (far, partner_left, partner_right, out_other, branch, in_low)
    )
    in_other = move(in_low, lambda yh, z, c, x, yl: (yh + 1, z, c, x, yl + 1))
    out_pair = both(out_low, out_other, place.yh)
    partner_far_top = move(partner_left[:half], along_x(1))
    partner_far_low = move(partner_right[half:], along_x(-1))

    vector = own_shards[:, :, :, SHARD_IN : SHARD_IN + 2].transpose(2, 0, 1, 3, 4)
    vector = vector.reshape(N_FSDP, 6 * WIDE)[:, :SHARD_SMALL].reshape(-1).astype(F32)
    offset = 0
    gain_in = vector[None, :D]
    offset = D
    gain_row = lax.dynamic_slice_in_dim(vector, offset + r * OWN, OWN, 0)[None, :]
    offset += DI
    taps = vector[offset : offset + (CONV + 1) * CHANNELS].reshape(CONV + 1, CHANNELS)
    offset += (CONV + 1) * CHANNELS
    per_head = vector[offset:].reshape(3, H)
    dt_bias, a_log, d_skip = lax.dynamic_slice_in_dim(per_head, r * OWN_H, OWN_H, 1)
    taps_bc = taps[:, DI:]
    conv_par = jnp.concatenate([lax.dynamic_slice_in_dim(taps, r * OWN, OWN, 1), taps_bc], 1)
    head_par = jnp.stack(
        [
            jnp.pad(jnp.broadcast_to(d_skip[:, None], (OWN_H, P_SIZE)).reshape(-1), (0, 2 * N)),
            jnp.pad(dt_bias, (0, 640 - OWN_H)),
            jnp.pad(-jnp.exp(a_log), (0, 640 - OWN_H)),
        ],
        0,
    )
    par = jnp.concatenate([conv_par, head_par, jnp.zeros((8, 640), F32)], 0)

    partner_far_top, partner_far_low, own_shards = lax.optimization_barrier(
        (partner_far_top, partner_far_low, own_shards)
    )
    full_out = gather_eight(tie(out_pair, own_shards))
    b_left = move(branch, along_x(1))
    b_right = move(branch, along_x(-1))
    b_partner = move(branch, swap_y)
    token_pieces = [
        tokens, partner, from_right, partner_right, far,
        partner_far_top, partner_far_low, from_left, partner_left,
    ]
    normed, proj, low_dt = run_project(ahead, token_pieces, gain_in, own_shards)
    b_left, b_right, b_partner, proj = lax.optimization_barrier((b_left, b_right, b_partner, proj))
    b_far = move(b_left, along_x(1))
    b_partner_left = move(b_left, swap_y)
    b_partner_right = move(b_partner, along_x(-1))
    before = run_forward(0, seg_ends, proj, par)
    b_far, b_partner_left, b_partner_right, before = lax.optimization_barrier(
        (b_far, b_partner_left, b_partner_right, before)
    )
    b_partner_far_top = move(b_partner_left[:half], along_x(1))
    b_partner_far_low = move(b_partner_right[half:], along_x(-1))
    pre, mixed, states, _ = run_forward(1, seg_ends, proj, par, before)
    mixed, in_low, in_other, b_partner_far_top, b_partner_far_low = lax.optimization_barrier(
        (mixed, in_low, in_other, b_partner_far_top, b_partner_far_low)
    )
    full_in = gather_eight(jnp.stack([in_low, in_other], 0))
    branch_pieces = [
        branch, b_partner, b_right, b_partner_right, b_far,
        b_partner_far_top, b_partner_far_low, b_left, b_partner_left,
    ]
    rep_table = jnp.concatenate([ahead, r[None]])
    grad_branch, grad_normed_out, sums = run_out_grad(rep_table, branch_pieces, full_out, mixed, proj, gain_row)
    sums = share_rep(sums[:2].reshape(32, 128)).sum(0).reshape(2, PACK)
    sums = jnp.concatenate([sums, jnp.zeros((6, PACK), F32)], 0)

    low, grad_mixed, grad_gain = run_gate(grad_normed_out, mixed, proj, sums, gain_row)

    low_rows = exchange(low.reshape(N_REP, ROWS, 2 * OWN), "rep")
    grad_x, grad_dtraw, grad_bc, grad_sums, grad_heads = run_backward(
        seg_ends, proj, pre, mixed, grad_mixed, states, par
    )
    low, grad_x = lax.optimization_barrier((low, grad_x))
    early_grad = run_early_grad(low, grad_branch, normed)
    low_rows, early_grad, grad_bc, grad_x = lax.optimization_barrier((low_rows, early_grad, grad_bc, grad_x))

    grad_bc = exchange(grad_bc, "rep").reshape(N_REP, OWN_BC, PACK)
    early = scatter_eight(early_grad)
    grad_rows = run_z_grad(low_rows, full_in)
    grad_bc, grad_rows = lax.optimization_barrier((grad_bc, grad_rows))

    tail, small_own = run_rest(
        seg_ends, grad_bc, pre, proj, par, grad_x, grad_dtraw, grad_sums, grad_heads, grad_gain, (r * OWN_BC)[None]
    )
    grad_tail = run_tail_grad(normed, tail, small_own)
    tail, grad_tail, low_rows = lax.optimization_barrier((tail, grad_tail, low_rows))
    tail_rows = exchange(tail.reshape(N_REP, ROWS, TAIL), "rep")
    tail_part = scatter_eight(grad_tail)
    block_out = run_block_out(low_rows, full_out, tokens, own_live)
    early, block_out = lax.optimization_barrier((early, block_out))
    mine, other = at(early, place.yh), at(early, 1 - place.yh)
    out_mine = move(
        mine[:SHARD_IN], lambda yh, z, c, x, yl: (x // 2, (x % 2) * 2 + yl, z % 2, 2 * c + yh, z // 2)
    )
    out_other = move(
        other[:SHARD_IN], lambda yh, z, c, x, yl: (x // 2, (x % 2) * 2 + yl, z % 2, 2 * c + 1 - yh, z // 2)
    )
    z_other = move(other[SHARD_IN:], swap_y_hi)
    tail_rows, out_mine, out_other, z_other = lax.optimization_barrier((tail_rows, out_mine, out_other, z_other))

    early_parts = share_rep(jnp.concatenate([out_mine + out_other, mine[SHARD_IN:] + z_other], 0))
    input_grad, grad_gain_in = run_input_grad(
        place.yh[None], grad_rows, tail_rows, full_in, low_dt, tokens, cotangent, gain_in
    )
    tail_part, grad_gain_in = lax.optimization_barrier((tail_part, grad_gain_in))

    tail_other = move(at(tail_part, 1 - place.yh), swap_y_hi)
    grad_gain_in = sum_z(grad_gain_in + move(grad_gain_in, swap_core))
    tail_part = at(tail_part, place.yh) + tail_other
    grad_gain_in = grad_gain_in + move(grad_gain_in, swap_y_hi)
    tail_part = jnp.concatenate([tail_part, grad_gain_in], 0)

    tail_part, early_parts = lax.optimization_barrier((tail_part, early_parts))
    tail_parts = share_rep(tail_part)

    grad_out, new_first_out, new_second_out, new_out = run_adam_early(
        lambda i: (i // 2, i % 2), slice(0, SHARD_IN), early_parts, w_out, first_out, second_out
    )
    updated = run_adam_early(
        lambda i: (0, i), slice(SHARD_IN, 2 * SHARD_IN), early_parts, w_in, first_in, second_in
    )
    grad_in, new_first_in, new_second_in, new_in = run_adam_tail(tail_parts, w_in, first_in, second_in, updated)

    def columns(parts):
        return parts.transpose(1, 0, 2).reshape(parts.shape[1], -1)

    small_parts = tail_parts[:, SHARD_IN : SHARD_IN + 8]
    grad_gain_in = tail_parts[:, SHARD_IN + 8 : SHARD_IN + 8 + D // TAIL].sum(0).reshape(-1)
    small_x = small_parts[:, :, :OWN].transpose(1, 0, 2).reshape(8, DI)
    small_bc = small_parts[:, :, OWN:].transpose(1, 0, 2)

    def channels(row):
        return jnp.concatenate([small_x[row], small_bc[row, :, :OWN_BC].reshape(-1)])

    grad_small_all = jnp.concatenate(
        [grad_gain_in, small_x[0]]
        + [channels(row) for row in range(1, 6)]
        + [
            small_bc[0, :, :OWN_H].reshape(-1),
            small_parts[:, 6, :OWN_H].reshape(-1),
            small_parts[:, 7, :OWN_H].reshape(-1),
        ]
    )
    grad_small = lax.dynamic_slice_in_dim(grad_small_all, place.f * SHARD_SMALL, SHARD_SMALL, 0)
    grad_dt = columns(tail_parts[:, :SHARD_IN, OWN + OWN_BC : OWN + OWN_BC + OWN_H])
    new_dt, new_first_dt, new_second_dt = adam_update(
        w_dt, grad_dt, first_dt, second_dt, RATE_MATRIX, WEIGHT_DECAY
    )
    new_small, new_first_small, new_second_small = adam_update(
        small, grad_small, first_small, second_small, RATE_SMALL, 0.0
    )
    return (
        block_out,
        input_grad,
        grad_in,
        grad_dt,
        grad_out,
        grad_small,
        new_first_in,
        new_first_dt,
        new_first_out,
        new_first_small,
        new_second_in,
        new_second_dt,
        new_second_out,
        new_second_small,
        new_in,
        new_dt,
        new_out,
        new_small,
    )


def solution(mesh):
    rows = P(("fsdp", "rep"), None)
    matrix = P("fsdp", None)
    vector = P("fsdp")
    group = (matrix, matrix, matrix, vector)
    return jax.shard_map(
        body,
        mesh=mesh,
        in_specs=(rows, rows, P()) + group * 3,
        out_specs=(rows, rows) + group * 4,
        check_vma=False,
    )
```

```python
from functools import partial

import jax
import jax.numpy as jnp
from jax import lax
from jax.experimental import pallas as pl
from jax.experimental.pallas import tpu as pltpu
from jax.sharding import PartitionSpec as P

D = 1536
H = 48
P_SIZE = 64
N = 128
CONV = 4
STEP = 10
DI = 3072
CHANNELS = DI + 2 * N
SMALL = 21392
N_FSDP = 16
N_REP = 8
ROWS = 256
PACK = 2048
OWN = DI // N_REP
OWN_H = H // N_REP
OWN_BC = 2 * N // N_REP
SHARD_IN = D // N_FSDP
SHARD_OUT = DI // N_FSDP
SHARD_SMALL = SMALL // N_FSDP
WIDE = 384
CHUNK = 128
CHUNKS = PACK // CHUNK
HALF = CHUNKS // 2
TAIL = 512
VMEM_LIMIT = 60 * 1024 * 1024

NORM_EPS = 1e-05
BETA_ONE = 0.9
BETA_TWO = 0.999
ADAM_EPS = 1e-08
WEIGHT_DECAY = 0.1
RATE_MATRIX = 0.04
RATE_SMALL = 0.4
PRECISE = lax.Precision.HIGHEST
BF16 = jnp.bfloat16
F32 = jnp.float32
COST = pl.CostEstimate(flops=1_000_000, bytes_accessed=100_000, transcendentals=0)
FILL = pl.CostEstimate(flops=2_400_000_000, bytes_accessed=20_000_000, transcendentals=0)


def move(value, target):
    pairs = []
    for f in range(N_FSDP):
        for r in range(N_REP):
            yh, z, c, x, yl = target(f // 8, (f // 2) % 4, f % 2, r // 2, r % 2)
            pairs.append((f * N_REP + r, ((yh % 2) * 8 + (z % 4) * 2 + c % 2) * N_REP + (x % 4) * 2 + yl % 2))
    return lax.ppermute(value, ("fsdp", "rep"), pairs)


def along_x(steps):
    return lambda yh, z, c, x, yl: (yh, z, c, x + steps, yl)


def along_z(steps):
    return lambda yh, z, c, x, yl: (yh, z + steps, c, x, yl)


def swap_y(yh, z, c, x, yl):
    return (yh, z, c, x, yl + 1)


def swap_y_hi(yh, z, c, x, yl):
    return (yh + 1, z, c, x, yl)


def swap_core(yh, z, c, x, yl):
    return (yh, z, c + 1, x, yl)


class Place:
    def __init__(self):
        f = lax.axis_index("fsdp")
        r = lax.axis_index("rep")
        self.f, self.r = f, r
        self.yh, self.z, self.c = f // 8, (f // 2) % 4, f % 2
        self.x, self.yl = r // 2, r % 2


def at(value, index, axis=0):
    return lax.dynamic_index_in_dim(value, index, axis, keepdims=False)


def tie(values, *others):
    return lax.optimization_barrier((values, others))[0]


def both(mine, other, second):
    first = jnp.where(second == 0, mine, other)
    last = jnp.where(second == 0, other, mine)
    return jnp.stack([first, last], 0)


def put(out, piece, axis, index):
    starts = [jnp.int32(0)] * out.ndim
    starts[axis] = jnp.int32(index)
    return lax.dynamic_update_slice(out, jnp.expand_dims(piece, axis), tuple(starts))


def swap_shards(value, place):
    other = move(value, lambda yh, z, c, x, yl: (yh + 1, z, c, x, yl + 1))
    return both(value, other, place.yh)


def gather_eight(pair):
    groups = [list(range(8)), list(range(8, 16))]
    out = lax.all_gather(pair, "fsdp", axis=0, tiled=True, axis_index_groups=groups)
    return out.reshape((4, 2) + pair.shape)


def exchange(value, axis):
    return lax.all_to_all(value, axis, 0, 0, tiled=True)


def share_rep(value):
    return exchange(jnp.broadcast_to(value[None], (N_REP,) + value.shape), "rep")


def sum_z(value):
    steps = [move(value, along_z(step)) for step in (1, 3, 2)]
    return value + steps[0] + steps[1] + steps[2]


def scatter_eight(value):
    groups = [list(range(8)), list(range(8, 16))]
    flat = value.reshape(-1, value.shape[-1])
    out = lax.psum_scatter(flat, "fsdp", scatter_dimension=0, tiled=True, axis_index_groups=groups)
    return out.reshape((2,) + value.shape[1:])


def eight_order(f):
    return ((f // 2) % 4 * 2 + f % 2) * 2 + f // 8


def adam_update(weight, gradient, moment_one, moment_two, learn_rate, decay_rate):
    moment_one = BETA_ONE * moment_one + (1.0 - BETA_ONE) * gradient
    moment_two = BETA_TWO * moment_two + (1.0 - BETA_TWO) * gradient * gradient
    scaled = (
        moment_one
        / (1.0 - BETA_ONE**STEP)
        / (jnp.sqrt(moment_two / (1.0 - BETA_TWO**STEP)) + ADAM_EPS)
    )
    return (weight - learn_rate * (scaled + decay_rate * weight), moment_one, moment_two)


def contract_rows(left_side, right_side):
    return lax.dot_general(
        left_side, right_side, (((0,), (0,)), ((), ())), preferred_element_type=F32
    )


def contract_cols(left_side, right_side):
    return lax.dot_general(
        left_side, right_side, (((1,), (1,)), ((), ())), preferred_element_type=F32
    )


def matmul(left_side, right_side):
    return jnp.dot(left_side, right_side, preferred_element_type=F32)


def segment_at(positions, seg_ends):
    counted = jnp.sum((positions[:, None] >= seg_ends[None, :]).astype(jnp.int32), axis=1)
    return jnp.where(positions < 0, jnp.int32(-1), counted)


def split_two(value):
    high = value.astype(BF16)
    return high, (value - high.astype(F32)).astype(BF16)


def split_three(value):
    high = value.astype(BF16)
    rest = value - high.astype(F32)
    middle = rest.astype(BF16)
    return high, middle, (rest - middle.astype(F32)).astype(BF16)


def product(left, right, left_dim, right_dim):
    return lax.dot_general(
        left, right, (((left_dim,), (right_dim,)), ((), ())), preferred_element_type=F32
    )


def joined_product(left_parts, right_parts, left_dim=1, right_dim=0):
    left_high, left_low = left_parts
    right_high, right_low = right_parts
    return product(
        jnp.concatenate([left_high, left_high, left_low], left_dim),
        jnp.concatenate([right_high, right_low, right_high], right_dim),
        left_dim,
        right_dim,
    )


def precise_product(left, right, left_dim=1, right_dim=0):
    return joined_product(split_two(left), split_two(right), left_dim, right_dim)


def ones_product(ones, value):
    return product(jnp.concatenate([ones] * 3, 1), jnp.concatenate(split_three(value), 0), 1, 0)


def spread(per_head, lane):
    return jnp.concatenate(
        [
            jnp.where(lane < P_SIZE, per_head[:, 2 * k : 2 * k + 1], per_head[:, 2 * k + 1 : 2 * k + 2])
            for k in range(OWN_H // 2)
        ],
        1,
    )


def head_sums(value):
    column = lax.broadcasted_iota(jnp.int32, (OWN, N), 0)
    head = lax.broadcasted_iota(jnp.int32, (OWN, N), 1)
    members = ((column >= head * P_SIZE) & (column < (head + 1) * P_SIZE)).astype(F32).astype(BF16)
    high, low = split_two(value)
    return product(jnp.concatenate([high, low], 1), jnp.concatenate([members, members], 0), 1, 0)


def two_heads(pair, lane):
    zero = jnp.zeros_like(pair)
    return jnp.concatenate([jnp.where(lane < P_SIZE, pair, zero), jnp.where(lane < P_SIZE, zero, pair)], 0)


def chunk_facts(ends, chunk, dt_pre, par):
    column = lax.broadcasted_iota(jnp.int32, (CHUNK, 1), 0) + chunk * CHUNK
    row = lax.broadcasted_iota(jnp.int32, (1, CHUNK), 1) + chunk * CHUNK

    def segment(position):
        counted = jnp.zeros_like(position)
        for k in range(3):
            counted = counted + (position >= ends[k]).astype(jnp.int32)
        return jnp.where(position < 0, -1, counted)

    def one_segment(position):
        counted = jnp.int32(0)
        for k in range(3):
            counted = counted + (position >= ends[k]).astype(jnp.int32)
        return jnp.where(position < 0, -1, counted)

    here_column, here_row = segment(column), segment(row)
    prior = one_segment(chunk * CHUNK - 1)
    last = one_segment(chunk * CHUNK + CHUNK - 1)
    lane = lax.broadcasted_iota(jnp.int32, (CHUNK, N), 1)
    shifted = dt_pre + par[6:7, :N]
    soft = jnp.maximum(shifted, 0.0) + jnp.log1p(jnp.exp(-jnp.abs(shifted)))
    step = jnp.where(lane < OWN_H, soft, 0.0)
    decay = step * par[7:8, :N]
    tri_row = lax.broadcasted_iota(jnp.int32, (CHUNK, CHUNK), 0)
    tri_column = lax.broadcasted_iota(jnp.int32, (CHUNK, CHUNK), 1)
    lower = (tri_row >= tri_column).astype(F32).astype(BF16)
    upper = (tri_row <= tri_column).astype(F32).astype(BF16)
    total = ones_product(lower, decay)
    entering = (here_column == prior).astype(F32) * jnp.exp(total)
    end = total[CHUNK - 1 : CHUNK]
    leaving = (here_column == last).astype(F32) * jnp.exp(jnp.minimum(end - total, 0.0))
    passing = jnp.where(last == prior, 1.0, 0.0) * jnp.exp(end)
    return dict(
        column=column,
        segment=segment,
        here_column=here_column,
        here_row=here_row,
        lane=lane,
        shifted=shifted,
        step=step,
        decay=decay,
        total=total,
        entering=entering,
        leaving=leaving,
        passing=passing,
        tri_row=tri_row,
        tri_column=tri_column,
        upper=upper,
    )


def forward_kernel(part, ends, proj, par, *refs):
    if part:
        carry_in, refs = refs[3], refs[4:]
    pre_out, mixed_out, state_out, carry_out, extended, state = refs
    chunk = pl.program_id(0) + part * HALF

    @pl.when(pl.program_id(0) == 0)
    def _():
        if part:
            state[...] = carry_in[:N, :OWN]
            extended[0:8, :] = carry_in[N:, :]
        else:
            state[...] = jnp.zeros_like(state)
            extended[0:8, :] = jnp.zeros((8, 640), F32)

    facts = chunk_facts(ends, chunk, proj[:, 1024:1152], par)
    lane = facts["lane"]
    conv = proj[:, OWN:1024].astype(BF16).astype(F32)
    extended[8 : 8 + CHUNK, :] = conv
    pre = par[4:5] + par[3:4] * conv
    for back in range(1, CONV):
        same = (facts["segment"](facts["column"] - back) == facts["here_column"]).astype(F32)
        pre = pre + par[3 - back : 4 - back] * (extended[8 - back : 8 - back + CHUNK, :] * same)
    extended[0:8, :] = extended[CHUNK : CHUNK + 8, :]
    pre_out[...] = pre
    act = pre * jax.nn.sigmoid(pre)
    own_x, state_b, state_c = act[:, :OWN], act[:, OWN : OWN + N], act[:, OWN + N :]
    stepped = own_x * spread(facts["step"], lane)
    b_parts, c_parts = split_two(state_b), split_two(state_c)
    inside = (facts["tri_row"] >= facts["tri_column"]) & (facts["here_column"] == facts["here_row"])
    scores = jnp.where(inside, joined_product(c_parts, b_parts, 1, 1), 0.0)
    total_rows = facts["total"].T
    state_in = state[...]
    state_out[...] = state_in
    outs = []
    for pair in range(OWN_H // 2):
        mixing = []
        for head in (2 * pair, 2 * pair + 1):
            span = facts["total"][:, head : head + 1] - total_rows[head : head + 1, :]
            mixing.append(jnp.exp(jnp.minimum(span, 0.0)) * scores)
        inner = two_heads(stepped[:, pair * N : pair * N + N], lane)
        outs.append(precise_product(jnp.concatenate(mixing, 1), inner))
    scanned = jnp.concatenate(outs, 1) + spread(facts["entering"], lane) * joined_product(
        c_parts, split_two(state_in)
    )
    state[...] = spread(facts["passing"], lane[:1]) * state_in + precise_product(
        state_b.T, stepped * spread(facts["leaving"], lane)
    )
    mixed_out[...] = scanned + par[5:6, :OWN] * own_x

    @pl.when(pl.program_id(0) == HALF - 1)
    def _():
        carry_out[:N, :OWN] = state[...]
        carry_out[:N, OWN:] = jnp.zeros((N, 640 - OWN), F32)
        carry_out[N:, :] = extended[0:8, :]


def run_forward(part, ends, proj, par, before=()):
    here = lambda i: (i + part * HALF, 0)
    chunked = lambda width: pl.BlockSpec((CHUNK, width), here)
    fixed = lambda shape: pl.BlockSpec(shape, lambda i: (0, 0))
    carry = fixed((N + 8, 640))
    return pl.pallas_call(
        partial(forward_kernel, part),
        grid=(HALF,),
        in_specs=[pl.BlockSpec(memory_space=pltpu.SMEM), chunked(1152), fixed((16, 640))]
        + ([pl.BlockSpec(memory_space=pl.ANY)] * 3 + [carry] if part else []),
        out_specs=[chunked(640), chunked(OWN), pl.BlockSpec((N, OWN), here), carry],
        out_shape=[
            jax.ShapeDtypeStruct((PACK, 640), F32),
            jax.ShapeDtypeStruct((PACK, OWN), F32),
            jax.ShapeDtypeStruct((CHUNKS * N, OWN), F32),
            jax.ShapeDtypeStruct((N + 8, 640), F32),
        ],
        input_output_aliases={3: 0, 4: 1, 5: 2} if part else {},
        scratch_shapes=[pltpu.VMEM((CHUNK + 8, 640), F32), pltpu.VMEM((N, OWN), F32)],
        compiler_params=pltpu.CompilerParams(
            dimension_semantics=("arbitrary",), vmem_limit_bytes=VMEM_LIMIT
        ),
        cost_estimate=COST,
        name="scan_forward",
    )(ends, proj, par, *before)


def backward_kernel(ends, conv_in, dt_in, pre_in, mixed_in, grad_mixed, state_all, par, *refs):
    grad_x, grad_dt, grad_bc, sums, head_acc, carried, extended, end_dot = refs
    step_index = pl.program_id(0)
    chunk = CHUNKS - 1 - step_index

    @pl.when(step_index == 0)
    def _():
        carried[...] = jnp.zeros_like(carried)
        extended[CHUNK : CHUNK + 8, :] = jnp.zeros((8, OWN), F32)
        end_dot[...] = jnp.zeros_like(end_dot)
        sums[...] = jnp.zeros_like(sums)
        head_acc[...] = jnp.zeros_like(head_acc)

    facts = chunk_facts(ends, chunk, dt_in[...], par)
    lane = facts["lane"]
    pre = pre_in[...]
    sig = jax.nn.sigmoid(pre)
    act = pre * sig
    own_x, state_b, state_c = act[:, :OWN], act[:, OWN : OWN + N], act[:, OWN + N :]
    step = facts["step"]
    step_wide = spread(step, lane)
    stepped = own_x * step_wide
    skip = par[5:6, :OWN]
    scanned = mixed_in[...] - skip * own_x
    grad_m = grad_mixed[...]
    sums[6:7] += jnp.sum(grad_m * own_x, 0, keepdims=True)

    b_parts, c_parts = split_two(state_b), split_two(state_c)
    inside = (facts["tri_row"] <= facts["tri_column"]) & (facts["here_column"] == facts["here_row"])
    scores = jnp.where(inside, joined_product(b_parts, c_parts, 1, 1), 0.0)
    total_rows = facts["total"].T
    grad_scores = jnp.zeros((CHUNK, CHUNK), F32)
    grad_stepped = []
    for pair in range(OWN_H // 2):
        columns = slice(pair * N, pair * N + N)
        grad_pair = grad_m[:, columns]
        high, low = split_two(grad_pair)
        stepped_parts = split_two(two_heads(stepped[:, columns], lane))
        grad_mixing = joined_product(stepped_parts, (high, low), 1, 1)
        mixing = []
        for k in range(2):
            head = 2 * pair + k
            span = total_rows[head : head + 1, :] - facts["total"][:, head : head + 1]
            decays = jnp.exp(jnp.minimum(span, 0.0))
            mixing.append(decays * scores)
            grad_scores = grad_scores + decays * grad_mixing[k * CHUNK : (k + 1) * CHUNK]
        grad_stepped.append(
            joined_product(
                split_two(jnp.concatenate(mixing, 1)), (two_heads(high, lane), two_heads(low, lane))
            )
        )
    grad_scores = jnp.where(inside, grad_scores, 0.0)
    carry = carried[...]
    carry_parts = split_two(carry)
    leaving = spread(facts["leaving"], lane)
    grad_stepped = jnp.concatenate(grad_stepped, 1) + leaving * joined_product(b_parts, carry_parts)
    state_in = state_all[...]
    entered = spread(facts["entering"], lane) * grad_m
    entered_parts = split_two(entered)
    grad_b = precise_product(grad_scores, state_c) + joined_product(
        split_two(leaving * stepped), carry_parts, 1, 1
    )
    grad_c = precise_product(grad_scores.T, state_b) + joined_product(
        entered_parts, split_two(state_in), 1, 1
    )
    grad_bc[0:N, :] = grad_b.T
    grad_bc[N:, :] = grad_c.T
    new_carry = spread(facts["passing"], lane[:1]) * carry + joined_product(
        split_two(state_c.T), entered_parts
    )
    carried[...] = new_carry

    grad_step = head_sums(own_x * grad_stepped)
    last_row = lax.broadcasted_iota(jnp.int32, (CHUNK, N), 0) == CHUNK - 1
    grad_total = head_sums(grad_m * scanned) - step * grad_step
    grad_total = grad_total + jnp.where(last_row, end_dot[0:1, :], 0.0)
    grad_decay = ones_product(facts["upper"], grad_total)
    end_dot[...] = head_sums(
        jnp.broadcast_to(jnp.sum(new_carry * state_in, 0, keepdims=True), (8, OWN))
    )
    grad_pre_dt = (grad_step + grad_decay * par[7:8, :N]) * jax.nn.sigmoid(facts["shifted"])
    grad_pre_dt = jnp.where(lane < OWN_H, grad_pre_dt, 0.0)
    grad_dt[...] = grad_pre_dt.astype(BF16)
    head_acc[0:1] += jnp.sum(grad_pre_dt, 0, keepdims=True)
    head_acc[1:2] += jnp.sum(grad_decay * facts["decay"], 0, keepdims=True)

    sig_x, pre_x = sig[:, :OWN], pre[:, :OWN]
    grad_pre = (step_wide * grad_stepped + skip * grad_m) * (sig_x * (1.0 + pre_x * (1.0 - sig_x)))
    extended[0:CHUNK, :] = grad_pre
    conv = conv_in[...].astype(BF16).astype(F32)
    sums[5:6] += jnp.sum(grad_pre, 0, keepdims=True)
    sums[4:5] += jnp.sum(conv * grad_pre, 0, keepdims=True)
    grad_conv = par[3:4, :OWN] * grad_pre
    for ahead in range(1, CONV):
        same = (facts["segment"](facts["column"] + ahead) == facts["here_column"]).astype(F32)
        later = extended[ahead : ahead + CHUNK, :] * same
        sums[4 - ahead : 5 - ahead] += jnp.sum(conv * later, 0, keepdims=True)
        grad_conv = grad_conv + par[3 - ahead : 4 - ahead, :OWN] * later
    extended[CHUNK : CHUNK + 8, :] = extended[0:8, :]
    grad_x[...] = grad_conv.astype(BF16)


def run_backward(ends, proj, pre, mixed, grad_mixed, states, par):
    last = CHUNKS - 1
    chunked = lambda width, column=0: pl.BlockSpec((CHUNK, width), lambda i: (last - i, column))
    fixed = lambda shape: pl.BlockSpec(shape, lambda i: (0, 0))
    return pl.pallas_call(
        backward_kernel,
        grid=(CHUNKS,),
        in_specs=[
            pl.BlockSpec(memory_space=pltpu.SMEM),
            chunked(OWN, 1),
            chunked(N, 8),
            chunked(640),
            chunked(OWN),
            chunked(OWN),
            pl.BlockSpec((N, OWN), lambda i: (last - i, 0)),
            fixed((16, 640)),
        ],
        out_specs=[
            chunked(OWN),
            chunked(N),
            pl.BlockSpec((2 * N, CHUNK), lambda i: (0, last - i)),
            fixed((8, OWN)),
            fixed((8, N)),
        ],
        out_shape=[
            jax.ShapeDtypeStruct((PACK, OWN), BF16),
            jax.ShapeDtypeStruct((PACK, N), BF16),
            jax.ShapeDtypeStruct((2 * N, PACK), F32),
            jax.ShapeDtypeStruct((8, OWN), F32),
            jax.ShapeDtypeStruct((8, N), F32),
        ],
        scratch_shapes=[
            pltpu.VMEM((N, OWN), F32),
            pltpu.VMEM((CHUNK + 8, OWN), F32),
            pltpu.VMEM((8, N), F32),
        ],
        compiler_params=pltpu.CompilerParams(
            dimension_semantics=("arbitrary",), vmem_limit_bytes=VMEM_LIMIT
        ),
        cost_estimate=COST,
        name="scan_backward",
    )(ends, proj, proj, pre, mixed, grad_mixed, states, par)


PARTS = (1, 1, 1, 1, 1, 2, 1, 1)


def piece_copies(pieces, parts, blocks, sems):
    copies = []
    taken = 0
    for slot, count in enumerate(parts):
        rows = ROWS // count
        copies.append(
            [
                pltpu.make_async_copy(
                    pieces[taken + k], blocks.at[slot, pl.ds(k * rows, rows)], sems.at[taken + k]
                )
                for k in range(count)
            ]
        )
        taken += count
    return copies


def fetch_block(pieces, parts, blocks, sems):
    copies = piece_copies(pieces, parts, blocks, sems)
    step = pl.program_id(0)

    @pl.when(step == 0)
    def _():
        for group in copies:
            for copy in group:
                copy.start()

    for slot, group in enumerate(copies):

        @pl.when(step == slot)
        def _(group=group):
            for copy in group:
                copy.wait()

    return blocks[step]


def project_kernel(parts, table, *refs):
    pieces = refs[: sum(parts)]
    gain, shards, normed_out, proj, dt_out, blocks, weight, sems = refs[sum(parts) :]
    block = fetch_block(pieces, parts, blocks, sems)

    @pl.when(pl.program_id(0) == 0)
    def _():
        for f in range(N_FSDP):
            weight[f * SHARD_IN : (f + 1) * SHARD_IN, :] = shards[(f // 2) % 4, f % 2, f // 8, :SHARD_IN]
        dt_out[...] = weight[:, 1024:]

    values = block.astype(F32)
    scale = lax.rsqrt(jnp.mean(values * values, axis=1, keepdims=True) + NORM_EPS)
    normed = (values * scale * gain[...]).astype(BF16)
    normed_out[...] = normed
    proj[...] = matmul(normed, weight[...])


def run_project(table, pieces, gain, shards):
    fixed = lambda shape: pl.BlockSpec(shape, lambda i, table: (0,) * len(shape))
    placed = lambda width: pl.BlockSpec((ROWS, width), lambda i, table: (table[i], 0))
    return pl.pallas_call(
        partial(project_kernel, PARTS),
        grid_spec=pltpu.PrefetchScalarGridSpec(
            num_scalar_prefetch=1,
            grid=(N_REP,),
            in_specs=[pl.BlockSpec(memory_space=pl.ANY)] * len(pieces) + [fixed((1, D)), fixed(shards.shape)],
            out_specs=[placed(D), placed(3 * WIDE), fixed((D, N))],
            scratch_shapes=[
                pltpu.VMEM((N_REP, ROWS, D), BF16),
                pltpu.VMEM((D, 3 * WIDE), BF16),
                pltpu.SemaphoreType.DMA((len(pieces),)),
            ],
        ),
        out_shape=[
            jax.ShapeDtypeStruct((PACK, D), BF16),
            jax.ShapeDtypeStruct((PACK, 3 * WIDE), F32),
            jax.ShapeDtypeStruct((D, N), BF16),
        ],
        compiler_params=pltpu.CompilerParams(
            dimension_semantics=("arbitrary",), vmem_limit_bytes=VMEM_LIMIT
        ),
        cost_estimate=COST,
        name="project",
    )(table, *pieces, gain, shards)


def row_sums(value):
    folded = value[:, :N] + value[:, N : 2 * N] + value[:, 2 * N :]
    return jnp.sum(folded.T, 0, keepdims=True)


def out_grad_kernel(table, *refs):
    pieces = refs[: sum(PARTS)]
    w_out, mixed, gate_in, gain, branch_out, grad_out, sums, blocks, turned, sems = refs[sum(PARTS) :]
    branch = fetch_block(pieces, PARTS, blocks, sems)

    @pl.when(pl.program_id(0) == 0)
    def _():
        turned[...] = w_out[...].reshape(OWN, D).T

    branch_out[...] = branch
    total = matmul(branch, turned[...])
    grad_out[...] = total
    gate = gate_in[...]
    gated = mixed[...] * (gate * jax.nn.sigmoid(gate))
    row = lax.broadcasted_iota(jnp.int32, (8, ROWS), 0)
    sums[...] = jnp.where(
        row == 0, row_sums(gated * gated), jnp.where(row == 1, row_sums(total * gain[...] * gated), 0.0)
    )


def run_out_grad(table, pieces, w_out, mixed, proj, gain):
    fixed = lambda shape: pl.BlockSpec(shape, lambda i, table: (0, 0))
    placed = lambda width: pl.BlockSpec((ROWS, width), lambda i, table: (table[i], 0))
    own = pl.BlockSpec(
        (1, 2, 1, SHARD_OUT, D), lambda i, table: (table[N_REP] % 4, 0, table[N_REP] // 4, 0, 0)
    )
    return pl.pallas_call(
        out_grad_kernel,
        grid_spec=pltpu.PrefetchScalarGridSpec(
            num_scalar_prefetch=1,
            grid=(N_REP,),
            in_specs=[pl.BlockSpec(memory_space=pl.ANY)] * len(pieces)
            + [own, placed(OWN), placed(OWN), fixed((1, OWN))],
            out_specs=[placed(D), placed(OWN), pl.BlockSpec((8, ROWS), lambda i, table: (0, table[i]))],
            scratch_shapes=[
                pltpu.VMEM((N_REP, ROWS, D), BF16),
                pltpu.VMEM((D, WIDE), BF16),
                pltpu.SemaphoreType.DMA((len(pieces),)),
            ],
        ),
        out_shape=[
            jax.ShapeDtypeStruct((PACK, D), BF16),
            jax.ShapeDtypeStruct((PACK, OWN), F32),
            jax.ShapeDtypeStruct((8, PACK), F32),
        ],
        compiler_params=pltpu.CompilerParams(
            dimension_semantics=("arbitrary",), vmem_limit_bytes=VMEM_LIMIT
        ),
        cost_estimate=COST,
        name="out_grad",
    )(table, *pieces, w_out, mixed, proj, gain)


def gate_kernel(grad_out, mixed_in, gate_in, sums, gain, low_out, grad_mixed, grad_gain):
    rows = grad_out.shape[0]
    mixed, gate, grad_o = mixed_in[...], gate_in[...], grad_out[...]
    stats = jnp.concatenate([sums[...], jnp.zeros((N - 8, rows), F32)], 0).T
    out_scale = lax.rsqrt(stats[:, 0:1] * (1.0 / DI) + NORM_EPS)
    pull = out_scale * out_scale * out_scale * (stats[:, 1:2] * (1.0 / DI))
    gate_sig = jax.nn.sigmoid(gate)
    silu = gate * gate_sig
    gated = mixed * silu
    unit = gated * out_scale
    grad_gated = out_scale * (grad_o * gain[...]) - gated * pull
    grad_mixed[...] = grad_gated * silu
    low_out[:, :OWN] = (unit * gain[...]).astype(BF16)
    low_out[:, OWN:] = (grad_gated * mixed * (gate_sig * (1.0 + gate * (1.0 - gate_sig)))).astype(BF16)
    gain_part = jnp.sum(grad_o * unit, 0, keepdims=True)

    @pl.when(pl.program_id(0) == 0)
    def _():
        grad_gain[...] = jnp.broadcast_to(gain_part, grad_gain.shape)

    @pl.when(pl.program_id(0) > 0)
    def _():
        grad_gain[...] += gain_part


def run_gate(grad_out, mixed, proj, sums, gain):
    rows = lambda width: pl.BlockSpec((ROWS, width), lambda i: (i, 0))
    fixed = lambda shape: pl.BlockSpec(shape, lambda i: (0, 0))
    return pl.pallas_call(
        gate_kernel,
        grid=(PACK // ROWS,),
        in_specs=[
            rows(OWN),
            rows(OWN),
            rows(OWN),
            pl.BlockSpec((8, ROWS), lambda i: (0, i)),
            fixed((1, OWN)),
        ],
        out_specs=[rows(2 * OWN), rows(OWN), fixed((8, OWN))],
        out_shape=[
            jax.ShapeDtypeStruct((PACK, 2 * OWN), BF16),
            jax.ShapeDtypeStruct((PACK, OWN), F32),
            jax.ShapeDtypeStruct((8, OWN), F32),
        ],
        compiler_params=pltpu.CompilerParams(
            dimension_semantics=("arbitrary",), vmem_limit_bytes=VMEM_LIMIT
        ),
        cost_estimate=COST,
        name="gate_backward",
    )(grad_out, mixed, proj, sums, gain)


def early_grad_kernel(low, grad_branch, normed, out):
    step = pl.program_id(0)

    @pl.when(step == 0)
    def _():
        out[...] = jnp.zeros_like(out)

    for k in range(4):
        part = product(low[:, :OWN], grad_branch[:, k * WIDE : (k + 1) * WIDE], 0, 0)
        for m in range(4):
            out[eight_order(4 * k + m), :SHARD_IN] += part[m * SHARD_IN : (m + 1) * SHARD_IN]
    part = product(normed[...], low[:, OWN:], 0, 0)
    for f in range(N_FSDP):
        out[eight_order(f), SHARD_IN:] += part[f * SHARD_IN : (f + 1) * SHARD_IN]


def run_early_grad(low, grad_branch, normed):
    count = 2 * ROWS
    rows = lambda width: pl.BlockSpec((count, width), lambda i: (i, 0))
    shape = (N_FSDP, 2 * SHARD_IN, WIDE)
    return pl.pallas_call(
        early_grad_kernel,
        grid=(PACK // count,),
        in_specs=[rows(2 * OWN), rows(D), rows(D)],
        out_specs=pl.BlockSpec(shape, lambda i: (0, 0, 0)),
        out_shape=jax.ShapeDtypeStruct(shape, F32),
        compiler_params=pltpu.CompilerParams(
            dimension_semantics=("arbitrary",), vmem_limit_bytes=VMEM_LIMIT
        ),
        cost_estimate=COST,
        name="early_grad",
    )(low, grad_branch, normed)


def block_out_kernel(rows, weight, tokens, live, out):
    step = pl.program_id(0)
    part = matmul(jnp.concatenate([rows[0], rows[1]], 1), weight[...].reshape(2 * OWN, D))

    @pl.when(step == 0)
    def _():
        out[...] = part

    @pl.when(step > 0)
    def _():
        out[...] += part

    @pl.when(step == N_REP // 2 - 1)
    def _():
        out[...] = tokens[...].astype(F32) + live[...] * out[...]


def run_block_out(rows, weight, tokens, live):
    fixed = lambda shape: pl.BlockSpec(shape, lambda i: (0, 0))
    return pl.pallas_call(
        block_out_kernel,
        grid=(N_REP // 2,),
        in_specs=[
            pl.BlockSpec((2, ROWS, OWN), lambda i: (i, 0, 0)),
            pl.BlockSpec((2, 2, 1, SHARD_OUT, D), lambda i: (i % 2, 0, i // 2, 0, 0)),
            fixed((ROWS, D)),
            fixed((ROWS, 1)),
        ],
        out_specs=fixed((ROWS, D)),
        out_shape=jax.ShapeDtypeStruct((ROWS, D), F32),
        compiler_params=pltpu.CompilerParams(
            dimension_semantics=("arbitrary",), vmem_limit_bytes=VMEM_LIMIT
        ),
        cost_estimate=FILL,
        name="block_out",
    )(rows, weight, tokens, live)


def turned_part(weight, rows):
    return product(weight[...].reshape(D, weight.shape[-1]), rows, 1, 1)


def columns_of(full_in, width, index):
    return pl.BlockSpec(full_in.shape[:-1] + (width,), lambda i: (0, 0, 0, 0, index(i)))


def z_grad_kernel(rows, weight, out):
    part = turned_part(weight, jnp.concatenate([rows[0], rows[1]], 1))

    @pl.when(pl.program_id(0) == 0)
    def _():
        out[...] = part

    @pl.when(pl.program_id(0) > 0)
    def _():
        out[...] += part


def run_z_grad(rows, full_in):
    return pl.pallas_call(
        z_grad_kernel,
        grid=(N_REP // 2,),
        in_specs=[
            pl.BlockSpec((2, ROWS, OWN), lambda i: (i, 0, 1)),
            columns_of(full_in, 2 * OWN, lambda i: i),
        ],
        out_specs=pl.BlockSpec((D, ROWS), lambda i: (0, 0)),
        out_shape=jax.ShapeDtypeStruct((D, ROWS), F32),
        compiler_params=pltpu.CompilerParams(
            dimension_semantics=("arbitrary",), vmem_limit_bytes=VMEM_LIMIT
        ),
        cost_estimate=COST,
        name="z_grad",
    )(rows, full_in)


def input_grad_kernel(
    own_half, grad_z, x_rows, rest_rows, w_x, w_bc, low_dt, tokens, cotangent, gain, out, gain_out, total, ordered
):
    step = pl.program_id(0)
    part = turned_part(w_x, jnp.concatenate([x_rows[0], x_rows[1]], 1))

    @pl.when(step == 0)
    def _():
        total[...] = grad_z[...] + part

    @pl.when(step > 0)
    def _():
        total[...] += part

    @pl.when(step == N_REP // 2 - 1)
    def _():
        lane = lax.broadcasted_iota(jnp.int32, (ROWS, N), 1)
        groups = []
        for k in range(2):
            group = jnp.zeros((ROWS, N), F32)
            for m in range(4):
                value = rest_rows[4 * k + m].astype(F32)
                value = value if m == 0 else pltpu.roll(value, m * OWN_BC, 1)
                group = jnp.where((lane >= m * OWN_BC) & (lane < (m + 1) * OWN_BC), value, group)
            groups.append(group.astype(BF16))
        steps = jnp.zeros((ROWS, N), F32)
        for m in range(N_REP):
            start = 8 + m * OWN_H
            value = pltpu.roll(rest_rows[m].astype(F32), (start - OWN_BC) % N, 1)
            steps = jnp.where((lane >= start) & (lane < start + OWN_H), value, steps)
        total[...] += turned_part(w_bc, jnp.concatenate(groups, 1))
        for f in range(N_FSDP):
            place = eight_order(f) - f // 8 + (f // 8 + own_half[0]) % 2
            start = pl.multiple_of(place * SHARD_IN, SHARD_IN)
            ordered[f * SHARD_IN : (f + 1) * SHARD_IN, :] = total[pl.ds(start, SHARD_IN), :]
        grad_h = (ordered[...] + product(low_dt[...], steps.astype(BF16), 1, 1)).T
        values = tokens[...].astype(F32)
        scale = lax.rsqrt(jnp.mean(values * values, axis=1, keepdims=True) + NORM_EPS)
        unit = values * scale
        gain_sum = jnp.sum(grad_h * unit, 0, keepdims=True)
        gain_out[...] = jnp.zeros_like(gain_out)
        for k in range(D // TAIL):
            gain_out[k : k + 1, :] = gain_sum[:, k * TAIL : (k + 1) * TAIL]
        grad_unit = grad_h * gain[...]
        inner = jnp.mean(grad_unit * unit, axis=1, keepdims=True)
        out[...] = cotangent[...].astype(F32) + scale * (grad_unit - unit * inner)


def run_input_grad(own_half, grad_z, tail_rows, full_in, low_dt, tokens, cotangent, gain):
    fixed = lambda shape: pl.BlockSpec(shape, lambda i: (0,) * len(shape))
    return pl.pallas_call(
        input_grad_kernel,
        grid=(N_REP // 2,),
        in_specs=[
            pl.BlockSpec(memory_space=pltpu.SMEM),
            fixed((D, ROWS)),
            pl.BlockSpec((2, ROWS, OWN), lambda i: (i, 0, 0)),
            pl.BlockSpec((N_REP, ROWS, N), lambda i: (0, 0, OWN // N)),
            columns_of(full_in, 2 * OWN, lambda i: N_REP // 2 + i),
            columns_of(full_in, 2 * N, lambda i: DI // N),
            fixed((D, N)),
            fixed((ROWS, D)),
            fixed((ROWS, D)),
            fixed((1, D)),
        ],
        out_specs=[fixed((ROWS, D)), fixed((8, TAIL))],
        out_shape=[jax.ShapeDtypeStruct((ROWS, D), F32), jax.ShapeDtypeStruct((8, TAIL), F32)],
        scratch_shapes=[pltpu.VMEM((D, ROWS), F32), pltpu.VMEM((D, ROWS), F32)],
        compiler_params=pltpu.CompilerParams(
            dimension_semantics=("arbitrary",), vmem_limit_bytes=VMEM_LIMIT
        ),
        cost_estimate=COST,
        name="input_grad",
    )(own_half, grad_z, tail_rows, tail_rows, full_in, full_in, low_dt, tokens, cotangent, gain)


def rest_kernel(
    ends, parts, pre_b, pre_c, conv_in, par, grad_x, grad_dt, sums, head_acc, grad_gain, first, tail_out, small_out
):
    own = lax.broadcasted_iota(jnp.int32, (OWN_BC, 2 * N), 0) + first[0]
    chosen = (lax.broadcasted_iota(jnp.int32, (OWN_BC, 2 * N), 1) == own).astype(F32).astype(BF16)

    def pick(value):
        return product(jnp.concatenate([chosen] * 3, 1), jnp.concatenate(split_three(value), 1), 1, 1)

    grad = parts[0]
    for k in range(1, N_REP):
        grad = grad + parts[k]
    own_pre = pick(jnp.concatenate([pre_b[...], pre_c[...]], 1))
    own_conv = product(chosen, conv_in[...].astype(BF16), 1, 1)
    taps = pick(par[:, OWN:])
    sig = jax.nn.sigmoid(own_pre)
    grad_pre = grad * (sig * (1.0 + own_pre * (1.0 - sig)))
    position = lax.broadcasted_iota(jnp.int32, (1, PACK), 1)

    def segment(places):
        counted = jnp.zeros_like(places)
        for k in range(3):
            counted = counted + (places >= ends[k]).astype(jnp.int32)
        return counted

    grad_conv = taps[:, CONV - 1 : CONV] * grad_pre
    column = lax.broadcasted_iota(jnp.int32, (OWN_BC, N), 1)
    found = jnp.where(column == CONV, jnp.sum(grad_pre, 1, keepdims=True), 0.0)
    found = jnp.where(column == CONV - 1, jnp.sum(own_conv * grad_pre, 1, keepdims=True), found)
    for later_by in range(1, CONV):
        same = (segment(position + later_by) == segment(position)) & (position < PACK - later_by)
        later = jnp.where(same, pltpu.roll(grad_pre, PACK - later_by, 1), 0.0)
        tap = CONV - 1 - later_by
        found = jnp.where(column == tap, jnp.sum(own_conv * later, 1, keepdims=True), found)
        grad_conv = grad_conv + taps[:, tap : tap + 1] * later
    lane = lax.broadcasted_iota(jnp.int32, (N, N), 1)
    filler = jnp.zeros((N - OWN_BC, N), F32)
    for k in range(PACK // N):
        rows = slice(k * N, (k + 1) * N)
        columns = jnp.concatenate([grad_conv[:, rows], filler], 0).T
        steps = pltpu.roll(grad_dt[rows, :].astype(F32), OWN_BC, 1)
        tail_out[rows, :OWN] = grad_x[rows, :]
        tail_out[rows, OWN:] = jnp.where(
            lane < OWN_BC, columns, jnp.where(lane < OWN_BC + OWN_H, steps, 0.0)
        ).astype(BF16)
    row = lax.broadcasted_iota(jnp.int32, (8, OWN), 0)
    skip = head_sums(sums[...])
    by_head = jnp.concatenate([skip, jnp.zeros((8, OWN - N), F32)], 1)
    logs = jnp.concatenate([head_acc[...], jnp.zeros((8, OWN - N), F32)], 1)
    wide = jnp.where(row == 0, grad_gain[0:1, :], jnp.where(row < 6, sums[...], 0.0))
    wide = jnp.where(row == 6, logs[1:2, :], jnp.where(row == 7, by_head[6:7, :], wide))
    turned = jnp.concatenate([found, filler], 0).T
    first_row = lax.broadcasted_iota(jnp.int32, (8, N), 0) == 0
    small_out[:, :OWN] = wide
    small_out[:, OWN:] = jnp.where(first_row, head_acc[0:1, :], pltpu.roll(turned[:8], 1, 0))


def run_rest(ends, parts, pre, proj, par, grad_x, grad_dt, sums, head_acc, grad_gain, first):
    fixed = lambda shape: pl.BlockSpec(shape, lambda i: (0,) * len(shape))
    return pl.pallas_call(
        rest_kernel,
        grid=(1,),
        in_specs=[
            pl.BlockSpec(memory_space=pltpu.SMEM),
            fixed((N_REP, OWN_BC, PACK)),
            pl.BlockSpec((PACK, N), lambda i: (0, 3)),
            pl.BlockSpec((PACK, N), lambda i: (0, 4)),
            pl.BlockSpec((PACK, 2 * N), lambda i: (0, 3)),
            fixed((16, 640)),
            fixed((PACK, OWN)),
            fixed((PACK, N)),
            fixed((8, OWN)),
            fixed((8, N)),
            fixed((8, OWN)),
            pl.BlockSpec(memory_space=pltpu.SMEM),
        ],
        out_specs=[fixed((PACK, TAIL)), fixed((8, TAIL))],
        out_shape=[jax.ShapeDtypeStruct((PACK, TAIL), BF16), jax.ShapeDtypeStruct((8, TAIL), F32)],
        compiler_params=pltpu.CompilerParams(
            dimension_semantics=("arbitrary",), vmem_limit_bytes=VMEM_LIMIT
        ),
        cost_estimate=COST,
        name="rest_backward",
    )(ends, parts, pre, pre, proj, par, grad_x, grad_dt, sums, head_acc, grad_gain, first)


def tail_grad_kernel(normed, tail, small, out):
    step = pl.program_id(0)
    part = product(normed[...], tail[...], 0, 0)
    for f in range(N_FSDP):
        rows = part[f * SHARD_IN : (f + 1) * SHARD_IN]

        @pl.when(step == 0)
        def _(f=f, rows=rows):
            out[eight_order(f), :SHARD_IN] = rows
            out[eight_order(f), SHARD_IN:] = small[...]

        @pl.when(step > 0)
        def _(f=f, rows=rows):
            out[eight_order(f), :SHARD_IN] += rows


def run_tail_grad(normed, tail, small):
    count = 2 * ROWS
    shape = (N_FSDP, SHARD_IN + 8, TAIL)
    return pl.pallas_call(
        tail_grad_kernel,
        grid=(PACK // count,),
        in_specs=[
            pl.BlockSpec((count, D), lambda i: (i, 0)),
            pl.BlockSpec((count, TAIL), lambda i: (i, 0)),
            pl.BlockSpec((8, TAIL), lambda i: (0, 0)),
        ],
        out_specs=pl.BlockSpec(shape, lambda i: (0, 0, 0)),
        out_shape=jax.ShapeDtypeStruct(shape, F32),
        compiler_params=pltpu.CompilerParams(
            dimension_semantics=("arbitrary",), vmem_limit_bytes=VMEM_LIMIT
        ),
        cost_estimate=COST,
        name="tail_grad",
    )(normed, tail, small)


def adam_step(grad, weight, first, second, grad_out, first_out, second_out, weight_out):
    new_weight, new_first, new_second = adam_update(
        weight[...], grad, first[...], second[...], RATE_MATRIX, WEIGHT_DECAY
    )
    grad_out[...] = grad
    first_out[...] = new_first
    second_out[...] = new_second
    weight_out[...] = new_weight


def adam_early_kernel(rows, pair, *refs):
    arrays, grad = refs[:-1], refs[-1]
    grad[:, :WIDE] = pair[0, rows, :]
    grad[:, WIDE:] = pair[1, rows, :]
    adam_step(grad[...], *arrays)


def run_adam_early(place_of, rows, parts, weight, first, second):
    part = pl.BlockSpec((SHARD_IN, 2 * WIDE), place_of)
    shape = jax.ShapeDtypeStruct(weight.shape, F32)
    return pl.pallas_call(
        partial(adam_early_kernel, rows),
        grid=(N_REP // 2,),
        in_specs=[pl.BlockSpec((2,) + parts.shape[1:], lambda i: (i, 0, 0))] + [part] * 3,
        out_specs=[part] * 4,
        out_shape=[shape] * 4,
        scratch_shapes=[pltpu.VMEM((SHARD_IN, 2 * WIDE), F32)],
        compiler_params=pltpu.CompilerParams(
            dimension_semantics=("arbitrary",), vmem_limit_bytes=VMEM_LIMIT
        ),
        cost_estimate=FILL,
        name="adam",
    )(parts, weight, first, second)


def adam_tail_kernel(pair, rest, *refs):
    arrays, grad = refs[:3] + refs[-5:-1], refs[-1]
    step = pl.program_id(0)

    @pl.when(step < N_REP // 2)
    def _():
        grad[:, :WIDE] = pair[0, :SHARD_IN]
        grad[:, WIDE:] = pair[1, :SHARD_IN]

    @pl.when(step == N_REP // 2)
    def _():
        lane = lax.broadcasted_iota(jnp.int32, (SHARD_IN, N), 1)
        for k in range(2):
            group = jnp.zeros((SHARD_IN, N), F32)
            for m in range(4):
                value = rest[4 * k + m, :SHARD_IN]
                value = value if m == 0 else pltpu.roll(value, m * OWN_BC, 1)
                group = jnp.where((lane >= m * OWN_BC) & (lane < (m + 1) * OWN_BC), value, group)
            grad[:, k * N : (k + 1) * N] = group

    adam_step(grad[...], *arrays)


def run_adam_tail(parts, weight, first, second, before):
    half = N_REP // 2
    rows = parts.shape[1]
    column = pl.BlockSpec((SHARD_IN, 2 * WIDE), lambda i: (0, half + i))
    shape = jax.ShapeDtypeStruct(weight.shape, F32)
    return pl.pallas_call(
        adam_tail_kernel,
        grid=(half + 1,),
        in_specs=[
            pl.BlockSpec((2, rows, OWN), lambda i: (jnp.minimum(i, half - 1), 0, 0)),
            pl.BlockSpec((N_REP, rows, N), lambda i: (0, 0, OWN // N)),
        ]
        + [column] * 3
        + [pl.BlockSpec(memory_space=pl.ANY)] * 4,
        out_specs=[column] * 4,
        out_shape=[shape] * 4,
        input_output_aliases={5 + k: k for k in range(4)},
        scratch_shapes=[pltpu.VMEM((SHARD_IN, 2 * WIDE), F32)],
        compiler_params=pltpu.CompilerParams(
            dimension_semantics=("arbitrary",), vmem_limit_bytes=VMEM_LIMIT
        ),
        cost_estimate=COST,
        name="adam_tail",
    )(parts, parts, weight, first, second, *before)


def body(
    tokens,
    cotangent,
    lengths,
    w_in,
    w_dt,
    w_out,
    small,
    first_in,
    first_dt,
    first_out,
    first_small,
    second_in,
    second_dt,
    second_out,
    second_small,
):
    place = Place()
    r = place.r
    zero = jnp.int32(0)
    pack_lengths = lax.dynamic_slice_in_dim(lengths, place.f, 1, 0)[0]
    seg_ends = jnp.cumsum(pack_lengths)
    own_positions = r * ROWS + jnp.arange(ROWS, dtype=jnp.int32)
    own_live = (segment_at(own_positions, seg_ends) < 3).astype(F32)[:, None]
    slots = jnp.arange(N_REP, dtype=jnp.int32)
    ahead = ((place.x + slots // 2) % 4) * 2 + (place.yl + slots) % 2
    half = ROWS // 2

    in_low = w_in.astype(BF16)
    dt_low = w_dt.astype(BF16)
    out_low = w_out.astype(BF16)

    small_rows = jnp.pad(small.astype(BF16), (0, 16 * 3 * WIDE - SHARD_SMALL)).reshape(16, 3 * WIDE)

    def own_columns(rep):
        columns = jnp.concatenate(
            [
                lax.dynamic_slice_in_dim(in_low, rep * OWN, OWN, 1),
                lax.dynamic_slice_in_dim(in_low, DI + rep * OWN, OWN, 1),
                in_low[:, 2 * DI :],
                lax.dynamic_slice_in_dim(dt_low, rep * OWN_H, OWN_H, 1),
                jnp.zeros((SHARD_IN, 2), BF16),
                dt_low,
                jnp.zeros((SHARD_IN, N - 8 - H), BF16),
            ],
            1,
        )
        return jnp.concatenate([columns, small_rows], 0)

    other_columns = move(
        own_columns(2 * place.x + 1 - place.yl), lambda yh, z, c, x, yl: (yh + 1, z, c, x, yl + 1)
    )
    from_left = move(tokens, along_x(1))
    from_right = move(tokens, along_x(-1))
    partner = move(tokens, swap_y)

    out_low, other_columns = lax.optimization_barrier((out_low, other_columns))
    out_other = move(out_low, lambda yh, z, c, x, yl: (yh + 1, z, c, x, yl + 1))
    branch = (cotangent.astype(F32) * own_live).astype(BF16)
    from_left, from_right, partner, other_columns, branch = lax.optimization_barrier(
        (from_left, from_right, partner, other_columns, branch)
    )
    own_shards = gather_eight(both(own_columns(r), other_columns, place.yh))
    far = move(from_left, along_x(1))
    partner_left = move(from_left, swap_y)
    partner_right = move(partner, along_x(-1))

    far, partner_left, partner_right, out_other, branch, in_low = lax.optimization_barrier(
        (far, partner_left, partner_right, out_other, branch, in_low)
    )
    in_other = move(in_low, lambda yh, z, c, x, yl: (yh + 1, z, c, x, yl + 1))
    out_pair = both(out_low, out_other, place.yh)
    partner_far_top = move(partner_left[:half], along_x(1))
    partner_far_low = move(partner_right[half:], along_x(-1))

    vector = own_shards[:, :, :, SHARD_IN : SHARD_IN + 2].transpose(2, 0, 1, 3, 4)
    vector = vector.reshape(N_FSDP, 6 * WIDE)[:, :SHARD_SMALL].reshape(-1).astype(F32)
    offset = 0
    gain_in = vector[None, :D]
    offset = D
    gain_row = lax.dynamic_slice_in_dim(vector, offset + r * OWN, OWN, 0)[None, :]
    offset += DI
    taps = vector[offset : offset + (CONV + 1) * CHANNELS].reshape(CONV + 1, CHANNELS)
    offset += (CONV + 1) * CHANNELS
    per_head = vector[offset:].reshape(3, H)
    dt_bias, a_log, d_skip = lax.dynamic_slice_in_dim(per_head, r * OWN_H, OWN_H, 1)
    taps_bc = taps[:, DI:]
    conv_par = jnp.concatenate([lax.dynamic_slice_in_dim(taps, r * OWN, OWN, 1), taps_bc], 1)
    head_par = jnp.stack(
        [
            jnp.pad(jnp.broadcast_to(d_skip[:, None], (OWN_H, P_SIZE)).reshape(-1), (0, 2 * N)),
            jnp.pad(dt_bias, (0, 640 - OWN_H)),
            jnp.pad(-jnp.exp(a_log), (0, 640 - OWN_H)),
        ],
        0,
    )
    par = jnp.concatenate([conv_par, head_par, jnp.zeros((8, 640), F32)], 0)

    partner_far_top, partner_far_low, own_shards = lax.optimization_barrier(
        (partner_far_top, partner_far_low, own_shards)
    )
    full_out = gather_eight(tie(out_pair, own_shards))
    b_left = move(branch, along_x(1))
    b_right = move(branch, along_x(-1))
    b_partner = move(branch, swap_y)
    token_pieces = [
        tokens, partner, from_right, partner_right, far,
        partner_far_top, partner_far_low, from_left, partner_left,
    ]
    normed, proj, low_dt = run_project(ahead, token_pieces, gain_in, own_shards)
    b_left, b_right, b_partner, proj = lax.optimization_barrier((b_left, b_right, b_partner, proj))
    b_far = move(b_left, along_x(1))
    b_partner_left = move(b_left, swap_y)
    b_partner_right = move(b_partner, along_x(-1))
    before = run_forward(0, seg_ends, proj, par)
    b_far, b_partner_left, b_partner_right, before = lax.optimization_barrier(
        (b_far, b_partner_left, b_partner_right, before)
    )
    b_partner_far_top = move(b_partner_left[:half], along_x(1))
    b_partner_far_low = move(b_partner_right[half:], along_x(-1))
    pre, mixed, states, _ = run_forward(1, seg_ends, proj, par, before)
    mixed, in_low, in_other, b_partner_far_top, b_partner_far_low = lax.optimization_barrier(
        (mixed, in_low, in_other, b_partner_far_top, b_partner_far_low)
    )
    full_in = gather_eight(jnp.stack([in_low, in_other], 0))
    branch_pieces = [
        branch, b_partner, b_right, b_partner_right, b_far,
        b_partner_far_top, b_partner_far_low, b_left, b_partner_left,
    ]
    rep_table = jnp.concatenate([ahead, r[None]])
    grad_branch, grad_normed_out, sums = run_out_grad(rep_table, branch_pieces, full_out, mixed, proj, gain_row)
    sums = share_rep(sums[:2].reshape(32, 128)).sum(0).reshape(2, PACK)
    sums = jnp.concatenate([sums, jnp.zeros((6, PACK), F32)], 0)

    low, grad_mixed, grad_gain = run_gate(grad_normed_out, mixed, proj, sums, gain_row)

    low_rows = exchange(low.reshape(N_REP, ROWS, 2 * OWN), "rep")
    grad_x, grad_dtraw, grad_bc, grad_sums, grad_heads = run_backward(
        seg_ends, proj, pre, mixed, grad_mixed, states, par
    )
    low_rows, low, grad_bc, grad_x = lax.optimization_barrier((low_rows, low, grad_bc, grad_x))

    grad_bc = exchange(grad_bc, "rep").reshape(N_REP, OWN_BC, PACK)
    early_grad = run_early_grad(low, grad_branch, normed)
    early = scatter_eight(early_grad)
    early_grad, low_rows = lax.optimization_barrier((early_grad, low_rows))
    grad_rows = run_z_grad(low_rows, full_in)
    grad_bc, grad_rows, early_grad = lax.optimization_barrier((grad_bc, grad_rows, early_grad))

    tail, small_own = run_rest(
        seg_ends, grad_bc, pre, proj, par, grad_x, grad_dtraw, grad_sums, grad_heads, grad_gain, (r * OWN_BC)[None]
    )
    grad_tail = run_tail_grad(normed, tail, small_own)
    tail, grad_tail, low_rows = lax.optimization_barrier((tail, grad_tail, low_rows))
    tail_rows = exchange(tail.reshape(N_REP, ROWS, TAIL), "rep")
    early, grad_tail = lax.optimization_barrier((early, grad_tail))
    tail_part = scatter_eight(grad_tail)
    mine, other = at(early, place.yh), at(early, 1 - place.yh)
    out_mine = move(
        mine[:SHARD_IN], lambda yh, z, c, x, yl: (x // 2, (x % 2) * 2 + yl, z % 2, 2 * c + yh, z // 2)
    )
    out_other = move(
        other[:SHARD_IN], lambda yh, z, c, x, yl: (x // 2, (x % 2) * 2 + yl, z % 2, 2 * c + 1 - yh, z // 2)
    )
    z_other = move(other[SHARD_IN:], swap_y_hi)
    tail_rows, out_mine, out_other, z_other = lax.optimization_barrier((tail_rows, out_mine, out_other, z_other))

    early_parts = share_rep(jnp.concatenate([out_mine + out_other, mine[SHARD_IN:] + z_other], 0))
    input_grad, grad_gain_in = run_input_grad(
        place.yh[None], grad_rows, tail_rows, full_in, low_dt, tokens, cotangent, gain_in
    )
    tail_part, grad_gain_in = lax.optimization_barrier((tail_part, grad_gain_in))

    tail_other = move(at(tail_part, 1 - place.yh), swap_y_hi)
    grad_gain_in = sum_z(grad_gain_in + move(grad_gain_in, swap_core))
    tail_part = at(tail_part, place.yh) + tail_other
    grad_gain_in = grad_gain_in + move(grad_gain_in, swap_y_hi)
    tail_part = jnp.concatenate([tail_part, grad_gain_in], 0)

    tail_part, early_parts, low_rows = lax.optimization_barrier((tail_part, early_parts, low_rows))
    tail_parts = share_rep(tail_part)
    block_out = run_block_out(low_rows, full_out, tokens, own_live)

    grad_out, new_first_out, new_second_out, new_out = run_adam_early(
        lambda i: (i // 2, i % 2), slice(0, SHARD_IN), early_parts, w_out, first_out, second_out
    )
    updated = run_adam_early(
        lambda i: (0, i), slice(SHARD_IN, 2 * SHARD_IN), early_parts, w_in, first_in, second_in
    )
    grad_in, new_first_in, new_second_in, new_in = run_adam_tail(tail_parts, w_in, first_in, second_in, updated)

    def columns(parts):
        return parts.transpose(1, 0, 2).reshape(parts.shape[1], -1)

    small_parts = tail_parts[:, SHARD_IN : SHARD_IN + 8]
    grad_gain_in = tail_parts[:, SHARD_IN + 8 : SHARD_IN + 8 + D // TAIL].sum(0).reshape(-1)
    small_x = small_parts[:, :, :OWN].transpose(1, 0, 2).reshape(8, DI)
    small_bc = small_parts[:, :, OWN:].transpose(1, 0, 2)

    def channels(row):
        return jnp.concatenate([small_x[row], small_bc[row, :, :OWN_BC].reshape(-1)])

    grad_small_all = jnp.concatenate(
        [grad_gain_in, small_x[0]]
        + [channels(row) for row in range(1, 6)]
        + [
            small_bc[0, :, :OWN_H].reshape(-1),
            small_parts[:, 6, :OWN_H].reshape(-1),
            small_parts[:, 7, :OWN_H].reshape(-1),
        ]
    )
    grad_small = lax.dynamic_slice_in_dim(grad_small_all, place.f * SHARD_SMALL, SHARD_SMALL, 0)
    grad_dt = columns(tail_parts[:, :SHARD_IN, OWN + OWN_BC : OWN + OWN_BC + OWN_H])
    new_dt, new_first_dt, new_second_dt = adam_update(
        w_dt, grad_dt, first_dt, second_dt, RATE_MATRIX, WEIGHT_DECAY
    )
    new_small, new_first_small, new_second_small = adam_update(
        small, grad_small, first_small, second_small, RATE_SMALL, 0.0
    )
    return (
        block_out,
        input_grad,
        grad_in,
        grad_dt,
        grad_out,
        grad_small,
        new_first_in,
        new_first_dt,
        new_first_out,
        new_first_small,
        new_second_in,
        new_second_dt,
        new_second_out,
        new_second_small,
        new_in,
        new_dt,
        new_out,
        new_small,
    )


def solution(mesh):
    rows = P(("fsdp", "rep"), None)
    matrix = P("fsdp", None)
    vector = P("fsdp")
    group = (matrix, matrix, matrix, vector)
    return jax.shard_map(
        body,
        mesh=mesh,
        in_specs=(rows, rows, P()) + group * 3,
        out_specs=(rows, rows) + group * 4,
        check_vma=False,
    )
```

```python
from functools import partial

import jax
import jax.numpy as jnp
from jax import lax
from jax.experimental import pallas as pl
from jax.experimental.pallas import tpu as pltpu
from jax.sharding import PartitionSpec as P

D = 1536
H = 48
P_SIZE = 64
N = 128
CONV = 4
STEP = 10
DI = 3072
CHANNELS = DI + 2 * N
SMALL = 21392
N_FSDP = 16
N_REP = 8
ROWS = 256
PACK = 2048
OWN = DI // N_REP
OWN_H = H // N_REP
OWN_BC = 2 * N // N_REP
SHARD_IN = D // N_FSDP
SHARD_OUT = DI // N_FSDP
SHARD_SMALL = SMALL // N_FSDP
WIDE = 384
CHUNK = 128
CHUNKS = PACK // CHUNK
HALF = CHUNKS // 2
TAIL = 512
VMEM_LIMIT = 60 * 1024 * 1024

NORM_EPS = 1e-05
BETA_ONE = 0.9
BETA_TWO = 0.999
ADAM_EPS = 1e-08
WEIGHT_DECAY = 0.1
RATE_MATRIX = 0.04
RATE_SMALL = 0.4
PRECISE = lax.Precision.HIGHEST
BF16 = jnp.bfloat16
F32 = jnp.float32
COST = pl.CostEstimate(flops=1_000_000, bytes_accessed=100_000, transcendentals=0)
FILL = pl.CostEstimate(flops=2_400_000_000, bytes_accessed=20_000_000, transcendentals=0)


def move(value, target):
    pairs = []
    for f in range(N_FSDP):
        for r in range(N_REP):
            yh, z, c, x, yl = target(f // 8, (f // 2) % 4, f % 2, r // 2, r % 2)
            pairs.append((f * N_REP + r, ((yh % 2) * 8 + (z % 4) * 2 + c % 2) * N_REP + (x % 4) * 2 + yl % 2))
    return lax.ppermute(value, ("fsdp", "rep"), pairs)


def along_x(steps):
    return lambda yh, z, c, x, yl: (yh, z, c, x + steps, yl)


def along_z(steps):
    return lambda yh, z, c, x, yl: (yh, z + steps, c, x, yl)


def swap_y(yh, z, c, x, yl):
    return (yh, z, c, x, yl + 1)


def swap_y_hi(yh, z, c, x, yl):
    return (yh + 1, z, c, x, yl)


def swap_core(yh, z, c, x, yl):
    return (yh, z, c + 1, x, yl)


class Place:
    def __init__(self):
        f = lax.axis_index("fsdp")
        r = lax.axis_index("rep")
        self.f, self.r = f, r
        self.yh, self.z, self.c = f // 8, (f // 2) % 4, f % 2
        self.x, self.yl = r // 2, r % 2


def at(value, index, axis=0):
    return lax.dynamic_index_in_dim(value, index, axis, keepdims=False)


def tie(values, *others):
    return lax.optimization_barrier((values, others))[0]


def both(mine, other, second):
    first = jnp.where(second == 0, mine, other)
    last = jnp.where(second == 0, other, mine)
    return jnp.stack([first, last], 0)


def put(out, piece, axis, index):
    starts = [jnp.int32(0)] * out.ndim
    starts[axis] = jnp.int32(index)
    return lax.dynamic_update_slice(out, jnp.expand_dims(piece, axis), tuple(starts))


def swap_shards(value, place):
    other = move(value, lambda yh, z, c, x, yl: (yh + 1, z, c, x, yl + 1))
    return both(value, other, place.yh)


def gather_eight(pair):
    groups = [list(range(8)), list(range(8, 16))]
    out = lax.all_gather(pair, "fsdp", axis=0, tiled=True, axis_index_groups=groups)
    return out.reshape((4, 2) + pair.shape)


def exchange(value, axis):
    return lax.all_to_all(value, axis, 0, 0, tiled=True)


def share_rep(value):
    return exchange(jnp.broadcast_to(value[None], (N_REP,) + value.shape), "rep")


def sum_z(value):
    steps = [move(value, along_z(step)) for step in (1, 3, 2)]
    return value + steps[0] + steps[1] + steps[2]


def scatter_eight(value):
    groups = [list(range(8)), list(range(8, 16))]
    flat = value.reshape(-1, value.shape[-1])
    out = lax.psum_scatter(flat, "fsdp", scatter_dimension=0, tiled=True, axis_index_groups=groups)
    return out.reshape((2,) + value.shape[1:])


def eight_order(f):
    return ((f // 2) % 4 * 2 + f % 2) * 2 + f // 8


def adam_update(weight, gradient, moment_one, moment_two, learn_rate, decay_rate):
    moment_one = BETA_ONE * moment_one + (1.0 - BETA_ONE) * gradient
    moment_two = BETA_TWO * moment_two + (1.0 - BETA_TWO) * gradient * gradient
    scaled = (
        moment_one
        / (1.0 - BETA_ONE**STEP)
        / (jnp.sqrt(moment_two / (1.0 - BETA_TWO**STEP)) + ADAM_EPS)
    )
    return (weight - learn_rate * (scaled + decay_rate * weight), moment_one, moment_two)


def contract_rows(left_side, right_side):
    return lax.dot_general(
        left_side, right_side, (((0,), (0,)), ((), ())), preferred_element_type=F32
    )


def contract_cols(left_side, right_side):
    return lax.dot_general(
        left_side, right_side, (((1,), (1,)), ((), ())), preferred_element_type=F32
    )


def matmul(left_side, right_side):
    return jnp.dot(left_side, right_side, preferred_element_type=F32)


def segment_at(positions, seg_ends):
    counted = jnp.sum((positions[:, None] >= seg_ends[None, :]).astype(jnp.int32), axis=1)
    return jnp.where(positions < 0, jnp.int32(-1), counted)


def split_two(value):
    high = value.astype(BF16)
    return high, (value - high.astype(F32)).astype(BF16)


def split_three(value):
    high = value.astype(BF16)
    rest = value - high.astype(F32)
    middle = rest.astype(BF16)
    return high, middle, (rest - middle.astype(F32)).astype(BF16)


def product(left, right, left_dim, right_dim):
    return lax.dot_general(
        left, right, (((left_dim,), (right_dim,)), ((), ())), preferred_element_type=F32
    )


def joined_product(left_parts, right_parts, left_dim=1, right_dim=0):
    left_high, left_low = left_parts
    right_high, right_low = right_parts
    return product(
        jnp.concatenate([left_high, left_high, left_low], left_dim),
        jnp.concatenate([right_high, right_low, right_high], right_dim),
        left_dim,
        right_dim,
    )


def precise_product(left, right, left_dim=1, right_dim=0):
    return joined_product(split_two(left), split_two(right), left_dim, right_dim)


def ones_product(ones, value):
    return product(jnp.concatenate([ones] * 3, 1), jnp.concatenate(split_three(value), 0), 1, 0)


def spread(per_head, lane):
    return jnp.concatenate(
        [
            jnp.where(lane < P_SIZE, per_head[:, 2 * k : 2 * k + 1], per_head[:, 2 * k + 1 : 2 * k + 2])
            for k in range(OWN_H // 2)
        ],
        1,
    )


def head_sums(value):
    column = lax.broadcasted_iota(jnp.int32, (OWN, N), 0)
    head = lax.broadcasted_iota(jnp.int32, (OWN, N), 1)
    members = ((column >= head * P_SIZE) & (column < (head + 1) * P_SIZE)).astype(F32).astype(BF16)
    high, low = split_two(value)
    return product(jnp.concatenate([high, low], 1), jnp.concatenate([members, members], 0), 1, 0)


def two_heads(pair, lane):
    zero = jnp.zeros_like(pair)
    return jnp.concatenate([jnp.where(lane < P_SIZE, pair, zero), jnp.where(lane < P_SIZE, zero, pair)], 0)


def chunk_facts(ends, chunk, dt_pre, par):
    column = lax.broadcasted_iota(jnp.int32, (CHUNK, 1), 0) + chunk * CHUNK
    row = lax.broadcasted_iota(jnp.int32, (1, CHUNK), 1) + chunk * CHUNK

    def segment(position):
        counted = jnp.zeros_like(position)
        for k in range(3):
            counted = counted + (position >= ends[k]).astype(jnp.int32)
        return jnp.where(position < 0, -1, counted)

    def one_segment(position):
        counted = jnp.int32(0)
        for k in range(3):
            counted = counted + (position >= ends[k]).astype(jnp.int32)
        return jnp.where(position < 0, -1, counted)

    here_column, here_row = segment(column), segment(row)
    prior = one_segment(chunk * CHUNK - 1)
    last = one_segment(chunk * CHUNK + CHUNK - 1)
    lane = lax.broadcasted_iota(jnp.int32, (CHUNK, N), 1)
    shifted = dt_pre + par[6:7, :N]
    soft = jnp.maximum(shifted, 0.0) + jnp.log1p(jnp.exp(-jnp.abs(shifted)))
    step = jnp.where(lane < OWN_H, soft, 0.0)
    decay = step * par[7:8, :N]
    tri_row = lax.broadcasted_iota(jnp.int32, (CHUNK, CHUNK), 0)
    tri_column = lax.broadcasted_iota(jnp.int32, (CHUNK, CHUNK), 1)
    lower = (tri_row >= tri_column).astype(F32).astype(BF16)
    upper = (tri_row <= tri_column).astype(F32).astype(BF16)
    total = ones_product(lower, decay)
    entering = (here_column == prior).astype(F32) * jnp.exp(total)
    end = total[CHUNK - 1 : CHUNK]
    leaving = (here_column == last).astype(F32) * jnp.exp(jnp.minimum(end - total, 0.0))
    passing = jnp.where(last == prior, 1.0, 0.0) * jnp.exp(end)
    return dict(
        column=column,
        segment=segment,
        here_column=here_column,
        here_row=here_row,
        lane=lane,
        shifted=shifted,
        step=step,
        decay=decay,
        total=total,
        entering=entering,
        leaving=leaving,
        passing=passing,
        tri_row=tri_row,
        tri_column=tri_column,
        upper=upper,
    )


def forward_kernel(part, ends, proj, par, *refs):
    if part:
        carry_in, refs = refs[3], refs[4:]
    pre_out, mixed_out, state_out, carry_out, extended, state = refs
    chunk = pl.program_id(0) + part * HALF

    @pl.when(pl.program_id(0) == 0)
    def _():
        if part:
            state[...] = carry_in[:N, :OWN]
            extended[0:8, :] = carry_in[N:, :]
        else:
            state[...] = jnp.zeros_like(state)
            extended[0:8, :] = jnp.zeros((8, 640), F32)

    facts = chunk_facts(ends, chunk, proj[:, 1024:1152], par)
    lane = facts["lane"]
    conv = proj[:, OWN:1024].astype(BF16).astype(F32)
    extended[8 : 8 + CHUNK, :] = conv
    pre = par[4:5] + par[3:4] * conv
    for back in range(1, CONV):
        same = (facts["segment"](facts["column"] - back) == facts["here_column"]).astype(F32)
        pre = pre + par[3 - back : 4 - back] * (extended[8 - back : 8 - back + CHUNK, :] * same)
    extended[0:8, :] = extended[CHUNK : CHUNK + 8, :]
    pre_out[...] = pre
    act = pre * jax.nn.sigmoid(pre)
    own_x, state_b, state_c = act[:, :OWN], act[:, OWN : OWN + N], act[:, OWN + N :]
    stepped = own_x * spread(facts["step"], lane)
    b_parts, c_parts = split_two(state_b), split_two(state_c)
    inside = (facts["tri_row"] >= facts["tri_column"]) & (facts["here_column"] == facts["here_row"])
    scores = jnp.where(inside, joined_product(c_parts, b_parts, 1, 1), 0.0)
    total_rows = facts["total"].T
    state_in = state[...]
    state_out[...] = state_in
    outs = []
    for pair in range(OWN_H // 2):
        mixing = []
        for head in (2 * pair, 2 * pair + 1):
            span = facts["total"][:, head : head + 1] - total_rows[head : head + 1, :]
            mixing.append(jnp.exp(jnp.minimum(span, 0.0)) * scores)
        inner = two_heads(stepped[:, pair * N : pair * N + N], lane)
        outs.append(precise_product(jnp.concatenate(mixing, 1), inner))
    scanned = jnp.concatenate(outs, 1) + spread(facts["entering"], lane) * joined_product(
        c_parts, split_two(state_in)
    )
    state[...] = spread(facts["passing"], lane[:1]) * state_in + precise_product(
        state_b.T, stepped * spread(facts["leaving"], lane)
    )
    mixed_out[...] = scanned + par[5:6, :OWN] * own_x

    @pl.when(pl.program_id(0) == HALF - 1)
    def _():
        carry_out[:N, :OWN] = state[...]
        carry_out[:N, OWN:] = jnp.zeros((N, 640 - OWN), F32)
        carry_out[N:, :] = extended[0:8, :]


def run_forward(part, ends, proj, par, before=()):
    here = lambda i: (i + part * HALF, 0)
    chunked = lambda width: pl.BlockSpec((CHUNK, width), here)
    fixed = lambda shape: pl.BlockSpec(shape, lambda i: (0, 0))
    carry = fixed((N + 8, 640))
    return pl.pallas_call(
        partial(forward_kernel, part),
        grid=(HALF,),
        in_specs=[pl.BlockSpec(memory_space=pltpu.SMEM), chunked(1152), fixed((16, 640))]
        + ([pl.BlockSpec(memory_space=pl.ANY)] * 3 + [carry] if part else []),
        out_specs=[chunked(640), chunked(OWN), pl.BlockSpec((N, OWN), here), carry],
        out_shape=[
            jax.ShapeDtypeStruct((PACK, 640), F32),
            jax.ShapeDtypeStruct((PACK, OWN), F32),
            jax.ShapeDtypeStruct((CHUNKS * N, OWN), F32),
            jax.ShapeDtypeStruct((N + 8, 640), F32),
        ],
        input_output_aliases={3: 0, 4: 1, 5: 2} if part else {},
        scratch_shapes=[pltpu.VMEM((CHUNK + 8, 640), F32), pltpu.VMEM((N, OWN), F32)],
        compiler_params=pltpu.CompilerParams(
            dimension_semantics=("arbitrary",), vmem_limit_bytes=VMEM_LIMIT
        ),
        cost_estimate=COST,
        name="scan_forward",
    )(ends, proj, par, *before)


def backward_kernel(ends, conv_in, dt_in, pre_in, mixed_in, grad_mixed, state_all, par, *refs):
    grad_x, grad_dt, grad_bc, sums, head_acc, carried, extended, end_dot = refs
    step_index = pl.program_id(0)
    chunk = CHUNKS - 1 - step_index

    @pl.when(step_index == 0)
    def _():
        carried[...] = jnp.zeros_like(carried)
        extended[CHUNK : CHUNK + 8, :] = jnp.zeros((8, OWN), F32)
        end_dot[...] = jnp.zeros_like(end_dot)
        sums[...] = jnp.zeros_like(sums)
        head_acc[...] = jnp.zeros_like(head_acc)

    facts = chunk_facts(ends, chunk, dt_in[...], par)
    lane = facts["lane"]
    pre = pre_in[...]
    sig = jax.nn.sigmoid(pre)
    act = pre * sig
    own_x, state_b, state_c = act[:, :OWN], act[:, OWN : OWN + N], act[:, OWN + N :]
    step = facts["step"]
    step_wide = spread(step, lane)
    stepped = own_x * step_wide
    skip = par[5:6, :OWN]
    scanned = mixed_in[...] - skip * own_x
    grad_m = grad_mixed[...]
    sums[6:7] += jnp.sum(grad_m * own_x, 0, keepdims=True)

    b_parts, c_parts = split_two(state_b), split_two(state_c)
    inside = (facts["tri_row"] <= facts["tri_column"]) & (facts["here_column"] == facts["here_row"])
    scores = jnp.where(inside, joined_product(b_parts, c_parts, 1, 1), 0.0)
    total_rows = facts["total"].T
    grad_scores = jnp.zeros((CHUNK, CHUNK), F32)
    grad_stepped = []
    for pair in range(OWN_H // 2):
        columns = slice(pair * N, pair * N + N)
        grad_pair = grad_m[:, columns]
        high, low = split_two(grad_pair)
        stepped_parts = split_two(two_heads(stepped[:, columns], lane))
        grad_mixing = joined_product(stepped_parts, (high, low), 1, 1)
        mixing = []
        for k in range(2):
            head = 2 * pair + k
            span = total_rows[head : head + 1, :] - facts["total"][:, head : head + 1]
            decays = jnp.exp(jnp.minimum(span, 0.0))
            mixing.append(decays * scores)
            grad_scores = grad_scores + decays * grad_mixing[k * CHUNK : (k + 1) * CHUNK]
        grad_stepped.append(
            joined_product(
                split_two(jnp.concatenate(mixing, 1)), (two_heads(high, lane), two_heads(low, lane))
            )
        )
    grad_scores = jnp.where(inside, grad_scores, 0.0)
    carry = carried[...]
    carry_parts = split_two(carry)
    leaving = spread(facts["leaving"], lane)
    grad_stepped = jnp.concatenate(grad_stepped, 1) + leaving * joined_product(b_parts, carry_parts)
    state_in = state_all[...]
    entered = spread(facts["entering"], lane) * grad_m
    entered_parts = split_two(entered)
    grad_b = precise_product(grad_scores, state_c) + joined_product(
        split_two(leaving * stepped), carry_parts, 1, 1
    )
    grad_c = precise_product(grad_scores.T, state_b) + joined_product(
        entered_parts, split_two(state_in), 1, 1
    )
    grad_bc[0:N, :] = grad_b.T
    grad_bc[N:, :] = grad_c.T
    new_carry = spread(facts["passing"], lane[:1]) * carry + joined_product(
        split_two(state_c.T), entered_parts
    )
    carried[...] = new_carry

    grad_step = head_sums(own_x * grad_stepped)
    last_row = lax.broadcasted_iota(jnp.int32, (CHUNK, N), 0) == CHUNK - 1
    grad_total = head_sums(grad_m * scanned) - step * grad_step
    grad_total = grad_total + jnp.where(last_row, end_dot[0:1, :], 0.0)
    grad_decay = ones_product(facts["upper"], grad_total)
    end_dot[...] = head_sums(
        jnp.broadcast_to(jnp.sum(new_carry * state_in, 0, keepdims=True), (8, OWN))
    )
    grad_pre_dt = (grad_step + grad_decay * par[7:8, :N]) * jax.nn.sigmoid(facts["shifted"])
    grad_pre_dt = jnp.where(lane < OWN_H, grad_pre_dt, 0.0)
    grad_dt[...] = grad_pre_dt.astype(BF16)
    head_acc[0:1] += jnp.sum(grad_pre_dt, 0, keepdims=True)
    head_acc[1:2] += jnp.sum(grad_decay * facts["decay"], 0, keepdims=True)

    sig_x, pre_x = sig[:, :OWN], pre[:, :OWN]
    grad_pre = (step_wide * grad_stepped + skip * grad_m) * (sig_x * (1.0 + pre_x * (1.0 - sig_x)))
    extended[0:CHUNK, :] = grad_pre
    conv = conv_in[...].astype(BF16).astype(F32)
    sums[5:6] += jnp.sum(grad_pre, 0, keepdims=True)
    sums[4:5] += jnp.sum(conv * grad_pre, 0, keepdims=True)
    grad_conv = par[3:4, :OWN] * grad_pre
    for ahead in range(1, CONV):
        same = (facts["segment"](facts["column"] + ahead) == facts["here_column"]).astype(F32)
        later = extended[ahead : ahead + CHUNK, :] * same
        sums[4 - ahead : 5 - ahead] += jnp.sum(conv * later, 0, keepdims=True)
        grad_conv = grad_conv + par[3 - ahead : 4 - ahead, :OWN] * later
    extended[CHUNK : CHUNK + 8, :] = extended[0:8, :]
    grad_x[...] = grad_conv.astype(BF16)


def run_backward(ends, proj, pre, mixed, grad_mixed, states, par):
    last = CHUNKS - 1
    chunked = lambda width, column=0: pl.BlockSpec((CHUNK, width), lambda i: (last - i, column))
    fixed = lambda shape: pl.BlockSpec(shape, lambda i: (0, 0))
    return pl.pallas_call(
        backward_kernel,
        grid=(CHUNKS,),
        in_specs=[
            pl.BlockSpec(memory_space=pltpu.SMEM),
            chunked(OWN, 1),
            chunked(N, 8),
            chunked(640),
            chunked(OWN),
            chunked(OWN),
            pl.BlockSpec((N, OWN), lambda i: (last - i, 0)),
            fixed((16, 640)),
        ],
        out_specs=[
            chunked(OWN),
            chunked(N),
            pl.BlockSpec((2 * N, CHUNK), lambda i: (0, last - i)),
            fixed((8, OWN)),
            fixed((8, N)),
        ],
        out_shape=[
            jax.ShapeDtypeStruct((PACK, OWN), BF16),
            jax.ShapeDtypeStruct((PACK, N), BF16),
            jax.ShapeDtypeStruct((2 * N, PACK), F32),
            jax.ShapeDtypeStruct((8, OWN), F32),
            jax.ShapeDtypeStruct((8, N), F32),
        ],
        scratch_shapes=[
            pltpu.VMEM((N, OWN), F32),
            pltpu.VMEM((CHUNK + 8, OWN), F32),
            pltpu.VMEM((8, N), F32),
        ],
        compiler_params=pltpu.CompilerParams(
            dimension_semantics=("arbitrary",), vmem_limit_bytes=VMEM_LIMIT
        ),
        cost_estimate=COST,
        name="scan_backward",
    )(ends, proj, proj, pre, mixed, grad_mixed, states, par)


PARTS = (1, 1, 1, 1, 1, 2, 1, 1)


def piece_copies(pieces, parts, blocks, sems):
    copies = []
    taken = 0
    for slot, count in enumerate(parts):
        rows = ROWS // count
        copies.append(
            [
                pltpu.make_async_copy(
                    pieces[taken + k], blocks.at[slot, pl.ds(k * rows, rows)], sems.at[taken + k]
                )
                for k in range(count)
            ]
        )
        taken += count
    return copies


def fetch_block(pieces, parts, blocks, sems):
    copies = piece_copies(pieces, parts, blocks, sems)
    step = pl.program_id(0)

    @pl.when(step == 0)
    def _():
        for group in copies:
            for copy in group:
                copy.start()

    for slot, group in enumerate(copies):

        @pl.when(step == slot)
        def _(group=group):
            for copy in group:
                copy.wait()

    return blocks[step]


def project_kernel(parts, table, *refs):
    pieces = refs[: sum(parts)]
    gain, shards, normed_out, proj, dt_out, blocks, weight, sems = refs[sum(parts) :]
    block = fetch_block(pieces, parts, blocks, sems)

    @pl.when(pl.program_id(0) == 0)
    def _():
        for f in range(N_FSDP):
            weight[f * SHARD_IN : (f + 1) * SHARD_IN, :] = shards[(f // 2) % 4, f % 2, f // 8, :SHARD_IN]
        dt_out[...] = weight[:, 1024:]

    values = block.astype(F32)
    scale = lax.rsqrt(jnp.mean(values * values, axis=1, keepdims=True) + NORM_EPS)
    normed = (values * scale * gain[...]).astype(BF16)
    normed_out[...] = normed
    proj[...] = matmul(normed, weight[...])


def run_project(table, pieces, gain, shards):
    fixed = lambda shape: pl.BlockSpec(shape, lambda i, table: (0,) * len(shape))
    placed = lambda width: pl.BlockSpec((ROWS, width), lambda i, table: (table[i], 0))
    return pl.pallas_call(
        partial(project_kernel, PARTS),
        grid_spec=pltpu.PrefetchScalarGridSpec(
            num_scalar_prefetch=1,
            grid=(N_REP,),
            in_specs=[pl.BlockSpec(memory_space=pl.ANY)] * len(pieces) + [fixed((1, D)), fixed(shards.shape)],
            out_specs=[placed(D), placed(3 * WIDE), fixed((D, N))],
            scratch_shapes=[
                pltpu.VMEM((N_REP, ROWS, D), BF16),
                pltpu.VMEM((D, 3 * WIDE), BF16),
                pltpu.SemaphoreType.DMA((len(pieces),)),
            ],
        ),
        out_shape=[
            jax.ShapeDtypeStruct((PACK, D), BF16),
            jax.ShapeDtypeStruct((PACK, 3 * WIDE), F32),
            jax.ShapeDtypeStruct((D, N), BF16),
        ],
        compiler_params=pltpu.CompilerParams(
            dimension_semantics=("arbitrary",), vmem_limit_bytes=VMEM_LIMIT
        ),
        cost_estimate=COST,
        name="project",
    )(table, *pieces, gain, shards)


def row_sums(value):
    folded = value[:, :N] + value[:, N : 2 * N] + value[:, 2 * N :]
    return jnp.sum(folded.T, 0, keepdims=True)


def out_grad_kernel(table, *refs):
    pieces = refs[: sum(PARTS)]
    w_out, mixed, gate_in, gain, branch_out, grad_out, sums, blocks, turned, sems = refs[sum(PARTS) :]
    branch = fetch_block(pieces, PARTS, blocks, sems)

    @pl.when(pl.program_id(0) == 0)
    def _():
        turned[...] = w_out[...].reshape(OWN, D).T

    branch_out[...] = branch
    total = matmul(branch, turned[...])
    grad_out[...] = total
    gate = gate_in[...]
    gated = mixed[...] * (gate * jax.nn.sigmoid(gate))
    row = lax.broadcasted_iota(jnp.int32, (8, ROWS), 0)
    sums[...] = jnp.where(
        row == 0, row_sums(gated * gated), jnp.where(row == 1, row_sums(total * gain[...] * gated), 0.0)
    )


def run_out_grad(table, pieces, w_out, mixed, proj, gain):
    fixed = lambda shape: pl.BlockSpec(shape, lambda i, table: (0, 0))
    placed = lambda width: pl.BlockSpec((ROWS, width), lambda i, table: (table[i], 0))
    own = pl.BlockSpec(
        (1, 2, 1, SHARD_OUT, D), lambda i, table: (table[N_REP] % 4, 0, table[N_REP] // 4, 0, 0)
    )
    return pl.pallas_call(
        out_grad_kernel,
        grid_spec=pltpu.PrefetchScalarGridSpec(
            num_scalar_prefetch=1,
            grid=(N_REP,),
            in_specs=[pl.BlockSpec(memory_space=pl.ANY)] * len(pieces)
            + [own, placed(OWN), placed(OWN), fixed((1, OWN))],
            out_specs=[placed(D), placed(OWN), pl.BlockSpec((8, ROWS), lambda i, table: (0, table[i]))],
            scratch_shapes=[
                pltpu.VMEM((N_REP, ROWS, D), BF16),
                pltpu.VMEM((D, WIDE), BF16),
                pltpu.SemaphoreType.DMA((len(pieces),)),
            ],
        ),
        out_shape=[
            jax.ShapeDtypeStruct((PACK, D), BF16),
            jax.ShapeDtypeStruct((PACK, OWN), F32),
            jax.ShapeDtypeStruct((8, PACK), F32),
        ],
        compiler_params=pltpu.CompilerParams(
            dimension_semantics=("arbitrary",), vmem_limit_bytes=VMEM_LIMIT
        ),
        cost_estimate=COST,
        name="out_grad",
    )(table, *pieces, w_out, mixed, proj, gain)


def gate_kernel(grad_out, mixed_in, gate_in, sums, gain, low_out, grad_mixed, grad_gain):
    rows = grad_out.shape[0]
    mixed, gate, grad_o = mixed_in[...], gate_in[...], grad_out[...]
    stats = jnp.concatenate([sums[...], jnp.zeros((N - 8, rows), F32)], 0).T
    out_scale = lax.rsqrt(stats[:, 0:1] * (1.0 / DI) + NORM_EPS)
    pull = out_scale * out_scale * out_scale * (stats[:, 1:2] * (1.0 / DI))
    gate_sig = jax.nn.sigmoid(gate)
    silu = gate * gate_sig
    gated = mixed * silu
    unit = gated * out_scale
    grad_gated = out_scale * (grad_o * gain[...]) - gated * pull
    grad_mixed[...] = grad_gated * silu
    low_out[:, :OWN] = (unit * gain[...]).astype(BF16)
    low_out[:, OWN:] = (grad_gated * mixed * (gate_sig * (1.0 + gate * (1.0 - gate_sig)))).astype(BF16)
    gain_part = jnp.sum(grad_o * unit, 0, keepdims=True)

    @pl.when(pl.program_id(0) == 0)
    def _():
        grad_gain[...] = jnp.broadcast_to(gain_part, grad_gain.shape)

    @pl.when(pl.program_id(0) > 0)
    def _():
        grad_gain[...] += gain_part


def run_gate(grad_out, mixed, proj, sums, gain):
    rows = lambda width: pl.BlockSpec((ROWS, width), lambda i: (i, 0))
    fixed = lambda shape: pl.BlockSpec(shape, lambda i: (0, 0))
    return pl.pallas_call(
        gate_kernel,
        grid=(PACK // ROWS,),
        in_specs=[
            rows(OWN),
            rows(OWN),
            rows(OWN),
            pl.BlockSpec((8, ROWS), lambda i: (0, i)),
            fixed((1, OWN)),
        ],
        out_specs=[rows(2 * OWN), rows(OWN), fixed((8, OWN))],
        out_shape=[
            jax.ShapeDtypeStruct((PACK, 2 * OWN), BF16),
            jax.ShapeDtypeStruct((PACK, OWN), F32),
            jax.ShapeDtypeStruct((8, OWN), F32),
        ],
        compiler_params=pltpu.CompilerParams(
            dimension_semantics=("arbitrary",), vmem_limit_bytes=VMEM_LIMIT
        ),
        cost_estimate=COST,
        name="gate_backward",
    )(grad_out, mixed, proj, sums, gain)


def early_grad_kernel(low, grad_branch, normed, out):
    step = pl.program_id(0)

    @pl.when(step == 0)
    def _():
        out[...] = jnp.zeros_like(out)

    for k in range(4):
        part = product(low[:, :OWN], grad_branch[:, k * WIDE : (k + 1) * WIDE], 0, 0)
        for m in range(4):
            out[eight_order(4 * k + m), :SHARD_IN] += part[m * SHARD_IN : (m + 1) * SHARD_IN]
    part = product(normed[...], low[:, OWN:], 0, 0)
    for f in range(N_FSDP):
        out[eight_order(f), SHARD_IN:] += part[f * SHARD_IN : (f + 1) * SHARD_IN]


def run_early_grad(low, grad_branch, normed):
    count = 2 * ROWS
    rows = lambda width: pl.BlockSpec((count, width), lambda i: (i, 0))
    shape = (N_FSDP, 2 * SHARD_IN, WIDE)
    return pl.pallas_call(
        early_grad_kernel,
        grid=(PACK // count,),
        in_specs=[rows(2 * OWN), rows(D), rows(D)],
        out_specs=pl.BlockSpec(shape, lambda i: (0, 0, 0)),
        out_shape=jax.ShapeDtypeStruct(shape, F32),
        compiler_params=pltpu.CompilerParams(
            dimension_semantics=("arbitrary",), vmem_limit_bytes=VMEM_LIMIT
        ),
        cost_estimate=COST,
        name="early_grad",
    )(low, grad_branch, normed)


def block_out_kernel(rows, weight, tokens, live, out):
    step = pl.program_id(0)
    part = matmul(jnp.concatenate([rows[0], rows[1]], 1), weight[...].reshape(2 * OWN, D))

    @pl.when(step == 0)
    def _():
        out[...] = part

    @pl.when(step > 0)
    def _():
        out[...] += part

    @pl.when(step == N_REP // 2 - 1)
    def _():
        out[...] = tokens[...].astype(F32) + live[...] * out[...]


def run_block_out(rows, weight, tokens, live):
    fixed = lambda shape: pl.BlockSpec(shape, lambda i: (0, 0))
    return pl.pallas_call(
        block_out_kernel,
        grid=(N_REP // 2,),
        in_specs=[
            pl.BlockSpec((2, ROWS, OWN), lambda i: (i, 0, 0)),
            pl.BlockSpec((2, 2, 1, SHARD_OUT, D), lambda i: (i % 2, 0, i // 2, 0, 0)),
            fixed((ROWS, D)),
            fixed((ROWS, 1)),
        ],
        out_specs=fixed((ROWS, D)),
        out_shape=jax.ShapeDtypeStruct((ROWS, D), F32),
        compiler_params=pltpu.CompilerParams(
            dimension_semantics=("arbitrary",), vmem_limit_bytes=VMEM_LIMIT
        ),
        cost_estimate=FILL,
        name="block_out",
    )(rows, weight, tokens, live)


def turned_part(weight, rows):
    return product(weight[...].reshape(D, weight.shape[-1]), rows, 1, 1)


def columns_of(full_in, width, index):
    return pl.BlockSpec(full_in.shape[:-1] + (width,), lambda i: (0, 0, 0, 0, index(i)))


def z_grad_kernel(rows, weight, out):
    part = turned_part(weight, jnp.concatenate([rows[0], rows[1]], 1))

    @pl.when(pl.program_id(0) == 0)
    def _():
        out[...] = part

    @pl.when(pl.program_id(0) > 0)
    def _():
        out[...] += part


def run_z_grad(rows, full_in):
    return pl.pallas_call(
        z_grad_kernel,
        grid=(N_REP // 2,),
        in_specs=[
            pl.BlockSpec((2, ROWS, OWN), lambda i: (i, 0, 1)),
            columns_of(full_in, 2 * OWN, lambda i: i),
        ],
        out_specs=pl.BlockSpec((D, ROWS), lambda i: (0, 0)),
        out_shape=jax.ShapeDtypeStruct((D, ROWS), F32),
        compiler_params=pltpu.CompilerParams(
            dimension_semantics=("arbitrary",), vmem_limit_bytes=VMEM_LIMIT
        ),
        cost_estimate=FILL,
        name="z_grad",
    )(rows, full_in)


def input_grad_kernel(
    own_half, grad_z, x_rows, rest_rows, w_x, w_bc, low_dt, tokens, cotangent, gain, out, gain_out, total, ordered
):
    step = pl.program_id(0)
    part = turned_part(w_x, jnp.concatenate([x_rows[0], x_rows[1]], 1))

    @pl.when(step == 0)
    def _():
        total[...] = grad_z[...] + part

    @pl.when(step > 0)
    def _():
        total[...] += part

    @pl.when(step == N_REP // 2 - 1)
    def _():
        lane = lax.broadcasted_iota(jnp.int32, (ROWS, N), 1)
        groups = []
        for k in range(2):
            group = jnp.zeros((ROWS, N), F32)
            for m in range(4):
                value = rest_rows[4 * k + m].astype(F32)
                value = value if m == 0 else pltpu.roll(value, m * OWN_BC, 1)
                group = jnp.where((lane >= m * OWN_BC) & (lane < (m + 1) * OWN_BC), value, group)
            groups.append(group.astype(BF16))
        steps = jnp.zeros((ROWS, N), F32)
        for m in range(N_REP):
            start = 8 + m * OWN_H
            value = pltpu.roll(rest_rows[m].astype(F32), (start - OWN_BC) % N, 1)
            steps = jnp.where((lane >= start) & (lane < start + OWN_H), value, steps)
        total[...] += turned_part(w_bc, jnp.concatenate(groups, 1))
        for f in range(N_FSDP):
            place = eight_order(f) - f // 8 + (f // 8 + own_half[0]) % 2
            start = pl.multiple_of(place * SHARD_IN, SHARD_IN)
            ordered[f * SHARD_IN : (f + 1) * SHARD_IN, :] = total[pl.ds(start, SHARD_IN), :]
        grad_h = (ordered[...] + product(low_dt[...], steps.astype(BF16), 1, 1)).T
        values = tokens[...].astype(F32)
        scale = lax.rsqrt(jnp.mean(values * values, axis=1, keepdims=True) + NORM_EPS)
        unit = values * scale
        gain_sum = jnp.sum(grad_h * unit, 0, keepdims=True)
        gain_out[...] = jnp.zeros_like(gain_out)
        for k in range(D // TAIL):
            gain_out[k : k + 1, :] = gain_sum[:, k * TAIL : (k + 1) * TAIL]
        grad_unit = grad_h * gain[...]
        inner = jnp.mean(grad_unit * unit, axis=1, keepdims=True)
        out[...] = cotangent[...].astype(F32) + scale * (grad_unit - unit * inner)


def run_input_grad(own_half, grad_z, tail_rows, full_in, low_dt, tokens, cotangent, gain):
    fixed = lambda shape: pl.BlockSpec(shape, lambda i: (0,) * len(shape))
    return pl.pallas_call(
        input_grad_kernel,
        grid=(N_REP // 2,),
        in_specs=[
            pl.BlockSpec(memory_space=pltpu.SMEM),
            fixed((D, ROWS)),
            pl.BlockSpec((2, ROWS, OWN), lambda i: (i, 0, 0)),
            pl.BlockSpec((N_REP, ROWS, N), lambda i: (0, 0, OWN // N)),
            columns_of(full_in, 2 * OWN, lambda i: N_REP // 2 + i),
            columns_of(full_in, 2 * N, lambda i: DI // N),
            fixed((D, N)),
            fixed((ROWS, D)),
            fixed((ROWS, D)),
            fixed((1, D)),
        ],
        out_specs=[fixed((ROWS, D)), fixed((8, TAIL))],
        out_shape=[jax.ShapeDtypeStruct((ROWS, D), F32), jax.ShapeDtypeStruct((8, TAIL), F32)],
        scratch_shapes=[pltpu.VMEM((D, ROWS), F32), pltpu.VMEM((D, ROWS), F32)],
        compiler_params=pltpu.CompilerParams(
            dimension_semantics=("arbitrary",), vmem_limit_bytes=VMEM_LIMIT
        ),
        cost_estimate=COST,
        name="input_grad",
    )(own_half, grad_z, tail_rows, tail_rows, full_in, full_in, low_dt, tokens, cotangent, gain)


def rest_kernel(
    ends, parts, pre_b, pre_c, conv_in, par, grad_x, grad_dt, sums, head_acc, grad_gain, first, tail_out, small_out
):
    own = lax.broadcasted_iota(jnp.int32, (OWN_BC, 2 * N), 0) + first[0]
    chosen = (lax.broadcasted_iota(jnp.int32, (OWN_BC, 2 * N), 1) == own).astype(F32).astype(BF16)

    def pick(value):
        return product(jnp.concatenate([chosen] * 3, 1), jnp.concatenate(split_three(value), 1), 1, 1)

    grad = parts[0]
    for k in range(1, N_REP):
        grad = grad + parts[k]
    own_pre = pick(jnp.concatenate([pre_b[...], pre_c[...]], 1))
    own_conv = product(chosen, conv_in[...].astype(BF16), 1, 1)
    taps = pick(par[:, OWN:])
    sig = jax.nn.sigmoid(own_pre)
    grad_pre = grad * (sig * (1.0 + own_pre * (1.0 - sig)))
    position = lax.broadcasted_iota(jnp.int32, (1, PACK), 1)

    def segment(places):
        counted = jnp.zeros_like(places)
        for k in range(3):
            counted = counted + (places >= ends[k]).astype(jnp.int32)
        return counted

    grad_conv = taps[:, CONV - 1 : CONV] * grad_pre
    column = lax.broadcasted_iota(jnp.int32, (OWN_BC, N), 1)
    found = jnp.where(column == CONV, jnp.sum(grad_pre, 1, keepdims=True), 0.0)
    found = jnp.where(column == CONV - 1, jnp.sum(own_conv * grad_pre, 1, keepdims=True), found)
    for later_by in range(1, CONV):
        same = (segment(position + later_by) == segment(position)) & (position < PACK - later_by)
        later = jnp.where(same, pltpu.roll(grad_pre, PACK - later_by, 1), 0.0)
        tap = CONV - 1 - later_by
        found = jnp.where(column == tap, jnp.sum(own_conv * later, 1, keepdims=True), found)
        grad_conv = grad_conv + taps[:, tap : tap + 1] * later
    lane = lax.broadcasted_iota(jnp.int32, (N, N), 1)
    filler = jnp.zeros((N - OWN_BC, N), F32)
    for k in range(PACK // N):
        rows = slice(k * N, (k + 1) * N)
        columns = jnp.concatenate([grad_conv[:, rows], filler], 0).T
        steps = pltpu.roll(grad_dt[rows, :].astype(F32), OWN_BC, 1)
        tail_out[rows, :OWN] = grad_x[rows, :]
        tail_out[rows, OWN:] = jnp.where(
            lane < OWN_BC, columns, jnp.where(lane < OWN_BC + OWN_H, steps, 0.0)
        ).astype(BF16)
    row = lax.broadcasted_iota(jnp.int32, (8, OWN), 0)
    skip = head_sums(sums[...])
    by_head = jnp.concatenate([skip, jnp.zeros((8, OWN - N), F32)], 1)
    logs = jnp.concatenate([head_acc[...], jnp.zeros((8, OWN - N), F32)], 1)
    wide = jnp.where(row == 0, grad_gain[0:1, :], jnp.where(row < 6, sums[...], 0.0))
    wide = jnp.where(row == 6, logs[1:2, :], jnp.where(row == 7, by_head[6:7, :], wide))
    turned = jnp.concatenate([found, filler], 0).T
    first_row = lax.broadcasted_iota(jnp.int32, (8, N), 0) == 0
    small_out[:, :OWN] = wide
    small_out[:, OWN:] = jnp.where(first_row, head_acc[0:1, :], pltpu.roll(turned[:8], 1, 0))


def run_rest(ends, parts, pre, proj, par, grad_x, grad_dt, sums, head_acc, grad_gain, first):
    fixed = lambda shape: pl.BlockSpec(shape, lambda i: (0,) * len(shape))
    return pl.pallas_call(
        rest_kernel,
        grid=(1,),
        in_specs=[
            pl.BlockSpec(memory_space=pltpu.SMEM),
            fixed((N_REP, OWN_BC, PACK)),
            pl.BlockSpec((PACK, N), lambda i: (0, 3)),
            pl.BlockSpec((PACK, N), lambda i: (0, 4)),
            pl.BlockSpec((PACK, 2 * N), lambda i: (0, 3)),
            fixed((16, 640)),
            fixed((PACK, OWN)),
            fixed((PACK, N)),
            fixed((8, OWN)),
            fixed((8, N)),
            fixed((8, OWN)),
            pl.BlockSpec(memory_space=pltpu.SMEM),
        ],
        out_specs=[fixed((PACK, TAIL)), fixed((8, TAIL))],
        out_shape=[jax.ShapeDtypeStruct((PACK, TAIL), BF16), jax.ShapeDtypeStruct((8, TAIL), F32)],
        compiler_params=pltpu.CompilerParams(
            dimension_semantics=("arbitrary",), vmem_limit_bytes=VMEM_LIMIT
        ),
        cost_estimate=COST,
        name="rest_backward",
    )(ends, parts, pre, pre, proj, par, grad_x, grad_dt, sums, head_acc, grad_gain, first)


def tail_grad_kernel(normed, tail, small, out):
    step = pl.program_id(0)
    part = product(normed[...], tail[...], 0, 0)
    for f in range(N_FSDP):
        rows = part[f * SHARD_IN : (f + 1) * SHARD_IN]

        @pl.when(step == 0)
        def _(f=f, rows=rows):
            out[eight_order(f), :SHARD_IN] = rows
            out[eight_order(f), SHARD_IN:] = small[...]

        @pl.when(step > 0)
        def _(f=f, rows=rows):
            out[eight_order(f), :SHARD_IN] += rows


def run_tail_grad(normed, tail, small):
    count = 2 * ROWS
    shape = (N_FSDP, SHARD_IN + 8, TAIL)
    return pl.pallas_call(
        tail_grad_kernel,
        grid=(PACK // count,),
        in_specs=[
            pl.BlockSpec((count, D), lambda i: (i, 0)),
            pl.BlockSpec((count, TAIL), lambda i: (i, 0)),
            pl.BlockSpec((8, TAIL), lambda i: (0, 0)),
        ],
        out_specs=pl.BlockSpec(shape, lambda i: (0, 0, 0)),
        out_shape=jax.ShapeDtypeStruct(shape, F32),
        compiler_params=pltpu.CompilerParams(
            dimension_semantics=("arbitrary",), vmem_limit_bytes=VMEM_LIMIT
        ),
        cost_estimate=COST,
        name="tail_grad",
    )(normed, tail, small)


def adam_step(grad, weight, first, second, grad_out, first_out, second_out, weight_out):
    new_weight, new_first, new_second = adam_update(
        weight[...], grad, first[...], second[...], RATE_MATRIX, WEIGHT_DECAY
    )
    grad_out[...] = grad
    first_out[...] = new_first
    second_out[...] = new_second
    weight_out[...] = new_weight


def adam_early_kernel(rows, pair, *refs):
    arrays, grad = refs[:-1], refs[-1]
    grad[:, :WIDE] = pair[0, rows, :]
    grad[:, WIDE:] = pair[1, rows, :]
    adam_step(grad[...], *arrays)


def run_adam_early(place_of, rows, parts, weight, first, second):
    part = pl.BlockSpec((SHARD_IN, 2 * WIDE), place_of)
    shape = jax.ShapeDtypeStruct(weight.shape, F32)
    return pl.pallas_call(
        partial(adam_early_kernel, rows),
        grid=(N_REP // 2,),
        in_specs=[pl.BlockSpec((2,) + parts.shape[1:], lambda i: (i, 0, 0))] + [part] * 3,
        out_specs=[part] * 4,
        out_shape=[shape] * 4,
        scratch_shapes=[pltpu.VMEM((SHARD_IN, 2 * WIDE), F32)],
        compiler_params=pltpu.CompilerParams(
            dimension_semantics=("arbitrary",), vmem_limit_bytes=VMEM_LIMIT
        ),
        cost_estimate=FILL,
        name="adam",
    )(parts, weight, first, second)


def adam_tail_kernel(pair, rest, *refs):
    arrays, grad = refs[:3] + refs[-5:-1], refs[-1]
    step = pl.program_id(0)

    @pl.when(step < N_REP // 2)
    def _():
        grad[:, :WIDE] = pair[0, :SHARD_IN]
        grad[:, WIDE:] = pair[1, :SHARD_IN]

    @pl.when(step == N_REP // 2)
    def _():
        lane = lax.broadcasted_iota(jnp.int32, (SHARD_IN, N), 1)
        for k in range(2):
            group = jnp.zeros((SHARD_IN, N), F32)
            for m in range(4):
                value = rest[4 * k + m, :SHARD_IN]
                value = value if m == 0 else pltpu.roll(value, m * OWN_BC, 1)
                group = jnp.where((lane >= m * OWN_BC) & (lane < (m + 1) * OWN_BC), value, group)
            grad[:, k * N : (k + 1) * N] = group

    adam_step(grad[...], *arrays)


def run_adam_tail(parts, weight, first, second, before):
    half = N_REP // 2
    rows = parts.shape[1]
    column = pl.BlockSpec((SHARD_IN, 2 * WIDE), lambda i: (0, half + i))
    shape = jax.ShapeDtypeStruct(weight.shape, F32)
    return pl.pallas_call(
        adam_tail_kernel,
        grid=(half + 1,),
        in_specs=[
            pl.BlockSpec((2, rows, OWN), lambda i: (jnp.minimum(i, half - 1), 0, 0)),
            pl.BlockSpec((N_REP, rows, N), lambda i: (0, 0, OWN // N)),
        ]
        + [column] * 3
        + [pl.BlockSpec(memory_space=pl.ANY)] * 4,
        out_specs=[column] * 4,
        out_shape=[shape] * 4,
        input_output_aliases={5 + k: k for k in range(4)},
        scratch_shapes=[pltpu.VMEM((SHARD_IN, 2 * WIDE), F32)],
        compiler_params=pltpu.CompilerParams(
            dimension_semantics=("arbitrary",), vmem_limit_bytes=VMEM_LIMIT
        ),
        cost_estimate=COST,
        name="adam_tail",
    )(parts, parts, weight, first, second, *before)


def body(
    tokens,
    cotangent,
    lengths,
    w_in,
    w_dt,
    w_out,
    small,
    first_in,
    first_dt,
    first_out,
    first_small,
    second_in,
    second_dt,
    second_out,
    second_small,
):
    place = Place()
    r = place.r
    zero = jnp.int32(0)
    pack_lengths = lax.dynamic_slice_in_dim(lengths, place.f, 1, 0)[0]
    seg_ends = jnp.cumsum(pack_lengths)
    own_positions = r * ROWS + jnp.arange(ROWS, dtype=jnp.int32)
    own_live = (segment_at(own_positions, seg_ends) < 3).astype(F32)[:, None]
    slots = jnp.arange(N_REP, dtype=jnp.int32)
    ahead = ((place.x + slots // 2) % 4) * 2 + (place.yl + slots) % 2
    half = ROWS // 2

    in_low = w_in.astype(BF16)
    dt_low = w_dt.astype(BF16)
    out_low = w_out.astype(BF16)

    small_rows = jnp.pad(small.astype(BF16), (0, 16 * 3 * WIDE - SHARD_SMALL)).reshape(16, 3 * WIDE)

    def own_columns(rep):
        columns = jnp.concatenate(
            [
                lax.dynamic_slice_in_dim(in_low, rep * OWN, OWN, 1),
                lax.dynamic_slice_in_dim(in_low, DI + rep * OWN, OWN, 1),
                in_low[:, 2 * DI :],
                lax.dynamic_slice_in_dim(dt_low, rep * OWN_H, OWN_H, 1),
                jnp.zeros((SHARD_IN, 2), BF16),
                dt_low,
                jnp.zeros((SHARD_IN, N - 8 - H), BF16),
            ],
            1,
        )
        return jnp.concatenate([columns, small_rows], 0)

    other_columns = move(
        own_columns(2 * place.x + 1 - place.yl), lambda yh, z, c, x, yl: (yh + 1, z, c, x, yl + 1)
    )
    from_left = move(tokens, along_x(1))
    from_right = move(tokens, along_x(-1))
    partner = move(tokens, swap_y)

    out_low, other_columns = lax.optimization_barrier((out_low, other_columns))
    out_other = move(out_low, lambda yh, z, c, x, yl: (yh + 1, z, c, x, yl + 1))
    branch = (cotangent.astype(F32) * own_live).astype(BF16)
    from_left, from_right, partner, other_columns, branch = lax.optimization_barrier(
        (from_left, from_right, partner, other_columns, branch)
    )
    own_shards = gather_eight(both(own_columns(r), other_columns, place.yh))
    far = move(from_left, along_x(1))
    partner_left = move(from_left, swap_y)
    partner_right = move(partner, along_x(-1))

    far, partner_left, partner_right, out_other, branch, in_low = lax.optimization_barrier(
        (far, partner_left, partner_right, out_other, branch, in_low)
    )
    in_other = move(in_low, lambda yh, z, c, x, yl: (yh + 1, z, c, x, yl + 1))
    out_pair = both(out_low, out_other, place.yh)
    partner_far_top = move(partner_left[:half], along_x(1))
    partner_far_low = move(partner_right[half:], along_x(-1))

    vector = own_shards[:, :, :, SHARD_IN : SHARD_IN + 2].transpose(2, 0, 1, 3, 4)
    vector = vector.reshape(N_FSDP, 6 * WIDE)[:, :SHARD_SMALL].reshape(-1).astype(F32)
    offset = 0
    gain_in = vector[None, :D]
    offset = D
    gain_row = lax.dynamic_slice_in_dim(vector, offset + r * OWN, OWN, 0)[None, :]
    offset += DI
    taps = vector[offset : offset + (CONV + 1) * CHANNELS].reshape(CONV + 1, CHANNELS)
    offset += (CONV + 1) * CHANNELS
    per_head = vector[offset:].reshape(3, H)
    dt_bias, a_log, d_skip = lax.dynamic_slice_in_dim(per_head, r * OWN_H, OWN_H, 1)
    taps_bc = taps[:, DI:]
    conv_par = jnp.concatenate([lax.dynamic_slice_in_dim(taps, r * OWN, OWN, 1), taps_bc], 1)
    head_par = jnp.stack(
        [
            jnp.pad(jnp.broadcast_to(d_skip[:, None], (OWN_H, P_SIZE)).reshape(-1), (0, 2 * N)),
            jnp.pad(dt_bias, (0, 640 - OWN_H)),
            jnp.pad(-jnp.exp(a_log), (0, 640 - OWN_H)),
        ],
        0,
    )
    par = jnp.concatenate([conv_par, head_par, jnp.zeros((8, 640), F32)], 0)

    partner_far_top, partner_far_low, own_shards = lax.optimization_barrier(
        (partner_far_top, partner_far_low, own_shards)
    )
    full_out = gather_eight(tie(out_pair, own_shards))
    b_left = move(branch, along_x(1))
    b_right = move(branch, along_x(-1))
    b_partner = move(branch, swap_y)
    token_pieces = [
        tokens, partner, from_right, partner_right, far,
        partner_far_top, partner_far_low, from_left, partner_left,
    ]
    normed, proj, low_dt = run_project(ahead, token_pieces, gain_in, own_shards)
    b_left, b_right, b_partner, proj = lax.optimization_barrier((b_left, b_right, b_partner, proj))
    b_far = move(b_left, along_x(1))
    b_partner_left = move(b_left, swap_y)
    b_partner_right = move(b_partner, along_x(-1))
    before = run_forward(0, seg_ends, proj, par)
    b_far, b_partner_left, b_partner_right, before = lax.optimization_barrier(
        (b_far, b_partner_left, b_partner_right, before)
    )
    b_partner_far_top = move(b_partner_left[:half], along_x(1))
    b_partner_far_low = move(b_partner_right[half:], along_x(-1))
    pre, mixed, states, _ = run_forward(1, seg_ends, proj, par, before)
    mixed, in_low, in_other, b_partner_far_top, b_partner_far_low = lax.optimization_barrier(
        (mixed, in_low, in_other, b_partner_far_top, b_partner_far_low)
    )
    full_in = gather_eight(jnp.stack([in_low, in_other], 0))
    branch_pieces = [
        branch, b_partner, b_right, b_partner_right, b_far,
        b_partner_far_top, b_partner_far_low, b_left, b_partner_left,
    ]
    rep_table = jnp.concatenate([ahead, r[None]])
    grad_branch, grad_normed_out, sums = run_out_grad(rep_table, branch_pieces, full_out, mixed, proj, gain_row)
    sums = share_rep(sums[:2].reshape(32, 128)).sum(0).reshape(2, PACK)
    sums = jnp.concatenate([sums, jnp.zeros((6, PACK), F32)], 0)

    low, grad_mixed, grad_gain = run_gate(grad_normed_out, mixed, proj, sums, gain_row)

    low_rows = exchange(low.reshape(N_REP, ROWS, 2 * OWN), "rep")
    grad_x, grad_dtraw, grad_bc, grad_sums, grad_heads = run_backward(
        seg_ends, proj, pre, mixed, grad_mixed, states, par
    )
    low, grad_x = lax.optimization_barrier((low, grad_x))
    early_grad = run_early_grad(low, grad_branch, normed)
    low_rows, early_grad, grad_bc, grad_x = lax.optimization_barrier((low_rows, early_grad, grad_bc, grad_x))

    grad_bc = exchange(grad_bc, "rep").reshape(N_REP, OWN_BC, PACK)
    early = scatter_eight(early_grad)
    grad_rows = run_z_grad(low_rows, full_in)
    grad_bc, grad_rows = lax.optimization_barrier((grad_bc, grad_rows))

    tail, small_own = run_rest(
        seg_ends, grad_bc, pre, proj, par, grad_x, grad_dtraw, grad_sums, grad_heads, grad_gain, (r * OWN_BC)[None]
    )
    grad_tail = run_tail_grad(normed, tail, small_own)
    tail, grad_tail, low_rows = lax.optimization_barrier((tail, grad_tail, low_rows))
    tail_rows = exchange(tail.reshape(N_REP, ROWS, TAIL), "rep")
    early, grad_tail = lax.optimization_barrier((early, grad_tail))
    tail_part = scatter_eight(grad_tail)
    mine, other = at(early, place.yh), at(early, 1 - place.yh)
    out_mine = move(
        mine[:SHARD_IN], lambda yh, z, c, x, yl: (x // 2, (x % 2) * 2 + yl, z % 2, 2 * c + yh, z // 2)
    )
    out_other = move(
        other[:SHARD_IN], lambda yh, z, c, x, yl: (x // 2, (x % 2) * 2 + yl, z % 2, 2 * c + 1 - yh, z // 2)
    )
    z_other = move(other[SHARD_IN:], swap_y_hi)
    tail_rows, out_mine, out_other, z_other = lax.optimization_barrier((tail_rows, out_mine, out_other, z_other))

    early_parts = share_rep(jnp.concatenate([out_mine + out_other, mine[SHARD_IN:] + z_other], 0))
    input_grad, grad_gain_in = run_input_grad(
        place.yh[None], grad_rows, tail_rows, full_in, low_dt, tokens, cotangent, gain_in
    )
    tail_part, grad_gain_in = lax.optimization_barrier((tail_part, grad_gain_in))

    tail_other = move(at(tail_part, 1 - place.yh), swap_y_hi)
    grad_gain_in = sum_z(grad_gain_in + move(grad_gain_in, swap_core))
    tail_part = at(tail_part, place.yh) + tail_other
    grad_gain_in = grad_gain_in + move(grad_gain_in, swap_y_hi)
    tail_part = jnp.concatenate([tail_part, grad_gain_in], 0)

    tail_part, early_parts, low_rows = lax.optimization_barrier((tail_part, early_parts, low_rows))
    tail_parts = share_rep(tail_part)
    block_out = run_block_out(low_rows, full_out, tokens, own_live)

    grad_out, new_first_out, new_second_out, new_out = run_adam_early(
        lambda i: (i // 2, i % 2), slice(0, SHARD_IN), early_parts, w_out, first_out, second_out
    )
    updated = run_adam_early(
        lambda i: (0, i), slice(SHARD_IN, 2 * SHARD_IN), early_parts, w_in, first_in, second_in
    )
    grad_in, new_first_in, new_second_in, new_in = run_adam_tail(tail_parts, w_in, first_in, second_in, updated)

    def columns(parts):
        return parts.transpose(1, 0, 2).reshape(parts.shape[1], -1)

    small_parts = tail_parts[:, SHARD_IN : SHARD_IN + 8]
    grad_gain_in = tail_parts[:, SHARD_IN + 8 : SHARD_IN + 8 + D // TAIL].sum(0).reshape(-1)
    small_x = small_parts[:, :, :OWN].transpose(1, 0, 2).reshape(8, DI)
    small_bc = small_parts[:, :, OWN:].transpose(1, 0, 2)

    def channels(row):
        return jnp.concatenate([small_x[row], small_bc[row, :, :OWN_BC].reshape(-1)])

    grad_small_all = jnp.concatenate(
        [grad_gain_in, small_x[0]]
        + [channels(row) for row in range(1, 6)]
        + [
            small_bc[0, :, :OWN_H].reshape(-1),
            small_parts[:, 6, :OWN_H].reshape(-1),
            small_parts[:, 7, :OWN_H].reshape(-1),
        ]
    )
    grad_small = lax.dynamic_slice_in_dim(grad_small_all, place.f * SHARD_SMALL, SHARD_SMALL, 0)
    grad_dt = columns(tail_parts[:, :SHARD_IN, OWN + OWN_BC : OWN + OWN_BC + OWN_H])
    new_dt, new_first_dt, new_second_dt = adam_update(
        w_dt, grad_dt, first_dt, second_dt, RATE_MATRIX, WEIGHT_DECAY
    )
    new_small, new_first_small, new_second_small = adam_update(
        small, grad_small, first_small, second_small, RATE_SMALL, 0.0
    )
    return (
        block_out,
        input_grad,
        grad_in,
        grad_dt,
        grad_out,
        grad_small,
        new_first_in,
        new_first_dt,
        new_first_out,
        new_first_small,
        new_second_in,
        new_second_dt,
        new_second_out,
        new_second_small,
        new_in,
        new_dt,
        new_out,
        new_small,
    )


def solution(mesh):
    rows = P(("fsdp", "rep"), None)
    matrix = P("fsdp", None)
    vector = P("fsdp")
    group = (matrix, matrix, matrix, vector)
    return jax.shard_map(
        body,
        mesh=mesh,
        in_specs=(rows, rows, P()) + group * 3,
        out_specs=(rows, rows) + group * 4,
        check_vma=False,
    )
```

```python
from functools import partial

import jax
import jax.numpy as jnp
from jax import lax
from jax.experimental import pallas as pl
from jax.experimental.pallas import tpu as pltpu
from jax.sharding import PartitionSpec as P

D = 1536
H = 48
P_SIZE = 64
N = 128
CONV = 4
STEP = 10
DI = 3072
CHANNELS = DI + 2 * N
SMALL = 21392
N_FSDP = 16
N_REP = 8
ROWS = 256
PACK = 2048
OWN = DI // N_REP
OWN_H = H // N_REP
OWN_BC = 2 * N // N_REP
SHARD_IN = D // N_FSDP
SHARD_OUT = DI // N_FSDP
SHARD_SMALL = SMALL // N_FSDP
WIDE = 384
CHUNK = 128
CHUNKS = PACK // CHUNK
HALF = CHUNKS // 2
TAIL = 512
VMEM_LIMIT = 60 * 1024 * 1024

NORM_EPS = 1e-05
BETA_ONE = 0.9
BETA_TWO = 0.999
ADAM_EPS = 1e-08
WEIGHT_DECAY = 0.1
RATE_MATRIX = 0.04
RATE_SMALL = 0.4
PRECISE = lax.Precision.HIGHEST
BF16 = jnp.bfloat16
F32 = jnp.float32
COST = pl.CostEstimate(flops=1_000_000, bytes_accessed=100_000, transcendentals=0)
FILL = pl.CostEstimate(flops=2_400_000_000, bytes_accessed=20_000_000, transcendentals=0)


def move(value, target):
    pairs = []
    for f in range(N_FSDP):
        for r in range(N_REP):
            yh, z, c, x, yl = target(f // 8, (f // 2) % 4, f % 2, r // 2, r % 2)
            pairs.append((f * N_REP + r, ((yh % 2) * 8 + (z % 4) * 2 + c % 2) * N_REP + (x % 4) * 2 + yl % 2))
    return lax.ppermute(value, ("fsdp", "rep"), pairs)


def along_x(steps):
    return lambda yh, z, c, x, yl: (yh, z, c, x + steps, yl)


def along_z(steps):
    return lambda yh, z, c, x, yl: (yh, z + steps, c, x, yl)


def swap_y(yh, z, c, x, yl):
    return (yh, z, c, x, yl + 1)


def swap_y_hi(yh, z, c, x, yl):
    return (yh + 1, z, c, x, yl)


def swap_core(yh, z, c, x, yl):
    return (yh, z, c + 1, x, yl)


class Place:
    def __init__(self):
        f = lax.axis_index("fsdp")
        r = lax.axis_index("rep")
        self.f, self.r = f, r
        self.yh, self.z, self.c = f // 8, (f // 2) % 4, f % 2
        self.x, self.yl = r // 2, r % 2


def at(value, index, axis=0):
    return lax.dynamic_index_in_dim(value, index, axis, keepdims=False)


def tie(values, *others):
    return lax.optimization_barrier((values, others))[0]


def both(mine, other, second):
    first = jnp.where(second == 0, mine, other)
    last = jnp.where(second == 0, other, mine)
    return jnp.stack([first, last], 0)


def put(out, piece, axis, index):
    starts = [jnp.int32(0)] * out.ndim
    starts[axis] = jnp.int32(index)
    return lax.dynamic_update_slice(out, jnp.expand_dims(piece, axis), tuple(starts))


def swap_shards(value, place):
    other = move(value, lambda yh, z, c, x, yl: (yh + 1, z, c, x, yl + 1))
    return both(value, other, place.yh)


def gather_eight(pair):
    groups = [list(range(8)), list(range(8, 16))]
    out = lax.all_gather(pair, "fsdp", axis=0, tiled=True, axis_index_groups=groups)
    return out.reshape((4, 2) + pair.shape)


def exchange(value, axis):
    return lax.all_to_all(value, axis, 0, 0, tiled=True)


def share_rep(value):
    return exchange(jnp.broadcast_to(value[None], (N_REP,) + value.shape), "rep")


def sum_z(value):
    steps = [move(value, along_z(step)) for step in (1, 3, 2)]
    return value + steps[0] + steps[1] + steps[2]


def scatter_eight(value):
    groups = [list(range(8)), list(range(8, 16))]
    flat = value.reshape(-1, value.shape[-1])
    out = lax.psum_scatter(flat, "fsdp", scatter_dimension=0, tiled=True, axis_index_groups=groups)
    return out.reshape((2,) + value.shape[1:])


def eight_order(f):
    return ((f // 2) % 4 * 2 + f % 2) * 2 + f // 8


def adam_update(weight, gradient, moment_one, moment_two, learn_rate, decay_rate):
    moment_one = BETA_ONE * moment_one + (1.0 - BETA_ONE) * gradient
    moment_two = BETA_TWO * moment_two + (1.0 - BETA_TWO) * gradient * gradient
    scaled = (
        moment_one
        / (1.0 - BETA_ONE**STEP)
        / (jnp.sqrt(moment_two / (1.0 - BETA_TWO**STEP)) + ADAM_EPS)
    )
    return (weight - learn_rate * (scaled + decay_rate * weight), moment_one, moment_two)


def contract_rows(left_side, right_side):
    return lax.dot_general(
        left_side, right_side, (((0,), (0,)), ((), ())), preferred_element_type=F32
    )


def contract_cols(left_side, right_side):
    return lax.dot_general(
        left_side, right_side, (((1,), (1,)), ((), ())), preferred_element_type=F32
    )


def matmul(left_side, right_side):
    return jnp.dot(left_side, right_side, preferred_element_type=F32)


def segment_at(positions, seg_ends):
    counted = jnp.sum((positions[:, None] >= seg_ends[None, :]).astype(jnp.int32), axis=1)
    return jnp.where(positions < 0, jnp.int32(-1), counted)


def split_two(value):
    high = value.astype(BF16)
    return high, (value - high.astype(F32)).astype(BF16)


def split_three(value):
    high = value.astype(BF16)
    rest = value - high.astype(F32)
    middle = rest.astype(BF16)
    return high, middle, (rest - middle.astype(F32)).astype(BF16)


def product(left, right, left_dim, right_dim):
    return lax.dot_general(
        left, right, (((left_dim,), (right_dim,)), ((), ())), preferred_element_type=F32
    )


def joined_product(left_parts, right_parts, left_dim=1, right_dim=0):
    left_high, left_low = left_parts
    right_high, right_low = right_parts
    return product(
        jnp.concatenate([left_high, left_high, left_low], left_dim),
        jnp.concatenate([right_high, right_low, right_high], right_dim),
        left_dim,
        right_dim,
    )


def precise_product(left, right, left_dim=1, right_dim=0):
    return joined_product(split_two(left), split_two(right), left_dim, right_dim)


def ones_product(ones, value):
    return product(jnp.concatenate([ones] * 3, 1), jnp.concatenate(split_three(value), 0), 1, 0)


def spread(per_head, lane):
    return jnp.concatenate(
        [
            jnp.where(lane < P_SIZE, per_head[:, 2 * k : 2 * k + 1], per_head[:, 2 * k + 1 : 2 * k + 2])
            for k in range(OWN_H // 2)
        ],
        1,
    )


def head_sums(value):
    column = lax.broadcasted_iota(jnp.int32, (OWN, N), 0)
    head = lax.broadcasted_iota(jnp.int32, (OWN, N), 1)
    members = ((column >= head * P_SIZE) & (column < (head + 1) * P_SIZE)).astype(F32).astype(BF16)
    high, low = split_two(value)
    return product(jnp.concatenate([high, low], 1), jnp.concatenate([members, members], 0), 1, 0)


def two_heads(pair, lane):
    zero = jnp.zeros_like(pair)
    return jnp.concatenate([jnp.where(lane < P_SIZE, pair, zero), jnp.where(lane < P_SIZE, zero, pair)], 0)


def chunk_facts(ends, chunk, dt_pre, par):
    column = lax.broadcasted_iota(jnp.int32, (CHUNK, 1), 0) + chunk * CHUNK
    row = lax.broadcasted_iota(jnp.int32, (1, CHUNK), 1) + chunk * CHUNK

    def segment(position):
        counted = jnp.zeros_like(position)
        for k in range(3):
            counted = counted + (position >= ends[k]).astype(jnp.int32)
        return jnp.where(position < 0, -1, counted)

    def one_segment(position):
        counted = jnp.int32(0)
        for k in range(3):
            counted = counted + (position >= ends[k]).astype(jnp.int32)
        return jnp.where(position < 0, -1, counted)

    here_column, here_row = segment(column), segment(row)
    prior = one_segment(chunk * CHUNK - 1)
    last = one_segment(chunk * CHUNK + CHUNK - 1)
    lane = lax.broadcasted_iota(jnp.int32, (CHUNK, N), 1)
    shifted = dt_pre + par[6:7, :N]
    soft = jnp.maximum(shifted, 0.0) + jnp.log1p(jnp.exp(-jnp.abs(shifted)))
    step = jnp.where(lane < OWN_H, soft, 0.0)
    decay = step * par[7:8, :N]
    tri_row = lax.broadcasted_iota(jnp.int32, (CHUNK, CHUNK), 0)
    tri_column = lax.broadcasted_iota(jnp.int32, (CHUNK, CHUNK), 1)
    lower = (tri_row >= tri_column).astype(F32).astype(BF16)
    upper = (tri_row <= tri_column).astype(F32).astype(BF16)
    total = ones_product(lower, decay)
    entering = (here_column == prior).astype(F32) * jnp.exp(total)
    end = total[CHUNK - 1 : CHUNK]
    leaving = (here_column == last).astype(F32) * jnp.exp(jnp.minimum(end - total, 0.0))
    passing = jnp.where(last == prior, 1.0, 0.0) * jnp.exp(end)
    return dict(
        column=column,
        segment=segment,
        here_column=here_column,
        here_row=here_row,
        lane=lane,
        shifted=shifted,
        step=step,
        decay=decay,
        total=total,
        entering=entering,
        leaving=leaving,
        passing=passing,
        tri_row=tri_row,
        tri_column=tri_column,
        upper=upper,
    )


def forward_kernel(part, ends, proj, par, *refs):
    if part:
        carry_in, refs = refs[3], refs[4:]
    pre_out, mixed_out, state_out, carry_out, extended, state = refs
    chunk = pl.program_id(0) + part * HALF

    @pl.when(pl.program_id(0) == 0)
    def _():
        if part:
            state[...] = carry_in[:N, :OWN]
            extended[0:8, :] = carry_in[N:, :]
        else:
            state[...] = jnp.zeros_like(state)
            extended[0:8, :] = jnp.zeros((8, 640), F32)

    facts = chunk_facts(ends, chunk, proj[:, 1024:1152], par)
    lane = facts["lane"]
    conv = proj[:, OWN:1024].astype(BF16).astype(F32)
    extended[8 : 8 + CHUNK, :] = conv
    pre = par[4:5] + par[3:4] * conv
    for back in range(1, CONV):
        same = (facts["segment"](facts["column"] - back) == facts["here_column"]).astype(F32)
        pre = pre + par[3 - back : 4 - back] * (extended[8 - back : 8 - back + CHUNK, :] * same)
    extended[0:8, :] = extended[CHUNK : CHUNK + 8, :]
    pre_out[...] = pre
    act = pre * jax.nn.sigmoid(pre)
    own_x, state_b, state_c = act[:, :OWN], act[:, OWN : OWN + N], act[:, OWN + N :]
    stepped = own_x * spread(facts["step"], lane)
    b_parts, c_parts = split_two(state_b), split_two(state_c)
    inside = (facts["tri_row"] >= facts["tri_column"]) & (facts["here_column"] == facts["here_row"])
    scores = jnp.where(inside, joined_product(c_parts, b_parts, 1, 1), 0.0)
    total_rows = facts["total"].T
    state_in = state[...]
    state_out[...] = state_in
    outs = []
    for pair in range(OWN_H // 2):
        mixing = []
        for head in (2 * pair, 2 * pair + 1):
            span = facts["total"][:, head : head + 1] - total_rows[head : head + 1, :]
            mixing.append(jnp.exp(jnp.minimum(span, 0.0)) * scores)
        inner = two_heads(stepped[:, pair * N : pair * N + N], lane)
        outs.append(precise_product(jnp.concatenate(mixing, 1), inner))
    scanned = jnp.concatenate(outs, 1) + spread(facts["entering"], lane) * joined_product(
        c_parts, split_two(state_in)
    )
    state[...] = spread(facts["passing"], lane[:1]) * state_in + precise_product(
        state_b.T, stepped * spread(facts["leaving"], lane)
    )
    mixed_out[...] = scanned + par[5:6, :OWN] * own_x

    @pl.when(pl.program_id(0) == HALF - 1)
    def _():
        carry_out[:N, :OWN] = state[...]
        carry_out[:N, OWN:] = jnp.zeros((N, 640 - OWN), F32)
        carry_out[N:, :] = extended[0:8, :]


def run_forward(part, ends, proj, par, before=()):
    here = lambda i: (i + part * HALF, 0)
    chunked = lambda width: pl.BlockSpec((CHUNK, width), here)
    fixed = lambda shape: pl.BlockSpec(shape, lambda i: (0, 0))
    carry = fixed((N + 8, 640))
    return pl.pallas_call(
        partial(forward_kernel, part),
        grid=(HALF,),
        in_specs=[pl.BlockSpec(memory_space=pltpu.SMEM), chunked(1152), fixed((16, 640))]
        + ([pl.BlockSpec(memory_space=pl.ANY)] * 3 + [carry] if part else []),
        out_specs=[chunked(640), chunked(OWN), pl.BlockSpec((N, OWN), here), carry],
        out_shape=[
            jax.ShapeDtypeStruct((PACK, 640), F32),
            jax.ShapeDtypeStruct((PACK, OWN), F32),
            jax.ShapeDtypeStruct((CHUNKS * N, OWN), F32),
            jax.ShapeDtypeStruct((N + 8, 640), F32),
        ],
        input_output_aliases={3: 0, 4: 1, 5: 2} if part else {},
        scratch_shapes=[pltpu.VMEM((CHUNK + 8, 640), F32), pltpu.VMEM((N, OWN), F32)],
        compiler_params=pltpu.CompilerParams(
            dimension_semantics=("arbitrary",), vmem_limit_bytes=VMEM_LIMIT
        ),
        cost_estimate=COST,
        name="scan_forward",
    )(ends, proj, par, *before)


def backward_kernel(ends, conv_in, dt_in, pre_in, mixed_in, grad_mixed, state_all, par, *refs):
    grad_x, grad_dt, grad_bc, sums, head_acc, carried, extended, end_dot = refs
    step_index = pl.program_id(0)
    chunk = CHUNKS - 1 - step_index

    @pl.when(step_index == 0)
    def _():
        carried[...] = jnp.zeros_like(carried)
        extended[CHUNK : CHUNK + 8, :] = jnp.zeros((8, OWN), F32)
        end_dot[...] = jnp.zeros_like(end_dot)
        sums[...] = jnp.zeros_like(sums)
        head_acc[...] = jnp.zeros_like(head_acc)

    facts = chunk_facts(ends, chunk, dt_in[...], par)
    lane = facts["lane"]
    pre = pre_in[...]
    sig = jax.nn.sigmoid(pre)
    act = pre * sig
    own_x, state_b, state_c = act[:, :OWN], act[:, OWN : OWN + N], act[:, OWN + N :]
    step = facts["step"]
    step_wide = spread(step, lane)
    stepped = own_x * step_wide
    skip = par[5:6, :OWN]
    scanned = mixed_in[...] - skip * own_x
    grad_m = grad_mixed[...]
    sums[6:7] += jnp.sum(grad_m * own_x, 0, keepdims=True)

    b_parts, c_parts = split_two(state_b), split_two(state_c)
    inside = (facts["tri_row"] <= facts["tri_column"]) & (facts["here_column"] == facts["here_row"])
    scores = jnp.where(inside, joined_product(b_parts, c_parts, 1, 1), 0.0)
    total_rows = facts["total"].T
    grad_scores = jnp.zeros((CHUNK, CHUNK), F32)
    grad_stepped = []
    for pair in range(OWN_H // 2):
        columns = slice(pair * N, pair * N + N)
        grad_pair = grad_m[:, columns]
        high, low = split_two(grad_pair)
        stepped_parts = split_two(two_heads(stepped[:, columns], lane))
        grad_mixing = joined_product(stepped_parts, (high, low), 1, 1)
        mixing = []
        for k in range(2):
            head = 2 * pair + k
            span = total_rows[head : head + 1, :] - facts["total"][:, head : head + 1]
            decays = jnp.exp(jnp.minimum(span, 0.0))
            mixing.append(decays * scores)
            grad_scores = grad_scores + decays * grad_mixing[k * CHUNK : (k + 1) * CHUNK]
        grad_stepped.append(
            joined_product(
                split_two(jnp.concatenate(mixing, 1)), (two_heads(high, lane), two_heads(low, lane))
            )
        )
    grad_scores = jnp.where(inside, grad_scores, 0.0)
    carry = carried[...]
    carry_parts = split_two(carry)
    leaving = spread(facts["leaving"], lane)
    grad_stepped = jnp.concatenate(grad_stepped, 1) + leaving * joined_product(b_parts, carry_parts)
    state_in = state_all[...]
    entered = spread(facts["entering"], lane) * grad_m
    entered_parts = split_two(entered)
    grad_b = precise_product(grad_scores, state_c) + joined_product(
        split_two(leaving * stepped), carry_parts, 1, 1
    )
    grad_c = precise_product(grad_scores.T, state_b) + joined_product(
        entered_parts, split_two(state_in), 1, 1
    )
    grad_bc[0:N, :] = grad_b.T
    grad_bc[N:, :] = grad_c.T
    new_carry = spread(facts["passing"], lane[:1]) * carry + joined_product(
        split_two(state_c.T), entered_parts
    )
    carried[...] = new_carry

    grad_step = head_sums(own_x * grad_stepped)
    last_row = lax.broadcasted_iota(jnp.int32, (CHUNK, N), 0) == CHUNK - 1
    grad_total = head_sums(grad_m * scanned) - step * grad_step
    grad_total = grad_total + jnp.where(last_row, end_dot[0:1, :], 0.0)
    grad_decay = ones_product(facts["upper"], grad_total)
    end_dot[...] = head_sums(
        jnp.broadcast_to(jnp.sum(new_carry * state_in, 0, keepdims=True), (8, OWN))
    )
    grad_pre_dt = (grad_step + grad_decay * par[7:8, :N]) * jax.nn.sigmoid(facts["shifted"])
    grad_pre_dt = jnp.where(lane < OWN_H, grad_pre_dt, 0.0)
    grad_dt[...] = grad_pre_dt.astype(BF16)
    head_acc[0:1] += jnp.sum(grad_pre_dt, 0, keepdims=True)
    head_acc[1:2] += jnp.sum(grad_decay * facts["decay"], 0, keepdims=True)

    sig_x, pre_x = sig[:, :OWN], pre[:, :OWN]
    grad_pre = (step_wide * grad_stepped + skip * grad_m) * (sig_x * (1.0 + pre_x * (1.0 - sig_x)))
    extended[0:CHUNK, :] = grad_pre
    conv = conv_in[...].astype(BF16).astype(F32)
    sums[5:6] += jnp.sum(grad_pre, 0, keepdims=True)
    sums[4:5] += jnp.sum(conv * grad_pre, 0, keepdims=True)
    grad_conv = par[3:4, :OWN] * grad_pre
    for ahead in range(1, CONV):
        same = (facts["segment"](facts["column"] + ahead) == facts["here_column"]).astype(F32)
        later = extended[ahead : ahead + CHUNK, :] * same
        sums[4 - ahead : 5 - ahead] += jnp.sum(conv * later, 0, keepdims=True)
        grad_conv = grad_conv + par[3 - ahead : 4 - ahead, :OWN] * later
    extended[CHUNK : CHUNK + 8, :] = extended[0:8, :]
    grad_x[...] = grad_conv.astype(BF16)


def run_backward(ends, proj, pre, mixed, grad_mixed, states, par):
    last = CHUNKS - 1
    chunked = lambda width, column=0: pl.BlockSpec((CHUNK, width), lambda i: (last - i, column))
    fixed = lambda shape: pl.BlockSpec(shape, lambda i: (0, 0))
    return pl.pallas_call(
        backward_kernel,
        grid=(CHUNKS,),
        in_specs=[
            pl.BlockSpec(memory_space=pltpu.SMEM),
            chunked(OWN, 1),
            chunked(N, 8),
            chunked(640),
            chunked(OWN),
            chunked(OWN),
            pl.BlockSpec((N, OWN), lambda i: (last - i, 0)),
            fixed((16, 640)),
        ],
        out_specs=[
            chunked(OWN),
            chunked(N),
            pl.BlockSpec((2 * N, CHUNK), lambda i: (0, last - i)),
            fixed((8, OWN)),
            fixed((8, N)),
        ],
        out_shape=[
            jax.ShapeDtypeStruct((PACK, OWN), BF16),
            jax.ShapeDtypeStruct((PACK, N), BF16),
            jax.ShapeDtypeStruct((2 * N, PACK), F32),
            jax.ShapeDtypeStruct((8, OWN), F32),
            jax.ShapeDtypeStruct((8, N), F32),
        ],
        scratch_shapes=[
            pltpu.VMEM((N, OWN), F32),
            pltpu.VMEM((CHUNK + 8, OWN), F32),
            pltpu.VMEM((8, N), F32),
        ],
        compiler_params=pltpu.CompilerParams(
            dimension_semantics=("arbitrary",), vmem_limit_bytes=VMEM_LIMIT
        ),
        cost_estimate=COST,
        name="scan_backward",
    )(ends, proj, proj, pre, mixed, grad_mixed, states, par)


PARTS = (1, 1, 1, 1, 1, 2, 1, 1)


def piece_copies(pieces, parts, blocks, sems):
    copies = []
    taken = 0
    for slot, count in enumerate(parts):
        rows = ROWS // count
        copies.append(
            [
                pltpu.make_async_copy(
                    pieces[taken + k], blocks.at[slot, pl.ds(k * rows, rows)], sems.at[taken + k]
                )
                for k in range(count)
            ]
        )
        taken += count
    return copies


def fetch_block(pieces, parts, blocks, sems):
    copies = piece_copies(pieces, parts, blocks, sems)
    step = pl.program_id(0)

    @pl.when(step == 0)
    def _():
        for group in copies:
            for copy in group:
                copy.start()

    for slot, group in enumerate(copies):

        @pl.when(step == slot)
        def _(group=group):
            for copy in group:
                copy.wait()

    return blocks[step]


def project_kernel(parts, table, *refs):
    pieces = refs[: sum(parts)]
    gain, shards, normed_out, proj, dt_out, blocks, weight, sems = refs[sum(parts) :]
    block = fetch_block(pieces, parts, blocks, sems)

    @pl.when(pl.program_id(0) == 0)
    def _():
        for f in range(N_FSDP):
            weight[f * SHARD_IN : (f + 1) * SHARD_IN, :] = shards[(f // 2) % 4, f % 2, f // 8, :SHARD_IN]
        dt_out[...] = weight[:, 1024:]

    values = block.astype(F32)
    scale = lax.rsqrt(jnp.mean(values * values, axis=1, keepdims=True) + NORM_EPS)
    normed = (values * scale * gain[...]).astype(BF16)
    normed_out[...] = normed
    proj[...] = matmul(normed, weight[...])


def run_project(table, pieces, gain, shards):
    fixed = lambda shape: pl.BlockSpec(shape, lambda i, table: (0,) * len(shape))
    placed = lambda width: pl.BlockSpec((ROWS, width), lambda i, table: (table[i], 0))
    return pl.pallas_call(
        partial(project_kernel, PARTS),
        grid_spec=pltpu.PrefetchScalarGridSpec(
            num_scalar_prefetch=1,
            grid=(N_REP,),
            in_specs=[pl.BlockSpec(memory_space=pl.ANY)] * len(pieces) + [fixed((1, D)), fixed(shards.shape)],
            out_specs=[placed(D), placed(3 * WIDE), fixed((D, N))],
            scratch_shapes=[
                pltpu.VMEM((N_REP, ROWS, D), BF16),
                pltpu.VMEM((D, 3 * WIDE), BF16),
                pltpu.SemaphoreType.DMA((len(pieces),)),
            ],
        ),
        out_shape=[
            jax.ShapeDtypeStruct((PACK, D), BF16),
            jax.ShapeDtypeStruct((PACK, 3 * WIDE), F32),
            jax.ShapeDtypeStruct((D, N), BF16),
        ],
        compiler_params=pltpu.CompilerParams(
            dimension_semantics=("arbitrary",), vmem_limit_bytes=VMEM_LIMIT
        ),
        cost_estimate=COST,
        name="project",
    )(table, *pieces, gain, shards)


def row_sums(value):
    folded = value[:, :N] + value[:, N : 2 * N] + value[:, 2 * N :]
    return jnp.sum(folded.T, 0, keepdims=True)


def out_grad_kernel(table, *refs):
    pieces = refs[: sum(PARTS)]
    w_out, mixed, gate_in, gain, branch_out, grad_out, sums, blocks, turned, sems = refs[sum(PARTS) :]
    branch = fetch_block(pieces, PARTS, blocks, sems)

    @pl.when(pl.program_id(0) == 0)
    def _():
        turned[...] = w_out[...].reshape(OWN, D).T

    branch_out[...] = branch
    total = matmul(branch, turned[...])
    grad_out[...] = total
    gate = gate_in[...]
    gated = mixed[...] * (gate * jax.nn.sigmoid(gate))
    row = lax.broadcasted_iota(jnp.int32, (8, ROWS), 0)
    sums[...] = jnp.where(
        row == 0, row_sums(gated * gated), jnp.where(row == 1, row_sums(total * gain[...] * gated), 0.0)
    )


def run_out_grad(table, pieces, w_out, mixed, proj, gain):
    fixed = lambda shape: pl.BlockSpec(shape, lambda i, table: (0, 0))
    placed = lambda width: pl.BlockSpec((ROWS, width), lambda i, table: (table[i], 0))
    own = pl.BlockSpec(
        (1, 2, 1, SHARD_OUT, D), lambda i, table: (table[N_REP] % 4, 0, table[N_REP] // 4, 0, 0)
    )
    return pl.pallas_call(
        out_grad_kernel,
        grid_spec=pltpu.PrefetchScalarGridSpec(
            num_scalar_prefetch=1,
            grid=(N_REP,),
            in_specs=[pl.BlockSpec(memory_space=pl.ANY)] * len(pieces)
            + [own, placed(OWN), placed(OWN), fixed((1, OWN))],
            out_specs=[placed(D), placed(OWN), pl.BlockSpec((8, ROWS), lambda i, table: (0, table[i]))],
            scratch_shapes=[
                pltpu.VMEM((N_REP, ROWS, D), BF16),
                pltpu.VMEM((D, WIDE), BF16),
                pltpu.SemaphoreType.DMA((len(pieces),)),
            ],
        ),
        out_shape=[
            jax.ShapeDtypeStruct((PACK, D), BF16),
            jax.ShapeDtypeStruct((PACK, OWN), F32),
            jax.ShapeDtypeStruct((8, PACK), F32),
        ],
        compiler_params=pltpu.CompilerParams(
            dimension_semantics=("arbitrary",), vmem_limit_bytes=VMEM_LIMIT
        ),
        cost_estimate=COST,
        name="out_grad",
    )(table, *pieces, w_out, mixed, proj, gain)


def gate_kernel(grad_out, mixed_in, gate_in, sums, gain, low_out, grad_mixed, grad_gain):
    rows = grad_out.shape[0]
    mixed, gate, grad_o = mixed_in[...], gate_in[...], grad_out[...]
    stats = jnp.concatenate([sums[...], jnp.zeros((N - 8, rows), F32)], 0).T
    out_scale = lax.rsqrt(stats[:, 0:1] * (1.0 / DI) + NORM_EPS)
    pull = out_scale * out_scale * out_scale * (stats[:, 1:2] * (1.0 / DI))
    gate_sig = jax.nn.sigmoid(gate)
    silu = gate * gate_sig
    gated = mixed * silu
    unit = gated * out_scale
    grad_gated = out_scale * (grad_o * gain[...]) - gated * pull
    grad_mixed[...] = grad_gated * silu
    low_out[:, :OWN] = (unit * gain[...]).astype(BF16)
    low_out[:, OWN:] = (grad_gated * mixed * (gate_sig * (1.0 + gate * (1.0 - gate_sig)))).astype(BF16)
    gain_part = jnp.sum(grad_o * unit, 0, keepdims=True)

    @pl.when(pl.program_id(0) == 0)
    def _():
        grad_gain[...] = jnp.broadcast_to(gain_part, grad_gain.shape)

    @pl.when(pl.program_id(0) > 0)
    def _():
        grad_gain[...] += gain_part


def run_gate(grad_out, mixed, proj, sums, gain):
    rows = lambda width: pl.BlockSpec((ROWS, width), lambda i: (i, 0))
    fixed = lambda shape: pl.BlockSpec(shape, lambda i: (0, 0))
    return pl.pallas_call(
        gate_kernel,
        grid=(PACK // ROWS,),
        in_specs=[
            rows(OWN),
            rows(OWN),
            rows(OWN),
            pl.BlockSpec((8, ROWS), lambda i: (0, i)),
            fixed((1, OWN)),
        ],
        out_specs=[rows(2 * OWN), rows(OWN), fixed((8, OWN))],
        out_shape=[
            jax.ShapeDtypeStruct((PACK, 2 * OWN), BF16),
            jax.ShapeDtypeStruct((PACK, OWN), F32),
            jax.ShapeDtypeStruct((8, OWN), F32),
        ],
        compiler_params=pltpu.CompilerParams(
            dimension_semantics=("arbitrary",), vmem_limit_bytes=VMEM_LIMIT
        ),
        cost_estimate=COST,
        name="gate_backward",
    )(grad_out, mixed, proj, sums, gain)


def early_grad_kernel(low, grad_branch, normed, out):
    step = pl.program_id(0)

    @pl.when(step == 0)
    def _():
        out[...] = jnp.zeros_like(out)

    for k in range(4):
        part = product(low[:, :OWN], grad_branch[:, k * WIDE : (k + 1) * WIDE], 0, 0)
        for m in range(4):
            out[eight_order(4 * k + m), :SHARD_IN] += part[m * SHARD_IN : (m + 1) * SHARD_IN]
    part = product(normed[...], low[:, OWN:], 0, 0)
    for f in range(N_FSDP):
        out[eight_order(f), SHARD_IN:] += part[f * SHARD_IN : (f + 1) * SHARD_IN]


def run_early_grad(low, grad_branch, normed):
    count = 2 * ROWS
    rows = lambda width: pl.BlockSpec((count, width), lambda i: (i, 0))
    shape = (N_FSDP, 2 * SHARD_IN, WIDE)
    return pl.pallas_call(
        early_grad_kernel,
        grid=(PACK // count,),
        in_specs=[rows(2 * OWN), rows(D), rows(D)],
        out_specs=pl.BlockSpec(shape, lambda i: (0, 0, 0)),
        out_shape=jax.ShapeDtypeStruct(shape, F32),
        compiler_params=pltpu.CompilerParams(
            dimension_semantics=("arbitrary",), vmem_limit_bytes=VMEM_LIMIT
        ),
        cost_estimate=COST,
        name="early_grad",
    )(low, grad_branch, normed)


def block_out_kernel(rows, weight, tokens, live, out):
    step = pl.program_id(0)
    part = matmul(jnp.concatenate([rows[0], rows[1]], 1), weight[...].reshape(2 * OWN, D))

    @pl.when(step == 0)
    def _():
        out[...] = part

    @pl.when(step > 0)
    def _():
        out[...] += part

    @pl.when(step == N_REP // 2 - 1)
    def _():
        out[...] = tokens[...].astype(F32) + live[...] * out[...]


def run_block_out(rows, weight, tokens, live):
    fixed = lambda shape: pl.BlockSpec(shape, lambda i: (0, 0))
    return pl.pallas_call(
        block_out_kernel,
        grid=(N_REP // 2,),
        in_specs=[
            pl.BlockSpec((2, ROWS, OWN), lambda i: (i, 0, 0)),
            pl.BlockSpec((2, 2, 1, SHARD_OUT, D), lambda i: (i % 2, 0, i // 2, 0, 0)),
            fixed((ROWS, D)),
            fixed((ROWS, 1)),
        ],
        out_specs=fixed((ROWS, D)),
        out_shape=jax.ShapeDtypeStruct((ROWS, D), F32),
        compiler_params=pltpu.CompilerParams(
            dimension_semantics=("arbitrary",), vmem_limit_bytes=VMEM_LIMIT
        ),
        cost_estimate=FILL,
        name="block_out",
    )(rows, weight, tokens, live)


def turned_part(weight, rows):
    return product(weight[...].reshape(D, weight.shape[-1]), rows, 1, 1)


def columns_of(full_in, width, index):
    return pl.BlockSpec(full_in.shape[:-1] + (width,), lambda i: (0, 0, 0, 0, index(i)))


def z_grad_kernel(rows, weight, out):
    part = turned_part(weight, jnp.concatenate([rows[0], rows[1]], 1))

    @pl.when(pl.program_id(0) == 0)
    def _():
        out[...] = part

    @pl.when(pl.program_id(0) > 0)
    def _():
        out[...] += part


def run_z_grad(rows, full_in):
    return pl.pallas_call(
        z_grad_kernel,
        grid=(N_REP // 2,),
        in_specs=[
            pl.BlockSpec((2, ROWS, OWN), lambda i: (i, 0, 1)),
            columns_of(full_in, 2 * OWN, lambda i: i),
        ],
        out_specs=pl.BlockSpec((D, ROWS), lambda i: (0, 0)),
        out_shape=jax.ShapeDtypeStruct((D, ROWS), F32),
        compiler_params=pltpu.CompilerParams(
            dimension_semantics=("arbitrary",), vmem_limit_bytes=VMEM_LIMIT
        ),
        cost_estimate=FILL,
        name="z_grad",
    )(rows, full_in)


def input_grad_kernel(
    own_half, grad_z, x_rows, rest_rows, w_x, w_bc, low_dt, tokens, cotangent, gain, out, gain_out, total, ordered
):
    step = pl.program_id(0)
    part = turned_part(w_x, jnp.concatenate([x_rows[0], x_rows[1]], 1))

    @pl.when(step == 0)
    def _():
        total[...] = grad_z[...] + part

    @pl.when(step > 0)
    def _():
        total[...] += part

    @pl.when(step == N_REP // 2 - 1)
    def _():
        lane = lax.broadcasted_iota(jnp.int32, (ROWS, N), 1)
        groups = []
        for k in range(2):
            group = jnp.zeros((ROWS, N), F32)
            for m in range(4):
                value = rest_rows[4 * k + m].astype(F32)
                value = value if m == 0 else pltpu.roll(value, m * OWN_BC, 1)
                group = jnp.where((lane >= m * OWN_BC) & (lane < (m + 1) * OWN_BC), value, group)
            groups.append(group.astype(BF16))
        steps = jnp.zeros((ROWS, N), F32)
        for m in range(N_REP):
            start = 8 + m * OWN_H
            value = pltpu.roll(rest_rows[m].astype(F32), (start - OWN_BC) % N, 1)
            steps = jnp.where((lane >= start) & (lane < start + OWN_H), value, steps)
        total[...] += turned_part(w_bc, jnp.concatenate(groups, 1))
        for f in range(N_FSDP):
            place = eight_order(f) - f // 8 + (f // 8 + own_half[0]) % 2
            start = pl.multiple_of(place * SHARD_IN, SHARD_IN)
            ordered[f * SHARD_IN : (f + 1) * SHARD_IN, :] = total[pl.ds(start, SHARD_IN), :]
        grad_h = (ordered[...] + product(low_dt[...], steps.astype(BF16), 1, 1)).T
        values = tokens[...].astype(F32)
        scale = lax.rsqrt(jnp.mean(values * values, axis=1, keepdims=True) + NORM_EPS)
        unit = values * scale
        gain_sum = jnp.sum(grad_h * unit, 0, keepdims=True)
        gain_out[...] = jnp.zeros_like(gain_out)
        for k in range(D // TAIL):
            gain_out[k : k + 1, :] = gain_sum[:, k * TAIL : (k + 1) * TAIL]
        grad_unit = grad_h * gain[...]
        inner = jnp.mean(grad_unit * unit, axis=1, keepdims=True)
        out[...] = cotangent[...].astype(F32) + scale * (grad_unit - unit * inner)


def run_input_grad(own_half, grad_z, tail_rows, full_in, low_dt, tokens, cotangent, gain):
    fixed = lambda shape: pl.BlockSpec(shape, lambda i: (0,) * len(shape))
    return pl.pallas_call(
        input_grad_kernel,
        grid=(N_REP // 2,),
        in_specs=[
            pl.BlockSpec(memory_space=pltpu.SMEM),
            fixed((D, ROWS)),
            pl.BlockSpec((2, ROWS, OWN), lambda i: (i, 0, 0)),
            pl.BlockSpec((N_REP, ROWS, N), lambda i: (0, 0, OWN // N)),
            columns_of(full_in, 2 * OWN, lambda i: N_REP // 2 + i),
            columns_of(full_in, 2 * N, lambda i: DI // N),
            fixed((D, N)),
            fixed((ROWS, D)),
            fixed((ROWS, D)),
            fixed((1, D)),
        ],
        out_specs=[fixed((ROWS, D)), fixed((8, TAIL))],
        out_shape=[jax.ShapeDtypeStruct((ROWS, D), F32), jax.ShapeDtypeStruct((8, TAIL), F32)],
        scratch_shapes=[pltpu.VMEM((D, ROWS), F32), pltpu.VMEM((D, ROWS), F32)],
        compiler_params=pltpu.CompilerParams(
            dimension_semantics=("arbitrary",), vmem_limit_bytes=VMEM_LIMIT
        ),
        cost_estimate=COST,
        name="input_grad",
    )(own_half, grad_z, tail_rows, tail_rows, full_in, full_in, low_dt, tokens, cotangent, gain)


def rest_kernel(
    ends, parts, pre_b, pre_c, conv_in, par, grad_x, grad_dt, sums, head_acc, grad_gain, first, tail_out, small_out
):
    own = lax.broadcasted_iota(jnp.int32, (OWN_BC, 2 * N), 0) + first[0]
    chosen = (lax.broadcasted_iota(jnp.int32, (OWN_BC, 2 * N), 1) == own).astype(F32).astype(BF16)

    def pick(value):
        return product(jnp.concatenate([chosen] * 3, 1), jnp.concatenate(split_three(value), 1), 1, 1)

    grad = parts[0]
    for k in range(1, N_REP):
        grad = grad + parts[k]
    own_pre = pick(jnp.concatenate([pre_b[...], pre_c[...]], 1))
    own_conv = product(chosen, conv_in[...].astype(BF16), 1, 1)
    taps = pick(par[:, OWN:])
    sig = jax.nn.sigmoid(own_pre)
    grad_pre = grad * (sig * (1.0 + own_pre * (1.0 - sig)))
    position = lax.broadcasted_iota(jnp.int32, (1, PACK), 1)

    def segment(places):
        counted = jnp.zeros_like(places)
        for k in range(3):
            counted = counted + (places >= ends[k]).astype(jnp.int32)
        return counted

    grad_conv = taps[:, CONV - 1 : CONV] * grad_pre
    column = lax.broadcasted_iota(jnp.int32, (OWN_BC, N), 1)
    found = jnp.where(column == CONV, jnp.sum(grad_pre, 1, keepdims=True), 0.0)
    found = jnp.where(column == CONV - 1, jnp.sum(own_conv * grad_pre, 1, keepdims=True), found)
    for later_by in range(1, CONV):
        same = (segment(position + later_by) == segment(position)) & (position < PACK - later_by)
        later = jnp.where(same, pltpu.roll(grad_pre, PACK - later_by, 1), 0.0)
        tap = CONV - 1 - later_by
        found = jnp.where(column == tap, jnp.sum(own_conv * later, 1, keepdims=True), found)
        grad_conv = grad_conv + taps[:, tap : tap + 1] * later
    lane = lax.broadcasted_iota(jnp.int32, (N, N), 1)
    filler = jnp.zeros((N - OWN_BC, N), F32)
    for k in range(PACK // N):
        rows = slice(k * N, (k + 1) * N)
        columns = jnp.concatenate([grad_conv[:, rows], filler], 0).T
        steps = pltpu.roll(grad_dt[rows, :].astype(F32), OWN_BC, 1)
        tail_out[rows, :OWN] = grad_x[rows, :]
        tail_out[rows, OWN:] = jnp.where(
            lane < OWN_BC, columns, jnp.where(lane < OWN_BC + OWN_H, steps, 0.0)
        ).astype(BF16)
    row = lax.broadcasted_iota(jnp.int32, (8, OWN), 0)
    skip = head_sums(sums[...])
    by_head = jnp.concatenate([skip, jnp.zeros((8, OWN - N), F32)], 1)
    logs = jnp.concatenate([head_acc[...], jnp.zeros((8, OWN - N), F32)], 1)
    wide = jnp.where(row == 0, grad_gain[0:1, :], jnp.where(row < 6, sums[...], 0.0))
    wide = jnp.where(row == 6, logs[1:2, :], jnp.where(row == 7, by_head[6:7, :], wide))
    turned = jnp.concatenate([found, filler], 0).T
    first_row = lax.broadcasted_iota(jnp.int32, (8, N), 0) == 0
    small_out[:, :OWN] = wide
    small_out[:, OWN:] = jnp.where(first_row, head_acc[0:1, :], pltpu.roll(turned[:8], 1, 0))


def run_rest(ends, parts, pre, proj, par, grad_x, grad_dt, sums, head_acc, grad_gain, first):
    fixed = lambda shape: pl.BlockSpec(shape, lambda i: (0,) * len(shape))
    return pl.pallas_call(
        rest_kernel,
        grid=(1,),
        in_specs=[
            pl.BlockSpec(memory_space=pltpu.SMEM),
            fixed((N_REP, OWN_BC, PACK)),
            pl.BlockSpec((PACK, N), lambda i: (0, 3)),
            pl.BlockSpec((PACK, N), lambda i: (0, 4)),
            pl.BlockSpec((PACK, 2 * N), lambda i: (0, 3)),
            fixed((16, 640)),
            fixed((PACK, OWN)),
            fixed((PACK, N)),
            fixed((8, OWN)),
            fixed((8, N)),
            fixed((8, OWN)),
            pl.BlockSpec(memory_space=pltpu.SMEM),
        ],
        out_specs=[fixed((PACK, TAIL)), fixed((8, TAIL))],
        out_shape=[jax.ShapeDtypeStruct((PACK, TAIL), BF16), jax.ShapeDtypeStruct((8, TAIL), F32)],
        compiler_params=pltpu.CompilerParams(
            dimension_semantics=("arbitrary",), vmem_limit_bytes=VMEM_LIMIT
        ),
        cost_estimate=COST,
        name="rest_backward",
    )(ends, parts, pre, pre, proj, par, grad_x, grad_dt, sums, head_acc, grad_gain, first)


def tail_grad_kernel(normed, tail, small, out):
    step = pl.program_id(0)
    part = product(normed[...], tail[...], 0, 0)
    for f in range(N_FSDP):
        rows = part[f * SHARD_IN : (f + 1) * SHARD_IN]

        @pl.when(step == 0)
        def _(f=f, rows=rows):
            out[eight_order(f), :SHARD_IN] = rows
            out[eight_order(f), SHARD_IN:] = small[...]

        @pl.when(step > 0)
        def _(f=f, rows=rows):
            out[eight_order(f), :SHARD_IN] += rows


def run_tail_grad(normed, tail, small):
    count = 2 * ROWS
    shape = (N_FSDP, SHARD_IN + 8, TAIL)
    return pl.pallas_call(
        tail_grad_kernel,
        grid=(PACK // count,),
        in_specs=[
            pl.BlockSpec((count, D), lambda i: (i, 0)),
            pl.BlockSpec((count, TAIL), lambda i: (i, 0)),
            pl.BlockSpec((8, TAIL), lambda i: (0, 0)),
        ],
        out_specs=pl.BlockSpec(shape, lambda i: (0, 0, 0)),
        out_shape=jax.ShapeDtypeStruct(shape, F32),
        compiler_params=pltpu.CompilerParams(
            dimension_semantics=("arbitrary",), vmem_limit_bytes=VMEM_LIMIT
        ),
        cost_estimate=COST,
        name="tail_grad",
    )(normed, tail, small)


def adam_step(grad, weight, first, second, grad_out, first_out, second_out, weight_out):
    new_weight, new_first, new_second = adam_update(
        weight[...], grad, first[...], second[...], RATE_MATRIX, WEIGHT_DECAY
    )
    grad_out[...] = grad
    first_out[...] = new_first
    second_out[...] = new_second
    weight_out[...] = new_weight


def adam_early_kernel(rows, pair, *refs):
    arrays, grad = refs[:-1], refs[-1]
    grad[:, :WIDE] = pair[0, rows, :]
    grad[:, WIDE:] = pair[1, rows, :]
    adam_step(grad[...], *arrays)


def run_adam_early(place_of, rows, parts, weight, first, second):
    part = pl.BlockSpec((SHARD_IN, 2 * WIDE), place_of)
    shape = jax.ShapeDtypeStruct(weight.shape, F32)
    return pl.pallas_call(
        partial(adam_early_kernel, rows),
        grid=(N_REP // 2,),
        in_specs=[pl.BlockSpec((2,) + parts.shape[1:], lambda i: (i, 0, 0))] + [part] * 3,
        out_specs=[part] * 4,
        out_shape=[shape] * 4,
        scratch_shapes=[pltpu.VMEM((SHARD_IN, 2 * WIDE), F32)],
        compiler_params=pltpu.CompilerParams(
            dimension_semantics=("arbitrary",), vmem_limit_bytes=VMEM_LIMIT
        ),
        cost_estimate=FILL,
        name="adam",
    )(parts, weight, first, second)


def adam_tail_kernel(pair, rest, *refs):
    arrays, grad = refs[:3] + refs[-5:-1], refs[-1]
    step = pl.program_id(0)

    @pl.when(step < N_REP // 2)
    def _():
        grad[:, :WIDE] = pair[0, :SHARD_IN]
        grad[:, WIDE:] = pair[1, :SHARD_IN]

    @pl.when(step == N_REP // 2)
    def _():
        lane = lax.broadcasted_iota(jnp.int32, (SHARD_IN, N), 1)
        for k in range(2):
            group = jnp.zeros((SHARD_IN, N), F32)
            for m in range(4):
                value = rest[4 * k + m, :SHARD_IN]
                value = value if m == 0 else pltpu.roll(value, m * OWN_BC, 1)
                group = jnp.where((lane >= m * OWN_BC) & (lane < (m + 1) * OWN_BC), value, group)
            grad[:, k * N : (k + 1) * N] = group

    adam_step(grad[...], *arrays)


def run_adam_tail(parts, weight, first, second, before):
    half = N_REP // 2
    rows = parts.shape[1]
    column = pl.BlockSpec((SHARD_IN, 2 * WIDE), lambda i: (0, half + i))
    shape = jax.ShapeDtypeStruct(weight.shape, F32)
    return pl.pallas_call(
        adam_tail_kernel,
        grid=(half + 1,),
        in_specs=[
            pl.BlockSpec((2, rows, OWN), lambda i: (jnp.minimum(i, half - 1), 0, 0)),
            pl.BlockSpec((N_REP, rows, N), lambda i: (0, 0, OWN // N)),
        ]
        + [column] * 3
        + [pl.BlockSpec(memory_space=pl.ANY)] * 4,
        out_specs=[column] * 4,
        out_shape=[shape] * 4,
        input_output_aliases={5 + k: k for k in range(4)},
        scratch_shapes=[pltpu.VMEM((SHARD_IN, 2 * WIDE), F32)],
        compiler_params=pltpu.CompilerParams(
            dimension_semantics=("arbitrary",), vmem_limit_bytes=VMEM_LIMIT
        ),
        cost_estimate=COST,
        name="adam_tail",
    )(parts, parts, weight, first, second, *before)


def body(
    tokens,
    cotangent,
    lengths,
    w_in,
    w_dt,
    w_out,
    small,
    first_in,
    first_dt,
    first_out,
    first_small,
    second_in,
    second_dt,
    second_out,
    second_small,
):
    place = Place()
    r = place.r
    zero = jnp.int32(0)
    pack_lengths = lax.dynamic_slice_in_dim(lengths, place.f, 1, 0)[0]
    seg_ends = jnp.cumsum(pack_lengths)
    own_positions = r * ROWS + jnp.arange(ROWS, dtype=jnp.int32)
    own_live = (segment_at(own_positions, seg_ends) < 3).astype(F32)[:, None]
    slots = jnp.arange(N_REP, dtype=jnp.int32)
    ahead = ((place.x + slots // 2) % 4) * 2 + (place.yl + slots) % 2
    half = ROWS // 2

    in_low = w_in.astype(BF16)
    dt_low = w_dt.astype(BF16)
    out_low = w_out.astype(BF16)

    small_rows = jnp.pad(small.astype(BF16), (0, 16 * 3 * WIDE - SHARD_SMALL)).reshape(16, 3 * WIDE)

    def own_columns(rep):
        columns = jnp.concatenate(
            [
                lax.dynamic_slice_in_dim(in_low, rep * OWN, OWN, 1),
                lax.dynamic_slice_in_dim(in_low, DI + rep * OWN, OWN, 1),
                in_low[:, 2 * DI :],
                lax.dynamic_slice_in_dim(dt_low, rep * OWN_H, OWN_H, 1),
                jnp.zeros((SHARD_IN, 2), BF16),
                dt_low,
                jnp.zeros((SHARD_IN, N - 8 - H), BF16),
            ],
            1,
        )
        return jnp.concatenate([columns, small_rows], 0)

    other_columns = move(
        own_columns(2 * place.x + 1 - place.yl), lambda yh, z, c, x, yl: (yh + 1, z, c, x, yl + 1)
    )
    from_left = move(tokens, along_x(1))
    from_right = move(tokens, along_x(-1))
    partner = move(tokens, swap_y)

    out_low, other_columns = lax.optimization_barrier((out_low, other_columns))
    out_other = move(out_low, lambda yh, z, c, x, yl: (yh + 1, z, c, x, yl + 1))
    branch = (cotangent.astype(F32) * own_live).astype(BF16)
    from_left, from_right, partner, other_columns, branch = lax.optimization_barrier(
        (from_left, from_right, partner, other_columns, branch)
    )
    own_shards = gather_eight(both(own_columns(r), other_columns, place.yh))
    far = move(from_left, along_x(1))
    partner_left = move(from_left, swap_y)
    partner_right = move(partner, along_x(-1))

    far, partner_left, partner_right, out_other, branch, in_low = lax.optimization_barrier(
        (far, partner_left, partner_right, out_other, branch, in_low)
    )
    in_other = move(in_low, lambda yh, z, c, x, yl: (yh + 1, z, c, x, yl + 1))
    out_pair = both(out_low, out_other, place.yh)
    partner_far_top = move(partner_left[:half], along_x(1))
    partner_far_low = move(partner_right[half:], along_x(-1))

    vector = own_shards[:, :, :, SHARD_IN : SHARD_IN + 2].transpose(2, 0, 1, 3, 4)
    vector = vector.reshape(N_FSDP, 6 * WIDE)[:, :SHARD_SMALL].reshape(-1).astype(F32)
    offset = 0
    gain_in = vector[None, :D]
    offset = D
    gain_row = lax.dynamic_slice_in_dim(vector, offset + r * OWN, OWN, 0)[None, :]
    offset += DI
    taps = vector[offset : offset + (CONV + 1) * CHANNELS].reshape(CONV + 1, CHANNELS)
    offset += (CONV + 1) * CHANNELS
    per_head = vector[offset:].reshape(3, H)
    dt_bias, a_log, d_skip = lax.dynamic_slice_in_dim(per_head, r * OWN_H, OWN_H, 1)
    taps_bc = taps[:, DI:]
    conv_par = jnp.concatenate([lax.dynamic_slice_in_dim(taps, r * OWN, OWN, 1), taps_bc], 1)
    head_par = jnp.stack(
        [
            jnp.pad(jnp.broadcast_to(d_skip[:, None], (OWN_H, P_SIZE)).reshape(-1), (0, 2 * N)),
            jnp.pad(dt_bias, (0, 640 - OWN_H)),
            jnp.pad(-jnp.exp(a_log), (0, 640 - OWN_H)),
        ],
        0,
    )
    par = jnp.concatenate([conv_par, head_par, jnp.zeros((8, 640), F32)], 0)

    partner_far_top, partner_far_low, own_shards = lax.optimization_barrier(
        (partner_far_top, partner_far_low, own_shards)
    )
    full_out = gather_eight(tie(out_pair, own_shards))
    b_left = move(branch, along_x(1))
    b_right = move(branch, along_x(-1))
    b_partner = move(branch, swap_y)
    token_pieces = [
        tokens, partner, from_right, partner_right, far,
        partner_far_top, partner_far_low, from_left, partner_left,
    ]
    normed, proj, low_dt = run_project(ahead, token_pieces, gain_in, own_shards)
    b_left, b_right, b_partner, proj = lax.optimization_barrier((b_left, b_right, b_partner, proj))
    b_far = move(b_left, along_x(1))
    b_partner_left = move(b_left, swap_y)
    b_partner_right = move(b_partner, along_x(-1))
    before = run_forward(0, seg_ends, proj, par)
    b_far, b_partner_left, b_partner_right, before = lax.optimization_barrier(
        (b_far, b_partner_left, b_partner_right, before)
    )
    b_partner_far_top = move(b_partner_left[:half], along_x(1))
    b_partner_far_low = move(b_partner_right[half:], along_x(-1))
    pre, mixed, states, _ = run_forward(1, seg_ends, proj, par, before)
    mixed, in_low, in_other, b_partner_far_top, b_partner_far_low = lax.optimization_barrier(
        (mixed, in_low, in_other, b_partner_far_top, b_partner_far_low)
    )
    full_in = gather_eight(jnp.stack([in_low, in_other], 0))
    branch_pieces = [
        branch, b_partner, b_right, b_partner_right, b_far,
        b_partner_far_top, b_partner_far_low, b_left, b_partner_left,
    ]
    rep_table = jnp.concatenate([ahead, r[None]])
    grad_branch, grad_normed_out, sums = run_out_grad(rep_table, branch_pieces, full_out, mixed, proj, gain_row)
    sums = share_rep(sums[:2].reshape(32, 128)).sum(0).reshape(2, PACK)
    sums = jnp.concatenate([sums, jnp.zeros((6, PACK), F32)], 0)

    low, grad_mixed, grad_gain = run_gate(grad_normed_out, mixed, proj, sums, gain_row)

    low_rows = exchange(low.reshape(N_REP, ROWS, 2 * OWN), "rep")
    grad_x, grad_dtraw, grad_bc, grad_sums, grad_heads = run_backward(
        seg_ends, proj, pre, mixed, grad_mixed, states, par
    )
    low, grad_x = lax.optimization_barrier((low, grad_x))
    early_grad = run_early_grad(low, grad_branch, normed)
    low_rows, early_grad, grad_bc, grad_x = lax.optimization_barrier((low_rows, early_grad, grad_bc, grad_x))

    grad_bc = exchange(grad_bc, "rep").reshape(N_REP, OWN_BC, PACK)
    early = scatter_eight(early_grad)
    grad_rows = run_z_grad(low_rows, full_in)
    grad_bc, grad_rows = lax.optimization_barrier((grad_bc, grad_rows))

    tail, small_own = run_rest(
        seg_ends, grad_bc, pre, proj, par, grad_x, grad_dtraw, grad_sums, grad_heads, grad_gain, (r * OWN_BC)[None]
    )
    tail, small_own, low_rows = lax.optimization_barrier((tail, small_own, low_rows))
    tail_rows = exchange(tail.reshape(N_REP, ROWS, TAIL), "rep")
    block_out = run_block_out(low_rows, full_out, tokens, own_live)
    block_out, early, small_own = lax.optimization_barrier((block_out, early, small_own))
    tail_part = scatter_eight(run_tail_grad(normed, tail, small_own))
    mine, other = at(early, place.yh), at(early, 1 - place.yh)
    out_mine = move(
        mine[:SHARD_IN], lambda yh, z, c, x, yl: (x // 2, (x % 2) * 2 + yl, z % 2, 2 * c + yh, z // 2)
    )
    out_other = move(
        other[:SHARD_IN], lambda yh, z, c, x, yl: (x // 2, (x % 2) * 2 + yl, z % 2, 2 * c + 1 - yh, z // 2)
    )
    z_other = move(other[SHARD_IN:], swap_y_hi)
    tail_rows, out_mine, out_other, z_other = lax.optimization_barrier((tail_rows, out_mine, out_other, z_other))

    early_parts = share_rep(jnp.concatenate([out_mine + out_other, mine[SHARD_IN:] + z_other], 0))
    input_grad, grad_gain_in = run_input_grad(
        place.yh[None], grad_rows, tail_rows, full_in, low_dt, tokens, cotangent, gain_in
    )
    tail_part, grad_gain_in = lax.optimization_barrier((tail_part, grad_gain_in))

    tail_other = move(at(tail_part, 1 - place.yh), swap_y_hi)
    grad_gain_in = sum_z(grad_gain_in + move(grad_gain_in, swap_core))
    tail_part = at(tail_part, place.yh) + tail_other
    grad_gain_in = grad_gain_in + move(grad_gain_in, swap_y_hi)
    tail_part = jnp.concatenate([tail_part, grad_gain_in], 0)

    tail_part, early_parts = lax.optimization_barrier((tail_part, early_parts))
    tail_parts = share_rep(tail_part)

    grad_out, new_first_out, new_second_out, new_out = run_adam_early(
        lambda i: (i // 2, i % 2), slice(0, SHARD_IN), early_parts, w_out, first_out, second_out
    )
    updated = run_adam_early(
        lambda i: (0, i), slice(SHARD_IN, 2 * SHARD_IN), early_parts, w_in, first_in, second_in
    )
    grad_in, new_first_in, new_second_in, new_in = run_adam_tail(tail_parts, w_in, first_in, second_in, updated)

    def columns(parts):
        return parts.transpose(1, 0, 2).reshape(parts.shape[1], -1)

    small_parts = tail_parts[:, SHARD_IN : SHARD_IN + 8]
    grad_gain_in = tail_parts[:, SHARD_IN + 8 : SHARD_IN + 8 + D // TAIL].sum(0).reshape(-1)
    small_x = small_parts[:, :, :OWN].transpose(1, 0, 2).reshape(8, DI)
    small_bc = small_parts[:, :, OWN:].transpose(1, 0, 2)

    def channels(row):
        return jnp.concatenate([small_x[row], small_bc[row, :, :OWN_BC].reshape(-1)])

    grad_small_all = jnp.concatenate(
        [grad_gain_in, small_x[0]]
        + [channels(row) for row in range(1, 6)]
        + [
            small_bc[0, :, :OWN_H].reshape(-1),
            small_parts[:, 6, :OWN_H].reshape(-1),
            small_parts[:, 7, :OWN_H].reshape(-1),
        ]
    )
    grad_small = lax.dynamic_slice_in_dim(grad_small_all, place.f * SHARD_SMALL, SHARD_SMALL, 0)
    grad_dt = columns(tail_parts[:, :SHARD_IN, OWN + OWN_BC : OWN + OWN_BC + OWN_H])
    new_dt, new_first_dt, new_second_dt = adam_update(
        w_dt, grad_dt, first_dt, second_dt, RATE_MATRIX, WEIGHT_DECAY
    )
    new_small, new_first_small, new_second_small = adam_update(
        small, grad_small, first_small, second_small, RATE_SMALL, 0.0
    )
    return (
        block_out,
        input_grad,
        grad_in,
        grad_dt,
        grad_out,
        grad_small,
        new_first_in,
        new_first_dt,
        new_first_out,
        new_first_small,
        new_second_in,
        new_second_dt,
        new_second_out,
        new_second_small,
        new_in,
        new_dt,
        new_out,
        new_small,
    )


def solution(mesh):
    rows = P(("fsdp", "rep"), None)
    matrix = P("fsdp", None)
    vector = P("fsdp")
    group = (matrix, matrix, matrix, vector)
    return jax.shard_map(
        body,
        mesh=mesh,
        in_specs=(rows, rows, P()) + group * 3,
        out_specs=(rows, rows) + group * 4,
        check_vma=False,
    )
```
